32 devices in a mesh: pipe: 2 (over core), dp: 8 (over z, y), tensor: 2 (over x).
Axes of the slice: x: 2, y: 2, z: 4, core: 2. Of those that a mesh axis runs over, the one named last changes fastest.
Arguments:
- tokens: bfloat16 [2, 8, 64, 1024], P(None, 'dp'), may hold values from -6 to 6
- conv_grid: bfloat16 [2, 8, 8, 8, 1536], P(None, 'dp'), may hold values from -6 to 6
- order: int32 [8, 2], P('dp'), may hold values from 0 to 1, as said below
- trainable: int32 [2, 5], P('pipe'), may hold values from 0 to 1, as said below
- ln_attn: bfloat16 [2, 1024], P('pipe', 'dp'), may hold values from 0.099609375 to 1.8984375
- w_qkv: bfloat16 [2, 3, 1024, 1024], P('pipe', None, 'dp', 'tensor'), may hold values from -0.1875 to 0.1875
- w_attn_out: bfloat16 [2, 1024, 1024], P('pipe', 'tensor', 'dp'), may hold values from -1.5 to 1.5
- ln_mlp: bfloat16 [2, 1024], P('pipe', 'dp'), may hold values from 0.099609375 to 1.8984375
- w_fc_in: bfloat16 [2, 1024, 4096], P('pipe', 'dp', 'tensor'), may hold values from -0.1875 to 0.1875
- w_fc_out: bfloat16 [2, 4096, 1024], P('pipe', 'tensor', 'dp'), may hold values from -0.09375 to 0.09375
- conv_depth: bfloat16 [2, 49, 1536], P('pipe', None, 'dp'), may hold values from -0.875 to 0.875
- ln_conv: bfloat16 [2, 1536], P('pipe', 'dp'), may hold values from 0.099609375 to 1.8984375
- w_pw_in: bfloat16 [2, 1536, 6144], P('pipe', 'dp', 'tensor'), may hold values from -0.15625 to 0.15625
- w_pw_out: bfloat16 [2, 6144, 1536], P('pipe', 'tensor', 'dp'), may hold values from -0.078125 to 0.078125
- layer_scale: bfloat16 [2, 1536], P('pipe', 'dp'), may hold values from 0.5 to 1.5
- w_adapt: bfloat16 [2, 1536, 1024], P('pipe', 'dp', 'tensor'), may hold values from -0.15625 to 0.15625
- adapt_depth: bfloat16 [2, 9, 1024], P('pipe', None, 'tensor'), may hold values from -2 to 2
- w_gate_in: bfloat16 [2, 1024, 512], P('pipe', 'tensor', 'dp'), may hold values from -2 to 2
- w_gate_out: bfloat16 [2, 512, 1024], P('pipe', 'dp', 'tensor'), may hold values from -0.25 to 0.25
- tok_cot: bfloat16 [2, 8, 64, 1024], P(None, 'dp'), may hold values from -6 to 6
- grid_cot: bfloat16 [2, 8, 8, 8, 1536], P(None, 'dp'), may hold values from -6 to 6
Outputs:
- hidden_tokens: bfloat16 [2, 2, 8, 64, 1024], P('pipe', None, 'dp')
- hidden_grids: bfloat16 [2, 2, 8, 8, 8, 1536], P('pipe', None, 'dp')
- token_grads: bfloat16 [2, 2, 8, 64, 1024], P('pipe', None, 'dp')
- grid_grads: bfloat16 [2, 2, 8, 8, 8, 1536], P('pipe', None, 'dp')
- grad_ln_attn: float32 [2, 1024], P('pipe', 'dp')
- grad_w_qkv: float32 [2, 3, 1024, 1024], P('pipe', None, 'dp', 'tensor')
- grad_w_attn_out: float32 [2, 1024, 1024], P('pipe', 'tensor', 'dp')
- grad_ln_mlp: float32 [2, 1024], P('pipe', 'dp')
- grad_w_fc_in: float32 [2, 1024, 4096], P('pipe', 'dp', 'tensor')
- grad_w_fc_out: float32 [2, 4096, 1024], P('pipe', 'tensor', 'dp')
- grad_conv_depth: float32 [2, 49, 1536], P('pipe', None, 'dp')
- grad_ln_conv: float32 [2, 1536], P('pipe', 'dp')
- grad_w_pw_in: float32 [2, 1536, 6144], P('pipe', 'dp', 'tensor')
- grad_w_pw_out: float32 [2, 6144, 1536], P('pipe', 'tensor', 'dp')
- grad_layer_scale: float32 [2, 1536], P('pipe', 'dp')
- grad_w_adapt: float32 [2, 1536, 1024], P('pipe', 'dp', 'tensor')
- grad_adapt_depth: float32 [2, 9, 1024], P('pipe', None, 'tensor')
- grad_w_gate_in: float32 [2, 1024, 512], P('pipe', 'tensor', 'dp')
- grad_w_gate_out: float32 [2, 512, 1024], P('pipe', 'dp', 'tensor')
The draws below stay inside these ranges and needn't reach their ends.
Inputs may be any that keep to these rules, and one draw needn't show every extreme that they name: `order`: each row holds every micro-batch number exactly once. Each weight is trained in exactly one of the two layers: trainable[1, j] = 1 - trainable[0, j].
All inputs are finite; a program needn't handle non-finite values.
Results may differ from the reference program's by a relative error of at most 0.04.
Values may be sent and summed in bfloat16 or wider, within the bound.
A program may use at most 320 MiB of HBM per device.

```python
import jax
import jax.numpy as jnp
from jax import lax

D = 1024
HEADS = 16
HD = 64
FF = 4096
C = 1536
CF = 6144
DG = 512
G = 8
MB = 2
TOK = 64
IMAGES = 8


def draw_order(key, part):
    key = jax.random.fold_in(key, 11)
    scores = jax.random.randint(key, (IMAGES, MB), 0, 1 << 20) * MB + jnp.arange(MB, dtype=jnp.int32)[None, :]
    return jnp.argsort(scores, axis=-1, stable=True).astype(jnp.int32)


def draw_trainable(key, part):
    key = jax.random.fold_in(key, 23)
    first_row = jax.random.randint(key, (5,), 0, 2).astype(jnp.int32)
    return jnp.stack([first_row, 1 - first_row]).astype(jnp.int32)


def strengthened(array, stream_key, source, target, parts, factor):
    owner, partner = [(jnp.arange(array.shape[axis_at]) // (array.shape[axis_at] // parts)).reshape([-1 if axis == axis_at else 1 for axis in range(array.ndim)]) for axis_at in (source, target)]
    chosen = jax.random.permutation(stream_key, parts)[partner]
    strong = (owner == chosen) | (owner == (partner + parts // 2) % parts)
    return jnp.where(strong, factor * array, array)


def level_of(stream_key, extent, split, least, high):
    loudness = 1.0
    for position, shards_of in split:
        draws = jax.random.uniform(jax.random.fold_in(jax.random.fold_in(stream_key, 6), position), (shards_of,), jnp.float32, least / len(split), high / len(split))
        loudness = loudness * jnp.repeat(jnp.exp(draws), extent[position] // shards_of).reshape((-1,) + (1,) * (len(extent) - 1 - position))
    return loudness


def gaussian(stream_key, dims, scale, limit, split=(), kind=jnp.bfloat16):
    array = scale * jax.random.normal(stream_key, dims, jnp.float32)
    if split:
        array = array * level_of(stream_key, dims, split, -0.22, 0.18)
    return jnp.clip(array, -limit, limit).astype(kind)


def noise_with(own_key, extent, scale, reach, shards, heavy, held_as=jnp.bfloat16):
    drawn = scale * jax.random.normal(own_key, extent, jnp.float32)
    if shards:
        drawn = drawn * level_of(own_key, extent, shards, -0.22, 0.18)
    return jnp.clip(strengthened(drawn, jax.random.fold_in(own_key, 3), *heavy), -reach, reach).astype(held_as)


def setup_inputs(seed: int = 0) -> dict:
    key_of = jax.random.split(jax.random.key(seed), 22)
    tokens = gaussian(key_of[0], (MB, IMAGES, TOK, D), 1.0, 6.0, ((1, 8),))
    conv_grid = gaussian(key_of[1], (MB, IMAGES, G, G, C), 1.0, 6.0, ((1, 8),))
    order = draw_order(jax.random.fold_in(key_of[21], 71), 0)
    trainable = draw_trainable(jax.random.fold_in(key_of[21], 71), 0)
    ln_attn = jnp.clip(1.0 + 0.18 * jax.random.normal(key_of[4], (2, D), jnp.float32), 0.099609375, 1.8984375).astype(jnp.bfloat16)
    w_qkv = gaussian(key_of[5], (2, 3, D, D), D ** -0.5, 0.1875, ((0, 2), (2, 8), (3, 2)))
    w_attn_out = gaussian(key_of[6], (2, D, D), (max(D // 64, 1)) ** -0.5, 1.5, ((0, 2), (1, 2), (2, 8)))
    ln_mlp = jnp.clip(1.0 + 0.18 * jax.random.normal(key_of[7], (2, D), jnp.float32), 0.099609375, 1.8984375).astype(jnp.bfloat16)
    w_fc_in = gaussian(key_of[8], (2, D, FF), D ** -0.5, 0.1875, ((0, 2), (1, 8), (2, 2)))
    w_fc_out = gaussian(key_of[9], (2, FF, D), FF ** -0.5, 0.09375, ((0, 2), (1, 2), (2, 8)))
    conv_depth = gaussian(key_of[10], (2, 49, C), 49 ** -0.5, 0.875, ((0, 2), (2, 8)))
    ln_conv = jnp.clip(1.0 + 0.18 * jax.random.normal(key_of[11], (2, C), jnp.float32), 0.099609375, 1.8984375).astype(jnp.bfloat16)
    w_pw_in = gaussian(key_of[12], (2, C, CF), C ** -0.5, 0.15625, ((0, 2), (1, 8), (2, 2)))
    w_pw_out = gaussian(key_of[13], (2, CF, C), CF ** -0.5, 0.078125, ((0, 2), (1, 2), (2, 8)))
    layer_scale = jnp.clip(0.5 + 1.0 * jax.random.uniform(key_of[14], (2, C), jnp.float32) ** level_of(key_of[14], (2, C), ((0, 2), (1, 8)), -0.2, 0.2), 0.5, 1.5).astype(jnp.bfloat16)
    w_adapt = gaussian(key_of[15], (2, C, D), C ** -0.5, 0.15625, ((0, 2), (1, 8), (2, 2)))
    adapt_depth = gaussian(key_of[16], (2, 9, D), 9 ** -0.5, 2.0, ((0, 2), (2, 2)))
    w_gate_in = gaussian(key_of[17], (2, D, DG), (max(D // 128, 1)) ** -0.5, 2.0, ((0, 2), (1, 2), (2, 8)))
    w_gate_out = gaussian(key_of[18], (2, DG, D), DG ** -0.5, 0.25, ((0, 2), (1, 8), (2, 2)))
    tok_cot = noise_with(key_of[19], (MB, IMAGES, TOK, D), 1.0, 6.0, ((1, 8),), (1, 3, 8, 2.0))
    grid_cot = noise_with(key_of[20], (MB, IMAGES, G, G, C), 1.0, 6.0, ((1, 8),), (1, 4, 8, 2.0))
    return dict(tokens=tokens, conv_grid=conv_grid, order=order, trainable=trainable, ln_attn=ln_attn, w_qkv=w_qkv, w_attn_out=w_attn_out, ln_mlp=ln_mlp, w_fc_in=w_fc_in, w_fc_out=w_fc_out, conv_depth=conv_depth, ln_conv=ln_conv, w_pw_in=w_pw_in, w_pw_out=w_pw_out, layer_scale=layer_scale, w_adapt=w_adapt, adapt_depth=adapt_depth, w_gate_in=w_gate_in, w_gate_out=w_gate_out, tok_cot=tok_cot, grid_cot=grid_cot)


precise = lax.Precision.HIGHEST

@jax.custom_vjp
def low(v):
    return lax.optimization_barrier(v.astype(jnp.bfloat16)).astype(jnp.float32)

@jax.custom_vjp
def low_back(v):
    return v

def low_keep(v):
    return (low(v), None)

def low_pass(kept, grad):
    return (grad,)

def back_keep(v):
    return (v, None)

def back_low(kept, grad):
    return (low(grad),)
low.defvjp(low_keep, low_pass)
low_back.defvjp(back_keep, back_low)

def layer_norm(value_in, gain_vec):
    average = lax.optimization_barrier(jnp.mean(value_in, axis=-1, keepdims=True))
    centred = value_in - average
    variance = lax.optimization_barrier(jnp.mean(centred * centred, axis=-1, keepdims=True))
    return centred * lax.rsqrt(variance + 1e-06) * gain_vec

def depthwise(grid_in, kernel, side_len):
    reach_cells = side_len // 2
    padded = jnp.pad(grid_in, ((0, 0), (reach_cells, reach_cells), (reach_cells, reach_cells), (0, 0)))
    summed = jnp.zeros(grid_in.shape, jnp.float32)
    for row_at in range(side_len):
        for col_at in range(side_len):
            summed = summed + padded[:, row_at:row_at + G, col_at:col_at + G, :] * kernel[row_at * side_len + col_at]
    return summed

def layer(params, tokens_in, grid_in):
    ln_attn, w_qkv, w_attn_out, ln_mlp, w_fc_in, w_fc_out, conv_depth, ln_conv, w_pw_in, w_pw_out, layer_scale, w_adapt, adapt_depth, w_gate_in, w_gate_out = params
    batch_rows = tokens_in.shape[0]
    normed = low(layer_norm(tokens_in, ln_attn))
    projected = low_back(low(jnp.einsum('btd,sde->sbte', normed, w_qkv, precision=precise)))
    query_rows = projected[0].reshape(batch_rows, TOK, HEADS, HD)
    key_rows = projected[1].reshape(batch_rows, TOK, HEADS, HD)
    value_rows = projected[2].reshape(batch_rows, TOK, HEADS, HD)
    scores = jnp.einsum('bqhe,bkhe->bhqk', query_rows, key_rows, precision=precise) * HD ** (-0.5)
    attn_weights = low(jax.nn.softmax(scores, axis=-1))
    context = low(jnp.einsum('bhqk,bkhe->bqhe', attn_weights, value_rows, precision=precise).reshape(batch_rows, TOK, D))
    after_attn = tokens_in + jnp.einsum('btd,de->bte', context, w_attn_out, precision=precise)
    normed_mlp = low(layer_norm(after_attn, ln_mlp))
    inner_act = low(jax.nn.gelu(jnp.einsum('btd,df->btf', normed_mlp, w_fc_in, precision=precise), approximate=False))
    after_mlp = after_attn + jnp.einsum('btf,fd->btd', inner_act, w_fc_out, precision=precise)
    features = low(layer_norm(depthwise(grid_in, conv_depth, 7), ln_conv))
    conv_inner = low(jax.nn.gelu(jnp.einsum('bxyc,cf->bxyf', features, w_pw_in, precision=precise), approximate=False))
    grid_out = grid_in + layer_scale * jnp.einsum('bxyf,fc->bxyc', conv_inner, w_pw_out, precision=precise)
    adapted = jnp.einsum('bxyc,cd->bxyd', low(grid_out), w_adapt, precision=precise)
    spread = depthwise(adapted, adapt_depth, 3)
    pooled = lax.optimization_barrier(jnp.mean(spread, axis=(1, 2)))
    gate_hidden = jax.nn.gelu(jnp.dot(pooled, w_gate_in, precision=precise), approximate=False)
    gate_vec = jnp.tanh(jnp.dot(gate_hidden, w_gate_out, precision=precise))
    tokens_out = after_mlp + gate_vec[:, None, :] * spread.reshape(batch_rows, TOK, D)
    return (tokens_out, grid_out)

def reference(tokens, conv_grid, order, trainable, ln_attn, w_qkv, w_attn_out, ln_mlp, w_fc_in, w_fc_out, conv_depth, ln_conv, w_pw_in, w_pw_out, layer_scale, w_adapt, adapt_depth, w_gate_in, w_gate_out, tok_cot, grid_cot):
    weights = (ln_attn, w_qkv, w_attn_out, ln_mlp, w_fc_in, w_fc_out, conv_depth, ln_conv, w_pw_in, w_pw_out, layer_scale, w_adapt, adapt_depth, w_gate_in, w_gate_out)
    batch_rows = MB * IMAGES
    slot_ids = order.T.astype(jnp.int32)
    image_ids = jnp.arange(IMAGES, dtype=jnp.int32)[None, :]
    first_tok = tokens[slot_ids, image_ids].astype(jnp.float32).reshape(batch_rows, TOK, D)
    first_grid = conv_grid[slot_ids, image_ids].astype(jnp.float32).reshape(batch_rows, G, G, C)
    params_zero = tuple((piece[0].astype(jnp.float32) for piece in weights))
    params_one = tuple((piece[1].astype(jnp.float32) for piece in weights))
    (mid_tok, mid_grid), pull_zero = jax.vjp(layer, params_zero, first_tok, first_grid)
    mid_tok = low(mid_tok)
    mid_grid = low(mid_grid)
    (end_tok, end_grid), pull_one = jax.vjp(layer, params_one, mid_tok, mid_grid)
    grads_one, back_tok, back_grid = pull_one((tok_cot.astype(jnp.float32).reshape(batch_rows, TOK, D), grid_cot.astype(jnp.float32).reshape(batch_rows, G, G, C)))
    back_tok = low(back_tok)
    back_grid = low(back_grid)
    grads_zero, first_tok_grad, first_grid_grad = pull_zero((back_tok, back_grid))
    tok_arg_grad = jnp.zeros((MB, IMAGES, TOK, D), jnp.float32).at[slot_ids, image_ids].set(first_tok_grad.reshape(MB, IMAGES, TOK, D))
    grid_arg_grad = jnp.zeros((MB, IMAGES, G, G, C), jnp.float32).at[slot_ids, image_ids].set(first_grid_grad.reshape(MB, IMAGES, G, G, C))
    hidden_tokens = jnp.stack([mid_tok, end_tok]).reshape(2, MB, IMAGES, TOK, D).astype(jnp.bfloat16)
    hidden_grids = jnp.stack([mid_grid, end_grid]).reshape(2, MB, IMAGES, G, G, C).astype(jnp.bfloat16)
    token_grads = jnp.stack([tok_arg_grad, back_tok.reshape(MB, IMAGES, TOK, D)]).astype(jnp.bfloat16)
    grid_grads = jnp.stack([grid_arg_grad, back_grid.reshape(MB, IMAGES, G, G, C)]).astype(jnp.bfloat16)
    flags = trainable.astype(jnp.float32)
    stacked = []
    for number in range(15):
        both = jnp.stack([grads_zero[number], grads_one[number]])
        if 6 <= number <= 10:
            both = both * flags[:, number - 6].reshape((2,) + (1,) * (both.ndim - 1))
        stacked.append(both)
    return (hidden_tokens, hidden_grids, token_grads, grid_grads, stacked[0], stacked[1], stacked[2], stacked[3], stacked[4], stacked[5], stacked[6], stacked[7], stacked[8], stacked[9], stacked[10], stacked[11], stacked[12], stacked[13], stacked[14])
```

```python
import functools

import jax
import jax.numpy as jnp
from jax import lax
from jax.experimental import pallas as pl
from jax.experimental.pallas import tpu as pltpu
from jax.sharding import PartitionSpec as P

HD = 64
Z = 4
R = 2
TOK = 64
SIDE = 8
LANE = 128
BF = jnp.bfloat16
F32 = jnp.float32
ARRAYS = ("A", "P1", "P2", "F1", "F2", "E", "G")
EVENTS = (
    "n1", "f", "o", "cv", "n2", "c2", "m", "br", "gs",
    "dx3", "dgh", "dn2", "dc2", "dx1", "dcv", "dn1", "df", "gv", "gad",
)


def mm(a, b):
    return lax.dot_general(a, b, (((1,), (0,)), ((), ())), preferred_element_type=F32)


def mm_nt(a, b):
    return lax.dot_general(a, b, (((1,), (1,)), ((), ())), preferred_element_type=F32)


def mm_tn(a, b):
    return lax.dot_general(a, b, (((0,), (0,)), ((), ())), preferred_element_type=F32)


def flat(value):
    return value.reshape(-1, value.shape[-1])


def low(value):
    return value.astype(BF)


def wide(value):
    return value.astype(F32)


def gelu_pair(h):
    phi = 0.5 * (1.0 + lax.erf(h * 0.7071067811865476))
    dens = jnp.exp(-0.5 * h * h) * 0.3989422804014327
    return h * phi, phi + h * dens


def normed(value):
    centred = value - jnp.mean(value, axis=-1, keepdims=True)
    rs = lax.rsqrt(jnp.mean(centred * centred, axis=-1, keepdims=True) + 1e-06)
    return centred * rs, rs


def norm_back(dn, n_hat, rs, gain):
    gd = dn * gain
    return (
        gd
        - jnp.mean(gd, axis=-1, keepdims=True)
        - n_hat * jnp.mean(gd * n_hat, axis=-1, keepdims=True)
    ) * rs


def col_shift(value, by):
    if by == 0:
        return value
    at = lax.broadcasted_iota(jnp.int32, value.shape, 0) % SIDE
    rolled = pltpu.roll(value, (-by) % TOK, 0)
    return jnp.where((at + by >= 0) & (at + by < SIDE), rolled, 0.0)


def row_shift(value, by):
    if by == 0:
        return value
    gap = jnp.zeros((abs(by) * SIDE, value.shape[1]), value.dtype)
    if by > 0:
        return jnp.concatenate([value[by * SIDE :], gap], axis=0)
    return jnp.concatenate([gap, value[: TOK + by * SIDE]], axis=0)


def depthwise(value, tap, side):
    half = side // 2
    shifted = [col_shift(value, b - half) for b in range(side)]
    total = None
    for a in range(side):
        line = None
        for b in range(side):
            term = shifted[b] * tap(a * side + b)
            line = term if line is None else line + term
        line = row_shift(line, a - half)
        total = line if total is None else total + line
    return total


def depthwise_taps(value, grad, side, put):
    half = side // 2
    shifted = [col_shift(value, b - half) for b in range(side)]
    for a in range(side):
        d = a - half
        lo, hi = max(0, -d) * SIDE, (SIDE - max(0, d)) * SIDE
        for b in range(side):
            part = shifted[b][lo + d * SIDE : hi + d * SIDE] * grad[lo:hi]
            put(a * side + b, jnp.sum(part, axis=0, keepdims=True))


def main_kernel(dims, outer, *refs):
    at = iter(refs)

    def take(count):
        return [next(at) for _ in range(count)]

    packed = dict(zip(ARRAYS, take(len(ARRAYS))))
    v_in, adq_in, tok_in, grid_in, tcot_in, gcot_in = take(6)
    hid_tok, hid_grid, out_gtok, out_ggrid = take(4)
    native = dict(zip(ARRAYS, take(len(ARRAYS))))
    out_gv, out_gad = take(2)
    W = dict(zip(ARRAYS, take(len(ARRAYS))))
    RX = dict(zip(ARRAYS, take(len(ARRAYS))))
    (
        vv, aq, vec_c, vec_d, x_in, c_in, n1_all, f_all, n2_all, c2_all,
        o_sb, o_rb, cv_sb, cv_rb, m_sb, m_rb, br_sb, br_rb, gsb, dgb,
        qkv, prob, ctx, u, up, r, rp, cn, crs, cv_sum, x1, c2f,
        adapted, spread, pooled, gate,
        dx3, dcot, dx3_all, dn2_sb, dn2_rb, dc2_sb, dc2_rb, dx1_all, dcv_all,
        dn1_sb, dn1_rb, df_sb, df_rb, dh, dqkv, dhc, dx1, dc2t, dad, dct, dcn,
        gvs, gv_rb, gvx, gad, gad_rb,
    ) = take(62)
    (
        zs_send, zs_recv, s1_send, s1_recv, loc_sem, s2_send, s2_recv,
        v_send, v_recv, q_send, q_recv, h_send, h_recv, b_send, b_recv,
        xo_send, xo_recv, g_send, g_recv, a_send, a_recv, gx_send, gx_recv, go,
    ) = take(24)

    p = lax.axis_index("pipe")
    dpi = lax.axis_index("dp")
    x = lax.axis_index("tensor")
    rest = dpi % outer
    zi = dpi // (outer * R)
    ri = (dpi // outer) % R
    d_dim, c_dim, hq, ffq, cfq, adq, dg = dims
    adh = Z * adq

    def dev(z=None, rr=None, xx=None, pp=None):
        z = zi if z is None else z
        rr = ri if rr is None else rr
        return (
            p if pp is None else pp,
            (z * R + rr) * outer + rest,
            x if xx is None else xx,
        )

    def zto(d):
        return lax.rem(zi + d, Z)

    def zfrom(d):
        return lax.rem(zi + Z - d, Z)

    def remote(src, dst, ssem, rsem, device):
        return pltpu.make_async_remote_copy(
            src_ref=src, dst_ref=dst, send_sem=ssem, recv_sem=rsem,
            device_id=device, device_id_type=pl.DeviceIdType.MESH,
        )

    pending = []
    ev = {name: number for number, name in enumerate(EVENTS)}

    def gather_start(name, buf):
        e = ev[name]
        for d in range(1, Z):
            c = remote(buf.at[zi], buf.at[zi], zs_send.at[e, d - 1], zs_recv.at[e, d - 1], dev(zto(d)))
            c.start()
            pending.append(c)

    def gather_wait(name, buf):
        e = ev[name]
        for d in range(1, Z):
            slot = buf.at[zfrom(d)]
            remote(slot, slot, zs_send.at[e, d - 1], zs_recv.at[e, d - 1], dev(zto(d))).wait_recv()

    def scatter_start(name, sb, rb):
        e = ev[name]
        for d in range(1, Z):
            c = remote(sb.at[zto(d)], rb.at[d - 1], zs_send.at[e, d - 1], zs_recv.at[e, d - 1], dev(zto(d)))
            c.start()
            pending.append(c)

    def scatter_wait(name, sb, rb):
        e = ev[name]
        for d in range(1, Z):
            slot = rb.at[d - 1]
            remote(slot, slot, zs_send.at[e, d - 1], zs_recv.at[e, d - 1], dev(zto(d))).wait_recv()

    def scattered(sb, rb):
        return (wide(sb[zi]) + wide(rb[0])) + (wide(rb[1]) + wide(rb[2]))

    barrier = pltpu.get_barrier_semaphore()
    xo = 1 - x
    ro = 1 - ri
    greeted = [dev(pp=1 - p)]
    for d in range(1, Z):
        greeted += [dev(zto(d)), dev(zto(d), ro)]
    greeted += [dev(rr=ro), dev(xx=xo), dev(rr=ro, xx=xo)]
    for device in greeted:
        pl.semaphore_signal(barrier, inc=1, device_id=device, device_id_type=pl.DeviceIdType.MESH)
    pl.semaphore_wait(barrier, len(greeted))

    me8 = zi * R + ri
    vcopies = []
    for n, (d, flip) in enumerate([(d, s) for d in range(Z) for s in (0, 1)][1:]):
        tz = zto(d)
        tr = ro if flip else ri
        c = remote(v_in, vv.at[me8], v_send.at[n], v_recv.at[n], dev(tz, tr))
        c.start()
        pending.append(c)
        fr = zfrom(d) * R + tr
        vcopies.append(remote(vv.at[fr], vv.at[fr], v_send.at[n], v_recv.at[n], dev(tz, tr)))
    vv[me8] = v_in[...]
    cq = remote(adq_in, aq.at[x], q_send, q_recv, dev(xx=xo))
    cq.start()
    pending.append(cq)
    aq[x] = adq_in[...]

    @pl.when(p == 1)
    def _():
        pl.semaphore_wait(go, 1)

    step1 = {}
    for k, name in enumerate(ARRAYS):
        src, dst = packed[name], W[name]
        own = pltpu.make_async_copy(src.at[zi], dst.at[x, zi, ri], loc_sem.at[k])
        own.start()
        sends = []
        for d in range(1, Z):
            c = remote(src.at[zto(d)], dst.at[x, zi, ri], s1_send.at[k, d - 1], s1_recv.at[k, d - 1], dev(zto(d)))
            c.start()
            sends.append(c)
        step1[name] = (own, sends)

    def relay1(name):
        k = ARRAYS.index(name)
        w = W[name]
        own, sends = step1[name]
        own.wait()
        for d in range(1, Z):
            slot = w.at[x, zfrom(d), ri]
            remote(slot, slot, s1_send.at[k, d - 1], s1_recv.at[k, d - 1], dev(zto(d))).wait_recv()
        blk = w.at[x, :, ri]
        remote(blk, blk, s2_send.at[k, 0], s2_recv.at[k, 0], dev(rr=ro)).start()
        remote(blk, blk, s2_send.at[k, 1], s2_recv.at[k, 1], dev(xx=xo)).start()

    def relay2(name):
        k = ARRAYS.index(name)
        w = W[name]
        half = w.shape[3] // 2
        blk = w.at[x, :, ro]
        remote(blk, blk, s2_send.at[k, 0], s2_recv.at[k, 0], dev(rr=ro)).wait_recv()
        part = w.at[x, :, ro, :half]
        remote(part, part, s2_send.at[k, 2], s2_recv.at[k, 2], dev(xx=xo)).start()
        blk = w.at[xo, :, ri]
        remote(blk, blk, s2_send.at[k, 1], s2_recv.at[k, 1], dev(xx=xo)).wait_recv()
        part = w.at[xo, :, ri, half:]
        remote(part, part, s2_send.at[k, 3], s2_recv.at[k, 3], dev(rr=ro)).start()

    def relay3(name):
        k = ARRAYS.index(name)
        w = W[name]
        half = w.shape[3] // 2
        part = w.at[xo, :, ro, :half]
        remote(part, part, s2_send.at[k, 2], s2_recv.at[k, 2], dev(xx=xo)).wait_recv()
        part = w.at[xo, :, ro, half:]
        remote(part, part, s2_send.at[k, 3], s2_recv.at[k, 3], dev(rr=ro)).wait_recv()

    def relay_sent(name):
        k = ARRAYS.index(name)
        w = W[name]
        half = w.shape[3] // 2
        for c in step1[name][1]:
            c.wait_send()
        blk = w.at[x, :, ri]
        remote(blk, blk, s2_send.at[k, 0], s2_recv.at[k, 0], dev(rr=ro)).wait_send()
        remote(blk, blk, s2_send.at[k, 1], s2_recv.at[k, 1], dev(xx=xo)).wait_send()
        part = w.at[x, :, ro, :half]
        remote(part, part, s2_send.at[k, 2], s2_recv.at[k, 2], dev(xx=xo)).wait_send()
        part = w.at[xo, :, ri, half:]
        remote(part, part, s2_send.at[k, 3], s2_recv.at[k, 3], dev(rr=ro)).wait_send()

    for name in ARRAYS:
        relay1(name)
    for name in ARRAYS:
        relay2(name)
    for name in ARRAYS:
        relay3(name)
    for name in ARRAYS:
        relay_sent(name)

    @pl.when(p == 0)
    def _():
        pl.semaphore_signal(go, inc=1, device_id=dev(pp=1 - p), device_id_type=pl.DeviceIdType.MESH)

    for c in vcopies:
        c.wait_recv()
    remote(aq.at[xo], aq.at[xo], q_send, q_recv, dev(xx=xo)).wait_recv()
    for tile in range(c_dim // LANE):
        ua, ub = 2 * tile, 2 * tile + 1
        vec_c[:, tile * LANE : (tile + 1) * LANE] = wide(vv[ua // 3, ua % 3]) + wide(vv[ub // 3, ub % 3])
    for i in range(Z * R):
        vec_d[:, i * LANE : (i + 1) * LANE] = wide(vv[i, 0])[56:64]

    @pl.when(p == 0)
    def _():
        x_in[...] = tok_in[...]
        c_in[...] = grid_in[...]

    sib = dev(pp=1 - p)

    @pl.when(p == 1)
    def _():
        remote(x_in, x_in, h_send.at[0], h_recv.at[0], sib).wait_recv()
        remote(c_in, c_in, h_send.at[1], h_recv.at[1], sib).wait_recv()

    def gain_d(row):
        return vec_d[row : row + 1, :]

    def gain_c(row):
        return vec_c[row : row + 1, :]

    n_hat, _ = normed(wide(x_in[...]))
    n1_all[zi] = low(n_hat * gain_d(0))
    gather_start("n1", n1_all)

    @pl.loop(0, c_dim // LANE)
    def _(ch):
        lanes = pl.ds(pl.multiple_of(ch * LANE, LANE), LANE)
        taps = vec_c[:, lanes]
        cn[:, lanes] = depthwise(wide(c_in[:, lanes]), lambda k: taps[k : k + 1], 7)

    n_hat, rs = normed(cn[...])
    cn[...] = n_hat
    crs[...] = jnp.broadcast_to(rs, crs.shape)
    f_all[zi] = low(n_hat * gain_c(49))
    gather_start("f", f_all)

    gather_wait("n1", n1_all)
    for j in range(2):
        wj = flat(W["A"][j, :, :, :, 0 : 3 * hq].reshape(-1, 3 * hq))
        qkv[j] = low(mm(flat(n1_all[...]), wj))
    for j in range(2):

        @pl.loop(0, Z)
        def _(b):
            rows = pl.ds(pl.multiple_of(b * TOK, TOK), TOK)
            outs = []
            for h in range(hq // HD):
                q, kk, vv_ = (qkv[j, rows, s * hq + h * HD : s * hq + (h + 1) * HD] for s in range(3))
                sc = mm_nt(q, kk) * HD ** (-0.5)
                e = jnp.exp(sc - jnp.max(sc, axis=-1, keepdims=True))
                pr = low(e / jnp.sum(e, axis=-1, keepdims=True))
                prob[j, h, b] = pr
                outs.append(mm(pr, vv_))
            ctx[j, rows, :] = low(jnp.concatenate(outs, axis=1))

    @pl.loop(0, Z)
    def _(z):
        acc = mm_nt(ctx[0], flat(W["A"][0, z, :, :, 3 * hq :]))
        acc += mm_nt(ctx[1], flat(W["A"][1, z, :, :, 3 * hq :]))
        lanes = pl.ds(pl.multiple_of(z * (d_dim // Z), LANE), d_dim // Z)
        o_sb[:, :, lanes] = low(acc).reshape(Z, TOK, d_dim // Z)

    scatter_start("o", o_sb, o_rb)

    gather_wait("f", f_all)
    tile = 256
    for j in range(2):

        @pl.loop(0, cfq // tile)
        def _(t):
            lanes = pl.ds(pl.multiple_of(t * tile, tile), tile)
            act, der = gelu_pair(mm(flat(f_all[...]), flat(W["P1"][j, :, :, :, lanes].reshape(-1, tile))))
            r[j, :, lanes] = low(act)
            rp[j, :, lanes] = low(der)

    @pl.loop(0, Z)
    def _(z):
        acc = mm_nt(r[0], flat(W["P2"][0, z])) + mm_nt(r[1], flat(W["P2"][1, z]))
        lanes = pl.ds(pl.multiple_of(z * (c_dim // Z), LANE), c_dim // Z)
        cv_sb[:, :, lanes] = low(acc).reshape(Z, TOK, c_dim // Z)

    scatter_start("cv", cv_sb, cv_rb)

    scatter_wait("o", o_sb, o_rb)
    x1[...] = wide(x_in[...]) + scattered(o_sb, o_rb)
    n_hat, _ = normed(x1[...])
    n2_all[zi] = low(n_hat * gain_d(1))
    gather_start("n2", n2_all)

    scatter_wait("cv", cv_sb, cv_rb)
    cv_sum[...] = scattered(cv_sb, cv_rb)
    c2f[...] = wide(c_in[...]) + gain_c(50) * cv_sum[...]
    c2_all[zi] = low(c2f[...])
    gather_start("c2", c2_all)
    hid_grid[x] = low(c2f[...])

    gather_wait("n2", n2_all)
    for j in range(2):

        @pl.loop(0, ffq // tile)
        def _(t):
            lanes = pl.ds(pl.multiple_of(t * tile, tile), tile)
            act, der = gelu_pair(mm(flat(n2_all[...]), flat(W["F1"][j, :, :, :, lanes].reshape(-1, tile))))
            u[j, :, lanes] = low(act)
            up[j, :, lanes] = low(der)

    @pl.loop(0, Z)
    def _(z):
        acc = mm_nt(u[0], flat(W["F2"][0, z])) + mm_nt(u[1], flat(W["F2"][1, z]))
        lanes = pl.ds(pl.multiple_of(z * (d_dim // Z), LANE), d_dim // Z)
        m_sb[:, :, lanes] = low(acc).reshape(Z, TOK, d_dim // Z)

    scatter_start("m", m_sb, m_rb)

    gather_wait("c2", c2_all)
    row8 = lax.broadcasted_iota(jnp.int32, (8, adq), 0)
    gs_part = None
    for j in range(2):
        ad = mm(flat(c2_all[...]), flat(W["E"][j].reshape(-1, adq)))
        adapted[j] = ad
        taps = wide(aq[j])
        pool = jnp.zeros((8, adq), F32)
        for b in range(Z):
            sp = depthwise(ad[b * TOK : (b + 1) * TOK], lambda k: taps[k : k + 1], 3)
            spread[j, b] = sp
            pool = jnp.where(row8 == b, jnp.mean(sp, axis=0, keepdims=True), pool)
        pooled[j] = pool
        term = mm_nt(low(pool), flat(W["G"][j, :, :, :, 0:adq].reshape(-1, adq)))
        gs_part = term if gs_part is None else gs_part + term
    gsb[3] = gs_part
    e = ev["gs"]
    for d in range(1, Z):
        c = remote(gsb.at[3], gsb.at[d - 1], zs_send.at[e, d - 1], zs_recv.at[e, d - 1], dev(zto(d)))
        c.start()
        pending.append(c)
    for d in range(1, Z):
        remote(gsb.at[d - 1], gsb.at[d - 1], zs_send.at[e, d - 1], zs_recv.at[e, d - 1], dev(zto(d))).wait_recv()

    def gate_hidden():
        return gelu_pair((gsb[0] + gsb[1]) + (gsb[2] + gsb[3]))

    gh, _ = gate_hidden()
    for j in range(2):
        g8 = jnp.tanh(mm(low(gh), flat(W["G"][j, :, :, :, adq:].reshape(-1, adq))))
        gate[j] = g8
        for b in range(Z):
            br_sb[b, :, j * adq : (j + 1) * adq] = low(g8[b : b + 1] * spread[j, b])
    scatter_start("br", br_sb, br_rb)

    scatter_wait("m", m_sb, m_rb)
    x3 = x1[...] + scattered(m_sb, m_rb)
    dx1[...] = x3
    scatter_wait("br", br_sb, br_rb)
    for d in range(Z):
        src = zfrom(d)
        piece = br_sb[zi] if d == 0 else br_rb[d - 1]
        for j in range(2):
            lanes = pl.ds(pl.multiple_of(j * adh + src * adq, LANE), adq)
            dx1[:, lanes] += wide(piece[:, j * adq : (j + 1) * adq])
    hid_tok[x] = low(dx1[...])

    @pl.when(p == 0)
    def _():
        remote(hid_tok.at[x], x_in, h_send.at[0], h_recv.at[0], sib).start()
        remote(hid_grid.at[x], c_in, h_send.at[1], h_recv.at[1], sib).start()

    out_copies = []
    for n, buf in enumerate((hid_tok, hid_grid)):
        c = remote(buf.at[x], buf.at[x], xo_send.at[n], xo_recv.at[n], dev(xx=xo))
        c.start()
        pending.append(c)
        out_copies.append(remote(buf.at[xo], buf.at[xo], xo_send.at[n], xo_recv.at[n], dev(xx=xo)))

    @pl.when(p == 1)
    def _():
        dx3[...] = tcot_in[...]
        dcot[...] = gcot_in[...]

    @pl.when(p == 0)
    def _():
        remote(dx3, dx3, b_send.at[0], b_recv.at[0], sib).wait_recv()

    dx3_all[zi] = dx3[...]
    gather_start("dx3", dx3_all)
    gather_wait("dx3", dx3_all)

    def own_lanes(j):
        return pl.ds(pl.multiple_of(j * adh + zi * adq, LANE), adq)

    gh, ghp = gate_hidden()
    dgh_part = None
    dgp = []
    for j in range(2):
        dgate = jnp.zeros((8, adq), F32)
        for b in range(Z):
            dbr = wide(dx3_all[b, :, own_lanes(j)])
            dgate = jnp.where(row8 == b, jnp.sum(dbr * spread[j, b], axis=0, keepdims=True), dgate)
        dg8 = dgate * (1.0 - gate[j] * gate[j])
        dgp.append(dg8)
        term = mm_nt(low(dg8), flat(W["G"][j, :, :, :, adq:].reshape(-1, adq)))
        dgh_part = term if dgh_part is None else dgh_part + term
    dgb[3] = dgh_part
    e2 = ev["dgh"]
    for d in range(1, Z):
        c = remote(dgb.at[3], dgb.at[d - 1], zs_send.at[e2, d - 1], zs_recv.at[e2, d - 1], dev(zto(d)))
        c.start()
        pending.append(c)

    for j in range(2):

        @pl.loop(0, ffq // tile)
        def _(t):
            lanes = pl.ds(pl.multiple_of(t * tile, tile), tile)
            du = mm(flat(dx3_all[...]), flat(W["F2"][j, :, :, :, lanes].reshape(-1, tile)))
            dh[j, :, lanes] = low(du * wide(up[j, :, lanes]))

    @pl.loop(0, Z)
    def _(z):
        acc = mm_nt(dh[0], flat(W["F1"][0, z])) + mm_nt(dh[1], flat(W["F1"][1, z]))
        lanes = pl.ds(pl.multiple_of(z * (d_dim // Z), LANE), d_dim // Z)
        dn2_sb[:, :, lanes] = low(acc).reshape(Z, TOK, d_dim // Z)

    scatter_start("dn2", dn2_sb, dn2_rb)

    for d in range(1, Z):
        remote(dgb.at[d - 1], dgb.at[d - 1], zs_send.at[e2, d - 1], zs_recv.at[e2, d - 1], dev(zto(d))).wait_recv()
    dgs = ((dgb[0] + dgb[1]) + (dgb[2] + dgb[3])) * ghp
    for j in range(2):
        dpool = mm(low(dgs), flat(W["G"][j, :, :, :, 0:adq].reshape(-1, adq))) * (1.0 / TOK)
        taps = wide(aq[j])
        tap_rows = [None] * 9
        for b in range(Z):
            dsp = gate[j, b : b + 1] * wide(dx3_all[b, :, own_lanes(j)]) + dpool[b : b + 1]
            dad[j, b * TOK : (b + 1) * TOK] = low(depthwise(dsp, lambda k: taps[8 - k : 9 - k], 3))

            def put(k, row):
                tap_rows[k] = row if tap_rows[k] is None else tap_rows[k] + row

            depthwise_taps(adapted[j, b * TOK : (b + 1) * TOK], dsp, 3, put)
        for k in range(9):
            gad[j, k : k + 1] = tap_rows[k]
        gad[j, 9:16] = jnp.zeros((7, adq), F32)
        W["G"][j, :, :, :, 0:adq] = low(mm_tn(low(dgs), low(pooled[j]))).reshape(Z, R, -1, adq)
        W["G"][j, :, :, :, adq:] = low(mm_tn(low(gh), low(dgp[j]))).reshape(Z, R, -1, adq)

    @pl.loop(0, Z)
    def _(z):
        acc = mm_nt(dad[0], flat(W["E"][0, z])) + mm_nt(dad[1], flat(W["E"][1, z]))
        lanes = pl.ds(pl.multiple_of(z * (c_dim // Z), LANE), c_dim // Z)
        dc2_sb[:, :, lanes] = low(acc).reshape(Z, TOK, c_dim // Z)

    scatter_start("dc2", dc2_sb, dc2_rb)

    peers = ((1, 0), (0, 1), (1, 1))

    def owner(k):
        return (ro if peers[k][0] else ri), (xo if peers[k][1] else x)

    def reduce_start(name):
        n = ARRAYS.index(name)
        for k in range(3):
            rr, xx = owner(k)
            c = remote(W[name].at[xx, :, rr], RX[name].at[k], g_send.at[n, k], g_recv.at[n, k], dev(rr=rr, xx=xx))
            c.start()
            pending.append(c)

    def weight_grad(name, lanes, left, right):
        width = W[name].shape[3]

        @pl.loop(0, Z)
        def _(z):
            span = R * width
            cols = pl.ds(pl.multiple_of(z * span, LANE), span)
            lhs = flat(left[:, :, cols])
            for j in range(2):
                W[name][j, z, :, :, lanes] = low(mm_tn(lhs, right[j])).reshape(R, width, -1)

    weight_grad("F2", slice(None), dx3_all, u)
    reduce_start("F2")
    weight_grad("F1", slice(None), n2_all, dh)
    reduce_start("F1")

    scatter_wait("dn2", dn2_sb, dn2_rb)
    dn2 = scattered(dn2_sb, dn2_rb)
    n_hat, rs = normed(x1[...])
    gvs_d1 = jnp.sum(dn2 * n_hat, axis=0, keepdims=True)
    dx1[...] = wide(dx3[...]) + norm_back(dn2, n_hat, rs, gain_d(1))
    dx1_all[zi] = low(dx1[...])
    gather_start("dx1", dx1_all)

    @pl.when(p == 0)
    def _():
        remote(dcot, dcot, b_send.at[1], b_recv.at[1], sib).wait_recv()

    scatter_wait("dc2", dc2_sb, dc2_rb)
    dc2t[...] = wide(dcot[...]) + scattered(dc2_sb, dc2_rb)
    gvs_ls = jnp.sum(cv_sum[...] * dc2t[...], axis=0, keepdims=True)
    dcv_all[zi] = low(dc2t[...] * gain_c(50))
    gather_start("dcv", dcv_all)

    reduce_start("G")
    weight_grad("E", slice(None), c2_all, dad)
    reduce_start("E")

    gather_wait("dx1", dx1_all)
    for j in range(2):
        do = mm(flat(dx1_all[...]), flat(W["A"][j, :, :, :, 3 * hq :].reshape(-1, hq)))
        dh[j, :, 0:hq] = low(do)
    for j in range(2):

        @pl.loop(0, Z)
        def _(b):
            rows = pl.ds(pl.multiple_of(b * TOK, TOK), TOK)
            parts = [[], [], []]
            for h in range(hq // HD):
                q, kk, vv_ = (qkv[j, rows, s * hq + h * HD : s * hq + (h + 1) * HD] for s in range(3))
                do = dh[j, rows, h * HD : (h + 1) * HD]
                pr = prob[j, h, b]
                dp = mm_nt(do, vv_)
                prw = wide(pr)
                ds = low(prw * (dp - jnp.sum(dp * prw, axis=-1, keepdims=True)) * HD ** (-0.5))
                parts[0].append(mm(ds, kk))
                parts[1].append(mm_tn(ds, q))
                parts[2].append(mm_tn(pr, do))
            for s in range(3):
                dqkv[j, rows, s * hq : (s + 1) * hq] = low(jnp.concatenate(parts[s], axis=1))

    @pl.loop(0, Z)
    def _(z):
        acc = mm_nt(dqkv[0], flat(W["A"][0, z, :, :, 0 : 3 * hq]))
        acc += mm_nt(dqkv[1], flat(W["A"][1, z, :, :, 0 : 3 * hq]))
        lanes = pl.ds(pl.multiple_of(z * (d_dim // Z), LANE), d_dim // Z)
        dn1_sb[:, :, lanes] = low(acc).reshape(Z, TOK, d_dim // Z)

    scatter_start("dn1", dn1_sb, dn1_rb)

    gather_wait("dcv", dcv_all)
    for j in range(2):

        @pl.loop(0, cfq // tile)
        def _(t):
            lanes = pl.ds(pl.multiple_of(t * tile, tile), tile)
            dr = mm(flat(dcv_all[...]), flat(W["P2"][j, :, :, :, lanes].reshape(-1, tile)))
            dhc[j, :, lanes] = low(dr * wide(rp[j, :, lanes]))

    @pl.loop(0, Z)
    def _(z):
        acc = mm_nt(dhc[0], flat(W["P1"][0, z])) + mm_nt(dhc[1], flat(W["P1"][1, z]))
        lanes = pl.ds(pl.multiple_of(z * (c_dim // Z), LANE), c_dim // Z)
        df_sb[:, :, lanes] = low(acc).reshape(Z, TOK, c_dim // Z)

    scatter_start("df", df_sb, df_rb)

    scatter_wait("dn1", dn1_sb, dn1_rb)
    dn1 = scattered(dn1_sb, dn1_rb)
    n_hat, rs = normed(wide(x_in[...]))
    gvs_d0 = jnp.sum(dn1 * n_hat, axis=0, keepdims=True)
    out_gtok[x] = low(dx1[...] + norm_back(dn1, n_hat, rs, gain_d(0)))

    @pl.when(p == 1)
    def _():
        remote(out_gtok.at[x], dx3, b_send.at[0], b_recv.at[0], sib).start()

    scatter_wait("df", df_sb, df_rb)
    dfv = scattered(df_sb, df_rb)
    gvs_lc = jnp.sum(dfv * cn[...], axis=0, keepdims=True)
    dcn[...] = norm_back(dfv, cn[...], crs[:, 0:1], gain_c(49))

    @pl.loop(0, c_dim // LANE)
    def _(ch):
        lanes = pl.ds(pl.multiple_of(ch * LANE, LANE), LANE)
        taps = vec_c[:, lanes]
        back = depthwise(dcn[:, lanes], lambda k: taps[48 - k : 49 - k], 7)
        out_ggrid[x, :, lanes] = low(dc2t[:, lanes] + back)

    @pl.when(p == 1)
    def _():
        remote(out_ggrid.at[x], dcot, b_send.at[1], b_recv.at[1], sib).start()

    for n, buf in enumerate((out_gtok, out_ggrid)):
        c = remote(buf.at[x], buf.at[x], xo_send.at[n + 2], xo_recv.at[n + 2], dev(xx=xo))
        c.start()
        pending.append(c)
        out_copies.append(remote(buf.at[xo], buf.at[xo], xo_send.at[n + 2], xo_recv.at[n + 2], dev(xx=xo)))

    weight_grad("P2", slice(None), dcv_all, r)
    reduce_start("P2")
    weight_grad("P1", slice(None), f_all, dhc)
    reduce_start("P1")
    weight_grad("A", slice(0, 3 * hq), n1_all, dqkv)
    weight_grad("A", slice(3 * hq, 4 * hq), dx1_all, ctx)
    reduce_start("A")

    third = c_dim // Z
    quarter = d_dim // Z

    @pl.loop(0, Z)
    def _(z):
        for part in range(third // LANE):
            lanes = pl.ds(pl.multiple_of(z * third + part * LANE, LANE), LANE)

            def put(k, row):
                gvs[z, k : k + 1, part * LANE : (part + 1) * LANE] = row

            depthwise_taps(wide(c_in[:, lanes]), dcn[:, lanes], 7, put)

    for z in range(Z):
        gvs[z, 49:50] = gvs_lc[:, z * third : (z + 1) * third]
        gvs[z, 50:51] = gvs_ls[:, z * third : (z + 1) * third]
        gvs[z, 51:64] = jnp.zeros((13, third), F32)
        gvs[z, 56:57, 0:quarter] = gvs_d0[:, z * quarter : (z + 1) * quarter]
        gvs[z, 57:58, 0:quarter] = gvs_d1[:, z * quarter : (z + 1) * quarter]
    scatter_start("gv", gvs, gv_rb)
    for k in range(3):
        rr, xx = owner(k)
        c = remote(gad, gad_rb.at[k], gx_send.at[1, k], gx_recv.at[1, k], dev(rr=rr, xx=xx))
        c.start()
        pending.append(c)
    scatter_wait("gv", gvs, gv_rb)
    gvx[3] = (gvs[zi] + gv_rb[0]) + (gv_rb[1] + gv_rb[2])
    for k in range(3):
        rr, xx = owner(k)
        c = remote(gvx.at[3], gvx.at[k], gx_send.at[0, k], gx_recv.at[0, k], dev(rr=rr, xx=xx))
        c.start()
        pending.append(c)
    for k in range(3):
        remote(gad, gad_rb.at[k], gx_send.at[1, k], gx_recv.at[1, k], dev(xx=xo)).wait_recv()
    out_gad[zi] = (gad[x] + gad_rb[0, x]) + (gad_rb[1, x] + gad_rb[2, x])
    gather_start("gad", out_gad)

    for name in ("F2", "F1", "G", "E", "P2", "P1", "A"):
        n = ARRAYS.index(name)
        rx = RX[name]
        for k in range(3):
            remote(rx.at[k], rx.at[k], g_send.at[n, k], g_recv.at[n, k], dev(xx=xo)).wait_recv()

        @pl.loop(0, Z)
        def _(z):
            total = (wide(W[name][x, z, ri]) + wide(rx[0, z])) + (wide(rx[1, z]) + wide(rx[2, z]))
            rx[0, z] = low(total)

        for d in range(1, Z):
            c = remote(rx.at[0, zto(d)], native[name].at[zi], a_send.at[n, d - 1], a_recv.at[n, d - 1], dev(zto(d)))
            c.start()
            pending.append(c)
        own = pltpu.make_async_copy(rx.at[0, zi], native[name].at[zi], loc_sem.at[n])
        own.start()

    for k in range(3):
        remote(gvx.at[k], gvx.at[k], gx_send.at[0, k], gx_recv.at[0, k], dev(xx=xo)).wait_recv()
    out_gv[...] = (gvx[0] + gvx[1]) + (gvx[2] + gvx[3])
    gather_wait("gad", out_gad)
    for name in ARRAYS:
        n = ARRAYS.index(name)
        pltpu.make_async_copy(RX[name].at[0, zi], native[name].at[zi], loc_sem.at[n]).wait()
        for d in range(1, Z):
            slot = native[name].at[zfrom(d)]
            remote(slot, slot, a_send.at[n, d - 1], a_recv.at[n, d - 1], dev(zto(d))).wait_recv()
    for c in out_copies:
        c.wait_recv()

    @pl.when(p == 0)
    def _():
        remote(hid_tok.at[x], x_in, h_send.at[0], h_recv.at[0], sib).wait_send()
        remote(hid_grid.at[x], c_in, h_send.at[1], h_recv.at[1], sib).wait_send()

    @pl.when(p == 1)
    def _():
        remote(out_gtok.at[x], dx3, b_send.at[0], b_recv.at[0], sib).wait_send()
        remote(out_ggrid.at[x], dcot, b_send.at[1], b_recv.at[1], sib).wait_send()

    for c in pending:
        c.wait_send()


def run_layers(packed, vec, adq, tok, grid, tcot, gcot, sizes, outer):
    d_dim, c_dim, hq, ffq, cfq, adw, dg = sizes
    vm = pltpu.VMEM
    shapes = [value.shape for value in packed]
    gather = [(2, Z, R) + s[1:] for s in shapes]
    partial = [(3, Z) + s[1:] for s in shapes]
    rows = Z * TOK

    def act(width, count=Z, kind=BF):
        return vm((count, TOK, width), kind)

    scratch = [vm(s, BF) for s in gather] + [vm(s, BF) for s in partial]
    scratch += [
        vm((Z * R, 3, 64, LANE), BF), vm((2, 16, adw), BF), vm((64, c_dim), F32), vm((8, d_dim), F32),
        vm((TOK, d_dim), BF), vm((TOK, c_dim), BF), act(d_dim), act(c_dim), act(d_dim), act(c_dim),
        act(d_dim), act(d_dim, 3), act(c_dim), act(c_dim, 3), act(d_dim), act(d_dim, 3),
        act(2 * adw), act(2 * adw, 3), vm((4, 8, dg), F32), vm((4, 8, dg), F32),
        vm((2, rows, 3 * hq), BF), vm((2, hq // HD, Z, TOK, TOK), BF), vm((2, rows, hq), BF),
        vm((2, rows, ffq), BF), vm((2, rows, ffq), BF), vm((2, rows, cfq), BF), vm((2, rows, cfq), BF),
        vm((TOK, c_dim), F32), vm((TOK, LANE), F32), vm((TOK, c_dim), F32), vm((TOK, d_dim), F32), vm((TOK, c_dim), F32),
        vm((2, rows, adw), F32), vm((2, Z, TOK, adw), F32), vm((2, 8, adw), F32), vm((2, 8, adw), F32),
        vm((TOK, d_dim), BF), vm((TOK, c_dim), BF), act(d_dim), act(d_dim), act(d_dim, 3), act(c_dim), act(c_dim, 3),
        act(d_dim), act(c_dim),
        act(d_dim), act(d_dim, 3), act(c_dim), act(c_dim, 3), vm((2, rows, ffq), BF), vm((2, rows, 3 * hq), BF),
        vm((2, rows, cfq), BF), vm((TOK, d_dim), F32), vm((TOK, c_dim), F32), vm((2, rows, adw), BF),
        vm((8, LANE), F32), vm((TOK, c_dim), F32),
        vm((Z, 64, c_dim // Z), F32), vm((3, 64, c_dim // Z), F32), vm((4, 64, c_dim // Z), F32),
        vm((2, 16, adw), F32), vm((3, 2, 16, adw), F32),
    ]
    dma = pltpu.SemaphoreType.DMA
    na = len(ARRAYS)
    scratch += [
        dma((len(EVENTS), 3)), dma((len(EVENTS), 3)), dma((na, 3)), dma((na, 3)), dma((na,)),
        dma((na, 4)), dma((na, 4)), dma((7,)), dma((7,)), dma, dma, dma((2,)), dma((2,)), dma((2,)), dma((2,)),
        dma((4,)), dma((4,)), dma((na, 3)), dma((na, 3)), dma((na, 3)), dma((na, 3)), dma((2, 3)), dma((2, 3)),
        pltpu.SemaphoreType.REGULAR,
    ]
    out_shape = [
        jax.ShapeDtypeStruct((2, TOK, d_dim), BF),
        jax.ShapeDtypeStruct((2, TOK, c_dim), BF),
        jax.ShapeDtypeStruct((2, TOK, d_dim), BF),
        jax.ShapeDtypeStruct((2, TOK, c_dim), BF),
    ]
    out_shape += [jax.ShapeDtypeStruct(s, BF) for s in shapes]
    out_shape += [
        jax.ShapeDtypeStruct((64, c_dim // Z), F32),
        jax.ShapeDtypeStruct((Z, 16, adw), F32),
    ]
    any_spec = pl.BlockSpec(memory_space=pl.ANY)
    vm_spec = pl.BlockSpec(memory_space=pltpu.VMEM)
    return pl.pallas_call(
        functools.partial(main_kernel, sizes, outer),
        out_shape=out_shape,
        in_specs=[any_spec] * na + [vm_spec] * 6,
        out_specs=[vm_spec] * 4 + [any_spec] * na + [vm_spec] * 2,
        scratch_shapes=scratch,
        compiler_params=pltpu.CompilerParams(
            collective_id=0, has_side_effects=True, vmem_limit_bytes=62 * 1024 * 1024
        ),
        cost_estimate=pl.CostEstimate(flops=26 * 10**9, bytes_accessed=10**8, transcendentals=10**7),
        name="layers",
    )(*packed, vec, adq, tok, grid, tcot, gcot)


def quarters(value):
    rows = value.shape[0]
    return value.reshape(rows, Z, -1).transpose(1, 0, 2)


def quarters_t(value):
    return value.reshape(Z, -1, value.shape[1]).transpose(0, 2, 1)


def joined(value):
    return value.transpose(1, 0, 2).reshape(value.shape[1], -1)


def joined_t(value):
    return value.transpose(0, 2, 1).reshape(-1, value.shape[1])


def per_device(
    tokens,
    conv_grid,
    order,
    trainable,
    ln_attn,
    w_qkv,
    w_attn_out,
    ln_mlp,
    w_fc_in,
    w_fc_out,
    conv_depth,
    ln_conv,
    w_pw_in,
    w_pw_out,
    layer_scale,
    w_adapt,
    adapt_depth,
    w_gate_in,
    w_gate_out,
    tok_cot,
    grid_cot,
):
    dp_count = lax.axis_size("dp")
    outer = dp_count // (Z * R)
    groups = [[g * outer + o for o in range(outer)] for g in range(Z * R)]
    layer_at = lax.axis_index("pipe")
    slot = lax.axis_index("tensor")
    dp_at = lax.axis_index("dp")
    zi = dp_at // (outer * R)
    group_at = dp_at // outer

    def block(value, axis):
        value = value[0]
        if outer == 1:
            return value
        return lax.all_gather(value, "dp", axis=axis, tiled=True, axis_index_groups=groups)

    def share(value, axis):
        if outer == 1:
            return value
        return lax.psum_scatter(
            value, "dp", scatter_dimension=axis, tiled=True, axis_index_groups=groups
        )

    qkv = block(w_qkv, 1)
    attn_out = block(w_attn_out, 1)
    fc_in = block(w_fc_in, 0)
    fc_out = block(w_fc_out, 1)
    pw_in = block(w_pw_in, 0)
    pw_out = block(w_pw_out, 1)
    adapt = block(w_adapt, 0)
    gate_in = block(w_gate_in, 1)
    gate_out = block(w_gate_out, 0)
    taps = block(conv_depth, 1)
    gain_a = block(ln_attn, 0)
    gain_m = block(ln_mlp, 0)
    gain_c = block(ln_conv, 0)
    scale = block(layer_scale, 0)

    rows_d = qkv.shape[1]
    rows_c = pw_in.shape[0]
    hq = qkv.shape[2] // Z
    ffq = fc_in.shape[1] // Z
    cfq = pw_in.shape[1] // Z
    adw = adapt.shape[1] // Z
    rows_g = gate_in.shape[1]
    sizes = (rows_d * Z * R, rows_c * Z * R, hq, ffq, cfq, adw, rows_g * Z * R)
    packed = (
        jnp.concatenate(
            [
                qkv.reshape(3, rows_d, Z, hq).transpose(2, 1, 0, 3).reshape(Z, rows_d, 3 * hq),
                quarters_t(attn_out),
            ],
            axis=2,
        ),
        quarters(pw_in),
        quarters_t(pw_out),
        quarters(fc_in),
        quarters_t(fc_out),
        quarters(adapt),
        jnp.concatenate([quarters_t(gate_in), quarters(gate_out)], axis=2),
    )
    lines = jnp.concatenate([taps, gain_c[None], scale[None]], axis=0)
    units = jnp.pad(lines.reshape(lines.shape[0], 3, 64), ((0, 64 - lines.shape[0]), (0, 0), (0, 0)))
    units = units.transpose(1, 0, 2)
    unit_at = group_at * 3 + jnp.arange(3)
    upper = (unit_at % 2 == 1)[:, None, None]
    nothing = jnp.zeros_like(units)
    vec = jnp.concatenate(
        [jnp.where(upper, nothing, units), jnp.where(upper, units, nothing)], axis=2
    )
    vec = vec.at[0, 56].set(gain_a).at[0, 57].set(gain_m)
    adq = lax.dynamic_slice_in_dim(adapt_depth[0], zi * adw, adw, 1)
    adq = jnp.pad(adq, ((0, 7), (0, 0)))

    def slot_of(values, at):
        return lax.dynamic_index_in_dim(values, at, 0, keepdims=False).reshape(
            TOK, values.shape[-1]
        )

    source = lax.dynamic_index_in_dim(order[0], slot, 0, keepdims=False)
    outs = run_layers(
        packed,
        vec,
        adq,
        slot_of(tokens, source),
        slot_of(conv_grid, source),
        slot_of(tok_cot, slot),
        slot_of(grid_cot, slot),
        sizes,
        outer,
    )
    hid_tok, hid_grid, g_tok, g_grid = outs[:4]
    g_a, g_p1, g_p2, g_f1, g_f2, g_e, g_g = [value.astype(F32) for value in outs[4:11]]
    g_vec, g_ad = outs[11:]

    swap = (layer_at == 0) & (order[0, 0] == 1)
    g_tok = jnp.where(swap, g_tok[::-1], g_tok)
    g_grid = jnp.where(swap, g_grid[::-1], g_grid)
    grid_shape = (1,) + conv_grid.shape
    tok_shape = (1,) + tokens.shape

    flags = trainable[0].astype(F32)
    own_r = group_at % R
    vec_c = lax.dynamic_slice_in_dim(g_vec, own_r * rows_c, rows_c, 1)
    vec_d = lax.dynamic_slice_in_dim(g_vec, own_r * rows_d, rows_d, 1)
    g_qkv = g_a[:, :, : 3 * hq].reshape(Z, rows_d, 3, hq).transpose(2, 1, 0, 3)
    g_qkv = g_qkv.reshape(3, rows_d, Z * hq)
    side_taps = taps.shape[0]
    g_depth = joined(g_ad)[: adapt_depth.shape[1]]
    if outer > 1:
        g_depth = lax.psum(g_depth, "dp", axis_index_groups=groups)
    return (
        hid_tok.reshape(tok_shape),
        hid_grid.reshape(grid_shape),
        g_tok.reshape(tok_shape),
        g_grid.reshape(grid_shape),
        share(vec_d[56], 0)[None],
        share(g_qkv, 1)[None],
        share(joined_t(g_a[:, :, 3 * hq :]), 1)[None],
        share(vec_d[57], 0)[None],
        share(joined(g_f1), 0)[None],
        share(joined_t(g_f2), 1)[None],
        share(vec_c[:side_taps] * flags[0], 1)[None],
        share(vec_c[side_taps] * flags[1], 0)[None],
        share(joined(g_p1) * flags[2], 0)[None],
        share(joined_t(g_p2) * flags[3], 1)[None],
        share(vec_c[side_taps + 1] * flags[4], 0)[None],
        share(joined(g_e), 0)[None],
        g_depth[None],
        share(joined_t(g_g[:, :, :adw]), 1)[None],
        share(joined(g_g[:, :, adw:]), 0)[None],
    )


def solution(mesh):
    in_specs = (
        P(None, "dp", None, None),
        P(None, "dp", None, None, None),
        P("dp", None),
        P("pipe", None),
        P("pipe", "dp"),
        P("pipe", None, "dp", "tensor"),
        P("pipe", "tensor", "dp"),
        P("pipe", "dp"),
        P("pipe", "dp", "tensor"),
        P("pipe", "tensor", "dp"),
        P("pipe", None, "dp"),
        P("pipe", "dp"),
        P("pipe", "dp", "tensor"),
        P("pipe", "tensor", "dp"),
        P("pipe", "dp"),
        P("pipe", "dp", "tensor"),
        P("pipe", None, "tensor"),
        P("pipe", "tensor", "dp"),
        P("pipe", "dp", "tensor"),
        P(None, "dp", None, None),
        P(None, "dp", None, None, None),
    )
    out_specs = (
        P("pipe", None, "dp", None, None),
        P("pipe", None, "dp", None, None, None),
        P("pipe", None, "dp", None, None),
        P("pipe", None, "dp", None, None, None),
        P("pipe", "dp"),
        P("pipe", None, "dp", "tensor"),
        P("pipe", "tensor", "dp"),
        P("pipe", "dp"),
        P("pipe", "dp", "tensor"),
        P("pipe", "tensor", "dp"),
        P("pipe", None, "dp"),
        P("pipe", "dp"),
        P("pipe", "dp", "tensor"),
        P("pipe", "tensor", "dp"),
        P("pipe", "dp"),
        P("pipe", "dp", "tensor"),
        P("pipe", None, "tensor"),
        P("pipe", "tensor", "dp"),
        P("pipe", "dp", "tensor"),
    )
    return jax.shard_map(
        per_device, mesh=mesh, in_specs=in_specs, out_specs=out_specs, check_vma=False
    )
```

```python
import functools

import jax
import jax.numpy as jnp
from jax import lax
from jax.experimental import pallas as pl
from jax.experimental.pallas import tpu as pltpu
from jax.sharding import PartitionSpec as P

HD = 64
Z = 4
R = 2
TOK = 64
SIDE = 8
LANE = 128
BF = jnp.bfloat16
F32 = jnp.float32
ARRAYS = ("P1", "P2", "Q", "O", "E", "Gi", "Go", "F1", "F2")
EVENTS = (
    "n1", "f", "o", "cv", "n2", "c2", "m", "br", "gs",
    "dx3", "dgh", "dn2", "dc2", "dx1", "dcv", "dn1", "df", "gv", "gad",
)


def mm(a, b):
    return lax.dot_general(a, b, (((1,), (0,)), ((), ())), preferred_element_type=F32)


def mm_nt(a, b):
    return lax.dot_general(a, b, (((1,), (1,)), ((), ())), preferred_element_type=F32)


def mm_tn(a, b):
    return lax.dot_general(a, b, (((0,), (0,)), ((), ())), preferred_element_type=F32)


def flat(value):
    return value.reshape(-1, value.shape[-1])


def low(value):
    return value.astype(BF)


def wide(value):
    return value.astype(F32)


def gelu_pair(h):
    phi = 0.5 * (1.0 + lax.erf(h * 0.7071067811865476))
    dens = jnp.exp(-0.5 * h * h) * 0.3989422804014327
    return h * phi, phi + h * dens


def normed(value):
    centred = value - jnp.mean(value, axis=-1, keepdims=True)
    rs = lax.rsqrt(jnp.mean(centred * centred, axis=-1, keepdims=True) + 1e-06)
    return centred * rs, rs


def norm_back(dn, n_hat, rs, gain):
    gd = dn * gain
    return (
        gd
        - jnp.mean(gd, axis=-1, keepdims=True)
        - n_hat * jnp.mean(gd * n_hat, axis=-1, keepdims=True)
    ) * rs


def col_shift(value, by):
    if by == 0:
        return value
    at = lax.broadcasted_iota(jnp.int32, value.shape, 0) % SIDE
    rolled = pltpu.roll(value, (-by) % TOK, 0)
    return jnp.where((at + by >= 0) & (at + by < SIDE), rolled, 0.0)


def row_shift(value, by):
    if by == 0:
        return value
    gap = jnp.zeros((abs(by) * SIDE, value.shape[1]), value.dtype)
    if by > 0:
        return jnp.concatenate([value[by * SIDE :], gap], axis=0)
    return jnp.concatenate([gap, value[: TOK + by * SIDE]], axis=0)


def depthwise(value, tap, side):
    half = side // 2
    shifted = [col_shift(value, b - half) for b in range(side)]
    total = None
    for a in range(side):
        line = None
        for b in range(side):
            term = shifted[b] * tap(a * side + b)
            line = term if line is None else line + term
        line = row_shift(line, a - half)
        total = line if total is None else total + line
    return total


def depthwise_taps(value, grad, side, put):
    half = side // 2
    shifted = [col_shift(value, b - half) for b in range(side)]
    for a in range(side):
        d = a - half
        lo, hi = max(0, -d) * SIDE, (SIDE - max(0, d)) * SIDE
        for b in range(side):
            part = shifted[b][lo + d * SIDE : hi + d * SIDE] * grad[lo:hi]
            put(a * side + b, jnp.sum(part, axis=0, keepdims=True))


def lanes_of(at, width):
    return pl.ds(pl.multiple_of(at * width, width), width)


def side_by_side(blocks):
    return jnp.concatenate(blocks, axis=1)


def main_kernel(dims, outer, *refs):
    at = iter(refs)

    def take(count):
        return [next(at) for _ in range(count)]

    na = len(ARRAYS)
    source = dict(zip(ARRAYS, take(na)))
    (
        depth_in, ln_conv_in, scale_in, ln_attn_in, ln_mlp_in, adapt_depth_in,
        order_in, train_in, tok_in, grid_in, tcot_in, gcot_in,
    ) = take(12)
    hid_tok, hid_grid, out_gtok, out_ggrid = take(4)
    native = dict(zip(ARRAYS, take(na)))
    out_depth, out_ln_conv, out_scale, out_ln_attn, out_ln_mlp, out_ad = take(6)
    W = dict(zip(ARRAYS, take(na)))
    RX = dict(zip(ARRAYS, take(na)))
    (
        v_loc, vv, aq, vec_c, vec_d, x_in, c_in, n1_all, f_all, n2_all, c2_all,
        o_sb, o_rb, cv_sb, cv_rb, m_sb, m_rb, br_sb, br_rb, gsb, dgb,
        qkv, prob, ctx, u, up, r, rp, cn, crs, cv_sum, x1, c2f,
        adapted, spread, pooled, gate,
        dx3, dcot, dx3_all, dn2_sb, dn2_rb, dc2_sb, dc2_rb, dx1_all, dcv_all,
        dn1_sb, dn1_rb, df_sb, df_rb, dh, do_all, dqkv, dhc, dx1, dc2t, dad, dcn,
        gvs, gv_rb, gvx, gad, gad_rb, gad_all,
    ) = take(64)
    (
        zs_send, zs_recv, s1_send, s1_recv, loc_sem, s2_send, s2_recv,
        v_send, v_recv, q_send, q_recv, h_send, h_recv, b_send, b_recv,
        xo_send, xo_recv, g_send, g_recv, a_send, a_recv, gx_send, gx_recv, go,
    ) = take(24)

    p = lax.axis_index("pipe")
    dpi = lax.axis_index("dp")
    x = lax.axis_index("tensor")
    rest = dpi % outer
    zi = dpi // (outer * R)
    ri = (dpi // outer) % R
    xo = 1 - x
    ro = 1 - ri
    d_dim, c_dim, hq, ffq, cfq, adq, dg = dims
    adh = Z * adq
    dz, cz = d_dim // Z, c_dim // Z
    tile = 256
    ids = {name: number for number, name in enumerate(ARRAYS)}
    ev = {name: number for number, name in enumerate(EVENTS)}

    def dev(z=None, rr=None, xx=None, pp=None):
        z = zi if z is None else z
        rr = ri if rr is None else rr
        return (
            p if pp is None else pp,
            (z * R + rr) * outer + rest,
            x if xx is None else xx,
        )

    def zto(d):
        return lax.rem(zi + d, Z)

    def zfrom(d):
        return lax.rem(zi + Z - d, Z)

    def remote(src, dst, ssem, rsem, device):
        return pltpu.make_async_remote_copy(
            src_ref=src, dst_ref=dst, send_sem=ssem, recv_sem=rsem,
            device_id=device, device_id_type=pl.DeviceIdType.MESH,
        )

    sib = dev(pp=1 - p)
    over_r, over_x = dev(rr=ro), dev(xx=xo)

    def z_copy(e, d, src, dst):
        return remote(src, dst, zs_send.at[e, d - 1], zs_recv.at[e, d - 1], dev(zto(d)))

    sent = []

    def gather_copies(name, buf):
        return [z_copy(ev[name], d, buf.at[zi], buf.at[zi]) for d in range(1, Z)]

    def gather_start(name, buf, keep=True):
        copies = gather_copies(name, buf)
        for c in copies:
            c.start()
        if keep:
            sent.extend(copies)

    def gather_wait(name, buf):
        for d in range(1, Z):
            slot = buf.at[zfrom(d)]
            z_copy(ev[name], d, slot, slot).wait_recv()

    def scatter_start(name, sb, rb):
        for d in range(1, Z):
            c = z_copy(ev[name], d, sb.at[zto(d)], rb.at[d - 1])
            c.start()
            sent.append(c)

    def scatter_wait(name, rb):
        for d in range(1, Z):
            z_copy(ev[name], d, rb.at[d - 1], rb.at[d - 1]).wait_recv()

    def share_start(name, buf):
        for d in range(1, Z):
            c = z_copy(ev[name], d, buf.at[3], buf.at[d - 1])
            c.start()
            sent.append(c)

    def scattered(sb, rb):
        return (wide(sb[zi]) + wide(rb[0])) + (wide(rb[1]) + wide(rb[2]))

    barrier = pltpu.get_barrier_semaphore()
    greeted = [sib]
    for d in range(1, Z):
        greeted += [dev(zto(d)), dev(zto(d), ro)]
    greeted += [over_r, over_x, dev(rr=ro, xx=xo)]
    for device in greeted:
        pl.semaphore_signal(barrier, inc=1, device_id=device, device_id_type=pl.DeviceIdType.MESH)
    v_loc[...] = jnp.zeros(v_loc.shape, F32)
    taps7 = depth_in.shape[0]
    c_own = depth_in.shape[1]
    v_loc[0:taps7, 0:c_own] = wide(depth_in[...])
    v_loc[49:50, 0:c_own] = wide(ln_conv_in[...])
    v_loc[50:51, 0:c_own] = wide(scale_in[...])
    v_loc[56:57, 0:LANE] = wide(ln_attn_in[...])
    v_loc[57:58, 0:LANE] = wide(ln_mlp_in[...])
    aq[x] = jnp.zeros(aq.shape[1:], F32)
    aq[x, 0:9] = wide(adapt_depth_in[:, lanes_of(zi, adq)])
    pl.semaphore_wait(barrier, len(greeted))

    me8 = zi * R + ri
    v_arrivals = []
    for n, (d, flip) in enumerate([(d, s) for d in range(Z) for s in (0, 1)][1:]):
        tr = ro if flip else ri
        c = remote(v_loc, vv.at[me8], v_send.at[n], v_recv.at[n], dev(zto(d), tr))
        c.start()
        sent.append(c)
        fr = zfrom(d) * R + tr
        v_arrivals.append(remote(vv.at[fr], vv.at[fr], v_send.at[n], v_recv.at[n], dev(zto(d), tr)))
    vv[me8] = v_loc[...]
    c = remote(aq.at[x], aq.at[x], q_send, q_recv, over_x)
    c.start()
    sent.append(c)

    by_rows = ("O", "F2")

    def quarter_of(name, ref, z):
        if name == "Q":
            return ref.at[:, :, lanes_of(z, hq)]
        if name in by_rows:
            height = ref.shape[0] // Z
            return ref.at[pl.ds(pl.multiple_of(z * height, height), height)]
        return ref.at[:, lanes_of(z, ref.shape[1] // Z)]

    def step1_local(name):
        return pltpu.make_async_copy(
            quarter_of(name, source[name], zi), W[name].at[x, zi, ri], loc_sem.at[ids[name]]
        )

    def step1_copy(name, d):
        k = ids[name]
        return remote(
            quarter_of(name, source[name], zto(d)), W[name].at[x, zi, ri],
            s1_send.at[k, d - 1], s1_recv.at[k, d - 1], dev(zto(d)),
        )

    def step1(name):
        step1_local(name).start()
        for d in range(1, Z):
            step1_copy(name, d).start()

    def half_of(name, j, rr, upper):
        w = W[name]
        half = w.shape[-2] // 2
        rows = slice(half, None) if upper else slice(0, half)
        if len(w.shape) == 6:
            return w.at[j, :, rr, :, rows]
        return w.at[j, :, rr, rows]

    def step2_copy(name, which):
        k = ids[name]
        ref = (
            lambda: W[name].at[x, :, ri],
            lambda: W[name].at[x, :, ri],
            lambda: half_of(name, x, ro, False),
            lambda: half_of(name, xo, ri, True),
        )[which]()
        return remote(ref, ref, s2_send.at[k, which], s2_recv.at[k, which], over_x if which in (1, 2) else over_r)

    def step2_arrival(name, which):
        k = ids[name]
        ref = (
            lambda: W[name].at[x, :, ro],
            lambda: W[name].at[xo, :, ri],
            lambda: half_of(name, xo, ro, False),
            lambda: half_of(name, xo, ro, True),
        )[which]()
        return remote(ref, ref, s2_send.at[k, which], s2_recv.at[k, which], over_x if which in (1, 2) else over_r)

    def relay1(*names):
        for name in names:
            k = ids[name]
            step1_local(name).wait()
            for d in range(1, Z):
                slot = W[name].at[x, zfrom(d), ri]
                remote(slot, slot, s1_send.at[k, d - 1], s1_recv.at[k, d - 1], dev(zto(d))).wait_recv()
            step2_copy(name, 0).start()
            step2_copy(name, 1).start()

    def relay2(*names):
        for name in names:
            step2_arrival(name, 0).wait_recv()
            step2_copy(name, 2).start()
            step2_arrival(name, 1).wait_recv()
            step2_copy(name, 3).start()

    def relay3(*names):
        for name in names:
            step2_arrival(name, 2).wait_recv()
            step2_arrival(name, 3).wait_recv()

    def relay_sent():
        for name in ARRAYS:
            for d in range(1, Z):
                step1_copy(name, d).wait_send()
            for which in range(4):
                step2_copy(name, which).wait_send()

    @pl.when(p == 1)
    def _():
        pl.semaphore_wait(go, 1)

    step1("P1")
    step1("P2")

    for c in v_arrivals:
        c.wait_recv()
    remote(aq.at[xo], aq.at[xo], q_send, q_recv, over_x).wait_recv()
    low_lanes = lax.broadcasted_iota(jnp.int32, (64, LANE), 1) < LANE // 2
    for z in range(Z):
        first, second = vv[2 * z], pltpu.roll(vv[2 * z + 1], LANE // 2, 1)
        vec_c[:, z * cz : z * cz + LANE] = first[:, 0:LANE]
        vec_c[:, z * cz + LANE : z * cz + 2 * LANE] = jnp.where(
            low_lanes, first[:, LANE:], second[:, 0:LANE]
        )
        vec_c[:, z * cz + 2 * LANE : (z + 1) * cz] = second[:, LANE:]
    for i in range(Z * R):
        vec_d[:, i * LANE : (i + 1) * LANE] = vv[i, 56:64, 0:LANE]

    def gain_d(row):
        return vec_d[row : row + 1, :]

    def gain_c(row):
        return vec_c[row : row + 1, :]

    def token_entry():
        n_hat, _ = normed(wide(x_in[...]))
        n1_all[zi] = low(n_hat * gain_d(0))
        gather_start("n1", n1_all, keep=False)

    sent.extend(gather_copies("n1", n1_all))

    @pl.when(p == 0)
    def _():
        first = order_in[0, x] == 0
        c_in[...] = jnp.where(first, grid_in[0], grid_in[1])
        x_in[...] = jnp.where(first, tok_in[0], tok_in[1])
        token_entry()

    @pl.when(p == 1)
    def _():
        remote(c_in, c_in, h_send.at[1], h_recv.at[1], sib).wait_recv()

    @pl.loop(0, c_dim // LANE)
    def _(ch):
        lanes = lanes_of(ch, LANE)
        taps = vec_c[:, lanes]
        cn[:, lanes] = depthwise(wide(c_in[:, lanes]), lambda k: taps[k : k + 1], 7)

    n_hat, rs = normed(cn[...])
    cn[...] = n_hat
    crs[...] = jnp.broadcast_to(rs, crs.shape)
    f_all[zi] = low(n_hat * gain_c(49))
    gather_start("f", f_all)

    relay1("P1")
    step1("Q")
    step1("O")
    relay1("P2")
    step1("E")
    step1("Gi")
    step1("Go")
    relay2("P1")
    relay1("Q", "O")
    step1("F1")
    relay2("P2")
    relay3("P1")
    gather_wait("f", f_all)
    for j in range(2):

        @pl.loop(0, cfq // tile)
        def _(t):
            lanes = lanes_of(t, tile)
            act, der = gelu_pair(mm(flat(f_all[...]), flat(W["P1"][j, :, :, :, lanes])))
            r[j, :, lanes] = low(act)
            rp[j, :, lanes] = low(der)

    relay1("E", "Gi", "Go")
    step1("F2")
    relay2("Q", "O")
    relay3("P2")

    @pl.loop(0, Z)
    def _(z):
        acc = mm_nt(r[0], flat(W["P2"][0, z])) + mm_nt(r[1], flat(W["P2"][1, z]))
        cv_sb[:, :, lanes_of(z, cz)] = low(acc).reshape(Z, TOK, cz)

    scatter_start("cv", cv_sb, cv_rb)

    relay1("F1")
    relay2("E", "Gi", "Go")

    @pl.when(p == 1)
    def _():
        remote(x_in, x_in, h_send.at[0], h_recv.at[0], sib).wait_recv()
        token_entry()

    relay3("Q", "O")
    gather_wait("n1", n1_all)
    for j in range(2):
        wj = side_by_side([flat(W["Q"][j, :, :, s]) for s in range(3)])
        qkv[j] = low(mm(flat(n1_all[...]), wj))
    for j in range(2):

        @pl.loop(0, Z)
        def _(b):
            rows = lanes_of(b, TOK)
            outs = []
            for h in range(hq // HD):
                q, kk, vals = (qkv[j, rows, s * hq + h * HD : s * hq + (h + 1) * HD] for s in range(3))
                sc = mm_nt(q, kk) * HD ** (-0.5)
                e = jnp.exp(sc - jnp.max(sc, axis=-1, keepdims=True))
                pr = low(e / jnp.sum(e, axis=-1, keepdims=True))
                prob[j, h, b] = pr
                outs.append(mm(pr, vals))
            ctx[j, rows, :] = low(side_by_side(outs))

    def out_block(j, z):
        return side_by_side([W["O"][j, z, 0], W["O"][j, z, 1]])

    @pl.loop(0, Z)
    def _(z):
        both = jnp.concatenate([out_block(0, z), out_block(1, z)], axis=0)
        acc = mm(side_by_side([ctx[0], ctx[1]]), both)
        o_sb[:, :, lanes_of(z, dz)] = low(acc).reshape(Z, TOK, dz)

    scatter_start("o", o_sb, o_rb)
    relay1("F2")
    relay2("F1")

    scatter_wait("cv", cv_rb)
    cv_sum[...] = scattered(cv_sb, cv_rb)
    c2f[...] = wide(c_in[...]) + gain_c(50) * cv_sum[...]
    c2_low = low(c2f[...])
    c2_all[zi] = c2_low
    gather_start("c2", c2_all)
    hid_grid[x] = c2_low

    @pl.when(p == 0)
    def _():
        remote(hid_grid.at[x], c_in, h_send.at[1], h_recv.at[1], sib).start()

    relay3("E", "Gi", "Go")
    scatter_wait("o", o_rb)
    x1[...] = wide(x_in[...]) + scattered(o_sb, o_rb)
    n_hat, _ = normed(x1[...])
    n2_all[zi] = low(n_hat * gain_d(1))
    gather_start("n2", n2_all)
    relay2("F2")

    @pl.when(p == 0)
    def _():
        pl.semaphore_signal(go, inc=1, device_id=sib, device_id_type=pl.DeviceIdType.MESH)

    gather_wait("c2", c2_all)
    row8 = lax.broadcasted_iota(jnp.int32, (8, adq), 0)
    gs_part = None
    for j in range(2):
        ad = mm(flat(c2_all[...]), flat(W["E"][j]))
        adapted[j] = ad
        taps = aq[j]
        pool = jnp.zeros((8, adq), F32)
        for b in range(Z):
            sp = depthwise(ad[b * TOK : (b + 1) * TOK], lambda k: taps[k : k + 1], 3)
            spread[j, b] = sp
            pool = jnp.where(row8 == b, jnp.mean(sp, axis=0, keepdims=True), pool)
        pooled[j] = pool
        term = mm_nt(low(pool), flat(W["Gi"][j]))
        gs_part = term if gs_part is None else gs_part + term
    gsb[3] = gs_part
    share_start("gs", gsb)

    relay3("F1")
    gather_wait("n2", n2_all)
    for j in range(2):

        @pl.loop(0, ffq // tile)
        def _(t):
            lanes = lanes_of(t, tile)
            act, der = gelu_pair(mm(flat(n2_all[...]), flat(W["F1"][j, :, :, :, lanes])))
            u[j, :, lanes] = low(act)
            up[j, :, lanes] = low(der)

    scatter_wait("gs", gsb)

    def gate_hidden():
        return gelu_pair((gsb[0] + gsb[1]) + (gsb[2] + gsb[3]))

    gh, _ = gate_hidden()
    for j in range(2):
        g8 = jnp.tanh(mm(low(gh), flat(W["Go"][j])))
        gate[j] = g8
        for b in range(Z):
            br_sb[b, :, j * adq : (j + 1) * adq] = low(g8[b : b + 1] * spread[j, b])
    scatter_start("br", br_sb, br_rb)
    relay3("F2")

    @pl.loop(0, Z)
    def _(z):
        acc = None
        for j in range(2):
            term = mm(u[j], side_by_side([W["F2"][j, z, 0], W["F2"][j, z, 1]]))
            acc = term if acc is None else acc + term
        m_sb[:, :, lanes_of(z, dz)] = low(acc).reshape(Z, TOK, dz)

    scatter_start("m", m_sb, m_rb)
    scatter_wait("br", br_rb)
    dx1[...] = x1[...]
    for d in range(Z):
        piece = br_sb[zi] if d == 0 else br_rb[d - 1]
        for j in range(2):
            lanes = pl.ds(pl.multiple_of(j * adh + zfrom(d) * adq, LANE), adq)
            dx1[:, lanes] += wide(piece[:, j * adq : (j + 1) * adq])
    scatter_wait("m", m_rb)
    hid_tok[x] = low(dx1[...] + scattered(m_sb, m_rb))

    @pl.when(p == 0)
    def _():
        remote(hid_tok.at[x], x_in, h_send.at[0], h_recv.at[0], sib).start()

    out_arrivals = []

    def exchange(n, buf):
        c = remote(buf.at[x], buf.at[x], xo_send.at[n], xo_recv.at[n], over_x)
        c.start()
        sent.append(c)
        out_arrivals.append(remote(buf.at[xo], buf.at[xo], xo_send.at[n], xo_recv.at[n], over_x))

    exchange(0, hid_tok)
    exchange(1, hid_grid)
    relay_sent()

    @pl.when(p == 1)
    def _():
        dx3[...] = tcot_in[x]
        dcot[...] = gcot_in[x]

    @pl.when(p == 0)
    def _():
        remote(dx3, dx3, b_send.at[0], b_recv.at[0], sib).wait_recv()

    dx3_all[zi] = dx3[...]
    gather_start("dx3", dx3_all)
    gather_wait("dx3", dx3_all)

    def own_lanes(j):
        return pl.ds(pl.multiple_of(j * adh + zi * adq, LANE), adq)

    gh, ghp = gate_hidden()
    dgh_part = None
    dgp = []
    for j in range(2):
        dgate = jnp.zeros((8, adq), F32)
        for b in range(Z):
            dbr = wide(dx3_all[b, :, own_lanes(j)])
            dgate = jnp.where(row8 == b, jnp.sum(dbr * spread[j, b], axis=0, keepdims=True), dgate)
        dg8 = low(dgate * (1.0 - gate[j] * gate[j]))
        dgp.append(dg8)
        term = mm_nt(dg8, flat(W["Go"][j]))
        dgh_part = term if dgh_part is None else dgh_part + term
    dgb[3] = dgh_part
    share_start("dgh", dgb)

    for j in range(2):

        @pl.loop(0, ffq // tile)
        def _(t):
            rows = lanes_of(t, tile)
            both = side_by_side([W["F2"][j, z, rr, rows] for z in range(Z) for rr in range(R)])
            du = mm_nt(flat(dx3_all[...]), both)
            dh[j, :, rows] = low(du * wide(up[j, :, rows]))

    scatter_wait("dgh", dgb)
    dgs = low(((dgb[0] + dgb[1]) + (dgb[2] + dgb[3])) * ghp)
    for j in range(2):
        dpool = mm(dgs, flat(W["Gi"][j])) * (1.0 / TOK)
        taps = aq[j]
        tap_rows = [None] * 9
        for b in range(Z):
            dsp = gate[j, b : b + 1] * wide(dx3_all[b, :, own_lanes(j)]) + dpool[b : b + 1]
            dad[j, b * TOK : (b + 1) * TOK] = low(depthwise(dsp, lambda k: taps[8 - k : 9 - k], 3))

            def put(k, row):
                tap_rows[k] = row if tap_rows[k] is None else tap_rows[k] + row

            depthwise_taps(adapted[j, b * TOK : (b + 1) * TOK], dsp, 3, put)
        for k in range(9):
            gad[j, k : k + 1] = tap_rows[k]
        gad[j, 9:16] = jnp.zeros((7, adq), F32)

    @pl.loop(0, Z)
    def _(z):
        acc = mm_nt(dad[0], flat(W["E"][0, z])) + mm_nt(dad[1], flat(W["E"][1, z]))
        dc2_sb[:, :, lanes_of(z, cz)] = low(acc).reshape(Z, TOK, cz)

    scatter_start("dc2", dc2_sb, dc2_rb)

    @pl.loop(0, Z)
    def _(z):
        acc = mm_nt(dh[0], flat(W["F1"][0, z])) + mm_nt(dh[1], flat(W["F1"][1, z]))
        dn2_sb[:, :, lanes_of(z, dz)] = low(acc).reshape(Z, TOK, dz)

    scatter_start("dn2", dn2_sb, dn2_rb)

    peers = ((1, 0), (0, 1), (1, 1))

    def owner(k):
        return (ro if peers[k][0] else ri), (xo if peers[k][1] else x)

    def reduce_copy(name, k):
        rr, xx = owner(k)
        n = ids[name]
        return remote(W[name].at[xx, :, rr], RX[name].at[k], g_send.at[n, k], g_recv.at[n, k], dev(rr=rr, xx=xx))

    def reduce_start(name):
        for k in (2, 0, 1):
            reduce_copy(name, k).start()

    def row_grad(name, left, right):
        width = W[name].shape[3]

        @pl.loop(0, Z)
        def _(z):
            lhs = flat(left[:, :, lanes_of(z, R * width)])
            for j in range(2):
                W[name][j, z] = low(mm_tn(lhs, right[j])).reshape(R, width, -1)

        reduce_start(name)

    def col_grad(name, left, right):
        @pl.loop(0, Z)
        def _(z):
            rhs = flat(right[:, :, lanes_of(z, dz)])
            for j in range(2):
                g = low(mm_tn(left[j], rhs))
                for rr in range(R):
                    W[name][j, z, rr] = g[:, rr * LANE : (rr + 1) * LANE]

        reduce_start(name)

    for j in range(2):
        W["Gi"][j] = low(mm_tn(dgs, low(pooled[j]))).reshape(Z, R, -1, adq)
        W["Go"][j] = low(mm_tn(low(gh), dgp[j])).reshape(Z, R, -1, adq)
    reduce_start("Gi")
    reduce_start("Go")
    row_grad("E", c2_all, dad)

    @pl.when(p == 0)
    def _():
        remote(dcot, dcot, b_send.at[1], b_recv.at[1], sib).wait_recv()

    scatter_wait("dc2", dc2_rb)
    dc2t[...] = wide(dcot[...]) + scattered(dc2_sb, dc2_rb)
    gvs_ls = jnp.sum(cv_sum[...] * dc2t[...], axis=0, keepdims=True)
    dcv_all[zi] = low(dc2t[...] * gain_c(50))
    gather_start("dcv", dcv_all)

    scatter_wait("dn2", dn2_rb)
    dn2 = scattered(dn2_sb, dn2_rb)
    n_hat, rs = normed(x1[...])
    gvs_d1 = jnp.sum(dn2 * n_hat, axis=0, keepdims=True)
    dx1[...] = wide(dx3[...]) + norm_back(dn2, n_hat, rs, gain_d(1))
    dx1_all[zi] = low(dx1[...])
    gather_start("dx1", dx1_all)

    col_grad("F2", u, dx3_all)
    row_grad("F1", n2_all, dh)

    gather_wait("dcv", dcv_all)
    for j in range(2):

        @pl.loop(0, cfq // tile)
        def _(t):
            lanes = lanes_of(t, tile)
            dr = mm(flat(dcv_all[...]), flat(W["P2"][j, :, :, :, lanes]))
            dhc[j, :, lanes] = low(dr * wide(rp[j, :, lanes]))

    @pl.loop(0, Z)
    def _(z):
        acc = mm_nt(dhc[0], flat(W["P1"][0, z])) + mm_nt(dhc[1], flat(W["P1"][1, z]))
        df_sb[:, :, lanes_of(z, cz)] = low(acc).reshape(Z, TOK, cz)

    scatter_start("df", df_sb, df_rb)

    gather_wait("dx1", dx1_all)
    for j in range(2):
        both = side_by_side([W["O"][j, z, rr] for z in range(Z) for rr in range(R)])
        do_all[j] = low(mm_nt(flat(dx1_all[...]), both))
    for j in range(2):

        @pl.loop(0, Z)
        def _(b):
            rows = lanes_of(b, TOK)
            parts = [[], [], []]
            for h in range(hq // HD):
                q, kk, vals = (qkv[j, rows, s * hq + h * HD : s * hq + (h + 1) * HD] for s in range(3))
                do = do_all[j, rows, h * HD : (h + 1) * HD]
                pr = prob[j, h, b]
                dp = mm_nt(do, vals)
                prw = wide(pr)
                ds = low(prw * (dp - jnp.sum(dp * prw, axis=-1, keepdims=True)) * HD ** (-0.5))
                parts[0].append(mm(ds, kk))
                parts[1].append(mm_tn(ds, q))
                parts[2].append(mm_tn(pr, do))
            for s in range(3):
                dqkv[j, rows, s * hq : (s + 1) * hq] = low(side_by_side(parts[s]))

    @pl.loop(0, Z)
    def _(z):
        acc = None
        for j in range(2):
            term = mm_nt(dqkv[j], side_by_side([flat(W["Q"][j, z, :, s]) for s in range(3)]))
            acc = term if acc is None else acc + term
        dn1_sb[:, :, lanes_of(z, dz)] = low(acc).reshape(Z, TOK, dz)

    scatter_start("dn1", dn1_sb, dn1_rb)

    def pw_grads():
        row_grad("P2", dcv_all, r)
        row_grad("P1", f_all, dhc)

    @pl.when(p == 0)
    def _():
        pw_grads()

    scatter_wait("dn1", dn1_rb)
    dn1 = scattered(dn1_sb, dn1_rb)
    n_hat, rs = normed(wide(x_in[...]))
    gvs_d0 = jnp.sum(dn1 * n_hat, axis=0, keepdims=True)
    out_gtok[x] = low(dx1[...] + norm_back(dn1, n_hat, rs, gain_d(0)))

    @pl.when(p == 1)
    def _():
        remote(out_gtok.at[x], dx3, b_send.at[0], b_recv.at[0], sib).start()

    scatter_wait("df", df_rb)
    dfv = scattered(df_sb, df_rb)
    gvs_lc = jnp.sum(dfv * cn[...], axis=0, keepdims=True)
    dcn[...] = norm_back(dfv, cn[...], crs[:, 0:1], gain_c(49))

    @pl.loop(0, c_dim // LANE)
    def _(ch):
        lanes = lanes_of(ch, LANE)
        taps = vec_c[:, lanes]
        back = depthwise(dcn[:, lanes], lambda k: taps[48 - k : 49 - k], 7)
        out_ggrid[x, :, lanes] = low(dc2t[:, lanes] + back)

    @pl.when(p == 1)
    def _():
        remote(out_ggrid.at[x], dcot, b_send.at[1], b_recv.at[1], sib).start()
        pw_grads()

    @pl.loop(0, Z)
    def _(z):
        lhs = flat(n1_all[:, :, lanes_of(z, dz)])
        for j in range(2):
            g = low(mm_tn(lhs, dqkv[j]))
            for s in range(3):
                W["Q"][j, z, :, s] = g[:, s * hq : (s + 1) * hq].reshape(R, -1, hq)

    reduce_start("Q")
    col_grad("O", ctx, dx1_all)

    exchange(2, out_gtok)
    exchange(3, out_ggrid)

    @pl.loop(0, Z)
    def _(z):
        for part in range(cz // LANE):
            lanes = pl.ds(pl.multiple_of(z * cz + part * LANE, LANE), LANE)

            def put(k, row):
                gvs[z, k : k + 1, part * LANE : (part + 1) * LANE] = row

            depthwise_taps(wide(c_in[:, lanes]), dcn[:, lanes], 7, put)

    for z in range(Z):
        gvs[z, 49:50] = gvs_lc[:, z * cz : (z + 1) * cz]
        gvs[z, 50:51] = gvs_ls[:, z * cz : (z + 1) * cz]
        gvs[z, 51:64] = jnp.zeros((13, cz), F32)
        gvs[z, 56:57, 0:dz] = gvs_d0[:, z * dz : (z + 1) * dz]
        gvs[z, 57:58, 0:dz] = gvs_d1[:, z * dz : (z + 1) * dz]
    scatter_start("gv", gvs, gv_rb)

    def group_copy(n, k, src, dst):
        rr, xx = owner(k)
        return remote(src, dst, gx_send.at[n, k], gx_recv.at[n, k], dev(rr=rr, xx=xx))

    for k in range(3):
        c = group_copy(1, k, gad, gad_rb.at[k])
        c.start()
        sent.append(c)
    scatter_wait("gv", gv_rb)
    gvx[3] = (gvs[zi] + gv_rb[0]) + (gv_rb[1] + gv_rb[2])
    for k in range(3):
        c = group_copy(0, k, gvx.at[3], gvx.at[k])
        c.start()
        sent.append(c)
    for k in range(3):
        group_copy(1, k, gad, gad_rb.at[k]).wait_recv()
    gad_all[zi] = (gad[x] + gad_rb[0, x]) + (gad_rb[1, x] + gad_rb[2, x])
    gather_start("gad", gad_all)

    def back_copy(name, d):
        n = ids[name]
        return remote(
            RX[name].at[0, zto(d)], quarter_of(name, native[name], zi),
            a_send.at[n, d - 1], a_recv.at[n, d - 1], dev(zto(d)),
        )

    def back_local(name):
        return pltpu.make_async_copy(
            RX[name].at[0, zi], quarter_of(name, native[name], zi), loc_sem.at[ids[name]]
        )

    for name in ("Gi", "Go", "E", "F2", "F1", "P2", "P1", "Q", "O"):
        n = ids[name]
        rx = RX[name]
        for k in range(3):
            reduce_copy(name, k).wait_recv()

        @pl.loop(0, Z)
        def _(z):
            total = (wide(W[name][x, z, ri]) + wide(rx[0, z])) + (wide(rx[1, z]) + wide(rx[2, z]))
            rx[0, z] = low(total)

        for d in range(1, Z):
            back_copy(name, d).start()
        back_local(name).start()

    for k in range(3):
        group_copy(0, k, gvx.at[k], gvx.at[k]).wait_recv()
    total = (gvx[0] + gvx[1]) + (gvx[2] + gvx[3])
    mine = jnp.where(ri == 1, pltpu.roll(total, c_own, 1), total)[:, 0:c_own]
    mine_d = jnp.where(ri == 1, total[:, LANE : 2 * LANE], total[:, 0:LANE])

    def flag(n):
        return train_in[0, n].astype(F32)

    out_depth[...] = mine[0:taps7] * flag(0)
    out_ln_conv[...] = mine[49:50] * flag(1)
    out_scale[...] = mine[50:51] * flag(4)
    out_ln_attn[...] = mine_d[56:57]
    out_ln_mlp[...] = mine_d[57:58]
    gather_wait("gad", gad_all)
    for z in range(Z):
        out_ad[:, z * adq : (z + 1) * adq] = gad_all[z][0:9]
    for name in ARRAYS:
        back_local(name).wait()
        for d in range(1, Z):
            n = ids[name]
            slot = quarter_of(name, native[name], zfrom(d))
            remote(slot, slot, a_send.at[n, d - 1], a_recv.at[n, d - 1], dev(zto(d))).wait_recv()
    for c in out_arrivals:
        c.wait_recv()

    @pl.when(p == 0)
    def _():
        remote(hid_tok.at[x], x_in, h_send.at[0], h_recv.at[0], sib).wait_send()
        remote(hid_grid.at[x], c_in, h_send.at[1], h_recv.at[1], sib).wait_send()

    @pl.when(p == 1)
    def _():
        remote(out_gtok.at[x], dx3, b_send.at[0], b_recv.at[0], sib).wait_send()
        remote(out_ggrid.at[x], dcot, b_send.at[1], b_recv.at[1], sib).wait_send()

    for c in sent:
        c.wait_send()
    for name in ARRAYS:
        for k in range(3):
            reduce_copy(name, k).wait_send()
        for d in range(1, Z):
            back_copy(name, d).wait_send()


def run_layers(weights, vectors, order, train, streams, sizes, outer):
    d_dim, c_dim, hq, ffq, cfq, adw, dg = sizes
    vm = pltpu.VMEM
    blocks = []
    for name, value in zip(ARRAYS, weights):
        if name == "Q":
            blocks.append((3, value.shape[1], hq))
        elif name in ("O", "F2"):
            blocks.append((value.shape[0] // Z, value.shape[1]))
        else:
            blocks.append((value.shape[0], value.shape[1] // Z))
    rows = Z * TOK

    def act(width, count=Z, kind=BF):
        return vm((count, TOK, width), kind)

    scratch = [vm((2, Z, R) + s, BF) for s in blocks] + [vm((3, Z) + s, BF) for s in blocks]
    scratch += [
        vm((64, 2 * LANE), F32), vm((Z * R, 64, 2 * LANE), F32), vm((2, 16, adw), F32), vm((64, c_dim), F32), vm((8, d_dim), F32),
        vm((TOK, d_dim), BF), vm((TOK, c_dim), BF), act(d_dim), act(c_dim), act(d_dim), act(c_dim),
        act(d_dim), act(d_dim, 3), act(c_dim), act(c_dim, 3), act(d_dim), act(d_dim, 3),
        act(2 * adw), act(2 * adw, 3), vm((4, 8, dg), F32), vm((4, 8, dg), F32),
        vm((2, rows, 3 * hq), BF), vm((2, hq // HD, Z, TOK, TOK), BF), vm((2, rows, hq), BF),
        vm((2, rows, ffq), BF), vm((2, rows, ffq), BF), vm((2, rows, cfq), BF), vm((2, rows, cfq), BF),
        vm((TOK, c_dim), F32), vm((TOK, LANE), F32), vm((TOK, c_dim), F32), vm((TOK, d_dim), F32), vm((TOK, c_dim), F32),
        vm((2, rows, adw), F32), vm((2, Z, TOK, adw), F32), vm((2, 8, adw), F32), vm((2, 8, adw), F32),
        vm((TOK, d_dim), BF), vm((TOK, c_dim), BF), act(d_dim), act(d_dim), act(d_dim, 3), act(c_dim), act(c_dim, 3),
        act(d_dim), act(c_dim),
        act(d_dim), act(d_dim, 3), act(c_dim), act(c_dim, 3), vm((2, rows, ffq), BF), vm((2, rows, hq), BF),
        vm((2, rows, 3 * hq), BF), vm((2, rows, cfq), BF), vm((TOK, d_dim), F32), vm((TOK, c_dim), F32), vm((2, rows, adw), BF),
        vm((TOK, c_dim), F32),
        vm((Z, 64, c_dim // Z), F32), vm((3, 64, c_dim // Z), F32), vm((4, 64, c_dim // Z), F32),
        vm((2, 16, adw), F32), vm((3, 2, 16, adw), F32), vm((Z, 16, adw), F32),
    ]
    dma = pltpu.SemaphoreType.DMA
    na = len(ARRAYS)
    scratch += [
        dma((len(EVENTS), 3)), dma((len(EVENTS), 3)), dma((na, 3)), dma((na, 3)), dma((na,)),
        dma((na, 4)), dma((na, 4)), dma((7,)), dma((7,)), dma, dma, dma((2,)), dma((2,)), dma((2,)), dma((2,)),
        dma((4,)), dma((4,)), dma((na, 3)), dma((na, 3)), dma((na, 3)), dma((na, 3)), dma((2, 3)), dma((2, 3)),
        pltpu.SemaphoreType.REGULAR,
    ]
    sds = jax.ShapeDtypeStruct
    out_shape = [sds((2, TOK, d_dim), BF), sds((2, TOK, c_dim), BF)] * 2
    out_shape += [sds(value.shape, BF) for value in weights]
    out_shape += [sds(value.shape, F32) for value in vectors]
    any_spec = pl.BlockSpec(memory_space=pl.ANY)
    vm_spec = pl.BlockSpec(memory_space=pltpu.VMEM)
    sm_spec = pl.BlockSpec(memory_space=pltpu.SMEM)
    return pl.pallas_call(
        functools.partial(main_kernel, sizes, outer),
        out_shape=out_shape,
        in_specs=[any_spec] * na + [vm_spec] * 6 + [sm_spec] * 2 + [vm_spec] * 4,
        out_specs=[vm_spec] * 4 + [any_spec] * na + [vm_spec] * 6,
        scratch_shapes=scratch,
        compiler_params=pltpu.CompilerParams(
            collective_id=0, has_side_effects=True, vmem_limit_bytes=62 * 1024 * 1024
        ),
        cost_estimate=pl.CostEstimate(flops=26 * 10**9, bytes_accessed=10**8, transcendentals=10**7),
        name="layers",
    )(*weights, *vectors, order, train, *streams)


def per_device(
    tokens,
    conv_grid,
    order,
    trainable,
    ln_attn,
    w_qkv,
    w_attn_out,
    ln_mlp,
    w_fc_in,
    w_fc_out,
    conv_depth,
    ln_conv,
    w_pw_in,
    w_pw_out,
    layer_scale,
    w_adapt,
    adapt_depth,
    w_gate_in,
    w_gate_out,
    tok_cot,
    grid_cot,
):
    dp_count = lax.axis_size("dp")
    outer = dp_count // (Z * R)
    groups = [[g * outer + o for o in range(outer)] for g in range(Z * R)]
    layer_at = lax.axis_index("pipe")

    def block(value, axis):
        value = value[0]
        if outer == 1:
            return value
        return lax.all_gather(value, "dp", axis=axis, tiled=True, axis_index_groups=groups)

    def share(value, axis):
        if outer > 1:
            value = lax.psum_scatter(
                value, "dp", scatter_dimension=axis, tiled=True, axis_index_groups=groups
            )
        return value[None]

    qkv = block(w_qkv, 1)
    gate_in = block(w_gate_in, 1).T
    pw_in = block(w_pw_in, 0)
    adapt = block(w_adapt, 0)
    fc_in = block(w_fc_in, 0)
    weights = (
        pw_in,
        block(w_pw_out, 1).T,
        qkv,
        block(w_attn_out, 1),
        adapt,
        gate_in,
        block(w_gate_out, 0),
        fc_in,
        block(w_fc_out, 1),
    )
    vectors = (
        block(conv_depth, 1),
        block(ln_conv, 0)[None],
        block(layer_scale, 0)[None],
        block(ln_attn, 0)[None],
        block(ln_mlp, 0)[None],
        adapt_depth[0],
    )
    spread = Z * R
    sizes = (
        qkv.shape[1] * spread, pw_in.shape[0] * spread, qkv.shape[2] // Z, fc_in.shape[1] // Z,
        pw_in.shape[1] // Z, adapt.shape[1] // Z, gate_in.shape[0] * spread,
    )

    def rows_of(value):
        return value.reshape(value.shape[0], TOK, value.shape[-1])

    streams = [rows_of(value) for value in (tokens, conv_grid, tok_cot, grid_cot)]
    outs = run_layers(weights, vectors, order, trainable, streams, sizes, outer)
    hid_tok, hid_grid, g_tok, g_grid = outs[:4]
    g_p1, g_p2, g_q, g_o, g_e, g_gi, g_go, g_f1, g_f2 = [value.astype(F32) for value in outs[4:13]]
    g_depth, g_ln_conv, g_scale, g_ln_attn, g_ln_mlp, g_ad = outs[13:]

    swap = (layer_at == 0) & (order[0, 0] == 1)
    g_tok = jnp.where(swap, g_tok[::-1], g_tok)
    g_grid = jnp.where(swap, g_grid[::-1], g_grid)
    grid_shape = (1,) + conv_grid.shape
    tok_shape = (1,) + tokens.shape
    flags = trainable[0].astype(F32)
    if outer > 1:
        g_ad = lax.psum(g_ad, "dp", axis_index_groups=groups)
    return (
        hid_tok.reshape(tok_shape),
        hid_grid.reshape(grid_shape),
        g_tok.reshape(tok_shape),
        g_grid.reshape(grid_shape),
        share(g_ln_attn[0], 0),
        share(g_q, 1),
        share(g_o, 1),
        share(g_ln_mlp[0], 0),
        share(g_f1, 0),
        share(g_f2, 1),
        share(g_depth, 1),
        share(g_ln_conv[0], 0),
        share(g_p1 * flags[2], 0),
        share((g_p2 * flags[3]).T, 1),
        share(g_scale[0], 0),
        share(g_e, 0),
        g_ad[None],
        share(g_gi.T, 1),
        share(g_go, 0),
    )


def solution(mesh):
    in_specs = (
        P(None, "dp", None, None),
        P(None, "dp", None, None, None),
        P("dp", None),
        P("pipe", None),
        P("pipe", "dp"),
        P("pipe", None, "dp", "tensor"),
        P("pipe", "tensor", "dp"),
        P("pipe", "dp"),
        P("pipe", "dp", "tensor"),
        P("pipe", "tensor", "dp"),
        P("pipe", None, "dp"),
        P("pipe", "dp"),
        P("pipe", "dp", "tensor"),
        P("pipe", "tensor", "dp"),
        P("pipe", "dp"),
        P("pipe", "dp", "tensor"),
        P("pipe", None, "tensor"),
        P("pipe", "tensor", "dp"),
        P("pipe", "dp", "tensor"),
        P(None, "dp", None, None),
        P(None, "dp", None, None, None),
    )
    out_specs = (
        P("pipe", None, "dp", None, None),
        P("pipe", None, "dp", None, None, None),
        P("pipe", None, "dp", None, None),
        P("pipe", None, "dp", None, None, None),
        P("pipe", "dp"),
        P("pipe", None, "dp", "tensor"),
        P("pipe", "tensor", "dp"),
        P("pipe", "dp"),
        P("pipe", "dp", "tensor"),
        P("pipe", "tensor", "dp"),
        P("pipe", None, "dp"),
        P("pipe", "dp"),
        P("pipe", "dp", "tensor"),
        P("pipe", "tensor", "dp"),
        P("pipe", "dp"),
        P("pipe", "dp", "tensor"),
        P("pipe", None, "tensor"),
        P("pipe", "tensor", "dp"),
        P("pipe", "dp", "tensor"),
    )
    return jax.shard_map(
        per_device, mesh=mesh, in_specs=in_specs, out_specs=out_specs, check_vma=False
    )
```

```python
import functools

import jax
import jax.numpy as jnp
from jax import lax
from jax.experimental import pallas as pl
from jax.experimental.pallas import tpu as pltpu
from jax.sharding import PartitionSpec as P

HD = 64
Z = 4
R = 2
TOK = 64
SIDE = 8
LANE = 128
BF = jnp.bfloat16
F32 = jnp.float32
ARRAYS = ("P1", "P2", "Q", "O", "E", "Gi", "Go", "F1", "F2")
EVENTS = (
    "n1", "f", "o", "cv", "n2", "c2", "m", "br", "gs",
    "dx3", "dgh", "dn2", "dc2", "dx1", "dcv", "dn1", "df", "gv", "gad",
)


def mm(a, b):
    return lax.dot_general(a, b, (((1,), (0,)), ((), ())), preferred_element_type=F32)


def mm_nt(a, b):
    return lax.dot_general(a, b, (((1,), (1,)), ((), ())), preferred_element_type=F32)


def mm_tn(a, b):
    return lax.dot_general(a, b, (((0,), (0,)), ((), ())), preferred_element_type=F32)


def flat(value):
    return value.reshape(-1, value.shape[-1])


def low(value):
    return value.astype(BF)


def wide(value):
    return value.astype(F32)


def gelu_pair(h):
    phi = 0.5 * (1.0 + lax.erf(h * 0.7071067811865476))
    dens = jnp.exp(-0.5 * h * h) * 0.3989422804014327
    return h * phi, phi + h * dens


def normed(value):
    centred = value - jnp.mean(value, axis=-1, keepdims=True)
    rs = lax.rsqrt(jnp.mean(centred * centred, axis=-1, keepdims=True) + 1e-06)
    return centred * rs, rs


def norm_back(dn, n_hat, rs, gain):
    gd = dn * gain
    return (
        gd
        - jnp.mean(gd, axis=-1, keepdims=True)
        - n_hat * jnp.mean(gd * n_hat, axis=-1, keepdims=True)
    ) * rs


def col_shift(value, by):
    if by == 0:
        return value
    at = lax.broadcasted_iota(jnp.int32, value.shape, 0) % SIDE
    rolled = pltpu.roll(value, (-by) % TOK, 0)
    return jnp.where((at + by >= 0) & (at + by < SIDE), rolled, 0.0)


def row_shift(value, by):
    if by == 0:
        return value
    gap = jnp.zeros((abs(by) * SIDE, value.shape[1]), value.dtype)
    if by > 0:
        return jnp.concatenate([value[by * SIDE :], gap], axis=0)
    return jnp.concatenate([gap, value[: TOK + by * SIDE]], axis=0)


def depthwise(value, tap, side):
    half = side // 2
    shifted = [col_shift(value, b - half) for b in range(side)]
    total = None
    for a in range(side):
        line = None
        for b in range(side):
            term = shifted[b] * tap(a * side + b)
            line = term if line is None else line + term
        line = row_shift(line, a - half)
        total = line if total is None else total + line
    return total


def depthwise_taps(value, grad, side, put):
    half = side // 2
    shifted = [col_shift(value, b - half) for b in range(side)]
    for a in range(side):
        d = a - half
        lo, hi = max(0, -d) * SIDE, (SIDE - max(0, d)) * SIDE
        for b in range(side):
            part = shifted[b][lo + d * SIDE : hi + d * SIDE] * grad[lo:hi]
            put(a * side + b, jnp.sum(part, axis=0, keepdims=True))


def lanes_of(at, width):
    return pl.ds(pl.multiple_of(at * width, width), width)


def side_by_side(blocks):
    return jnp.concatenate(blocks, axis=1)


def main_kernel(dims, outer, *refs):
    at = iter(refs)

    def take(count):
        return [next(at) for _ in range(count)]

    na = len(ARRAYS)
    source = dict(zip(ARRAYS, take(na)))
    (
        depth_in, ln_conv_in, scale_in, ln_attn_in, ln_mlp_in, adapt_depth_in,
        order_in, train_in, tok_in, grid_in, tcot_in, gcot_in,
    ) = take(12)
    hid_tok, hid_grid, out_gtok, out_ggrid = take(4)
    native = dict(zip(ARRAYS, take(na)))
    out_depth, out_ln_conv, out_scale, out_ln_attn, out_ln_mlp, out_ad = take(6)
    W = dict(zip(ARRAYS, take(na)))
    RX = dict(zip(ARRAYS, take(na)))
    (
        v_loc, vv, aq, vec_c, vec_d, x_in, c_in, n1_all, f_all, n2_all, c2_all,
        o_sb, o_rb, cv_sb, cv_rb, m_sb, m_rb, br_sb, br_rb, gsb, dgb,
        qkv, prob, ctx, u, up, r, rp, cn, crs, cv_sum, x1, c2f,
        adapted, spread, pooled, gate,
        dx3, dcot, dx3_all, dn2_sb, dn2_rb, dc2_sb, dc2_rb, dx1_all, dcv_all,
        dn1_sb, dn1_rb, df_sb, df_rb, dh, do_all, dqkv, dhc, dx1, dc2t, dad, dcn,
        gvs, gv_rb, gvx, gad, gad_rb, gad_all, turned,
    ) = take(65)
    (
        zs_send, zs_recv, s1_send, s1_recv, loc_sem, s2_send, s2_recv,
        v_send, v_recv, q_send, q_recv, h_send, h_recv, b_send, b_recv,
        xo_send, xo_recv, g_send, g_recv, a_send, a_recv, gx_send, gx_recv, go,
    ) = take(24)

    p = lax.axis_index("pipe")
    dpi = lax.axis_index("dp")
    x = lax.axis_index("tensor")
    rest = dpi % outer
    zi = dpi // (outer * R)
    ri = (dpi // outer) % R
    xo = 1 - x
    ro = 1 - ri
    d_dim, c_dim, hq, ffq, cfq, adq, dg = dims
    adh = Z * adq
    dz, cz = d_dim // Z, c_dim // Z
    tile = 256
    ids = {name: number for number, name in enumerate(ARRAYS)}
    ev = {name: number for number, name in enumerate(EVENTS)}

    def dev(z=None, rr=None, xx=None, pp=None):
        z = zi if z is None else z
        rr = ri if rr is None else rr
        return (
            p if pp is None else pp,
            (z * R + rr) * outer + rest,
            x if xx is None else xx,
        )

    def zto(d):
        return lax.rem(zi + d, Z)

    def zfrom(d):
        return lax.rem(zi + Z - d, Z)

    def remote(src, dst, ssem, rsem, device):
        return pltpu.make_async_remote_copy(
            src_ref=src, dst_ref=dst, send_sem=ssem, recv_sem=rsem,
            device_id=device, device_id_type=pl.DeviceIdType.MESH,
        )

    sib = dev(pp=1 - p)
    over_r, over_x = dev(rr=ro), dev(xx=xo)

    def z_copy(e, d, src, dst):
        return remote(src, dst, zs_send.at[e, d - 1], zs_recv.at[e, d - 1], dev(zto(d)))

    sent = []

    def gather_copies(name, buf):
        return [z_copy(ev[name], d, buf.at[zi], buf.at[zi]) for d in range(1, Z)]

    def gather_start(name, buf, keep=True):
        copies = gather_copies(name, buf)
        for c in copies:
            c.start()
        if keep:
            sent.extend(copies)

    def gather_wait(name, buf):
        for d in range(1, Z):
            slot = buf.at[zfrom(d)]
            z_copy(ev[name], d, slot, slot).wait_recv()

    def scatter_start(name, sb, rb):
        for d in range(1, Z):
            c = z_copy(ev[name], d, sb.at[zto(d)], rb.at[d - 1])
            c.start()
            sent.append(c)

    def scatter_wait(name, rb):
        for d in range(1, Z):
            z_copy(ev[name], d, rb.at[d - 1], rb.at[d - 1]).wait_recv()

    def share_start(name, buf):
        for d in range(1, Z):
            c = z_copy(ev[name], d, buf.at[3], buf.at[d - 1])
            c.start()
            sent.append(c)

    def scattered(sb, rb):
        return (wide(sb[zi]) + wide(rb[0])) + (wide(rb[1]) + wide(rb[2]))

    barrier = pltpu.get_barrier_semaphore()
    greeted = [sib]
    for d in range(1, Z):
        greeted += [dev(zto(d)), dev(zto(d), ro)]
    greeted += [over_r, over_x, dev(rr=ro, xx=xo)]
    for device in greeted:
        pl.semaphore_signal(barrier, inc=1, device_id=device, device_id_type=pl.DeviceIdType.MESH)
    v_loc[...] = jnp.zeros(v_loc.shape, F32)
    taps7 = depth_in.shape[0]
    c_own = depth_in.shape[1]
    v_loc[0:taps7, 0:c_own] = wide(depth_in[...])
    v_loc[49:50, 0:c_own] = wide(ln_conv_in[...])
    v_loc[50:51, 0:c_own] = wide(scale_in[...])
    v_loc[56:57, 0:LANE] = wide(ln_attn_in[...])
    v_loc[57:58, 0:LANE] = wide(ln_mlp_in[...])
    aq[x] = jnp.zeros(aq.shape[1:], F32)
    aq[x, 0:9] = wide(adapt_depth_in[:, lanes_of(zi, adq)])
    pl.semaphore_wait(barrier, len(greeted))

    me8 = zi * R + ri
    v_arrivals = []
    for n, (d, flip) in enumerate([(d, s) for d in range(Z) for s in (0, 1)][1:]):
        tr = ro if flip else ri
        c = remote(v_loc, vv.at[me8], v_send.at[n], v_recv.at[n], dev(zto(d), tr))
        c.start()
        sent.append(c)
        fr = zfrom(d) * R + tr
        v_arrivals.append(remote(vv.at[fr], vv.at[fr], v_send.at[n], v_recv.at[n], dev(zto(d), tr)))
    vv[me8] = v_loc[...]
    c = remote(aq.at[x], aq.at[x], q_send, q_recv, over_x)
    c.start()
    sent.append(c)

    by_rows = ("O", "F2")

    def quarter_of(name, ref, z):
        if name == "Q":
            return ref.at[:, :, lanes_of(z, hq)]
        if name in by_rows:
            height = ref.shape[0] // Z
            return ref.at[pl.ds(pl.multiple_of(z * height, height), height)]
        return ref.at[:, lanes_of(z, ref.shape[1] // Z)]

    def step1_local(name):
        return pltpu.make_async_copy(
            quarter_of(name, source[name], zi), W[name].at[x, zi, ri], loc_sem.at[ids[name]]
        )

    def step1_copy(name, d):
        k = ids[name]
        return remote(
            quarter_of(name, source[name], zto(d)), W[name].at[x, zi, ri],
            s1_send.at[k, d - 1], s1_recv.at[k, d - 1], dev(zto(d)),
        )

    def half_of(name, j, z, rr, upper):
        w = W[name]
        half = w.shape[-2] // 2
        rows = slice(half, None) if upper else slice(0, half)
        if len(w.shape) == 6:
            return w.at[j, z, rr, :, rows]
        return w.at[j, z, rr, rows]

    def step2_copy(name, which, d):
        k = ids[name]
        z = zfrom(d)
        if which < 2:
            src = quarter_of(name, source[name], zi) if d == 0 else W[name].at[x, z, ri]
            dst = W[name].at[x, z, ri]
        else:
            src = dst = half_of(name, x, z, ro, False) if which == 2 else half_of(name, xo, z, ri, True)
        to = over_x if which in (1, 2) else over_r
        return remote(src, dst, s2_send.at[k, which, d], s2_recv.at[k, which, d], to)

    def step2_arrival(name, which, d):
        k = ids[name]
        z = zfrom(d)
        if which < 2:
            ref = W[name].at[x, z, ro] if which == 0 else W[name].at[xo, z, ri]
        else:
            ref = half_of(name, xo, z, ro, which == 3)
        to = over_x if which in (1, 2) else over_r
        return remote(ref, ref, s2_send.at[k, which, d], s2_recv.at[k, which, d], to)

    def relay1(*names):
        for name in names:
            step1_local(name).start()
            for d in range(1, Z):
                step1_copy(name, d).start()
            step2_copy(name, 0, 0).start()
            step2_copy(name, 1, 0).start()

    def relay2(name, ds=(1, 2, 3)):
        k = ids[name]
        for d in ds:
            slot = W[name].at[x, zfrom(d), ri]
            remote(slot, slot, s1_send.at[k, d - 1], s1_recv.at[k, d - 1], dev(zto(d))).wait_recv()
            step2_copy(name, 0, d).start()
            step2_copy(name, 1, d).start()

    def relay3(name, ds=(0, 1, 2, 3)):
        for d in ds:
            step2_arrival(name, 0, d).wait_recv()
            step2_copy(name, 2, d).start()
            step2_arrival(name, 1, d).wait_recv()
            step2_copy(name, 3, d).start()

    def relay4(*names):
        for name in names:
            step1_local(name).wait()
            for d in range(Z):
                step2_arrival(name, 2, d).wait_recv()
                step2_arrival(name, 3, d).wait_recv()

    def relay_sent():
        for name in ARRAYS:
            for d in range(1, Z):
                step1_copy(name, d).wait_send()
            for which in range(4):
                for d in range(Z):
                    step2_copy(name, which, d).wait_send()

    @pl.when(p == 1)
    def _():
        pl.semaphore_wait(go, 1)

    relay1("P1")

    for c in v_arrivals:
        c.wait_recv()
    remote(aq.at[xo], aq.at[xo], q_send, q_recv, over_x).wait_recv()
    low_lanes = lax.broadcasted_iota(jnp.int32, (64, LANE), 1) < LANE // 2
    for z in range(Z):
        first, second = vv[2 * z], pltpu.roll(vv[2 * z + 1], LANE // 2, 1)
        vec_c[:, z * cz : z * cz + LANE] = first[:, 0:LANE]
        vec_c[:, z * cz + LANE : z * cz + 2 * LANE] = jnp.where(
            low_lanes, first[:, LANE:], second[:, 0:LANE]
        )
        vec_c[:, z * cz + 2 * LANE : (z + 1) * cz] = second[:, LANE:]
    for i in range(Z * R):
        vec_d[:, i * LANE : (i + 1) * LANE] = vv[i, 56:64, 0:LANE]

    def gain_d(row):
        return vec_d[row : row + 1, :]

    def gain_c(row):
        return vec_c[row : row + 1, :]

    def token_entry():
        n_hat, _ = normed(wide(x_in[...]))
        n1_all[zi] = low(n_hat * gain_d(0))
        gather_start("n1", n1_all, keep=False)

    sent.extend(gather_copies("n1", n1_all))

    @pl.when(p == 0)
    def _():
        first = order_in[0, x] == 0
        c_in[...] = jnp.where(first, grid_in[0], grid_in[1])
        x_in[...] = jnp.where(first, tok_in[0], tok_in[1])
        token_entry()

    @pl.when(p == 1)
    def _():
        remote(c_in, c_in, h_send.at[1], h_recv.at[1], sib).wait_recv()

    @pl.loop(0, c_dim // LANE)
    def _(ch):
        lanes = lanes_of(ch, LANE)
        taps = vec_c[:, lanes]
        cn[:, lanes] = depthwise(wide(c_in[:, lanes]), lambda k: taps[k : k + 1], 7)

    n_hat, rs = normed(cn[...])
    cn[...] = n_hat
    crs[...] = jnp.broadcast_to(rs, crs.shape)
    f_all[zi] = low(n_hat * gain_c(49))
    gather_start("f", f_all)

    relay2("P1", (1,))
    relay1("P2")
    relay2("P1", (2, 3))
    relay2("P2", (1,))
    relay1("Q", "O")
    relay2("P2", (2, 3))
    relay3("P1")
    relay2("Q")
    relay2("O")
    relay1("E", "Gi", "Go")
    relay3("P2", (0, 1))
    relay4("P1")
    gather_wait("f", f_all)

    def conv_hidden(j):
        @pl.loop(0, cfq // tile)
        def _(t):
            lanes = lanes_of(t, tile)
            act, der = gelu_pair(mm(flat(f_all[...]), flat(W["P1"][j, :, :, :, lanes])))
            r[j, :, lanes] = low(act)
            rp[j, :, lanes] = low(der)

    conv_hidden(0)
    relay3("P2", (2, 3))
    for name in ("E", "Gi", "Go"):
        relay2(name)
    relay1("F1")
    conv_hidden(1)
    relay3("Q")
    relay3("O")
    relay2("F1")
    relay1("F2")
    relay4("P2")

    @pl.loop(0, Z)
    def _(z):
        acc = mm_nt(r[0], flat(W["P2"][0, z])) + mm_nt(r[1], flat(W["P2"][1, z]))
        cv_sb[:, :, lanes_of(z, cz)] = low(acc).reshape(Z, TOK, cz)

    scatter_start("cv", cv_sb, cv_rb)

    for name in ("E", "Gi", "Go"):
        relay3(name)
    relay2("F2")

    @pl.when(p == 0)
    def _():
        pl.semaphore_signal(go, inc=1, device_id=sib, device_id_type=pl.DeviceIdType.MESH)

    @pl.when(p == 1)
    def _():
        relay3("F1")
        relay3("F2")
        remote(x_in, x_in, h_send.at[0], h_recv.at[0], sib).wait_recv()
        token_entry()

    relay4("Q", "O")
    gather_wait("n1", n1_all)
    for j in range(2):
        wj = side_by_side([flat(W["Q"][j, :, :, s]) for s in range(3)])
        qkv[j] = low(mm(flat(n1_all[...]), wj))
    for j in range(2):
        for b in range(Z):
            rows = slice(b * TOK, (b + 1) * TOK)
            outs = []
            for h in range(hq // HD):
                q, kk, vals = (qkv[j, rows, s * hq + h * HD : s * hq + (h + 1) * HD] for s in range(3))
                sc = mm_nt(q, kk) * HD ** (-0.5)
                e = jnp.exp(sc - jnp.max(sc, axis=-1, keepdims=True))
                pr = low(e / jnp.sum(e, axis=-1, keepdims=True))
                prob[j, h, b] = pr
                outs.append(mm(pr, vals))
            ctx[j, rows, :] = low(side_by_side(outs))

    def out_block(j, z):
        return side_by_side([W["O"][j, z, 0], W["O"][j, z, 1]])

    @pl.loop(0, Z)
    def _(z):
        both = jnp.concatenate([out_block(0, z), out_block(1, z)], axis=0)
        acc = mm(side_by_side([ctx[0], ctx[1]]), both)
        o_sb[:, :, lanes_of(z, dz)] = low(acc).reshape(Z, TOK, dz)

    scatter_start("o", o_sb, o_rb)

    @pl.when(p == 0)
    def _():
        relay3("F1")

    scatter_wait("cv", cv_rb)
    cv_sum[...] = scattered(cv_sb, cv_rb)
    c2f[...] = wide(c_in[...]) + gain_c(50) * cv_sum[...]
    c2_low = low(c2f[...])
    c2_all[zi] = c2_low
    gather_start("c2", c2_all)
    hid_grid[x] = c2_low

    @pl.when(p == 0)
    def _():
        remote(hid_grid.at[x], c_in, h_send.at[1], h_recv.at[1], sib).start()

    @pl.when(p == 0)
    def _():
        relay3("F2")

    scatter_wait("o", o_rb)
    x1[...] = wide(x_in[...]) + scattered(o_sb, o_rb)
    n_hat, _ = normed(x1[...])
    n2_all[zi] = low(n_hat * gain_d(1))
    gather_start("n2", n2_all)

    relay4("E", "Gi", "Go")
    gather_wait("c2", c2_all)
    row8 = lax.broadcasted_iota(jnp.int32, (8, adq), 0)
    gs_part = None
    for j in range(2):
        ad = mm(flat(c2_all[...]), flat(W["E"][j]))
        adapted[j] = ad
        taps = aq[j]
        pool = jnp.zeros((8, adq), F32)
        for b in range(Z):
            sp = depthwise(ad[b * TOK : (b + 1) * TOK], lambda k: taps[k : k + 1], 3)
            spread[j, b] = sp
            pool = jnp.where(row8 == b, jnp.mean(sp, axis=0, keepdims=True), pool)
        pooled[j] = pool
        term = mm_nt(low(pool), flat(W["Gi"][j]))
        gs_part = term if gs_part is None else gs_part + term
    gsb[3] = gs_part
    share_start("gs", gsb)

    relay4("F1")
    gather_wait("n2", n2_all)
    for j in range(2):

        @pl.loop(0, ffq // tile)
        def _(t):
            lanes = lanes_of(t, tile)
            act, der = gelu_pair(mm(flat(n2_all[...]), flat(W["F1"][j, :, :, :, lanes])))
            u[j, :, lanes] = low(act)
            up[j, :, lanes] = low(der)

    scatter_wait("gs", gsb)

    def gate_hidden():
        return gelu_pair((gsb[0] + gsb[1]) + (gsb[2] + gsb[3]))

    gh, _ = gate_hidden()
    for j in range(2):
        g8 = jnp.tanh(mm(low(gh), flat(W["Go"][j])))
        gate[j] = g8
        for b in range(Z):
            br_sb[b, :, j * adq : (j + 1) * adq] = low(g8[b : b + 1] * spread[j, b])
    scatter_start("br", br_sb, br_rb)
    relay4("F2")

    @pl.loop(0, Z)
    def _(z):
        acc = None
        for j in range(2):
            term = mm(u[j], side_by_side([W["F2"][j, z, 0], W["F2"][j, z, 1]]))
            acc = term if acc is None else acc + term
        m_sb[:, :, lanes_of(z, dz)] = low(acc).reshape(Z, TOK, dz)

    scatter_start("m", m_sb, m_rb)
    scatter_wait("br", br_rb)
    dx1[...] = x1[...]
    for d in range(Z):
        piece = br_sb[zi] if d == 0 else br_rb[d - 1]
        for j in range(2):
            lanes = pl.ds(pl.multiple_of(j * adh + zfrom(d) * adq, LANE), adq)
            dx1[:, lanes] += wide(piece[:, j * adq : (j + 1) * adq])
    scatter_wait("m", m_rb)
    hid_tok[x] = low(dx1[...] + scattered(m_sb, m_rb))

    @pl.when(p == 0)
    def _():
        remote(hid_tok.at[x], x_in, h_send.at[0], h_recv.at[0], sib).start()

    out_arrivals = []

    def exchange(n, buf):
        c = remote(buf.at[x], buf.at[x], xo_send.at[n], xo_recv.at[n], over_x)
        c.start()
        sent.append(c)
        out_arrivals.append(remote(buf.at[xo], buf.at[xo], xo_send.at[n], xo_recv.at[n], over_x))

    exchange(0, hid_tok)
    exchange(1, hid_grid)
    relay_sent()

    @pl.when(p == 1)
    def _():
        dx3[...] = tcot_in[x]
        dcot[...] = gcot_in[x]

    @pl.when(p == 0)
    def _():
        remote(dx3, dx3, b_send.at[0], b_recv.at[0], sib).wait_recv()

    dx3_all[zi] = dx3[...]
    gather_start("dx3", dx3_all)
    gather_wait("dx3", dx3_all)

    def own_lanes(j):
        return pl.ds(pl.multiple_of(j * adh + zi * adq, LANE), adq)

    gh, ghp = gate_hidden()
    dgh_part = None
    dgp = []
    for j in range(2):
        dgate = jnp.zeros((8, adq), F32)
        for b in range(Z):
            dbr = wide(dx3_all[b, :, own_lanes(j)])
            dgate = jnp.where(row8 == b, jnp.sum(dbr * spread[j, b], axis=0, keepdims=True), dgate)
        dg8 = low(dgate * (1.0 - gate[j] * gate[j]))
        dgp.append(dg8)
        term = mm_nt(dg8, flat(W["Go"][j]))
        dgh_part = term if dgh_part is None else dgh_part + term
    dgb[3] = dgh_part
    share_start("dgh", dgb)

    for j in range(2):

        @pl.loop(0, ffq // tile)
        def _(t):
            rows = lanes_of(t, tile)
            both = side_by_side([W["F2"][j, z, rr, rows] for z in range(Z) for rr in range(R)])
            du = mm_nt(flat(dx3_all[...]), both)
            dh[j, :, rows] = low(du * wide(up[j, :, rows]))

    scatter_wait("dgh", dgb)
    dgs = low(((dgb[0] + dgb[1]) + (dgb[2] + dgb[3])) * ghp)
    for j in range(2):
        dpool = mm(dgs, flat(W["Gi"][j])) * (1.0 / TOK)
        taps = aq[j]
        tap_rows = [None] * 9
        for b in range(Z):
            dsp = gate[j, b : b + 1] * wide(dx3_all[b, :, own_lanes(j)]) + dpool[b : b + 1]
            dad[j, b * TOK : (b + 1) * TOK] = low(depthwise(dsp, lambda k: taps[8 - k : 9 - k], 3))

            def put(k, row):
                tap_rows[k] = row if tap_rows[k] is None else tap_rows[k] + row

            depthwise_taps(adapted[j, b * TOK : (b + 1) * TOK], dsp, 3, put)
        for k in range(9):
            gad[j, k : k + 1] = tap_rows[k]
        gad[j, 9:16] = jnp.zeros((7, adq), F32)

    @pl.loop(0, Z)
    def _(z):
        acc = mm_nt(dad[0], flat(W["E"][0, z])) + mm_nt(dad[1], flat(W["E"][1, z]))
        dc2_sb[:, :, lanes_of(z, cz)] = low(acc).reshape(Z, TOK, cz)

    scatter_start("dc2", dc2_sb, dc2_rb)

    @pl.loop(0, Z)
    def _(z):
        acc = mm_nt(dh[0], flat(W["F1"][0, z])) + mm_nt(dh[1], flat(W["F1"][1, z]))
        dn2_sb[:, :, lanes_of(z, dz)] = low(acc).reshape(Z, TOK, dz)

    scatter_start("dn2", dn2_sb, dn2_rb)

    peers = ((1, 0), (0, 1), (1, 1))

    def owner(k):
        return (ro if peers[k][0] else ri), (xo if peers[k][1] else x)

    def reduce_copy(name, k):
        rr, xx = owner(k)
        n = ids[name]
        return remote(W[name].at[xx, :, rr], RX[name].at[k], g_send.at[n, k], g_recv.at[n, k], dev(rr=rr, xx=xx))

    def reduce_start(name):
        for k in (2, 0, 1):
            reduce_copy(name, k).start()

    def row_grad(name, left, right):
        width = W[name].shape[3]
        span = R * width

        @pl.loop(0, Z)
        def _(z):
            turned[0:span] = flat(left[:, :, lanes_of(z, span)]).T
            for j in range(2):
                W[name][j, z] = low(mm(turned[0:span], right[j])).reshape(R, width, -1)

        reduce_start(name)

    def col_grad(name, left, right):
        width = left.shape[2]
        for j in range(2):
            turned[j * width : (j + 1) * width] = left[j].T

        @pl.loop(0, Z)
        def _(z):
            rhs = flat(right[:, :, lanes_of(z, dz)])
            for j in range(2):
                g = low(mm(turned[j * width : (j + 1) * width], rhs))
                for rr in range(R):
                    W[name][j, z, rr] = g[:, rr * LANE : (rr + 1) * LANE]

        reduce_start(name)

    for j in range(2):
        W["Gi"][j] = low(mm_tn(dgs, low(pooled[j]))).reshape(Z, R, -1, adq)
        W["Go"][j] = low(mm_tn(low(gh), dgp[j])).reshape(Z, R, -1, adq)
    reduce_start("Gi")
    reduce_start("Go")
    row_grad("E", c2_all, dad)

    @pl.when(p == 0)
    def _():
        remote(dcot, dcot, b_send.at[1], b_recv.at[1], sib).wait_recv()

    scatter_wait("dc2", dc2_rb)
    dc2t[...] = wide(dcot[...]) + scattered(dc2_sb, dc2_rb)
    gvs_ls = jnp.sum(cv_sum[...] * dc2t[...], axis=0, keepdims=True)
    dcv_all[zi] = low(dc2t[...] * gain_c(50))
    gather_start("dcv", dcv_all)

    scatter_wait("dn2", dn2_rb)
    dn2 = scattered(dn2_sb, dn2_rb)
    n_hat, rs = normed(x1[...])
    gvs_d1 = jnp.sum(dn2 * n_hat, axis=0, keepdims=True)
    dx1[...] = wide(dx3[...]) + norm_back(dn2, n_hat, rs, gain_d(1))
    dx1_all[zi] = low(dx1[...])
    gather_start("dx1", dx1_all)

    col_grad("F2", u, dx3_all)
    row_grad("F1", n2_all, dh)

    gather_wait("dcv", dcv_all)
    for j in range(2):

        @pl.loop(0, cfq // tile)
        def _(t):
            lanes = lanes_of(t, tile)
            dr = mm(flat(dcv_all[...]), flat(W["P2"][j, :, :, :, lanes]))
            dhc[j, :, lanes] = low(dr * wide(rp[j, :, lanes]))

    @pl.loop(0, Z)
    def _(z):
        acc = mm_nt(dhc[0], flat(W["P1"][0, z])) + mm_nt(dhc[1], flat(W["P1"][1, z]))
        df_sb[:, :, lanes_of(z, cz)] = low(acc).reshape(Z, TOK, cz)

    scatter_start("df", df_sb, df_rb)

    gather_wait("dx1", dx1_all)
    for j in range(2):
        both = side_by_side([W["O"][j, z, rr] for z in range(Z) for rr in range(R)])
        do_all[j] = low(mm_nt(flat(dx1_all[...]), both))
    for j in range(2):
        for b in range(Z):
            rows = slice(b * TOK, (b + 1) * TOK)
            parts = [[], [], []]
            for h in range(hq // HD):
                q, kk, vals = (qkv[j, rows, s * hq + h * HD : s * hq + (h + 1) * HD] for s in range(3))
                do = do_all[j, rows, h * HD : (h + 1) * HD]
                pr = prob[j, h, b]
                dp = mm_nt(do, vals)
                prw = wide(pr)
                ds = low(prw * (dp - jnp.sum(dp * prw, axis=-1, keepdims=True)) * HD ** (-0.5))
                parts[0].append(mm(ds, kk))
                parts[1].append(mm_tn(ds, q))
                parts[2].append(mm_tn(pr, do))
            for s in range(3):
                dqkv[j, rows, s * hq : (s + 1) * hq] = low(side_by_side(parts[s]))

    @pl.loop(0, Z)
    def _(z):
        acc = None
        for j in range(2):
            term = mm_nt(dqkv[j], side_by_side([flat(W["Q"][j, z, :, s]) for s in range(3)]))
            acc = term if acc is None else acc + term
        dn1_sb[:, :, lanes_of(z, dz)] = low(acc).reshape(Z, TOK, dz)

    scatter_start("dn1", dn1_sb, dn1_rb)

    def pw_grads():
        row_grad("P2", dcv_all, r)
        row_grad("P1", f_all, dhc)

    @pl.when(p == 0)
    def _():
        pw_grads()

    scatter_wait("dn1", dn1_rb)
    dn1 = scattered(dn1_sb, dn1_rb)
    n_hat, rs = normed(wide(x_in[...]))
    gvs_d0 = jnp.sum(dn1 * n_hat, axis=0, keepdims=True)
    out_gtok[x] = low(dx1[...] + norm_back(dn1, n_hat, rs, gain_d(0)))

    @pl.when(p == 1)
    def _():
        remote(out_gtok.at[x], dx3, b_send.at[0], b_recv.at[0], sib).start()

    scatter_wait("df", df_rb)
    dfv = scattered(df_sb, df_rb)
    gvs_lc = jnp.sum(dfv * cn[...], axis=0, keepdims=True)
    dcn[...] = norm_back(dfv, cn[...], crs[:, 0:1], gain_c(49))

    @pl.loop(0, c_dim // LANE)
    def _(ch):
        lanes = lanes_of(ch, LANE)
        taps = vec_c[:, lanes]
        back = depthwise(dcn[:, lanes], lambda k: taps[48 - k : 49 - k], 7)
        out_ggrid[x, :, lanes] = low(dc2t[:, lanes] + back)

    @pl.when(p == 1)
    def _():
        remote(out_ggrid.at[x], dcot, b_send.at[1], b_recv.at[1], sib).start()
        pw_grads()

    @pl.loop(0, Z)
    def _(z):
        turned[0:dz] = flat(n1_all[:, :, lanes_of(z, dz)]).T
        for j in range(2):
            g = low(mm(turned[0:dz], dqkv[j]))
            for s in range(3):
                W["Q"][j, z, :, s] = g[:, s * hq : (s + 1) * hq].reshape(R, -1, hq)

    reduce_start("Q")
    col_grad("O", ctx, dx1_all)

    exchange(2, out_gtok)
    exchange(3, out_ggrid)

    @pl.loop(0, Z)
    def _(z):
        for part in range(cz // LANE):
            lanes = pl.ds(pl.multiple_of(z * cz + part * LANE, LANE), LANE)

            def put(k, row):
                gvs[z, k : k + 1, part * LANE : (part + 1) * LANE] = row

            depthwise_taps(wide(c_in[:, lanes]), dcn[:, lanes], 7, put)

    for z in range(Z):
        gvs[z, 49:50] = gvs_lc[:, z * cz : (z + 1) * cz]
        gvs[z, 50:51] = gvs_ls[:, z * cz : (z + 1) * cz]
        gvs[z, 51:64] = jnp.zeros((13, cz), F32)
        gvs[z, 56:57, 0:dz] = gvs_d0[:, z * dz : (z + 1) * dz]
        gvs[z, 57:58, 0:dz] = gvs_d1[:, z * dz : (z + 1) * dz]
    scatter_start("gv", gvs, gv_rb)

    def group_copy(n, k, src, dst):
        rr, xx = owner(k)
        return remote(src, dst, gx_send.at[n, k], gx_recv.at[n, k], dev(rr=rr, xx=xx))

    for k in range(3):
        c = group_copy(1, k, gad, gad_rb.at[k])
        c.start()
        sent.append(c)
    scatter_wait("gv", gv_rb)
    gvx[3] = (gvs[zi] + gv_rb[0]) + (gv_rb[1] + gv_rb[2])
    for k in range(3):
        c = group_copy(0, k, gvx.at[3], gvx.at[k])
        c.start()
        sent.append(c)
    for k in range(3):
        group_copy(1, k, gad, gad_rb.at[k]).wait_recv()
    gad_all[zi] = (gad[x] + gad_rb[0, x]) + (gad_rb[1, x] + gad_rb[2, x])
    gather_start("gad", gad_all)

    def back_copy(name, d):
        n = ids[name]
        return remote(
            RX[name].at[0, zto(d)], quarter_of(name, native[name], zi),
            a_send.at[n, d - 1], a_recv.at[n, d - 1], dev(zto(d)),
        )

    def back_local(name):
        return pltpu.make_async_copy(
            RX[name].at[0, zi], quarter_of(name, native[name], zi), loc_sem.at[ids[name]]
        )

    for name in ("Gi", "Go", "E", "F2", "F1", "P2", "P1", "Q", "O"):
        n = ids[name]
        rx = RX[name]
        for k in range(3):
            reduce_copy(name, k).wait_recv()

        @pl.loop(0, Z)
        def _(z):
            total = (wide(W[name][x, z, ri]) + wide(rx[0, z])) + (wide(rx[1, z]) + wide(rx[2, z]))
            rx[0, z] = low(total)

        for d in range(1, Z):
            back_copy(name, d).start()
        back_local(name).start()

    for k in range(3):
        group_copy(0, k, gvx.at[k], gvx.at[k]).wait_recv()
    total = (gvx[0] + gvx[1]) + (gvx[2] + gvx[3])
    mine = jnp.where(ri == 1, pltpu.roll(total, c_own, 1), total)[:, 0:c_own]
    mine_d = jnp.where(ri == 1, total[:, LANE : 2 * LANE], total[:, 0:LANE])

    def flag(n):
        return train_in[0, n].astype(F32)

    out_depth[...] = mine[0:taps7] * flag(0)
    out_ln_conv[...] = mine[49:50] * flag(1)
    out_scale[...] = mine[50:51] * flag(4)
    out_ln_attn[...] = mine_d[56:57]
    out_ln_mlp[...] = mine_d[57:58]
    gather_wait("gad", gad_all)
    for z in range(Z):
        out_ad[:, z * adq : (z + 1) * adq] = gad_all[z][0:9]
    for name in ARRAYS:
        back_local(name).wait()
        for d in range(1, Z):
            n = ids[name]
            slot = quarter_of(name, native[name], zfrom(d))
            remote(slot, slot, a_send.at[n, d - 1], a_recv.at[n, d - 1], dev(zto(d))).wait_recv()
    for c in out_arrivals:
        c.wait_recv()

    @pl.when(p == 0)
    def _():
        remote(hid_tok.at[x], x_in, h_send.at[0], h_recv.at[0], sib).wait_send()
        remote(hid_grid.at[x], c_in, h_send.at[1], h_recv.at[1], sib).wait_send()

    @pl.when(p == 1)
    def _():
        remote(out_gtok.at[x], dx3, b_send.at[0], b_recv.at[0], sib).wait_send()
        remote(out_ggrid.at[x], dcot, b_send.at[1], b_recv.at[1], sib).wait_send()

    for c in sent:
        c.wait_send()
    for name in ARRAYS:
        for k in range(3):
            reduce_copy(name, k).wait_send()
        for d in range(1, Z):
            back_copy(name, d).wait_send()


def run_layers(weights, vectors, order, train, streams, sizes, outer):
    d_dim, c_dim, hq, ffq, cfq, adw, dg = sizes
    vm = pltpu.VMEM
    blocks = []
    for name, value in zip(ARRAYS, weights):
        if name == "Q":
            blocks.append((3, value.shape[1], hq))
        elif name in ("O", "F2"):
            blocks.append((value.shape[0] // Z, value.shape[1]))
        else:
            blocks.append((value.shape[0], value.shape[1] // Z))
    rows = Z * TOK

    def act(width, count=Z, kind=BF):
        return vm((count, TOK, width), kind)

    scratch = [vm((2, Z, R) + s, BF) for s in blocks] + [vm((3, Z) + s, BF) for s in blocks]
    scratch += [
        vm((64, 2 * LANE), F32), vm((Z * R, 64, 2 * LANE), F32), vm((2, 16, adw), F32), vm((64, c_dim), F32), vm((8, d_dim), F32),
        vm((TOK, d_dim), BF), vm((TOK, c_dim), BF), act(d_dim), act(c_dim), act(d_dim), act(c_dim),
        act(d_dim), act(d_dim, 3), act(c_dim), act(c_dim, 3), act(d_dim), act(d_dim, 3),
        act(2 * adw), act(2 * adw, 3), vm((4, 8, dg), F32), vm((4, 8, dg), F32),
        vm((2, rows, 3 * hq), BF), vm((2, hq // HD, Z, TOK, TOK), BF), vm((2, rows, hq), BF),
        vm((2, rows, ffq), BF), vm((2, rows, ffq), BF), vm((2, rows, cfq), BF), vm((2, rows, cfq), BF),
        vm((TOK, c_dim), F32), vm((TOK, LANE), F32), vm((TOK, c_dim), F32), vm((TOK, d_dim), F32), vm((TOK, c_dim), F32),
        vm((2, rows, adw), F32), vm((2, Z, TOK, adw), F32), vm((2, 8, adw), F32), vm((2, 8, adw), F32),
        vm((TOK, d_dim), BF), vm((TOK, c_dim), BF), act(d_dim), act(d_dim), act(d_dim, 3), act(c_dim), act(c_dim, 3),
        act(d_dim), act(c_dim),
        act(d_dim), act(d_dim, 3), act(c_dim), act(c_dim, 3), vm((2, rows, ffq), BF), vm((2, rows, hq), BF),
        vm((2, rows, 3 * hq), BF), vm((2, rows, cfq), BF), vm((TOK, d_dim), F32), vm((TOK, c_dim), F32), vm((2, rows, adw), BF),
        vm((TOK, c_dim), F32),
        vm((Z, 64, c_dim // Z), F32), vm((3, 64, c_dim // Z), F32), vm((4, 64, c_dim // Z), F32),
        vm((2, 16, adw), F32), vm((3, 2, 16, adw), F32), vm((Z, 16, adw), F32),
        vm((2 * ffq, rows), BF),
    ]
    dma = pltpu.SemaphoreType.DMA
    na = len(ARRAYS)
    scratch += [
        dma((len(EVENTS), 3)), dma((len(EVENTS), 3)), dma((na, 3)), dma((na, 3)), dma((na,)),
        dma((na, 4, Z)), dma((na, 4, Z)), dma((7,)), dma((7,)), dma, dma, dma((2,)), dma((2,)), dma((2,)), dma((2,)),
        dma((4,)), dma((4,)), dma((na, 3)), dma((na, 3)), dma((na, 3)), dma((na, 3)), dma((2, 3)), dma((2, 3)),
        pltpu.SemaphoreType.REGULAR,
    ]
    sds = jax.ShapeDtypeStruct
    out_shape = [sds((2, TOK, d_dim), BF), sds((2, TOK, c_dim), BF)] * 2
    out_shape += [sds(value.shape, BF) for value in weights]
    out_shape += [sds(value.shape, F32) for value in vectors]
    any_spec = pl.BlockSpec(memory_space=pl.ANY)
    vm_spec = pl.BlockSpec(memory_space=pltpu.VMEM)
    sm_spec = pl.BlockSpec(memory_space=pltpu.SMEM)
    return pl.pallas_call(
        functools.partial(main_kernel, sizes, outer),
        out_shape=out_shape,
        in_specs=[any_spec] * na + [vm_spec] * 6 + [sm_spec] * 2 + [vm_spec] * 4,
        out_specs=[vm_spec] * 4 + [any_spec] * na + [vm_spec] * 6,
        scratch_shapes=scratch,
        compiler_params=pltpu.CompilerParams(
            collective_id=0, has_side_effects=True, vmem_limit_bytes=62 * 1024 * 1024
        ),
        cost_estimate=pl.CostEstimate(flops=26 * 10**9, bytes_accessed=10**8, transcendentals=10**7),
        name="layers",
    )(*weights, *vectors, order, train, *streams)


def per_device(
    tokens,
    conv_grid,
    order,
    trainable,
    ln_attn,
    w_qkv,
    w_attn_out,
    ln_mlp,
    w_fc_in,
    w_fc_out,
    conv_depth,
    ln_conv,
    w_pw_in,
    w_pw_out,
    layer_scale,
    w_adapt,
    adapt_depth,
    w_gate_in,
    w_gate_out,
    tok_cot,
    grid_cot,
):
    dp_count = lax.axis_size("dp")
    outer = dp_count // (Z * R)
    groups = [[g * outer + o for o in range(outer)] for g in range(Z * R)]
    layer_at = lax.axis_index("pipe")

    def block(value, axis):
        value = value[0]
        if outer == 1:
            return value
        return lax.all_gather(value, "dp", axis=axis, tiled=True, axis_index_groups=groups)

    def share(value, axis):
        if outer > 1:
            value = lax.psum_scatter(
                value, "dp", scatter_dimension=axis, tiled=True, axis_index_groups=groups
            )
        return value[None]

    qkv = block(w_qkv, 1)
    gate_in = block(w_gate_in, 1).T
    pw_in = block(w_pw_in, 0)
    adapt = block(w_adapt, 0)
    fc_in = block(w_fc_in, 0)
    weights = (
        pw_in,
        block(w_pw_out, 1).T,
        qkv,
        block(w_attn_out, 1),
        adapt,
        gate_in,
        block(w_gate_out, 0),
        fc_in,
        block(w_fc_out, 1),
    )
    vectors = (
        block(conv_depth, 1),
        block(ln_conv, 0)[None],
        block(layer_scale, 0)[None],
        block(ln_attn, 0)[None],
        block(ln_mlp, 0)[None],
        adapt_depth[0],
    )
    spread = Z * R
    sizes = (
        qkv.shape[1] * spread, pw_in.shape[0] * spread, qkv.shape[2] // Z, fc_in.shape[1] // Z,
        pw_in.shape[1] // Z, adapt.shape[1] // Z, gate_in.shape[0] * spread,
    )

    def rows_of(value):
        return value.reshape(value.shape[0], TOK, value.shape[-1])

    streams = [rows_of(value) for value in (tokens, conv_grid, tok_cot, grid_cot)]
    outs = run_layers(weights, vectors, order, trainable, streams, sizes, outer)
    hid_tok, hid_grid, g_tok, g_grid = outs[:4]
    g_p1, g_p2, g_q, g_o, g_e, g_gi, g_go, g_f1, g_f2 = [value.astype(F32) for value in outs[4:13]]
    g_depth, g_ln_conv, g_scale, g_ln_attn, g_ln_mlp, g_ad = outs[13:]

    swap = (layer_at == 0) & (order[0, 0] == 1)
    g_tok = jnp.where(swap, g_tok[::-1], g_tok)
    g_grid = jnp.where(swap, g_grid[::-1], g_grid)
    grid_shape = (1,) + conv_grid.shape
    tok_shape = (1,) + tokens.shape
    flags = trainable[0].astype(F32)
    if outer > 1:
        g_ad = lax.psum(g_ad, "dp", axis_index_groups=groups)
    return (
        hid_tok.reshape(tok_shape),
        hid_grid.reshape(grid_shape),
        g_tok.reshape(tok_shape),
        g_grid.reshape(grid_shape),
        share(g_ln_attn[0], 0),
        share(g_q, 1),
        share(g_o, 1),
        share(g_ln_mlp[0], 0),
        share(g_f1, 0),
        share(g_f2, 1),
        share(g_depth, 1),
        share(g_ln_conv[0], 0),
        share(g_p1 * flags[2], 0),
        share((g_p2 * flags[3]).T, 1),
        share(g_scale[0], 0),
        share(g_e, 0),
        g_ad[None],
        share(g_gi.T, 1),
        share(g_go, 0),
    )


def solution(mesh):
    in_specs = (
        P(None, "dp", None, None),
        P(None, "dp", None, None, None),
        P("dp", None),
        P("pipe", None),
        P("pipe", "dp"),
        P("pipe", None, "dp", "tensor"),
        P("pipe", "tensor", "dp"),
        P("pipe", "dp"),
        P("pipe", "dp", "tensor"),
        P("pipe", "tensor", "dp"),
        P("pipe", None, "dp"),
        P("pipe", "dp"),
        P("pipe", "dp", "tensor"),
        P("pipe", "tensor", "dp"),
        P("pipe", "dp"),
        P("pipe", "dp", "tensor"),
        P("pipe", None, "tensor"),
        P("pipe", "tensor", "dp"),
        P("pipe", "dp", "tensor"),
        P(None, "dp", None, None),
        P(None, "dp", None, None, None),
    )
    out_specs = (
        P("pipe", None, "dp", None, None),
        P("pipe", None, "dp", None, None, None),
        P("pipe", None, "dp", None, None),
        P("pipe", None, "dp", None, None, None),
        P("pipe", "dp"),
        P("pipe", None, "dp", "tensor"),
        P("pipe", "tensor", "dp"),
        P("pipe", "dp"),
        P("pipe", "dp", "tensor"),
        P("pipe", "tensor", "dp"),
        P("pipe", None, "dp"),
        P("pipe", "dp"),
        P("pipe", "dp", "tensor"),
        P("pipe", "tensor", "dp"),
        P("pipe", "dp"),
        P("pipe", "dp", "tensor"),
        P("pipe", None, "tensor"),
        P("pipe", "tensor", "dp"),
        P("pipe", "dp", "tensor"),
    )
    return jax.shard_map(
        per_device, mesh=mesh, in_specs=in_specs, out_specs=out_specs, check_vma=False
    )
```

```python
import functools

import jax
import jax.numpy as jnp
from jax import lax
from jax.experimental import pallas as pl
from jax.experimental.pallas import tpu as pltpu
from jax.sharding import PartitionSpec as P

HD = 64
Z = 4
R = 2
TOK = 64
SIDE = 8
LANE = 128
BF = jnp.bfloat16
F32 = jnp.float32
ARRAYS = ("P1", "P2", "Q", "O", "E", "Gi", "Go", "F1", "F2")
EVENTS = (
    "n1", "f", "o", "cv", "n2", "c2", "m", "br", "gs",
    "dx3", "dgh", "dn2", "dc2", "dx1", "dcv", "dn1", "df", "gv", "gad",
)


def mm(a, b):
    return lax.dot_general(a, b, (((1,), (0,)), ((), ())), preferred_element_type=F32)


def mm_nt(a, b):
    return lax.dot_general(a, b, (((1,), (1,)), ((), ())), preferred_element_type=F32)


def mm_tn(a, b):
    return lax.dot_general(a, b, (((0,), (0,)), ((), ())), preferred_element_type=F32)


def flat(value):
    return value.reshape(-1, value.shape[-1])


def low(value):
    return value.astype(BF)


def wide(value):
    return value.astype(F32)


def gelu_pair(h):
    phi = 0.5 * (1.0 + lax.erf(h * 0.7071067811865476))
    dens = jnp.exp(-0.5 * h * h) * 0.3989422804014327
    return h * phi, phi + h * dens


def normed(value):
    centred = value - jnp.mean(value, axis=-1, keepdims=True)
    rs = lax.rsqrt(jnp.mean(centred * centred, axis=-1, keepdims=True) + 1e-06)
    return centred * rs, rs


def norm_back(dn, n_hat, rs, gain):
    gd = dn * gain
    return (
        gd
        - jnp.mean(gd, axis=-1, keepdims=True)
        - n_hat * jnp.mean(gd * n_hat, axis=-1, keepdims=True)
    ) * rs


def col_shift(value, by):
    if by == 0:
        return value
    at = lax.broadcasted_iota(jnp.int32, value.shape, 0) % SIDE
    rolled = pltpu.roll(value, (-by) % TOK, 0)
    return jnp.where((at + by >= 0) & (at + by < SIDE), rolled, 0.0)


def row_shift(value, by):
    if by == 0:
        return value
    gap = jnp.zeros((abs(by) * SIDE, value.shape[1]), value.dtype)
    if by > 0:
        return jnp.concatenate([value[by * SIDE :], gap], axis=0)
    return jnp.concatenate([gap, value[: TOK + by * SIDE]], axis=0)


def depthwise(value, tap, side):
    half = side // 2
    shifted = [col_shift(value, b - half) for b in range(side)]
    total = None
    for a in range(side):
        line = None
        for b in range(side):
            term = shifted[b] * tap(a * side + b)
            line = term if line is None else line + term
        line = row_shift(line, a - half)
        total = line if total is None else total + line
    return total


def depthwise_taps(value, grad, side, put):
    half = side // 2
    shifted = [col_shift(value, b - half) for b in range(side)]
    for a in range(side):
        d = a - half
        lo, hi = max(0, -d) * SIDE, (SIDE - max(0, d)) * SIDE
        for b in range(side):
            part = shifted[b][lo + d * SIDE : hi + d * SIDE] * grad[lo:hi]
            put(a * side + b, jnp.sum(part, axis=0, keepdims=True))


def lanes_of(at, width):
    return pl.ds(pl.multiple_of(at * width, width), width)


def side_by_side(blocks):
    return jnp.concatenate(blocks, axis=1)


def main_kernel(dims, outer, *refs):
    at = iter(refs)

    def take(count):
        return [next(at) for _ in range(count)]

    na = len(ARRAYS)
    source = dict(zip(ARRAYS, take(na)))
    (
        depth_in, ln_conv_in, scale_in, ln_attn_in, ln_mlp_in, adapt_depth_in,
        order_in, train_in, tok_in, grid_in, tcot_in, gcot_in,
    ) = take(12)
    hid_tok, hid_grid, out_gtok, out_ggrid = take(4)
    native = dict(zip(ARRAYS, take(na)))
    out_depth, out_ln_conv, out_scale, out_ln_attn, out_ln_mlp, out_ad = take(6)
    W = dict(zip(ARRAYS, take(na)))
    RX = dict(zip(ARRAYS, take(na)))
    (
        v_loc, vv, aq, vec_c, vec_d, x_in, c_in, n1_all, f_all, n2_all, c2_all,
        o_sb, o_rb, cv_sb, cv_rb, m_sb, m_rb, br_sb, br_rb, gsb, dgb,
        qkv, prob, ctx, u, up, r, rp, cn, crs, cv_sum, x1, c2f,
        adapted, spread, pooled, gate,
        dx3, dcot, dx3_all, dn2_sb, dn2_rb, dc2_sb, dc2_rb, dx1_all, dcv_all,
        dn1_sb, dn1_rb, df_sb, df_rb, dh, do_all, dqkv, dhc, dx1, dc2t, dad, dcn,
        gvs, gv_rb, gvx, gad, gad_rb, gad_all, turned,
    ) = take(65)
    (
        zs_send, zs_recv, s1_send, s1_recv, loc_sem, s2_send, s2_recv,
        v_send, v_recv, q_send, q_recv, h_send, h_recv, b_send, b_recv,
        xo_send, xo_recv, g_send, g_recv, a_send, a_recv, gx_send, gx_recv,
    ) = take(23)

    p = lax.axis_index("pipe")
    dpi = lax.axis_index("dp")
    x = lax.axis_index("tensor")
    rest = dpi % outer
    zi = dpi // (outer * R)
    ri = (dpi // outer) % R
    xo = 1 - x
    ro = 1 - ri
    d_dim, c_dim, hq, ffq, cfq, adq, dg = dims
    adh = Z * adq
    dz, cz = d_dim // Z, c_dim // Z
    tile = 256
    ids = {name: number for number, name in enumerate(ARRAYS)}
    ev = {name: number for number, name in enumerate(EVENTS)}

    def dev(z=None, rr=None, xx=None, pp=None):
        z = zi if z is None else z
        rr = ri if rr is None else rr
        return (
            p if pp is None else pp,
            (z * R + rr) * outer + rest,
            x if xx is None else xx,
        )

    def zto(d):
        return lax.rem(zi + d, Z)

    def zfrom(d):
        return lax.rem(zi + Z - d, Z)

    def remote(src, dst, ssem, rsem, device):
        return pltpu.make_async_remote_copy(
            src_ref=src, dst_ref=dst, send_sem=ssem, recv_sem=rsem,
            device_id=device, device_id_type=pl.DeviceIdType.MESH,
        )

    sib = dev(pp=1 - p)
    over_r, over_x = dev(rr=ro), dev(xx=xo)

    def z_copy(e, d, src, dst):
        return remote(src, dst, zs_send.at[e, d - 1], zs_recv.at[e, d - 1], dev(zto(d)))

    sent = []

    def gather_copies(name, buf):
        return [z_copy(ev[name], d, buf.at[zi], buf.at[zi]) for d in range(1, Z)]

    def gather_start(name, buf, keep=True):
        copies = gather_copies(name, buf)
        for c in copies:
            c.start()
        if keep:
            sent.extend(copies)

    def gather_wait(name, buf):
        for d in range(1, Z):
            slot = buf.at[zfrom(d)]
            z_copy(ev[name], d, slot, slot).wait_recv()

    def scatter_start(name, sb, rb):
        for d in range(1, Z):
            c = z_copy(ev[name], d, sb.at[zto(d)], rb.at[d - 1])
            c.start()
            sent.append(c)

    def scatter_wait(name, rb):
        for d in range(1, Z):
            z_copy(ev[name], d, rb.at[d - 1], rb.at[d - 1]).wait_recv()

    def share_start(name, buf):
        for d in range(1, Z):
            c = z_copy(ev[name], d, buf.at[3], buf.at[d - 1])
            c.start()
            sent.append(c)

    def scattered(sb, rb):
        return (wide(sb[zi]) + wide(rb[0])) + (wide(rb[1]) + wide(rb[2]))

    barrier = pltpu.get_barrier_semaphore()
    greeted = [sib]
    for d in range(1, Z):
        greeted += [dev(zto(d)), dev(zto(d), ro)]
    greeted += [over_r, over_x, dev(rr=ro, xx=xo)]
    for device in greeted:
        pl.semaphore_signal(barrier, inc=1, device_id=device, device_id_type=pl.DeviceIdType.MESH)
    v_loc[...] = jnp.zeros(v_loc.shape, F32)
    taps7 = depth_in.shape[0]
    c_own = depth_in.shape[1]
    v_loc[0:taps7, 0:c_own] = wide(depth_in[...])
    v_loc[49:50, 0:c_own] = wide(ln_conv_in[...])
    v_loc[50:51, 0:c_own] = wide(scale_in[...])
    v_loc[56:57, 0:LANE] = wide(ln_attn_in[...])
    v_loc[57:58, 0:LANE] = wide(ln_mlp_in[...])
    aq[x] = jnp.zeros(aq.shape[1:], F32)
    aq[x, 0:9] = wide(adapt_depth_in[:, lanes_of(zi, adq)])
    pl.semaphore_wait(barrier, len(greeted))

    me8 = zi * R + ri
    v_arrivals = []
    for n, (d, flip) in enumerate([(d, s) for d in range(Z) for s in (0, 1)][1:]):
        tr = ro if flip else ri
        c = remote(v_loc, vv.at[me8], v_send.at[n], v_recv.at[n], dev(zto(d), tr))
        c.start()
        sent.append(c)
        fr = zfrom(d) * R + tr
        v_arrivals.append(remote(vv.at[fr], vv.at[fr], v_send.at[n], v_recv.at[n], dev(zto(d), tr)))
    vv[me8] = v_loc[...]
    c = remote(aq.at[x], aq.at[x], q_send, q_recv, over_x)
    c.start()
    sent.append(c)

    by_rows = ("O", "F2")

    def quarter_of(name, ref, z):
        if name == "Q":
            return ref.at[:, :, lanes_of(z, hq)]
        if name in by_rows:
            height = ref.shape[0] // Z
            return ref.at[pl.ds(pl.multiple_of(z * height, height), height)]
        return ref.at[:, lanes_of(z, ref.shape[1] // Z)]

    def step1_local(name):
        return pltpu.make_async_copy(
            quarter_of(name, source[name], zi), W[name].at[x, zi, ri], loc_sem.at[ids[name]]
        )

    def step1_copy(name, d):
        k = ids[name]
        return remote(
            quarter_of(name, source[name], zto(d)), W[name].at[x, zi, ri],
            s1_send.at[k, d - 1], s1_recv.at[k, d - 1], dev(zto(d)),
        )

    def half_of(name, j, z, rr, upper):
        w = W[name]
        half = w.shape[-2] // 2
        rows = slice(half, None) if upper else slice(0, half)
        if len(w.shape) == 6:
            return w.at[j, z, rr, :, rows]
        return w.at[j, z, rr, rows]

    def step2_copy(name, which, d):
        k = ids[name]
        z = zfrom(d)
        if which < 2:
            src = quarter_of(name, source[name], zi) if d == 0 else W[name].at[x, z, ri]
            dst = W[name].at[x, z, ri]
        else:
            src = dst = half_of(name, x, z, ro, False) if which == 2 else half_of(name, xo, z, ri, True)
        to = over_x if which in (1, 2) else over_r
        return remote(src, dst, s2_send.at[k, which, d], s2_recv.at[k, which, d], to)

    def step2_arrival(name, which, d):
        k = ids[name]
        z = zfrom(d)
        if which < 2:
            ref = W[name].at[x, z, ro] if which == 0 else W[name].at[xo, z, ri]
        else:
            ref = half_of(name, xo, z, ro, which == 3)
        to = over_x if which in (1, 2) else over_r
        return remote(ref, ref, s2_send.at[k, which, d], s2_recv.at[k, which, d], to)

    def relay1(*names):
        for name in names:
            step1_local(name).start()
            for d in range(1, Z):
                step1_copy(name, d).start()
            step2_copy(name, 0, 0).start()
            step2_copy(name, 1, 0).start()

    def relay2(name, ds=(1, 2, 3)):
        k = ids[name]
        for d in ds:
            slot = W[name].at[x, zfrom(d), ri]
            remote(slot, slot, s1_send.at[k, d - 1], s1_recv.at[k, d - 1], dev(zto(d))).wait_recv()
            step2_copy(name, 0, d).start()
            step2_copy(name, 1, d).start()

    def relay3(name, ds=(0, 1, 2, 3)):
        for d in ds:
            step2_arrival(name, 0, d).wait_recv()
            step2_copy(name, 2, d).start()
            step2_arrival(name, 1, d).wait_recv()
            step2_copy(name, 3, d).start()

    def relay4(*names):
        for name in names:
            step1_local(name).wait()
            for d in range(Z):
                step2_arrival(name, 2, d).wait_recv()
                step2_arrival(name, 3, d).wait_recv()

    def relay_sent():
        for name in ARRAYS:
            for d in range(1, Z):
                step1_copy(name, d).wait_send()
            for which in range(4):
                for d in range(Z):
                    step2_copy(name, which, d).wait_send()

    relay1("P1", "P2")

    @pl.when(p == 1)
    def _():
        relay1("Q", "O")
        relay2("P1")
        relay1("E", "Gi", "Go")
        relay2("P2")
        relay1("F1")
        relay3("P1")
        relay2("Q")
        relay2("O")
        relay1("F2")
        relay3("P2")
        for name in ("E", "Gi", "Go"):
            relay2(name)
        relay2("F1")
        relay3("Q")
        relay3("O")
        relay2("F2")
        for name in ("E", "Gi", "Go"):
            relay3(name)
        relay3("F1")
        relay3("F2")

    for c in v_arrivals:
        c.wait_recv()
    remote(aq.at[xo], aq.at[xo], q_send, q_recv, over_x).wait_recv()
    low_lanes = lax.broadcasted_iota(jnp.int32, (64, LANE), 1) < LANE // 2
    for z in range(Z):
        first, second = vv[2 * z], pltpu.roll(vv[2 * z + 1], LANE // 2, 1)
        vec_c[:, z * cz : z * cz + LANE] = first[:, 0:LANE]
        vec_c[:, z * cz + LANE : z * cz + 2 * LANE] = jnp.where(
            low_lanes, first[:, LANE:], second[:, 0:LANE]
        )
        vec_c[:, z * cz + 2 * LANE : (z + 1) * cz] = second[:, LANE:]
    for i in range(Z * R):
        vec_d[:, i * LANE : (i + 1) * LANE] = vv[i, 56:64, 0:LANE]

    def gain_d(row):
        return vec_d[row : row + 1, :]

    def gain_c(row):
        return vec_c[row : row + 1, :]

    def token_entry():
        n_hat, _ = normed(wide(x_in[...]))
        n1_all[zi] = low(n_hat * gain_d(0))
        gather_start("n1", n1_all, keep=False)

    sent.extend(gather_copies("n1", n1_all))

    @pl.when(p == 0)
    def _():
        first = order_in[0, x] == 0
        c_in[...] = jnp.where(first, grid_in[0], grid_in[1])
        x_in[...] = jnp.where(first, tok_in[0], tok_in[1])
        token_entry()

    @pl.when(p == 1)
    def _():
        remote(c_in, c_in, h_send.at[1], h_recv.at[1], sib).wait_recv()

    @pl.loop(0, c_dim // LANE)
    def _(ch):
        lanes = lanes_of(ch, LANE)
        taps = vec_c[:, lanes]
        cn[:, lanes] = depthwise(wide(c_in[:, lanes]), lambda k: taps[k : k + 1], 7)

    n_hat, rs = normed(cn[...])
    cn[...] = n_hat
    crs[...] = jnp.broadcast_to(rs, crs.shape)
    f_all[zi] = low(n_hat * gain_c(49))
    gather_start("f", f_all)

    @pl.when(p == 0)
    def _():
        relay2("P1")
        relay1("Q", "O")
        relay2("P2")
        relay3("P1")
        relay2("Q")
        relay2("O")
        relay1("E", "Gi", "Go")
        relay3("P2", (0, 1))

    relay4("P1")
    gather_wait("f", f_all)

    def conv_hidden(j):
        @pl.loop(0, cfq // tile)
        def _(t):
            lanes = lanes_of(t, tile)
            act, der = gelu_pair(mm(flat(f_all[...]), flat(W["P1"][j, :, :, :, lanes])))
            r[j, :, lanes] = low(act)
            rp[j, :, lanes] = low(der)

    conv_hidden(0)

    @pl.when(p == 0)
    def _():
        relay3("P2", (2, 3))
        for name in ("E", "Gi", "Go"):
            relay2(name)
        relay1("F1")

    conv_hidden(1)

    @pl.when(p == 0)
    def _():
        relay3("Q")
        relay3("O")
        relay2("F1")
        relay1("F2")

    relay4("P2")

    @pl.loop(0, Z)
    def _(z):
        acc = mm_nt(r[0], flat(W["P2"][0, z])) + mm_nt(r[1], flat(W["P2"][1, z]))
        cv_sb[:, :, lanes_of(z, cz)] = low(acc).reshape(Z, TOK, cz)

    scatter_start("cv", cv_sb, cv_rb)

    @pl.when(p == 0)
    def _():
        for name in ("E", "Gi", "Go"):
            relay3(name)
        relay2("F2")

    @pl.when(p == 1)
    def _():
        remote(x_in, x_in, h_send.at[0], h_recv.at[0], sib).wait_recv()
        token_entry()

    relay4("Q", "O")
    gather_wait("n1", n1_all)
    for j in range(2):
        wj = side_by_side([flat(W["Q"][j, :, :, s]) for s in range(3)])
        qkv[j] = low(mm(flat(n1_all[...]), wj))
    for j in range(2):
        for b in range(Z):
            rows = slice(b * TOK, (b + 1) * TOK)
            outs = []
            for h in range(hq // HD):
                q, kk, vals = (qkv[j, rows, s * hq + h * HD : s * hq + (h + 1) * HD] for s in range(3))
                sc = mm_nt(q, kk) * HD ** (-0.5)
                e = jnp.exp(sc - jnp.max(sc, axis=-1, keepdims=True))
                pr = low(e / jnp.sum(e, axis=-1, keepdims=True))
                prob[j, h, b] = pr
                outs.append(mm(pr, vals))
            ctx[j, rows, :] = low(side_by_side(outs))

    def out_block(j, z):
        return side_by_side([W["O"][j, z, 0], W["O"][j, z, 1]])

    @pl.loop(0, Z)
    def _(z):
        both = jnp.concatenate([out_block(0, z), out_block(1, z)], axis=0)
        acc = mm(side_by_side([ctx[0], ctx[1]]), both)
        o_sb[:, :, lanes_of(z, dz)] = low(acc).reshape(Z, TOK, dz)

    scatter_start("o", o_sb, o_rb)

    @pl.when(p == 0)
    def _():
        relay3("F1")

    scatter_wait("cv", cv_rb)
    cv_sum[...] = scattered(cv_sb, cv_rb)
    c2f[...] = wide(c_in[...]) + gain_c(50) * cv_sum[...]
    c2_low = low(c2f[...])
    c2_all[zi] = c2_low
    gather_start("c2", c2_all)
    hid_grid[x] = c2_low

    @pl.when(p == 0)
    def _():
        remote(hid_grid.at[x], c_in, h_send.at[1], h_recv.at[1], sib).start()

    @pl.when(p == 0)
    def _():
        relay3("F2")

    scatter_wait("o", o_rb)
    x1[...] = wide(x_in[...]) + scattered(o_sb, o_rb)
    n_hat, _ = normed(x1[...])
    n2_all[zi] = low(n_hat * gain_d(1))
    gather_start("n2", n2_all)

    relay4("E", "Gi", "Go")
    gather_wait("c2", c2_all)
    row8 = lax.broadcasted_iota(jnp.int32, (8, adq), 0)
    gs_part = None
    for j in range(2):
        ad = mm(flat(c2_all[...]), flat(W["E"][j]))
        adapted[j] = ad
        taps = aq[j]
        pool = jnp.zeros((8, adq), F32)
        for b in range(Z):
            sp = depthwise(ad[b * TOK : (b + 1) * TOK], lambda k: taps[k : k + 1], 3)
            spread[j, b] = sp
            pool = jnp.where(row8 == b, jnp.mean(sp, axis=0, keepdims=True), pool)
        pooled[j] = pool
        term = mm_nt(low(pool), flat(W["Gi"][j]))
        gs_part = term if gs_part is None else gs_part + term
    gsb[3] = gs_part
    share_start("gs", gsb)

    relay4("F1")
    gather_wait("n2", n2_all)
    for j in range(2):

        @pl.loop(0, ffq // tile)
        def _(t):
            lanes = lanes_of(t, tile)
            act, der = gelu_pair(mm(flat(n2_all[...]), flat(W["F1"][j, :, :, :, lanes])))
            u[j, :, lanes] = low(act)
            up[j, :, lanes] = low(der)

    scatter_wait("gs", gsb)

    def gate_hidden():
        return gelu_pair((gsb[0] + gsb[1]) + (gsb[2] + gsb[3]))

    gh, _ = gate_hidden()
    for j in range(2):
        g8 = jnp.tanh(mm(low(gh), flat(W["Go"][j])))
        gate[j] = g8
        for b in range(Z):
            br_sb[b, :, j * adq : (j + 1) * adq] = low(g8[b : b + 1] * spread[j, b])
    scatter_start("br", br_sb, br_rb)
    relay4("F2")

    @pl.loop(0, Z)
    def _(z):
        acc = None
        for j in range(2):
            term = mm(u[j], side_by_side([W["F2"][j, z, 0], W["F2"][j, z, 1]]))
            acc = term if acc is None else acc + term
        m_sb[:, :, lanes_of(z, dz)] = low(acc).reshape(Z, TOK, dz)

    scatter_start("m", m_sb, m_rb)
    scatter_wait("br", br_rb)
    dx1[...] = x1[...]
    for d in range(Z):
        piece = br_sb[zi] if d == 0 else br_rb[d - 1]
        for j in range(2):
            lanes = pl.ds(pl.multiple_of(j * adh + zfrom(d) * adq, LANE), adq)
            dx1[:, lanes] += wide(piece[:, j * adq : (j + 1) * adq])
    scatter_wait("m", m_rb)
    hid_tok[x] = low(dx1[...] + scattered(m_sb, m_rb))

    @pl.when(p == 0)
    def _():
        remote(hid_tok.at[x], x_in, h_send.at[0], h_recv.at[0], sib).start()

    out_arrivals = []

    def exchange(n, buf):
        c = remote(buf.at[x], buf.at[x], xo_send.at[n], xo_recv.at[n], over_x)
        c.start()
        sent.append(c)
        out_arrivals.append(remote(buf.at[xo], buf.at[xo], xo_send.at[n], xo_recv.at[n], over_x))

    exchange(0, hid_tok)
    exchange(1, hid_grid)
    relay_sent()

    @pl.when(p == 1)
    def _():
        dx3[...] = tcot_in[x]
        dcot[...] = gcot_in[x]

    @pl.when(p == 0)
    def _():
        remote(dx3, dx3, b_send.at[0], b_recv.at[0], sib).wait_recv()

    dx3_all[zi] = dx3[...]
    gather_start("dx3", dx3_all)
    gather_wait("dx3", dx3_all)

    def own_lanes(j):
        return pl.ds(pl.multiple_of(j * adh + zi * adq, LANE), adq)

    gh, ghp = gate_hidden()
    dgh_part = None
    dgp = []
    for j in range(2):
        dgate = jnp.zeros((8, adq), F32)
        for b in range(Z):
            dbr = wide(dx3_all[b, :, own_lanes(j)])
            dgate = jnp.where(row8 == b, jnp.sum(dbr * spread[j, b], axis=0, keepdims=True), dgate)
        dg8 = low(dgate * (1.0 - gate[j] * gate[j]))
        dgp.append(dg8)
        term = mm_nt(dg8, flat(W["Go"][j]))
        dgh_part = term if dgh_part is None else dgh_part + term
    dgb[3] = dgh_part
    share_start("dgh", dgb)

    for j in range(2):

        @pl.loop(0, ffq // tile)
        def _(t):
            rows = lanes_of(t, tile)
            both = side_by_side([W["F2"][j, z, rr, rows] for z in range(Z) for rr in range(R)])
            du = mm_nt(flat(dx3_all[...]), both)
            dh[j, :, rows] = low(du * wide(up[j, :, rows]))

    scatter_wait("dgh", dgb)
    dgs = low(((dgb[0] + dgb[1]) + (dgb[2] + dgb[3])) * ghp)
    for j in range(2):
        dpool = mm(dgs, flat(W["Gi"][j])) * (1.0 / TOK)
        taps = aq[j]
        tap_rows = [None] * 9
        for b in range(Z):
            dsp = gate[j, b : b + 1] * wide(dx3_all[b, :, own_lanes(j)]) + dpool[b : b + 1]
            dad[j, b * TOK : (b + 1) * TOK] = low(depthwise(dsp, lambda k: taps[8 - k : 9 - k], 3))

            def put(k, row):
                tap_rows[k] = row if tap_rows[k] is None else tap_rows[k] + row

            depthwise_taps(adapted[j, b * TOK : (b + 1) * TOK], dsp, 3, put)
        for k in range(9):
            gad[j, k : k + 1] = tap_rows[k]
        gad[j, 9:16] = jnp.zeros((7, adq), F32)

    @pl.loop(0, Z)
    def _(z):
        acc = mm_nt(dad[0], flat(W["E"][0, z])) + mm_nt(dad[1], flat(W["E"][1, z]))
        dc2_sb[:, :, lanes_of(z, cz)] = low(acc).reshape(Z, TOK, cz)

    scatter_start("dc2", dc2_sb, dc2_rb)

    @pl.loop(0, Z)
    def _(z):
        acc = mm_nt(dh[0], flat(W["F1"][0, z])) + mm_nt(dh[1], flat(W["F1"][1, z]))
        dn2_sb[:, :, lanes_of(z, dz)] = low(acc).reshape(Z, TOK, dz)

    scatter_start("dn2", dn2_sb, dn2_rb)

    peers = ((1, 0), (0, 1), (1, 1))

    def owner(k):
        return (ro if peers[k][0] else ri), (xo if peers[k][1] else x)

    def reduce_copy(name, k):
        rr, xx = owner(k)
        n = ids[name]
        return remote(W[name].at[xx, :, rr], RX[name].at[k], g_send.at[n, k], g_recv.at[n, k], dev(rr=rr, xx=xx))

    def reduce_start(name):
        for k in (2, 0, 1):
            reduce_copy(name, k).start()

    def row_grad(name, left, right):
        width = W[name].shape[3]
        span = R * width

        @pl.loop(0, Z)
        def _(z):
            turned[0:span] = flat(left[:, :, lanes_of(z, span)]).T
            for j in range(2):
                W[name][j, z] = low(mm(turned[0:span], right[j])).reshape(R, width, -1)

        reduce_start(name)

    def col_grad(name, left, right):
        width = left.shape[2]
        for j in range(2):
            turned[j * width : (j + 1) * width] = left[j].T

        @pl.loop(0, Z)
        def _(z):
            rhs = flat(right[:, :, lanes_of(z, dz)])
            for j in range(2):
                g = low(mm(turned[j * width : (j + 1) * width], rhs))
                for rr in range(R):
                    W[name][j, z, rr] = g[:, rr * LANE : (rr + 1) * LANE]

        reduce_start(name)

    for j in range(2):
        W["Gi"][j] = low(mm_tn(dgs, low(pooled[j]))).reshape(Z, R, -1, adq)
        W["Go"][j] = low(mm_tn(low(gh), dgp[j])).reshape(Z, R, -1, adq)
    reduce_start("Gi")
    reduce_start("Go")
    row_grad("E", c2_all, dad)

    @pl.when(p == 0)
    def _():
        remote(dcot, dcot, b_send.at[1], b_recv.at[1], sib).wait_recv()

    scatter_wait("dc2", dc2_rb)
    dc2t[...] = wide(dcot[...]) + scattered(dc2_sb, dc2_rb)
    gvs_ls = jnp.sum(cv_sum[...] * dc2t[...], axis=0, keepdims=True)
    dcv_all[zi] = low(dc2t[...] * gain_c(50))
    gather_start("dcv", dcv_all)

    scatter_wait("dn2", dn2_rb)
    dn2 = scattered(dn2_sb, dn2_rb)
    n_hat, rs = normed(x1[...])
    gvs_d1 = jnp.sum(dn2 * n_hat, axis=0, keepdims=True)
    dx1[...] = wide(dx3[...]) + norm_back(dn2, n_hat, rs, gain_d(1))
    dx1_all[zi] = low(dx1[...])
    gather_start("dx1", dx1_all)

    col_grad("F2", u, dx3_all)
    row_grad("F1", n2_all, dh)

    gather_wait("dcv", dcv_all)
    for j in range(2):

        @pl.loop(0, cfq // tile)
        def _(t):
            lanes = lanes_of(t, tile)
            dr = mm(flat(dcv_all[...]), flat(W["P2"][j, :, :, :, lanes]))
            dhc[j, :, lanes] = low(dr * wide(rp[j, :, lanes]))

    @pl.loop(0, Z)
    def _(z):
        acc = mm_nt(dhc[0], flat(W["P1"][0, z])) + mm_nt(dhc[1], flat(W["P1"][1, z]))
        df_sb[:, :, lanes_of(z, cz)] = low(acc).reshape(Z, TOK, cz)

    scatter_start("df", df_sb, df_rb)

    gather_wait("dx1", dx1_all)
    for j in range(2):
        both = side_by_side([W["O"][j, z, rr] for z in range(Z) for rr in range(R)])
        do_all[j] = low(mm_nt(flat(dx1_all[...]), both))
    for j in range(2):
        for b in range(Z):
            rows = slice(b * TOK, (b + 1) * TOK)
            parts = [[], [], []]
            for h in range(hq // HD):
                q, kk, vals = (qkv[j, rows, s * hq + h * HD : s * hq + (h + 1) * HD] for s in range(3))
                do = do_all[j, rows, h * HD : (h + 1) * HD]
                pr = prob[j, h, b]
                dp = mm_nt(do, vals)
                prw = wide(pr)
                ds = low(prw * (dp - jnp.sum(dp * prw, axis=-1, keepdims=True)) * HD ** (-0.5))
                parts[0].append(mm(ds, kk))
                parts[1].append(mm_tn(ds, q))
                parts[2].append(mm_tn(pr, do))
            for s in range(3):
                dqkv[j, rows, s * hq : (s + 1) * hq] = low(side_by_side(parts[s]))

    @pl.loop(0, Z)
    def _(z):
        acc = None
        for j in range(2):
            term = mm_nt(dqkv[j], side_by_side([flat(W["Q"][j, z, :, s]) for s in range(3)]))
            acc = term if acc is None else acc + term
        dn1_sb[:, :, lanes_of(z, dz)] = low(acc).reshape(Z, TOK, dz)

    scatter_start("dn1", dn1_sb, dn1_rb)

    def pw_grads():
        row_grad("P2", dcv_all, r)
        row_grad("P1", f_all, dhc)

    @pl.when(p == 0)
    def _():
        pw_grads()

    scatter_wait("dn1", dn1_rb)
    dn1 = scattered(dn1_sb, dn1_rb)
    n_hat, rs = normed(wide(x_in[...]))
    gvs_d0 = jnp.sum(dn1 * n_hat, axis=0, keepdims=True)
    out_gtok[x] = low(dx1[...] + norm_back(dn1, n_hat, rs, gain_d(0)))

    @pl.when(p == 1)
    def _():
        remote(out_gtok.at[x], dx3, b_send.at[0], b_recv.at[0], sib).start()

    scatter_wait("df", df_rb)
    dfv = scattered(df_sb, df_rb)
    gvs_lc = jnp.sum(dfv * cn[...], axis=0, keepdims=True)
    dcn[...] = norm_back(dfv, cn[...], crs[:, 0:1], gain_c(49))

    @pl.loop(0, c_dim // LANE)
    def _(ch):
        lanes = lanes_of(ch, LANE)
        taps = vec_c[:, lanes]
        back = depthwise(dcn[:, lanes], lambda k: taps[48 - k : 49 - k], 7)
        out_ggrid[x, :, lanes] = low(dc2t[:, lanes] + back)

    @pl.when(p == 1)
    def _():
        remote(out_ggrid.at[x], dcot, b_send.at[1], b_recv.at[1], sib).start()
        pw_grads()

    @pl.loop(0, Z)
    def _(z):
        turned[0:dz] = flat(n1_all[:, :, lanes_of(z, dz)]).T
        for j in range(2):
            g = low(mm(turned[0:dz], dqkv[j]))
            for s in range(3):
                W["Q"][j, z, :, s] = g[:, s * hq : (s + 1) * hq].reshape(R, -1, hq)

    reduce_start("Q")
    col_grad("O", ctx, dx1_all)

    exchange(2, out_gtok)
    exchange(3, out_ggrid)

    @pl.loop(0, Z)
    def _(z):
        for part in range(cz // LANE):
            lanes = pl.ds(pl.multiple_of(z * cz + part * LANE, LANE), LANE)

            def put(k, row):
                gvs[z, k : k + 1, part * LANE : (part + 1) * LANE] = row

            depthwise_taps(wide(c_in[:, lanes]), dcn[:, lanes], 7, put)

    for z in range(Z):
        gvs[z, 49:50] = gvs_lc[:, z * cz : (z + 1) * cz]
        gvs[z, 50:51] = gvs_ls[:, z * cz : (z + 1) * cz]
        gvs[z, 51:64] = jnp.zeros((13, cz), F32)
        gvs[z, 56:57, 0:dz] = gvs_d0[:, z * dz : (z + 1) * dz]
        gvs[z, 57:58, 0:dz] = gvs_d1[:, z * dz : (z + 1) * dz]
    scatter_start("gv", gvs, gv_rb)

    def group_copy(n, k, src, dst):
        rr, xx = owner(k)
        return remote(src, dst, gx_send.at[n, k], gx_recv.at[n, k], dev(rr=rr, xx=xx))

    for k in range(3):
        c = group_copy(1, k, gad, gad_rb.at[k])
        c.start()
        sent.append(c)
    scatter_wait("gv", gv_rb)
    gvx[3] = (gvs[zi] + gv_rb[0]) + (gv_rb[1] + gv_rb[2])
    for k in range(3):
        c = group_copy(0, k, gvx.at[3], gvx.at[k])
        c.start()
        sent.append(c)
    for k in range(3):
        group_copy(1, k, gad, gad_rb.at[k]).wait_recv()
    gad_all[zi] = (gad[x] + gad_rb[0, x]) + (gad_rb[1, x] + gad_rb[2, x])
    gather_start("gad", gad_all)

    def back_copy(name, d):
        n = ids[name]
        return remote(
            RX[name].at[0, zto(d)], quarter_of(name, native[name], zi),
            a_send.at[n, d - 1], a_recv.at[n, d - 1], dev(zto(d)),
        )

    def back_local(name):
        return pltpu.make_async_copy(
            RX[name].at[0, zi], quarter_of(name, native[name], zi), loc_sem.at[ids[name]]
        )

    for name in ("Gi", "Go", "E", "F2", "F1", "P2", "P1", "Q", "O"):
        n = ids[name]
        rx = RX[name]
        for k in range(3):
            reduce_copy(name, k).wait_recv()

        @pl.loop(0, Z)
        def _(z):
            total = (wide(W[name][x, z, ri]) + wide(rx[0, z])) + (wide(rx[1, z]) + wide(rx[2, z]))
            rx[0, z] = low(total)

        for d in range(1, Z):
            back_copy(name, d).start()
        back_local(name).start()

    for k in range(3):
        group_copy(0, k, gvx.at[k], gvx.at[k]).wait_recv()
    total = (gvx[0] + gvx[1]) + (gvx[2] + gvx[3])
    mine = jnp.where(ri == 1, pltpu.roll(total, c_own, 1), total)[:, 0:c_own]
    mine_d = jnp.where(ri == 1, total[:, LANE : 2 * LANE], total[:, 0:LANE])

    def flag(n):
        return train_in[0, n].astype(F32)

    out_depth[...] = mine[0:taps7] * flag(0)
    out_ln_conv[...] = mine[49:50] * flag(1)
    out_scale[...] = mine[50:51] * flag(4)
    out_ln_attn[...] = mine_d[56:57]
    out_ln_mlp[...] = mine_d[57:58]
    gather_wait("gad", gad_all)
    for z in range(Z):
        out_ad[:, z * adq : (z + 1) * adq] = gad_all[z][0:9]
    for name in ARRAYS:
        back_local(name).wait()
        for d in range(1, Z):
            n = ids[name]
            slot = quarter_of(name, native[name], zfrom(d))
            remote(slot, slot, a_send.at[n, d - 1], a_recv.at[n, d - 1], dev(zto(d))).wait_recv()
    for c in out_arrivals:
        c.wait_recv()

    @pl.when(p == 0)
    def _():
        remote(hid_tok.at[x], x_in, h_send.at[0], h_recv.at[0], sib).wait_send()
        remote(hid_grid.at[x], c_in, h_send.at[1], h_recv.at[1], sib).wait_send()

    @pl.when(p == 1)
    def _():
        remote(out_gtok.at[x], dx3, b_send.at[0], b_recv.at[0], sib).wait_send()
        remote(out_ggrid.at[x], dcot, b_send.at[1], b_recv.at[1], sib).wait_send()

    for c in sent:
        c.wait_send()
    for name in ARRAYS:
        for k in range(3):
            reduce_copy(name, k).wait_send()
        for d in range(1, Z):
            back_copy(name, d).wait_send()


def run_layers(weights, vectors, order, train, streams, sizes, outer):
    d_dim, c_dim, hq, ffq, cfq, adw, dg = sizes
    vm = pltpu.VMEM
    blocks = []
    for name, value in zip(ARRAYS, weights):
        if name == "Q":
            blocks.append((3, value.shape[1], hq))
        elif name in ("O", "F2"):
            blocks.append((value.shape[0] // Z, value.shape[1]))
        else:
            blocks.append((value.shape[0], value.shape[1] // Z))
    rows = Z * TOK

    def act(width, count=Z, kind=BF):
        return vm((count, TOK, width), kind)

    scratch = [vm((2, Z, R) + s, BF) for s in blocks] + [vm((3, Z) + s, BF) for s in blocks]
    scratch += [
        vm((64, 2 * LANE), F32), vm((Z * R, 64, 2 * LANE), F32), vm((2, 16, adw), F32), vm((64, c_dim), F32), vm((8, d_dim), F32),
        vm((TOK, d_dim), BF), vm((TOK, c_dim), BF), act(d_dim), act(c_dim), act(d_dim), act(c_dim),
        act(d_dim), act(d_dim, 3), act(c_dim), act(c_dim, 3), act(d_dim), act(d_dim, 3),
        act(2 * adw), act(2 * adw, 3), vm((4, 8, dg), F32), vm((4, 8, dg), F32),
        vm((2, rows, 3 * hq), BF), vm((2, hq // HD, Z, TOK, TOK), BF), vm((2, rows, hq), BF),
        vm((2, rows, ffq), BF), vm((2, rows, ffq), BF), vm((2, rows, cfq), BF), vm((2, rows, cfq), BF),
        vm((TOK, c_dim), F32), vm((TOK, LANE), F32), vm((TOK, c_dim), F32), vm((TOK, d_dim), F32), vm((TOK, c_dim), F32),
        vm((2, rows, adw), F32), vm((2, Z, TOK, adw), F32), vm((2, 8, adw), F32), vm((2, 8, adw), F32),
        vm((TOK, d_dim), BF), vm((TOK, c_dim), BF), act(d_dim), act(d_dim), act(d_dim, 3), act(c_dim), act(c_dim, 3),
        act(d_dim), act(c_dim),
        act(d_dim), act(d_dim, 3), act(c_dim), act(c_dim, 3), vm((2, rows, ffq), BF), vm((2, rows, hq), BF),
        vm((2, rows, 3 * hq), BF), vm((2, rows, cfq), BF), vm((TOK, d_dim), F32), vm((TOK, c_dim), F32), vm((2, rows, adw), BF),
        vm((TOK, c_dim), F32),
        vm((Z, 64, c_dim // Z), F32), vm((3, 64, c_dim // Z), F32), vm((4, 64, c_dim // Z), F32),
        vm((2, 16, adw), F32), vm((3, 2, 16, adw), F32), vm((Z, 16, adw), F32),
        vm((2 * ffq, rows), BF),
    ]
    dma = pltpu.SemaphoreType.DMA
    na = len(ARRAYS)
    scratch += [
        dma((len(EVENTS), 3)), dma((len(EVENTS), 3)), dma((na, 3)), dma((na, 3)), dma((na,)),
        dma((na, 4, Z)), dma((na, 4, Z)), dma((7,)), dma((7,)), dma, dma, dma((2,)), dma((2,)), dma((2,)), dma((2,)),
        dma((4,)), dma((4,)), dma((na, 3)), dma((na, 3)), dma((na, 3)), dma((na, 3)), dma((2, 3)), dma((2, 3)),
    ]
    sds = jax.ShapeDtypeStruct
    out_shape = [sds((2, TOK, d_dim), BF), sds((2, TOK, c_dim), BF)] * 2
    out_shape += [sds(value.shape, BF) for value in weights]
    out_shape += [sds(value.shape, F32) for value in vectors]
    any_spec = pl.BlockSpec(memory_space=pl.ANY)
    vm_spec = pl.BlockSpec(memory_space=pltpu.VMEM)
    sm_spec = pl.BlockSpec(memory_space=pltpu.SMEM)
    return pl.pallas_call(
        functools.partial(main_kernel, sizes, outer),
        out_shape=out_shape,
        in_specs=[any_spec] * na + [vm_spec] * 6 + [sm_spec] * 2 + [vm_spec] * 4,
        out_specs=[vm_spec] * 4 + [any_spec] * na + [vm_spec] * 6,
        scratch_shapes=scratch,
        compiler_params=pltpu.CompilerParams(
            collective_id=0, has_side_effects=True, vmem_limit_bytes=62 * 1024 * 1024
        ),
        cost_estimate=pl.CostEstimate(flops=26 * 10**9, bytes_accessed=10**8, transcendentals=10**7),
        name="layers",
    )(*weights, *vectors, order, train, *streams)


def per_device(
    tokens,
    conv_grid,
    order,
    trainable,
    ln_attn,
    w_qkv,
    w_attn_out,
    ln_mlp,
    w_fc_in,
    w_fc_out,
    conv_depth,
    ln_conv,
    w_pw_in,
    w_pw_out,
    layer_scale,
    w_adapt,
    adapt_depth,
    w_gate_in,
    w_gate_out,
    tok_cot,
    grid_cot,
):
    dp_count = lax.axis_size("dp")
    outer = dp_count // (Z * R)
    groups = [[g * outer + o for o in range(outer)] for g in range(Z * R)]
    layer_at = lax.axis_index("pipe")

    def block(value, axis):
        value = value[0]
        if outer == 1:
            return value
        return lax.all_gather(value, "dp", axis=axis, tiled=True, axis_index_groups=groups)

    def share(value, axis):
        if outer > 1:
            value = lax.psum_scatter(
                value, "dp", scatter_dimension=axis, tiled=True, axis_index_groups=groups
            )
        return value[None]

    qkv = block(w_qkv, 1)
    gate_in = block(w_gate_in, 1).T
    pw_in = block(w_pw_in, 0)
    adapt = block(w_adapt, 0)
    fc_in = block(w_fc_in, 0)
    weights = (
        pw_in,
        block(w_pw_out, 1).T,
        qkv,
        block(w_attn_out, 1),
        adapt,
        gate_in,
        block(w_gate_out, 0),
        fc_in,
        block(w_fc_out, 1),
    )
    vectors = (
        block(conv_depth, 1),
        block(ln_conv, 0)[None],
        block(layer_scale, 0)[None],
        block(ln_attn, 0)[None],
        block(ln_mlp, 0)[None],
        adapt_depth[0],
    )
    spread = Z * R
    sizes = (
        qkv.shape[1] * spread, pw_in.shape[0] * spread, qkv.shape[2] // Z, fc_in.shape[1] // Z,
        pw_in.shape[1] // Z, adapt.shape[1] // Z, gate_in.shape[0] * spread,
    )

    def rows_of(value):
        return value.reshape(value.shape[0], TOK, value.shape[-1])

    streams = [rows_of(value) for value in (tokens, conv_grid, tok_cot, grid_cot)]
    outs = run_layers(weights, vectors, order, trainable, streams, sizes, outer)
    hid_tok, hid_grid, g_tok, g_grid = outs[:4]
    g_p1, g_p2, g_q, g_o, g_e, g_gi, g_go, g_f1, g_f2 = [value.astype(F32) for value in outs[4:13]]
    g_depth, g_ln_conv, g_scale, g_ln_attn, g_ln_mlp, g_ad = outs[13:]

    swap = (layer_at == 0) & (order[0, 0] == 1)
    g_tok = jnp.where(swap, g_tok[::-1], g_tok)
    g_grid = jnp.where(swap, g_grid[::-1], g_grid)
    grid_shape = (1,) + conv_grid.shape
    tok_shape = (1,) + tokens.shape
    flags = trainable[0].astype(F32)
    if outer > 1:
        g_ad = lax.psum(g_ad, "dp", axis_index_groups=groups)
    return (
        hid_tok.reshape(tok_shape),
        hid_grid.reshape(grid_shape),
        g_tok.reshape(tok_shape),
        g_grid.reshape(grid_shape),
        share(g_ln_attn[0], 0),
        share(g_q, 1),
        share(g_o, 1),
        share(g_ln_mlp[0], 0),
        share(g_f1, 0),
        share(g_f2, 1),
        share(g_depth, 1),
        share(g_ln_conv[0], 0),
        share(g_p1 * flags[2], 0),
        share((g_p2 * flags[3]).T, 1),
        share(g_scale[0], 0),
        share(g_e, 0),
        g_ad[None],
        share(g_gi.T, 1),
        share(g_go, 0),
    )


def solution(mesh):
    in_specs = (
        P(None, "dp", None, None),
        P(None, "dp", None, None, None),
        P("dp", None),
        P("pipe", None),
        P("pipe", "dp"),
        P("pipe", None, "dp", "tensor"),
        P("pipe", "tensor", "dp"),
        P("pipe", "dp"),
        P("pipe", "dp", "tensor"),
        P("pipe", "tensor", "dp"),
        P("pipe", None, "dp"),
        P("pipe", "dp"),
        P("pipe", "dp", "tensor"),
        P("pipe", "tensor", "dp"),
        P("pipe", "dp"),
        P("pipe", "dp", "tensor"),
        P("pipe", None, "tensor"),
        P("pipe", "tensor", "dp"),
        P("pipe", "dp", "tensor"),
        P(None, "dp", None, None),
        P(None, "dp", None, None, None),
    )
    out_specs = (
        P("pipe", None, "dp", None, None),
        P("pipe", None, "dp", None, None, None),
        P("pipe", None, "dp", None, None),
        P("pipe", None, "dp", None, None, None),
        P("pipe", "dp"),
        P("pipe", None, "dp", "tensor"),
        P("pipe", "tensor", "dp"),
        P("pipe", "dp"),
        P("pipe", "dp", "tensor"),
        P("pipe", "tensor", "dp"),
        P("pipe", None, "dp"),
        P("pipe", "dp"),
        P("pipe", "dp", "tensor"),
        P("pipe", "tensor", "dp"),
        P("pipe", "dp"),
        P("pipe", "dp", "tensor"),
        P("pipe", None, "tensor"),
        P("pipe", "tensor", "dp"),
        P("pipe", "dp", "tensor"),
    )
    return jax.shard_map(
        per_device, mesh=mesh, in_specs=in_specs, out_specs=out_specs, check_vma=False
    )
```

```python
import functools

import jax
import jax.numpy as jnp
from jax import lax
from jax.experimental import pallas as pl
from jax.experimental.pallas import tpu as pltpu
from jax.sharding import PartitionSpec as P

HD = 64
Z = 4
R = 2
TOK = 64
SIDE = 8
LANE = 128
BF = jnp.bfloat16
F32 = jnp.float32
ARRAYS = ("P1", "P2", "Q", "O", "E", "Gi", "Go", "F1", "F2")
EVENTS = (
    "n1", "f", "o", "cv", "n2", "c2", "m", "br", "gs",
    "dx3", "dgh", "dn2", "dc2", "dx1", "dcv", "dn1", "df", "gv", "gad",
)


def mm(a, b):
    return lax.dot_general(a, b, (((1,), (0,)), ((), ())), preferred_element_type=F32)


def mm_nt(a, b):
    return lax.dot_general(a, b, (((1,), (1,)), ((), ())), preferred_element_type=F32)


def mm_tn(a, b):
    return lax.dot_general(a, b, (((0,), (0,)), ((), ())), preferred_element_type=F32)


def flat(value):
    return value.reshape(-1, value.shape[-1])


def low(value):
    return value.astype(BF)


def wide(value):
    return value.astype(F32)


def gelu_pair(h):
    phi = 0.5 * (1.0 + lax.erf(h * 0.7071067811865476))
    dens = jnp.exp(-0.5 * h * h) * 0.3989422804014327
    return h * phi, phi + h * dens


def normed(value):
    centred = value - jnp.mean(value, axis=-1, keepdims=True)
    rs = lax.rsqrt(jnp.mean(centred * centred, axis=-1, keepdims=True) + 1e-06)
    return centred * rs, rs


def norm_back(dn, n_hat, rs, gain):
    gd = dn * gain
    return (
        gd
        - jnp.mean(gd, axis=-1, keepdims=True)
        - n_hat * jnp.mean(gd * n_hat, axis=-1, keepdims=True)
    ) * rs


def col_shift(value, by):
    if by == 0:
        return value
    at = lax.broadcasted_iota(jnp.int32, value.shape, 0) % SIDE
    rolled = pltpu.roll(value, (-by) % TOK, 0)
    return jnp.where((at + by >= 0) & (at + by < SIDE), rolled, 0.0)


def row_shift(value, by):
    if by == 0:
        return value
    gap = jnp.zeros((abs(by) * SIDE, value.shape[1]), value.dtype)
    if by > 0:
        return jnp.concatenate([value[by * SIDE :], gap], axis=0)
    return jnp.concatenate([gap, value[: TOK + by * SIDE]], axis=0)


def depthwise(value, tap, side):
    half = side // 2
    shifted = [col_shift(value, b - half) for b in range(side)]
    total = None
    for a in range(side):
        line = None
        for b in range(side):
            term = shifted[b] * tap(a * side + b)
            line = term if line is None else line + term
        line = row_shift(line, a - half)
        total = line if total is None else total + line
    return total


def depthwise_taps(value, grad, side, put):
    half = side // 2
    shifted = [col_shift(value, b - half) for b in range(side)]
    for a in range(side):
        d = a - half
        lo, hi = max(0, -d) * SIDE, (SIDE - max(0, d)) * SIDE
        for b in range(side):
            part = shifted[b][lo + d * SIDE : hi + d * SIDE] * grad[lo:hi]
            put(a * side + b, jnp.sum(part, axis=0, keepdims=True))


def lanes_of(at, width):
    return pl.ds(pl.multiple_of(at * width, width), width)


def side_by_side(blocks):
    return jnp.concatenate(blocks, axis=1)


def main_kernel(dims, outer, *refs):
    at = iter(refs)

    def take(count):
        return [next(at) for _ in range(count)]

    na = len(ARRAYS)
    source = dict(zip(ARRAYS, take(na)))
    (
        depth_in, ln_conv_in, scale_in, ln_attn_in, ln_mlp_in, adapt_depth_in,
        order_in, train_in, tok_in, grid_in, tcot_in, gcot_in,
    ) = take(12)
    hid_tok, hid_grid, out_gtok, out_ggrid = take(4)
    native = dict(zip(ARRAYS, take(na)))
    out_depth, out_ln_conv, out_scale, out_ln_attn, out_ln_mlp, out_ad = take(6)
    W = dict(zip(ARRAYS, take(na)))
    hops = take(4 * na)
    RX = {name: hops[4 * n : 4 * n + 4] for n, name in enumerate(ARRAYS)}
    (
        v_loc, vv, aq, vec_c, vec_d, x_in, c_in, n1_all, f_all, n2_all, c2_all,
        o_sb, o_rb, cv_sb, cv_rb, m_sb, m_rb, br_sb, br_rb, gsb, dgb,
        qkv, prob, ctx, u, up, r, rp, cn, crs, cv_sum, x1, c2f,
        adapted, spread, pooled, gate,
        dx3, dcot, dx3_all, dn2_sb, dn2_rb, dc2_sb, dc2_rb, dx1_all, dcv_all,
        dn1_sb, dn1_rb, df_sb, df_rb, dh, do_all, dqkv, dhc, dx1, dc2t, dad, dcn,
        gvs, gv_rb, gvx, gad, gad_rb, gad_all, turned,
    ) = take(65)
    (
        zs_send, zs_recv, s1_send, s1_recv, loc_sem, s2_send, s2_recv,
        v_send, v_recv, q_send, q_recv, h_send, h_recv, b_send, b_recv,
        xo_send, xo_recv, g_send, g_recv, a_send, a_recv, gx_send, gx_recv, go,
    ) = take(24)

    p = lax.axis_index("pipe")
    dpi = lax.axis_index("dp")
    x = lax.axis_index("tensor")
    rest = dpi % outer
    zi = dpi // (outer * R)
    ri = (dpi // outer) % R
    xo = 1 - x
    ro = 1 - ri
    d_dim, c_dim, hq, ffq, cfq, adq, dg = dims
    adh = Z * adq
    dz, cz = d_dim // Z, c_dim // Z
    tile = 256
    ids = {name: number for number, name in enumerate(ARRAYS)}
    ev = {name: number for number, name in enumerate(EVENTS)}

    def dev(z=None, rr=None, xx=None, pp=None):
        z = zi if z is None else z
        rr = ri if rr is None else rr
        return (
            p if pp is None else pp,
            (z * R + rr) * outer + rest,
            x if xx is None else xx,
        )

    def zto(d):
        return lax.rem(zi + d, Z)

    def zfrom(d):
        return lax.rem(zi + Z - d, Z)

    def remote(src, dst, ssem, rsem, device):
        return pltpu.make_async_remote_copy(
            src_ref=src, dst_ref=dst, send_sem=ssem, recv_sem=rsem,
            device_id=device, device_id_type=pl.DeviceIdType.MESH,
        )

    sib = dev(pp=1 - p)
    over_r, over_x = dev(rr=ro), dev(xx=xo)

    def z_copy(e, d, src, dst):
        return remote(src, dst, zs_send.at[e, d - 1], zs_recv.at[e, d - 1], dev(zto(d)))

    sent = []

    def gather_copies(name, buf):
        return [z_copy(ev[name], d, buf.at[zi], buf.at[zi]) for d in range(1, Z)]

    def gather_start(name, buf, keep=True):
        copies = gather_copies(name, buf)
        for c in copies:
            c.start()
        if keep:
            sent.extend(copies)

    def gather_wait(name, buf):
        for d in range(1, Z):
            slot = buf.at[zfrom(d)]
            z_copy(ev[name], d, slot, slot).wait_recv()

    def scatter_start(name, sb, rb):
        for d in range(1, Z):
            c = z_copy(ev[name], d, sb.at[zto(d)], rb.at[d - 1])
            c.start()
            sent.append(c)

    def scatter_wait(name, rb):
        for d in range(1, Z):
            z_copy(ev[name], d, rb.at[d - 1], rb.at[d - 1]).wait_recv()

    def share_start(name, buf):
        for d in range(1, Z):
            c = z_copy(ev[name], d, buf.at[3], buf.at[d - 1])
            c.start()
            sent.append(c)

    def scattered(sb, rb):
        return (wide(sb[zi]) + wide(rb[0])) + (wide(rb[1]) + wide(rb[2]))

    barrier = pltpu.get_barrier_semaphore()
    greeted = [sib]
    for d in range(1, Z):
        greeted += [dev(zto(d)), dev(zto(d), ro)]
    greeted += [over_r, over_x, dev(rr=ro, xx=xo)]
    for device in greeted:
        pl.semaphore_signal(barrier, inc=1, device_id=device, device_id_type=pl.DeviceIdType.MESH)
    v_loc[...] = jnp.zeros(v_loc.shape, F32)
    taps7 = depth_in.shape[0]
    c_own = depth_in.shape[1]
    v_loc[0:taps7, 0:c_own] = wide(depth_in[...])
    v_loc[49:50, 0:c_own] = wide(ln_conv_in[...])
    v_loc[50:51, 0:c_own] = wide(scale_in[...])
    v_loc[56:57, 0:LANE] = wide(ln_attn_in[...])
    v_loc[57:58, 0:LANE] = wide(ln_mlp_in[...])
    aq[x] = jnp.zeros(aq.shape[1:], F32)
    aq[x, 0:9] = wide(adapt_depth_in[:, lanes_of(zi, adq)])
    pl.semaphore_wait(barrier, len(greeted))

    me8 = zi * R + ri
    v_arrivals = []
    for n, (d, flip) in enumerate([(d, s) for d in range(Z) for s in (0, 1)][1:]):
        tr = ro if flip else ri
        c = remote(v_loc, vv.at[me8], v_send.at[n], v_recv.at[n], dev(zto(d), tr))
        c.start()
        sent.append(c)
        fr = zfrom(d) * R + tr
        v_arrivals.append(remote(vv.at[fr], vv.at[fr], v_send.at[n], v_recv.at[n], dev(zto(d), tr)))
    vv[me8] = v_loc[...]
    c = remote(aq.at[x], aq.at[x], q_send, q_recv, over_x)
    c.start()
    sent.append(c)

    by_rows = ("O", "F2")

    def quarter_of(name, ref, z):
        if name == "Q":
            return ref.at[:, :, lanes_of(z, hq)]
        if name in by_rows:
            height = ref.shape[0] // Z
            return ref.at[pl.ds(pl.multiple_of(z * height, height), height)]
        return ref.at[:, lanes_of(z, ref.shape[1] // Z)]

    def step1_local(name):
        return pltpu.make_async_copy(
            quarter_of(name, source[name], zi), W[name].at[x, zi, ri], loc_sem.at[ids[name]]
        )

    def step1_copy(name, d):
        k = ids[name]
        return remote(
            quarter_of(name, source[name], zto(d)), W[name].at[x, zi, ri],
            s1_send.at[k, d - 1], s1_recv.at[k, d - 1], dev(zto(d)),
        )

    def half_of(name, j, z, rr, upper):
        w = W[name]
        half = w.shape[-2] // 2
        rows = slice(half, None) if upper else slice(0, half)
        if len(w.shape) == 6:
            return w.at[j, z, rr, :, rows]
        return w.at[j, z, rr, rows]

    def step2_copy(name, which, d):
        k = ids[name]
        z = zfrom(d)
        if which < 2:
            src = quarter_of(name, source[name], zi) if d == 0 else W[name].at[x, z, ri]
            dst = W[name].at[x, z, ri]
        else:
            src = dst = half_of(name, x, z, ro, False) if which == 2 else half_of(name, xo, z, ri, True)
        to = over_x if which in (1, 2) else over_r
        return remote(src, dst, s2_send.at[k, which, d], s2_recv.at[k, which, d], to)

    def step2_arrival(name, which, d):
        k = ids[name]
        z = zfrom(d)
        if which < 2:
            ref = W[name].at[x, z, ro] if which == 0 else W[name].at[xo, z, ri]
        else:
            ref = half_of(name, xo, z, ro, which == 3)
        to = over_x if which in (1, 2) else over_r
        return remote(ref, ref, s2_send.at[k, which, d], s2_recv.at[k, which, d], to)

    def relay1(*names):
        for name in names:
            step1_local(name).start()
            for d in range(1, Z):
                step1_copy(name, d).start()
            step2_copy(name, 0, 0).start()
            step2_copy(name, 1, 0).start()

    def relay2(name, ds=(1, 2, 3)):
        k = ids[name]
        for d in ds:
            slot = W[name].at[x, zfrom(d), ri]
            remote(slot, slot, s1_send.at[k, d - 1], s1_recv.at[k, d - 1], dev(zto(d))).wait_recv()
            step2_copy(name, 0, d).start()
            step2_copy(name, 1, d).start()

    def relay3(name, ds=(0, 1, 2, 3)):
        for d in ds:
            step2_arrival(name, 0, d).wait_recv()
            step2_copy(name, 2, d).start()
            step2_arrival(name, 1, d).wait_recv()
            step2_copy(name, 3, d).start()

    def relay4(*names):
        for name in names:
            step1_local(name).wait()
            for d in range(Z):
                step2_arrival(name, 2, d).wait_recv()
                step2_arrival(name, 3, d).wait_recv()

    def relay_sent():
        for name in ARRAYS:
            for d in range(1, Z):
                step1_copy(name, d).wait_send()
            for which in range(4):
                for d in range(Z):
                    step2_copy(name, which, d).wait_send()

    @pl.when(p == 0)
    def _():
        relay1("P1", "P2")

    for c in v_arrivals:
        c.wait_recv()
    remote(aq.at[xo], aq.at[xo], q_send, q_recv, over_x).wait_recv()
    low_lanes = lax.broadcasted_iota(jnp.int32, (64, LANE), 1) < LANE // 2
    for z in range(Z):
        first, second = vv[2 * z], pltpu.roll(vv[2 * z + 1], LANE // 2, 1)
        vec_c[:, z * cz : z * cz + LANE] = first[:, 0:LANE]
        vec_c[:, z * cz + LANE : z * cz + 2 * LANE] = jnp.where(
            low_lanes, first[:, LANE:], second[:, 0:LANE]
        )
        vec_c[:, z * cz + 2 * LANE : (z + 1) * cz] = second[:, LANE:]
    for i in range(Z * R):
        vec_d[:, i * LANE : (i + 1) * LANE] = vv[i, 56:64, 0:LANE]

    def gain_d(row):
        return vec_d[row : row + 1, :]

    def gain_c(row):
        return vec_c[row : row + 1, :]

    def token_entry():
        n_hat, _ = normed(wide(x_in[...]))
        n1_all[zi] = low(n_hat * gain_d(0))
        gather_start("n1", n1_all, keep=False)

    def conv_entry():
        @pl.loop(0, c_dim // LANE)
        def _(ch):
            lanes = lanes_of(ch, LANE)
            taps = vec_c[:, lanes]
            cn[:, lanes] = depthwise(wide(c_in[:, lanes]), lambda k: taps[k : k + 1], 7)

        n_hat, rs = normed(cn[...])
        cn[...] = n_hat
        crs[...] = jnp.broadcast_to(rs, crs.shape)
        f_all[zi] = low(n_hat * gain_c(49))
        gather_start("f", f_all, keep=False)

    def first_relays():
        relay2("P1")
        relay1("Q", "O")
        relay2("P2")
        relay3("P1")

    sent.extend(gather_copies("n1", n1_all))
    sent.extend(gather_copies("f", f_all))

    @pl.when(p == 0)
    def _():
        first = order_in[0, x] == 0
        c_in[...] = jnp.where(first, grid_in[0], grid_in[1])
        x_in[...] = jnp.where(first, tok_in[0], tok_in[1])
        conv_entry()
        token_entry()
        first_relays()

    @pl.when(p == 1)
    def _():
        pl.semaphore_wait(go, 1)
        relay1("P1", "P2")
        first_relays()
        remote(c_in, c_in, h_send.at[1], h_recv.at[1], sib).wait_recv()
        conv_entry()

    relay2("Q")
    relay2("O")
    relay1("E", "Gi", "Go")
    relay3("P2", (0, 1))
    relay4("P1")
    gather_wait("f", f_all)

    def conv_hidden(j):
        @pl.loop(0, cfq // tile)
        def _(t):
            lanes = lanes_of(t, tile)
            act, der = gelu_pair(mm(flat(f_all[...]), flat(W["P1"][j, :, :, :, lanes])))
            r[j, :, lanes] = low(act)
            rp[j, :, lanes] = low(der)

    conv_hidden(0)

    relay3("P2", (2, 3))
    for name in ("E", "Gi", "Go"):
        relay2(name)
    relay1("F1")
    conv_hidden(1)
    relay3("Q")
    relay3("O")
    relay2("F1")
    relay1("F2")

    relay4("P2")

    @pl.loop(0, Z)
    def _(z):
        acc = mm_nt(r[0], flat(W["P2"][0, z])) + mm_nt(r[1], flat(W["P2"][1, z]))
        cv_sb[:, :, lanes_of(z, cz)] = low(acc).reshape(Z, TOK, cz)

    scatter_start("cv", cv_sb, cv_rb)

    for name in ("E", "Gi", "Go"):
        relay3(name)
    relay2("F2")

    @pl.when(p == 0)
    def _():
        pl.semaphore_signal(go, inc=1, device_id=sib, device_id_type=pl.DeviceIdType.MESH)

    @pl.when(p == 1)
    def _():
        remote(x_in, x_in, h_send.at[0], h_recv.at[0], sib).wait_recv()
        token_entry()

    relay4("Q", "O")
    gather_wait("n1", n1_all)
    for j in range(2):
        wj = side_by_side([flat(W["Q"][j, :, :, s]) for s in range(3)])
        qkv[j] = low(mm(flat(n1_all[...]), wj))
    for j in range(2):
        for b in range(Z):
            rows = slice(b * TOK, (b + 1) * TOK)
            outs = []
            for h in range(hq // HD):
                q, kk, vals = (qkv[j, rows, s * hq + h * HD : s * hq + (h + 1) * HD] for s in range(3))
                sc = mm_nt(q, kk) * HD ** (-0.5)
                e = jnp.exp(sc - jnp.max(sc, axis=-1, keepdims=True))
                pr = low(e / jnp.sum(e, axis=-1, keepdims=True))
                prob[j, h, b] = pr
                outs.append(mm(pr, vals))
            ctx[j, rows, :] = low(side_by_side(outs))

    def out_block(j, z):
        return side_by_side([W["O"][j, z, 0], W["O"][j, z, 1]])

    @pl.loop(0, Z)
    def _(z):
        both = jnp.concatenate([out_block(0, z), out_block(1, z)], axis=0)
        acc = mm(side_by_side([ctx[0], ctx[1]]), both)
        o_sb[:, :, lanes_of(z, dz)] = low(acc).reshape(Z, TOK, dz)

    scatter_start("o", o_sb, o_rb)

    relay3("F1")

    scatter_wait("cv", cv_rb)
    cv_sum[...] = scattered(cv_sb, cv_rb)
    c2f[...] = wide(c_in[...]) + gain_c(50) * cv_sum[...]
    c2_low = low(c2f[...])
    c2_all[zi] = c2_low
    gather_start("c2", c2_all)
    hid_grid[x] = c2_low

    @pl.when(p == 0)
    def _():
        remote(hid_grid.at[x], c_in, h_send.at[1], h_recv.at[1], sib).start()

    relay3("F2")
    scatter_wait("o", o_rb)
    x1[...] = wide(x_in[...]) + scattered(o_sb, o_rb)
    n_hat, _ = normed(x1[...])
    n2_all[zi] = low(n_hat * gain_d(1))
    gather_start("n2", n2_all)

    relay4("E", "Gi", "Go")
    gather_wait("c2", c2_all)
    row8 = lax.broadcasted_iota(jnp.int32, (8, adq), 0)
    gs_part = None
    for j in range(2):
        ad = mm(flat(c2_all[...]), flat(W["E"][j]))
        adapted[j] = ad
        taps = aq[j]
        pool = jnp.zeros((8, adq), F32)
        for b in range(Z):
            sp = depthwise(ad[b * TOK : (b + 1) * TOK], lambda k: taps[k : k + 1], 3)
            spread[j, b] = sp
            pool = jnp.where(row8 == b, jnp.mean(sp, axis=0, keepdims=True), pool)
        pooled[j] = pool
        term = mm_nt(low(pool), flat(W["Gi"][j]))
        gs_part = term if gs_part is None else gs_part + term
    gsb[3] = gs_part
    share_start("gs", gsb)

    relay4("F1")
    gather_wait("n2", n2_all)
    for j in range(2):

        @pl.loop(0, ffq // tile)
        def _(t):
            lanes = lanes_of(t, tile)
            act, der = gelu_pair(mm(flat(n2_all[...]), flat(W["F1"][j, :, :, :, lanes])))
            u[j, :, lanes] = low(act)
            up[j, :, lanes] = low(der)

    scatter_wait("gs", gsb)

    def gate_hidden():
        return gelu_pair((gsb[0] + gsb[1]) + (gsb[2] + gsb[3]))

    gh, _ = gate_hidden()
    for j in range(2):
        g8 = jnp.tanh(mm(low(gh), flat(W["Go"][j])))
        gate[j] = g8
        for b in range(Z):
            br_sb[b, :, j * adq : (j + 1) * adq] = low(g8[b : b + 1] * spread[j, b])
    scatter_start("br", br_sb, br_rb)
    relay4("F2")

    @pl.loop(0, Z)
    def _(z):
        acc = None
        for j in range(2):
            term = mm(u[j], side_by_side([W["F2"][j, z, 0], W["F2"][j, z, 1]]))
            acc = term if acc is None else acc + term
        m_sb[:, :, lanes_of(z, dz)] = low(acc).reshape(Z, TOK, dz)

    scatter_start("m", m_sb, m_rb)
    scatter_wait("br", br_rb)
    dx1[...] = x1[...]
    for d in range(Z):
        piece = br_sb[zi] if d == 0 else br_rb[d - 1]
        for j in range(2):
            lanes = pl.ds(pl.multiple_of(j * adh + zfrom(d) * adq, LANE), adq)
            dx1[:, lanes] += wide(piece[:, j * adq : (j + 1) * adq])
    scatter_wait("m", m_rb)
    hid_tok[x] = low(dx1[...] + scattered(m_sb, m_rb))

    @pl.when(p == 0)
    def _():
        remote(hid_tok.at[x], x_in, h_send.at[0], h_recv.at[0], sib).start()

    out_arrivals = []

    def exchange(n, buf):
        c = remote(buf.at[x], buf.at[x], xo_send.at[n], xo_recv.at[n], over_x)
        c.start()
        sent.append(c)
        out_arrivals.append(remote(buf.at[xo], buf.at[xo], xo_send.at[n], xo_recv.at[n], over_x))

    exchange(0, hid_tok)
    exchange(1, hid_grid)
    relay_sent()

    @pl.when(p == 1)
    def _():
        dx3[...] = tcot_in[x]
        dcot[...] = gcot_in[x]

    @pl.when(p == 0)
    def _():
        remote(dx3, dx3, b_send.at[0], b_recv.at[0], sib).wait_recv()

    dx3_all[zi] = dx3[...]
    gather_start("dx3", dx3_all)
    gather_wait("dx3", dx3_all)

    def own_lanes(j):
        return pl.ds(pl.multiple_of(j * adh + zi * adq, LANE), adq)

    gh, ghp = gate_hidden()
    dgh_part = None
    dgp = []
    for j in range(2):
        dgate = jnp.zeros((8, adq), F32)
        for b in range(Z):
            dbr = wide(dx3_all[b, :, own_lanes(j)])
            dgate = jnp.where(row8 == b, jnp.sum(dbr * spread[j, b], axis=0, keepdims=True), dgate)
        dg8 = low(dgate * (1.0 - gate[j] * gate[j]))
        dgp.append(dg8)
        term = mm_nt(dg8, flat(W["Go"][j]))
        dgh_part = term if dgh_part is None else dgh_part + term
    dgb[3] = dgh_part
    share_start("dgh", dgb)

    for j in range(2):

        @pl.loop(0, ffq // tile)
        def _(t):
            rows = lanes_of(t, tile)
            both = side_by_side([W["F2"][j, z, rr, rows] for z in range(Z) for rr in range(R)])
            du = mm_nt(flat(dx3_all[...]), both)
            dh[j, :, rows] = low(du * wide(up[j, :, rows]))

    scatter_wait("dgh", dgb)
    dgs = low(((dgb[0] + dgb[1]) + (dgb[2] + dgb[3])) * ghp)
    for j in range(2):
        dpool = mm(dgs, flat(W["Gi"][j])) * (1.0 / TOK)
        taps = aq[j]
        tap_rows = [None] * 9
        for b in range(Z):
            dsp = gate[j, b : b + 1] * wide(dx3_all[b, :, own_lanes(j)]) + dpool[b : b + 1]
            dad[j, b * TOK : (b + 1) * TOK] = low(depthwise(dsp, lambda k: taps[8 - k : 9 - k], 3))

            def put(k, row):
                tap_rows[k] = row if tap_rows[k] is None else tap_rows[k] + row

            depthwise_taps(adapted[j, b * TOK : (b + 1) * TOK], dsp, 3, put)
        for k in range(9):
            gad[j, k : k + 1] = tap_rows[k]
        gad[j, 9:16] = jnp.zeros((7, adq), F32)

    @pl.loop(0, Z)
    def _(z):
        acc = mm_nt(dad[0], flat(W["E"][0, z])) + mm_nt(dad[1], flat(W["E"][1, z]))
        dc2_sb[:, :, lanes_of(z, cz)] = low(acc).reshape(Z, TOK, cz)

    scatter_start("dc2", dc2_sb, dc2_rb)

    @pl.loop(0, Z)
    def _(z):
        acc = mm_nt(dh[0], flat(W["F1"][0, z])) + mm_nt(dh[1], flat(W["F1"][1, z]))
        dn2_sb[:, :, lanes_of(z, dz)] = low(acc).reshape(Z, TOK, dz)

    scatter_start("dn2", dn2_sb, dn2_rb)

    def half_rows(name, upper):
        half = W[name].shape[-2] // 2
        rows = slice(half, None) if upper else slice(0, half)
        return (slice(None), rows) if len(W[name].shape) == 6 else (rows,)

    def hop_copy(name, which):
        n = ids[name]
        lower, upper = half_rows(name, False), half_rows(name, True)
        src, to = (
            lambda: (W[name].at[(xo, slice(None), slice(None)) + lower], over_x),
            lambda: (W[name].at[(slice(None), slice(None), ro) + upper], over_r),
            lambda: (RX[name][0].at[:, ro], over_r),
            lambda: (RX[name][1].at[xo], over_x),
        )[which]()
        return remote(src, RX[name][which], g_send.at[n, which], g_recv.at[n, which], to)

    def reduce_start(name):
        hop_copy(name, 0).start()
        hop_copy(name, 1).start()

    def reduce_middle(*names):
        for name in names:
            lower, upper = half_rows(name, False), half_rows(name, True)
            buf = RX[name]
            hop_copy(name, 0).wait_recv()

            @pl.loop(0, Z)
            def _(z):
                for rr in range(R):
                    own = W[name][(x, z, rr) + lower]
                    buf[0][z, rr] = low(wide(own) + wide(buf[0][z, rr]))

            hop_copy(name, 2).start()
            hop_copy(name, 1).wait_recv()

            @pl.loop(0, Z)
            def _(z):
                for j in range(2):
                    own = W[name][(j, z, ri) + upper]
                    buf[1][j, z] = low(wide(own) + wide(buf[1][j, z]))

            hop_copy(name, 3).start()

    def reduce_end(*names):
        for name in names:
            lower, upper = half_rows(name, False), half_rows(name, True)
            buf = RX[name]
            hop_copy(name, 2).wait_recv()
            hop_copy(name, 3).wait_recv()

            @pl.loop(0, Z)
            def _(z):
                W[name][(x, z, ri) + lower] = low(wide(buf[0][z, ri]) + wide(buf[2][z]))
                W[name][(x, z, ri) + upper] = low(wide(buf[1][x, z]) + wide(buf[3][z]))

            for d in range(1, Z):
                back_copy(name, d).start()
            back_local(name).start()

    def back_copy(name, d):
        n = ids[name]
        return remote(
            W[name].at[x, zto(d), ri], quarter_of(name, native[name], zi),
            a_send.at[n, d - 1], a_recv.at[n, d - 1], dev(zto(d)),
        )

    def back_local(name):
        return pltpu.make_async_copy(
            W[name].at[x, zi, ri], quarter_of(name, native[name], zi), loc_sem.at[ids[name]]
        )

    peers = ((1, 0), (0, 1), (1, 1))

    def owner(k):
        return (ro if peers[k][0] else ri), (xo if peers[k][1] else x)

    def row_grad(name, left, right):
        width = W[name].shape[3]
        span = R * width

        @pl.loop(0, Z)
        def _(z):
            turned[0:span] = flat(left[:, :, lanes_of(z, span)]).T
            for j in range(2):
                W[name][j, z] = low(mm(turned[0:span], right[j])).reshape(R, width, -1)

        reduce_start(name)

    def col_grad(name, left, right):
        width = left.shape[2]
        for j in range(2):
            turned[j * width : (j + 1) * width] = left[j].T

        @pl.loop(0, Z)
        def _(z):
            rhs = flat(right[:, :, lanes_of(z, dz)])
            for j in range(2):
                g = low(mm(turned[j * width : (j + 1) * width], rhs))
                for rr in range(R):
                    W[name][j, z, rr] = g[:, rr * LANE : (rr + 1) * LANE]

        reduce_start(name)

    for j in range(2):
        W["Gi"][j] = low(mm_tn(dgs, low(pooled[j]))).reshape(Z, R, -1, adq)
        W["Go"][j] = low(mm_tn(low(gh), dgp[j])).reshape(Z, R, -1, adq)
    reduce_start("Gi")
    reduce_start("Go")
    row_grad("E", c2_all, dad)

    @pl.when(p == 0)
    def _():
        remote(dcot, dcot, b_send.at[1], b_recv.at[1], sib).wait_recv()

    scatter_wait("dc2", dc2_rb)
    dc2t[...] = wide(dcot[...]) + scattered(dc2_sb, dc2_rb)
    gvs_ls = jnp.sum(cv_sum[...] * dc2t[...], axis=0, keepdims=True)
    dcv_all[zi] = low(dc2t[...] * gain_c(50))
    gather_start("dcv", dcv_all)

    scatter_wait("dn2", dn2_rb)
    dn2 = scattered(dn2_sb, dn2_rb)
    n_hat, rs = normed(x1[...])
    gvs_d1 = jnp.sum(dn2 * n_hat, axis=0, keepdims=True)
    dx1[...] = wide(dx3[...]) + norm_back(dn2, n_hat, rs, gain_d(1))
    dx1_all[zi] = low(dx1[...])
    gather_start("dx1", dx1_all)

    col_grad("F2", u, dx3_all)
    row_grad("F1", n2_all, dh)

    gather_wait("dcv", dcv_all)
    for j in range(2):

        @pl.loop(0, cfq // tile)
        def _(t):
            lanes = lanes_of(t, tile)
            dr = mm(flat(dcv_all[...]), flat(W["P2"][j, :, :, :, lanes]))
            dhc[j, :, lanes] = low(dr * wide(rp[j, :, lanes]))

    @pl.loop(0, Z)
    def _(z):
        acc = mm_nt(dhc[0], flat(W["P1"][0, z])) + mm_nt(dhc[1], flat(W["P1"][1, z]))
        df_sb[:, :, lanes_of(z, cz)] = low(acc).reshape(Z, TOK, cz)

    scatter_start("df", df_sb, df_rb)

    gather_wait("dx1", dx1_all)
    for j in range(2):
        both = side_by_side([W["O"][j, z, rr] for z in range(Z) for rr in range(R)])
        do_all[j] = low(mm_nt(flat(dx1_all[...]), both))
    for j in range(2):
        for b in range(Z):
            rows = slice(b * TOK, (b + 1) * TOK)
            parts = [[], [], []]
            for h in range(hq // HD):
                q, kk, vals = (qkv[j, rows, s * hq + h * HD : s * hq + (h + 1) * HD] for s in range(3))
                do = do_all[j, rows, h * HD : (h + 1) * HD]
                pr = prob[j, h, b]
                dp = mm_nt(do, vals)
                prw = wide(pr)
                ds = low(prw * (dp - jnp.sum(dp * prw, axis=-1, keepdims=True)) * HD ** (-0.5))
                parts[0].append(mm(ds, kk))
                parts[1].append(mm_tn(ds, q))
                parts[2].append(mm_tn(pr, do))
            for s in range(3):
                dqkv[j, rows, s * hq : (s + 1) * hq] = low(side_by_side(parts[s]))

    @pl.loop(0, Z)
    def _(z):
        acc = None
        for j in range(2):
            term = mm_nt(dqkv[j], side_by_side([flat(W["Q"][j, z, :, s]) for s in range(3)]))
            acc = term if acc is None else acc + term
        dn1_sb[:, :, lanes_of(z, dz)] = low(acc).reshape(Z, TOK, dz)

    scatter_start("dn1", dn1_sb, dn1_rb)

    reduce_middle("Gi", "Go", "E", "F2", "F1")

    def pw_grads():
        row_grad("P2", dcv_all, r)
        row_grad("P1", f_all, dhc)

    @pl.when(p == 0)
    def _():
        pw_grads()

    scatter_wait("dn1", dn1_rb)
    dn1 = scattered(dn1_sb, dn1_rb)
    n_hat, rs = normed(wide(x_in[...]))
    gvs_d0 = jnp.sum(dn1 * n_hat, axis=0, keepdims=True)
    out_gtok[x] = low(dx1[...] + norm_back(dn1, n_hat, rs, gain_d(0)))

    @pl.when(p == 1)
    def _():
        remote(out_gtok.at[x], dx3, b_send.at[0], b_recv.at[0], sib).start()

    scatter_wait("df", df_rb)
    dfv = scattered(df_sb, df_rb)
    gvs_lc = jnp.sum(dfv * cn[...], axis=0, keepdims=True)
    dcn[...] = norm_back(dfv, cn[...], crs[:, 0:1], gain_c(49))

    @pl.loop(0, c_dim // LANE)
    def _(ch):
        lanes = lanes_of(ch, LANE)
        taps = vec_c[:, lanes]
        back = depthwise(dcn[:, lanes], lambda k: taps[48 - k : 49 - k], 7)
        out_ggrid[x, :, lanes] = low(dc2t[:, lanes] + back)

    @pl.when(p == 1)
    def _():
        remote(out_ggrid.at[x], dcot, b_send.at[1], b_recv.at[1], sib).start()
        pw_grads()

    @pl.loop(0, Z)
    def _(z):
        turned[0:dz] = flat(n1_all[:, :, lanes_of(z, dz)]).T
        for j in range(2):
            g = low(mm(turned[0:dz], dqkv[j]))
            for s in range(3):
                W["Q"][j, z, :, s] = g[:, s * hq : (s + 1) * hq].reshape(R, -1, hq)

    reduce_start("Q")
    col_grad("O", ctx, dx1_all)

    exchange(2, out_gtok)
    exchange(3, out_ggrid)
    reduce_end("Gi", "Go", "E", "F2", "F1")
    reduce_middle("P2")

    @pl.loop(0, Z)
    def _(z):
        for part in range(cz // LANE):
            lanes = pl.ds(pl.multiple_of(z * cz + part * LANE, LANE), LANE)

            def put(k, row):
                gvs[z, k : k + 1, part * LANE : (part + 1) * LANE] = row

            depthwise_taps(wide(c_in[:, lanes]), dcn[:, lanes], 7, put)

    for z in range(Z):
        gvs[z, 49:50] = gvs_lc[:, z * cz : (z + 1) * cz]
        gvs[z, 50:51] = gvs_ls[:, z * cz : (z + 1) * cz]
        gvs[z, 51:64] = jnp.zeros((13, cz), F32)
        gvs[z, 56:57, 0:dz] = gvs_d0[:, z * dz : (z + 1) * dz]
        gvs[z, 57:58, 0:dz] = gvs_d1[:, z * dz : (z + 1) * dz]
    scatter_start("gv", gvs, gv_rb)

    def group_copy(n, k, src, dst):
        rr, xx = owner(k)
        return remote(src, dst, gx_send.at[n, k], gx_recv.at[n, k], dev(rr=rr, xx=xx))

    for k in range(3):
        c = group_copy(1, k, gad, gad_rb.at[k])
        c.start()
        sent.append(c)
    scatter_wait("gv", gv_rb)
    gvx[3] = (gvs[zi] + gv_rb[0]) + (gv_rb[1] + gv_rb[2])
    for k in range(3):
        c = group_copy(0, k, gvx.at[3], gvx.at[k])
        c.start()
        sent.append(c)
    for k in range(3):
        group_copy(1, k, gad, gad_rb.at[k]).wait_recv()
    gad_all[zi] = (gad[x] + gad_rb[0, x]) + (gad_rb[1, x] + gad_rb[2, x])
    gather_start("gad", gad_all)

    reduce_middle("P1", "Q", "O")
    reduce_end("P2", "P1", "Q", "O")

    for k in range(3):
        group_copy(0, k, gvx.at[k], gvx.at[k]).wait_recv()
    total = (gvx[0] + gvx[1]) + (gvx[2] + gvx[3])
    mine = jnp.where(ri == 1, pltpu.roll(total, c_own, 1), total)[:, 0:c_own]
    mine_d = jnp.where(ri == 1, total[:, LANE : 2 * LANE], total[:, 0:LANE])

    def flag(n):
        return train_in[0, n].astype(F32)

    out_depth[...] = mine[0:taps7] * flag(0)
    out_ln_conv[...] = mine[49:50] * flag(1)
    out_scale[...] = mine[50:51] * flag(4)
    out_ln_attn[...] = mine_d[56:57]
    out_ln_mlp[...] = mine_d[57:58]
    gather_wait("gad", gad_all)
    for z in range(Z):
        out_ad[:, z * adq : (z + 1) * adq] = gad_all[z][0:9]
    for name in ARRAYS:
        back_local(name).wait()
        for d in range(1, Z):
            n = ids[name]
            slot = quarter_of(name, native[name], zfrom(d))
            remote(slot, slot, a_send.at[n, d - 1], a_recv.at[n, d - 1], dev(zto(d))).wait_recv()
    for c in out_arrivals:
        c.wait_recv()

    @pl.when(p == 0)
    def _():
        remote(hid_tok.at[x], x_in, h_send.at[0], h_recv.at[0], sib).wait_send()
        remote(hid_grid.at[x], c_in, h_send.at[1], h_recv.at[1], sib).wait_send()

    @pl.when(p == 1)
    def _():
        remote(out_gtok.at[x], dx3, b_send.at[0], b_recv.at[0], sib).wait_send()
        remote(out_ggrid.at[x], dcot, b_send.at[1], b_recv.at[1], sib).wait_send()

    for c in sent:
        c.wait_send()
    for name in ARRAYS:
        for which in range(4):
            hop_copy(name, which).wait_send()
        for d in range(1, Z):
            back_copy(name, d).wait_send()


def run_layers(weights, vectors, order, train, streams, sizes, outer):
    d_dim, c_dim, hq, ffq, cfq, adw, dg = sizes
    vm = pltpu.VMEM
    blocks = []
    for name, value in zip(ARRAYS, weights):
        if name == "Q":
            blocks.append((3, value.shape[1], hq))
        elif name in ("O", "F2"):
            blocks.append((value.shape[0] // Z, value.shape[1]))
        else:
            blocks.append((value.shape[0], value.shape[1] // Z))
    rows = Z * TOK

    def act(width, count=Z, kind=BF):
        return vm((count, TOK, width), kind)

    scratch = [vm((2, Z, R) + s, BF) for s in blocks] + [
        vm(lead + s[:-2] + (s[-2] // 2, s[-1]), BF)
        for s in blocks
        for lead in ((Z, R), (2, Z), (Z,), (Z,))
    ]
    scratch += [
        vm((64, 2 * LANE), F32), vm((Z * R, 64, 2 * LANE), F32), vm((2, 16, adw), F32), vm((64, c_dim), F32), vm((8, d_dim), F32),
        vm((TOK, d_dim), BF), vm((TOK, c_dim), BF), act(d_dim), act(c_dim), act(d_dim), act(c_dim),
        act(d_dim), act(d_dim, 3), act(c_dim), act(c_dim, 3), act(d_dim), act(d_dim, 3),
        act(2 * adw), act(2 * adw, 3), vm((4, 8, dg), F32), vm((4, 8, dg), F32),
        vm((2, rows, 3 * hq), BF), vm((2, hq // HD, Z, TOK, TOK), BF), vm((2, rows, hq), BF),
        vm((2, rows, ffq), BF), vm((2, rows, ffq), BF), vm((2, rows, cfq), BF), vm((2, rows, cfq), BF),
        vm((TOK, c_dim), F32), vm((TOK, LANE), F32), vm((TOK, c_dim), F32), vm((TOK, d_dim), F32), vm((TOK, c_dim), F32),
        vm((2, rows, adw), F32), vm((2, Z, TOK, adw), F32), vm((2, 8, adw), F32), vm((2, 8, adw), F32),
        vm((TOK, d_dim), BF), vm((TOK, c_dim), BF), act(d_dim), act(d_dim), act(d_dim, 3), act(c_dim), act(c_dim, 3),
        act(d_dim), act(c_dim),
        act(d_dim), act(d_dim, 3), act(c_dim), act(c_dim, 3), vm((2, rows, ffq), BF), vm((2, rows, hq), BF),
        vm((2, rows, 3 * hq), BF), vm((2, rows, cfq), BF), vm((TOK, d_dim), F32), vm((TOK, c_dim), F32), vm((2, rows, adw), BF),
        vm((TOK, c_dim), F32),
        vm((Z, 64, c_dim // Z), F32), vm((3, 64, c_dim // Z), F32), vm((4, 64, c_dim // Z), F32),
        vm((2, 16, adw), F32), vm((3, 2, 16, adw), F32), vm((Z, 16, adw), F32),
        vm((2 * ffq, rows), BF),
    ]
    dma = pltpu.SemaphoreType.DMA
    na = len(ARRAYS)
    scratch += [
        dma((len(EVENTS), 3)), dma((len(EVENTS), 3)), dma((na, 3)), dma((na, 3)), dma((na,)),
        dma((na, 4, Z)), dma((na, 4, Z)), dma((7,)), dma((7,)), dma, dma, dma((2,)), dma((2,)), dma((2,)), dma((2,)),
        dma((4,)), dma((4,)), dma((na, 4)), dma((na, 4)), dma((na, 3)), dma((na, 3)), dma((2, 3)), dma((2, 3)),
        pltpu.SemaphoreType.REGULAR,
    ]
    sds = jax.ShapeDtypeStruct
    out_shape = [sds((2, TOK, d_dim), BF), sds((2, TOK, c_dim), BF)] * 2
    out_shape += [sds(value.shape, BF) for value in weights]
    out_shape += [sds(value.shape, F32) for value in vectors]
    any_spec = pl.BlockSpec(memory_space=pl.ANY)
    vm_spec = pl.BlockSpec(memory_space=pltpu.VMEM)
    sm_spec = pl.BlockSpec(memory_space=pltpu.SMEM)
    return pl.pallas_call(
        functools.partial(main_kernel, sizes, outer),
        out_shape=out_shape,
        in_specs=[any_spec] * na + [vm_spec] * 6 + [sm_spec] * 2 + [vm_spec] * 4,
        out_specs=[vm_spec] * 4 + [any_spec] * na + [vm_spec] * 6,
        scratch_shapes=scratch,
        compiler_params=pltpu.CompilerParams(
            collective_id=0, has_side_effects=True, vmem_limit_bytes=62 * 1024 * 1024
        ),
        cost_estimate=pl.CostEstimate(flops=26 * 10**9, bytes_accessed=10**8, transcendentals=10**7),
        name="layers",
    )(*weights, *vectors, order, train, *streams)


def per_device(
    tokens,
    conv_grid,
    order,
    trainable,
    ln_attn,
    w_qkv,
    w_attn_out,
    ln_mlp,
    w_fc_in,
    w_fc_out,
    conv_depth,
    ln_conv,
    w_pw_in,
    w_pw_out,
    layer_scale,
    w_adapt,
    adapt_depth,
    w_gate_in,
    w_gate_out,
    tok_cot,
    grid_cot,
):
    dp_count = lax.axis_size("dp")
    outer = dp_count // (Z * R)
    groups = [[g * outer + o for o in range(outer)] for g in range(Z * R)]
    layer_at = lax.axis_index("pipe")

    def block(value, axis):
        value = value[0]
        if outer == 1:
            return value
        return lax.all_gather(value, "dp", axis=axis, tiled=True, axis_index_groups=groups)

    def share(value, axis):
        if outer > 1:
            value = lax.psum_scatter(
                value, "dp", scatter_dimension=axis, tiled=True, axis_index_groups=groups
            )
        return value[None]

    qkv = block(w_qkv, 1)
    gate_in = block(w_gate_in, 1).T
    pw_in = block(w_pw_in, 0)
    adapt = block(w_adapt, 0)
    fc_in = block(w_fc_in, 0)
    weights = (
        pw_in,
        block(w_pw_out, 1).T,
        qkv,
        block(w_attn_out, 1),
        adapt,
        gate_in,
        block(w_gate_out, 0),
        fc_in,
        block(w_fc_out, 1),
    )
    vectors = (
        block(conv_depth, 1),
        block(ln_conv, 0)[None],
        block(layer_scale, 0)[None],
        block(ln_attn, 0)[None],
        block(ln_mlp, 0)[None],
        adapt_depth[0],
    )
    spread = Z * R
    sizes = (
        qkv.shape[1] * spread, pw_in.shape[0] * spread, qkv.shape[2] // Z, fc_in.shape[1] // Z,
        pw_in.shape[1] // Z, adapt.shape[1] // Z, gate_in.shape[0] * spread,
    )

    def rows_of(value):
        return value.reshape(value.shape[0], TOK, value.shape[-1])

    streams = [rows_of(value) for value in (tokens, conv_grid, tok_cot, grid_cot)]
    outs = run_layers(weights, vectors, order, trainable, streams, sizes, outer)
    hid_tok, hid_grid, g_tok, g_grid = outs[:4]
    g_p1, g_p2, g_q, g_o, g_e, g_gi, g_go, g_f1, g_f2 = [value.astype(F32) for value in outs[4:13]]
    g_depth, g_ln_conv, g_scale, g_ln_attn, g_ln_mlp, g_ad = outs[13:]

    swap = (layer_at == 0) & (order[0, 0] == 1)
    g_tok = jnp.where(swap, g_tok[::-1], g_tok)
    g_grid = jnp.where(swap, g_grid[::-1], g_grid)
    grid_shape = (1,) + conv_grid.shape
    tok_shape = (1,) + tokens.shape
    flags = trainable[0].astype(F32)
    if outer > 1:
        g_ad = lax.psum(g_ad, "dp", axis_index_groups=groups)
    return (
        hid_tok.reshape(tok_shape),
        hid_grid.reshape(grid_shape),
        g_tok.reshape(tok_shape),
        g_grid.reshape(grid_shape),
        share(g_ln_attn[0], 0),
        share(g_q, 1),
        share(g_o, 1),
        share(g_ln_mlp[0], 0),
        share(g_f1, 0),
        share(g_f2, 1),
        share(g_depth, 1),
        share(g_ln_conv[0], 0),
        share(g_p1 * flags[2], 0),
        share((g_p2 * flags[3]).T, 1),
        share(g_scale[0], 0),
        share(g_e, 0),
        g_ad[None],
        share(g_gi.T, 1),
        share(g_go, 0),
    )


def solution(mesh):
    in_specs = (
        P(None, "dp", None, None),
        P(None, "dp", None, None, None),
        P("dp", None),
        P("pipe", None),
        P("pipe", "dp"),
        P("pipe", None, "dp", "tensor"),
        P("pipe", "tensor", "dp"),
        P("pipe", "dp"),
        P("pipe", "dp", "tensor"),
        P("pipe", "tensor", "dp"),
        P("pipe", None, "dp"),
        P("pipe", "dp"),
        P("pipe", "dp", "tensor"),
        P("pipe", "tensor", "dp"),
        P("pipe", "dp"),
        P("pipe", "dp", "tensor"),
        P("pipe", None, "tensor"),
        P("pipe", "tensor", "dp"),
        P("pipe", "dp", "tensor"),
        P(None, "dp", None, None),
        P(None, "dp", None, None, None),
    )
    out_specs = (
        P("pipe", None, "dp", None, None),
        P("pipe", None, "dp", None, None, None),
        P("pipe", None, "dp", None, None),
        P("pipe", None, "dp", None, None, None),
        P("pipe", "dp"),
        P("pipe", None, "dp", "tensor"),
        P("pipe", "tensor", "dp"),
        P("pipe", "dp"),
        P("pipe", "dp", "tensor"),
        P("pipe", "tensor", "dp"),
        P("pipe", None, "dp"),
        P("pipe", "dp"),
        P("pipe", "dp", "tensor"),
        P("pipe", "tensor", "dp"),
        P("pipe", "dp"),
        P("pipe", "dp", "tensor"),
        P("pipe", None, "tensor"),
        P("pipe", "tensor", "dp"),
        P("pipe", "dp", "tensor"),
    )
    return jax.shard_map(
        per_device, mesh=mesh, in_specs=in_specs, out_specs=out_specs, check_vma=False
    )
```

```python
import functools

import jax
import jax.numpy as jnp
from jax import lax
from jax.experimental import pallas as pl
from jax.experimental.pallas import tpu as pltpu
from jax.sharding import PartitionSpec as P

HD = 64
Z = 4
R = 2
TOK = 64
SIDE = 8
LANE = 128
BF = jnp.bfloat16
F32 = jnp.float32
ARRAYS = ("P1", "P2", "Q", "O", "E", "Gi", "Go", "F1", "F2")
EVENTS = (
    "n1", "f", "o", "cv", "n2", "c2", "m", "br", "gs",
    "dx3", "dgh", "dn2", "dc2", "dx1", "dcv", "dn1", "df", "gv", "gad",
)


def mm(a, b):
    return lax.dot_general(a, b, (((1,), (0,)), ((), ())), preferred_element_type=F32)


def mm_nt(a, b):
    return lax.dot_general(a, b, (((1,), (1,)), ((), ())), preferred_element_type=F32)


def mm_tn(a, b):
    return lax.dot_general(a, b, (((0,), (0,)), ((), ())), preferred_element_type=F32)


def flat(value):
    return value.reshape(-1, value.shape[-1])


def low(value):
    return value.astype(BF)


def wide(value):
    return value.astype(F32)


def gelu_pair(h):
    phi = 0.5 * (1.0 + lax.erf(h * 0.7071067811865476))
    dens = jnp.exp(-0.5 * h * h) * 0.3989422804014327
    return h * phi, phi + h * dens


def normed(value):
    centred = value - jnp.mean(value, axis=-1, keepdims=True)
    rs = lax.rsqrt(jnp.mean(centred * centred, axis=-1, keepdims=True) + 1e-06)
    return centred * rs, rs


def norm_back(dn, n_hat, rs, gain):
    gd = dn * gain
    return (
        gd
        - jnp.mean(gd, axis=-1, keepdims=True)
        - n_hat * jnp.mean(gd * n_hat, axis=-1, keepdims=True)
    ) * rs


def col_shift(value, by):
    if by == 0:
        return value
    at = lax.broadcasted_iota(jnp.int32, value.shape, 0) % SIDE
    rolled = pltpu.roll(value, (-by) % TOK, 0)
    return jnp.where((at + by >= 0) & (at + by < SIDE), rolled, 0.0)


def row_shift(value, by):
    if by == 0:
        return value
    gap = jnp.zeros((abs(by) * SIDE, value.shape[1]), value.dtype)
    if by > 0:
        return jnp.concatenate([value[by * SIDE :], gap], axis=0)
    return jnp.concatenate([gap, value[: TOK + by * SIDE]], axis=0)


def depthwise(value, tap, side):
    half = side // 2
    shifted = [col_shift(value, b - half) for b in range(side)]
    total = None
    for a in range(side):
        line = None
        for b in range(side):
            term = shifted[b] * tap(a * side + b)
            line = term if line is None else line + term
        line = row_shift(line, a - half)
        total = line if total is None else total + line
    return total


def depthwise_taps(value, grad, side, put):
    half = side // 2
    shifted = [col_shift(value, b - half) for b in range(side)]
    for a in range(side):
        d = a - half
        lo, hi = max(0, -d) * SIDE, (SIDE - max(0, d)) * SIDE
        for b in range(side):
            part = shifted[b][lo + d * SIDE : hi + d * SIDE] * grad[lo:hi]
            put(a * side + b, jnp.sum(part, axis=0, keepdims=True))


def lanes_of(at, width):
    return pl.ds(pl.multiple_of(at * width, width), width)


def side_by_side(blocks):
    return jnp.concatenate(blocks, axis=1)


def main_kernel(dims, outer, *refs):
    at = iter(refs)

    def take(count):
        return [next(at) for _ in range(count)]

    na = len(ARRAYS)
    source = dict(zip(ARRAYS, take(na)))
    (
        depth_in, ln_conv_in, scale_in, ln_attn_in, ln_mlp_in, adapt_depth_in,
        order_in, train_in, tok_in, grid_in, tcot_in, gcot_in,
    ) = take(12)
    hid_tok, hid_grid, out_gtok, out_ggrid = take(4)
    native = dict(zip(ARRAYS, take(na)))
    out_depth, out_ln_conv, out_scale, out_ln_attn, out_ln_mlp, out_ad = take(6)
    W = dict(zip(ARRAYS, take(na)))
    hops = take(4 * na)
    RX = {name: hops[4 * n : 4 * n + 4] for n, name in enumerate(ARRAYS)}
    (
        v_loc, vv, aq, vec_c, vec_d, x_in, c_in, n1_all, f_all, n2_all, c2_all,
        o_sb, o_rb, cv_sb, cv_rb, m_sb, m_rb, br_sb, br_rb, gsb, dgb,
        qkv, prob, ctx, u, up, r, rp, cn, crs, cv_sum, x1, c2f,
        adapted, spread, pooled, gate,
        dx3, dcot, dx3_all, dn2_sb, dn2_rb, dc2_sb, dc2_rb, dx1_all, dcv_all,
        dn1_sb, dn1_rb, df_sb, df_rb, dh, do_all, dqkv, dhc, dx1, dc2t, dad, dcn,
        gvs, gv_rb, gvx, gad, gad_rb, gad_all, turned,
    ) = take(65)
    (
        zs_send, zs_recv, s1_send, s1_recv, loc_sem, s2_send, s2_recv,
        v_send, v_recv, q_send, q_recv, h_send, h_recv, b_send, b_recv, c_send, c_recv,
        xo_send, xo_recv, g_send, g_recv, a_send, a_recv, gx_send, gx_recv, go,
    ) = take(26)

    p = lax.axis_index("pipe")
    dpi = lax.axis_index("dp")
    x = lax.axis_index("tensor")
    rest = dpi % outer
    zi = dpi // (outer * R)
    ri = (dpi // outer) % R
    xo = 1 - x
    ro = 1 - ri
    d_dim, c_dim, hq, ffq, cfq, adq, dg = dims
    adh = Z * adq
    dz, cz = d_dim // Z, c_dim // Z
    tile = 256
    ids = {name: number for number, name in enumerate(ARRAYS)}
    ev = {name: number for number, name in enumerate(EVENTS)}

    def dev(z=None, rr=None, xx=None, pp=None):
        z = zi if z is None else z
        rr = ri if rr is None else rr
        return (
            p if pp is None else pp,
            (z * R + rr) * outer + rest,
            x if xx is None else xx,
        )

    def zto(d):
        return lax.rem(zi + d, Z)

    def zfrom(d):
        return lax.rem(zi + Z - d, Z)

    def remote(src, dst, ssem, rsem, device):
        return pltpu.make_async_remote_copy(
            src_ref=src, dst_ref=dst, send_sem=ssem, recv_sem=rsem,
            device_id=device, device_id_type=pl.DeviceIdType.MESH,
        )

    sib = dev(pp=1 - p)
    over_r, over_x = dev(rr=ro), dev(xx=xo)

    def z_copy(e, d, src, dst):
        return remote(src, dst, zs_send.at[e, d - 1], zs_recv.at[e, d - 1], dev(zto(d)))

    sent = []

    def gather_copies(name, buf):
        return [z_copy(ev[name], d, buf.at[zi], buf.at[zi]) for d in range(1, Z)]

    def gather_start(name, buf, keep=True):
        copies = gather_copies(name, buf)
        for c in copies:
            c.start()
        if keep:
            sent.extend(copies)

    def gather_wait(name, buf):
        for d in range(1, Z):
            slot = buf.at[zfrom(d)]
            z_copy(ev[name], d, slot, slot).wait_recv()

    def scatter_start(name, sb, rb):
        for d in range(1, Z):
            c = z_copy(ev[name], d, sb.at[zto(d)], rb.at[d - 1])
            c.start()
            sent.append(c)

    def scatter_wait(name, rb):
        for d in range(1, Z):
            z_copy(ev[name], d, rb.at[d - 1], rb.at[d - 1]).wait_recv()

    def share_start(name, buf):
        for d in range(1, Z):
            c = z_copy(ev[name], d, buf.at[3], buf.at[d - 1])
            c.start()
            sent.append(c)

    def scattered(sb, rb):
        return (wide(sb[zi]) + wide(rb[0])) + (wide(rb[1]) + wide(rb[2]))

    barrier = pltpu.get_barrier_semaphore()
    greeted = [sib]
    for d in range(1, Z):
        greeted += [dev(zto(d)), dev(zto(d), ro), dev(zto(d), pp=1 - p)]
    greeted += [over_r, over_x, dev(rr=ro, xx=xo)]
    for device in greeted:
        pl.semaphore_signal(barrier, inc=1, device_id=device, device_id_type=pl.DeviceIdType.MESH)
    v_loc[...] = jnp.zeros(v_loc.shape, F32)
    taps7 = depth_in.shape[0]
    c_own = depth_in.shape[1]
    v_loc[0:taps7, 0:c_own] = wide(depth_in[...])
    v_loc[49:50, 0:c_own] = wide(ln_conv_in[...])
    v_loc[50:51, 0:c_own] = wide(scale_in[...])
    v_loc[56:57, 0:LANE] = wide(ln_attn_in[...])
    v_loc[57:58, 0:LANE] = wide(ln_mlp_in[...])
    aq[x] = jnp.zeros(aq.shape[1:], F32)
    aq[x, 0:9] = wide(adapt_depth_in[:, lanes_of(zi, adq)])
    pl.semaphore_wait(barrier, len(greeted))

    me8 = zi * R + ri
    v_arrivals = []
    for n, (d, flip) in enumerate([(d, s) for d in range(Z) for s in (0, 1)][1:]):
        tr = ro if flip else ri
        c = remote(v_loc, vv.at[me8], v_send.at[n], v_recv.at[n], dev(zto(d), tr))
        c.start()
        sent.append(c)
        fr = zfrom(d) * R + tr
        v_arrivals.append(remote(vv.at[fr], vv.at[fr], v_send.at[n], v_recv.at[n], dev(zto(d), tr)))
    vv[me8] = v_loc[...]
    c = remote(aq.at[x], aq.at[x], q_send, q_recv, over_x)
    c.start()
    sent.append(c)

    by_rows = ("O", "F2")

    def quarter_of(name, ref, z):
        if name == "Q":
            return ref.at[:, :, lanes_of(z, hq)]
        if name in by_rows:
            height = ref.shape[0] // Z
            return ref.at[pl.ds(pl.multiple_of(z * height, height), height)]
        return ref.at[:, lanes_of(z, ref.shape[1] // Z)]

    def step1_local(name):
        return pltpu.make_async_copy(
            quarter_of(name, source[name], zi), W[name].at[x, zi, ri], loc_sem.at[ids[name]]
        )

    def step1_copy(name, d):
        k = ids[name]
        return remote(
            quarter_of(name, source[name], zto(d)), W[name].at[x, zi, ri],
            s1_send.at[k, d - 1], s1_recv.at[k, d - 1], dev(zto(d)),
        )

    def half_of(name, j, z, rr, upper):
        w = W[name]
        half = w.shape[-2] // 2
        rows = slice(half, None) if upper else slice(0, half)
        if len(w.shape) == 6:
            return w.at[j, z, rr, :, rows]
        return w.at[j, z, rr, rows]

    def step2_copy(name, which, d):
        k = ids[name]
        z = zfrom(d)
        if which < 2:
            src = quarter_of(name, source[name], zi) if d == 0 else W[name].at[x, z, ri]
            dst = W[name].at[x, z, ri]
        else:
            src = dst = half_of(name, x, z, ro, False) if which == 2 else half_of(name, xo, z, ri, True)
        to = over_x if which in (1, 2) else over_r
        return remote(src, dst, s2_send.at[k, which, d], s2_recv.at[k, which, d], to)

    def step2_arrival(name, which, d):
        k = ids[name]
        z = zfrom(d)
        if which < 2:
            ref = W[name].at[x, z, ro] if which == 0 else W[name].at[xo, z, ri]
        else:
            ref = half_of(name, xo, z, ro, which == 3)
        to = over_x if which in (1, 2) else over_r
        return remote(ref, ref, s2_send.at[k, which, d], s2_recv.at[k, which, d], to)

    def relay1(*names):
        for name in names:
            for d in range(1, Z):
                step1_copy(name, d).start()

    def relay0(*names):
        for name in names:
            step1_local(name).start()
            step2_copy(name, 0, 0).start()
            step2_copy(name, 1, 0).start()

    def relay2(name, ds=(1, 2, 3)):
        k = ids[name]
        for d in ds:
            slot = W[name].at[x, zfrom(d), ri]
            remote(slot, slot, s1_send.at[k, d - 1], s1_recv.at[k, d - 1], dev(zto(d))).wait_recv()
            step2_copy(name, 0, d).start()
            step2_copy(name, 1, d).start()

    def relay3(name, ds=(0, 1, 2, 3)):
        for d in ds:
            step2_arrival(name, 0, d).wait_recv()
            step2_copy(name, 2, d).start()
            step2_arrival(name, 1, d).wait_recv()
            step2_copy(name, 3, d).start()

    def relay4(*names):
        for name in names:
            step1_local(name).wait()
            for d in range(Z):
                step2_arrival(name, 2, d).wait_recv()
                step2_arrival(name, 3, d).wait_recv()

    def relay_sent():
        for name in ARRAYS:
            for d in range(1, Z):
                step1_copy(name, d).wait_send()
            for which in range(4):
                for d in range(Z):
                    step2_copy(name, which, d).wait_send()

    @pl.when(p == 0)
    def _():
        relay0("P1", "P2")
        relay1("P1", "P2")
        relay0("Q", "O", "E", "Gi", "Go", "F1", "F2")

    @pl.when(p == 1)
    def _():
        dx3[...] = tcot_in[x]
        dcot[...] = gcot_in[x]
        dx3_all[zi] = tcot_in[x]
        gather_start("dx3", dx3_all, keep=False)

    for c in v_arrivals:
        c.wait_recv()
    remote(aq.at[xo], aq.at[xo], q_send, q_recv, over_x).wait_recv()
    low_lanes = lax.broadcasted_iota(jnp.int32, (64, LANE), 1) < LANE // 2
    for z in range(Z):
        first, second = vv[2 * z], pltpu.roll(vv[2 * z + 1], LANE // 2, 1)
        vec_c[:, z * cz : z * cz + LANE] = first[:, 0:LANE]
        vec_c[:, z * cz + LANE : z * cz + 2 * LANE] = jnp.where(
            low_lanes, first[:, LANE:], second[:, 0:LANE]
        )
        vec_c[:, z * cz + 2 * LANE : (z + 1) * cz] = second[:, LANE:]
    for i in range(Z * R):
        vec_d[:, i * LANE : (i + 1) * LANE] = vv[i, 56:64, 0:LANE]

    def gain_d(row):
        return vec_d[row : row + 1, :]

    def gain_c(row):
        return vec_c[row : row + 1, :]

    def token_entry():
        n_hat, _ = normed(wide(x_in[...]))
        n1_all[zi] = low(n_hat * gain_d(0))
        gather_start("n1", n1_all, keep=False)

    def conv_entry():
        @pl.loop(0, c_dim // LANE)
        def _(ch):
            lanes = lanes_of(ch, LANE)
            taps = vec_c[:, lanes]
            cn[:, lanes] = depthwise(wide(c_in[:, lanes]), lambda k: taps[k : k + 1], 7)

        n_hat, rs = normed(cn[...])
        cn[...] = n_hat
        crs[...] = jnp.broadcast_to(rs, crs.shape)
        f_all[zi] = low(n_hat * gain_c(49))
        gather_start("f", f_all, keep=False)

    def first_relays():
        relay2("P1")
        relay1("Q", "O")
        relay2("P2")
        relay3("P1")

    sent.extend(gather_copies("n1", n1_all))
    sent.extend(gather_copies("f", f_all))

    @pl.when(p == 0)
    def _():
        first = order_in[0, x] == 0
        c_in[...] = jnp.where(first, grid_in[0], grid_in[1])
        x_in[...] = jnp.where(first, tok_in[0], tok_in[1])
        conv_entry()
        token_entry()
        first_relays()

    @pl.when(p == 1)
    def _():
        pl.semaphore_wait(go, 1)
        relay0("P1", "P2")
        relay1("P1", "P2")
        relay0("Q", "O", "E", "Gi", "Go", "F1", "F2")
        first_relays()
        remote(c_in, c_in, h_send.at[1], h_recv.at[1], sib).wait_recv()
        conv_entry()

    relay2("Q")
    relay2("O")
    relay1("E", "Gi", "Go")
    relay3("P2", (0, 1))
    relay4("P1")
    gather_wait("f", f_all)

    def conv_hidden(j):
        act, der = gelu_pair(mm(flat(f_all[...]), flat(W["P1"][j])))
        r[j] = low(act)
        rp[j] = low(der)

    conv_hidden(0)

    relay3("P2", (2, 3))
    for name in ("E", "Gi", "Go"):
        relay2(name)
    relay1("F1")
    conv_hidden(1)
    relay3("Q")
    relay3("O")
    relay2("F1")
    relay1("F2")

    @pl.when(p == 0)
    def _():
        pl.semaphore_signal(go, inc=1, device_id=sib, device_id_type=pl.DeviceIdType.MESH)

    relay4("P2")

    def pair_rows(name, pair):
        zs = pl.ds(pair * 2, 2)
        return side_by_side([flat(W[name][0, zs]), flat(W[name][1, zs])])

    def pair_out(left, name, sb, width):
        both = side_by_side([left[0], left[1]])

        @pl.loop(0, Z // 2)
        def _(pair):
            acc = mm_nt(both, pair_rows(name, pair))
            sb[:, :, lanes_of(pair, 2 * width)] = low(acc).reshape(Z, TOK, 2 * width)

    pair_out(r, "P2", cv_sb, cz)
    scatter_start("cv", cv_sb, cv_rb)

    for name in ("E", "Gi", "Go"):
        relay3(name)
    relay2("F2")

    @pl.when(p == 1)
    def _():
        remote(x_in, x_in, h_send.at[0], h_recv.at[0], sib).wait_recv()
        token_entry()

    relay4("Q", "O")
    gather_wait("n1", n1_all)
    wide_q = side_by_side([flat(W["Q"][j, :, :, s]) for j in range(2) for s in range(3)])
    qkv_both = low(mm(flat(n1_all[...]), wide_q))
    for j in range(2):
        qkv[j] = qkv_both[:, j * 3 * hq : (j + 1) * 3 * hq]
    for j in range(2):
        for b in range(Z):
            rows = slice(b * TOK, (b + 1) * TOK)
            outs = []
            for h in range(hq // HD):
                q, kk, vals = (qkv[j, rows, s * hq + h * HD : s * hq + (h + 1) * HD] for s in range(3))
                sc = mm_nt(q, kk) * HD ** (-0.5)
                e = jnp.exp(sc - jnp.max(sc, axis=-1, keepdims=True))
                pr = low(e / jnp.sum(e, axis=-1, keepdims=True))
                prob[j, h, b] = pr
                outs.append(mm(pr, vals))
            ctx[j, rows, :] = low(side_by_side(outs))

    out_cols = [
        jnp.concatenate([W["O"][0, z, rr], W["O"][1, z, rr]], axis=0) for z in range(Z) for rr in range(R)
    ]
    o_sb[...] = low(mm(side_by_side([ctx[0], ctx[1]]), side_by_side(out_cols))).reshape(Z, TOK, d_dim)
    scatter_start("o", o_sb, o_rb)

    relay3("F1")

    scatter_wait("cv", cv_rb)
    cv_sum[...] = scattered(cv_sb, cv_rb)
    c2f[...] = wide(c_in[...]) + gain_c(50) * cv_sum[...]
    c2_low = low(c2f[...])
    c2_all[zi] = c2_low
    gather_start("c2", c2_all)
    hid_grid[x] = c2_low

    @pl.when(p == 0)
    def _():
        remote(hid_grid.at[x], c_in, h_send.at[1], h_recv.at[1], sib).start()

    relay3("F2")
    scatter_wait("o", o_rb)
    x1[...] = wide(x_in[...]) + scattered(o_sb, o_rb)
    n_hat, _ = normed(x1[...])
    n2_all[zi] = low(n_hat * gain_d(1))
    gather_start("n2", n2_all)

    relay4("E", "Gi", "Go")
    gather_wait("c2", c2_all)
    row8 = lax.broadcasted_iota(jnp.int32, (8, adq), 0)
    gs_part = None
    ad_both = mm(flat(c2_all[...]), side_by_side([flat(W["E"][0]), flat(W["E"][1])]))
    for j in range(2):
        ad = ad_both[:, j * adq : (j + 1) * adq]
        adapted[j] = ad
        taps = aq[j]
        pool = jnp.zeros((8, adq), F32)
        for b in range(Z):
            sp = depthwise(ad[b * TOK : (b + 1) * TOK], lambda k: taps[k : k + 1], 3)
            spread[j, b] = sp
            pool = jnp.where(row8 == b, jnp.mean(sp, axis=0, keepdims=True), pool)
        pooled[j] = pool
        term = mm_nt(low(pool), flat(W["Gi"][j]))
        gs_part = term if gs_part is None else gs_part + term
    gsb[3] = gs_part
    share_start("gs", gsb)

    relay4("F1")
    gather_wait("n2", n2_all)
    for j in range(2):
        act, der = gelu_pair(mm(flat(n2_all[...]), flat(W["F1"][j])))
        u[j] = low(act)
        up[j] = low(der)

    scatter_wait("gs", gsb)

    def gate_hidden():
        return gelu_pair((gsb[0] + gsb[1]) + (gsb[2] + gsb[3]))

    gh, _ = gate_hidden()
    for j in range(2):
        g8 = jnp.tanh(mm(low(gh), flat(W["Go"][j])))
        gate[j] = g8
        for b in range(Z):
            br_sb[b, :, j * adq : (j + 1) * adq] = low(g8[b : b + 1] * spread[j, b])
    scatter_start("br", br_sb, br_rb)
    relay4("F2")

    u_both = side_by_side([u[0], u[1]])

    @pl.loop(0, Z // 2)
    def _(pair):
        halves = [
            side_by_side([W["F2"][j, 2 * pair + dz_, rr] for dz_ in range(2) for rr in range(R)])
            for j in range(2)
        ]
        acc = mm(u_both, jnp.concatenate(halves, axis=0))
        m_sb[:, :, lanes_of(pair, 2 * dz)] = low(acc).reshape(Z, TOK, 2 * dz)

    scatter_start("m", m_sb, m_rb)

    def exchange(n, buf):
        remote(buf.at[x], buf.at[x], xo_send.at[n], xo_recv.at[n], over_x).start()

    def layer_output(total):
        scatter_wait("br", br_rb)
        total[...] = x1[...]
        for d in range(Z):
            piece = br_sb[zi] if d == 0 else br_rb[d - 1]
            for j in range(2):
                lanes = pl.ds(pl.multiple_of(j * adh + zfrom(d) * adq, LANE), adq)
                total[:, lanes] += wide(piece[:, j * adq : (j + 1) * adq])
        scatter_wait("m", m_rb)
        hid_tok[x] = low(total[...] + scattered(m_sb, m_rb))

    @pl.when(p == 0)
    def _():
        layer_output(dx1)
        remote(hid_tok.at[x], x_in, h_send.at[0], h_recv.at[0], sib).start()
        exchange(0, hid_tok)

    exchange(1, hid_grid)
    relay_sent()

    def over_cores(d):
        return remote(
            out_gtok.at[x], dx3_all.at[zi], b_send.at[d], b_recv.at[d], dev(zto(d), pp=1 - p)
        )

    @pl.when(p == 1)
    def _():
        gather_wait("dx3", dx3_all)
        for c in gather_copies("dx3", dx3_all):
            c.wait_send()

    @pl.when(p == 0)
    def _():
        for d in range(Z):
            slot = dx3_all.at[zfrom(d)]
            remote(slot, slot, b_send.at[d], b_recv.at[d], sib).wait_recv()
        dx3[...] = dx3_all[zi]

    def own_lanes(j):
        return pl.ds(pl.multiple_of(j * adh + zi * adq, LANE), adq)

    gh, ghp = gate_hidden()
    dgh_part = None
    dgp = []
    for j in range(2):
        dgate = jnp.zeros((8, adq), F32)
        for b in range(Z):
            dbr = wide(dx3_all[b, :, own_lanes(j)])
            dgate = jnp.where(row8 == b, jnp.sum(dbr * spread[j, b], axis=0, keepdims=True), dgate)
        dg8 = low(dgate * (1.0 - gate[j] * gate[j]))
        dgp.append(dg8)
        term = mm_nt(dg8, flat(W["Go"][j]))
        dgh_part = term if dgh_part is None else dgh_part + term
    dgb[3] = dgh_part
    share_start("dgh", dgb)

    for j in range(2):
        cols = side_by_side([W["F2"][j, z, rr] for z in range(Z) for rr in range(R)])
        dh[j] = low(mm_nt(flat(dx3_all[...]), cols) * wide(up[j]))

    scatter_wait("dgh", dgb)
    dgs = low(((dgb[0] + dgb[1]) + (dgb[2] + dgb[3])) * ghp)
    for j in range(2):
        dpool = mm(dgs, flat(W["Gi"][j])) * (1.0 / TOK)
        taps = aq[j]
        tap_rows = [None] * 9
        for b in range(Z):
            dsp = gate[j, b : b + 1] * wide(dx3_all[b, :, own_lanes(j)]) + dpool[b : b + 1]
            dad[j, b * TOK : (b + 1) * TOK] = low(depthwise(dsp, lambda k: taps[8 - k : 9 - k], 3))

            def put(k, row):
                tap_rows[k] = row if tap_rows[k] is None else tap_rows[k] + row

            depthwise_taps(adapted[j, b * TOK : (b + 1) * TOK], dsp, 3, put)
        for k in range(9):
            gad[j, k : k + 1] = tap_rows[k]
        gad[j, 9:16] = jnp.zeros((7, adq), F32)

    pair_out(dad, "E", dc2_sb, cz)

    scatter_start("dc2", dc2_sb, dc2_rb)

    pair_out(dh, "F1", dn2_sb, dz)

    scatter_start("dn2", dn2_sb, dn2_rb)

    def half_rows(name, upper):
        half = W[name].shape[-2] // 2
        rows = slice(half, None) if upper else slice(0, half)
        return (slice(None), rows) if len(W[name].shape) == 6 else (rows,)

    def hop_copy(name, which):
        n = ids[name]
        lower, upper = half_rows(name, False), half_rows(name, True)
        src, to = (
            lambda: (W[name].at[(xo, slice(None), slice(None)) + lower], over_x),
            lambda: (W[name].at[(slice(None), slice(None), ro) + upper], over_r),
            lambda: (RX[name][0].at[:, ro], over_r),
            lambda: (RX[name][1].at[xo], over_x),
        )[which]()
        return remote(src, RX[name][which], g_send.at[n, which], g_recv.at[n, which], to)

    def reduce_start(name):
        hop_copy(name, 0).start()
        hop_copy(name, 1).start()

    def reduce_middle(*names):
        for name in names:
            lower, upper = half_rows(name, False), half_rows(name, True)
            buf = RX[name]
            hop_copy(name, 0).wait_recv()

            @pl.loop(0, Z)
            def _(z):
                for rr in range(R):
                    own = W[name][(x, z, rr) + lower]
                    buf[0][z, rr] = low(wide(own) + wide(buf[0][z, rr]))

            hop_copy(name, 2).start()
            hop_copy(name, 1).wait_recv()

            @pl.loop(0, Z)
            def _(z):
                for j in range(2):
                    own = W[name][(j, z, ri) + upper]
                    buf[1][j, z] = low(wide(own) + wide(buf[1][j, z]))

            hop_copy(name, 3).start()

    def reduce_end(*names):
        for name in names:
            lower, upper = half_rows(name, False), half_rows(name, True)
            buf = RX[name]
            hop_copy(name, 2).wait_recv()
            hop_copy(name, 3).wait_recv()

            @pl.loop(0, Z)
            def _(z):
                W[name][(x, z, ri) + lower] = low(wide(buf[0][z, ri]) + wide(buf[2][z]))
                W[name][(x, z, ri) + upper] = low(wide(buf[1][x, z]) + wide(buf[3][z]))

            for d in range(1, Z):
                back_copy(name, d).start()
            back_local(name).start()

    def back_copy(name, d):
        n = ids[name]
        return remote(
            W[name].at[x, zto(d), ri], quarter_of(name, native[name], zi),
            a_send.at[n, d - 1], a_recv.at[n, d - 1], dev(zto(d)),
        )

    def back_local(name):
        return pltpu.make_async_copy(
            W[name].at[x, zi, ri], quarter_of(name, native[name], zi), loc_sem.at[ids[name]]
        )

    peers = ((1, 0), (0, 1), (1, 1))

    def owner(k):
        return (ro if peers[k][0] else ri), (xo if peers[k][1] else x)

    def row_grad(name, left, right):
        width = W[name].shape[3]
        span = R * width

        @pl.loop(0, Z)
        def _(z):
            turned[0:span] = flat(left[:, :, lanes_of(z, span)]).T
            for j in range(2):
                W[name][j, z] = low(mm(turned[0:span], right[j])).reshape(R, width, -1)

        reduce_start(name)

    def col_grad(name, left, right):
        width = left.shape[2]
        for j in range(2):
            turned[j * width : (j + 1) * width] = left[j].T

        @pl.loop(0, Z)
        def _(z):
            rhs = flat(right[:, :, lanes_of(z, dz)])
            for j in range(2):
                g = low(mm(turned[j * width : (j + 1) * width], rhs))
                for rr in range(R):
                    W[name][j, z, rr] = g[:, rr * LANE : (rr + 1) * LANE]

        reduce_start(name)

    for j in range(2):
        W["Gi"][j] = low(mm_tn(dgs, low(pooled[j]))).reshape(Z, R, -1, adq)
        W["Go"][j] = low(mm_tn(low(gh), dgp[j])).reshape(Z, R, -1, adq)
    reduce_start("Gi")
    reduce_start("Go")
    row_grad("E", c2_all, dad)

    @pl.when(p == 0)
    def _():
        remote(dcot, dcot, c_send, c_recv, sib).wait_recv()

    scatter_wait("dc2", dc2_rb)
    dc2t[...] = wide(dcot[...]) + scattered(dc2_sb, dc2_rb)
    gvs_ls = jnp.sum(cv_sum[...] * dc2t[...], axis=0, keepdims=True)
    dcv_all[zi] = low(dc2t[...] * gain_c(50))
    gather_start("dcv", dcv_all)

    scatter_wait("dn2", dn2_rb)
    dn2 = scattered(dn2_sb, dn2_rb)
    n_hat, rs = normed(x1[...])
    gvs_d1 = jnp.sum(dn2 * n_hat, axis=0, keepdims=True)
    dx1[...] = wide(dx3[...]) + norm_back(dn2, n_hat, rs, gain_d(1))
    dx1_all[zi] = low(dx1[...])
    gather_start("dx1", dx1_all)

    col_grad("F2", u, dx3_all)
    row_grad("F1", n2_all, dh)

    gather_wait("dcv", dcv_all)
    for j in range(2):
        dhc[j] = low(mm(flat(dcv_all[...]), flat(W["P2"][j])) * wide(rp[j]))

    pair_out(dhc, "P1", df_sb, cz)
    scatter_start("df", df_sb, df_rb)

    early = ("Gi", "Go", "E", "F2", "F1")

    def pw_grads():
        row_grad("P2", dcv_all, r)
        row_grad("P1", f_all, dhc)

    @pl.when(p == 0)
    def _():
        pw_grads()
        reduce_middle(*early)

    gather_wait("dx1", dx1_all)
    out_rows = [
        side_by_side([W["O"][j, z, rr] for z in range(Z) for rr in range(R)]) for j in range(2)
    ]
    do_both = low(mm_nt(flat(dx1_all[...]), jnp.concatenate(out_rows, axis=0)))
    for j in range(2):
        do_all[j] = do_both[:, j * hq : (j + 1) * hq]
    for j in range(2):
        for b in range(Z):
            rows = slice(b * TOK, (b + 1) * TOK)
            parts = [[], [], []]
            for h in range(hq // HD):
                q, kk, vals = (qkv[j, rows, s * hq + h * HD : s * hq + (h + 1) * HD] for s in range(3))
                do = do_all[j, rows, h * HD : (h + 1) * HD]
                pr = prob[j, h, b]
                dp = mm_nt(do, vals)
                prw = wide(pr)
                ds = low(prw * (dp - jnp.sum(dp * prw, axis=-1, keepdims=True)) * HD ** (-0.5))
                parts[0].append(mm(ds, kk))
                parts[1].append(mm_tn(ds, q))
                parts[2].append(mm_tn(pr, do))
            for s in range(3):
                dqkv[j, rows, s * hq : (s + 1) * hq] = low(side_by_side(parts[s]))

    dqkv_both = side_by_side([dqkv[0], dqkv[1]])

    @pl.loop(0, Z // 2)
    def _(pair):
        zs = pl.ds(pair * 2, 2)
        rows_q = side_by_side([flat(W["Q"][j, zs, :, s]) for j in range(2) for s in range(3)])
        acc = mm_nt(dqkv_both, rows_q)
        dn1_sb[:, :, lanes_of(pair, 2 * dz)] = low(acc).reshape(Z, TOK, 2 * dz)

    scatter_start("dn1", dn1_sb, dn1_rb)

    def attention_grads():
        @pl.loop(0, Z)
        def _(z):
            turned[0:dz] = flat(n1_all[:, :, lanes_of(z, dz)]).T
            for j in range(2):
                g = low(mm(turned[0:dz], dqkv[j]))
                for s in range(3):
                    W["Q"][j, z, :, s] = g[:, s * hq : (s + 1) * hq].reshape(R, -1, hq)

        reduce_start("Q")
        col_grad("O", ctx, dx1_all)

    @pl.when(p == 0)
    def _():
        attention_grads()
        reduce_end(*early)
        reduce_middle("P2", "P1")

    scatter_wait("dn1", dn1_rb)
    dn1 = scattered(dn1_sb, dn1_rb)
    n_hat, rs = normed(wide(x_in[...]))
    gvs_d0 = jnp.sum(dn1 * n_hat, axis=0, keepdims=True)
    out_gtok[x] = low(dx1[...] + norm_back(dn1, n_hat, rs, gain_d(0)))

    @pl.when(p == 1)
    def _():
        for d in (1, 2, 3, 0):
            over_cores(d).start()

    scatter_wait("df", df_rb)
    dfv = scattered(df_sb, df_rb)
    gvs_lc = jnp.sum(dfv * cn[...], axis=0, keepdims=True)
    dcn[...] = norm_back(dfv, cn[...], crs[:, 0:1], gain_c(49))

    @pl.loop(0, c_dim // LANE)
    def _(ch):
        lanes = lanes_of(ch, LANE)
        taps = vec_c[:, lanes]
        back = depthwise(dcn[:, lanes], lambda k: taps[48 - k : 49 - k], 7)
        out_ggrid[x, :, lanes] = low(dc2t[:, lanes] + back)

    @pl.when(p == 1)
    def _():
        remote(out_ggrid.at[x], dcot, c_send, c_recv, sib).start()
        layer_output(dx1)
        exchange(0, hid_tok)
        pw_grads()
        reduce_middle(*early)
        attention_grads()
        reduce_end(*early)
        reduce_middle("P2", "P1")

    exchange(2, out_gtok)
    exchange(3, out_ggrid)

    @pl.loop(0, Z)
    def _(z):
        for part in range(cz // LANE):
            lanes = pl.ds(pl.multiple_of(z * cz + part * LANE, LANE), LANE)

            def put(k, row):
                gvs[z, k : k + 1, part * LANE : (part + 1) * LANE] = row

            depthwise_taps(wide(c_in[:, lanes]), dcn[:, lanes], 7, put)

    for z in range(Z):
        gvs[z, 49:50] = gvs_lc[:, z * cz : (z + 1) * cz]
        gvs[z, 50:51] = gvs_ls[:, z * cz : (z + 1) * cz]
        gvs[z, 51:64] = jnp.zeros((13, cz), F32)
        gvs[z, 56:57, 0:dz] = gvs_d0[:, z * dz : (z + 1) * dz]
        gvs[z, 57:58, 0:dz] = gvs_d1[:, z * dz : (z + 1) * dz]
    scatter_start("gv", gvs, gv_rb)

    def group_copy(n, k, src, dst):
        rr, xx = owner(k)
        return remote(src, dst, gx_send.at[n, k], gx_recv.at[n, k], dev(rr=rr, xx=xx))

    for k in range(3):
        c = group_copy(1, k, gad, gad_rb.at[k])
        c.start()
        sent.append(c)
    scatter_wait("gv", gv_rb)
    gvx[3] = (gvs[zi] + gv_rb[0]) + (gv_rb[1] + gv_rb[2])
    for k in range(3):
        c = group_copy(0, k, gvx.at[3], gvx.at[k])
        c.start()
        sent.append(c)
    for k in range(3):
        group_copy(1, k, gad, gad_rb.at[k]).wait_recv()
    gad_all[zi] = (gad[x] + gad_rb[0, x]) + (gad_rb[1, x] + gad_rb[2, x])
    gather_start("gad", gad_all)

    reduce_middle("Q", "O")
    reduce_end("P2", "P1", "Q", "O")

    for k in range(3):
        group_copy(0, k, gvx.at[k], gvx.at[k]).wait_recv()
    total = (gvx[0] + gvx[1]) + (gvx[2] + gvx[3])
    mine = jnp.where(ri == 1, pltpu.roll(total, c_own, 1), total)[:, 0:c_own]
    mine_d = jnp.where(ri == 1, total[:, LANE : 2 * LANE], total[:, 0:LANE])

    def flag(n):
        return train_in[0, n].astype(F32)

    out_depth[...] = mine[0:taps7] * flag(0)
    out_ln_conv[...] = mine[49:50] * flag(1)
    out_scale[...] = mine[50:51] * flag(4)
    out_ln_attn[...] = mine_d[56:57]
    out_ln_mlp[...] = mine_d[57:58]
    gather_wait("gad", gad_all)
    for z in range(Z):
        out_ad[:, z * adq : (z + 1) * adq] = gad_all[z][0:9]
    for name in ARRAYS:
        back_local(name).wait()
        for d in range(1, Z):
            n = ids[name]
            slot = quarter_of(name, native[name], zfrom(d))
            remote(slot, slot, a_send.at[n, d - 1], a_recv.at[n, d - 1], dev(zto(d))).wait_recv()
    for n, buf in enumerate((hid_tok, hid_grid, out_gtok, out_ggrid)):
        c = remote(buf.at[x], buf.at[x], xo_send.at[n], xo_recv.at[n], over_x)
        c.wait_send()
        remote(buf.at[xo], buf.at[xo], xo_send.at[n], xo_recv.at[n], over_x).wait_recv()

    @pl.when(p == 0)
    def _():
        remote(hid_tok.at[x], x_in, h_send.at[0], h_recv.at[0], sib).wait_send()
        remote(hid_grid.at[x], c_in, h_send.at[1], h_recv.at[1], sib).wait_send()

    @pl.when(p == 1)
    def _():
        for d in range(Z):
            over_cores(d).wait_send()
        remote(out_ggrid.at[x], dcot, c_send, c_recv, sib).wait_send()

    for c in sent:
        c.wait_send()
    for name in ARRAYS:
        for which in range(4):
            hop_copy(name, which).wait_send()
        for d in range(1, Z):
            back_copy(name, d).wait_send()


def run_layers(weights, vectors, order, train, streams, sizes, outer):
    d_dim, c_dim, hq, ffq, cfq, adw, dg = sizes
    vm = pltpu.VMEM
    blocks = []
    for name, value in zip(ARRAYS, weights):
        if name == "Q":
            blocks.append((3, value.shape[1], hq))
        elif name in ("O", "F2"):
            blocks.append((value.shape[0] // Z, value.shape[1]))
        else:
            blocks.append((value.shape[0], value.shape[1] // Z))
    rows = Z * TOK

    def act(width, count=Z, kind=BF):
        return vm((count, TOK, width), kind)

    scratch = [vm((2, Z, R) + s, BF) for s in blocks] + [
        vm(lead + s[:-2] + (s[-2] // 2, s[-1]), BF)
        for s in blocks
        for lead in ((Z, R), (2, Z), (Z,), (Z,))
    ]
    scratch += [
        vm((64, 2 * LANE), F32), vm((Z * R, 64, 2 * LANE), F32), vm((2, 16, adw), F32), vm((64, c_dim), F32), vm((8, d_dim), F32),
        vm((TOK, d_dim), BF), vm((TOK, c_dim), BF), act(d_dim), act(c_dim), act(d_dim), act(c_dim),
        act(d_dim), act(d_dim, 3), act(c_dim), act(c_dim, 3), act(d_dim), act(d_dim, 3),
        act(2 * adw), act(2 * adw, 3), vm((4, 8, dg), F32), vm((4, 8, dg), F32),
        vm((2, rows, 3 * hq), BF), vm((2, hq // HD, Z, TOK, TOK), BF), vm((2, rows, hq), BF),
        vm((2, rows, ffq), BF), vm((2, rows, ffq), BF), vm((2, rows, cfq), BF), vm((2, rows, cfq), BF),
        vm((TOK, c_dim), F32), vm((TOK, LANE), F32), vm((TOK, c_dim), F32), vm((TOK, d_dim), F32), vm((TOK, c_dim), F32),
        vm((2, rows, adw), F32), vm((2, Z, TOK, adw), F32), vm((2, 8, adw), F32), vm((2, 8, adw), F32),
        vm((TOK, d_dim), BF), vm((TOK, c_dim), BF), act(d_dim), act(d_dim), act(d_dim, 3), act(c_dim), act(c_dim, 3),
        act(d_dim), act(c_dim),
        act(d_dim), act(d_dim, 3), act(c_dim), act(c_dim, 3), vm((2, rows, ffq), BF), vm((2, rows, hq), BF),
        vm((2, rows, 3 * hq), BF), vm((2, rows, cfq), BF), vm((TOK, d_dim), F32), vm((TOK, c_dim), F32), vm((2, rows, adw), BF),
        vm((TOK, c_dim), F32),
        vm((Z, 64, c_dim // Z), F32), vm((3, 64, c_dim // Z), F32), vm((4, 64, c_dim // Z), F32),
        vm((2, 16, adw), F32), vm((3, 2, 16, adw), F32), vm((Z, 16, adw), F32),
        vm((2 * ffq, rows), BF),
    ]
    dma = pltpu.SemaphoreType.DMA
    na = len(ARRAYS)
    scratch += [
        dma((len(EVENTS), 3)), dma((len(EVENTS), 3)), dma((na, 3)), dma((na, 3)), dma((na,)),
        dma((na, 4, Z)), dma((na, 4, Z)), dma((7,)), dma((7,)), dma, dma, dma((2,)), dma((2,)), dma((Z,)), dma((Z,)), dma, dma,
        dma((4,)), dma((4,)), dma((na, 4)), dma((na, 4)), dma((na, 3)), dma((na, 3)), dma((2, 3)), dma((2, 3)),
        pltpu.SemaphoreType.REGULAR,
    ]
    sds = jax.ShapeDtypeStruct
    out_shape = [sds((2, TOK, d_dim), BF), sds((2, TOK, c_dim), BF)] * 2
    out_shape += [sds(value.shape, BF) for value in weights]
    out_shape += [sds(value.shape, F32) for value in vectors]
    any_spec = pl.BlockSpec(memory_space=pl.ANY)
    vm_spec = pl.BlockSpec(memory_space=pltpu.VMEM)
    sm_spec = pl.BlockSpec(memory_space=pltpu.SMEM)
    return pl.pallas_call(
        functools.partial(main_kernel, sizes, outer),
        out_shape=out_shape,
        in_specs=[any_spec] * na + [vm_spec] * 6 + [sm_spec] * 2 + [vm_spec] * 4,
        out_specs=[vm_spec] * 4 + [any_spec] * na + [vm_spec] * 6,
        scratch_shapes=scratch,
        compiler_params=pltpu.CompilerParams(
            collective_id=0, has_side_effects=True, vmem_limit_bytes=62 * 1024 * 1024
        ),
        cost_estimate=pl.CostEstimate(flops=26 * 10**9, bytes_accessed=10**8, transcendentals=10**7),
        name="layers",
    )(*weights, *vectors, order, train, *streams)


def per_device(
    tokens,
    conv_grid,
    order,
    trainable,
    ln_attn,
    w_qkv,
    w_attn_out,
    ln_mlp,
    w_fc_in,
    w_fc_out,
    conv_depth,
    ln_conv,
    w_pw_in,
    w_pw_out,
    layer_scale,
    w_adapt,
    adapt_depth,
    w_gate_in,
    w_gate_out,
    tok_cot,
    grid_cot,
):
    dp_count = lax.axis_size("dp")
    outer = dp_count // (Z * R)
    groups = [[g * outer + o for o in range(outer)] for g in range(Z * R)]
    layer_at = lax.axis_index("pipe")

    def block(value, axis):
        value = value[0]
        if outer == 1:
            return value
        return lax.all_gather(value, "dp", axis=axis, tiled=True, axis_index_groups=groups)

    def share(value, axis):
        if outer > 1:
            value = lax.psum_scatter(
                value, "dp", scatter_dimension=axis, tiled=True, axis_index_groups=groups
            )
        return value[None]

    qkv = block(w_qkv, 1)
    gate_in = block(w_gate_in, 1).T
    pw_in = block(w_pw_in, 0)
    adapt = block(w_adapt, 0)
    fc_in = block(w_fc_in, 0)
    weights = (
        pw_in,
        block(w_pw_out, 1).T,
        qkv,
        block(w_attn_out, 1),
        adapt,
        gate_in,
        block(w_gate_out, 0),
        fc_in,
        block(w_fc_out, 1),
    )
    vectors = (
        block(conv_depth, 1),
        block(ln_conv, 0)[None],
        block(layer_scale, 0)[None],
        block(ln_attn, 0)[None],
        block(ln_mlp, 0)[None],
        adapt_depth[0],
    )
    spread = Z * R
    sizes = (
        qkv.shape[1] * spread, pw_in.shape[0] * spread, qkv.shape[2] // Z, fc_in.shape[1] // Z,
        pw_in.shape[1] // Z, adapt.shape[1] // Z, gate_in.shape[0] * spread,
    )

    def rows_of(value):
        return value.reshape(value.shape[0], TOK, value.shape[-1])

    streams = [rows_of(value) for value in (tokens, conv_grid, tok_cot, grid_cot)]
    outs = run_layers(weights, vectors, order, trainable, streams, sizes, outer)
    hid_tok, hid_grid, g_tok, g_grid = outs[:4]
    g_p1, g_p2, g_q, g_o, g_e, g_gi, g_go, g_f1, g_f2 = [value.astype(F32) for value in outs[4:13]]
    g_depth, g_ln_conv, g_scale, g_ln_attn, g_ln_mlp, g_ad = outs[13:]

    swap = (layer_at == 0) & (order[0, 0] == 1)
    g_tok = jnp.where(swap, g_tok[::-1], g_tok)
    g_grid = jnp.where(swap, g_grid[::-1], g_grid)
    grid_shape = (1,) + conv_grid.shape
    tok_shape = (1,) + tokens.shape
    flags = trainable[0].astype(F32)
    if outer > 1:
        g_ad = lax.psum(g_ad, "dp", axis_index_groups=groups)
    return (
        hid_tok.reshape(tok_shape),
        hid_grid.reshape(grid_shape),
        g_tok.reshape(tok_shape),
        g_grid.reshape(grid_shape),
        share(g_ln_attn[0], 0),
        share(g_q, 1),
        share(g_o, 1),
        share(g_ln_mlp[0], 0),
        share(g_f1, 0),
        share(g_f2, 1),
        share(g_depth, 1),
        share(g_ln_conv[0], 0),
        share(g_p1 * flags[2], 0),
        share((g_p2 * flags[3]).T, 1),
        share(g_scale[0], 0),
        share(g_e, 0),
        g_ad[None],
        share(g_gi.T, 1),
        share(g_go, 0),
    )


def solution(mesh):
    in_specs = (
        P(None, "dp", None, None),
        P(None, "dp", None, None, None),
        P("dp", None),
        P("pipe", None),
        P("pipe", "dp"),
        P("pipe", None, "dp", "tensor"),
        P("pipe", "tensor", "dp"),
        P("pipe", "dp"),
        P("pipe", "dp", "tensor"),
        P("pipe", "tensor", "dp"),
        P("pipe", None, "dp"),
        P("pipe", "dp"),
        P("pipe", "dp", "tensor"),
        P("pipe", "tensor", "dp"),
        P("pipe", "dp"),
        P("pipe", "dp", "tensor"),
        P("pipe", None, "tensor"),
        P("pipe", "tensor", "dp"),
        P("pipe", "dp", "tensor"),
        P(None, "dp", None, None),
        P(None, "dp", None, None, None),
    )
    out_specs = (
        P("pipe", None, "dp", None, None),
        P("pipe", None, "dp", None, None, None),
        P("pipe", None, "dp", None, None),
        P("pipe", None, "dp", None, None, None),
        P("pipe", "dp"),
        P("pipe", None, "dp", "tensor"),
        P("pipe", "tensor", "dp"),
        P("pipe", "dp"),
        P("pipe", "dp", "tensor"),
        P("pipe", "tensor", "dp"),
        P("pipe", None, "dp"),
        P("pipe", "dp"),
        P("pipe", "dp", "tensor"),
        P("pipe", "tensor", "dp"),
        P("pipe", "dp"),
        P("pipe", "dp", "tensor"),
        P("pipe", None, "tensor"),
        P("pipe", "tensor", "dp"),
        P("pipe", "dp", "tensor"),
    )
    return jax.shard_map(
        per_device, mesh=mesh, in_specs=in_specs, out_specs=out_specs, check_vma=False
    )
```

```python
import functools

import jax
import jax.numpy as jnp
from jax import lax
from jax.experimental import pallas as pl
from jax.experimental.pallas import tpu as pltpu
from jax.sharding import PartitionSpec as P

HD = 64
Z = 4
R = 2
TOK = 64
SIDE = 8
LANE = 128
BF = jnp.bfloat16
F32 = jnp.float32
ARRAYS = ("P1", "P2", "Q", "O", "E", "Gi", "Go", "F1", "F2")
EVENTS = (
    "n1", "f", "o", "cv", "n2", "c2", "m", "br", "gs",
    "dx3", "dgh", "dn2", "dc2", "dx1", "dcv", "dn1", "df", "gv", "gad",
)


def mm(a, b):
    return lax.dot_general(a, b, (((1,), (0,)), ((), ())), preferred_element_type=F32)


def mm_nt(a, b):
    return lax.dot_general(a, b, (((1,), (1,)), ((), ())), preferred_element_type=F32)


def mm_tn(a, b):
    return lax.dot_general(a, b, (((0,), (0,)), ((), ())), preferred_element_type=F32)


def flat(value):
    return value.reshape(-1, value.shape[-1])


def low(value):
    return value.astype(BF)


def wide(value):
    return value.astype(F32)


def gelu_pair(h):
    phi = 0.5 * (1.0 + lax.erf(h * 0.7071067811865476))
    dens = jnp.exp(-0.5 * h * h) * 0.3989422804014327
    return h * phi, phi + h * dens


def normed(value):
    centred = value - jnp.mean(value, axis=-1, keepdims=True)
    rs = lax.rsqrt(jnp.mean(centred * centred, axis=-1, keepdims=True) + 1e-06)
    return centred * rs, rs


def norm_back(dn, n_hat, rs, gain):
    gd = dn * gain
    return (
        gd
        - jnp.mean(gd, axis=-1, keepdims=True)
        - n_hat * jnp.mean(gd * n_hat, axis=-1, keepdims=True)
    ) * rs


def col_shift(value, by):
    if by == 0:
        return value
    at = lax.broadcasted_iota(jnp.int32, value.shape, 0) % SIDE
    rolled = pltpu.roll(value, (-by) % TOK, 0)
    return jnp.where((at + by >= 0) & (at + by < SIDE), rolled, 0.0)


def row_shift(value, by):
    if by == 0:
        return value
    gap = jnp.zeros((abs(by) * SIDE, value.shape[1]), value.dtype)
    if by > 0:
        return jnp.concatenate([value[by * SIDE :], gap], axis=0)
    return jnp.concatenate([gap, value[: TOK + by * SIDE]], axis=0)


def depthwise(value, tap, side):
    half = side // 2
    shifted = [col_shift(value, b - half) for b in range(side)]
    total = None
    for a in range(side):
        line = None
        for b in range(side):
            term = shifted[b] * tap(a * side + b)
            line = term if line is None else line + term
        line = row_shift(line, a - half)
        total = line if total is None else total + line
    return total


def depthwise_taps(value, grad, side, put):
    half = side // 2
    shifted = [col_shift(value, b - half) for b in range(side)]
    for a in range(side):
        d = a - half
        lo, hi = max(0, -d) * SIDE, (SIDE - max(0, d)) * SIDE
        for b in range(side):
            part = shifted[b][lo + d * SIDE : hi + d * SIDE] * grad[lo:hi]
            put(a * side + b, jnp.sum(part, axis=0, keepdims=True))


def lanes_of(at, width):
    return pl.ds(pl.multiple_of(at * width, width), width)


def side_by_side(blocks):
    return jnp.concatenate(blocks, axis=1)


def main_kernel(dims, outer, *refs):
    at = iter(refs)

    def take(count):
        return [next(at) for _ in range(count)]

    na = len(ARRAYS)
    source = dict(zip(ARRAYS, take(na)))
    (
        depth_in, ln_conv_in, scale_in, ln_attn_in, ln_mlp_in, adapt_depth_in,
        order_in, train_in, tok_in, grid_in, tcot_in, gcot_in,
    ) = take(12)
    hid_tok, hid_grid, out_gtok, out_ggrid = take(4)
    native = dict(zip(ARRAYS, take(na)))
    out_depth, out_ln_conv, out_scale, out_ln_attn, out_ln_mlp, out_ad = take(6)
    W = dict(zip(ARRAYS, take(na)))
    hops = take(4 * na)
    RX = {name: hops[4 * n : 4 * n + 4] for n, name in enumerate(ARRAYS)}
    (
        v_loc, vv, aq, vec_c, vec_d, x_in, c_in, n1_all, f_all, n2_all, c2_all,
        o_sb, o_rb, cv_sb, cv_rb, m_sb, m_rb, br_sb, br_rb, gsb, dgb,
        qkv, prob, ctx, u, up, r, rp, cn, crs, cv_sum, x1, c2f,
        adapted, spread, pooled, gate,
        dx3, dcot, dx3_all, dn2_sb, dn2_rb, dc2_sb, dc2_rb, dx1_all, dcv_all,
        dn1_sb, dn1_rb, df_sb, df_rb, dh, do_all, dqkv, dhc, dx1, dc2t, dad, dcn,
        gvs, gv_rb, gvx, gad, gad_rb, gad_all, turned,
    ) = take(65)
    (
        zs_send, zs_recv, s1_send, s1_recv, loc_sem, s2_send, s2_recv,
        v_send, v_recv, q_send, q_recv, h_send, h_recv, b_send, b_recv, c_send, c_recv,
        xo_send, xo_recv, g_send, g_recv, a_send, a_recv, gx_send, gx_recv, go,
    ) = take(26)

    p = lax.axis_index("pipe")
    dpi = lax.axis_index("dp")
    x = lax.axis_index("tensor")
    rest = dpi % outer
    zi = dpi // (outer * R)
    ri = (dpi // outer) % R
    xo = 1 - x
    ro = 1 - ri
    d_dim, c_dim, hq, ffq, cfq, adq, dg = dims
    adh = Z * adq
    dz, cz = d_dim // Z, c_dim // Z
    tile = 256
    ids = {name: number for number, name in enumerate(ARRAYS)}
    ev = {name: number for number, name in enumerate(EVENTS)}

    def dev(z=None, rr=None, xx=None, pp=None):
        z = zi if z is None else z
        rr = ri if rr is None else rr
        return (
            p if pp is None else pp,
            (z * R + rr) * outer + rest,
            x if xx is None else xx,
        )

    def zto(d):
        return lax.rem(zi + d, Z)

    def zfrom(d):
        return lax.rem(zi + Z - d, Z)

    def remote(src, dst, ssem, rsem, device):
        return pltpu.make_async_remote_copy(
            src_ref=src, dst_ref=dst, send_sem=ssem, recv_sem=rsem,
            device_id=device, device_id_type=pl.DeviceIdType.MESH,
        )

    sib = dev(pp=1 - p)
    over_r, over_x = dev(rr=ro), dev(xx=xo)

    def z_copy(e, d, src, dst):
        return remote(src, dst, zs_send.at[e, d - 1], zs_recv.at[e, d - 1], dev(zto(d)))

    sent = []

    def gather_copies(name, buf):
        return [z_copy(ev[name], d, buf.at[zi], buf.at[zi]) for d in range(1, Z)]

    def gather_start(name, buf, keep=True):
        copies = gather_copies(name, buf)
        for c in copies:
            c.start()
        if keep:
            sent.extend(copies)

    def gather_wait(name, buf):
        for d in range(1, Z):
            slot = buf.at[zfrom(d)]
            z_copy(ev[name], d, slot, slot).wait_recv()

    def scatter_start(name, sb, rb):
        for d in range(1, Z):
            c = z_copy(ev[name], d, sb.at[zto(d)], rb.at[d - 1])
            c.start()
            sent.append(c)

    def scatter_wait(name, rb):
        for d in range(1, Z):
            z_copy(ev[name], d, rb.at[d - 1], rb.at[d - 1]).wait_recv()

    def share_start(name, buf):
        for d in range(1, Z):
            c = z_copy(ev[name], d, buf.at[3], buf.at[d - 1])
            c.start()
            sent.append(c)

    def scattered(sb, rb):
        return (wide(sb[zi]) + wide(rb[0])) + (wide(rb[1]) + wide(rb[2]))

    barrier = pltpu.get_barrier_semaphore()
    greeted = [sib]
    for d in range(1, Z):
        greeted += [dev(zto(d)), dev(zto(d), ro), dev(zto(d), pp=1 - p)]
    greeted += [over_r, over_x, dev(rr=ro, xx=xo)]
    for device in greeted:
        pl.semaphore_signal(barrier, inc=1, device_id=device, device_id_type=pl.DeviceIdType.MESH)
    v_loc[...] = jnp.zeros(v_loc.shape, F32)
    taps7 = depth_in.shape[0]
    c_own = depth_in.shape[1]
    v_loc[0:taps7, 0:c_own] = wide(depth_in[...])
    v_loc[49:50, 0:c_own] = wide(ln_conv_in[...])
    v_loc[50:51, 0:c_own] = wide(scale_in[...])
    v_loc[56:57, 0:LANE] = wide(ln_attn_in[...])
    v_loc[57:58, 0:LANE] = wide(ln_mlp_in[...])
    aq[x] = jnp.zeros(aq.shape[1:], F32)
    aq[x, 0:9] = wide(adapt_depth_in[:, lanes_of(zi, adq)])
    pl.semaphore_wait(barrier, len(greeted))

    me8 = zi * R + ri
    v_arrivals = []
    for n, (d, flip) in enumerate([(d, s) for d in range(Z) for s in (0, 1)][1:]):
        tr = ro if flip else ri
        c = remote(v_loc, vv.at[me8], v_send.at[n], v_recv.at[n], dev(zto(d), tr))
        c.start()
        sent.append(c)
        fr = zfrom(d) * R + tr
        v_arrivals.append(remote(vv.at[fr], vv.at[fr], v_send.at[n], v_recv.at[n], dev(zto(d), tr)))
    vv[me8] = v_loc[...]
    c = remote(aq.at[x], aq.at[x], q_send, q_recv, over_x)
    c.start()
    sent.append(c)

    by_rows = ("O", "F2")

    def quarter_of(name, ref, z):
        if name == "Q":
            return ref.at[:, :, lanes_of(z, hq)]
        if name in by_rows:
            height = ref.shape[0] // Z
            return ref.at[pl.ds(pl.multiple_of(z * height, height), height)]
        return ref.at[:, lanes_of(z, ref.shape[1] // Z)]

    def step1_local(name):
        return pltpu.make_async_copy(
            quarter_of(name, source[name], zi), W[name].at[x, zi, ri], loc_sem.at[ids[name]]
        )

    def step1_copy(name, d):
        k = ids[name]
        return remote(
            quarter_of(name, source[name], zto(d)), W[name].at[x, zi, ri],
            s1_send.at[k, d - 1], s1_recv.at[k, d - 1], dev(zto(d)),
        )

    def half_of(name, j, z, rr, upper):
        w = W[name]
        half = w.shape[-2] // 2
        rows = slice(half, None) if upper else slice(0, half)
        if len(w.shape) == 6:
            return w.at[j, z, rr, :, rows]
        return w.at[j, z, rr, rows]

    def step2_copy(name, which, d):
        k = ids[name]
        z = zfrom(d)
        if which < 2:
            src = quarter_of(name, source[name], zi) if d == 0 else W[name].at[x, z, ri]
            dst = W[name].at[x, z, ri]
        else:
            src = dst = half_of(name, x, z, ro, False) if which == 2 else half_of(name, xo, z, ri, True)
        to = over_x if which in (1, 2) else over_r
        return remote(src, dst, s2_send.at[k, which, d], s2_recv.at[k, which, d], to)

    def step2_arrival(name, which, d):
        k = ids[name]
        z = zfrom(d)
        if which < 2:
            ref = W[name].at[x, z, ro] if which == 0 else W[name].at[xo, z, ri]
        else:
            ref = half_of(name, xo, z, ro, which == 3)
        to = over_x if which in (1, 2) else over_r
        return remote(ref, ref, s2_send.at[k, which, d], s2_recv.at[k, which, d], to)

    def relay1(*names):
        for name in names:
            step1_local(name).start()
            for d in range(1, Z):
                step1_copy(name, d).start()
            step2_copy(name, 0, 0).start()
            step2_copy(name, 1, 0).start()

    def relay2(name, ds=(1, 2, 3)):
        k = ids[name]
        for d in ds:
            slot = W[name].at[x, zfrom(d), ri]
            remote(slot, slot, s1_send.at[k, d - 1], s1_recv.at[k, d - 1], dev(zto(d))).wait_recv()
            step2_copy(name, 0, d).start()
            step2_copy(name, 1, d).start()

    def relay3(name, ds=(0, 1, 2, 3)):
        for d in ds:
            step2_arrival(name, 0, d).wait_recv()
            step2_copy(name, 2, d).start()
            step2_arrival(name, 1, d).wait_recv()
            step2_copy(name, 3, d).start()

    def relay4(*names):
        for name in names:
            step1_local(name).wait()
            for d in range(Z):
                step2_arrival(name, 2, d).wait_recv()
                step2_arrival(name, 3, d).wait_recv()

    def relay_sent():
        for name in ARRAYS:
            for d in range(1, Z):
                step1_copy(name, d).wait_send()
            for which in range(4):
                for d in range(Z):
                    step2_copy(name, which, d).wait_send()

    @pl.when(p == 0)
    def _():
        relay1("P1", "P2")

    @pl.when(p == 1)
    def _():
        dx3[...] = tcot_in[x]
        dcot[...] = gcot_in[x]
        dx3_all[zi] = tcot_in[x]
        gather_start("dx3", dx3_all, keep=False)

    for c in v_arrivals:
        c.wait_recv()
    remote(aq.at[xo], aq.at[xo], q_send, q_recv, over_x).wait_recv()
    low_lanes = lax.broadcasted_iota(jnp.int32, (64, LANE), 1) < LANE // 2
    for z in range(Z):
        first, second = vv[2 * z], pltpu.roll(vv[2 * z + 1], LANE // 2, 1)
        vec_c[:, z * cz : z * cz + LANE] = first[:, 0:LANE]
        vec_c[:, z * cz + LANE : z * cz + 2 * LANE] = jnp.where(
            low_lanes, first[:, LANE:], second[:, 0:LANE]
        )
        vec_c[:, z * cz + 2 * LANE : (z + 1) * cz] = second[:, LANE:]
    for i in range(Z * R):
        vec_d[:, i * LANE : (i + 1) * LANE] = vv[i, 56:64, 0:LANE]

    def gain_d(row):
        return vec_d[row : row + 1, :]

    def gain_c(row):
        return vec_c[row : row + 1, :]

    def token_entry():
        n_hat, _ = normed(wide(x_in[...]))
        n1_all[zi] = low(n_hat * gain_d(0))
        gather_start("n1", n1_all, keep=False)

    def conv_entry():
        @pl.loop(0, c_dim // LANE)
        def _(ch):
            lanes = lanes_of(ch, LANE)
            taps = vec_c[:, lanes]
            cn[:, lanes] = depthwise(wide(c_in[:, lanes]), lambda k: taps[k : k + 1], 7)

        n_hat, rs = normed(cn[...])
        cn[...] = n_hat
        crs[...] = jnp.broadcast_to(rs, crs.shape)
        f_all[zi] = low(n_hat * gain_c(49))
        gather_start("f", f_all, keep=False)

    def first_relays():
        relay2("P1")
        relay1("Q", "O")
        relay2("P2")
        relay3("P1")

    sent.extend(gather_copies("n1", n1_all))
    sent.extend(gather_copies("f", f_all))

    @pl.when(p == 0)
    def _():
        first = order_in[0, x] == 0
        c_in[...] = jnp.where(first, grid_in[0], grid_in[1])
        x_in[...] = jnp.where(first, tok_in[0], tok_in[1])
        conv_entry()
        token_entry()
        first_relays()

    @pl.when(p == 1)
    def _():
        pl.semaphore_wait(go, 1)
        relay1("P1", "P2")
        first_relays()
        remote(c_in, c_in, h_send.at[1], h_recv.at[1], sib).wait_recv()
        conv_entry()

    relay2("Q")
    relay2("O")
    relay1("E", "Gi", "Go")
    relay3("P2", (0, 1))
    relay4("P1")
    gather_wait("f", f_all)

    def conv_hidden(j):
        @pl.loop(0, cfq // tile)
        def _(t):
            lanes = lanes_of(t, tile)
            act, der = gelu_pair(mm(flat(f_all[...]), flat(W["P1"][j, :, :, :, lanes])))
            r[j, :, lanes] = low(act)
            rp[j, :, lanes] = low(der)

    conv_hidden(0)

    relay3("P2", (2, 3))
    for name in ("E", "Gi", "Go"):
        relay2(name)
    relay1("F1")
    conv_hidden(1)
    relay3("Q")
    relay3("O")
    relay2("F1")
    relay1("F2")

    relay4("P2")

    @pl.loop(0, Z)
    def _(z):
        acc = mm_nt(r[0], flat(W["P2"][0, z])) + mm_nt(r[1], flat(W["P2"][1, z]))
        cv_sb[:, :, lanes_of(z, cz)] = low(acc).reshape(Z, TOK, cz)

    scatter_start("cv", cv_sb, cv_rb)

    for name in ("E", "Gi", "Go"):
        relay3(name)
    relay2("F2")

    @pl.when(p == 0)
    def _():
        pl.semaphore_signal(go, inc=1, device_id=sib, device_id_type=pl.DeviceIdType.MESH)

    @pl.when(p == 1)
    def _():
        remote(x_in, x_in, h_send.at[0], h_recv.at[0], sib).wait_recv()
        token_entry()

    relay4("Q", "O")
    gather_wait("n1", n1_all)
    for j in range(2):
        wj = side_by_side([flat(W["Q"][j, :, :, s]) for s in range(3)])
        qkv[j] = low(mm(flat(n1_all[...]), wj))
    for j in range(2):
        for b in range(Z):
            rows = slice(b * TOK, (b + 1) * TOK)
            outs = []
            for h in range(hq // HD):
                q, kk, vals = (qkv[j, rows, s * hq + h * HD : s * hq + (h + 1) * HD] for s in range(3))
                sc = mm_nt(q, kk) * HD ** (-0.5)
                e = jnp.exp(sc - jnp.max(sc, axis=-1, keepdims=True))
                pr = low(e / jnp.sum(e, axis=-1, keepdims=True))
                prob[j, h, b] = pr
                outs.append(mm(pr, vals))
            ctx[j, rows, :] = low(side_by_side(outs))

    def out_block(j, z):
        return side_by_side([W["O"][j, z, 0], W["O"][j, z, 1]])

    @pl.loop(0, Z)
    def _(z):
        both = jnp.concatenate([out_block(0, z), out_block(1, z)], axis=0)
        acc = mm(side_by_side([ctx[0], ctx[1]]), both)
        o_sb[:, :, lanes_of(z, dz)] = low(acc).reshape(Z, TOK, dz)

    scatter_start("o", o_sb, o_rb)

    relay3("F1")

    scatter_wait("cv", cv_rb)
    cv_sum[...] = scattered(cv_sb, cv_rb)
    c2f[...] = wide(c_in[...]) + gain_c(50) * cv_sum[...]
    c2_low = low(c2f[...])
    c2_all[zi] = c2_low
    gather_start("c2", c2_all)
    hid_grid[x] = c2_low

    @pl.when(p == 0)
    def _():
        remote(hid_grid.at[x], c_in, h_send.at[1], h_recv.at[1], sib).start()

    relay3("F2")
    scatter_wait("o", o_rb)
    x1[...] = wide(x_in[...]) + scattered(o_sb, o_rb)
    n_hat, _ = normed(x1[...])
    n2_all[zi] = low(n_hat * gain_d(1))
    gather_start("n2", n2_all)

    relay4("E", "Gi", "Go")
    gather_wait("c2", c2_all)
    row8 = lax.broadcasted_iota(jnp.int32, (8, adq), 0)
    gs_part = None
    for j in range(2):
        ad = mm(flat(c2_all[...]), flat(W["E"][j]))
        adapted[j] = ad
        taps = aq[j]
        pool = jnp.zeros((8, adq), F32)
        for b in range(Z):
            sp = depthwise(ad[b * TOK : (b + 1) * TOK], lambda k: taps[k : k + 1], 3)
            spread[j, b] = sp
            pool = jnp.where(row8 == b, jnp.mean(sp, axis=0, keepdims=True), pool)
        pooled[j] = pool
        term = mm_nt(low(pool), flat(W["Gi"][j]))
        gs_part = term if gs_part is None else gs_part + term
    gsb[3] = gs_part
    share_start("gs", gsb)

    relay4("F1")
    gather_wait("n2", n2_all)
    for j in range(2):

        @pl.loop(0, ffq // tile)
        def _(t):
            lanes = lanes_of(t, tile)
            act, der = gelu_pair(mm(flat(n2_all[...]), flat(W["F1"][j, :, :, :, lanes])))
            u[j, :, lanes] = low(act)
            up[j, :, lanes] = low(der)

    scatter_wait("gs", gsb)

    def gate_hidden():
        return gelu_pair((gsb[0] + gsb[1]) + (gsb[2] + gsb[3]))

    gh, _ = gate_hidden()
    for j in range(2):
        g8 = jnp.tanh(mm(low(gh), flat(W["Go"][j])))
        gate[j] = g8
        for b in range(Z):
            br_sb[b, :, j * adq : (j + 1) * adq] = low(g8[b : b + 1] * spread[j, b])
    scatter_start("br", br_sb, br_rb)
    relay4("F2")

    @pl.loop(0, Z)
    def _(z):
        acc = None
        for j in range(2):
            term = mm(u[j], side_by_side([W["F2"][j, z, 0], W["F2"][j, z, 1]]))
            acc = term if acc is None else acc + term
        m_sb[:, :, lanes_of(z, dz)] = low(acc).reshape(Z, TOK, dz)

    scatter_start("m", m_sb, m_rb)

    def exchange(n, buf):
        remote(buf.at[x], buf.at[x], xo_send.at[n], xo_recv.at[n], over_x).start()

    def layer_output(total):
        scatter_wait("br", br_rb)
        total[...] = x1[...]
        for d in range(Z):
            piece = br_sb[zi] if d == 0 else br_rb[d - 1]
            for j in range(2):
                lanes = pl.ds(pl.multiple_of(j * adh + zfrom(d) * adq, LANE), adq)
                total[:, lanes] += wide(piece[:, j * adq : (j + 1) * adq])
        scatter_wait("m", m_rb)
        hid_tok[x] = low(total[...] + scattered(m_sb, m_rb))

    @pl.when(p == 0)
    def _():
        layer_output(dx1)
        remote(hid_tok.at[x], x_in, h_send.at[0], h_recv.at[0], sib).start()
        exchange(0, hid_tok)

    exchange(1, hid_grid)
    relay_sent()

    def over_cores(d):
        return remote(
            out_gtok.at[x], dx3_all.at[zi], b_send.at[d], b_recv.at[d], dev(zto(d), pp=1 - p)
        )

    @pl.when(p == 1)
    def _():
        gather_wait("dx3", dx3_all)
        for c in gather_copies("dx3", dx3_all):
            c.wait_send()

    @pl.when(p == 0)
    def _():
        for d in range(Z):
            slot = dx3_all.at[zfrom(d)]
            remote(slot, slot, b_send.at[d], b_recv.at[d], sib).wait_recv()
        dx3[...] = dx3_all[zi]

    def own_lanes(j):
        return pl.ds(pl.multiple_of(j * adh + zi * adq, LANE), adq)

    gh, ghp = gate_hidden()
    dgh_part = None
    dgp = []
    for j in range(2):
        dgate = jnp.zeros((8, adq), F32)
        for b in range(Z):
            dbr = wide(dx3_all[b, :, own_lanes(j)])
            dgate = jnp.where(row8 == b, jnp.sum(dbr * spread[j, b], axis=0, keepdims=True), dgate)
        dg8 = low(dgate * (1.0 - gate[j] * gate[j]))
        dgp.append(dg8)
        term = mm_nt(dg8, flat(W["Go"][j]))
        dgh_part = term if dgh_part is None else dgh_part + term
    dgb[3] = dgh_part
    share_start("dgh", dgb)

    for j in range(2):

        @pl.loop(0, ffq // tile)
        def _(t):
            rows = lanes_of(t, tile)
            both = side_by_side([W["F2"][j, z, rr, rows] for z in range(Z) for rr in range(R)])
            du = mm_nt(flat(dx3_all[...]), both)
            dh[j, :, rows] = low(du * wide(up[j, :, rows]))

    scatter_wait("dgh", dgb)
    dgs = low(((dgb[0] + dgb[1]) + (dgb[2] + dgb[3])) * ghp)
    for j in range(2):
        dpool = mm(dgs, flat(W["Gi"][j])) * (1.0 / TOK)
        taps = aq[j]
        tap_rows = [None] * 9
        for b in range(Z):
            dsp = gate[j, b : b + 1] * wide(dx3_all[b, :, own_lanes(j)]) + dpool[b : b + 1]
            dad[j, b * TOK : (b + 1) * TOK] = low(depthwise(dsp, lambda k: taps[8 - k : 9 - k], 3))

            def put(k, row):
                tap_rows[k] = row if tap_rows[k] is None else tap_rows[k] + row

            depthwise_taps(adapted[j, b * TOK : (b + 1) * TOK], dsp, 3, put)
        for k in range(9):
            gad[j, k : k + 1] = tap_rows[k]
        gad[j, 9:16] = jnp.zeros((7, adq), F32)

    @pl.loop(0, Z)
    def _(z):
        acc = mm_nt(dad[0], flat(W["E"][0, z])) + mm_nt(dad[1], flat(W["E"][1, z]))
        dc2_sb[:, :, lanes_of(z, cz)] = low(acc).reshape(Z, TOK, cz)

    scatter_start("dc2", dc2_sb, dc2_rb)

    @pl.loop(0, Z)
    def _(z):
        acc = mm_nt(dh[0], flat(W["F1"][0, z])) + mm_nt(dh[1], flat(W["F1"][1, z]))
        dn2_sb[:, :, lanes_of(z, dz)] = low(acc).reshape(Z, TOK, dz)

    scatter_start("dn2", dn2_sb, dn2_rb)

    def half_rows(name, upper):
        half = W[name].shape[-2] // 2
        rows = slice(half, None) if upper else slice(0, half)
        return (slice(None), rows) if len(W[name].shape) == 6 else (rows,)

    def hop_copy(name, which):
        n = ids[name]
        lower, upper = half_rows(name, False), half_rows(name, True)
        src, to = (
            lambda: (W[name].at[(xo, slice(None), slice(None)) + lower], over_x),
            lambda: (W[name].at[(slice(None), slice(None), ro) + upper], over_r),
            lambda: (RX[name][0].at[:, ro], over_r),
            lambda: (RX[name][1].at[xo], over_x),
        )[which]()
        return remote(src, RX[name][which], g_send.at[n, which], g_recv.at[n, which], to)

    def reduce_start(name):
        hop_copy(name, 0).start()
        hop_copy(name, 1).start()

    def reduce_middle(*names):
        for name in names:
            lower, upper = half_rows(name, False), half_rows(name, True)
            buf = RX[name]
            hop_copy(name, 0).wait_recv()

            @pl.loop(0, Z)
            def _(z):
                for rr in range(R):
                    own = W[name][(x, z, rr) + lower]
                    buf[0][z, rr] = low(wide(own) + wide(buf[0][z, rr]))

            hop_copy(name, 2).start()
            hop_copy(name, 1).wait_recv()

            @pl.loop(0, Z)
            def _(z):
                for j in range(2):
                    own = W[name][(j, z, ri) + upper]
                    buf[1][j, z] = low(wide(own) + wide(buf[1][j, z]))

            hop_copy(name, 3).start()

    def reduce_end(*names):
        for name in names:
            lower, upper = half_rows(name, False), half_rows(name, True)
            buf = RX[name]
            hop_copy(name, 2).wait_recv()
            hop_copy(name, 3).wait_recv()

            @pl.loop(0, Z)
            def _(z):
                W[name][(x, z, ri) + lower] = low(wide(buf[0][z, ri]) + wide(buf[2][z]))
                W[name][(x, z, ri) + upper] = low(wide(buf[1][x, z]) + wide(buf[3][z]))

            for d in range(1, Z):
                back_copy(name, d).start()
            back_local(name).start()

    def back_copy(name, d):
        n = ids[name]
        return remote(
            W[name].at[x, zto(d), ri], quarter_of(name, native[name], zi),
            a_send.at[n, d - 1], a_recv.at[n, d - 1], dev(zto(d)),
        )

    def back_local(name):
        return pltpu.make_async_copy(
            W[name].at[x, zi, ri], quarter_of(name, native[name], zi), loc_sem.at[ids[name]]
        )

    peers = ((1, 0), (0, 1), (1, 1))

    def owner(k):
        return (ro if peers[k][0] else ri), (xo if peers[k][1] else x)

    def row_grad(name, left, right):
        width = W[name].shape[3]
        span = R * width

        @pl.loop(0, Z)
        def _(z):
            turned[0:span] = flat(left[:, :, lanes_of(z, span)]).T
            for j in range(2):
                W[name][j, z] = low(mm(turned[0:span], right[j])).reshape(R, width, -1)

        reduce_start(name)

    def col_grad(name, left, right):
        width = left.shape[2]
        for j in range(2):
            turned[j * width : (j + 1) * width] = left[j].T

        @pl.loop(0, Z)
        def _(z):
            rhs = flat(right[:, :, lanes_of(z, dz)])
            for j in range(2):
                g = low(mm(turned[j * width : (j + 1) * width], rhs))
                for rr in range(R):
                    W[name][j, z, rr] = g[:, rr * LANE : (rr + 1) * LANE]

        reduce_start(name)

    for j in range(2):
        W["Gi"][j] = low(mm_tn(dgs, low(pooled[j]))).reshape(Z, R, -1, adq)
        W["Go"][j] = low(mm_tn(low(gh), dgp[j])).reshape(Z, R, -1, adq)
    reduce_start("Gi")
    reduce_start("Go")
    row_grad("E", c2_all, dad)

    @pl.when(p == 0)
    def _():
        remote(dcot, dcot, c_send, c_recv, sib).wait_recv()

    scatter_wait("dc2", dc2_rb)
    dc2t[...] = wide(dcot[...]) + scattered(dc2_sb, dc2_rb)
    gvs_ls = jnp.sum(cv_sum[...] * dc2t[...], axis=0, keepdims=True)
    dcv_all[zi] = low(dc2t[...] * gain_c(50))
    gather_start("dcv", dcv_all)

    scatter_wait("dn2", dn2_rb)
    dn2 = scattered(dn2_sb, dn2_rb)
    n_hat, rs = normed(x1[...])
    gvs_d1 = jnp.sum(dn2 * n_hat, axis=0, keepdims=True)
    dx1[...] = wide(dx3[...]) + norm_back(dn2, n_hat, rs, gain_d(1))
    dx1_all[zi] = low(dx1[...])
    gather_start("dx1", dx1_all)

    col_grad("F2", u, dx3_all)
    row_grad("F1", n2_all, dh)

    gather_wait("dcv", dcv_all)
    for j in range(2):

        @pl.loop(0, cfq // tile)
        def _(t):
            lanes = lanes_of(t, tile)
            dr = mm(flat(dcv_all[...]), flat(W["P2"][j, :, :, :, lanes]))
            dhc[j, :, lanes] = low(dr * wide(rp[j, :, lanes]))

    @pl.loop(0, Z)
    def _(z):
        acc = mm_nt(dhc[0], flat(W["P1"][0, z])) + mm_nt(dhc[1], flat(W["P1"][1, z]))
        df_sb[:, :, lanes_of(z, cz)] = low(acc).reshape(Z, TOK, cz)

    scatter_start("df", df_sb, df_rb)

    early = ("Gi", "Go", "E", "F2", "F1")

    def pw_grads():
        row_grad("P2", dcv_all, r)
        row_grad("P1", f_all, dhc)

    @pl.when(p == 0)
    def _():
        pw_grads()
        reduce_middle(*early)

    gather_wait("dx1", dx1_all)
    for j in range(2):
        both = side_by_side([W["O"][j, z, rr] for z in range(Z) for rr in range(R)])
        do_all[j] = low(mm_nt(flat(dx1_all[...]), both))
    for j in range(2):
        for b in range(Z):
            rows = slice(b * TOK, (b + 1) * TOK)
            parts = [[], [], []]
            for h in range(hq // HD):
                q, kk, vals = (qkv[j, rows, s * hq + h * HD : s * hq + (h + 1) * HD] for s in range(3))
                do = do_all[j, rows, h * HD : (h + 1) * HD]
                pr = prob[j, h, b]
                dp = mm_nt(do, vals)
                prw = wide(pr)
                ds = low(prw * (dp - jnp.sum(dp * prw, axis=-1, keepdims=True)) * HD ** (-0.5))
                parts[0].append(mm(ds, kk))
                parts[1].append(mm_tn(ds, q))
                parts[2].append(mm_tn(pr, do))
            for s in range(3):
                dqkv[j, rows, s * hq : (s + 1) * hq] = low(side_by_side(parts[s]))

    @pl.loop(0, Z)
    def _(z):
        acc = None
        for j in range(2):
            term = mm_nt(dqkv[j], side_by_side([flat(W["Q"][j, z, :, s]) for s in range(3)]))
            acc = term if acc is None else acc + term
        dn1_sb[:, :, lanes_of(z, dz)] = low(acc).reshape(Z, TOK, dz)

    scatter_start("dn1", dn1_sb, dn1_rb)

    def attention_grads():
        @pl.loop(0, Z)
        def _(z):
            turned[0:dz] = flat(n1_all[:, :, lanes_of(z, dz)]).T
            for j in range(2):
                g = low(mm(turned[0:dz], dqkv[j]))
                for s in range(3):
                    W["Q"][j, z, :, s] = g[:, s * hq : (s + 1) * hq].reshape(R, -1, hq)

        reduce_start("Q")
        col_grad("O", ctx, dx1_all)

    @pl.when(p == 0)
    def _():
        attention_grads()
        reduce_end(*early)
        reduce_middle("P2", "P1")

    scatter_wait("dn1", dn1_rb)
    dn1 = scattered(dn1_sb, dn1_rb)
    n_hat, rs = normed(wide(x_in[...]))
    gvs_d0 = jnp.sum(dn1 * n_hat, axis=0, keepdims=True)
    out_gtok[x] = low(dx1[...] + norm_back(dn1, n_hat, rs, gain_d(0)))

    @pl.when(p == 1)
    def _():
        for d in (1, 2, 3, 0):
            over_cores(d).start()

    scatter_wait("df", df_rb)
    dfv = scattered(df_sb, df_rb)
    gvs_lc = jnp.sum(dfv * cn[...], axis=0, keepdims=True)
    dcn[...] = norm_back(dfv, cn[...], crs[:, 0:1], gain_c(49))

    @pl.loop(0, c_dim // LANE)
    def _(ch):
        lanes = lanes_of(ch, LANE)
        taps = vec_c[:, lanes]
        back = depthwise(dcn[:, lanes], lambda k: taps[48 - k : 49 - k], 7)
        out_ggrid[x, :, lanes] = low(dc2t[:, lanes] + back)

    @pl.when(p == 1)
    def _():
        remote(out_ggrid.at[x], dcot, c_send, c_recv, sib).start()
        layer_output(dx1)
        exchange(0, hid_tok)
        pw_grads()
        reduce_middle(*early)
        attention_grads()
        reduce_end(*early)
        reduce_middle("P2", "P1")

    exchange(2, out_gtok)
    exchange(3, out_ggrid)

    @pl.loop(0, Z)
    def _(z):
        for part in range(cz // LANE):
            lanes = pl.ds(pl.multiple_of(z * cz + part * LANE, LANE), LANE)

            def put(k, row):
                gvs[z, k : k + 1, part * LANE : (part + 1) * LANE] = row

            depthwise_taps(wide(c_in[:, lanes]), dcn[:, lanes], 7, put)

    for z in range(Z):
        gvs[z, 49:50] = gvs_lc[:, z * cz : (z + 1) * cz]
        gvs[z, 50:51] = gvs_ls[:, z * cz : (z + 1) * cz]
        gvs[z, 51:64] = jnp.zeros((13, cz), F32)
        gvs[z, 56:57, 0:dz] = gvs_d0[:, z * dz : (z + 1) * dz]
        gvs[z, 57:58, 0:dz] = gvs_d1[:, z * dz : (z + 1) * dz]
    scatter_start("gv", gvs, gv_rb)

    def group_copy(n, k, src, dst):
        rr, xx = owner(k)
        return remote(src, dst, gx_send.at[n, k], gx_recv.at[n, k], dev(rr=rr, xx=xx))

    for k in range(3):
        c = group_copy(1, k, gad, gad_rb.at[k])
        c.start()
        sent.append(c)
    scatter_wait("gv", gv_rb)
    gvx[3] = (gvs[zi] + gv_rb[0]) + (gv_rb[1] + gv_rb[2])
    for k in range(3):
        c = group_copy(0, k, gvx.at[3], gvx.at[k])
        c.start()
        sent.append(c)
    for k in range(3):
        group_copy(1, k, gad, gad_rb.at[k]).wait_recv()
    gad_all[zi] = (gad[x] + gad_rb[0, x]) + (gad_rb[1, x] + gad_rb[2, x])
    gather_start("gad", gad_all)

    reduce_middle("Q", "O")
    reduce_end("P2", "P1", "Q", "O")

    for k in range(3):
        group_copy(0, k, gvx.at[k], gvx.at[k]).wait_recv()
    total = (gvx[0] + gvx[1]) + (gvx[2] + gvx[3])
    mine = jnp.where(ri == 1, pltpu.roll(total, c_own, 1), total)[:, 0:c_own]
    mine_d = jnp.where(ri == 1, total[:, LANE : 2 * LANE], total[:, 0:LANE])

    def flag(n):
        return train_in[0, n].astype(F32)

    out_depth[...] = mine[0:taps7] * flag(0)
    out_ln_conv[...] = mine[49:50] * flag(1)
    out_scale[...] = mine[50:51] * flag(4)
    out_ln_attn[...] = mine_d[56:57]
    out_ln_mlp[...] = mine_d[57:58]
    gather_wait("gad", gad_all)
    for z in range(Z):
        out_ad[:, z * adq : (z + 1) * adq] = gad_all[z][0:9]
    for name in ARRAYS:
        back_local(name).wait()
        for d in range(1, Z):
            n = ids[name]
            slot = quarter_of(name, native[name], zfrom(d))
            remote(slot, slot, a_send.at[n, d - 1], a_recv.at[n, d - 1], dev(zto(d))).wait_recv()
    for n, buf in enumerate((hid_tok, hid_grid, out_gtok, out_ggrid)):
        c = remote(buf.at[x], buf.at[x], xo_send.at[n], xo_recv.at[n], over_x)
        c.wait_send()
        remote(buf.at[xo], buf.at[xo], xo_send.at[n], xo_recv.at[n], over_x).wait_recv()

    @pl.when(p == 0)
    def _():
        remote(hid_tok.at[x], x_in, h_send.at[0], h_recv.at[0], sib).wait_send()
        remote(hid_grid.at[x], c_in, h_send.at[1], h_recv.at[1], sib).wait_send()

    @pl.when(p == 1)
    def _():
        for d in range(Z):
            over_cores(d).wait_send()
        remote(out_ggrid.at[x], dcot, c_send, c_recv, sib).wait_send()

    for c in sent:
        c.wait_send()
    for name in ARRAYS:
        for which in range(4):
            hop_copy(name, which).wait_send()
        for d in range(1, Z):
            back_copy(name, d).wait_send()


def run_layers(weights, vectors, order, train, streams, sizes, outer):
    d_dim, c_dim, hq, ffq, cfq, adw, dg = sizes
    vm = pltpu.VMEM
    blocks = []
    for name, value in zip(ARRAYS, weights):
        if name == "Q":
            blocks.append((3, value.shape[1], hq))
        elif name in ("O", "F2"):
            blocks.append((value.shape[0] // Z, value.shape[1]))
        else:
            blocks.append((value.shape[0], value.shape[1] // Z))
    rows = Z * TOK

    def act(width, count=Z, kind=BF):
        return vm((count, TOK, width), kind)

    scratch = [vm((2, Z, R) + s, BF) for s in blocks] + [
        vm(lead + s[:-2] + (s[-2] // 2, s[-1]), BF)
        for s in blocks
        for lead in ((Z, R), (2, Z), (Z,), (Z,))
    ]
    scratch += [
        vm((64, 2 * LANE), F32), vm((Z * R, 64, 2 * LANE), F32), vm((2, 16, adw), F32), vm((64, c_dim), F32), vm((8, d_dim), F32),
        vm((TOK, d_dim), BF), vm((TOK, c_dim), BF), act(d_dim), act(c_dim), act(d_dim), act(c_dim),
        act(d_dim), act(d_dim, 3), act(c_dim), act(c_dim, 3), act(d_dim), act(d_dim, 3),
        act(2 * adw), act(2 * adw, 3), vm((4, 8, dg), F32), vm((4, 8, dg), F32),
        vm((2, rows, 3 * hq), BF), vm((2, hq // HD, Z, TOK, TOK), BF), vm((2, rows, hq), BF),
        vm((2, rows, ffq), BF), vm((2, rows, ffq), BF), vm((2, rows, cfq), BF), vm((2, rows, cfq), BF),
        vm((TOK, c_dim), F32), vm((TOK, LANE), F32), vm((TOK, c_dim), F32), vm((TOK, d_dim), F32), vm((TOK, c_dim), F32),
        vm((2, rows, adw), F32), vm((2, Z, TOK, adw), F32), vm((2, 8, adw), F32), vm((2, 8, adw), F32),
        vm((TOK, d_dim), BF), vm((TOK, c_dim), BF), act(d_dim), act(d_dim), act(d_dim, 3), act(c_dim), act(c_dim, 3),
        act(d_dim), act(c_dim),
        act(d_dim), act(d_dim, 3), act(c_dim), act(c_dim, 3), vm((2, rows, ffq), BF), vm((2, rows, hq), BF),
        vm((2, rows, 3 * hq), BF), vm((2, rows, cfq), BF), vm((TOK, d_dim), F32), vm((TOK, c_dim), F32), vm((2, rows, adw), BF),
        vm((TOK, c_dim), F32),
        vm((Z, 64, c_dim // Z), F32), vm((3, 64, c_dim // Z), F32), vm((4, 64, c_dim // Z), F32),
        vm((2, 16, adw), F32), vm((3, 2, 16, adw), F32), vm((Z, 16, adw), F32),
        vm((2 * ffq, rows), BF),
    ]
    dma = pltpu.SemaphoreType.DMA
    na = len(ARRAYS)
    scratch += [
        dma((len(EVENTS), 3)), dma((len(EVENTS), 3)), dma((na, 3)), dma((na, 3)), dma((na,)),
        dma((na, 4, Z)), dma((na, 4, Z)), dma((7,)), dma((7,)), dma, dma, dma((2,)), dma((2,)), dma((Z,)), dma((Z,)), dma, dma,
        dma((4,)), dma((4,)), dma((na, 4)), dma((na, 4)), dma((na, 3)), dma((na, 3)), dma((2, 3)), dma((2, 3)),
        pltpu.SemaphoreType.REGULAR,
    ]
    sds = jax.ShapeDtypeStruct
    out_shape = [sds((2, TOK, d_dim), BF), sds((2, TOK, c_dim), BF)] * 2
    out_shape += [sds(value.shape, BF) for value in weights]
    out_shape += [sds(value.shape, F32) for value in vectors]
    any_spec = pl.BlockSpec(memory_space=pl.ANY)
    vm_spec = pl.BlockSpec(memory_space=pltpu.VMEM)
    sm_spec = pl.BlockSpec(memory_space=pltpu.SMEM)
    return pl.pallas_call(
        functools.partial(main_kernel, sizes, outer),
        out_shape=out_shape,
        in_specs=[any_spec] * na + [vm_spec] * 6 + [sm_spec] * 2 + [vm_spec] * 4,
        out_specs=[vm_spec] * 4 + [any_spec] * na + [vm_spec] * 6,
        scratch_shapes=scratch,
        compiler_params=pltpu.CompilerParams(
            collective_id=0, has_side_effects=True, vmem_limit_bytes=62 * 1024 * 1024
        ),
        cost_estimate=pl.CostEstimate(flops=26 * 10**9, bytes_accessed=10**8, transcendentals=10**7),
        name="layers",
    )(*weights, *vectors, order, train, *streams)


def per_device(
    tokens,
    conv_grid,
    order,
    trainable,
    ln_attn,
    w_qkv,
    w_attn_out,
    ln_mlp,
    w_fc_in,
    w_fc_out,
    conv_depth,
    ln_conv,
    w_pw_in,
    w_pw_out,
    layer_scale,
    w_adapt,
    adapt_depth,
    w_gate_in,
    w_gate_out,
    tok_cot,
    grid_cot,
):
    dp_count = lax.axis_size("dp")
    outer = dp_count // (Z * R)
    groups = [[g * outer + o for o in range(outer)] for g in range(Z * R)]
    layer_at = lax.axis_index("pipe")

    def block(value, axis):
        value = value[0]
        if outer == 1:
            return value
        return lax.all_gather(value, "dp", axis=axis, tiled=True, axis_index_groups=groups)

    def share(value, axis):
        if outer > 1:
            value = lax.psum_scatter(
                value, "dp", scatter_dimension=axis, tiled=True, axis_index_groups=groups
            )
        return value[None]

    qkv = block(w_qkv, 1)
    gate_in = block(w_gate_in, 1).T
    pw_in = block(w_pw_in, 0)
    adapt = block(w_adapt, 0)
    fc_in = block(w_fc_in, 0)
    weights = (
        pw_in,
        block(w_pw_out, 1).T,
        qkv,
        block(w_attn_out, 1),
        adapt,
        gate_in,
        block(w_gate_out, 0),
        fc_in,
        block(w_fc_out, 1),
    )
    vectors = (
        block(conv_depth, 1),
        block(ln_conv, 0)[None],
        block(layer_scale, 0)[None],
        block(ln_attn, 0)[None],
        block(ln_mlp, 0)[None],
        adapt_depth[0],
    )
    spread = Z * R
    sizes = (
        qkv.shape[1] * spread, pw_in.shape[0] * spread, qkv.shape[2] // Z, fc_in.shape[1] // Z,
        pw_in.shape[1] // Z, adapt.shape[1] // Z, gate_in.shape[0] * spread,
    )

    def rows_of(value):
        return value.reshape(value.shape[0], TOK, value.shape[-1])

    streams = [rows_of(value) for value in (tokens, conv_grid, tok_cot, grid_cot)]
    outs = run_layers(weights, vectors, order, trainable, streams, sizes, outer)
    hid_tok, hid_grid, g_tok, g_grid = outs[:4]
    g_p1, g_p2, g_q, g_o, g_e, g_gi, g_go, g_f1, g_f2 = [value.astype(F32) for value in outs[4:13]]
    g_depth, g_ln_conv, g_scale, g_ln_attn, g_ln_mlp, g_ad = outs[13:]

    swap = (layer_at == 0) & (order[0, 0] == 1)
    g_tok = jnp.where(swap, g_tok[::-1], g_tok)
    g_grid = jnp.where(swap, g_grid[::-1], g_grid)
    grid_shape = (1,) + conv_grid.shape
    tok_shape = (1,) + tokens.shape
    flags = trainable[0].astype(F32)
    if outer > 1:
        g_ad = lax.psum(g_ad, "dp", axis_index_groups=groups)
    return (
        hid_tok.reshape(tok_shape),
        hid_grid.reshape(grid_shape),
        g_tok.reshape(tok_shape),
        g_grid.reshape(grid_shape),
        share(g_ln_attn[0], 0),
        share(g_q, 1),
        share(g_o, 1),
        share(g_ln_mlp[0], 0),
        share(g_f1, 0),
        share(g_f2, 1),
        share(g_depth, 1),
        share(g_ln_conv[0], 0),
        share(g_p1 * flags[2], 0),
        share((g_p2 * flags[3]).T, 1),
        share(g_scale[0], 0),
        share(g_e, 0),
        g_ad[None],
        share(g_gi.T, 1),
        share(g_go, 0),
    )


def solution(mesh):
    in_specs = (
        P(None, "dp", None, None),
        P(None, "dp", None, None, None),
        P("dp", None),
        P("pipe", None),
        P("pipe", "dp"),
        P("pipe", None, "dp", "tensor"),
        P("pipe", "tensor", "dp"),
        P("pipe", "dp"),
        P("pipe", "dp", "tensor"),
        P("pipe", "tensor", "dp"),
        P("pipe", None, "dp"),
        P("pipe", "dp"),
        P("pipe", "dp", "tensor"),
        P("pipe", "tensor", "dp"),
        P("pipe", "dp"),
        P("pipe", "dp", "tensor"),
        P("pipe", None, "tensor"),
        P("pipe", "tensor", "dp"),
        P("pipe", "dp", "tensor"),
        P(None, "dp", None, None),
        P(None, "dp", None, None, None),
    )
    out_specs = (
        P("pipe", None, "dp", None, None),
        P("pipe", None, "dp", None, None, None),
        P("pipe", None, "dp", None, None),
        P("pipe", None, "dp", None, None, None),
        P("pipe", "dp"),
        P("pipe", None, "dp", "tensor"),
        P("pipe", "tensor", "dp"),
        P("pipe", "dp"),
        P("pipe", "dp", "tensor"),
        P("pipe", "tensor", "dp"),
        P("pipe", None, "dp"),
        P("pipe", "dp"),
        P("pipe", "dp", "tensor"),
        P("pipe", "tensor", "dp"),
        P("pipe", "dp"),
        P("pipe", "dp", "tensor"),
        P("pipe", None, "tensor"),
        P("pipe", "tensor", "dp"),
        P("pipe", "dp", "tensor"),
    )
    return jax.shard_map(
        per_device, mesh=mesh, in_specs=in_specs, out_specs=out_specs, check_vma=False
    )
```

```python
import functools

import jax
import jax.numpy as jnp
from jax import lax
from jax.experimental import pallas as pl
from jax.experimental.pallas import tpu as pltpu
from jax.sharding import PartitionSpec as P

HD = 64
Z = 4
R = 2
TOK = 64
SIDE = 8
LANE = 128
BF = jnp.bfloat16
F32 = jnp.float32
ARRAYS = ("P1", "P2", "Q", "O", "E", "Gi", "Go", "F1", "F2")
EVENTS = (
    "n1", "f", "o", "cv", "n2", "c2", "m", "br", "gs",
    "dx3", "dgh", "dn2", "dc2", "dx1", "dcv", "dn1", "df", "gv", "gad",
)


def mm(a, b):
    return lax.dot_general(a, b, (((1,), (0,)), ((), ())), preferred_element_type=F32)


def mm_nt(a, b):
    return lax.dot_general(a, b, (((1,), (1,)), ((), ())), preferred_element_type=F32)


def mm_tn(a, b):
    return lax.dot_general(a, b, (((0,), (0,)), ((), ())), preferred_element_type=F32)


def flat(value):
    return value.reshape(-1, value.shape[-1])


def low(value):
    return value.astype(BF)


def wide(value):
    return value.astype(F32)


def gelu_pair(h):
    phi = 0.5 * (1.0 + lax.erf(h * 0.7071067811865476))
    dens = jnp.exp(-0.5 * h * h) * 0.3989422804014327
    return h * phi, phi + h * dens


def normed(value):
    centred = value - jnp.mean(value, axis=-1, keepdims=True)
    rs = lax.rsqrt(jnp.mean(centred * centred, axis=-1, keepdims=True) + 1e-06)
    return centred * rs, rs


def norm_back(dn, n_hat, rs, gain):
    gd = dn * gain
    return (
        gd
        - jnp.mean(gd, axis=-1, keepdims=True)
        - n_hat * jnp.mean(gd * n_hat, axis=-1, keepdims=True)
    ) * rs


def col_shift(value, by):
    if by == 0:
        return value
    at = lax.broadcasted_iota(jnp.int32, value.shape, 0) % SIDE
    rolled = pltpu.roll(value, (-by) % TOK, 0)
    return jnp.where((at + by >= 0) & (at + by < SIDE), rolled, 0.0)


def row_shift(value, by):
    if by == 0:
        return value
    gap = jnp.zeros((abs(by) * SIDE, value.shape[1]), value.dtype)
    if by > 0:
        return jnp.concatenate([value[by * SIDE :], gap], axis=0)
    return jnp.concatenate([gap, value[: TOK + by * SIDE]], axis=0)


def depthwise(value, tap, side):
    half = side // 2
    shifted = [col_shift(value, b - half) for b in range(side)]
    total = None
    for a in range(side):
        line = None
        for b in range(side):
            term = shifted[b] * tap(a * side + b)
            line = term if line is None else line + term
        line = row_shift(line, a - half)
        total = line if total is None else total + line
    return total


def depthwise_taps(value, grad, side, put):
    half = side // 2
    shifted = [col_shift(value, b - half) for b in range(side)]
    for a in range(side):
        d = a - half
        lo, hi = max(0, -d) * SIDE, (SIDE - max(0, d)) * SIDE
        for b in range(side):
            part = shifted[b][lo + d * SIDE : hi + d * SIDE] * grad[lo:hi]
            put(a * side + b, jnp.sum(part, axis=0, keepdims=True))


def lanes_of(at, width):
    return pl.ds(pl.multiple_of(at * width, width), width)


def side_by_side(blocks):
    return jnp.concatenate(blocks, axis=1)


def main_kernel(dims, outer, *refs):
    at = iter(refs)

    def take(count):
        return [next(at) for _ in range(count)]

    na = len(ARRAYS)
    source = dict(zip(ARRAYS, take(na)))
    (
        depth_in, ln_conv_in, scale_in, ln_attn_in, ln_mlp_in, adapt_depth_in,
        order_in, train_in, tok_in, grid_in, tcot_in, gcot_in,
    ) = take(12)
    hid_tok, hid_grid, out_gtok, out_ggrid = take(4)
    native = dict(zip(ARRAYS, take(na)))
    out_depth, out_ln_conv, out_scale, out_ln_attn, out_ln_mlp, out_ad = take(6)
    W = dict(zip(ARRAYS, take(na)))
    hops = take(4 * na)
    RX = {name: hops[4 * n : 4 * n + 4] for n, name in enumerate(ARRAYS)}
    (
        v_loc, vv, aq, vec_c, vec_d, x_in, c_in, n1_all, f_all, n2_all, c2_all,
        o_sb, o_rb, cv_sb, cv_rb, m_sb, m_rb, br_sb, br_rb, gsb, dgb,
        qkv, prob, ctx, u, up, r, rp, cn, crs, cv_sum, x1, c2f,
        adapted, spread, pooled, gate,
        dx3, dcot, dx3_all, dn2_sb, dn2_rb, dc2_sb, dc2_rb, dx1_all, dcv_all,
        dn1_sb, dn1_rb, df_sb, df_rb, dh, do_all, dqkv, dhc, dx1, dc2t, dad, dcn,
        gvs, gv_rb, gvx, gad, gad_rb, gad_all, turned,
    ) = take(65)
    (
        zs_send, zs_recv, s1_send, s1_recv, loc_sem, s2_send, s2_recv,
        v_send, v_recv, q_send, q_recv, h_send, h_recv, b_send, b_recv, c_send, c_recv,
        xo_send, xo_recv, g_send, g_recv, a_send, a_recv, gx_send, gx_recv, go,
    ) = take(26)

    p = lax.axis_index("pipe")
    dpi = lax.axis_index("dp")
    x = lax.axis_index("tensor")
    rest = dpi % outer
    zi = dpi // (outer * R)
    ri = (dpi // outer) % R
    xo = 1 - x
    ro = 1 - ri
    d_dim, c_dim, hq, ffq, cfq, adq, dg = dims
    adh = Z * adq
    dz, cz = d_dim // Z, c_dim // Z
    tile = 256
    ids = {name: number for number, name in enumerate(ARRAYS)}
    ev = {name: number for number, name in enumerate(EVENTS)}

    def dev(z=None, rr=None, xx=None, pp=None):
        z = zi if z is None else z
        rr = ri if rr is None else rr
        return (
            p if pp is None else pp,
            (z * R + rr) * outer + rest,
            x if xx is None else xx,
        )

    def zto(d):
        return lax.rem(zi + d, Z)

    def zfrom(d):
        return lax.rem(zi + Z - d, Z)

    def remote(src, dst, ssem, rsem, device):
        return pltpu.make_async_remote_copy(
            src_ref=src, dst_ref=dst, send_sem=ssem, recv_sem=rsem,
            device_id=device, device_id_type=pl.DeviceIdType.MESH,
        )

    sib = dev(pp=1 - p)
    over_r, over_x = dev(rr=ro), dev(xx=xo)

    def z_copy(e, d, src, dst):
        return remote(src, dst, zs_send.at[e, d - 1], zs_recv.at[e, d - 1], dev(zto(d)))

    sent = []

    def gather_copies(name, buf):
        return [z_copy(ev[name], d, buf.at[zi], buf.at[zi]) for d in range(1, Z)]

    def gather_start(name, buf, keep=True):
        copies = gather_copies(name, buf)
        for c in copies:
            c.start()
        if keep:
            sent.extend(copies)

    def gather_wait(name, buf):
        for d in range(1, Z):
            slot = buf.at[zfrom(d)]
            z_copy(ev[name], d, slot, slot).wait_recv()

    def scatter_start(name, sb, rb):
        for d in range(1, Z):
            c = z_copy(ev[name], d, sb.at[zto(d)], rb.at[d - 1])
            c.start()
            sent.append(c)

    def scatter_wait(name, rb):
        for d in range(1, Z):
            z_copy(ev[name], d, rb.at[d - 1], rb.at[d - 1]).wait_recv()

    def share_start(name, buf):
        for d in range(1, Z):
            c = z_copy(ev[name], d, buf.at[3], buf.at[d - 1])
            c.start()
            sent.append(c)

    def scattered(sb, rb):
        return (wide(sb[zi]) + wide(rb[0])) + (wide(rb[1]) + wide(rb[2]))

    barrier = pltpu.get_barrier_semaphore()
    greeted = [sib]
    for d in range(1, Z):
        greeted += [dev(zto(d)), dev(zto(d), ro), dev(zto(d), pp=1 - p)]
    greeted += [over_r, over_x, dev(rr=ro, xx=xo)]
    for device in greeted:
        pl.semaphore_signal(barrier, inc=1, device_id=device, device_id_type=pl.DeviceIdType.MESH)
    v_loc[...] = jnp.zeros(v_loc.shape, F32)
    taps7 = depth_in.shape[0]
    c_own = depth_in.shape[1]
    v_loc[0:taps7, 0:c_own] = wide(depth_in[...])
    v_loc[49:50, 0:c_own] = wide(ln_conv_in[...])
    v_loc[50:51, 0:c_own] = wide(scale_in[...])
    v_loc[56:57, 0:LANE] = wide(ln_attn_in[...])
    v_loc[57:58, 0:LANE] = wide(ln_mlp_in[...])
    aq[x] = jnp.zeros(aq.shape[1:], F32)
    aq[x, 0:9] = wide(adapt_depth_in[:, lanes_of(zi, adq)])
    pl.semaphore_wait(barrier, len(greeted))

    me8 = zi * R + ri
    v_arrivals = []
    for n, (d, flip) in enumerate([(d, s) for d in range(Z) for s in (0, 1)][1:]):
        tr = ro if flip else ri
        c = remote(v_loc, vv.at[me8], v_send.at[n], v_recv.at[n], dev(zto(d), tr))
        c.start()
        sent.append(c)
        fr = zfrom(d) * R + tr
        v_arrivals.append(remote(vv.at[fr], vv.at[fr], v_send.at[n], v_recv.at[n], dev(zto(d), tr)))
    vv[me8] = v_loc[...]
    c = remote(aq.at[x], aq.at[x], q_send, q_recv, over_x)
    c.start()
    sent.append(c)

    by_rows = ("O", "F2")

    def quarter_of(name, ref, z):
        if name == "Q":
            return ref.at[:, :, lanes_of(z, hq)]
        if name in by_rows:
            height = ref.shape[0] // Z
            return ref.at[pl.ds(pl.multiple_of(z * height, height), height)]
        return ref.at[:, lanes_of(z, ref.shape[1] // Z)]

    def step1_local(name):
        return pltpu.make_async_copy(
            quarter_of(name, source[name], zi), W[name].at[x, zi, ri], loc_sem.at[ids[name]]
        )

    def step1_copy(name, d):
        k = ids[name]
        return remote(
            quarter_of(name, source[name], zto(d)), W[name].at[x, zi, ri],
            s1_send.at[k, d - 1], s1_recv.at[k, d - 1], dev(zto(d)),
        )

    def half_of(name, j, z, rr, upper):
        w = W[name]
        half = w.shape[-2] // 2
        rows = slice(half, None) if upper else slice(0, half)
        if len(w.shape) == 6:
            return w.at[j, z, rr, :, rows]
        return w.at[j, z, rr, rows]

    def step2_copy(name, which, d):
        k = ids[name]
        z = zfrom(d)
        if which < 2:
            src = quarter_of(name, source[name], zi) if d == 0 else W[name].at[x, z, ri]
            dst = W[name].at[x, z, ri]
        else:
            src = dst = half_of(name, x, z, ro, False) if which == 2 else half_of(name, xo, z, ri, True)
        to = over_x if which in (1, 2) else over_r
        return remote(src, dst, s2_send.at[k, which, d], s2_recv.at[k, which, d], to)

    def step2_arrival(name, which, d):
        k = ids[name]
        z = zfrom(d)
        if which < 2:
            ref = W[name].at[x, z, ro] if which == 0 else W[name].at[xo, z, ri]
        else:
            ref = half_of(name, xo, z, ro, which == 3)
        to = over_x if which in (1, 2) else over_r
        return remote(ref, ref, s2_send.at[k, which, d], s2_recv.at[k, which, d], to)

    def relay1(*names):
        for name in names:
            step1_local(name).start()
            for d in range(1, Z):
                step1_copy(name, d).start()
            step2_copy(name, 0, 0).start()
            step2_copy(name, 1, 0).start()

    def relay2(name, ds=(1, 2, 3)):
        k = ids[name]
        for d in ds:
            slot = W[name].at[x, zfrom(d), ri]
            remote(slot, slot, s1_send.at[k, d - 1], s1_recv.at[k, d - 1], dev(zto(d))).wait_recv()
            step2_copy(name, 0, d).start()
            step2_copy(name, 1, d).start()

    def relay3(name, ds=(0, 1, 2, 3)):
        for d in ds:
            step2_arrival(name, 0, d).wait_recv()
            step2_copy(name, 2, d).start()
            step2_arrival(name, 1, d).wait_recv()
            step2_copy(name, 3, d).start()

    def relay4(*names):
        for name in names:
            step1_local(name).wait()
            for d in range(Z):
                step2_arrival(name, 2, d).wait_recv()
                step2_arrival(name, 3, d).wait_recv()

    def relay_sent():
        for name in ARRAYS:
            for d in range(1, Z):
                step1_copy(name, d).wait_send()
            for which in range(4):
                for d in range(Z):
                    step2_copy(name, which, d).wait_send()

    @pl.when(p == 0)
    def _():
        relay1("P1", "P2")

    @pl.when(p == 1)
    def _():
        dx3[...] = tcot_in[x]
        dcot[...] = gcot_in[x]
        dx3_all[zi] = tcot_in[x]
        gather_start("dx3", dx3_all, keep=False)

    for c in v_arrivals:
        c.wait_recv()
    remote(aq.at[xo], aq.at[xo], q_send, q_recv, over_x).wait_recv()
    low_lanes = lax.broadcasted_iota(jnp.int32, (64, LANE), 1) < LANE // 2
    for z in range(Z):
        first, second = vv[2 * z], pltpu.roll(vv[2 * z + 1], LANE // 2, 1)
        vec_c[:, z * cz : z * cz + LANE] = first[:, 0:LANE]
        vec_c[:, z * cz + LANE : z * cz + 2 * LANE] = jnp.where(
            low_lanes, first[:, LANE:], second[:, 0:LANE]
        )
        vec_c[:, z * cz + 2 * LANE : (z + 1) * cz] = second[:, LANE:]
    for i in range(Z * R):
        vec_d[:, i * LANE : (i + 1) * LANE] = vv[i, 56:64, 0:LANE]

    def gain_d(row):
        return vec_d[row : row + 1, :]

    def gain_c(row):
        return vec_c[row : row + 1, :]

    def token_entry():
        n_hat, _ = normed(wide(x_in[...]))
        n1_all[zi] = low(n_hat * gain_d(0))
        gather_start("n1", n1_all, keep=False)

    def conv_entry():
        @pl.loop(0, c_dim // LANE)
        def _(ch):
            lanes = lanes_of(ch, LANE)
            taps = vec_c[:, lanes]
            cn[:, lanes] = depthwise(wide(c_in[:, lanes]), lambda k: taps[k : k + 1], 7)

        n_hat, rs = normed(cn[...])
        cn[...] = n_hat
        crs[...] = jnp.broadcast_to(rs, crs.shape)
        f_all[zi] = low(n_hat * gain_c(49))
        gather_start("f", f_all, keep=False)

    def first_relays():
        relay2("P1")
        relay1("Q", "O")
        relay2("P2")
        relay3("P1")

    sent.extend(gather_copies("n1", n1_all))
    sent.extend(gather_copies("f", f_all))

    @pl.when(p == 0)
    def _():
        first = order_in[0, x] == 0
        c_in[...] = jnp.where(first, grid_in[0], grid_in[1])
        x_in[...] = jnp.where(first, tok_in[0], tok_in[1])
        conv_entry()
        token_entry()
        first_relays()

    @pl.when(p == 1)
    def _():
        pl.semaphore_wait(go, 1)
        relay1("P1", "P2")
        first_relays()
        remote(c_in, c_in, h_send.at[1], h_recv.at[1], sib).wait_recv()
        conv_entry()

    relay2("Q")
    relay2("O")
    relay1("E", "Gi", "Go")
    relay3("P2", (0, 1))
    relay4("P1")
    gather_wait("f", f_all)

    def conv_hidden(j):
        @pl.loop(0, cfq // tile)
        def _(t):
            lanes = lanes_of(t, tile)
            act, der = gelu_pair(mm(flat(f_all[...]), flat(W["P1"][j, :, :, :, lanes])))
            r[j, :, lanes] = low(act)
            rp[j, :, lanes] = low(der)

    conv_hidden(0)

    relay3("P2", (2, 3))
    for name in ("E", "Gi", "Go"):
        relay2(name)
    relay1("F1")
    conv_hidden(1)
    relay3("Q")
    relay3("O")
    relay2("F1")
    relay1("F2")

    relay4("P2")

    @pl.loop(0, Z)
    def _(z):
        acc = mm_nt(r[0], flat(W["P2"][0, z])) + mm_nt(r[1], flat(W["P2"][1, z]))
        cv_sb[:, :, lanes_of(z, cz)] = low(acc).reshape(Z, TOK, cz)

    scatter_start("cv", cv_sb, cv_rb)

    for name in ("E", "Gi", "Go"):
        relay3(name)
    relay2("F2")

    @pl.when(p == 0)
    def _():
        pl.semaphore_signal(go, inc=1, device_id=sib, device_id_type=pl.DeviceIdType.MESH)

    @pl.when(p == 1)
    def _():
        remote(x_in, x_in, h_send.at[0], h_recv.at[0], sib).wait_recv()
        token_entry()

    relay4("Q", "O")
    gather_wait("n1", n1_all)
    for j in range(2):
        wj = side_by_side([flat(W["Q"][j, :, :, s]) for s in range(3)])
        qkv[j] = low(mm(flat(n1_all[...]), wj))
    for j in range(2):
        for b in range(Z):
            rows = slice(b * TOK, (b + 1) * TOK)
            outs = []
            for h in range(hq // HD):
                q, kk, vals = (qkv[j, rows, s * hq + h * HD : s * hq + (h + 1) * HD] for s in range(3))
                sc = mm_nt(q, kk) * HD ** (-0.5)
                e = jnp.exp(sc - jnp.max(sc, axis=-1, keepdims=True))
                pr = low(e / jnp.sum(e, axis=-1, keepdims=True))
                prob[j, h, b] = pr
                outs.append(mm(pr, vals))
            ctx[j, rows, :] = low(side_by_side(outs))

    def out_block(j, z):
        return side_by_side([W["O"][j, z, 0], W["O"][j, z, 1]])

    @pl.loop(0, Z)
    def _(z):
        both = jnp.concatenate([out_block(0, z), out_block(1, z)], axis=0)
        acc = mm(side_by_side([ctx[0], ctx[1]]), both)
        o_sb[:, :, lanes_of(z, dz)] = low(acc).reshape(Z, TOK, dz)

    scatter_start("o", o_sb, o_rb)

    relay3("F1")

    scatter_wait("cv", cv_rb)
    cv_sum[...] = scattered(cv_sb, cv_rb)
    c2f[...] = wide(c_in[...]) + gain_c(50) * cv_sum[...]
    c2_low = low(c2f[...])
    c2_all[zi] = c2_low
    gather_start("c2", c2_all)
    hid_grid[x] = c2_low

    @pl.when(p == 0)
    def _():
        remote(hid_grid.at[x], c_in, h_send.at[1], h_recv.at[1], sib).start()

    relay3("F2")
    scatter_wait("o", o_rb)
    x1[...] = wide(x_in[...]) + scattered(o_sb, o_rb)
    n_hat, _ = normed(x1[...])
    n2_all[zi] = low(n_hat * gain_d(1))
    gather_start("n2", n2_all)

    relay4("E", "Gi", "Go")
    gather_wait("c2", c2_all)
    row8 = lax.broadcasted_iota(jnp.int32, (8, adq), 0)
    gs_part = None
    for j in range(2):
        ad = mm(flat(c2_all[...]), flat(W["E"][j]))
        adapted[j] = ad
        taps = aq[j]
        pool = jnp.zeros((8, adq), F32)
        for b in range(Z):
            sp = depthwise(ad[b * TOK : (b + 1) * TOK], lambda k: taps[k : k + 1], 3)
            spread[j, b] = sp
            pool = jnp.where(row8 == b, jnp.mean(sp, axis=0, keepdims=True), pool)
        pooled[j] = pool
        term = mm_nt(low(pool), flat(W["Gi"][j]))
        gs_part = term if gs_part is None else gs_part + term
    gsb[3] = gs_part
    share_start("gs", gsb)

    relay4("F1")
    gather_wait("n2", n2_all)
    for j in range(2):

        @pl.loop(0, ffq // tile)
        def _(t):
            lanes = lanes_of(t, tile)
            act, der = gelu_pair(mm(flat(n2_all[...]), flat(W["F1"][j, :, :, :, lanes])))
            u[j, :, lanes] = low(act)
            up[j, :, lanes] = low(der)

    scatter_wait("gs", gsb)

    def gate_hidden():
        return gelu_pair((gsb[0] + gsb[1]) + (gsb[2] + gsb[3]))

    gh, _ = gate_hidden()
    for j in range(2):
        g8 = jnp.tanh(mm(low(gh), flat(W["Go"][j])))
        gate[j] = g8
        for b in range(Z):
            br_sb[b, :, j * adq : (j + 1) * adq] = low(g8[b : b + 1] * spread[j, b])
    scatter_start("br", br_sb, br_rb)
    relay4("F2")

    @pl.loop(0, Z)
    def _(z):
        acc = None
        for j in range(2):
            term = mm(u[j], side_by_side([W["F2"][j, z, 0], W["F2"][j, z, 1]]))
            acc = term if acc is None else acc + term
        m_sb[:, :, lanes_of(z, dz)] = low(acc).reshape(Z, TOK, dz)

    scatter_start("m", m_sb, m_rb)

    def exchange(n, buf):
        remote(buf.at[x], buf.at[x], xo_send.at[n], xo_recv.at[n], over_x).start()

    def layer_output(total):
        scatter_wait("br", br_rb)
        total[...] = x1[...]
        for d in range(Z):
            piece = br_sb[zi] if d == 0 else br_rb[d - 1]
            for j in range(2):
                lanes = pl.ds(pl.multiple_of(j * adh + zfrom(d) * adq, LANE), adq)
                total[:, lanes] += wide(piece[:, j * adq : (j + 1) * adq])
        scatter_wait("m", m_rb)
        hid_tok[x] = low(total[...] + scattered(m_sb, m_rb))

    @pl.when(p == 0)
    def _():
        layer_output(dx1)
        remote(hid_tok.at[x], x_in, h_send.at[0], h_recv.at[0], sib).start()
        exchange(0, hid_tok)

    exchange(1, hid_grid)
    relay_sent()

    def over_cores(d):
        return remote(
            out_gtok.at[x], dx3_all.at[zi], b_send.at[d], b_recv.at[d], dev(zto(d), pp=1 - p)
        )

    @pl.when(p == 1)
    def _():
        gather_wait("dx3", dx3_all)
        for c in gather_copies("dx3", dx3_all):
            c.wait_send()

    @pl.when(p == 0)
    def _():
        for d in range(Z):
            slot = dx3_all.at[zfrom(d)]
            remote(slot, slot, b_send.at[d], b_recv.at[d], sib).wait_recv()
        dx3[...] = dx3_all[zi]

    def own_lanes(j):
        return pl.ds(pl.multiple_of(j * adh + zi * adq, LANE), adq)

    gh, ghp = gate_hidden()
    dgh_part = None
    dgp = []
    for j in range(2):
        dgate = jnp.zeros((8, adq), F32)
        for b in range(Z):
            dbr = wide(dx3_all[b, :, own_lanes(j)])
            dgate = jnp.where(row8 == b, jnp.sum(dbr * spread[j, b], axis=0, keepdims=True), dgate)
        dg8 = low(dgate * (1.0 - gate[j] * gate[j]))
        dgp.append(dg8)
        term = mm_nt(dg8, flat(W["Go"][j]))
        dgh_part = term if dgh_part is None else dgh_part + term
    dgb[3] = dgh_part
    share_start("dgh", dgb)

    for j in range(2):

        @pl.loop(0, ffq // tile)
        def _(t):
            rows = lanes_of(t, tile)
            both = side_by_side([W["F2"][j, z, rr, rows] for z in range(Z) for rr in range(R)])
            du = mm_nt(flat(dx3_all[...]), both)
            dh[j, :, rows] = low(du * wide(up[j, :, rows]))

    scatter_wait("dgh", dgb)
    dgs = low(((dgb[0] + dgb[1]) + (dgb[2] + dgb[3])) * ghp)
    for j in range(2):
        dpool = mm(dgs, flat(W["Gi"][j])) * (1.0 / TOK)
        taps = aq[j]
        tap_rows = [None] * 9
        for b in range(Z):
            dsp = gate[j, b : b + 1] * wide(dx3_all[b, :, own_lanes(j)]) + dpool[b : b + 1]
            dad[j, b * TOK : (b + 1) * TOK] = low(depthwise(dsp, lambda k: taps[8 - k : 9 - k], 3))

            def put(k, row):
                tap_rows[k] = row if tap_rows[k] is None else tap_rows[k] + row

            depthwise_taps(adapted[j, b * TOK : (b + 1) * TOK], dsp, 3, put)
        for k in range(9):
            gad[j, k : k + 1] = tap_rows[k]
        gad[j, 9:16] = jnp.zeros((7, adq), F32)

    @pl.loop(0, Z)
    def _(z):
        acc = mm_nt(dad[0], flat(W["E"][0, z])) + mm_nt(dad[1], flat(W["E"][1, z]))
        dc2_sb[:, :, lanes_of(z, cz)] = low(acc).reshape(Z, TOK, cz)

    scatter_start("dc2", dc2_sb, dc2_rb)

    @pl.loop(0, Z)
    def _(z):
        acc = mm_nt(dh[0], flat(W["F1"][0, z])) + mm_nt(dh[1], flat(W["F1"][1, z]))
        dn2_sb[:, :, lanes_of(z, dz)] = low(acc).reshape(Z, TOK, dz)

    scatter_start("dn2", dn2_sb, dn2_rb)

    def half_rows(name, upper):
        half = W[name].shape[-2] // 2
        rows = slice(half, None) if upper else slice(0, half)
        return (slice(None), rows) if len(W[name].shape) == 6 else (rows,)

    def hop_copy(name, which):
        n = ids[name]
        lower, upper = half_rows(name, False), half_rows(name, True)
        src, to = (
            lambda: (W[name].at[(xo, slice(None), slice(None)) + lower], over_x),
            lambda: (W[name].at[(slice(None), slice(None), ro) + upper], over_r),
            lambda: (RX[name][0].at[:, ro], over_r),
            lambda: (RX[name][1].at[xo], over_x),
        )[which]()
        return remote(src, RX[name][which], g_send.at[n, which], g_recv.at[n, which], to)

    def reduce_start(name):
        hop_copy(name, 0).start()
        hop_copy(name, 1).start()

    def reduce_middle(*names):
        for name in names:
            lower, upper = half_rows(name, False), half_rows(name, True)
            buf = RX[name]
            hop_copy(name, 0).wait_recv()

            @pl.loop(0, Z)
            def _(z):
                for rr in range(R):
                    own = W[name][(x, z, rr) + lower]
                    buf[0][z, rr] = low(wide(own) + wide(buf[0][z, rr]))

            hop_copy(name, 2).start()
            hop_copy(name, 1).wait_recv()

            @pl.loop(0, Z)
            def _(z):
                for j in range(2):
                    own = W[name][(j, z, ri) + upper]
                    buf[1][j, z] = low(wide(own) + wide(buf[1][j, z]))

            hop_copy(name, 3).start()

    def reduce_end(*names):
        for name in names:
            lower, upper = half_rows(name, False), half_rows(name, True)
            buf = RX[name]
            hop_copy(name, 2).wait_recv()
            hop_copy(name, 3).wait_recv()

            @pl.loop(0, Z)
            def _(z):
                W[name][(x, z, ri) + lower] = low(wide(buf[0][z, ri]) + wide(buf[2][z]))
                W[name][(x, z, ri) + upper] = low(wide(buf[1][x, z]) + wide(buf[3][z]))

            for d in range(1, Z):
                back_copy(name, d).start()
            back_local(name).start()

    def back_copy(name, d):
        n = ids[name]
        return remote(
            W[name].at[x, zto(d), ri], quarter_of(name, native[name], zi),
            a_send.at[n, d - 1], a_recv.at[n, d - 1], dev(zto(d)),
        )

    def back_local(name):
        return pltpu.make_async_copy(
            W[name].at[x, zi, ri], quarter_of(name, native[name], zi), loc_sem.at[ids[name]]
        )

    peers = ((1, 0), (0, 1), (1, 1))

    def owner(k):
        return (ro if peers[k][0] else ri), (xo if peers[k][1] else x)

    def row_grad(name, left, right):
        width = W[name].shape[3]
        span = R * width

        @pl.loop(0, Z)
        def _(z):
            turned[0:span] = flat(left[:, :, lanes_of(z, span)]).T
            for j in range(2):
                W[name][j, z] = low(mm(turned[0:span], right[j])).reshape(R, width, -1)

        reduce_start(name)

    def col_grad(name, left, right):
        width = left.shape[2]
        for j in range(2):
            turned[j * width : (j + 1) * width] = left[j].T

        @pl.loop(0, Z)
        def _(z):
            rhs = flat(right[:, :, lanes_of(z, dz)])
            for j in range(2):
                g = low(mm(turned[j * width : (j + 1) * width], rhs))
                for rr in range(R):
                    W[name][j, z, rr] = g[:, rr * LANE : (rr + 1) * LANE]

        reduce_start(name)

    for j in range(2):
        W["Gi"][j] = low(mm_tn(dgs, low(pooled[j]))).reshape(Z, R, -1, adq)
        W["Go"][j] = low(mm_tn(low(gh), dgp[j])).reshape(Z, R, -1, adq)
    reduce_start("Gi")
    reduce_start("Go")
    row_grad("E", c2_all, dad)

    @pl.when(p == 0)
    def _():
        remote(dcot, dcot, c_send, c_recv, sib).wait_recv()

    scatter_wait("dc2", dc2_rb)
    dc2t[...] = wide(dcot[...]) + scattered(dc2_sb, dc2_rb)
    gvs_ls = jnp.sum(cv_sum[...] * dc2t[...], axis=0, keepdims=True)
    dcv_all[zi] = low(dc2t[...] * gain_c(50))
    gather_start("dcv", dcv_all)

    scatter_wait("dn2", dn2_rb)
    dn2 = scattered(dn2_sb, dn2_rb)
    n_hat, rs = normed(x1[...])
    gvs_d1 = jnp.sum(dn2 * n_hat, axis=0, keepdims=True)
    dx1[...] = wide(dx3[...]) + norm_back(dn2, n_hat, rs, gain_d(1))
    dx1_all[zi] = low(dx1[...])
    gather_start("dx1", dx1_all)

    col_grad("F2", u, dx3_all)
    row_grad("F1", n2_all, dh)

    gather_wait("dcv", dcv_all)
    for j in range(2):

        @pl.loop(0, cfq // tile)
        def _(t):
            lanes = lanes_of(t, tile)
            dr = mm(flat(dcv_all[...]), flat(W["P2"][j, :, :, :, lanes]))
            dhc[j, :, lanes] = low(dr * wide(rp[j, :, lanes]))

    @pl.loop(0, Z)
    def _(z):
        acc = mm_nt(dhc[0], flat(W["P1"][0, z])) + mm_nt(dhc[1], flat(W["P1"][1, z]))
        df_sb[:, :, lanes_of(z, cz)] = low(acc).reshape(Z, TOK, cz)

    scatter_start("df", df_sb, df_rb)

    early = ("Gi", "Go", "E", "F2", "F1")

    def pw_grads():
        row_grad("P2", dcv_all, r)
        row_grad("P1", f_all, dhc)

    @pl.when(p == 0)
    def _():
        pw_grads()

    gather_wait("dx1", dx1_all)
    for j in range(2):
        both = side_by_side([W["O"][j, z, rr] for z in range(Z) for rr in range(R)])
        do_all[j] = low(mm_nt(flat(dx1_all[...]), both))
    for j in range(2):
        for b in range(Z):
            rows = slice(b * TOK, (b + 1) * TOK)
            parts = [[], [], []]
            for h in range(hq // HD):
                q, kk, vals = (qkv[j, rows, s * hq + h * HD : s * hq + (h + 1) * HD] for s in range(3))
                do = do_all[j, rows, h * HD : (h + 1) * HD]
                pr = prob[j, h, b]
                dp = mm_nt(do, vals)
                prw = wide(pr)
                ds = low(prw * (dp - jnp.sum(dp * prw, axis=-1, keepdims=True)) * HD ** (-0.5))
                parts[0].append(mm(ds, kk))
                parts[1].append(mm_tn(ds, q))
                parts[2].append(mm_tn(pr, do))
            for s in range(3):
                dqkv[j, rows, s * hq : (s + 1) * hq] = low(side_by_side(parts[s]))

    @pl.loop(0, Z)
    def _(z):
        acc = None
        for j in range(2):
            term = mm_nt(dqkv[j], side_by_side([flat(W["Q"][j, z, :, s]) for s in range(3)]))
            acc = term if acc is None else acc + term
        dn1_sb[:, :, lanes_of(z, dz)] = low(acc).reshape(Z, TOK, dz)

    scatter_start("dn1", dn1_sb, dn1_rb)

    def attention_grads():
        @pl.loop(0, Z)
        def _(z):
            turned[0:dz] = flat(n1_all[:, :, lanes_of(z, dz)]).T
            for j in range(2):
                g = low(mm(turned[0:dz], dqkv[j]))
                for s in range(3):
                    W["Q"][j, z, :, s] = g[:, s * hq : (s + 1) * hq].reshape(R, -1, hq)

        reduce_start("Q")
        col_grad("O", ctx, dx1_all)

    reduce_middle(*early)

    @pl.when(p == 0)
    def _():
        attention_grads()

    scatter_wait("dn1", dn1_rb)
    dn1 = scattered(dn1_sb, dn1_rb)
    n_hat, rs = normed(wide(x_in[...]))
    gvs_d0 = jnp.sum(dn1 * n_hat, axis=0, keepdims=True)
    out_gtok[x] = low(dx1[...] + norm_back(dn1, n_hat, rs, gain_d(0)))

    @pl.when(p == 1)
    def _():
        for d in (1, 2, 3, 0):
            over_cores(d).start()

    scatter_wait("df", df_rb)
    dfv = scattered(df_sb, df_rb)
    gvs_lc = jnp.sum(dfv * cn[...], axis=0, keepdims=True)
    dcn[...] = norm_back(dfv, cn[...], crs[:, 0:1], gain_c(49))

    @pl.loop(0, c_dim // LANE)
    def _(ch):
        lanes = lanes_of(ch, LANE)
        taps = vec_c[:, lanes]
        back = depthwise(dcn[:, lanes], lambda k: taps[48 - k : 49 - k], 7)
        out_ggrid[x, :, lanes] = low(dc2t[:, lanes] + back)

    @pl.when(p == 1)
    def _():
        remote(out_ggrid.at[x], dcot, c_send, c_recv, sib).start()
        layer_output(dx1)
        exchange(0, hid_tok)
        pw_grads()
        attention_grads()

    exchange(2, out_gtok)
    exchange(3, out_ggrid)

    @pl.loop(0, Z)
    def _(z):
        for part in range(cz // LANE):
            lanes = pl.ds(pl.multiple_of(z * cz + part * LANE, LANE), LANE)

            def put(k, row):
                gvs[z, k : k + 1, part * LANE : (part + 1) * LANE] = row

            depthwise_taps(wide(c_in[:, lanes]), dcn[:, lanes], 7, put)

    for z in range(Z):
        gvs[z, 49:50] = gvs_lc[:, z * cz : (z + 1) * cz]
        gvs[z, 50:51] = gvs_ls[:, z * cz : (z + 1) * cz]
        gvs[z, 51:64] = jnp.zeros((13, cz), F32)
        gvs[z, 56:57, 0:dz] = gvs_d0[:, z * dz : (z + 1) * dz]
        gvs[z, 57:58, 0:dz] = gvs_d1[:, z * dz : (z + 1) * dz]
    scatter_start("gv", gvs, gv_rb)

    def group_copy(n, k, src, dst):
        rr, xx = owner(k)
        return remote(src, dst, gx_send.at[n, k], gx_recv.at[n, k], dev(rr=rr, xx=xx))

    for k in range(3):
        c = group_copy(1, k, gad, gad_rb.at[k])
        c.start()
        sent.append(c)
    reduce_end(*early)
    reduce_middle("P2", "P1")
    scatter_wait("gv", gv_rb)
    gvx[3] = (gvs[zi] + gv_rb[0]) + (gv_rb[1] + gv_rb[2])
    for k in range(3):
        c = group_copy(0, k, gvx.at[3], gvx.at[k])
        c.start()
        sent.append(c)
    for k in range(3):
        group_copy(1, k, gad, gad_rb.at[k]).wait_recv()
    gad_all[zi] = (gad[x] + gad_rb[0, x]) + (gad_rb[1, x] + gad_rb[2, x])
    gather_start("gad", gad_all)

    reduce_middle("Q", "O")
    reduce_end("P2", "P1", "Q", "O")

    for k in range(3):
        group_copy(0, k, gvx.at[k], gvx.at[k]).wait_recv()
    total = (gvx[0] + gvx[1]) + (gvx[2] + gvx[3])
    mine = jnp.where(ri == 1, pltpu.roll(total, c_own, 1), total)[:, 0:c_own]
    mine_d = jnp.where(ri == 1, total[:, LANE : 2 * LANE], total[:, 0:LANE])

    def flag(n):
        return train_in[0, n].astype(F32)

    out_depth[...] = mine[0:taps7] * flag(0)
    out_ln_conv[...] = mine[49:50] * flag(1)
    out_scale[...] = mine[50:51] * flag(4)
    out_ln_attn[...] = mine_d[56:57]
    out_ln_mlp[...] = mine_d[57:58]
    gather_wait("gad", gad_all)
    for z in range(Z):
        out_ad[:, z * adq : (z + 1) * adq] = gad_all[z][0:9]
    for name in ARRAYS:
        back_local(name).wait()
        for d in range(1, Z):
            n = ids[name]
            slot = quarter_of(name, native[name], zfrom(d))
            remote(slot, slot, a_send.at[n, d - 1], a_recv.at[n, d - 1], dev(zto(d))).wait_recv()
    for n, buf in enumerate((hid_tok, hid_grid, out_gtok, out_ggrid)):
        c = remote(buf.at[x], buf.at[x], xo_send.at[n], xo_recv.at[n], over_x)
        c.wait_send()
        remote(buf.at[xo], buf.at[xo], xo_send.at[n], xo_recv.at[n], over_x).wait_recv()

    @pl.when(p == 0)
    def _():
        remote(hid_tok.at[x], x_in, h_send.at[0], h_recv.at[0], sib).wait_send()
        remote(hid_grid.at[x], c_in, h_send.at[1], h_recv.at[1], sib).wait_send()

    @pl.when(p == 1)
    def _():
        for d in range(Z):
            over_cores(d).wait_send()
        remote(out_ggrid.at[x], dcot, c_send, c_recv, sib).wait_send()

    for c in sent:
        c.wait_send()
    for name in ARRAYS:
        for which in range(4):
            hop_copy(name, which).wait_send()
        for d in range(1, Z):
            back_copy(name, d).wait_send()


def run_layers(weights, vectors, order, train, streams, sizes, outer):
    d_dim, c_dim, hq, ffq, cfq, adw, dg = sizes
    vm = pltpu.VMEM
    blocks = []
    for name, value in zip(ARRAYS, weights):
        if name == "Q":
            blocks.append((3, value.shape[1], hq))
        elif name in ("O", "F2"):
            blocks.append((value.shape[0] // Z, value.shape[1]))
        else:
            blocks.append((value.shape[0], value.shape[1] // Z))
    rows = Z * TOK

    def act(width, count=Z, kind=BF):
        return vm((count, TOK, width), kind)

    scratch = [vm((2, Z, R) + s, BF) for s in blocks] + [
        vm(lead + s[:-2] + (s[-2] // 2, s[-1]), BF)
        for s in blocks
        for lead in ((Z, R), (2, Z), (Z,), (Z,))
    ]
    scratch += [
        vm((64, 2 * LANE), F32), vm((Z * R, 64, 2 * LANE), F32), vm((2, 16, adw), F32), vm((64, c_dim), F32), vm((8, d_dim), F32),
        vm((TOK, d_dim), BF), vm((TOK, c_dim), BF), act(d_dim), act(c_dim), act(d_dim), act(c_dim),
        act(d_dim), act(d_dim, 3), act(c_dim), act(c_dim, 3), act(d_dim), act(d_dim, 3),
        act(2 * adw), act(2 * adw, 3), vm((4, 8, dg), F32), vm((4, 8, dg), F32),
        vm((2, rows, 3 * hq), BF), vm((2, hq // HD, Z, TOK, TOK), BF), vm((2, rows, hq), BF),
        vm((2, rows, ffq), BF), vm((2, rows, ffq), BF), vm((2, rows, cfq), BF), vm((2, rows, cfq), BF),
        vm((TOK, c_dim), F32), vm((TOK, LANE), F32), vm((TOK, c_dim), F32), vm((TOK, d_dim), F32), vm((TOK, c_dim), F32),
        vm((2, rows, adw), F32), vm((2, Z, TOK, adw), F32), vm((2, 8, adw), F32), vm((2, 8, adw), F32),
        vm((TOK, d_dim), BF), vm((TOK, c_dim), BF), act(d_dim), act(d_dim), act(d_dim, 3), act(c_dim), act(c_dim, 3),
        act(d_dim), act(c_dim),
        act(d_dim), act(d_dim, 3), act(c_dim), act(c_dim, 3), vm((2, rows, ffq), BF), vm((2, rows, hq), BF),
        vm((2, rows, 3 * hq), BF), vm((2, rows, cfq), BF), vm((TOK, d_dim), F32), vm((TOK, c_dim), F32), vm((2, rows, adw), BF),
        vm((TOK, c_dim), F32),
        vm((Z, 64, c_dim // Z), F32), vm((3, 64, c_dim // Z), F32), vm((4, 64, c_dim // Z), F32),
        vm((2, 16, adw), F32), vm((3, 2, 16, adw), F32), vm((Z, 16, adw), F32),
        vm((2 * ffq, rows), BF),
    ]
    dma = pltpu.SemaphoreType.DMA
    na = len(ARRAYS)
    scratch += [
        dma((len(EVENTS), 3)), dma((len(EVENTS), 3)), dma((na, 3)), dma((na, 3)), dma((na,)),
        dma((na, 4, Z)), dma((na, 4, Z)), dma((7,)), dma((7,)), dma, dma, dma((2,)), dma((2,)), dma((Z,)), dma((Z,)), dma, dma,
        dma((4,)), dma((4,)), dma((na, 4)), dma((na, 4)), dma((na, 3)), dma((na, 3)), dma((2, 3)), dma((2, 3)),
        pltpu.SemaphoreType.REGULAR,
    ]
    sds = jax.ShapeDtypeStruct
    out_shape = [sds((2, TOK, d_dim), BF), sds((2, TOK, c_dim), BF)] * 2
    out_shape += [sds(value.shape, BF) for value in weights]
    out_shape += [sds(value.shape, F32) for value in vectors]
    any_spec = pl.BlockSpec(memory_space=pl.ANY)
    vm_spec = pl.BlockSpec(memory_space=pltpu.VMEM)
    sm_spec = pl.BlockSpec(memory_space=pltpu.SMEM)
    return pl.pallas_call(
        functools.partial(main_kernel, sizes, outer),
        out_shape=out_shape,
        in_specs=[any_spec] * na + [vm_spec] * 6 + [sm_spec] * 2 + [vm_spec] * 4,
        out_specs=[vm_spec] * 4 + [any_spec] * na + [vm_spec] * 6,
        scratch_shapes=scratch,
        compiler_params=pltpu.CompilerParams(
            collective_id=0, has_side_effects=True, vmem_limit_bytes=62 * 1024 * 1024
        ),
        cost_estimate=pl.CostEstimate(flops=26 * 10**9, bytes_accessed=10**8, transcendentals=10**7),
        name="layers",
    )(*weights, *vectors, order, train, *streams)


def per_device(
    tokens,
    conv_grid,
    order,
    trainable,
    ln_attn,
    w_qkv,
    w_attn_out,
    ln_mlp,
    w_fc_in,
    w_fc_out,
    conv_depth,
    ln_conv,
    w_pw_in,
    w_pw_out,
    layer_scale,
    w_adapt,
    adapt_depth,
    w_gate_in,
    w_gate_out,
    tok_cot,
    grid_cot,
):
    dp_count = lax.axis_size("dp")
    outer = dp_count // (Z * R)
    groups = [[g * outer + o for o in range(outer)] for g in range(Z * R)]
    layer_at = lax.axis_index("pipe")

    def block(value, axis):
        value = value[0]
        if outer == 1:
            return value
        return lax.all_gather(value, "dp", axis=axis, tiled=True, axis_index_groups=groups)

    def share(value, axis):
        if outer > 1:
            value = lax.psum_scatter(
                value, "dp", scatter_dimension=axis, tiled=True, axis_index_groups=groups
            )
        return value[None]

    qkv = block(w_qkv, 1)
    gate_in = block(w_gate_in, 1).T
    pw_in = block(w_pw_in, 0)
    adapt = block(w_adapt, 0)
    fc_in = block(w_fc_in, 0)
    weights = (
        pw_in,
        block(w_pw_out, 1).T,
        qkv,
        block(w_attn_out, 1),
        adapt,
        gate_in,
        block(w_gate_out, 0),
        fc_in,
        block(w_fc_out, 1),
    )
    vectors = (
        block(conv_depth, 1),
        block(ln_conv, 0)[None],
        block(layer_scale, 0)[None],
        block(ln_attn, 0)[None],
        block(ln_mlp, 0)[None],
        adapt_depth[0],
    )
    spread = Z * R
    sizes = (
        qkv.shape[1] * spread, pw_in.shape[0] * spread, qkv.shape[2] // Z, fc_in.shape[1] // Z,
        pw_in.shape[1] // Z, adapt.shape[1] // Z, gate_in.shape[0] * spread,
    )

    def rows_of(value):
        return value.reshape(value.shape[0], TOK, value.shape[-1])

    streams = [rows_of(value) for value in (tokens, conv_grid, tok_cot, grid_cot)]
    outs = run_layers(weights, vectors, order, trainable, streams, sizes, outer)
    hid_tok, hid_grid, g_tok, g_grid = outs[:4]
    g_p1, g_p2, g_q, g_o, g_e, g_gi, g_go, g_f1, g_f2 = [value.astype(F32) for value in outs[4:13]]
    g_depth, g_ln_conv, g_scale, g_ln_attn, g_ln_mlp, g_ad = outs[13:]

    swap = (layer_at == 0) & (order[0, 0] == 1)
    g_tok = jnp.where(swap, g_tok[::-1], g_tok)
    g_grid = jnp.where(swap, g_grid[::-1], g_grid)
    grid_shape = (1,) + conv_grid.shape
    tok_shape = (1,) + tokens.shape
    flags = trainable[0].astype(F32)
    if outer > 1:
        g_ad = lax.psum(g_ad, "dp", axis_index_groups=groups)
    return (
        hid_tok.reshape(tok_shape),
        hid_grid.reshape(grid_shape),
        g_tok.reshape(tok_shape),
        g_grid.reshape(grid_shape),
        share(g_ln_attn[0], 0),
        share(g_q, 1),
        share(g_o, 1),
        share(g_ln_mlp[0], 0),
        share(g_f1, 0),
        share(g_f2, 1),
        share(g_depth, 1),
        share(g_ln_conv[0], 0),
        share(g_p1 * flags[2], 0),
        share((g_p2 * flags[3]).T, 1),
        share(g_scale[0], 0),
        share(g_e, 0),
        g_ad[None],
        share(g_gi.T, 1),
        share(g_go, 0),
    )


def solution(mesh):
    in_specs = (
        P(None, "dp", None, None),
        P(None, "dp", None, None, None),
        P("dp", None),
        P("pipe", None),
        P("pipe", "dp"),
        P("pipe", None, "dp", "tensor"),
        P("pipe", "tensor", "dp"),
        P("pipe", "dp"),
        P("pipe", "dp", "tensor"),
        P("pipe", "tensor", "dp"),
        P("pipe", None, "dp"),
        P("pipe", "dp"),
        P("pipe", "dp", "tensor"),
        P("pipe", "tensor", "dp"),
        P("pipe", "dp"),
        P("pipe", "dp", "tensor"),
        P("pipe", None, "tensor"),
        P("pipe", "tensor", "dp"),
        P("pipe", "dp", "tensor"),
        P(None, "dp", None, None),
        P(None, "dp", None, None, None),
    )
    out_specs = (
        P("pipe", None, "dp", None, None),
        P("pipe", None, "dp", None, None, None),
        P("pipe", None, "dp", None, None),
        P("pipe", None, "dp", None, None, None),
        P("pipe", "dp"),
        P("pipe", None, "dp", "tensor"),
        P("pipe", "tensor", "dp"),
        P("pipe", "dp"),
        P("pipe", "dp", "tensor"),
        P("pipe", "tensor", "dp"),
        P("pipe", None, "dp"),
        P("pipe", "dp"),
        P("pipe", "dp", "tensor"),
        P("pipe", "tensor", "dp"),
        P("pipe", "dp"),
        P("pipe", "dp", "tensor"),
        P("pipe", None, "tensor"),
        P("pipe", "tensor", "dp"),
        P("pipe", "dp", "tensor"),
    )
    return jax.shard_map(
        per_device, mesh=mesh, in_specs=in_specs, out_specs=out_specs, check_vma=False
    )
```

```python
import functools

import jax
import jax.numpy as jnp
from jax import lax
from jax.experimental import pallas as pl
from jax.experimental.pallas import tpu as pltpu
from jax.sharding import PartitionSpec as P

HD = 64
Z = 4
R = 2
TOK = 64
SIDE = 8
LANE = 128
BF = jnp.bfloat16
F32 = jnp.float32
ARRAYS = ("P1", "P2", "Q", "O", "E", "Gi", "Go", "F1", "F2")
EVENTS = (
    "n1", "f", "o", "cv", "n2", "c2", "m", "br", "gs",
    "dx3", "dgh", "dn2", "dc2", "dx1", "dcv", "dn1", "df", "gv", "gad",
)


def mm(a, b):
    return lax.dot_general(a, b, (((1,), (0,)), ((), ())), preferred_element_type=F32)


def mm_nt(a, b):
    return lax.dot_general(a, b, (((1,), (1,)), ((), ())), preferred_element_type=F32)


def mm_tn(a, b):
    return lax.dot_general(a, b, (((0,), (0,)), ((), ())), preferred_element_type=F32)


def flat(value):
    return value.reshape(-1, value.shape[-1])


def low(value):
    return value.astype(BF)


def wide(value):
    return value.astype(F32)


def gelu_pair(h):
    phi = 0.5 * (1.0 + lax.erf(h * 0.7071067811865476))
    dens = jnp.exp(-0.5 * h * h) * 0.3989422804014327
    return h * phi, phi + h * dens


def normed(value):
    centred = value - jnp.mean(value, axis=-1, keepdims=True)
    rs = lax.rsqrt(jnp.mean(centred * centred, axis=-1, keepdims=True) + 1e-06)
    return centred * rs, rs


def norm_back(dn, n_hat, rs, gain):
    gd = dn * gain
    return (
        gd
        - jnp.mean(gd, axis=-1, keepdims=True)
        - n_hat * jnp.mean(gd * n_hat, axis=-1, keepdims=True)
    ) * rs


def col_shift(value, by):
    if by == 0:
        return value
    at = lax.broadcasted_iota(jnp.int32, value.shape, 0) % SIDE
    rolled = pltpu.roll(value, (-by) % TOK, 0)
    return jnp.where((at + by >= 0) & (at + by < SIDE), rolled, 0.0)


def row_shift(value, by):
    if by == 0:
        return value
    gap = jnp.zeros((abs(by) * SIDE, value.shape[1]), value.dtype)
    if by > 0:
        return jnp.concatenate([value[by * SIDE :], gap], axis=0)
    return jnp.concatenate([gap, value[: TOK + by * SIDE]], axis=0)


def depthwise(value, tap, side):
    half = side // 2
    shifted = [col_shift(value, b - half) for b in range(side)]
    total = None
    for a in range(side):
        line = None
        for b in range(side):
            term = shifted[b] * tap(a * side + b)
            line = term if line is None else line + term
        line = row_shift(line, a - half)
        total = line if total is None else total + line
    return total


def depthwise_taps(value, grad, side, put):
    half = side // 2
    shifted = [col_shift(value, b - half) for b in range(side)]
    for a in range(side):
        d = a - half
        lo, hi = max(0, -d) * SIDE, (SIDE - max(0, d)) * SIDE
        for b in range(side):
            part = shifted[b][lo + d * SIDE : hi + d * SIDE] * grad[lo:hi]
            put(a * side + b, jnp.sum(part, axis=0, keepdims=True))


def lanes_of(at, width):
    return pl.ds(pl.multiple_of(at * width, width), width)


def side_by_side(blocks):
    return jnp.concatenate(blocks, axis=1)


def main_kernel(dims, outer, *refs):
    at = iter(refs)

    def take(count):
        return [next(at) for _ in range(count)]

    na = len(ARRAYS)
    source = dict(zip(ARRAYS, take(na)))
    (
        depth_in, ln_conv_in, scale_in, ln_attn_in, ln_mlp_in, adapt_depth_in,
        order_in, train_in, tok_in, grid_in, tcot_in, gcot_in,
    ) = take(12)
    hid_tok, hid_grid, out_gtok, out_ggrid = take(4)
    native = dict(zip(ARRAYS, take(na)))
    out_depth, out_ln_conv, out_scale, out_ln_attn, out_ln_mlp, out_ad = take(6)
    W = dict(zip(ARRAYS, take(na)))
    hops = take(4 * na)
    RX = {name: hops[4 * n : 4 * n + 4] for n, name in enumerate(ARRAYS)}
    (
        v_loc, vv, aq, vec_c, vec_d, x_in, c_in, n1_all, f_all, n2_all, c2_all,
        o_sb, o_rb, cv_sb, cv_rb, m_sb, m_rb, br_sb, br_rb, gsb, dgb,
        qkv, prob, ctx, u, up, r, rp, cn, crs, cv_sum, x1, c2f,
        adapted, spread, pooled, gate,
        dx3, dcot, dx3_all, dn2_sb, dn2_rb, dc2_sb, dc2_rb, dx1_all, dcv_all,
        dn1_sb, dn1_rb, df_sb, df_rb, dh, do_all, dqkv, dhc, dx1, dc2t, dad, dcn,
        gvs, gv_rb, gvx, gad, gad_rb, gad_all, turned,
    ) = take(65)
    (
        zs_send, zs_recv, s1_send, s1_recv, loc_sem, s2_send, s2_recv,
        v_send, v_recv, q_send, q_recv, h_send, h_recv, b_send, b_recv, c_send, c_recv,
        xo_send, xo_recv, g_send, g_recv, a_send, a_recv, gx_send, gx_recv, go,
    ) = take(26)

    p = lax.axis_index("pipe")
    dpi = lax.axis_index("dp")
    x = lax.axis_index("tensor")
    rest = dpi % outer
    zi = dpi // (outer * R)
    ri = (dpi // outer) % R
    xo = 1 - x
    ro = 1 - ri
    d_dim, c_dim, hq, ffq, cfq, adq, dg = dims
    adh = Z * adq
    dz, cz = d_dim // Z, c_dim // Z
    tile = 256
    ids = {name: number for number, name in enumerate(ARRAYS)}
    ev = {name: number for number, name in enumerate(EVENTS)}

    def dev(z=None, rr=None, xx=None, pp=None):
        z = zi if z is None else z
        rr = ri if rr is None else rr
        return (
            p if pp is None else pp,
            (z * R + rr) * outer + rest,
            x if xx is None else xx,
        )

    def zto(d):
        return lax.rem(zi + d, Z)

    def zfrom(d):
        return lax.rem(zi + Z - d, Z)

    def remote(src, dst, ssem, rsem, device):
        return pltpu.make_async_remote_copy(
            src_ref=src, dst_ref=dst, send_sem=ssem, recv_sem=rsem,
            device_id=device, device_id_type=pl.DeviceIdType.MESH,
        )

    sib = dev(pp=1 - p)
    over_r, over_x = dev(rr=ro), dev(xx=xo)

    def z_copy(e, d, src, dst):
        return remote(src, dst, zs_send.at[e, d - 1], zs_recv.at[e, d - 1], dev(zto(d)))

    sent = []

    def gather_copies(name, buf):
        return [z_copy(ev[name], d, buf.at[zi], buf.at[zi]) for d in range(1, Z)]

    def gather_start(name, buf, keep=True):
        copies = gather_copies(name, buf)
        for c in copies:
            c.start()
        if keep:
            sent.extend(copies)

    def gather_wait(name, buf):
        for d in range(1, Z):
            slot = buf.at[zfrom(d)]
            z_copy(ev[name], d, slot, slot).wait_recv()

    def scatter_start(name, sb, rb):
        for d in range(1, Z):
            c = z_copy(ev[name], d, sb.at[zto(d)], rb.at[d - 1])
            c.start()
            sent.append(c)

    def scatter_wait(name, rb):
        for d in range(1, Z):
            z_copy(ev[name], d, rb.at[d - 1], rb.at[d - 1]).wait_recv()

    def share_start(name, buf):
        for d in range(1, Z):
            c = z_copy(ev[name], d, buf.at[3], buf.at[d - 1])
            c.start()
            sent.append(c)

    def scattered(sb, rb):
        return (wide(sb[zi]) + wide(rb[0])) + (wide(rb[1]) + wide(rb[2]))

    barrier = pltpu.get_barrier_semaphore()
    greeted = [sib]
    for d in range(1, Z):
        greeted += [dev(zto(d)), dev(zto(d), ro), dev(zto(d), pp=1 - p)]
    greeted += [over_r, over_x, dev(rr=ro, xx=xo)]
    for device in greeted:
        pl.semaphore_signal(barrier, inc=1, device_id=device, device_id_type=pl.DeviceIdType.MESH)
    v_loc[...] = jnp.zeros(v_loc.shape, F32)
    taps7 = depth_in.shape[0]
    c_own = depth_in.shape[1]
    v_loc[0:taps7, 0:c_own] = wide(depth_in[...])
    v_loc[49:50, 0:c_own] = wide(ln_conv_in[...])
    v_loc[50:51, 0:c_own] = wide(scale_in[...])
    v_loc[56:57, 0:LANE] = wide(ln_attn_in[...])
    v_loc[57:58, 0:LANE] = wide(ln_mlp_in[...])
    aq[x] = jnp.zeros(aq.shape[1:], F32)
    aq[x, 0:9] = wide(adapt_depth_in[:, lanes_of(zi, adq)])
    pl.semaphore_wait(barrier, len(greeted))

    me8 = zi * R + ri
    v_arrivals = []
    for n, (d, flip) in enumerate([(d, s) for d in range(Z) for s in (0, 1)][1:]):
        tr = ro if flip else ri
        c = remote(v_loc, vv.at[me8], v_send.at[n], v_recv.at[n], dev(zto(d), tr))
        c.start()
        sent.append(c)
        fr = zfrom(d) * R + tr
        v_arrivals.append(remote(vv.at[fr], vv.at[fr], v_send.at[n], v_recv.at[n], dev(zto(d), tr)))
    vv[me8] = v_loc[...]
    c = remote(aq.at[x], aq.at[x], q_send, q_recv, over_x)
    c.start()
    sent.append(c)

    by_rows = ("O", "F2")

    def quarter_of(name, ref, z):
        if name == "Q":
            return ref.at[:, :, lanes_of(z, hq)]
        if name in by_rows:
            height = ref.shape[0] // Z
            return ref.at[pl.ds(pl.multiple_of(z * height, height), height)]
        return ref.at[:, lanes_of(z, ref.shape[1] // Z)]

    def step1_local(name):
        return pltpu.make_async_copy(
            quarter_of(name, source[name], zi), W[name].at[x, zi, ri], loc_sem.at[ids[name]]
        )

    def step1_copy(name, d):
        k = ids[name]
        return remote(
            quarter_of(name, source[name], zto(d)), W[name].at[x, zi, ri],
            s1_send.at[k, d - 1], s1_recv.at[k, d - 1], dev(zto(d)),
        )

    def half_of(name, j, z, rr, upper):
        w = W[name]
        half = w.shape[-2] // 2
        rows = slice(half, None) if upper else slice(0, half)
        if len(w.shape) == 6:
            return w.at[j, z, rr, :, rows]
        return w.at[j, z, rr, rows]

    def step2_copy(name, which, d):
        k = ids[name]
        z = zfrom(d)
        if which < 2:
            src = quarter_of(name, source[name], zi) if d == 0 else W[name].at[x, z, ri]
            dst = W[name].at[x, z, ri]
        else:
            src = dst = half_of(name, x, z, ro, False) if which == 2 else half_of(name, xo, z, ri, True)
        to = over_x if which in (1, 2) else over_r
        return remote(src, dst, s2_send.at[k, which, d], s2_recv.at[k, which, d], to)

    def step2_arrival(name, which, d):
        k = ids[name]
        z = zfrom(d)
        if which < 2:
            ref = W[name].at[x, z, ro] if which == 0 else W[name].at[xo, z, ri]
        else:
            ref = half_of(name, xo, z, ro, which == 3)
        to = over_x if which in (1, 2) else over_r
        return remote(ref, ref, s2_send.at[k, which, d], s2_recv.at[k, which, d], to)

    def relay1(*names):
        for name in names:
            step1_local(name).start()
            for d in range(1, Z):
                step1_copy(name, d).start()
            step2_copy(name, 0, 0).start()
            step2_copy(name, 1, 0).start()

    def relay2(name, ds=(1, 2, 3)):
        k = ids[name]
        for d in ds:
            slot = W[name].at[x, zfrom(d), ri]
            remote(slot, slot, s1_send.at[k, d - 1], s1_recv.at[k, d - 1], dev(zto(d))).wait_recv()
            step2_copy(name, 0, d).start()
            step2_copy(name, 1, d).start()

    def relay3(name, ds=(0, 1, 2, 3)):
        for d in ds:
            step2_arrival(name, 0, d).wait_recv()
            step2_copy(name, 2, d).start()
            step2_arrival(name, 1, d).wait_recv()
            step2_copy(name, 3, d).start()

    def relay4(*names):
        for name in names:
            step1_local(name).wait()
            for d in range(Z):
                step2_arrival(name, 2, d).wait_recv()
                step2_arrival(name, 3, d).wait_recv()

    def relay_sent():
        for name in ARRAYS:
            for d in range(1, Z):
                step1_copy(name, d).wait_send()
            for which in range(4):
                for d in range(Z):
                    step2_copy(name, which, d).wait_send()

    @pl.when(p == 0)
    def _():
        relay1("P1", "P2")

    @pl.when(p == 1)
    def _():
        dx3[...] = tcot_in[x]
        dcot[...] = gcot_in[x]
        dx3_all[zi] = tcot_in[x]
        gather_start("dx3", dx3_all, keep=False)

    for c in v_arrivals:
        c.wait_recv()
    remote(aq.at[xo], aq.at[xo], q_send, q_recv, over_x).wait_recv()
    low_lanes = lax.broadcasted_iota(jnp.int32, (64, LANE), 1) < LANE // 2
    for z in range(Z):
        first, second = vv[2 * z], pltpu.roll(vv[2 * z + 1], LANE // 2, 1)
        vec_c[:, z * cz : z * cz + LANE] = first[:, 0:LANE]
        vec_c[:, z * cz + LANE : z * cz + 2 * LANE] = jnp.where(
            low_lanes, first[:, LANE:], second[:, 0:LANE]
        )
        vec_c[:, z * cz + 2 * LANE : (z + 1) * cz] = second[:, LANE:]
    for i in range(Z * R):
        vec_d[:, i * LANE : (i + 1) * LANE] = vv[i, 56:64, 0:LANE]

    def gain_d(row):
        return vec_d[row : row + 1, :]

    def gain_c(row):
        return vec_c[row : row + 1, :]

    def token_entry():
        n_hat, _ = normed(wide(x_in[...]))
        n1_all[zi] = low(n_hat * gain_d(0))
        gather_start("n1", n1_all, keep=False)

    def conv_entry():
        @pl.loop(0, c_dim // LANE)
        def _(ch):
            lanes = lanes_of(ch, LANE)
            taps = vec_c[:, lanes]
            cn[:, lanes] = depthwise(wide(c_in[:, lanes]), lambda k: taps[k : k + 1], 7)

        n_hat, rs = normed(cn[...])
        cn[...] = n_hat
        crs[...] = jnp.broadcast_to(rs, crs.shape)
        f_all[zi] = low(n_hat * gain_c(49))
        gather_start("f", f_all, keep=False)

    def first_relays():
        relay2("P1")
        relay1("Q", "O")
        relay2("P2")
        relay3("P1")

    sent.extend(gather_copies("n1", n1_all))
    sent.extend(gather_copies("f", f_all))

    @pl.when(p == 0)
    def _():
        first = order_in[0, x] == 0
        c_in[...] = jnp.where(first, grid_in[0], grid_in[1])
        x_in[...] = jnp.where(first, tok_in[0], tok_in[1])
        conv_entry()
        token_entry()
        first_relays()

    @pl.when(p == 1)
    def _():
        pl.semaphore_wait(go, 1)
        relay1("P1", "P2")
        first_relays()
        remote(c_in, c_in, h_send.at[1], h_recv.at[1], sib).wait_recv()
        conv_entry()

    relay2("Q")
    relay2("O")
    relay1("E", "Gi", "Go")
    relay3("P2", (0, 1))
    relay4("P1")
    gather_wait("f", f_all)

    def conv_hidden(j):
        @pl.loop(0, cfq // tile)
        def _(t):
            lanes = lanes_of(t, tile)
            act, der = gelu_pair(mm(flat(f_all[...]), flat(W["P1"][j, :, :, :, lanes])))
            r[j, :, lanes] = low(act)
            rp[j, :, lanes] = low(der)

    conv_hidden(0)

    relay3("P2", (2, 3))
    for name in ("E", "Gi", "Go"):
        relay2(name)
    relay1("F1")
    conv_hidden(1)
    relay3("Q")
    relay3("O")
    relay2("F1")
    relay1("F2")

    relay4("P2")

    @pl.loop(0, Z)
    def _(z):
        acc = mm_nt(r[0], flat(W["P2"][0, z])) + mm_nt(r[1], flat(W["P2"][1, z]))
        cv_sb[:, :, lanes_of(z, cz)] = low(acc).reshape(Z, TOK, cz)

    scatter_start("cv", cv_sb, cv_rb)

    for name in ("E", "Gi", "Go"):
        relay3(name)
    relay2("F2")

    @pl.when(p == 0)
    def _():
        pl.semaphore_signal(go, inc=1, device_id=sib, device_id_type=pl.DeviceIdType.MESH)

    @pl.when(p == 1)
    def _():
        remote(x_in, x_in, h_send.at[0], h_recv.at[0], sib).wait_recv()
        token_entry()

    relay4("Q", "O")
    gather_wait("n1", n1_all)
    for j in range(2):
        wj = side_by_side([flat(W["Q"][j, :, :, s]) for s in range(3)])
        qkv[j] = low(mm(flat(n1_all[...]), wj))
    for j in range(2):
        for b in range(Z):
            rows = slice(b * TOK, (b + 1) * TOK)
            outs = []
            for h in range(hq // HD):
                q, kk, vals = (qkv[j, rows, s * hq + h * HD : s * hq + (h + 1) * HD] for s in range(3))
                sc = mm_nt(q, kk) * HD ** (-0.5)
                e = jnp.exp(sc - jnp.max(sc, axis=-1, keepdims=True))
                pr = low(e / jnp.sum(e, axis=-1, keepdims=True))
                prob[j, h, b] = pr
                outs.append(mm(pr, vals))
            ctx[j, rows, :] = low(side_by_side(outs))

    def out_block(j, z):
        return side_by_side([W["O"][j, z, 0], W["O"][j, z, 1]])

    @pl.loop(0, Z)
    def _(z):
        both = jnp.concatenate([out_block(0, z), out_block(1, z)], axis=0)
        acc = mm(side_by_side([ctx[0], ctx[1]]), both)
        o_sb[:, :, lanes_of(z, dz)] = low(acc).reshape(Z, TOK, dz)

    scatter_start("o", o_sb, o_rb)

    relay3("F1")

    scatter_wait("cv", cv_rb)
    cv_sum[...] = scattered(cv_sb, cv_rb)
    c2f[...] = wide(c_in[...]) + gain_c(50) * cv_sum[...]
    c2_low = low(c2f[...])
    c2_all[zi] = c2_low
    gather_start("c2", c2_all)
    hid_grid[x] = c2_low

    @pl.when(p == 0)
    def _():
        remote(hid_grid.at[x], c_in, h_send.at[1], h_recv.at[1], sib).start()

    relay3("F2")
    scatter_wait("o", o_rb)
    x1[...] = wide(x_in[...]) + scattered(o_sb, o_rb)
    n_hat, _ = normed(x1[...])
    n2_all[zi] = low(n_hat * gain_d(1))
    gather_start("n2", n2_all)

    relay4("E", "Gi", "Go")
    gather_wait("c2", c2_all)
    row8 = lax.broadcasted_iota(jnp.int32, (8, adq), 0)
    gs_part = None
    for j in range(2):
        ad = mm(flat(c2_all[...]), flat(W["E"][j]))
        adapted[j] = ad
        taps = aq[j]
        pool = jnp.zeros((8, adq), F32)
        for b in range(Z):
            sp = depthwise(ad[b * TOK : (b + 1) * TOK], lambda k: taps[k : k + 1], 3)
            spread[j, b] = sp
            pool = jnp.where(row8 == b, jnp.mean(sp, axis=0, keepdims=True), pool)
        pooled[j] = pool
        term = mm_nt(low(pool), flat(W["Gi"][j]))
        gs_part = term if gs_part is None else gs_part + term
    gsb[3] = gs_part
    share_start("gs", gsb)

    relay4("F1")
    gather_wait("n2", n2_all)
    for j in range(2):

        @pl.loop(0, ffq // tile)
        def _(t):
            lanes = lanes_of(t, tile)
            act, der = gelu_pair(mm(flat(n2_all[...]), flat(W["F1"][j, :, :, :, lanes])))
            u[j, :, lanes] = low(act)
            up[j, :, lanes] = low(der)

    scatter_wait("gs", gsb)

    def gate_hidden():
        return gelu_pair((gsb[0] + gsb[1]) + (gsb[2] + gsb[3]))

    gh, _ = gate_hidden()
    for j in range(2):
        g8 = jnp.tanh(mm(low(gh), flat(W["Go"][j])))
        gate[j] = g8
        for b in range(Z):
            br_sb[b, :, j * adq : (j + 1) * adq] = low(g8[b : b + 1] * spread[j, b])
    scatter_start("br", br_sb, br_rb)
    relay4("F2")

    @pl.loop(0, Z)
    def _(z):
        acc = None
        for j in range(2):
            term = mm(u[j], side_by_side([W["F2"][j, z, 0], W["F2"][j, z, 1]]))
            acc = term if acc is None else acc + term
        m_sb[:, :, lanes_of(z, dz)] = low(acc).reshape(Z, TOK, dz)

    scatter_start("m", m_sb, m_rb)

    def exchange(n, buf):
        remote(buf.at[x], buf.at[x], xo_send.at[n], xo_recv.at[n], over_x).start()

    def layer_output(total):
        scatter_wait("br", br_rb)
        total[...] = x1[...]
        for d in range(Z):
            piece = br_sb[zi] if d == 0 else br_rb[d - 1]
            for j in range(2):
                lanes = pl.ds(pl.multiple_of(j * adh + zfrom(d) * adq, LANE), adq)
                total[:, lanes] += wide(piece[:, j * adq : (j + 1) * adq])
        scatter_wait("m", m_rb)
        hid_tok[x] = low(total[...] + scattered(m_sb, m_rb))

    @pl.when(p == 0)
    def _():
        layer_output(dx1)
        remote(hid_tok.at[x], x_in, h_send.at[0], h_recv.at[0], sib).start()
        exchange(0, hid_tok)

    exchange(1, hid_grid)
    relay_sent()

    def over_cores(d):
        return remote(
            out_gtok.at[x], dx3_all.at[zi], b_send.at[d], b_recv.at[d], dev(zto(d), pp=1 - p)
        )

    @pl.when(p == 1)
    def _():
        gather_wait("dx3", dx3_all)
        for c in gather_copies("dx3", dx3_all):
            c.wait_send()

    @pl.when(p == 0)
    def _():
        for d in range(Z):
            slot = dx3_all.at[zfrom(d)]
            remote(slot, slot, b_send.at[d], b_recv.at[d], sib).wait_recv()
        dx3[...] = dx3_all[zi]

    def own_lanes(j):
        return pl.ds(pl.multiple_of(j * adh + zi * adq, LANE), adq)

    gh, ghp = gate_hidden()
    dgh_part = None
    dgp = []
    for j in range(2):
        dgate = jnp.zeros((8, adq), F32)
        for b in range(Z):
            dbr = wide(dx3_all[b, :, own_lanes(j)])
            dgate = jnp.where(row8 == b, jnp.sum(dbr * spread[j, b], axis=0, keepdims=True), dgate)
        dg8 = low(dgate * (1.0 - gate[j] * gate[j]))
        dgp.append(dg8)
        term = mm_nt(dg8, flat(W["Go"][j]))
        dgh_part = term if dgh_part is None else dgh_part + term
    dgb[3] = dgh_part
    share_start("dgh", dgb)

    for j in range(2):

        @pl.loop(0, ffq // tile)
        def _(t):
            rows = lanes_of(t, tile)
            both = side_by_side([W["F2"][j, z, rr, rows] for z in range(Z) for rr in range(R)])
            du = mm_nt(flat(dx3_all[...]), both)
            dh[j, :, rows] = low(du * wide(up[j, :, rows]))

    scatter_wait("dgh", dgb)
    dgs = low(((dgb[0] + dgb[1]) + (dgb[2] + dgb[3])) * ghp)
    for j in range(2):
        dpool = mm(dgs, flat(W["Gi"][j])) * (1.0 / TOK)
        taps = aq[j]
        tap_rows = [None] * 9
        for b in range(Z):
            dsp = gate[j, b : b + 1] * wide(dx3_all[b, :, own_lanes(j)]) + dpool[b : b + 1]
            dad[j, b * TOK : (b + 1) * TOK] = low(depthwise(dsp, lambda k: taps[8 - k : 9 - k], 3))

            def put(k, row):
                tap_rows[k] = row if tap_rows[k] is None else tap_rows[k] + row

            depthwise_taps(adapted[j, b * TOK : (b + 1) * TOK], dsp, 3, put)
        for k in range(9):
            gad[j, k : k + 1] = tap_rows[k]
        gad[j, 9:16] = jnp.zeros((7, adq), F32)

    @pl.loop(0, Z)
    def _(z):
        acc = mm_nt(dad[0], flat(W["E"][0, z])) + mm_nt(dad[1], flat(W["E"][1, z]))
        dc2_sb[:, :, lanes_of(z, cz)] = low(acc).reshape(Z, TOK, cz)

    scatter_start("dc2", dc2_sb, dc2_rb)

    @pl.loop(0, Z)
    def _(z):
        acc = mm_nt(dh[0], flat(W["F1"][0, z])) + mm_nt(dh[1], flat(W["F1"][1, z]))
        dn2_sb[:, :, lanes_of(z, dz)] = low(acc).reshape(Z, TOK, dz)

    scatter_start("dn2", dn2_sb, dn2_rb)

    def half_rows(name, upper):
        half = W[name].shape[-2] // 2
        rows = slice(half, None) if upper else slice(0, half)
        return (slice(None), rows) if len(W[name].shape) == 6 else (rows,)

    fine = ("P1", "P2", "F1", "F2")

    def pieces(name):
        return (1, 2, 3, 0) if name in fine else (None,)

    def block_at(d):
        return slice(None) if d is None else zto(d)

    def hop_copy(name, which, d):
        n = ids[name]
        lower, upper = half_rows(name, False), half_rows(name, True)
        z = block_at(d)
        w, buf = W[name], RX[name]
        src, dst, to = (
            lambda: (w.at[(xo, z, slice(None)) + lower], buf[0].at[z], over_x),
            lambda: (w.at[(slice(None), z, ro) + upper], buf[1].at[:, z], over_r),
            lambda: (buf[0].at[z, ro], buf[2].at[z], over_r),
            lambda: (buf[1].at[xo, z], buf[3].at[z], over_x),
        )[which]()
        k = 0 if d is None else d
        return remote(src, dst, g_send.at[n, which, k], g_recv.at[n, which, k], to)

    def reduce_start(name, d=None):
        hop_copy(name, 0, d).start()
        hop_copy(name, 1, d).start()

    def each_block(d, body):
        if d is None:
            pl.loop(0, Z)(body)
        else:
            body(zto(d))

    def reduce_middle(*names):
        for name in names:
            lower, upper = half_rows(name, False), half_rows(name, True)
            buf = RX[name]
            for d in pieces(name):
                hop_copy(name, 0, d).wait_recv()

                def add_lower(z):
                    for rr in range(R):
                        own = W[name][(x, z, rr) + lower]
                        buf[0][z, rr] = low(wide(own) + wide(buf[0][z, rr]))

                each_block(d, add_lower)
                hop_copy(name, 2, d).start()
                hop_copy(name, 1, d).wait_recv()

                def add_upper(z):
                    for j in range(2):
                        own = W[name][(j, z, ri) + upper]
                        buf[1][j, z] = low(wide(own) + wide(buf[1][j, z]))

                each_block(d, add_upper)
                hop_copy(name, 3, d).start()

    def reduce_end(*names):
        for name in names:
            lower, upper = half_rows(name, False), half_rows(name, True)
            buf = RX[name]
            for d in pieces(name):
                hop_copy(name, 2, d).wait_recv()
                hop_copy(name, 3, d).wait_recv()

                def add_both(z):
                    W[name][(x, z, ri) + lower] = low(wide(buf[0][z, ri]) + wide(buf[2][z]))
                    W[name][(x, z, ri) + upper] = low(wide(buf[1][x, z]) + wide(buf[3][z]))

                each_block(d, add_both)
                for k in range(Z) if d is None else (d,):
                    (back_copy(name, k) if k else back_local(name)).start()

    def back_copy(name, d):
        n = ids[name]
        return remote(
            W[name].at[x, zto(d), ri], quarter_of(name, native[name], zi),
            a_send.at[n, d - 1], a_recv.at[n, d - 1], dev(zto(d)),
        )

    def back_local(name):
        return pltpu.make_async_copy(
            W[name].at[x, zi, ri], quarter_of(name, native[name], zi), loc_sem.at[ids[name]]
        )

    peers = ((1, 0), (0, 1), (1, 1))

    def owner(k):
        return (ro if peers[k][0] else ri), (xo if peers[k][1] else x)

    def row_grad(name, left, right):
        width = W[name].shape[3]
        span = R * width
        for k, d in enumerate((1, 2, 3, 0)):
            z = zto(d)
            half = (k % 2) * span
            turned[half : half + span] = flat(left[:, :, lanes_of(z, span)]).T
            for j in range(2):
                W[name][j, z] = low(mm(turned[half : half + span], right[j])).reshape(R, width, -1)
            if name in fine:
                reduce_start(name, d)
        if name not in fine:
            reduce_start(name)

    def col_grad(name, left, right):
        width = left.shape[2]
        for j in range(2):
            turned[j * width : (j + 1) * width] = left[j].T
        for d in (1, 2, 3, 0):
            z = zto(d)
            rhs = flat(right[:, :, lanes_of(z, dz)])
            for j in range(2):
                g = low(mm(turned[j * width : (j + 1) * width], rhs))
                for rr in range(R):
                    W[name][j, z, rr] = g[:, rr * LANE : (rr + 1) * LANE]
            if name in fine:
                reduce_start(name, d)
        if name not in fine:
            reduce_start(name)

    for j in range(2):
        W["Gi"][j] = low(mm_tn(dgs, low(pooled[j]))).reshape(Z, R, -1, adq)
        W["Go"][j] = low(mm_tn(low(gh), dgp[j])).reshape(Z, R, -1, adq)
    reduce_start("Gi")
    reduce_start("Go")
    row_grad("E", c2_all, dad)

    @pl.when(p == 0)
    def _():
        remote(dcot, dcot, c_send, c_recv, sib).wait_recv()

    scatter_wait("dc2", dc2_rb)
    dc2t[...] = wide(dcot[...]) + scattered(dc2_sb, dc2_rb)
    gvs_ls = jnp.sum(cv_sum[...] * dc2t[...], axis=0, keepdims=True)
    dcv_all[zi] = low(dc2t[...] * gain_c(50))
    gather_start("dcv", dcv_all)

    scatter_wait("dn2", dn2_rb)
    dn2 = scattered(dn2_sb, dn2_rb)
    n_hat, rs = normed(x1[...])
    gvs_d1 = jnp.sum(dn2 * n_hat, axis=0, keepdims=True)
    dx1[...] = wide(dx3[...]) + norm_back(dn2, n_hat, rs, gain_d(1))
    dx1_all[zi] = low(dx1[...])
    gather_start("dx1", dx1_all)

    col_grad("F2", u, dx3_all)
    row_grad("F1", n2_all, dh)

    gather_wait("dcv", dcv_all)
    for j in range(2):

        @pl.loop(0, cfq // tile)
        def _(t):
            lanes = lanes_of(t, tile)
            dr = mm(flat(dcv_all[...]), flat(W["P2"][j, :, :, :, lanes]))
            dhc[j, :, lanes] = low(dr * wide(rp[j, :, lanes]))

    @pl.loop(0, Z)
    def _(z):
        acc = mm_nt(dhc[0], flat(W["P1"][0, z])) + mm_nt(dhc[1], flat(W["P1"][1, z]))
        df_sb[:, :, lanes_of(z, cz)] = low(acc).reshape(Z, TOK, cz)

    scatter_start("df", df_sb, df_rb)

    early = ("Gi", "Go", "E", "F2", "F1")

    def pw_grads():
        row_grad("P2", dcv_all, r)
        row_grad("P1", f_all, dhc)

    @pl.when(p == 0)
    def _():
        pw_grads()

    gather_wait("dx1", dx1_all)
    for j in range(2):
        both = side_by_side([W["O"][j, z, rr] for z in range(Z) for rr in range(R)])
        do_all[j] = low(mm_nt(flat(dx1_all[...]), both))
    for j in range(2):
        for b in range(Z):
            rows = slice(b * TOK, (b + 1) * TOK)
            parts = [[], [], []]
            for h in range(hq // HD):
                q, kk, vals = (qkv[j, rows, s * hq + h * HD : s * hq + (h + 1) * HD] for s in range(3))
                do = do_all[j, rows, h * HD : (h + 1) * HD]
                pr = prob[j, h, b]
                dp = mm_nt(do, vals)
                prw = wide(pr)
                ds = low(prw * (dp - jnp.sum(dp * prw, axis=-1, keepdims=True)) * HD ** (-0.5))
                parts[0].append(mm(ds, kk))
                parts[1].append(mm_tn(ds, q))
                parts[2].append(mm_tn(pr, do))
            for s in range(3):
                dqkv[j, rows, s * hq : (s + 1) * hq] = low(side_by_side(parts[s]))

    @pl.loop(0, Z)
    def _(z):
        acc = None
        for j in range(2):
            term = mm_nt(dqkv[j], side_by_side([flat(W["Q"][j, z, :, s]) for s in range(3)]))
            acc = term if acc is None else acc + term
        dn1_sb[:, :, lanes_of(z, dz)] = low(acc).reshape(Z, TOK, dz)

    scatter_start("dn1", dn1_sb, dn1_rb)

    def attention_grads():
        @pl.loop(0, Z)
        def _(z):
            turned[0:dz] = flat(n1_all[:, :, lanes_of(z, dz)]).T
            for j in range(2):
                g = low(mm(turned[0:dz], dqkv[j]))
                for s in range(3):
                    W["Q"][j, z, :, s] = g[:, s * hq : (s + 1) * hq].reshape(R, -1, hq)

        reduce_start("Q")
        col_grad("O", ctx, dx1_all)

    reduce_middle(*early)

    @pl.when(p == 0)
    def _():
        reduce_middle("P2")
        attention_grads()
        reduce_middle("P1")
        reduce_end(*early)

    scatter_wait("dn1", dn1_rb)
    dn1 = scattered(dn1_sb, dn1_rb)
    n_hat, rs = normed(wide(x_in[...]))
    gvs_d0 = jnp.sum(dn1 * n_hat, axis=0, keepdims=True)
    out_gtok[x] = low(dx1[...] + norm_back(dn1, n_hat, rs, gain_d(0)))

    @pl.when(p == 1)
    def _():
        for d in (1, 2, 3, 0):
            over_cores(d).start()

    scatter_wait("df", df_rb)
    dfv = scattered(df_sb, df_rb)
    gvs_lc = jnp.sum(dfv * cn[...], axis=0, keepdims=True)
    dcn[...] = norm_back(dfv, cn[...], crs[:, 0:1], gain_c(49))

    @pl.loop(0, c_dim // LANE)
    def _(ch):
        lanes = lanes_of(ch, LANE)
        taps = vec_c[:, lanes]
        back = depthwise(dcn[:, lanes], lambda k: taps[48 - k : 49 - k], 7)
        out_ggrid[x, :, lanes] = low(dc2t[:, lanes] + back)

    @pl.when(p == 1)
    def _():
        remote(out_ggrid.at[x], dcot, c_send, c_recv, sib).start()
        pw_grads()
        attention_grads()
        layer_output(dx1)
        exchange(0, hid_tok)
        reduce_end(*early)

    @pl.when(p == 0)
    def _():
        reduce_end("P2")

    exchange(2, out_gtok)
    exchange(3, out_ggrid)

    @pl.loop(0, Z)
    def _(z):
        for part in range(cz // LANE):
            lanes = pl.ds(pl.multiple_of(z * cz + part * LANE, LANE), LANE)

            def put(k, row):
                gvs[z, k : k + 1, part * LANE : (part + 1) * LANE] = row

            depthwise_taps(wide(c_in[:, lanes]), dcn[:, lanes], 7, put)

    for z in range(Z):
        gvs[z, 49:50] = gvs_lc[:, z * cz : (z + 1) * cz]
        gvs[z, 50:51] = gvs_ls[:, z * cz : (z + 1) * cz]
        gvs[z, 51:64] = jnp.zeros((13, cz), F32)
        gvs[z, 56:57, 0:dz] = gvs_d0[:, z * dz : (z + 1) * dz]
        gvs[z, 57:58, 0:dz] = gvs_d1[:, z * dz : (z + 1) * dz]
    scatter_start("gv", gvs, gv_rb)

    def group_copy(n, k, src, dst):
        rr, xx = owner(k)
        return remote(src, dst, gx_send.at[n, k], gx_recv.at[n, k], dev(rr=rr, xx=xx))

    for k in range(3):
        c = group_copy(1, k, gad, gad_rb.at[k])
        c.start()
        sent.append(c)
    @pl.when(p == 1)
    def _():
        reduce_middle("P2", "P1")
        reduce_end("P2")

    reduce_end("P1")
    scatter_wait("gv", gv_rb)
    gvx[3] = (gvs[zi] + gv_rb[0]) + (gv_rb[1] + gv_rb[2])
    for k in range(3):
        c = group_copy(0, k, gvx.at[3], gvx.at[k])
        c.start()
        sent.append(c)
    for k in range(3):
        group_copy(1, k, gad, gad_rb.at[k]).wait_recv()
    gad_all[zi] = (gad[x] + gad_rb[0, x]) + (gad_rb[1, x] + gad_rb[2, x])
    gather_start("gad", gad_all)

    reduce_middle("Q", "O")
    reduce_end("Q", "O")

    for k in range(3):
        group_copy(0, k, gvx.at[k], gvx.at[k]).wait_recv()
    total = (gvx[0] + gvx[1]) + (gvx[2] + gvx[3])
    mine = jnp.where(ri == 1, pltpu.roll(total, c_own, 1), total)[:, 0:c_own]
    mine_d = jnp.where(ri == 1, total[:, LANE : 2 * LANE], total[:, 0:LANE])

    def flag(n):
        return train_in[0, n].astype(F32)

    out_depth[...] = mine[0:taps7] * flag(0)
    out_ln_conv[...] = mine[49:50] * flag(1)
    out_scale[...] = mine[50:51] * flag(4)
    out_ln_attn[...] = mine_d[56:57]
    out_ln_mlp[...] = mine_d[57:58]
    gather_wait("gad", gad_all)
    for z in range(Z):
        out_ad[:, z * adq : (z + 1) * adq] = gad_all[z][0:9]
    for name in ARRAYS:
        back_local(name).wait()
        for d in range(1, Z):
            n = ids[name]
            slot = quarter_of(name, native[name], zfrom(d))
            remote(slot, slot, a_send.at[n, d - 1], a_recv.at[n, d - 1], dev(zto(d))).wait_recv()
    for n, buf in enumerate((hid_tok, hid_grid, out_gtok, out_ggrid)):
        c = remote(buf.at[x], buf.at[x], xo_send.at[n], xo_recv.at[n], over_x)
        c.wait_send()
        remote(buf.at[xo], buf.at[xo], xo_send.at[n], xo_recv.at[n], over_x).wait_recv()

    @pl.when(p == 0)
    def _():
        remote(hid_tok.at[x], x_in, h_send.at[0], h_recv.at[0], sib).wait_send()
        remote(hid_grid.at[x], c_in, h_send.at[1], h_recv.at[1], sib).wait_send()

    @pl.when(p == 1)
    def _():
        for d in range(Z):
            over_cores(d).wait_send()
        remote(out_ggrid.at[x], dcot, c_send, c_recv, sib).wait_send()

    for c in sent:
        c.wait_send()
    for name in ARRAYS:
        for which in range(4):
            for d in pieces(name):
                hop_copy(name, which, d).wait_send()
        for d in range(1, Z):
            back_copy(name, d).wait_send()


def run_layers(weights, vectors, order, train, streams, sizes, outer):
    d_dim, c_dim, hq, ffq, cfq, adw, dg = sizes
    vm = pltpu.VMEM
    blocks = []
    for name, value in zip(ARRAYS, weights):
        if name == "Q":
            blocks.append((3, value.shape[1], hq))
        elif name in ("O", "F2"):
            blocks.append((value.shape[0] // Z, value.shape[1]))
        else:
            blocks.append((value.shape[0], value.shape[1] // Z))
    rows = Z * TOK

    def act(width, count=Z, kind=BF):
        return vm((count, TOK, width), kind)

    scratch = [vm((2, Z, R) + s, BF) for s in blocks] + [
        vm(lead + s[:-2] + (s[-2] // 2, s[-1]), BF)
        for s in blocks
        for lead in ((Z, R), (2, Z), (Z,), (Z,))
    ]
    scratch += [
        vm((64, 2 * LANE), F32), vm((Z * R, 64, 2 * LANE), F32), vm((2, 16, adw), F32), vm((64, c_dim), F32), vm((8, d_dim), F32),
        vm((TOK, d_dim), BF), vm((TOK, c_dim), BF), act(d_dim), act(c_dim), act(d_dim), act(c_dim),
        act(d_dim), act(d_dim, 3), act(c_dim), act(c_dim, 3), act(d_dim), act(d_dim, 3),
        act(2 * adw), act(2 * adw, 3), vm((4, 8, dg), F32), vm((4, 8, dg), F32),
        vm((2, rows, 3 * hq), BF), vm((2, hq // HD, Z, TOK, TOK), BF), vm((2, rows, hq), BF),
        vm((2, rows, ffq), BF), vm((2, rows, ffq), BF), vm((2, rows, cfq), BF), vm((2, rows, cfq), BF),
        vm((TOK, c_dim), F32), vm((TOK, LANE), F32), vm((TOK, c_dim), F32), vm((TOK, d_dim), F32), vm((TOK, c_dim), F32),
        vm((2, rows, adw), F32), vm((2, Z, TOK, adw), F32), vm((2, 8, adw), F32), vm((2, 8, adw), F32),
        vm((TOK, d_dim), BF), vm((TOK, c_dim), BF), act(d_dim), act(d_dim), act(d_dim, 3), act(c_dim), act(c_dim, 3),
        act(d_dim), act(c_dim),
        act(d_dim), act(d_dim, 3), act(c_dim), act(c_dim, 3), vm((2, rows, ffq), BF), vm((2, rows, hq), BF),
        vm((2, rows, 3 * hq), BF), vm((2, rows, cfq), BF), vm((TOK, d_dim), F32), vm((TOK, c_dim), F32), vm((2, rows, adw), BF),
        vm((TOK, c_dim), F32),
        vm((Z, 64, c_dim // Z), F32), vm((3, 64, c_dim // Z), F32), vm((4, 64, c_dim // Z), F32),
        vm((2, 16, adw), F32), vm((3, 2, 16, adw), F32), vm((Z, 16, adw), F32),
        vm((2 * ffq, rows), BF),
    ]
    dma = pltpu.SemaphoreType.DMA
    na = len(ARRAYS)
    scratch += [
        dma((len(EVENTS), 3)), dma((len(EVENTS), 3)), dma((na, 3)), dma((na, 3)), dma((na,)),
        dma((na, 4, Z)), dma((na, 4, Z)), dma((7,)), dma((7,)), dma, dma, dma((2,)), dma((2,)), dma((Z,)), dma((Z,)), dma, dma,
        dma((4,)), dma((4,)), dma((na, 4, Z)), dma((na, 4, Z)), dma((na, 3)), dma((na, 3)), dma((2, 3)), dma((2, 3)),
        pltpu.SemaphoreType.REGULAR,
    ]
    sds = jax.ShapeDtypeStruct
    out_shape = [sds((2, TOK, d_dim), BF), sds((2, TOK, c_dim), BF)] * 2
    out_shape += [sds(value.shape, BF) for value in weights]
    out_shape += [sds(value.shape, F32) for value in vectors]
    any_spec = pl.BlockSpec(memory_space=pl.ANY)
    vm_spec = pl.BlockSpec(memory_space=pltpu.VMEM)
    sm_spec = pl.BlockSpec(memory_space=pltpu.SMEM)
    return pl.pallas_call(
        functools.partial(main_kernel, sizes, outer),
        out_shape=out_shape,
        in_specs=[any_spec] * na + [vm_spec] * 6 + [sm_spec] * 2 + [vm_spec] * 4,
        out_specs=[vm_spec] * 4 + [any_spec] * na + [vm_spec] * 6,
        scratch_shapes=scratch,
        compiler_params=pltpu.CompilerParams(
            collective_id=0, has_side_effects=True, vmem_limit_bytes=62 * 1024 * 1024
        ),
        cost_estimate=pl.CostEstimate(flops=26 * 10**9, bytes_accessed=10**8, transcendentals=10**7),
        name="layers",
    )(*weights, *vectors, order, train, *streams)


def per_device(
    tokens,
    conv_grid,
    order,
    trainable,
    ln_attn,
    w_qkv,
    w_attn_out,
    ln_mlp,
    w_fc_in,
    w_fc_out,
    conv_depth,
    ln_conv,
    w_pw_in,
    w_pw_out,
    layer_scale,
    w_adapt,
    adapt_depth,
    w_gate_in,
    w_gate_out,
    tok_cot,
    grid_cot,
):
    dp_count = lax.axis_size("dp")
    outer = dp_count // (Z * R)
    groups = [[g * outer + o for o in range(outer)] for g in range(Z * R)]
    layer_at = lax.axis_index("pipe")

    def block(value, axis):
        value = value[0]
        if outer == 1:
            return value
        return lax.all_gather(value, "dp", axis=axis, tiled=True, axis_index_groups=groups)

    def share(value, axis):
        if outer > 1:
            value = lax.psum_scatter(
                value, "dp", scatter_dimension=axis, tiled=True, axis_index_groups=groups
            )
        return value[None]

    qkv = block(w_qkv, 1)
    gate_in = block(w_gate_in, 1).T
    pw_in = block(w_pw_in, 0)
    adapt = block(w_adapt, 0)
    fc_in = block(w_fc_in, 0)
    weights = (
        pw_in,
        block(w_pw_out, 1).T,
        qkv,
        block(w_attn_out, 1),
        adapt,
        gate_in,
        block(w_gate_out, 0),
        fc_in,
        block(w_fc_out, 1),
    )
    vectors = (
        block(conv_depth, 1),
        block(ln_conv, 0)[None],
        block(layer_scale, 0)[None],
        block(ln_attn, 0)[None],
        block(ln_mlp, 0)[None],
        adapt_depth[0],
    )
    spread = Z * R
    sizes = (
        qkv.shape[1] * spread, pw_in.shape[0] * spread, qkv.shape[2] // Z, fc_in.shape[1] // Z,
        pw_in.shape[1] // Z, adapt.shape[1] // Z, gate_in.shape[0] * spread,
    )

    def rows_of(value):
        return value.reshape(value.shape[0], TOK, value.shape[-1])

    streams = [rows_of(value) for value in (tokens, conv_grid, tok_cot, grid_cot)]
    outs = run_layers(weights, vectors, order, trainable, streams, sizes, outer)
    hid_tok, hid_grid, g_tok, g_grid = outs[:4]
    g_p1, g_p2, g_q, g_o, g_e, g_gi, g_go, g_f1, g_f2 = [value.astype(F32) for value in outs[4:13]]
    g_depth, g_ln_conv, g_scale, g_ln_attn, g_ln_mlp, g_ad = outs[13:]

    swap = (layer_at == 0) & (order[0, 0] == 1)
    g_tok = jnp.where(swap, g_tok[::-1], g_tok)
    g_grid = jnp.where(swap, g_grid[::-1], g_grid)
    grid_shape = (1,) + conv_grid.shape
    tok_shape = (1,) + tokens.shape
    flags = trainable[0].astype(F32)
    if outer > 1:
        g_ad = lax.psum(g_ad, "dp", axis_index_groups=groups)
    return (
        hid_tok.reshape(tok_shape),
        hid_grid.reshape(grid_shape),
        g_tok.reshape(tok_shape),
        g_grid.reshape(grid_shape),
        share(g_ln_attn[0], 0),
        share(g_q, 1),
        share(g_o, 1),
        share(g_ln_mlp[0], 0),
        share(g_f1, 0),
        share(g_f2, 1),
        share(g_depth, 1),
        share(g_ln_conv[0], 0),
        share(g_p1 * flags[2], 0),
        share((g_p2 * flags[3]).T, 1),
        share(g_scale[0], 0),
        share(g_e, 0),
        g_ad[None],
        share(g_gi.T, 1),
        share(g_go, 0),
    )


def solution(mesh):
    in_specs = (
        P(None, "dp", None, None),
        P(None, "dp", None, None, None),
        P("dp", None),
        P("pipe", None),
        P("pipe", "dp"),
        P("pipe", None, "dp", "tensor"),
        P("pipe", "tensor", "dp"),
        P("pipe", "dp"),
        P("pipe", "dp", "tensor"),
        P("pipe", "tensor", "dp"),
        P("pipe", None, "dp"),
        P("pipe", "dp"),
        P("pipe", "dp", "tensor"),
        P("pipe", "tensor", "dp"),
        P("pipe", "dp"),
        P("pipe", "dp", "tensor"),
        P("pipe", None, "tensor"),
        P("pipe", "tensor", "dp"),
        P("pipe", "dp", "tensor"),
        P(None, "dp", None, None),
        P(None, "dp", None, None, None),
    )
    out_specs = (
        P("pipe", None, "dp", None, None),
        P("pipe", None, "dp", None, None, None),
        P("pipe", None, "dp", None, None),
        P("pipe", None, "dp", None, None, None),
        P("pipe", "dp"),
        P("pipe", None, "dp", "tensor"),
        P("pipe", "tensor", "dp"),
        P("pipe", "dp"),
        P("pipe", "dp", "tensor"),
        P("pipe", "tensor", "dp"),
        P("pipe", None, "dp"),
        P("pipe", "dp"),
        P("pipe", "dp", "tensor"),
        P("pipe", "tensor", "dp"),
        P("pipe", "dp"),
        P("pipe", "dp", "tensor"),
        P("pipe", None, "tensor"),
        P("pipe", "tensor", "dp"),
        P("pipe", "dp", "tensor"),
    )
    return jax.shard_map(
        per_device, mesh=mesh, in_specs=in_specs, out_specs=out_specs, check_vma=False
    )
```

```python
import functools

import jax
import jax.numpy as jnp
from jax import lax
from jax.experimental import pallas as pl
from jax.experimental.pallas import tpu as pltpu
from jax.sharding import PartitionSpec as P

HD = 64
Z = 4
R = 2
TOK = 64
SIDE = 8
LANE = 128
BF = jnp.bfloat16
F32 = jnp.float32
ARRAYS = ("P1", "P2", "Q", "O", "E", "Gi", "Go", "F1", "F2")
EVENTS = (
    "n1", "f", "o", "cv", "n2", "c2", "m", "br", "gs",
    "dx3", "dgh", "dn2", "dc2", "dx1", "dcv", "dn1", "df", "gv", "gad",
)


def mm(a, b):
    return lax.dot_general(a, b, (((1,), (0,)), ((), ())), preferred_element_type=F32)


def mm_nt(a, b):
    return lax.dot_general(a, b, (((1,), (1,)), ((), ())), preferred_element_type=F32)


def mm_tn(a, b):
    return lax.dot_general(a, b, (((0,), (0,)), ((), ())), preferred_element_type=F32)


def flat(value):
    return value.reshape(-1, value.shape[-1])


def low(value):
    return value.astype(BF)


def wide(value):
    return value.astype(F32)


def gelu_pair(h):
    phi = 0.5 * (1.0 + lax.erf(h * 0.7071067811865476))
    dens = jnp.exp(-0.5 * h * h) * 0.3989422804014327
    return h * phi, phi + h * dens


def normed(value):
    centred = value - jnp.mean(value, axis=-1, keepdims=True)
    rs = lax.rsqrt(jnp.mean(centred * centred, axis=-1, keepdims=True) + 1e-06)
    return centred * rs, rs


def norm_back(dn, n_hat, rs, gain):
    gd = dn * gain
    return (
        gd
        - jnp.mean(gd, axis=-1, keepdims=True)
        - n_hat * jnp.mean(gd * n_hat, axis=-1, keepdims=True)
    ) * rs


def col_shift(value, by):
    if by == 0:
        return value
    at = lax.broadcasted_iota(jnp.int32, value.shape, 0) % SIDE
    rolled = pltpu.roll(value, (-by) % TOK, 0)
    return jnp.where((at + by >= 0) & (at + by < SIDE), rolled, 0.0)


def row_shift(value, by):
    if by == 0:
        return value
    gap = jnp.zeros((abs(by) * SIDE, value.shape[1]), value.dtype)
    if by > 0:
        return jnp.concatenate([value[by * SIDE :], gap], axis=0)
    return jnp.concatenate([gap, value[: TOK + by * SIDE]], axis=0)


def depthwise(value, tap, side):
    half = side // 2
    shifted = [col_shift(value, b - half) for b in range(side)]
    total = None
    for a in range(side):
        line = None
        for b in range(side):
            term = shifted[b] * tap(a * side + b)
            line = term if line is None else line + term
        line = row_shift(line, a - half)
        total = line if total is None else total + line
    return total


def depthwise_taps(value, grad, side, put):
    half = side // 2
    shifted = [col_shift(value, b - half) for b in range(side)]
    for a in range(side):
        d = a - half
        lo, hi = max(0, -d) * SIDE, (SIDE - max(0, d)) * SIDE
        for b in range(side):
            part = shifted[b][lo + d * SIDE : hi + d * SIDE] * grad[lo:hi]
            put(a * side + b, jnp.sum(part, axis=0, keepdims=True))


def lanes_of(at, width):
    return pl.ds(pl.multiple_of(at * width, width), width)


def side_by_side(blocks):
    return jnp.concatenate(blocks, axis=1)


def main_kernel(dims, outer, *refs):
    at = iter(refs)

    def take(count):
        return [next(at) for _ in range(count)]

    na = len(ARRAYS)
    source = dict(zip(ARRAYS, take(na)))
    (
        depth_in, ln_conv_in, scale_in, ln_attn_in, ln_mlp_in, adapt_depth_in,
        order_in, train_in, tok_in, grid_in, tcot_in, gcot_in,
    ) = take(12)
    hid_tok, hid_grid, out_gtok, out_ggrid = take(4)
    native = dict(zip(ARRAYS, take(na)))
    out_depth, out_ln_conv, out_scale, out_ln_attn, out_ln_mlp, out_ad = take(6)
    W = dict(zip(ARRAYS, take(na)))
    hops = take(4 * na)
    RX = {name: hops[4 * n : 4 * n + 4] for n, name in enumerate(ARRAYS)}
    (
        v_loc, v_low, vv, aq, vec_c, vec_d, x_in, c_in, n1_all, f_all, n2_all, c2_all,
        o_sb, o_rb, cv_sb, cv_rb, m_sb, m_rb, br_sb, br_rb, gsb, dgb,
        qkv, prob, ctx, u, up, r, rp, cn, crs, cv_sum, x1, c2f,
        adapted, spread, pooled, gate,
        dx3, dcot, dx3_all, dn2_sb, dn2_rb, dc2_sb, dc2_rb, dx1_all, dcv_all,
        dn1_sb, dn1_rb, df_sb, df_rb, dh, do_all, dqkv, dhc, dx1, dc2t, dad, dcn,
        gvs, gvs_low, gv_rb, gvx, gad, gad_rb, gad_all, turned,
    ) = take(67)
    (
        zs_send, zs_recv, l_send, l_recv, s1_send, s1_recv, loc_sem, s2_send, s2_recv,
        v_send, v_recv, q_send, q_recv, h_send, h_recv, b_send, b_recv, c_send, c_recv,
        xo_send, xo_recv, g_send, g_recv, a_send, a_recv, gx_send, gx_recv, go,
    ) = take(28)

    p = lax.axis_index("pipe")
    dpi = lax.axis_index("dp")
    x = lax.axis_index("tensor")
    rest = dpi % outer
    zi = dpi // (outer * R)
    ri = (dpi // outer) % R
    xo = 1 - x
    ro = 1 - ri
    d_dim, c_dim, hq, ffq, cfq, adq, dg = dims
    adh = Z * adq
    dz, cz = d_dim // Z, c_dim // Z
    tile = 256
    ids = {name: number for number, name in enumerate(ARRAYS)}
    ev = {name: number for number, name in enumerate(EVENTS)}

    def dev(z=None, rr=None, xx=None, pp=None):
        z = zi if z is None else z
        rr = ri if rr is None else rr
        return (
            p if pp is None else pp,
            (z * R + rr) * outer + rest,
            x if xx is None else xx,
        )

    def zto(d):
        return lax.rem(zi + d, Z)

    def zfrom(d):
        return lax.rem(zi + Z - d, Z)

    def remote(src, dst, ssem, rsem, device):
        return pltpu.make_async_remote_copy(
            src_ref=src, dst_ref=dst, send_sem=ssem, recv_sem=rsem,
            device_id=device, device_id_type=pl.DeviceIdType.MESH,
        )

    sib = dev(pp=1 - p)
    over_r, over_x = dev(rr=ro), dev(xx=xo)

    def z_copy(e, d, src, dst):
        return remote(src, dst, zs_send.at[e, d - 1], zs_recv.at[e, d - 1], dev(zto(d)))

    sent = []

    def gather_copies(name, buf):
        return [z_copy(ev[name], d, buf.at[zi], buf.at[zi]) for d in range(1, Z)]

    def gather_start(name, buf, keep=True):
        copies = gather_copies(name, buf)
        for c in copies:
            c.start()
        if keep:
            sent.extend(copies)

    def gather_wait(name, buf):
        for d in range(1, Z):
            slot = buf.at[zfrom(d)]
            z_copy(ev[name], d, slot, slot).wait_recv()

    def scatter_start(name, sb, rb):
        for d in range(1, Z):
            c = z_copy(ev[name], d, sb.at[zto(d)], rb.at[d - 1])
            c.start()
            sent.append(c)

    def scatter_wait(name, rb):
        for d in range(1, Z):
            z_copy(ev[name], d, rb.at[d - 1], rb.at[d - 1]).wait_recv()

    def right():
        return dev(zi + 1)

    def left():
        return dev(zi - 1)

    def pass_copy(name, buf, toward, s):
        e, k = ev[name], (0 if toward > 0 else 3) + s
        blk = buf.at[zi - toward * s]
        return remote(blk, blk, l_send.at[e, k], l_recv.at[e, k], right() if toward > 0 else left())

    def pass_cond(toward, s):
        if toward > 0:
            return (zi < Z - 1) & (zi - s >= 0)
        return (zi > 0) & (zi + s <= Z - 1)

    def line_start(name, buf):
        for toward in (1, -1):

            @pl.when(pass_cond(toward, 0))
            def _():
                pass_copy(name, buf, toward, 0).start()

    def line_step(name, buf, *steps):
        e = ev[name]
        for s in steps:
            for toward in (1, -1):
                src = zi - toward * s

                @pl.when((src >= 0) & (src <= Z - 1))
                def _():
                    blk = buf.at[src]
                    k = (0 if toward > 0 else 3) + s - 1
                    remote(blk, blk, l_send.at[e, k], l_recv.at[e, k], sib).wait_recv()

                if s < Z - 1:

                    @pl.when(pass_cond(toward, s))
                    def _():
                        pass_copy(name, buf, toward, s).start()

    def line_sent(name, buf):
        for toward in (1, -1):
            for s in range(Z - 1):

                @pl.when(pass_cond(toward, s))
                def _():
                    pass_copy(name, buf, toward, s).wait_send()

    def sum_copy(name, sb, rb, toward, k, first):
        e, way = ev[name], (0 if toward > 0 else 1)
        src = sb.at[zi + toward * k] if first else rb.at[way, k]
        q = way * 3 + k - 1
        return remote(src, rb.at[way, k - 1], l_send.at[e, q], l_recv.at[e, q], right() if toward > 0 else left())

    def at_end(toward):
        return zi == (0 if toward > 0 else Z - 1)

    def passes(toward, k):
        dest = zi + toward * k
        return jnp.logical_not(at_end(toward)) & (dest >= 0) & (dest <= Z - 1)

    def sum_start(name, sb, rb):
        for toward in (1, -1):

            @pl.when(at_end(toward))
            def _():
                for k in (3, 2, 1):
                    sum_copy(name, sb, rb, toward, k, True).start()

    def sum_arrival(name, rb, way, k):
        e = ev[name]
        slot = rb.at[way, k]
        return remote(slot, slot, l_send.at[e, way * 3 + k], l_recv.at[e, way * 3 + k], sib)

    def sum_step(name, sb, rb, *ks):
        for k in ks:
            for way, toward in enumerate((1, -1)):

                @pl.when(passes(toward, k))
                def _():
                    sum_arrival(name, rb, way, k).wait_recv()
                    rb[way, k] = low(wide(rb[way, k]) + wide(sb[zi + toward * k]))
                    sum_copy(name, sb, rb, toward, k, False).start()

    def sum_wait(name, rb):
        for way, toward in enumerate((1, -1)):

            @pl.when(jnp.logical_not(at_end(toward)))
            def _():
                sum_arrival(name, rb, way, 0).wait_recv()

    def summed(sb, rb):
        return wide(sb[zi]) + (wide(rb[0, 0]) + wide(rb[1, 0]))

    def sum_sent(name, sb, rb):
        for toward in (1, -1):

            @pl.when(at_end(toward))
            def _():
                for k in (3, 2, 1):
                    sum_copy(name, sb, rb, toward, k, True).wait_send()

            for k in (2, 1):

                @pl.when(passes(toward, k))
                def _():
                    sum_copy(name, sb, rb, toward, k, False).wait_send()

    def share_start(name, buf):
        for d in range(1, Z):
            c = z_copy(ev[name], d, buf.at[3], buf.at[d - 1])
            c.start()
            sent.append(c)

    def scattered(sb, rb):
        return (wide(sb[zi]) + wide(rb[0])) + (wide(rb[1]) + wide(rb[2]))

    barrier = pltpu.get_barrier_semaphore()
    greeted = [sib]
    for d in range(1, Z):
        greeted += [dev(zto(d)), dev(zto(d), ro), dev(zto(d), pp=1 - p)]
    greeted += [over_r, over_x, dev(rr=ro, xx=xo)]
    for device in greeted:
        pl.semaphore_signal(barrier, inc=1, device_id=device, device_id_type=pl.DeviceIdType.MESH)
    v_loc[...] = jnp.zeros(v_loc.shape, F32)
    taps7 = depth_in.shape[0]
    c_own = depth_in.shape[1]
    v_loc[0:taps7, 0:c_own] = wide(depth_in[...])
    v_loc[49:50, 0:c_own] = wide(ln_conv_in[...])
    v_loc[50:51, 0:c_own] = wide(scale_in[...])
    v_loc[56:57, 0:LANE] = wide(ln_attn_in[...])
    v_loc[57:58, 0:LANE] = wide(ln_mlp_in[...])
    aq[x] = jnp.zeros(aq.shape[1:], F32)
    aq[x, 0:9] = wide(adapt_depth_in[:, lanes_of(zi, adq)])
    v_low[...] = low(v_loc[...])
    line_sums = (
        ("o", o_sb, o_rb), ("cv", cv_sb, cv_rb), ("m", m_sb, m_rb), ("dn2", dn2_sb, dn2_rb),
        ("dc2", dc2_sb, dc2_rb), ("dn1", dn1_sb, dn1_rb), ("df", df_sb, df_rb),
    )
    line_gathers = (
        ("n1", n1_all), ("f", f_all), ("n2", n2_all), ("c2", c2_all), ("dx1", dx1_all), ("dcv", dcv_all),
    )
    for _, _, rb in line_sums:
        for way, toward in enumerate((1, -1)):

            @pl.when(at_end(toward))
            def _():
                rb[way, 0] = jnp.zeros(rb.shape[2:], BF)

    pl.semaphore_wait(barrier, len(greeted))

    me8 = zi * R + ri
    v_arrivals = []
    for n, (d, flip) in enumerate([(d, s) for d in range(Z) for s in (0, 1)][1:]):
        tr = ro if flip else ri
        c = remote(v_low, vv.at[me8], v_send.at[n], v_recv.at[n], dev(zto(d), tr))
        c.start()
        sent.append(c)
        fr = zfrom(d) * R + tr
        v_arrivals.append(remote(vv.at[fr], vv.at[fr], v_send.at[n], v_recv.at[n], dev(zto(d), tr)))
    vv[me8] = v_low[...]
    c = remote(aq.at[x], aq.at[x], q_send, q_recv, over_x)
    c.start()
    sent.append(c)

    by_rows = ("O", "F2")

    def quarter_of(name, ref, z):
        if name == "Q":
            return ref.at[:, :, lanes_of(z, hq)]
        if name in by_rows:
            height = ref.shape[0] // Z
            return ref.at[pl.ds(pl.multiple_of(z * height, height), height)]
        return ref.at[:, lanes_of(z, ref.shape[1] // Z)]

    def step1_local(name):
        return pltpu.make_async_copy(
            quarter_of(name, source[name], zi), W[name].at[x, zi, ri], loc_sem.at[ids[name]]
        )

    def step1_copy(name, d):
        k = ids[name]
        return remote(
            quarter_of(name, source[name], zto(d)), W[name].at[x, zi, ri],
            s1_send.at[k, d - 1], s1_recv.at[k, d - 1], dev(zto(d)),
        )

    def half_of(name, j, z, rr, upper):
        w = W[name]
        half = w.shape[-2] // 2
        rows = slice(half, None) if upper else slice(0, half)
        if len(w.shape) == 6:
            return w.at[j, z, rr, :, rows]
        return w.at[j, z, rr, rows]

    def step2_copy(name, which, d):
        k = ids[name]
        z = zfrom(d)
        if which < 2:
            src = quarter_of(name, source[name], zi) if d == 0 else W[name].at[x, z, ri]
            dst = W[name].at[x, z, ri]
        else:
            src = dst = half_of(name, x, z, ro, False) if which == 2 else half_of(name, xo, z, ri, True)
        to = over_x if which in (1, 2) else over_r
        return remote(src, dst, s2_send.at[k, which, d], s2_recv.at[k, which, d], to)

    def step2_arrival(name, which, d):
        k = ids[name]
        z = zfrom(d)
        if which < 2:
            ref = W[name].at[x, z, ro] if which == 0 else W[name].at[xo, z, ri]
        else:
            ref = half_of(name, xo, z, ro, which == 3)
        to = over_x if which in (1, 2) else over_r
        return remote(ref, ref, s2_send.at[k, which, d], s2_recv.at[k, which, d], to)

    def relay1(*names):
        for name in names:
            step1_local(name).start()
            for d in range(1, Z):
                step1_copy(name, d).start()
            step2_copy(name, 0, 0).start()
            step2_copy(name, 1, 0).start()

    def relay2(name, ds=(1, 2, 3)):
        k = ids[name]
        for d in ds:
            slot = W[name].at[x, zfrom(d), ri]
            remote(slot, slot, s1_send.at[k, d - 1], s1_recv.at[k, d - 1], dev(zto(d))).wait_recv()
            step2_copy(name, 0, d).start()
            step2_copy(name, 1, d).start()

    def relay3(name, ds=(0, 1, 2, 3)):
        for d in ds:
            step2_arrival(name, 0, d).wait_recv()
            step2_copy(name, 2, d).start()
            step2_arrival(name, 1, d).wait_recv()
            step2_copy(name, 3, d).start()

    def relay4(*names):
        for name in names:
            step1_local(name).wait()
            for d in range(Z):
                step2_arrival(name, 2, d).wait_recv()
                step2_arrival(name, 3, d).wait_recv()

    def relay_sent():
        for name in ARRAYS:
            for d in range(1, Z):
                step1_copy(name, d).wait_send()
            for which in range(4):
                for d in range(Z):
                    step2_copy(name, which, d).wait_send()

    @pl.when(p == 0)
    def _():
        relay1("P1", "P2")

    @pl.when(p == 1)
    def _():
        dx3[...] = tcot_in[x]
        dcot[...] = gcot_in[x]
        dx3_all[zi] = tcot_in[x]
        line_start("dx3", dx3_all)

    for c in v_arrivals:
        c.wait_recv()
    remote(aq.at[xo], aq.at[xo], q_send, q_recv, over_x).wait_recv()
    low_lanes = lax.broadcasted_iota(jnp.int32, (64, LANE), 1) < LANE // 2
    for z in range(Z):
        first, second = wide(vv[2 * z]), pltpu.roll(wide(vv[2 * z + 1]), LANE // 2, 1)
        vec_c[:, z * cz : z * cz + LANE] = first[:, 0:LANE]
        vec_c[:, z * cz + LANE : z * cz + 2 * LANE] = jnp.where(
            low_lanes, first[:, LANE:], second[:, 0:LANE]
        )
        vec_c[:, z * cz + 2 * LANE : (z + 1) * cz] = second[:, LANE:]
    for i in range(Z * R):
        vec_d[:, i * LANE : (i + 1) * LANE] = wide(vv[i])[56:64, 0:LANE]

    def gain_d(row):
        return vec_d[row : row + 1, :]

    def gain_c(row):
        return vec_c[row : row + 1, :]

    def token_entry():
        n_hat, _ = normed(wide(x_in[...]))
        n1_all[zi] = low(n_hat * gain_d(0))
        line_start("n1", n1_all)

    def conv_entry():
        @pl.loop(0, c_dim // LANE)
        def _(ch):
            lanes = lanes_of(ch, LANE)
            taps = vec_c[:, lanes]
            cn[:, lanes] = depthwise(wide(c_in[:, lanes]), lambda k: taps[k : k + 1], 7)

        n_hat, rs = normed(cn[...])
        cn[...] = n_hat
        crs[...] = jnp.broadcast_to(rs, crs.shape)
        f_all[zi] = low(n_hat * gain_c(49))
        line_start("f", f_all)

    def first_relays(pump):
        relay2("P1")
        pump(1)
        relay1("Q", "O")
        relay2("P2")
        pump(2)
        relay3("P1")


    @pl.when(p == 0)
    def _():
        first = order_in[0, x] == 0
        c_in[...] = jnp.where(first, grid_in[0], grid_in[1])
        x_in[...] = jnp.where(first, tok_in[0], tok_in[1])
        conv_entry()
        token_entry()

        def pump(s):
            line_step("f", f_all, s)
            line_step("n1", n1_all, s)

        first_relays(pump)
        line_step("f", f_all, 3)
        line_step("n1", n1_all, 3)

    @pl.when(p == 1)
    def _():
        pl.semaphore_wait(go, 1)
        relay1("P1", "P2")
        first_relays(lambda s: line_step("dx3", dx3_all, s))
        remote(c_in, c_in, h_send.at[1], h_recv.at[1], sib).wait_recv()
        conv_entry()
        line_step("dx3", dx3_all, 3)
        line_step("f", f_all, 1)

    relay2("Q")
    relay2("O")
    relay1("E", "Gi", "Go")
    relay3("P2", (0, 1))

    @pl.when(p == 1)
    def _():
        line_step("f", f_all, 2, 3)

    relay4("P1")

    def conv_hidden(j):
        @pl.loop(0, cfq // tile)
        def _(t):
            lanes = lanes_of(t, tile)
            act, der = gelu_pair(mm(flat(f_all[...]), flat(W["P1"][j, :, :, :, lanes])))
            r[j, :, lanes] = low(act)
            rp[j, :, lanes] = low(der)

    conv_hidden(0)

    relay3("P2", (2, 3))
    for name in ("E", "Gi", "Go"):
        relay2(name)
    relay1("F1")
    conv_hidden(1)
    relay3("Q")
    relay3("O")
    relay2("F1")
    relay1("F2")

    relay4("P2")

    @pl.loop(0, Z)
    def _(z):
        acc = mm_nt(r[0], flat(W["P2"][0, z])) + mm_nt(r[1], flat(W["P2"][1, z]))
        cv_sb[:, :, lanes_of(z, cz)] = low(acc).reshape(Z, TOK, cz)

    sum_start("cv", cv_sb, cv_rb)

    for name in ("E", "Gi", "Go"):
        relay3(name)
    sum_step("cv", cv_sb, cv_rb, 2)
    relay2("F2")
    sum_step("cv", cv_sb, cv_rb, 1)

    @pl.when(p == 0)
    def _():
        pl.semaphore_signal(go, inc=1, device_id=sib, device_id_type=pl.DeviceIdType.MESH)

    @pl.when(p == 1)
    def _():
        remote(x_in, x_in, h_send.at[0], h_recv.at[0], sib).wait_recv()
        token_entry()
        line_step("n1", n1_all, 1, 2, 3)

    relay4("Q", "O")
    for j in range(2):
        wj = side_by_side([flat(W["Q"][j, :, :, s]) for s in range(3)])
        qkv[j] = low(mm(flat(n1_all[...]), wj))
    for j in range(2):
        for b in range(Z):
            rows = slice(b * TOK, (b + 1) * TOK)
            outs = []
            for h in range(hq // HD):
                q, kk, vals = (qkv[j, rows, s * hq + h * HD : s * hq + (h + 1) * HD] for s in range(3))
                sc = mm_nt(q, kk) * HD ** (-0.5)
                e = jnp.exp(sc - jnp.max(sc, axis=-1, keepdims=True))
                pr = low(e / jnp.sum(e, axis=-1, keepdims=True))
                prob[j, h, b] = pr
                outs.append(mm(pr, vals))
            ctx[j, rows, :] = low(side_by_side(outs))

    def out_block(j, z):
        return side_by_side([W["O"][j, z, 0], W["O"][j, z, 1]])

    @pl.loop(0, Z)
    def _(z):
        both = jnp.concatenate([out_block(0, z), out_block(1, z)], axis=0)
        acc = mm(side_by_side([ctx[0], ctx[1]]), both)
        o_sb[:, :, lanes_of(z, dz)] = low(acc).reshape(Z, TOK, dz)

    sum_start("o", o_sb, o_rb)

    relay3("F1")

    sum_wait("cv", cv_rb)
    cv_sum[...] = summed(cv_sb, cv_rb)
    c2f[...] = wide(c_in[...]) + gain_c(50) * cv_sum[...]
    c2_low = low(c2f[...])
    c2_all[zi] = c2_low
    line_start("c2", c2_all)
    sum_step("o", o_sb, o_rb, 2)
    hid_grid[x] = c2_low

    @pl.when(p == 0)
    def _():
        remote(hid_grid.at[x], c_in, h_send.at[1], h_recv.at[1], sib).start()

    relay3("F2")
    sum_step("o", o_sb, o_rb, 1)
    line_step("c2", c2_all, 1)
    sum_wait("o", o_rb)
    x1[...] = wide(x_in[...]) + summed(o_sb, o_rb)
    n_hat, _ = normed(x1[...])
    n2_all[zi] = low(n_hat * gain_d(1))
    line_start("n2", n2_all)

    relay4("E", "Gi", "Go")
    line_step("c2", c2_all, 2)
    line_step("n2", n2_all, 1)
    line_step("c2", c2_all, 3)
    row8 = lax.broadcasted_iota(jnp.int32, (8, adq), 0)
    gs_part = None
    for j in range(2):
        ad = mm(flat(c2_all[...]), flat(W["E"][j]))
        adapted[j] = ad
        taps = aq[j]
        pool = jnp.zeros((8, adq), F32)
        for b in range(Z):
            sp = depthwise(ad[b * TOK : (b + 1) * TOK], lambda k: taps[k : k + 1], 3)
            spread[j, b] = sp
            pool = jnp.where(row8 == b, jnp.mean(sp, axis=0, keepdims=True), pool)
        pooled[j] = pool
        term = mm_nt(low(pool), flat(W["Gi"][j]))
        gs_part = term if gs_part is None else gs_part + term
    gsb[3] = gs_part
    share_start("gs", gsb)
    line_step("n2", n2_all, 2)

    relay4("F1")
    line_step("n2", n2_all, 3)
    for j in range(2):

        @pl.loop(0, ffq // tile)
        def _(t):
            lanes = lanes_of(t, tile)
            act, der = gelu_pair(mm(flat(n2_all[...]), flat(W["F1"][j, :, :, :, lanes])))
            u[j, :, lanes] = low(act)
            up[j, :, lanes] = low(der)

    scatter_wait("gs", gsb)

    def gate_hidden():
        return gelu_pair((gsb[0] + gsb[1]) + (gsb[2] + gsb[3]))

    gh, _ = gate_hidden()
    for j in range(2):
        g8 = jnp.tanh(mm(low(gh), flat(W["Go"][j])))
        gate[j] = g8
        for b in range(Z):
            br_sb[b, :, j * adq : (j + 1) * adq] = low(g8[b : b + 1] * spread[j, b])
    scatter_start("br", br_sb, br_rb)
    relay4("F2")

    @pl.loop(0, Z)
    def _(z):
        acc = None
        for j in range(2):
            term = mm(u[j], side_by_side([W["F2"][j, z, 0], W["F2"][j, z, 1]]))
            acc = term if acc is None else acc + term
        m_sb[:, :, lanes_of(z, dz)] = low(acc).reshape(Z, TOK, dz)

    sum_start("m", m_sb, m_rb)

    def exchange(n, buf):
        remote(buf.at[x], buf.at[x], xo_send.at[n], xo_recv.at[n], over_x).start()

    def layer_output(total):
        sum_step("m", m_sb, m_rb, 2)
        scatter_wait("br", br_rb)
        total[...] = x1[...]
        for d in range(Z):
            piece = br_sb[zi] if d == 0 else br_rb[d - 1]
            for j in range(2):
                lanes = pl.ds(pl.multiple_of(j * adh + zfrom(d) * adq, LANE), adq)
                total[:, lanes] += wide(piece[:, j * adq : (j + 1) * adq])
        sum_step("m", m_sb, m_rb, 1)
        sum_wait("m", m_rb)
        hid_tok[x] = low(total[...] + summed(m_sb, m_rb))

    @pl.when(p == 0)
    def _():
        layer_output(dx1)
        remote(hid_tok.at[x], x_in, h_send.at[0], h_recv.at[0], sib).start()
        exchange(0, hid_tok)

    exchange(1, hid_grid)
    relay_sent()

    def over_cores(d):
        return remote(
            out_gtok.at[x], dx3_all.at[zi], b_send.at[d], b_recv.at[d], dev(zto(d), pp=1 - p)
        )

    @pl.when(p == 0)
    def _():
        for d in range(Z):
            slot = dx3_all.at[zfrom(d)]
            remote(slot, slot, b_send.at[d], b_recv.at[d], sib).wait_recv()
        dx3[...] = dx3_all[zi]

    def own_lanes(j):
        return pl.ds(pl.multiple_of(j * adh + zi * adq, LANE), adq)

    gh, ghp = gate_hidden()
    dgh_part = None
    dgp = []
    for j in range(2):
        dgate = jnp.zeros((8, adq), F32)
        for b in range(Z):
            dbr = wide(dx3_all[b, :, own_lanes(j)])
            dgate = jnp.where(row8 == b, jnp.sum(dbr * spread[j, b], axis=0, keepdims=True), dgate)
        dg8 = low(dgate * (1.0 - gate[j] * gate[j]))
        dgp.append(dg8)
        term = mm_nt(dg8, flat(W["Go"][j]))
        dgh_part = term if dgh_part is None else dgh_part + term
    dgb[3] = dgh_part
    share_start("dgh", dgb)

    for j in range(2):

        @pl.loop(0, ffq // tile)
        def _(t):
            rows = lanes_of(t, tile)
            both = side_by_side([W["F2"][j, z, rr, rows] for z in range(Z) for rr in range(R)])
            du = mm_nt(flat(dx3_all[...]), both)
            dh[j, :, rows] = low(du * wide(up[j, :, rows]))

    scatter_wait("dgh", dgb)
    dgs = low(((dgb[0] + dgb[1]) + (dgb[2] + dgb[3])) * ghp)
    for j in range(2):
        dpool = mm(dgs, flat(W["Gi"][j])) * (1.0 / TOK)
        taps = aq[j]
        tap_rows = [None] * 9
        for b in range(Z):
            dsp = gate[j, b : b + 1] * wide(dx3_all[b, :, own_lanes(j)]) + dpool[b : b + 1]
            dad[j, b * TOK : (b + 1) * TOK] = low(depthwise(dsp, lambda k: taps[8 - k : 9 - k], 3))

            def put(k, row):
                tap_rows[k] = row if tap_rows[k] is None else tap_rows[k] + row

            depthwise_taps(adapted[j, b * TOK : (b + 1) * TOK], dsp, 3, put)
        for k in range(9):
            gad[j, k : k + 1] = tap_rows[k]
        gad[j, 9:16] = jnp.zeros((7, adq), F32)

    @pl.loop(0, Z)
    def _(z):
        acc = mm_nt(dad[0], flat(W["E"][0, z])) + mm_nt(dad[1], flat(W["E"][1, z]))
        dc2_sb[:, :, lanes_of(z, cz)] = low(acc).reshape(Z, TOK, cz)

    sum_start("dc2", dc2_sb, dc2_rb)

    @pl.loop(0, Z)
    def _(z):
        acc = mm_nt(dh[0], flat(W["F1"][0, z])) + mm_nt(dh[1], flat(W["F1"][1, z]))
        dn2_sb[:, :, lanes_of(z, dz)] = low(acc).reshape(Z, TOK, dz)

    sum_start("dn2", dn2_sb, dn2_rb)
    sum_step("dc2", dc2_sb, dc2_rb, 2)

    def half_rows(name, upper):
        half = W[name].shape[-2] // 2
        rows = slice(half, None) if upper else slice(0, half)
        return (slice(None), rows) if len(W[name].shape) == 6 else (rows,)

    fine = ("P1", "P2")

    def pieces(name):
        return (1, 2, 3, 0) if name in fine else (None,)

    def block_at(d):
        return slice(None) if d is None else zto(d)

    def hop_copy(name, which, d):
        n = ids[name]
        lower, upper = half_rows(name, False), half_rows(name, True)
        z = block_at(d)
        w, buf = W[name], RX[name]
        src, dst, to = (
            lambda: (w.at[(xo, z, slice(None)) + lower], buf[0].at[z], over_x),
            lambda: (w.at[(slice(None), z, ro) + upper], buf[1].at[:, z], over_r),
            lambda: (buf[0].at[z, ro], buf[2].at[z], over_r),
            lambda: (buf[1].at[xo, z], buf[3].at[z], over_x),
        )[which]()
        k = 0 if d is None else d
        return remote(src, dst, g_send.at[n, which, k], g_recv.at[n, which, k], to)

    def reduce_start(name, d=None):
        hop_copy(name, 0, d).start()
        hop_copy(name, 1, d).start()

    def each_block(d, body):
        if d is None:
            pl.loop(0, Z)(body)
        else:
            body(zto(d))

    def reduce_middle(*names):
        for name in names:
            lower, upper = half_rows(name, False), half_rows(name, True)
            buf = RX[name]
            for d in pieces(name):
                hop_copy(name, 0, d).wait_recv()

                def add_lower(z):
                    for rr in range(R):
                        own = W[name][(x, z, rr) + lower]
                        buf[0][z, rr] = low(wide(own) + wide(buf[0][z, rr]))

                each_block(d, add_lower)
                hop_copy(name, 2, d).start()
                hop_copy(name, 1, d).wait_recv()

                def add_upper(z):
                    for j in range(2):
                        own = W[name][(j, z, ri) + upper]
                        buf[1][j, z] = low(wide(own) + wide(buf[1][j, z]))

                each_block(d, add_upper)
                hop_copy(name, 3, d).start()

    def reduce_end(*names):
        for name in names:
            lower, upper = half_rows(name, False), half_rows(name, True)
            buf = RX[name]
            for d in pieces(name):
                hop_copy(name, 2, d).wait_recv()
                hop_copy(name, 3, d).wait_recv()

                def add_both(z):
                    W[name][(x, z, ri) + lower] = low(wide(buf[0][z, ri]) + wide(buf[2][z]))
                    W[name][(x, z, ri) + upper] = low(wide(buf[1][x, z]) + wide(buf[3][z]))

                each_block(d, add_both)
                for k in range(Z) if d is None else (d,):
                    (back_copy(name, k) if k else back_local(name)).start()

    def back_copy(name, d):
        n = ids[name]
        return remote(
            W[name].at[x, zto(d), ri], quarter_of(name, native[name], zi),
            a_send.at[n, d - 1], a_recv.at[n, d - 1], dev(zto(d)),
        )

    def back_local(name):
        return pltpu.make_async_copy(
            W[name].at[x, zi, ri], quarter_of(name, native[name], zi), loc_sem.at[ids[name]]
        )

    peers = ((1, 0), (0, 1), (1, 1))

    def owner(k):
        return (ro if peers[k][0] else ri), (xo if peers[k][1] else x)

    def row_grad(name, left, right):
        width = W[name].shape[3]
        span = R * width
        for k, d in enumerate((1, 2, 3, 0)):
            z = zto(d)
            half = (k % 2) * span
            turned[half : half + span] = flat(left[:, :, lanes_of(z, span)]).T
            for j in range(2):
                W[name][j, z] = low(mm(turned[half : half + span], right[j])).reshape(R, width, -1)
            if name in fine:
                reduce_start(name, d)
        if name not in fine:
            reduce_start(name)

    def col_grad(name, left, right):
        width = left.shape[2]
        for j in range(2):
            turned[j * width : (j + 1) * width] = left[j].T
        for d in (1, 2, 3, 0):
            z = zto(d)
            rhs = flat(right[:, :, lanes_of(z, dz)])
            for j in range(2):
                g = low(mm(turned[j * width : (j + 1) * width], rhs))
                for rr in range(R):
                    W[name][j, z, rr] = g[:, rr * LANE : (rr + 1) * LANE]
            if name in fine:
                reduce_start(name, d)
        if name not in fine:
            reduce_start(name)

    for j in range(2):
        W["Gi"][j] = low(mm_tn(dgs, low(pooled[j]))).reshape(Z, R, -1, adq)
        W["Go"][j] = low(mm_tn(low(gh), dgp[j])).reshape(Z, R, -1, adq)
    sum_step("dc2", dc2_sb, dc2_rb, 1)
    sum_step("dn2", dn2_sb, dn2_rb, 2)
    reduce_start("Gi")
    reduce_start("Go")
    row_grad("E", c2_all, dad)
    sum_step("dn2", dn2_sb, dn2_rb, 1)

    @pl.when(p == 0)
    def _():
        remote(dcot, dcot, c_send, c_recv, sib).wait_recv()

    sum_wait("dc2", dc2_rb)
    dc2t[...] = wide(dcot[...]) + summed(dc2_sb, dc2_rb)
    gvs_ls = jnp.sum(cv_sum[...] * dc2t[...], axis=0, keepdims=True)
    dcv_all[zi] = low(dc2t[...] * gain_c(50))
    line_start("dcv", dcv_all)

    sum_wait("dn2", dn2_rb)
    dn2 = summed(dn2_sb, dn2_rb)
    n_hat, rs = normed(x1[...])
    gvs_d1 = jnp.sum(dn2 * n_hat, axis=0, keepdims=True)
    dx1[...] = wide(dx3[...]) + norm_back(dn2, n_hat, rs, gain_d(1))
    dx1_all[zi] = low(dx1[...])
    line_start("dx1", dx1_all)
    line_step("dcv", dcv_all, 1)
    col_grad("F2", u, dx3_all)
    line_step("dcv", dcv_all, 2)
    line_step("dx1", dx1_all, 1)
    row_grad("F1", n2_all, dh)

    line_step("dcv", dcv_all, 3)
    line_step("dx1", dx1_all, 2)
    for j in range(2):

        @pl.loop(0, cfq // tile)
        def _(t):
            lanes = lanes_of(t, tile)
            dr = mm(flat(dcv_all[...]), flat(W["P2"][j, :, :, :, lanes]))
            dhc[j, :, lanes] = low(dr * wide(rp[j, :, lanes]))

    @pl.loop(0, Z)
    def _(z):
        acc = mm_nt(dhc[0], flat(W["P1"][0, z])) + mm_nt(dhc[1], flat(W["P1"][1, z]))
        df_sb[:, :, lanes_of(z, cz)] = low(acc).reshape(Z, TOK, cz)

    sum_start("df", df_sb, df_rb)

    early = ("Gi", "Go", "E", "F2", "F1")

    def pw_grads():
        row_grad("P2", dcv_all, r)
        row_grad("P1", f_all, dhc)

    line_step("dx1", dx1_all, 3)

    @pl.when(p == 0)
    def _():
        pw_grads()

    sum_step("df", df_sb, df_rb, 2)

    for j in range(2):
        both = side_by_side([W["O"][j, z, rr] for z in range(Z) for rr in range(R)])
        do_all[j] = low(mm_nt(flat(dx1_all[...]), both))
    for j in range(2):
        for b in range(Z):
            rows = slice(b * TOK, (b + 1) * TOK)
            parts = [[], [], []]
            for h in range(hq // HD):
                q, kk, vals = (qkv[j, rows, s * hq + h * HD : s * hq + (h + 1) * HD] for s in range(3))
                do = do_all[j, rows, h * HD : (h + 1) * HD]
                pr = prob[j, h, b]
                dp = mm_nt(do, vals)
                prw = wide(pr)
                ds = low(prw * (dp - jnp.sum(dp * prw, axis=-1, keepdims=True)) * HD ** (-0.5))
                parts[0].append(mm(ds, kk))
                parts[1].append(mm_tn(ds, q))
                parts[2].append(mm_tn(pr, do))
            for s in range(3):
                dqkv[j, rows, s * hq : (s + 1) * hq] = low(side_by_side(parts[s]))

    @pl.loop(0, Z)
    def _(z):
        acc = None
        for j in range(2):
            term = mm_nt(dqkv[j], side_by_side([flat(W["Q"][j, z, :, s]) for s in range(3)]))
            acc = term if acc is None else acc + term
        dn1_sb[:, :, lanes_of(z, dz)] = low(acc).reshape(Z, TOK, dz)

    sum_start("dn1", dn1_sb, dn1_rb)
    sum_step("df", df_sb, df_rb, 1)

    def attention_grads():
        @pl.loop(0, Z)
        def _(z):
            turned[0:dz] = flat(n1_all[:, :, lanes_of(z, dz)]).T
            for j in range(2):
                g = low(mm(turned[0:dz], dqkv[j]))
                for s in range(3):
                    W["Q"][j, z, :, s] = g[:, s * hq : (s + 1) * hq].reshape(R, -1, hq)

        reduce_start("Q")
        col_grad("O", ctx, dx1_all)

    sum_step("dn1", dn1_sb, dn1_rb, 2)
    reduce_middle(*early)
    sum_step("dn1", dn1_sb, dn1_rb, 1)

    @pl.when(p == 0)
    def _():
        reduce_middle("P2")
        attention_grads()
        reduce_middle("P1")
        reduce_end(*early)

    sum_wait("dn1", dn1_rb)
    dn1 = summed(dn1_sb, dn1_rb)
    n_hat, rs = normed(wide(x_in[...]))
    gvs_d0 = jnp.sum(dn1 * n_hat, axis=0, keepdims=True)
    out_gtok[x] = low(dx1[...] + norm_back(dn1, n_hat, rs, gain_d(0)))

    @pl.when(p == 1)
    def _():
        for d in (1, 2, 3, 0):
            over_cores(d).start()

    sum_wait("df", df_rb)
    dfv = summed(df_sb, df_rb)
    gvs_lc = jnp.sum(dfv * cn[...], axis=0, keepdims=True)
    dcn[...] = norm_back(dfv, cn[...], crs[:, 0:1], gain_c(49))

    @pl.loop(0, c_dim // LANE)
    def _(ch):
        lanes = lanes_of(ch, LANE)
        taps = vec_c[:, lanes]
        back = depthwise(dcn[:, lanes], lambda k: taps[48 - k : 49 - k], 7)
        out_ggrid[x, :, lanes] = low(dc2t[:, lanes] + back)

    @pl.when(p == 1)
    def _():
        remote(out_ggrid.at[x], dcot, c_send, c_recv, sib).start()
        pw_grads()
        attention_grads()
        layer_output(dx1)
        exchange(0, hid_tok)
        reduce_end(*early)

    @pl.when(p == 0)
    def _():
        reduce_end("P2")

    exchange(2, out_gtok)
    exchange(3, out_ggrid)

    @pl.loop(0, Z)
    def _(z):
        for part in range(cz // LANE):
            lanes = pl.ds(pl.multiple_of(z * cz + part * LANE, LANE), LANE)

            def put(k, row):
                gvs[z, k : k + 1, part * LANE : (part + 1) * LANE] = row

            depthwise_taps(wide(c_in[:, lanes]), dcn[:, lanes], 7, put)

    for z in range(Z):
        gvs[z, 49:50] = gvs_lc[:, z * cz : (z + 1) * cz]
        gvs[z, 50:51] = gvs_ls[:, z * cz : (z + 1) * cz]
        gvs[z, 51:64] = jnp.zeros((13, cz), F32)
        gvs[z, 56:57, 0:dz] = gvs_d0[:, z * dz : (z + 1) * dz]
        gvs[z, 57:58, 0:dz] = gvs_d1[:, z * dz : (z + 1) * dz]
    gvs_low[...] = low(gvs[...])
    scatter_start("gv", gvs_low, gv_rb)

    def group_copy(n, k, src, dst):
        rr, xx = owner(k)
        return remote(src, dst, gx_send.at[n, k], gx_recv.at[n, k], dev(rr=rr, xx=xx))

    for k in range(3):
        c = group_copy(1, k, gad, gad_rb.at[k])
        c.start()
        sent.append(c)
    @pl.when(p == 1)
    def _():
        reduce_middle("P2", "P1")
        reduce_end("P2")

    reduce_end("P1")
    scatter_wait("gv", gv_rb)
    gvx[3] = (gvs[zi] + wide(gv_rb[0])) + (wide(gv_rb[1]) + wide(gv_rb[2]))
    for k in range(3):
        c = group_copy(0, k, gvx.at[3], gvx.at[k])
        c.start()
        sent.append(c)
    for k in range(3):
        group_copy(1, k, gad, gad_rb.at[k]).wait_recv()
    gad_all[zi] = (gad[x] + gad_rb[0, x]) + (gad_rb[1, x] + gad_rb[2, x])
    gather_start("gad", gad_all)

    reduce_middle("Q", "O")
    reduce_end("Q", "O")

    for k in range(3):
        group_copy(0, k, gvx.at[k], gvx.at[k]).wait_recv()
    total = (gvx[0] + gvx[1]) + (gvx[2] + gvx[3])
    mine = jnp.where(ri == 1, pltpu.roll(total, c_own, 1), total)[:, 0:c_own]
    mine_d = jnp.where(ri == 1, total[:, LANE : 2 * LANE], total[:, 0:LANE])

    def flag(n):
        return train_in[0, n].astype(F32)

    out_depth[...] = mine[0:taps7] * flag(0)
    out_ln_conv[...] = mine[49:50] * flag(1)
    out_scale[...] = mine[50:51] * flag(4)
    out_ln_attn[...] = mine_d[56:57]
    out_ln_mlp[...] = mine_d[57:58]
    gather_wait("gad", gad_all)
    for z in range(Z):
        out_ad[:, z * adq : (z + 1) * adq] = gad_all[z][0:9]
    for name in ARRAYS:
        back_local(name).wait()
        for d in range(1, Z):
            n = ids[name]
            slot = quarter_of(name, native[name], zfrom(d))
            remote(slot, slot, a_send.at[n, d - 1], a_recv.at[n, d - 1], dev(zto(d))).wait_recv()
    for n, buf in enumerate((hid_tok, hid_grid, out_gtok, out_ggrid)):
        c = remote(buf.at[x], buf.at[x], xo_send.at[n], xo_recv.at[n], over_x)
        c.wait_send()
        remote(buf.at[xo], buf.at[xo], xo_send.at[n], xo_recv.at[n], over_x).wait_recv()

    @pl.when(p == 0)
    def _():
        remote(hid_tok.at[x], x_in, h_send.at[0], h_recv.at[0], sib).wait_send()
        remote(hid_grid.at[x], c_in, h_send.at[1], h_recv.at[1], sib).wait_send()

    @pl.when(p == 1)
    def _():
        for d in range(Z):
            over_cores(d).wait_send()
        remote(out_ggrid.at[x], dcot, c_send, c_recv, sib).wait_send()

    for name, buf in line_gathers:
        line_sent(name, buf)

    @pl.when(p == 1)
    def _():
        line_sent("dx3", dx3_all)

    for name, sb, rb in line_sums:
        sum_sent(name, sb, rb)
    for c in sent:
        c.wait_send()
    for name in ARRAYS:
        for which in range(4):
            for d in pieces(name):
                hop_copy(name, which, d).wait_send()
        for d in range(1, Z):
            back_copy(name, d).wait_send()


def run_layers(weights, vectors, order, train, streams, sizes, outer):
    d_dim, c_dim, hq, ffq, cfq, adw, dg = sizes
    vm = pltpu.VMEM
    blocks = []
    for name, value in zip(ARRAYS, weights):
        if name == "Q":
            blocks.append((3, value.shape[1], hq))
        elif name in ("O", "F2"):
            blocks.append((value.shape[0] // Z, value.shape[1]))
        else:
            blocks.append((value.shape[0], value.shape[1] // Z))
    rows = Z * TOK

    def act(width, count=Z, kind=BF):
        return vm((count, TOK, width), kind)

    def line(width):
        return vm((2, 3, TOK, width), BF)

    scratch = [vm((2, Z, R) + s, BF) for s in blocks] + [
        vm(lead + s[:-2] + (s[-2] // 2, s[-1]), BF)
        for s in blocks
        for lead in ((Z, R), (2, Z), (Z,), (Z,))
    ]
    scratch += [
        vm((64, 2 * LANE), F32), vm((64, 2 * LANE), BF), vm((Z * R, 64, 2 * LANE), BF), vm((2, 16, adw), F32), vm((64, c_dim), F32), vm((8, d_dim), F32),
        vm((TOK, d_dim), BF), vm((TOK, c_dim), BF), act(d_dim), act(c_dim), act(d_dim), act(c_dim),
        act(d_dim), line(d_dim), act(c_dim), line(c_dim), act(d_dim), line(d_dim),
        act(2 * adw), act(2 * adw, 3), vm((4, 8, dg), F32), vm((4, 8, dg), F32),
        vm((2, rows, 3 * hq), BF), vm((2, hq // HD, Z, TOK, TOK), BF), vm((2, rows, hq), BF),
        vm((2, rows, ffq), BF), vm((2, rows, ffq), BF), vm((2, rows, cfq), BF), vm((2, rows, cfq), BF),
        vm((TOK, c_dim), F32), vm((TOK, LANE), F32), vm((TOK, c_dim), F32), vm((TOK, d_dim), F32), vm((TOK, c_dim), F32),
        vm((2, rows, adw), F32), vm((2, Z, TOK, adw), F32), vm((2, 8, adw), F32), vm((2, 8, adw), F32),
        vm((TOK, d_dim), BF), vm((TOK, c_dim), BF), act(d_dim), act(d_dim), line(d_dim), act(c_dim), line(c_dim),
        act(d_dim), act(c_dim),
        act(d_dim), line(d_dim), act(c_dim), line(c_dim), vm((2, rows, ffq), BF), vm((2, rows, hq), BF),
        vm((2, rows, 3 * hq), BF), vm((2, rows, cfq), BF), vm((TOK, d_dim), F32), vm((TOK, c_dim), F32), vm((2, rows, adw), BF),
        vm((TOK, c_dim), F32),
        vm((Z, 64, c_dim // Z), F32), vm((Z, 64, c_dim // Z), BF), vm((3, 64, c_dim // Z), BF), vm((4, 64, c_dim // Z), F32),
        vm((2, 16, adw), F32), vm((3, 2, 16, adw), F32), vm((Z, 16, adw), F32),
        vm((2 * ffq, rows), BF),
    ]
    dma = pltpu.SemaphoreType.DMA
    na = len(ARRAYS)
    scratch += [
        dma((len(EVENTS), 3)), dma((len(EVENTS), 3)), dma((len(EVENTS), 6)), dma((len(EVENTS), 6)), dma((na, 3)), dma((na, 3)), dma((na,)),
        dma((na, 4, Z)), dma((na, 4, Z)), dma((7,)), dma((7,)), dma, dma, dma((2,)), dma((2,)), dma((Z,)), dma((Z,)), dma, dma,
        dma((4,)), dma((4,)), dma((na, 4, Z)), dma((na, 4, Z)), dma((na, 3)), dma((na, 3)), dma((2, 3)), dma((2, 3)),
        pltpu.SemaphoreType.REGULAR,
    ]
    sds = jax.ShapeDtypeStruct
    out_shape = [sds((2, TOK, d_dim), BF), sds((2, TOK, c_dim), BF)] * 2
    out_shape += [sds(value.shape, BF) for value in weights]
    out_shape += [sds(value.shape, F32) for value in vectors]
    any_spec = pl.BlockSpec(memory_space=pl.ANY)
    vm_spec = pl.BlockSpec(memory_space=pltpu.VMEM)
    sm_spec = pl.BlockSpec(memory_space=pltpu.SMEM)
    return pl.pallas_call(
        functools.partial(main_kernel, sizes, outer),
        out_shape=out_shape,
        in_specs=[any_spec] * na + [vm_spec] * 6 + [sm_spec] * 2 + [vm_spec] * 4,
        out_specs=[vm_spec] * 4 + [any_spec] * na + [vm_spec] * 6,
        scratch_shapes=scratch,
        compiler_params=pltpu.CompilerParams(
            collective_id=0, has_side_effects=True, vmem_limit_bytes=62 * 1024 * 1024
        ),
        cost_estimate=pl.CostEstimate(flops=26 * 10**9, bytes_accessed=10**8, transcendentals=10**7),
        name="layers",
    )(*weights, *vectors, order, train, *streams)


def per_device(
    tokens,
    conv_grid,
    order,
    trainable,
    ln_attn,
    w_qkv,
    w_attn_out,
    ln_mlp,
    w_fc_in,
    w_fc_out,
    conv_depth,
    ln_conv,
    w_pw_in,
    w_pw_out,
    layer_scale,
    w_adapt,
    adapt_depth,
    w_gate_in,
    w_gate_out,
    tok_cot,
    grid_cot,
):
    dp_count = lax.axis_size("dp")
    outer = dp_count // (Z * R)
    groups = [[g * outer + o for o in range(outer)] for g in range(Z * R)]
    layer_at = lax.axis_index("pipe")

    def block(value, axis):
        value = value[0]
        if outer == 1:
            return value
        return lax.all_gather(value, "dp", axis=axis, tiled=True, axis_index_groups=groups)

    def share(value, axis):
        if outer > 1:
            value = lax.psum_scatter(
                value, "dp", scatter_dimension=axis, tiled=True, axis_index_groups=groups
            )
        return value[None]

    qkv = block(w_qkv, 1)
    gate_in = block(w_gate_in, 1).T
    pw_in = block(w_pw_in, 0)
    adapt = block(w_adapt, 0)
    fc_in = block(w_fc_in, 0)
    weights = (
        pw_in,
        block(w_pw_out, 1).T,
        qkv,
        block(w_attn_out, 1),
        adapt,
        gate_in,
        block(w_gate_out, 0),
        fc_in,
        block(w_fc_out, 1),
    )
    vectors = (
        block(conv_depth, 1),
        block(ln_conv, 0)[None],
        block(layer_scale, 0)[None],
        block(ln_attn, 0)[None],
        block(ln_mlp, 0)[None],
        adapt_depth[0],
    )
    spread = Z * R
    sizes = (
        qkv.shape[1] * spread, pw_in.shape[0] * spread, qkv.shape[2] // Z, fc_in.shape[1] // Z,
        pw_in.shape[1] // Z, adapt.shape[1] // Z, gate_in.shape[0] * spread,
    )

    def rows_of(value):
        return value.reshape(value.shape[0], TOK, value.shape[-1])

    streams = [rows_of(value) for value in (tokens, conv_grid, tok_cot, grid_cot)]
    outs = run_layers(weights, vectors, order, trainable, streams, sizes, outer)
    hid_tok, hid_grid, g_tok, g_grid = outs[:4]
    g_p1, g_p2, g_q, g_o, g_e, g_gi, g_go, g_f1, g_f2 = [value.astype(F32) for value in outs[4:13]]
    g_depth, g_ln_conv, g_scale, g_ln_attn, g_ln_mlp, g_ad = outs[13:]

    swap = (layer_at == 0) & (order[0, 0] == 1)
    g_tok = jnp.where(swap, g_tok[::-1], g_tok)
    g_grid = jnp.where(swap, g_grid[::-1], g_grid)
    grid_shape = (1,) + conv_grid.shape
    tok_shape = (1,) + tokens.shape
    flags = trainable[0].astype(F32)
    if outer > 1:
        g_ad = lax.psum(g_ad, "dp", axis_index_groups=groups)
    return (
        hid_tok.reshape(tok_shape),
        hid_grid.reshape(grid_shape),
        g_tok.reshape(tok_shape),
        g_grid.reshape(grid_shape),
        share(g_ln_attn[0], 0),
        share(g_q, 1),
        share(g_o, 1),
        share(g_ln_mlp[0], 0),
        share(g_f1, 0),
        share(g_f2, 1),
        share(g_depth, 1),
        share(g_ln_conv[0], 0),
        share(g_p1 * flags[2], 0),
        share((g_p2 * flags[3]).T, 1),
        share(g_scale[0], 0),
        share(g_e, 0),
        g_ad[None],
        share(g_gi.T, 1),
        share(g_go, 0),
    )


def solution(mesh):
    in_specs = (
        P(None, "dp", None, None),
        P(None, "dp", None, None, None),
        P("dp", None),
        P("pipe", None),
        P("pipe", "dp"),
        P("pipe", None, "dp", "tensor"),
        P("pipe", "tensor", "dp"),
        P("pipe", "dp"),
        P("pipe", "dp", "tensor"),
        P("pipe", "tensor", "dp"),
        P("pipe", None, "dp"),
        P("pipe", "dp"),
        P("pipe", "dp", "tensor"),
        P("pipe", "tensor", "dp"),
        P("pipe", "dp"),
        P("pipe", "dp", "tensor"),
        P("pipe", None, "tensor"),
        P("pipe", "tensor", "dp"),
        P("pipe", "dp", "tensor"),
        P(None, "dp", None, None),
        P(None, "dp", None, None, None),
    )
    out_specs = (
        P("pipe", None, "dp", None, None),
        P("pipe", None, "dp", None, None, None),
        P("pipe", None, "dp", None, None),
        P("pipe", None, "dp", None, None, None),
        P("pipe", "dp"),
        P("pipe", None, "dp", "tensor"),
        P("pipe", "tensor", "dp"),
        P("pipe", "dp"),
        P("pipe", "dp", "tensor"),
        P("pipe", "tensor", "dp"),
        P("pipe", None, "dp"),
        P("pipe", "dp"),
        P("pipe", "dp", "tensor"),
        P("pipe", "tensor", "dp"),
        P("pipe", "dp"),
        P("pipe", "dp", "tensor"),
        P("pipe", None, "tensor"),
        P("pipe", "tensor", "dp"),
        P("pipe", "dp", "tensor"),
    )
    return jax.shard_map(
        per_device, mesh=mesh, in_specs=in_specs, out_specs=out_specs, check_vma=False
    )
```

```python
import functools

import jax
import jax.numpy as jnp
from jax import lax
from jax.experimental import pallas as pl
from jax.experimental.pallas import tpu as pltpu
from jax.sharding import PartitionSpec as P

HD = 64
Z = 4
R = 2
TOK = 64
SIDE = 8
LANE = 128
BF = jnp.bfloat16
F32 = jnp.float32
ARRAYS = ("P1", "P2", "Q", "O", "E", "Gi", "Go", "F1", "F2")
EVENTS = (
    "n1", "f", "o", "cv", "n2", "c2", "m", "br", "gs",
    "dx3", "dgh", "dn2", "dc2", "dx1", "dcv", "dn1", "df", "gv", "gad",
)


def mm(a, b):
    return lax.dot_general(a, b, (((1,), (0,)), ((), ())), preferred_element_type=F32)


def mm_nt(a, b):
    return lax.dot_general(a, b, (((1,), (1,)), ((), ())), preferred_element_type=F32)


def mm_tn(a, b):
    return lax.dot_general(a, b, (((0,), (0,)), ((), ())), preferred_element_type=F32)


def flat(value):
    return value.reshape(-1, value.shape[-1])


def low(value):
    return value.astype(BF)


def wide(value):
    return value.astype(F32)


def gelu_pair(h):
    phi = 0.5 * (1.0 + lax.erf(h * 0.7071067811865476))
    dens = jnp.exp(-0.5 * h * h) * 0.3989422804014327
    return h * phi, phi + h * dens


def normed(value):
    centred = value - jnp.mean(value, axis=-1, keepdims=True)
    rs = lax.rsqrt(jnp.mean(centred * centred, axis=-1, keepdims=True) + 1e-06)
    return centred * rs, rs


def norm_back(dn, n_hat, rs, gain):
    gd = dn * gain
    return (
        gd
        - jnp.mean(gd, axis=-1, keepdims=True)
        - n_hat * jnp.mean(gd * n_hat, axis=-1, keepdims=True)
    ) * rs


def col_shift(value, by):
    if by == 0:
        return value
    at = lax.broadcasted_iota(jnp.int32, value.shape, 0) % SIDE
    rolled = pltpu.roll(value, (-by) % TOK, 0)
    return jnp.where((at + by >= 0) & (at + by < SIDE), rolled, 0.0)


def row_shift(value, by):
    if by == 0:
        return value
    gap = jnp.zeros((abs(by) * SIDE, value.shape[1]), value.dtype)
    if by > 0:
        return jnp.concatenate([value[by * SIDE :], gap], axis=0)
    return jnp.concatenate([gap, value[: TOK + by * SIDE]], axis=0)


def depthwise(value, tap, side):
    half = side // 2
    shifted = [col_shift(value, b - half) for b in range(side)]
    total = None
    for a in range(side):
        line = None
        for b in range(side):
            term = shifted[b] * tap(a * side + b)
            line = term if line is None else line + term
        line = row_shift(line, a - half)
        total = line if total is None else total + line
    return total


def depthwise_taps(value, grad, side, put):
    half = side // 2
    shifted = [col_shift(value, b - half) for b in range(side)]
    for a in range(side):
        d = a - half
        lo, hi = max(0, -d) * SIDE, (SIDE - max(0, d)) * SIDE
        for b in range(side):
            part = shifted[b][lo + d * SIDE : hi + d * SIDE] * grad[lo:hi]
            put(a * side + b, jnp.sum(part, axis=0, keepdims=True))


def lanes_of(at, width):
    return pl.ds(pl.multiple_of(at * width, width), width)


def side_by_side(blocks):
    return jnp.concatenate(blocks, axis=1)


def main_kernel(dims, outer, *refs):
    at = iter(refs)

    def take(count):
        return [next(at) for _ in range(count)]

    na = len(ARRAYS)
    source = dict(zip(ARRAYS, take(na)))
    (
        depth_in, ln_conv_in, scale_in, ln_attn_in, ln_mlp_in, adapt_depth_in,
        order_in, train_in, tok_in, grid_in, tcot_in, gcot_in,
    ) = take(12)
    hid_tok, hid_grid, out_gtok, out_ggrid = take(4)
    native = dict(zip(ARRAYS, take(na)))
    out_depth, out_ln_conv, out_scale, out_ln_attn, out_ln_mlp, out_ad = take(6)
    W = dict(zip(ARRAYS, take(na)))
    hops = take(4 * na)
    RX = {name: hops[4 * n : 4 * n + 4] for n, name in enumerate(ARRAYS)}
    (
        v_loc, v_low, vv, aq, vec_c, vec_d, x_in, c_in, n1_all, f_all, n2_all, c2_all,
        o_sb, o_rb, cv_sb, cv_rb, m_sb, m_rb, br_sb, br_rb, gsb, dgb,
        qkv, prob, ctx, u, up, r, rp, cn, crs, cv_sum, x1, c2f,
        adapted, spread, pooled, gate,
        dx3, dcot, dx3_all, dn2_sb, dn2_rb, dc2_sb, dc2_rb, dx1_all, dcv_all,
        dn1_sb, dn1_rb, df_sb, df_rb, dh, do_all, dqkv, dhc, dx1, dc2t, dad, dcn,
        gvs, gvs_low, gv_rb, gvx, gad, gad_rb, gad_all, turned,
    ) = take(67)
    (
        zs_send, zs_recv, l_send, l_recv, s1_send, s1_recv, loc_sem, s2_send, s2_recv,
        v_send, v_recv, q_send, q_recv, h_send, h_recv, b_send, b_recv, c_send, c_recv,
        xo_send, xo_recv, g_send, g_recv, a_send, a_recv, gx_send, gx_recv, go,
    ) = take(28)

    p = lax.axis_index("pipe")
    dpi = lax.axis_index("dp")
    x = lax.axis_index("tensor")
    rest = dpi % outer
    zi = dpi // (outer * R)
    ri = (dpi // outer) % R
    xo = 1 - x
    ro = 1 - ri
    d_dim, c_dim, hq, ffq, cfq, adq, dg = dims
    adh = Z * adq
    dz, cz = d_dim // Z, c_dim // Z
    tile = 256
    ids = {name: number for number, name in enumerate(ARRAYS)}
    ev = {name: number for number, name in enumerate(EVENTS)}

    def dev(z=None, rr=None, xx=None, pp=None):
        z = zi if z is None else z
        rr = ri if rr is None else rr
        return (
            p if pp is None else pp,
            (z * R + rr) * outer + rest,
            x if xx is None else xx,
        )

    def zto(d):
        return lax.rem(zi + d, Z)

    def zfrom(d):
        return lax.rem(zi + Z - d, Z)

    def remote(src, dst, ssem, rsem, device):
        return pltpu.make_async_remote_copy(
            src_ref=src, dst_ref=dst, send_sem=ssem, recv_sem=rsem,
            device_id=device, device_id_type=pl.DeviceIdType.MESH,
        )

    sib = dev(pp=1 - p)
    over_r, over_x = dev(rr=ro), dev(xx=xo)

    def z_copy(e, d, src, dst):
        return remote(src, dst, zs_send.at[e, d - 1], zs_recv.at[e, d - 1], dev(zto(d)))

    sent = []

    def gather_copies(name, buf):
        return [z_copy(ev[name], d, buf.at[zi], buf.at[zi]) for d in range(1, Z)]

    def gather_start(name, buf, keep=True):
        copies = gather_copies(name, buf)
        for c in copies:
            c.start()
        if keep:
            sent.extend(copies)

    def gather_wait(name, buf):
        for d in range(1, Z):
            slot = buf.at[zfrom(d)]
            z_copy(ev[name], d, slot, slot).wait_recv()

    def scatter_start(name, sb, rb):
        for d in range(1, Z):
            c = z_copy(ev[name], d, sb.at[zto(d)], rb.at[d - 1])
            c.start()
            sent.append(c)

    def scatter_wait(name, rb):
        for d in range(1, Z):
            z_copy(ev[name], d, rb.at[d - 1], rb.at[d - 1]).wait_recv()

    def right():
        return dev(zi + 1)

    def left():
        return dev(zi - 1)

    def pass_copy(name, buf, toward, s):
        e, k = ev[name], (0 if toward > 0 else 3) + s
        blk = buf.at[zi - toward * s]
        return remote(blk, blk, l_send.at[e, k], l_recv.at[e, k], right() if toward > 0 else left())

    def pass_cond(toward, s):
        if toward > 0:
            return (zi < Z - 1) & (zi - s >= 0)
        return (zi > 0) & (zi + s <= Z - 1)

    def line_start(name, buf):
        for toward in (1, -1):

            @pl.when(pass_cond(toward, 0))
            def _():
                pass_copy(name, buf, toward, 0).start()

    def line_step(name, buf, *steps):
        e = ev[name]
        for s in steps:
            for toward in (1, -1):
                src = zi - toward * s

                @pl.when((src >= 0) & (src <= Z - 1))
                def _():
                    blk = buf.at[src]
                    k = (0 if toward > 0 else 3) + s - 1
                    remote(blk, blk, l_send.at[e, k], l_recv.at[e, k], sib).wait_recv()

                if s < Z - 1:

                    @pl.when(pass_cond(toward, s))
                    def _():
                        pass_copy(name, buf, toward, s).start()

    def line_sent(name, buf):
        for toward in (1, -1):
            for s in range(Z - 1):

                @pl.when(pass_cond(toward, s))
                def _():
                    pass_copy(name, buf, toward, s).wait_send()

    def sum_copy(name, sb, rb, toward, k, first):
        e, way = ev[name], (0 if toward > 0 else 1)
        src = sb.at[zi + toward * k] if first else rb.at[way, k]
        q = way * 3 + k - 1
        return remote(src, rb.at[way, k - 1], l_send.at[e, q], l_recv.at[e, q], right() if toward > 0 else left())

    def at_end(toward):
        return zi == (0 if toward > 0 else Z - 1)

    def passes(toward, k):
        dest = zi + toward * k
        return jnp.logical_not(at_end(toward)) & (dest >= 0) & (dest <= Z - 1)

    def sum_start(name, sb, rb):
        for toward in (1, -1):

            @pl.when(at_end(toward))
            def _():
                for k in (3, 2, 1):
                    sum_copy(name, sb, rb, toward, k, True).start()

    def sum_arrival(name, rb, way, k):
        e = ev[name]
        slot = rb.at[way, k]
        return remote(slot, slot, l_send.at[e, way * 3 + k], l_recv.at[e, way * 3 + k], sib)

    def sum_step(name, sb, rb, *ks):
        for k in ks:
            for way, toward in enumerate((1, -1)):

                @pl.when(passes(toward, k))
                def _():
                    sum_arrival(name, rb, way, k).wait_recv()
                    rb[way, k] = low(wide(rb[way, k]) + wide(sb[zi + toward * k]))
                    sum_copy(name, sb, rb, toward, k, False).start()

    def sum_wait(name, rb):
        for way, toward in enumerate((1, -1)):

            @pl.when(jnp.logical_not(at_end(toward)))
            def _():
                sum_arrival(name, rb, way, 0).wait_recv()

    def summed(sb, rb):
        return wide(sb[zi]) + (wide(rb[0, 0]) + wide(rb[1, 0]))

    def sum_sent(name, sb, rb):
        for toward in (1, -1):

            @pl.when(at_end(toward))
            def _():
                for k in (3, 2, 1):
                    sum_copy(name, sb, rb, toward, k, True).wait_send()

            for k in (2, 1):

                @pl.when(passes(toward, k))
                def _():
                    sum_copy(name, sb, rb, toward, k, False).wait_send()

    def share_start(name, buf):
        for d in range(1, Z):
            c = z_copy(ev[name], d, buf.at[3], buf.at[d - 1])
            c.start()
            sent.append(c)

    def scattered(sb, rb):
        return (wide(sb[zi]) + wide(rb[0])) + (wide(rb[1]) + wide(rb[2]))

    barrier = pltpu.get_barrier_semaphore()
    greeted = [sib]
    for d in range(1, Z):
        greeted += [dev(zto(d)), dev(zto(d), ro), dev(zto(d), pp=1 - p)]
    greeted += [over_r, over_x, dev(rr=ro, xx=xo)]
    for device in greeted:
        pl.semaphore_signal(barrier, inc=1, device_id=device, device_id_type=pl.DeviceIdType.MESH)
    v_loc[...] = jnp.zeros(v_loc.shape, F32)
    taps7 = depth_in.shape[0]
    c_own = depth_in.shape[1]
    v_loc[0:taps7, 0:c_own] = wide(depth_in[...])
    v_loc[49:50, 0:c_own] = wide(ln_conv_in[...])
    v_loc[50:51, 0:c_own] = wide(scale_in[...])
    v_loc[56:57, 0:LANE] = wide(ln_attn_in[...])
    v_loc[57:58, 0:LANE] = wide(ln_mlp_in[...])
    aq[x] = jnp.zeros(aq.shape[1:], F32)
    aq[x, 0:9] = wide(adapt_depth_in[:, lanes_of(zi, adq)])
    v_low[...] = low(v_loc[...])
    line_sums = (
        ("o", o_sb, o_rb), ("cv", cv_sb, cv_rb), ("m", m_sb, m_rb), ("dn2", dn2_sb, dn2_rb),
        ("dc2", dc2_sb, dc2_rb), ("dn1", dn1_sb, dn1_rb), ("df", df_sb, df_rb),
    )
    line_gathers = (
        ("n1", n1_all), ("f", f_all), ("n2", n2_all), ("c2", c2_all), ("dx1", dx1_all), ("dcv", dcv_all),
    )
    for _, _, rb in line_sums:
        for way, toward in enumerate((1, -1)):

            @pl.when(at_end(toward))
            def _():
                rb[way, 0] = jnp.zeros(rb.shape[2:], BF)

    pl.semaphore_wait(barrier, len(greeted))

    me8 = zi * R + ri
    v_arrivals = []
    for n, (d, flip) in enumerate([(d, s) for d in range(Z) for s in (0, 1)][1:]):
        tr = ro if flip else ri
        c = remote(v_low, vv.at[me8], v_send.at[n], v_recv.at[n], dev(zto(d), tr))
        c.start()
        sent.append(c)
        fr = zfrom(d) * R + tr
        v_arrivals.append(remote(vv.at[fr], vv.at[fr], v_send.at[n], v_recv.at[n], dev(zto(d), tr)))
    vv[me8] = v_low[...]
    c = remote(aq.at[x], aq.at[x], q_send, q_recv, over_x)
    c.start()
    sent.append(c)

    by_rows = ("O", "F2")

    def quarter_of(name, ref, z):
        if name == "Q":
            return ref.at[:, :, lanes_of(z, hq)]
        if name in by_rows:
            height = ref.shape[0] // Z
            return ref.at[pl.ds(pl.multiple_of(z * height, height), height)]
        return ref.at[:, lanes_of(z, ref.shape[1] // Z)]

    def step1_local(name):
        return pltpu.make_async_copy(
            quarter_of(name, source[name], zi), W[name].at[x, zi, ri], loc_sem.at[ids[name]]
        )

    def step1_copy(name, d):
        k = ids[name]
        return remote(
            quarter_of(name, source[name], zto(d)), W[name].at[x, zi, ri],
            s1_send.at[k, d - 1], s1_recv.at[k, d - 1], dev(zto(d)),
        )

    def half_of(name, j, z, rr, upper):
        w = W[name]
        half = w.shape[-2] // 2
        rows = slice(half, None) if upper else slice(0, half)
        if len(w.shape) == 6:
            return w.at[j, z, rr, :, rows]
        return w.at[j, z, rr, rows]

    def step2_copy(name, which, d):
        k = ids[name]
        z = zfrom(d)
        if which < 2:
            src = quarter_of(name, source[name], zi) if d == 0 else W[name].at[x, z, ri]
            dst = W[name].at[x, z, ri]
        else:
            src = dst = half_of(name, x, z, ro, False) if which == 2 else half_of(name, xo, z, ri, True)
        to = over_x if which in (1, 2) else over_r
        return remote(src, dst, s2_send.at[k, which, d], s2_recv.at[k, which, d], to)

    def step2_arrival(name, which, d):
        k = ids[name]
        z = zfrom(d)
        if which < 2:
            ref = W[name].at[x, z, ro] if which == 0 else W[name].at[xo, z, ri]
        else:
            ref = half_of(name, xo, z, ro, which == 3)
        to = over_x if which in (1, 2) else over_r
        return remote(ref, ref, s2_send.at[k, which, d], s2_recv.at[k, which, d], to)

    def relay1(*names):
        for name in names:
            for d in range(1, Z):
                step1_copy(name, d).start()

    def relay0(*names):
        for name in names:
            step1_local(name).start()
            step2_copy(name, 0, 0).start()
            step2_copy(name, 1, 0).start()

    def relay2(name, ds=(1, 2, 3)):
        k = ids[name]
        for d in ds:
            slot = W[name].at[x, zfrom(d), ri]
            remote(slot, slot, s1_send.at[k, d - 1], s1_recv.at[k, d - 1], dev(zto(d))).wait_recv()
            step2_copy(name, 0, d).start()
            step2_copy(name, 1, d).start()

    def relay3(name, ds=(0, 1, 2, 3)):
        for d in ds:
            step2_arrival(name, 0, d).wait_recv()
            step2_copy(name, 2, d).start()
            step2_arrival(name, 1, d).wait_recv()
            step2_copy(name, 3, d).start()

    def relay4(*names):
        for name in names:
            step1_local(name).wait()
            for d in range(Z):
                step2_arrival(name, 2, d).wait_recv()
                step2_arrival(name, 3, d).wait_recv()

    def relay_sent():
        for name in ARRAYS:
            for d in range(1, Z):
                step1_copy(name, d).wait_send()
            for which in range(4):
                for d in range(Z):
                    step2_copy(name, which, d).wait_send()

    @pl.when(p == 0)
    def _():
        relay0("P1")
        relay1("P1")
        relay0("P2")
        relay1("P2")
        relay0("Q", "O", "E", "Gi", "Go", "F1", "F2")

    @pl.when(p == 1)
    def _():
        dx3[...] = tcot_in[x]
        dcot[...] = gcot_in[x]
        dx3_all[zi] = tcot_in[x]
        line_start("dx3", dx3_all)

    for c in v_arrivals:
        c.wait_recv()
    remote(aq.at[xo], aq.at[xo], q_send, q_recv, over_x).wait_recv()
    low_lanes = lax.broadcasted_iota(jnp.int32, (64, LANE), 1) < LANE // 2
    for z in range(Z):
        first, second = wide(vv[2 * z]), pltpu.roll(wide(vv[2 * z + 1]), LANE // 2, 1)
        vec_c[:, z * cz : z * cz + LANE] = first[:, 0:LANE]
        vec_c[:, z * cz + LANE : z * cz + 2 * LANE] = jnp.where(
            low_lanes, first[:, LANE:], second[:, 0:LANE]
        )
        vec_c[:, z * cz + 2 * LANE : (z + 1) * cz] = second[:, LANE:]
    for i in range(Z * R):
        vec_d[:, i * LANE : (i + 1) * LANE] = wide(vv[i])[56:64, 0:LANE]

    def gain_d(row):
        return vec_d[row : row + 1, :]

    def gain_c(row):
        return vec_c[row : row + 1, :]

    def token_entry():
        n_hat, _ = normed(wide(x_in[...]))
        n1_all[zi] = low(n_hat * gain_d(0))
        line_start("n1", n1_all)

    def conv_entry():
        @pl.loop(0, c_dim // LANE)
        def _(ch):
            lanes = lanes_of(ch, LANE)
            taps = vec_c[:, lanes]
            cn[:, lanes] = depthwise(wide(c_in[:, lanes]), lambda k: taps[k : k + 1], 7)

        n_hat, rs = normed(cn[...])
        cn[...] = n_hat
        crs[...] = jnp.broadcast_to(rs, crs.shape)
        f_all[zi] = low(n_hat * gain_c(49))
        line_start("f", f_all)

    def first_relays(pump):
        relay2("P1")
        pump(1)
        relay1("Q", "O")
        relay2("P2")
        pump(2)
        relay3("P1")


    @pl.when(p == 0)
    def _():
        first = order_in[0, x] == 0
        c_in[...] = jnp.where(first, grid_in[0], grid_in[1])
        x_in[...] = jnp.where(first, tok_in[0], tok_in[1])
        conv_entry()
        token_entry()

        def pump(s):
            line_step("f", f_all, s)
            line_step("n1", n1_all, s)

        first_relays(pump)
        line_step("f", f_all, 3)
        line_step("n1", n1_all, 3)

    @pl.when(p == 1)
    def _():
        pl.semaphore_wait(go, 1)
        relay0("P1")
        relay1("P1")
        relay0("P2")
        relay1("P2")
        relay0("Q", "O", "E", "Gi", "Go", "F1", "F2")
        first_relays(lambda s: line_step("dx3", dx3_all, s))
        remote(c_in, c_in, h_send.at[1], h_recv.at[1], sib).wait_recv()
        conv_entry()
        line_step("dx3", dx3_all, 3)
        line_step("f", f_all, 1)

    relay2("Q")
    relay2("O")
    relay1("E", "Gi", "Go")
    relay3("P2", (0, 1))

    @pl.when(p == 1)
    def _():
        line_step("f", f_all, 2, 3)

    relay4("P1")

    def conv_hidden(j):
        act, der = gelu_pair(mm(flat(f_all[...]), flat(W["P1"][j])))
        r[j] = low(act)
        rp[j] = low(der)

    conv_hidden(0)

    relay3("P2", (2, 3))
    for name in ("E", "Gi", "Go"):
        relay2(name)
    relay1("F1")
    conv_hidden(1)
    relay3("Q")
    relay3("O")
    relay2("F1")
    relay1("F2")

    @pl.when(p == 0)
    def _():
        pl.semaphore_signal(go, inc=1, device_id=sib, device_id_type=pl.DeviceIdType.MESH)

    relay4("P2")

    def pair_rows(name, pair):
        zs = pl.ds(pair * 2, 2)
        return side_by_side([flat(W[name][0, zs]), flat(W[name][1, zs])])

    def pair_out(left, name, sb, width):
        both = side_by_side([left[0], left[1]])

        @pl.loop(0, Z // 2)
        def _(pair):
            acc = mm_nt(both, pair_rows(name, pair))
            sb[:, :, lanes_of(pair, 2 * width)] = low(acc).reshape(Z, TOK, 2 * width)

    pair_out(r, "P2", cv_sb, cz)

    sum_start("cv", cv_sb, cv_rb)

    for name in ("E", "Gi", "Go"):
        relay3(name)
    sum_step("cv", cv_sb, cv_rb, 2)
    relay2("F2")
    sum_step("cv", cv_sb, cv_rb, 1)

    @pl.when(p == 1)
    def _():
        remote(x_in, x_in, h_send.at[0], h_recv.at[0], sib).wait_recv()
        token_entry()
        line_step("n1", n1_all, 1, 2, 3)

    relay4("Q", "O")
    wide_q = side_by_side([flat(W["Q"][j, :, :, s]) for j in range(2) for s in range(3)])
    qkv_both = low(mm(flat(n1_all[...]), wide_q))
    for j in range(2):
        qkv[j] = qkv_both[:, j * 3 * hq : (j + 1) * 3 * hq]
    for j in range(2):
        for b in range(Z):
            rows = slice(b * TOK, (b + 1) * TOK)
            outs = []
            for h in range(hq // HD):
                q, kk, vals = (qkv[j, rows, s * hq + h * HD : s * hq + (h + 1) * HD] for s in range(3))
                sc = mm_nt(q, kk) * HD ** (-0.5)
                e = jnp.exp(sc - jnp.max(sc, axis=-1, keepdims=True))
                pr = low(e / jnp.sum(e, axis=-1, keepdims=True))
                prob[j, h, b] = pr
                outs.append(mm(pr, vals))
            ctx[j, rows, :] = low(side_by_side(outs))

    out_cols = [
        jnp.concatenate([W["O"][0, z, rr], W["O"][1, z, rr]], axis=0) for z in range(Z) for rr in range(R)
    ]
    o_sb[...] = low(mm(side_by_side([ctx[0], ctx[1]]), side_by_side(out_cols))).reshape(Z, TOK, d_dim)
    sum_start("o", o_sb, o_rb)

    relay3("F1")

    sum_wait("cv", cv_rb)
    cv_sum[...] = summed(cv_sb, cv_rb)
    c2f[...] = wide(c_in[...]) + gain_c(50) * cv_sum[...]
    c2_low = low(c2f[...])
    c2_all[zi] = c2_low
    line_start("c2", c2_all)
    sum_step("o", o_sb, o_rb, 2)
    hid_grid[x] = c2_low

    @pl.when(p == 0)
    def _():
        remote(hid_grid.at[x], c_in, h_send.at[1], h_recv.at[1], sib).start()

    relay3("F2")
    sum_step("o", o_sb, o_rb, 1)
    line_step("c2", c2_all, 1)
    sum_wait("o", o_rb)
    x1[...] = wide(x_in[...]) + summed(o_sb, o_rb)
    n_hat, _ = normed(x1[...])
    n2_all[zi] = low(n_hat * gain_d(1))
    line_start("n2", n2_all)

    relay4("E", "Gi", "Go")
    line_step("c2", c2_all, 2)
    line_step("n2", n2_all, 1)
    line_step("c2", c2_all, 3)
    row8 = lax.broadcasted_iota(jnp.int32, (8, adq), 0)
    gs_part = None
    ad_both = mm(flat(c2_all[...]), side_by_side([flat(W["E"][0]), flat(W["E"][1])]))
    for j in range(2):
        ad = ad_both[:, j * adq : (j + 1) * adq]
        adapted[j] = ad
        taps = aq[j]
        pool = jnp.zeros((8, adq), F32)
        for b in range(Z):
            sp = depthwise(ad[b * TOK : (b + 1) * TOK], lambda k: taps[k : k + 1], 3)
            spread[j, b] = sp
            pool = jnp.where(row8 == b, jnp.mean(sp, axis=0, keepdims=True), pool)
        pooled[j] = pool
        term = mm_nt(low(pool), flat(W["Gi"][j]))
        gs_part = term if gs_part is None else gs_part + term
    gsb[3] = gs_part
    share_start("gs", gsb)
    line_step("n2", n2_all, 2)

    relay4("F1")
    line_step("n2", n2_all, 3)
    for j in range(2):
        act, der = gelu_pair(mm(flat(n2_all[...]), flat(W["F1"][j])))
        u[j] = low(act)
        up[j] = low(der)

    scatter_wait("gs", gsb)

    def gate_hidden():
        return gelu_pair((gsb[0] + gsb[1]) + (gsb[2] + gsb[3]))

    gh, _ = gate_hidden()
    for j in range(2):
        g8 = jnp.tanh(mm(low(gh), flat(W["Go"][j])))
        gate[j] = g8
        for b in range(Z):
            br_sb[b, :, j * adq : (j + 1) * adq] = low(g8[b : b + 1] * spread[j, b])
    scatter_start("br", br_sb, br_rb)
    relay4("F2")

    u_both = side_by_side([u[0], u[1]])

    @pl.loop(0, Z // 2)
    def _(pair):
        halves = [
            side_by_side([W["F2"][j, 2 * pair + dz_, rr] for dz_ in range(2) for rr in range(R)])
            for j in range(2)
        ]
        acc = mm(u_both, jnp.concatenate(halves, axis=0))
        m_sb[:, :, lanes_of(pair, 2 * dz)] = low(acc).reshape(Z, TOK, 2 * dz)

    sum_start("m", m_sb, m_rb)

    def exchange(n, buf):
        remote(buf.at[x], buf.at[x], xo_send.at[n], xo_recv.at[n], over_x).start()

    def layer_output(total):
        sum_step("m", m_sb, m_rb, 2)
        scatter_wait("br", br_rb)
        total[...] = x1[...]
        for d in range(Z):
            piece = br_sb[zi] if d == 0 else br_rb[d - 1]
            for j in range(2):
                lanes = pl.ds(pl.multiple_of(j * adh + zfrom(d) * adq, LANE), adq)
                total[:, lanes] += wide(piece[:, j * adq : (j + 1) * adq])
        sum_step("m", m_sb, m_rb, 1)
        sum_wait("m", m_rb)
        hid_tok[x] = low(total[...] + summed(m_sb, m_rb))

    @pl.when(p == 0)
    def _():
        layer_output(dx1)
        remote(hid_tok.at[x], x_in, h_send.at[0], h_recv.at[0], sib).start()
        exchange(0, hid_tok)

    exchange(1, hid_grid)
    relay_sent()

    def over_cores(d):
        return remote(
            out_gtok.at[x], dx3_all.at[zi], b_send.at[d], b_recv.at[d], dev(zto(d), pp=1 - p)
        )

    @pl.when(p == 0)
    def _():
        for d in range(Z):
            slot = dx3_all.at[zfrom(d)]
            remote(slot, slot, b_send.at[d], b_recv.at[d], sib).wait_recv()
        dx3[...] = dx3_all[zi]

    def own_lanes(j):
        return pl.ds(pl.multiple_of(j * adh + zi * adq, LANE), adq)

    gh, ghp = gate_hidden()
    dgh_part = None
    dgp = []
    for j in range(2):
        dgate = jnp.zeros((8, adq), F32)
        for b in range(Z):
            dbr = wide(dx3_all[b, :, own_lanes(j)])
            dgate = jnp.where(row8 == b, jnp.sum(dbr * spread[j, b], axis=0, keepdims=True), dgate)
        dg8 = low(dgate * (1.0 - gate[j] * gate[j]))
        dgp.append(dg8)
        term = mm_nt(dg8, flat(W["Go"][j]))
        dgh_part = term if dgh_part is None else dgh_part + term
    dgb[3] = dgh_part
    share_start("dgh", dgb)

    for j in range(2):
        cols = side_by_side([W["F2"][j, z, rr] for z in range(Z) for rr in range(R)])
        dh[j] = low(mm_nt(flat(dx3_all[...]), cols) * wide(up[j]))

    scatter_wait("dgh", dgb)
    dgs = low(((dgb[0] + dgb[1]) + (dgb[2] + dgb[3])) * ghp)
    for j in range(2):
        dpool = mm(dgs, flat(W["Gi"][j])) * (1.0 / TOK)
        taps = aq[j]
        tap_rows = [None] * 9
        for b in range(Z):
            dsp = gate[j, b : b + 1] * wide(dx3_all[b, :, own_lanes(j)]) + dpool[b : b + 1]
            dad[j, b * TOK : (b + 1) * TOK] = low(depthwise(dsp, lambda k: taps[8 - k : 9 - k], 3))

            def put(k, row):
                tap_rows[k] = row if tap_rows[k] is None else tap_rows[k] + row

            depthwise_taps(adapted[j, b * TOK : (b + 1) * TOK], dsp, 3, put)
        for k in range(9):
            gad[j, k : k + 1] = tap_rows[k]
        gad[j, 9:16] = jnp.zeros((7, adq), F32)

    pair_out(dad, "E", dc2_sb, cz)

    sum_start("dc2", dc2_sb, dc2_rb)

    pair_out(dh, "F1", dn2_sb, dz)

    sum_start("dn2", dn2_sb, dn2_rb)
    sum_step("dc2", dc2_sb, dc2_rb, 2)

    def half_rows(name, upper):
        half = W[name].shape[-2] // 2
        rows = slice(half, None) if upper else slice(0, half)
        return (slice(None), rows) if len(W[name].shape) == 6 else (rows,)

    fine = ("P1", "P2")

    def pieces(name):
        return (1, 2, 3, 0) if name in fine else (None,)

    def block_at(d):
        return slice(None) if d is None else zto(d)

    def hop_copy(name, which, d):
        n = ids[name]
        lower, upper = half_rows(name, False), half_rows(name, True)
        z = block_at(d)
        w, buf = W[name], RX[name]
        src, dst, to = (
            lambda: (w.at[(xo, z, slice(None)) + lower], buf[0].at[z], over_x),
            lambda: (w.at[(slice(None), z, ro) + upper], buf[1].at[:, z], over_r),
            lambda: (buf[0].at[z, ro], buf[2].at[z], over_r),
            lambda: (buf[1].at[xo, z], buf[3].at[z], over_x),
        )[which]()
        k = 0 if d is None else d
        return remote(src, dst, g_send.at[n, which, k], g_recv.at[n, which, k], to)

    def reduce_start(name, d=None):
        hop_copy(name, 0, d).start()
        hop_copy(name, 1, d).start()

    def each_block(d, body):
        if d is None:
            pl.loop(0, Z)(body)
        else:
            body(zto(d))

    def reduce_middle(*names):
        for name in names:
            lower, upper = half_rows(name, False), half_rows(name, True)
            buf = RX[name]
            for d in pieces(name):
                hop_copy(name, 0, d).wait_recv()

                def add_lower(z):
                    for rr in range(R):
                        own = W[name][(x, z, rr) + lower]
                        buf[0][z, rr] = low(wide(own) + wide(buf[0][z, rr]))

                each_block(d, add_lower)
                hop_copy(name, 2, d).start()
                hop_copy(name, 1, d).wait_recv()

                def add_upper(z):
                    for j in range(2):
                        own = W[name][(j, z, ri) + upper]
                        buf[1][j, z] = low(wide(own) + wide(buf[1][j, z]))

                each_block(d, add_upper)
                hop_copy(name, 3, d).start()

    def reduce_end(*names):
        for name in names:
            lower, upper = half_rows(name, False), half_rows(name, True)
            buf = RX[name]
            for d in pieces(name):
                hop_copy(name, 2, d).wait_recv()
                hop_copy(name, 3, d).wait_recv()

                def add_both(z):
                    W[name][(x, z, ri) + lower] = low(wide(buf[0][z, ri]) + wide(buf[2][z]))
                    W[name][(x, z, ri) + upper] = low(wide(buf[1][x, z]) + wide(buf[3][z]))

                each_block(d, add_both)
                for k in range(Z) if d is None else (d,):
                    (back_copy(name, k) if k else back_local(name)).start()

    def back_copy(name, d):
        n = ids[name]
        return remote(
            W[name].at[x, zto(d), ri], quarter_of(name, native[name], zi),
            a_send.at[n, d - 1], a_recv.at[n, d - 1], dev(zto(d)),
        )

    def back_local(name):
        return pltpu.make_async_copy(
            W[name].at[x, zi, ri], quarter_of(name, native[name], zi), loc_sem.at[ids[name]]
        )

    peers = ((1, 0), (0, 1), (1, 1))

    def owner(k):
        return (ro if peers[k][0] else ri), (xo if peers[k][1] else x)

    def row_grad(name, left, right):
        width = W[name].shape[3]
        span = R * width
        for k, d in enumerate((1, 2, 3, 0)):
            z = zto(d)
            half = (k % 2) * span
            turned[half : half + span] = flat(left[:, :, lanes_of(z, span)]).T
            for j in range(2):
                W[name][j, z] = low(mm(turned[half : half + span], right[j])).reshape(R, width, -1)
            if name in fine:
                reduce_start(name, d)
        if name not in fine:
            reduce_start(name)

    def col_grad(name, left, right):
        width = left.shape[2]
        for j in range(2):
            turned[j * width : (j + 1) * width] = left[j].T
        for d in (1, 2, 3, 0):
            z = zto(d)
            rhs = flat(right[:, :, lanes_of(z, dz)])
            for j in range(2):
                g = low(mm(turned[j * width : (j + 1) * width], rhs))
                for rr in range(R):
                    W[name][j, z, rr] = g[:, rr * LANE : (rr + 1) * LANE]
            if name in fine:
                reduce_start(name, d)
        if name not in fine:
            reduce_start(name)

    for j in range(2):
        W["Gi"][j] = low(mm_tn(dgs, low(pooled[j]))).reshape(Z, R, -1, adq)
        W["Go"][j] = low(mm_tn(low(gh), dgp[j])).reshape(Z, R, -1, adq)
    sum_step("dc2", dc2_sb, dc2_rb, 1)
    sum_step("dn2", dn2_sb, dn2_rb, 2)
    reduce_start("Gi")
    reduce_start("Go")
    row_grad("E", c2_all, dad)
    sum_step("dn2", dn2_sb, dn2_rb, 1)

    @pl.when(p == 0)
    def _():
        remote(dcot, dcot, c_send, c_recv, sib).wait_recv()

    sum_wait("dc2", dc2_rb)
    dc2t[...] = wide(dcot[...]) + summed(dc2_sb, dc2_rb)
    gvs_ls = jnp.sum(cv_sum[...] * dc2t[...], axis=0, keepdims=True)
    dcv_all[zi] = low(dc2t[...] * gain_c(50))
    line_start("dcv", dcv_all)

    sum_wait("dn2", dn2_rb)
    dn2 = summed(dn2_sb, dn2_rb)
    n_hat, rs = normed(x1[...])
    gvs_d1 = jnp.sum(dn2 * n_hat, axis=0, keepdims=True)
    dx1[...] = wide(dx3[...]) + norm_back(dn2, n_hat, rs, gain_d(1))
    dx1_all[zi] = low(dx1[...])
    line_start("dx1", dx1_all)
    line_step("dcv", dcv_all, 1)
    col_grad("F2", u, dx3_all)
    line_step("dcv", dcv_all, 2)
    line_step("dx1", dx1_all, 1)
    row_grad("F1", n2_all, dh)

    line_step("dcv", dcv_all, 3)
    line_step("dx1", dx1_all, 2)
    for j in range(2):
        dhc[j] = low(mm(flat(dcv_all[...]), flat(W["P2"][j])) * wide(rp[j]))

    pair_out(dhc, "P1", df_sb, cz)

    sum_start("df", df_sb, df_rb)

    early = ("Gi", "Go", "E", "F2", "F1")

    def pw_grads():
        row_grad("P2", dcv_all, r)
        row_grad("P1", f_all, dhc)

    line_step("dx1", dx1_all, 3)

    @pl.when(p == 0)
    def _():
        pw_grads()

    sum_step("df", df_sb, df_rb, 2)

    out_rows = [
        side_by_side([W["O"][j, z, rr] for z in range(Z) for rr in range(R)]) for j in range(2)
    ]
    do_both = low(mm_nt(flat(dx1_all[...]), jnp.concatenate(out_rows, axis=0)))
    for j in range(2):
        do_all[j] = do_both[:, j * hq : (j + 1) * hq]
    for j in range(2):
        for b in range(Z):
            rows = slice(b * TOK, (b + 1) * TOK)
            parts = [[], [], []]
            for h in range(hq // HD):
                q, kk, vals = (qkv[j, rows, s * hq + h * HD : s * hq + (h + 1) * HD] for s in range(3))
                do = do_all[j, rows, h * HD : (h + 1) * HD]
                pr = prob[j, h, b]
                dp = mm_nt(do, vals)
                prw = wide(pr)
                ds = low(prw * (dp - jnp.sum(dp * prw, axis=-1, keepdims=True)) * HD ** (-0.5))
                parts[0].append(mm(ds, kk))
                parts[1].append(mm_tn(ds, q))
                parts[2].append(mm_tn(pr, do))
            for s in range(3):
                dqkv[j, rows, s * hq : (s + 1) * hq] = low(side_by_side(parts[s]))

    dqkv_both = side_by_side([dqkv[0], dqkv[1]])

    @pl.loop(0, Z // 2)
    def _(pair):
        zs = pl.ds(pair * 2, 2)
        rows_q = side_by_side([flat(W["Q"][j, zs, :, s]) for j in range(2) for s in range(3)])
        acc = mm_nt(dqkv_both, rows_q)
        dn1_sb[:, :, lanes_of(pair, 2 * dz)] = low(acc).reshape(Z, TOK, 2 * dz)

    sum_start("dn1", dn1_sb, dn1_rb)
    sum_step("df", df_sb, df_rb, 1)
    reduce_middle("Gi", "Go", "E")

    def attention_grads():
        @pl.loop(0, Z)
        def _(z):
            turned[0:dz] = flat(n1_all[:, :, lanes_of(z, dz)]).T
            for j in range(2):
                g = low(mm(turned[0:dz], dqkv[j]))
                for s in range(3):
                    W["Q"][j, z, :, s] = g[:, s * hq : (s + 1) * hq].reshape(R, -1, hq)

        reduce_start("Q")
        col_grad("O", ctx, dx1_all)

    sum_step("dn1", dn1_sb, dn1_rb, 2)
    reduce_middle("F2", "F1")
    sum_step("dn1", dn1_sb, dn1_rb, 1)

    @pl.when(p == 0)
    def _():
        reduce_middle("P2")
        attention_grads()
        reduce_middle("P1")
        reduce_end(*early)

    sum_wait("dn1", dn1_rb)
    dn1 = summed(dn1_sb, dn1_rb)
    n_hat, rs = normed(wide(x_in[...]))
    gvs_d0 = jnp.sum(dn1 * n_hat, axis=0, keepdims=True)
    out_gtok[x] = low(dx1[...] + norm_back(dn1, n_hat, rs, gain_d(0)))

    @pl.when(p == 1)
    def _():
        for d in (1, 2, 3, 0):
            over_cores(d).start()

    sum_wait("df", df_rb)
    dfv = summed(df_sb, df_rb)
    gvs_lc = jnp.sum(dfv * cn[...], axis=0, keepdims=True)
    dcn[...] = norm_back(dfv, cn[...], crs[:, 0:1], gain_c(49))

    @pl.loop(0, c_dim // LANE)
    def _(ch):
        lanes = lanes_of(ch, LANE)
        taps = vec_c[:, lanes]
        back = depthwise(dcn[:, lanes], lambda k: taps[48 - k : 49 - k], 7)
        out_ggrid[x, :, lanes] = low(dc2t[:, lanes] + back)

    @pl.when(p == 1)
    def _():
        remote(out_ggrid.at[x], dcot, c_send, c_recv, sib).start()
        pw_grads()
        attention_grads()
        layer_output(dx1)
        exchange(0, hid_tok)
        reduce_end(*early)

    @pl.when(p == 0)
    def _():
        reduce_end("P2")

    exchange(2, out_gtok)
    exchange(3, out_ggrid)

    @pl.loop(0, Z)
    def _(z):
        for part in range(cz // LANE):
            lanes = pl.ds(pl.multiple_of(z * cz + part * LANE, LANE), LANE)

            def put(k, row):
                gvs[z, k : k + 1, part * LANE : (part + 1) * LANE] = row

            depthwise_taps(wide(c_in[:, lanes]), dcn[:, lanes], 7, put)

    for z in range(Z):
        gvs[z, 49:50] = gvs_lc[:, z * cz : (z + 1) * cz]
        gvs[z, 50:51] = gvs_ls[:, z * cz : (z + 1) * cz]
        gvs[z, 51:64] = jnp.zeros((13, cz), F32)
        gvs[z, 56:57, 0:dz] = gvs_d0[:, z * dz : (z + 1) * dz]
        gvs[z, 57:58, 0:dz] = gvs_d1[:, z * dz : (z + 1) * dz]
    gvs_low[...] = low(gvs[...])
    scatter_start("gv", gvs_low, gv_rb)

    def group_copy(n, k, src, dst):
        rr, xx = owner(k)
        return remote(src, dst, gx_send.at[n, k], gx_recv.at[n, k], dev(rr=rr, xx=xx))

    for k in range(3):
        c = group_copy(1, k, gad, gad_rb.at[k])
        c.start()
        sent.append(c)
    @pl.when(p == 1)
    def _():
        reduce_middle("P2", "P1")
        reduce_end("P2")

    reduce_end("P1")
    scatter_wait("gv", gv_rb)
    gvx[3] = (gvs[zi] + wide(gv_rb[0])) + (wide(gv_rb[1]) + wide(gv_rb[2]))
    for k in range(3):
        c = group_copy(0, k, gvx.at[3], gvx.at[k])
        c.start()
        sent.append(c)
    for k in range(3):
        group_copy(1, k, gad, gad_rb.at[k]).wait_recv()
    gad_all[zi] = (gad[x] + gad_rb[0, x]) + (gad_rb[1, x] + gad_rb[2, x])
    gather_start("gad", gad_all)

    reduce_middle("Q", "O")
    reduce_end("Q", "O")

    for k in range(3):
        group_copy(0, k, gvx.at[k], gvx.at[k]).wait_recv()
    total = (gvx[0] + gvx[1]) + (gvx[2] + gvx[3])
    mine = jnp.where(ri == 1, pltpu.roll(total, c_own, 1), total)[:, 0:c_own]
    mine_d = jnp.where(ri == 1, total[:, LANE : 2 * LANE], total[:, 0:LANE])

    def flag(n):
        return train_in[0, n].astype(F32)

    out_depth[...] = mine[0:taps7] * flag(0)
    out_ln_conv[...] = mine[49:50] * flag(1)
    out_scale[...] = mine[50:51] * flag(4)
    out_ln_attn[...] = mine_d[56:57]
    out_ln_mlp[...] = mine_d[57:58]
    gather_wait("gad", gad_all)
    for z in range(Z):
        out_ad[:, z * adq : (z + 1) * adq] = gad_all[z][0:9]
    for name in ARRAYS:
        back_local(name).wait()
        for d in range(1, Z):
            n = ids[name]
            slot = quarter_of(name, native[name], zfrom(d))
            remote(slot, slot, a_send.at[n, d - 1], a_recv.at[n, d - 1], dev(zto(d))).wait_recv()
    for n, buf in enumerate((hid_tok, hid_grid, out_gtok, out_ggrid)):
        c = remote(buf.at[x], buf.at[x], xo_send.at[n], xo_recv.at[n], over_x)
        c.wait_send()
        remote(buf.at[xo], buf.at[xo], xo_send.at[n], xo_recv.at[n], over_x).wait_recv()

    @pl.when(p == 0)
    def _():
        remote(hid_tok.at[x], x_in, h_send.at[0], h_recv.at[0], sib).wait_send()
        remote(hid_grid.at[x], c_in, h_send.at[1], h_recv.at[1], sib).wait_send()

    @pl.when(p == 1)
    def _():
        for d in range(Z):
            over_cores(d).wait_send()
        remote(out_ggrid.at[x], dcot, c_send, c_recv, sib).wait_send()

    for name, buf in line_gathers:
        line_sent(name, buf)

    @pl.when(p == 1)
    def _():
        line_sent("dx3", dx3_all)

    for name, sb, rb in line_sums:
        sum_sent(name, sb, rb)
    for c in sent:
        c.wait_send()
    for name in ARRAYS:
        for which in range(4):
            for d in pieces(name):
                hop_copy(name, which, d).wait_send()
        for d in range(1, Z):
            back_copy(name, d).wait_send()


def run_layers(weights, vectors, order, train, streams, sizes, outer):
    d_dim, c_dim, hq, ffq, cfq, adw, dg = sizes
    vm = pltpu.VMEM
    blocks = []
    for name, value in zip(ARRAYS, weights):
        if name == "Q":
            blocks.append((3, value.shape[1], hq))
        elif name in ("O", "F2"):
            blocks.append((value.shape[0] // Z, value.shape[1]))
        else:
            blocks.append((value.shape[0], value.shape[1] // Z))
    rows = Z * TOK

    def act(width, count=Z, kind=BF):
        return vm((count, TOK, width), kind)

    def line(width):
        return vm((2, 3, TOK, width), BF)

    scratch = [vm((2, Z, R) + s, BF) for s in blocks] + [
        vm(lead + s[:-2] + (s[-2] // 2, s[-1]), BF)
        for s in blocks
        for lead in ((Z, R), (2, Z), (Z,), (Z,))
    ]
    scratch += [
        vm((64, 2 * LANE), F32), vm((64, 2 * LANE), BF), vm((Z * R, 64, 2 * LANE), BF), vm((2, 16, adw), F32), vm((64, c_dim), F32), vm((8, d_dim), F32),
        vm((TOK, d_dim), BF), vm((TOK, c_dim), BF), act(d_dim), act(c_dim), act(d_dim), act(c_dim),
        act(d_dim), line(d_dim), act(c_dim), line(c_dim), act(d_dim), line(d_dim),
        act(2 * adw), act(2 * adw, 3), vm((4, 8, dg), F32), vm((4, 8, dg), F32),
        vm((2, rows, 3 * hq), BF), vm((2, hq // HD, Z, TOK, TOK), BF), vm((2, rows, hq), BF),
        vm((2, rows, ffq), BF), vm((2, rows, ffq), BF), vm((2, rows, cfq), BF), vm((2, rows, cfq), BF),
        vm((TOK, c_dim), F32), vm((TOK, LANE), F32), vm((TOK, c_dim), F32), vm((TOK, d_dim), F32), vm((TOK, c_dim), F32),
        vm((2, rows, adw), F32), vm((2, Z, TOK, adw), F32), vm((2, 8, adw), F32), vm((2, 8, adw), F32),
        vm((TOK, d_dim), BF), vm((TOK, c_dim), BF), act(d_dim), act(d_dim), line(d_dim), act(c_dim), line(c_dim),
        act(d_dim), act(c_dim),
        act(d_dim), line(d_dim), act(c_dim), line(c_dim), vm((2, rows, ffq), BF), vm((2, rows, hq), BF),
        vm((2, rows, 3 * hq), BF), vm((2, rows, cfq), BF), vm((TOK, d_dim), F32), vm((TOK, c_dim), F32), vm((2, rows, adw), BF),
        vm((TOK, c_dim), F32),
        vm((Z, 64, c_dim // Z), F32), vm((Z, 64, c_dim // Z), BF), vm((3, 64, c_dim // Z), BF), vm((4, 64, c_dim // Z), F32),
        vm((2, 16, adw), F32), vm((3, 2, 16, adw), F32), vm((Z, 16, adw), F32),
        vm((2 * ffq, rows), BF),
    ]
    dma = pltpu.SemaphoreType.DMA
    na = len(ARRAYS)
    scratch += [
        dma((len(EVENTS), 3)), dma((len(EVENTS), 3)), dma((len(EVENTS), 6)), dma((len(EVENTS), 6)), dma((na, 3)), dma((na, 3)), dma((na,)),
        dma((na, 4, Z)), dma((na, 4, Z)), dma((7,)), dma((7,)), dma, dma, dma((2,)), dma((2,)), dma((Z,)), dma((Z,)), dma, dma,
        dma((4,)), dma((4,)), dma((na, 4, Z)), dma((na, 4, Z)), dma((na, 3)), dma((na, 3)), dma((2, 3)), dma((2, 3)),
        pltpu.SemaphoreType.REGULAR,
    ]
    sds = jax.ShapeDtypeStruct
    out_shape = [sds((2, TOK, d_dim), BF), sds((2, TOK, c_dim), BF)] * 2
    out_shape += [sds(value.shape, BF) for value in weights]
    out_shape += [sds(value.shape, F32) for value in vectors]
    any_spec = pl.BlockSpec(memory_space=pl.ANY)
    vm_spec = pl.BlockSpec(memory_space=pltpu.VMEM)
    sm_spec = pl.BlockSpec(memory_space=pltpu.SMEM)
    return pl.pallas_call(
        functools.partial(main_kernel, sizes, outer),
        out_shape=out_shape,
        in_specs=[any_spec] * na + [vm_spec] * 6 + [sm_spec] * 2 + [vm_spec] * 4,
        out_specs=[vm_spec] * 4 + [any_spec] * na + [vm_spec] * 6,
        scratch_shapes=scratch,
        compiler_params=pltpu.CompilerParams(
            collective_id=0, has_side_effects=True, vmem_limit_bytes=62 * 1024 * 1024
        ),
        cost_estimate=pl.CostEstimate(flops=26 * 10**9, bytes_accessed=10**8, transcendentals=10**7),
        name="layers",
    )(*weights, *vectors, order, train, *streams)


def finish_kernel(flagged, layer_zero, count, *refs):
    grads, streams, vectors = refs[:count], refs[count : count + 4], refs[count + 4 : count + 10]
    order, train = refs[count + 10 : count + 12]
    refs = refs[count + 12 :]
    out_grads, out_streams, out_vectors = refs[:count], refs[count : count + 4], refs[count + 4 : count + 10]
    refs = refs[count + 10 :]
    held, wide_ones = refs[:count], refs[count : 2 * count]
    in_sem, out_sem, stream_sem, vector_sem = refs[2 * count :]

    def fetch(n):
        return pltpu.make_async_copy(grads[n], held[n], in_sem.at[n])

    def put_back(n):
        return pltpu.make_async_copy(wide_ones[n], out_grads[n], out_sem.at[n])

    for n in range(count):
        fetch(n).start()
    swap = (lax.axis_index("pipe") == layer_zero) & (order[0, 0] == 1)
    copies = []
    for n, (src, dst) in enumerate(zip(streams, out_streams)):
        for m in range(2):
            from_slot = jnp.where(swap, 1 - m, m) if n >= 2 else m
            copies.append(pltpu.make_async_copy(src.at[from_slot], dst.at[m], stream_sem.at[2 * n + m]))
    for n, (src, dst) in enumerate(zip(vectors, out_vectors)):
        copies.append(pltpu.make_async_copy(src, dst, vector_sem.at[n]))
    for c in copies:
        c.start()
    for n in range(count):
        fetch(n).wait()
        value = wide(held[n][...])
        if n in flagged:
            value = value * train[0, flagged[n]].astype(F32)
        wide_ones[n][...] = value
        put_back(n).start()
    for n in range(count):
        put_back(n).wait()
    for c in copies:
        c.wait()


def finish(outs, order, train):
    count = len(ARRAYS)
    streams, grads, vectors = outs[:4], outs[4 : 4 + count], outs[4 + count :]
    any_spec = pl.BlockSpec(memory_space=pl.ANY)
    sm_spec = pl.BlockSpec(memory_space=pltpu.SMEM)
    sds = jax.ShapeDtypeStruct
    dma = pltpu.SemaphoreType.DMA
    flagged = {ARRAYS.index("P1"): 2, ARRAYS.index("P2"): 3}
    return pl.pallas_call(
        functools.partial(finish_kernel, flagged, 0, count),
        out_shape=[sds(g.shape, F32) for g in grads]
        + [sds(value.shape, value.dtype) for value in (*streams, *vectors)],
        in_specs=[any_spec] * (count + 10) + [sm_spec] * 2,
        out_specs=[any_spec] * (count + 10),
        scratch_shapes=[pltpu.VMEM(g.shape, BF) for g in grads]
        + [pltpu.VMEM(g.shape, F32) for g in grads]
        + [dma((count,)), dma((count,)), dma((8,)), dma((6,))],
        compiler_params=pltpu.CompilerParams(vmem_limit_bytes=62 * 1024 * 1024),
        name="finish",
    )(*grads, *streams, *vectors, order, train)


def per_device(
    tokens,
    conv_grid,
    order,
    trainable,
    ln_attn,
    w_qkv,
    w_attn_out,
    ln_mlp,
    w_fc_in,
    w_fc_out,
    conv_depth,
    ln_conv,
    w_pw_in,
    w_pw_out,
    layer_scale,
    w_adapt,
    adapt_depth,
    w_gate_in,
    w_gate_out,
    tok_cot,
    grid_cot,
):
    dp_count = lax.axis_size("dp")
    outer = dp_count // (Z * R)
    groups = [[g * outer + o for o in range(outer)] for g in range(Z * R)]

    def block(value, axis):
        value = value[0]
        if outer == 1:
            return value
        return lax.all_gather(value, "dp", axis=axis, tiled=True, axis_index_groups=groups)

    def share(value, axis):
        if outer > 1:
            value = lax.psum_scatter(
                value, "dp", scatter_dimension=axis, tiled=True, axis_index_groups=groups
            )
        return value[None]

    qkv = block(w_qkv, 1)
    gate_in = block(w_gate_in, 1).T
    pw_in = block(w_pw_in, 0)
    adapt = block(w_adapt, 0)
    fc_in = block(w_fc_in, 0)
    weights = (
        pw_in,
        block(w_pw_out, 1).T,
        qkv,
        block(w_attn_out, 1),
        adapt,
        gate_in,
        block(w_gate_out, 0),
        fc_in,
        block(w_fc_out, 1),
    )
    vectors = (
        block(conv_depth, 1),
        block(ln_conv, 0)[None],
        block(layer_scale, 0)[None],
        block(ln_attn, 0)[None],
        block(ln_mlp, 0)[None],
        adapt_depth[0],
    )
    spread = Z * R
    sizes = (
        qkv.shape[1] * spread, pw_in.shape[0] * spread, qkv.shape[2] // Z, fc_in.shape[1] // Z,
        pw_in.shape[1] // Z, adapt.shape[1] // Z, gate_in.shape[0] * spread,
    )

    def rows_of(value):
        return value.reshape(value.shape[0], TOK, value.shape[-1])

    streams = [rows_of(value) for value in (tokens, conv_grid, tok_cot, grid_cot)]
    outs = run_layers(weights, vectors, order, trainable, streams, sizes, outer)
    done = finish(outs, order, trainable)
    g_p1, g_p2, g_q, g_o, g_e, g_gi, g_go, g_f1, g_f2 = done[:9]
    hid_tok, hid_grid, g_tok, g_grid = done[9:13]
    g_depth, g_ln_conv, g_scale, g_ln_attn, g_ln_mlp, g_ad = done[13:]
    grid_shape = (1,) + conv_grid.shape
    tok_shape = (1,) + tokens.shape
    if outer > 1:
        g_ad = lax.psum(g_ad, "dp", axis_index_groups=groups)
    return (
        hid_tok.reshape(tok_shape),
        hid_grid.reshape(grid_shape),
        g_tok.reshape(tok_shape),
        g_grid.reshape(grid_shape),
        share(g_ln_attn[0], 0),
        share(g_q, 1),
        share(g_o, 1),
        share(g_ln_mlp[0], 0),
        share(g_f1, 0),
        share(g_f2, 1),
        share(g_depth, 1),
        share(g_ln_conv[0], 0),
        share(g_p1, 0),
        share(g_p2.T, 1),
        share(g_scale[0], 0),
        share(g_e, 0),
        g_ad[None],
        share(g_gi.T, 1),
        share(g_go, 0),
    )


def solution(mesh):
    in_specs = (
        P(None, "dp", None, None),
        P(None, "dp", None, None, None),
        P("dp", None),
        P("pipe", None),
        P("pipe", "dp"),
        P("pipe", None, "dp", "tensor"),
        P("pipe", "tensor", "dp"),
        P("pipe", "dp"),
        P("pipe", "dp", "tensor"),
        P("pipe", "tensor", "dp"),
        P("pipe", None, "dp"),
        P("pipe", "dp"),
        P("pipe", "dp", "tensor"),
        P("pipe", "tensor", "dp"),
        P("pipe", "dp"),
        P("pipe", "dp", "tensor"),
        P("pipe", None, "tensor"),
        P("pipe", "tensor", "dp"),
        P("pipe", "dp", "tensor"),
        P(None, "dp", None, None),
        P(None, "dp", None, None, None),
    )
    out_specs = (
        P("pipe", None, "dp", None, None),
        P("pipe", None, "dp", None, None, None),
        P("pipe", None, "dp", None, None),
        P("pipe", None, "dp", None, None, None),
        P("pipe", "dp"),
        P("pipe", None, "dp", "tensor"),
        P("pipe", "tensor", "dp"),
        P("pipe", "dp"),
        P("pipe", "dp", "tensor"),
        P("pipe", "tensor", "dp"),
        P("pipe", None, "dp"),
        P("pipe", "dp"),
        P("pipe", "dp", "tensor"),
        P("pipe", "tensor", "dp"),
        P("pipe", "dp"),
        P("pipe", "dp", "tensor"),
        P("pipe", None, "tensor"),
        P("pipe", "tensor", "dp"),
        P("pipe", "dp", "tensor"),
    )
    return jax.shard_map(
        per_device, mesh=mesh, in_specs=in_specs, out_specs=out_specs, check_vma=False
    )
```

```python
import functools

import jax
import jax.numpy as jnp
from jax import lax
from jax.experimental import pallas as pl
from jax.experimental.pallas import tpu as pltpu
from jax.sharding import PartitionSpec as P

HD = 64
Z = 4
R = 2
TOK = 64
SIDE = 8
LANE = 128
BF = jnp.bfloat16
F32 = jnp.float32
ARRAYS = ("P1", "P2", "Q", "O", "E", "Gi", "Go", "F1", "F2")
EVENTS = (
    "n1", "f", "o", "cv", "n2", "c2", "m", "br", "gs",
    "dx3", "dgh", "dn2", "dc2", "dx1", "dcv", "dn1", "df", "gv", "gad",
)


def mm(a, b):
    return lax.dot_general(a, b, (((1,), (0,)), ((), ())), preferred_element_type=F32)


def mm_nt(a, b):
    return lax.dot_general(a, b, (((1,), (1,)), ((), ())), preferred_element_type=F32)


def mm_tn(a, b):
    return lax.dot_general(a, b, (((0,), (0,)), ((), ())), preferred_element_type=F32)


def flat(value):
    return value.reshape(-1, value.shape[-1])


def low(value):
    return value.astype(BF)


def wide(value):
    return value.astype(F32)


def gelu_pair(h):
    phi = 0.5 * (1.0 + lax.erf(h * 0.7071067811865476))
    dens = jnp.exp(-0.5 * h * h) * 0.3989422804014327
    return h * phi, phi + h * dens


def normed(value):
    centred = value - jnp.mean(value, axis=-1, keepdims=True)
    rs = lax.rsqrt(jnp.mean(centred * centred, axis=-1, keepdims=True) + 1e-06)
    return centred * rs, rs


def norm_back(dn, n_hat, rs, gain):
    gd = dn * gain
    return (
        gd
        - jnp.mean(gd, axis=-1, keepdims=True)
        - n_hat * jnp.mean(gd * n_hat, axis=-1, keepdims=True)
    ) * rs


def col_shift(value, by):
    if by == 0:
        return value
    at = lax.broadcasted_iota(jnp.int32, value.shape, 0) % SIDE
    rolled = pltpu.roll(value, (-by) % TOK, 0)
    return jnp.where((at + by >= 0) & (at + by < SIDE), rolled, 0.0)


def row_shift(value, by):
    if by == 0:
        return value
    gap = jnp.zeros((abs(by) * SIDE, value.shape[1]), value.dtype)
    if by > 0:
        return jnp.concatenate([value[by * SIDE :], gap], axis=0)
    return jnp.concatenate([gap, value[: TOK + by * SIDE]], axis=0)


def depthwise(value, tap, side):
    half = side // 2
    shifted = [col_shift(value, b - half) for b in range(side)]
    total = None
    for a in range(side):
        line = None
        for b in range(side):
            term = shifted[b] * tap(a * side + b)
            line = term if line is None else line + term
        line = row_shift(line, a - half)
        total = line if total is None else total + line
    return total


def depthwise_taps(value, grad, side, put):
    half = side // 2
    shifted = [col_shift(value, b - half) for b in range(side)]
    for a in range(side):
        d = a - half
        lo, hi = max(0, -d) * SIDE, (SIDE - max(0, d)) * SIDE
        for b in range(side):
            part = shifted[b][lo + d * SIDE : hi + d * SIDE] * grad[lo:hi]
            put(a * side + b, jnp.sum(part, axis=0, keepdims=True))


def lanes_of(at, width):
    return pl.ds(pl.multiple_of(at * width, width), width)


def side_by_side(blocks):
    return jnp.concatenate(blocks, axis=1)


def main_kernel(dims, outer, *refs):
    at = iter(refs)

    def take(count):
        return [next(at) for _ in range(count)]

    na = len(ARRAYS)
    source = dict(zip(ARRAYS, take(na)))
    (
        depth_in, ln_conv_in, scale_in, ln_attn_in, ln_mlp_in, adapt_depth_in,
        order_in, train_in, tok_in, grid_in, tcot_in, gcot_in,
    ) = take(12)
    hid_tok, hid_grid, out_gtok, out_ggrid = take(4)
    native = dict(zip(ARRAYS, take(na)))
    out_depth, out_ln_conv, out_scale, out_ln_attn, out_ln_mlp, out_ad = take(6)
    W = dict(zip(ARRAYS, take(na)))
    hops = take(4 * na)
    RX = {name: hops[4 * n : 4 * n + 4] for n, name in enumerate(ARRAYS)}
    (
        v_loc, v_low, vv, aq, vec_c, vec_d, x_in, c_in, n1_all, f_all, n2_all, c2_all,
        o_sb, o_rb, cv_sb, cv_rb, m_sb, m_rb, br_sb, br_rb, gsb, dgb,
        qkv, prob, ctx, u, up, r, rp, cn, crs, cv_sum, x1, c2f,
        adapted, spread, pooled, gate,
        dx3, dcot, dx3_all, dn2_sb, dn2_rb, dc2_sb, dc2_rb, dx1_all, dcv_all,
        dn1_sb, dn1_rb, df_sb, df_rb, dh, do_all, dqkv, dhc, dx1, dc2t, dad, dcn,
        gvs, gvs_low, gv_rb, gvx, gad, gad_rb, gad_all, turned,
    ) = take(67)
    (
        zs_send, zs_recv, l_send, l_recv, s1_send, s1_recv, loc_sem, s2_send, s2_recv,
        v_send, v_recv, q_send, q_recv, h_send, h_recv, b_send, b_recv, c_send, c_recv,
        xo_send, xo_recv, g_send, g_recv, a_send, a_recv, gx_send, gx_recv, go,
    ) = take(28)

    p = lax.axis_index("pipe")
    dpi = lax.axis_index("dp")
    x = lax.axis_index("tensor")
    rest = dpi % outer
    zi = dpi // (outer * R)
    ri = (dpi // outer) % R
    xo = 1 - x
    ro = 1 - ri
    d_dim, c_dim, hq, ffq, cfq, adq, dg = dims
    adh = Z * adq
    dz, cz = d_dim // Z, c_dim // Z
    tile = 256
    ids = {name: number for number, name in enumerate(ARRAYS)}
    ev = {name: number for number, name in enumerate(EVENTS)}

    def dev(z=None, rr=None, xx=None, pp=None):
        z = zi if z is None else z
        rr = ri if rr is None else rr
        return (
            p if pp is None else pp,
            (z * R + rr) * outer + rest,
            x if xx is None else xx,
        )

    def zto(d):
        return lax.rem(zi + d, Z)

    def zfrom(d):
        return lax.rem(zi + Z - d, Z)

    def remote(src, dst, ssem, rsem, device):
        return pltpu.make_async_remote_copy(
            src_ref=src, dst_ref=dst, send_sem=ssem, recv_sem=rsem,
            device_id=device, device_id_type=pl.DeviceIdType.MESH,
        )

    sib = dev(pp=1 - p)
    over_r, over_x = dev(rr=ro), dev(xx=xo)

    def z_copy(e, d, src, dst):
        return remote(src, dst, zs_send.at[e, d - 1], zs_recv.at[e, d - 1], dev(zto(d)))

    sent = []

    def gather_copies(name, buf):
        return [z_copy(ev[name], d, buf.at[zi], buf.at[zi]) for d in range(1, Z)]

    def gather_start(name, buf, keep=True):
        copies = gather_copies(name, buf)
        for c in copies:
            c.start()
        if keep:
            sent.extend(copies)

    def gather_wait(name, buf):
        for d in range(1, Z):
            slot = buf.at[zfrom(d)]
            z_copy(ev[name], d, slot, slot).wait_recv()

    def scatter_start(name, sb, rb):
        for d in range(1, Z):
            c = z_copy(ev[name], d, sb.at[zto(d)], rb.at[d - 1])
            c.start()
            sent.append(c)

    def scatter_wait(name, rb):
        for d in range(1, Z):
            z_copy(ev[name], d, rb.at[d - 1], rb.at[d - 1]).wait_recv()

    def right():
        return dev(zi + 1)

    def left():
        return dev(zi - 1)

    def pass_copy(name, buf, toward, s):
        e, k = ev[name], (0 if toward > 0 else 3) + s
        blk = buf.at[zi - toward * s]
        return remote(blk, blk, l_send.at[e, k], l_recv.at[e, k], right() if toward > 0 else left())

    def pass_cond(toward, s):
        if toward > 0:
            return (zi < Z - 1) & (zi - s >= 0)
        return (zi > 0) & (zi + s <= Z - 1)

    def line_start(name, buf):
        for toward in (1, -1):

            @pl.when(pass_cond(toward, 0))
            def _():
                pass_copy(name, buf, toward, 0).start()

    def line_step(name, buf, *steps):
        e = ev[name]
        for s in steps:
            for toward in (1, -1):
                src = zi - toward * s

                @pl.when((src >= 0) & (src <= Z - 1))
                def _():
                    blk = buf.at[src]
                    k = (0 if toward > 0 else 3) + s - 1
                    remote(blk, blk, l_send.at[e, k], l_recv.at[e, k], sib).wait_recv()

                if s < Z - 1:

                    @pl.when(pass_cond(toward, s))
                    def _():
                        pass_copy(name, buf, toward, s).start()

    def line_sent(name, buf):
        for toward in (1, -1):
            for s in range(Z - 1):

                @pl.when(pass_cond(toward, s))
                def _():
                    pass_copy(name, buf, toward, s).wait_send()

    def sum_copy(name, sb, rb, toward, k, first):
        e, way = ev[name], (0 if toward > 0 else 1)
        src = sb.at[zi + toward * k] if first else rb.at[way, k]
        q = way * 3 + k - 1
        return remote(src, rb.at[way, k - 1], l_send.at[e, q], l_recv.at[e, q], right() if toward > 0 else left())

    def at_end(toward):
        return zi == (0 if toward > 0 else Z - 1)

    def passes(toward, k):
        dest = zi + toward * k
        return jnp.logical_not(at_end(toward)) & (dest >= 0) & (dest <= Z - 1)

    def sum_start(name, sb, rb):
        for toward in (1, -1):

            @pl.when(at_end(toward))
            def _():
                for k in (3, 2, 1):
                    sum_copy(name, sb, rb, toward, k, True).start()

    def sum_arrival(name, rb, way, k):
        e = ev[name]
        slot = rb.at[way, k]
        return remote(slot, slot, l_send.at[e, way * 3 + k], l_recv.at[e, way * 3 + k], sib)

    def sum_step(name, sb, rb, *ks):
        for k in ks:
            for way, toward in enumerate((1, -1)):

                @pl.when(passes(toward, k))
                def _():
                    sum_arrival(name, rb, way, k).wait_recv()
                    rb[way, k] = low(wide(rb[way, k]) + wide(sb[zi + toward * k]))
                    sum_copy(name, sb, rb, toward, k, False).start()

    def sum_wait(name, rb):
        for way, toward in enumerate((1, -1)):

            @pl.when(jnp.logical_not(at_end(toward)))
            def _():
                sum_arrival(name, rb, way, 0).wait_recv()

    def summed(sb, rb):
        return wide(sb[zi]) + (wide(rb[0, 0]) + wide(rb[1, 0]))

    def sum_sent(name, sb, rb):
        for toward in (1, -1):

            @pl.when(at_end(toward))
            def _():
                for k in (3, 2, 1):
                    sum_copy(name, sb, rb, toward, k, True).wait_send()

            for k in (2, 1):

                @pl.when(passes(toward, k))
                def _():
                    sum_copy(name, sb, rb, toward, k, False).wait_send()

    def share_start(name, buf):
        for d in range(1, Z):
            c = z_copy(ev[name], d, buf.at[3], buf.at[d - 1])
            c.start()
            sent.append(c)

    def scattered(sb, rb):
        return (wide(sb[zi]) + wide(rb[0])) + (wide(rb[1]) + wide(rb[2]))

    barrier = pltpu.get_barrier_semaphore()
    greeted = [sib]
    for d in range(1, Z):
        greeted += [dev(zto(d)), dev(zto(d), ro), dev(zto(d), pp=1 - p)]
    greeted += [over_r, over_x, dev(rr=ro, xx=xo)]
    for device in greeted:
        pl.semaphore_signal(barrier, inc=1, device_id=device, device_id_type=pl.DeviceIdType.MESH)
    v_loc[...] = jnp.zeros(v_loc.shape, F32)
    taps7 = depth_in.shape[0]
    c_own = depth_in.shape[1]
    v_loc[0:taps7, 0:c_own] = wide(depth_in[...])
    v_loc[49:50, 0:c_own] = wide(ln_conv_in[...])
    v_loc[50:51, 0:c_own] = wide(scale_in[...])
    v_loc[56:57, 0:LANE] = wide(ln_attn_in[...])
    v_loc[57:58, 0:LANE] = wide(ln_mlp_in[...])
    aq[x] = jnp.zeros(aq.shape[1:], F32)
    aq[x, 0:9] = wide(adapt_depth_in[:, lanes_of(zi, adq)])
    v_low[...] = low(v_loc[...])
    line_sums = (
        ("o", o_sb, o_rb), ("cv", cv_sb, cv_rb), ("m", m_sb, m_rb), ("dn2", dn2_sb, dn2_rb),
        ("dc2", dc2_sb, dc2_rb), ("dn1", dn1_sb, dn1_rb), ("df", df_sb, df_rb),
    )
    line_gathers = (
        ("n1", n1_all), ("f", f_all), ("n2", n2_all), ("c2", c2_all), ("dx1", dx1_all), ("dcv", dcv_all),
    )
    for _, _, rb in line_sums:
        for way, toward in enumerate((1, -1)):

            @pl.when(at_end(toward))
            def _():
                rb[way, 0] = jnp.zeros(rb.shape[2:], BF)

    pl.semaphore_wait(barrier, len(greeted))

    me8 = zi * R + ri
    v_arrivals = []
    for n, (d, flip) in enumerate([(d, s) for d in range(Z) for s in (0, 1)][1:]):
        tr = ro if flip else ri
        c = remote(v_low, vv.at[me8], v_send.at[n], v_recv.at[n], dev(zto(d), tr))
        c.start()
        sent.append(c)
        fr = zfrom(d) * R + tr
        v_arrivals.append(remote(vv.at[fr], vv.at[fr], v_send.at[n], v_recv.at[n], dev(zto(d), tr)))
    vv[me8] = v_low[...]
    c = remote(aq.at[x], aq.at[x], q_send, q_recv, over_x)
    c.start()
    sent.append(c)

    by_rows = ("O", "F2")

    def quarter_of(name, ref, z):
        if name == "Q":
            return ref.at[:, :, lanes_of(z, hq)]
        if name in by_rows:
            height = ref.shape[0] // Z
            return ref.at[pl.ds(pl.multiple_of(z * height, height), height)]
        return ref.at[:, lanes_of(z, ref.shape[1] // Z)]

    def step1_local(name):
        return pltpu.make_async_copy(
            quarter_of(name, source[name], zi), W[name].at[x, zi, ri], loc_sem.at[ids[name]]
        )

    def step1_copy(name, d):
        k = ids[name]
        return remote(
            quarter_of(name, source[name], zto(d)), W[name].at[x, zi, ri],
            s1_send.at[k, d - 1], s1_recv.at[k, d - 1], dev(zto(d)),
        )

    def half_of(name, j, z, rr, upper):
        w = W[name]
        half = w.shape[-2] // 2
        rows = slice(half, None) if upper else slice(0, half)
        if len(w.shape) == 6:
            return w.at[j, z, rr, :, rows]
        return w.at[j, z, rr, rows]

    def step2_copy(name, which, d):
        k = ids[name]
        z = zfrom(d)
        if which < 2:
            src = quarter_of(name, source[name], zi) if d == 0 else W[name].at[x, z, ri]
            dst = W[name].at[x, z, ri]
        else:
            src = dst = half_of(name, x, z, ro, False) if which == 2 else half_of(name, xo, z, ri, True)
        to = over_x if which in (1, 2) else over_r
        return remote(src, dst, s2_send.at[k, which, d], s2_recv.at[k, which, d], to)

    def step2_arrival(name, which, d):
        k = ids[name]
        z = zfrom(d)
        if which < 2:
            ref = W[name].at[x, z, ro] if which == 0 else W[name].at[xo, z, ri]
        else:
            ref = half_of(name, xo, z, ro, which == 3)
        to = over_x if which in (1, 2) else over_r
        return remote(ref, ref, s2_send.at[k, which, d], s2_recv.at[k, which, d], to)

    def relay1(*names):
        for name in names:
            for d in range(1, Z):
                step1_copy(name, d).start()

    def relay0(*names):
        for name in names:
            step1_local(name).start()
            step2_copy(name, 0, 0).start()
            step2_copy(name, 1, 0).start()

    def relay2(name, ds=(1, 2, 3)):
        k = ids[name]
        for d in ds:
            slot = W[name].at[x, zfrom(d), ri]
            remote(slot, slot, s1_send.at[k, d - 1], s1_recv.at[k, d - 1], dev(zto(d))).wait_recv()
            step2_copy(name, 0, d).start()
            step2_copy(name, 1, d).start()

    def relay3(name, ds=(0, 1, 2, 3)):
        for d in ds:
            step2_arrival(name, 0, d).wait_recv()
            step2_copy(name, 2, d).start()
            step2_arrival(name, 1, d).wait_recv()
            step2_copy(name, 3, d).start()

    def relay4(*names):
        for name in names:
            step1_local(name).wait()
            for d in range(Z):
                step2_arrival(name, 2, d).wait_recv()
                step2_arrival(name, 3, d).wait_recv()

    def relay_sent():
        for name in ARRAYS:
            for d in range(1, Z):
                step1_copy(name, d).wait_send()
            for which in range(4):
                for d in range(Z):
                    step2_copy(name, which, d).wait_send()

    @pl.when(p == 0)
    def _():
        relay0("P1")
        relay1("P1")
        relay0("P2")
        relay1("P2")
        relay0("Q", "O", "E", "Gi", "Go", "F1", "F2")

    @pl.when(p == 1)
    def _():
        dx3[...] = tcot_in[x]
        dcot[...] = gcot_in[x]
        dx3_all[zi] = tcot_in[x]
        line_start("dx3", dx3_all)

    for c in v_arrivals:
        c.wait_recv()
    remote(aq.at[xo], aq.at[xo], q_send, q_recv, over_x).wait_recv()
    low_lanes = lax.broadcasted_iota(jnp.int32, (64, LANE), 1) < LANE // 2
    for z in range(Z):
        first, second = wide(vv[2 * z]), pltpu.roll(wide(vv[2 * z + 1]), LANE // 2, 1)
        vec_c[:, z * cz : z * cz + LANE] = first[:, 0:LANE]
        vec_c[:, z * cz + LANE : z * cz + 2 * LANE] = jnp.where(
            low_lanes, first[:, LANE:], second[:, 0:LANE]
        )
        vec_c[:, z * cz + 2 * LANE : (z + 1) * cz] = second[:, LANE:]
    for i in range(Z * R):
        vec_d[:, i * LANE : (i + 1) * LANE] = wide(vv[i])[56:64, 0:LANE]

    def gain_d(row):
        return vec_d[row : row + 1, :]

    def gain_c(row):
        return vec_c[row : row + 1, :]

    def token_entry():
        n_hat, _ = normed(wide(x_in[...]))
        n1_all[zi] = low(n_hat * gain_d(0))
        line_start("n1", n1_all)

    def conv_entry():
        @pl.loop(0, c_dim // LANE)
        def _(ch):
            lanes = lanes_of(ch, LANE)
            taps = vec_c[:, lanes]
            cn[:, lanes] = depthwise(wide(c_in[:, lanes]), lambda k: taps[k : k + 1], 7)

        n_hat, rs = normed(cn[...])
        cn[...] = n_hat
        crs[...] = jnp.broadcast_to(rs, crs.shape)
        f_all[zi] = low(n_hat * gain_c(49))
        line_start("f", f_all)

    def first_relays(pump):
        relay2("P1")
        pump(1)
        relay1("Q", "O")
        relay2("P2")
        pump(2)
        relay3("P1")


    @pl.when(p == 0)
    def _():
        first = order_in[0, x] == 0
        c_in[...] = jnp.where(first, grid_in[0], grid_in[1])
        x_in[...] = jnp.where(first, tok_in[0], tok_in[1])
        conv_entry()
        token_entry()

        def pump(s):
            line_step("f", f_all, s)
            line_step("n1", n1_all, s)

        first_relays(pump)
        line_step("f", f_all, 3)
        line_step("n1", n1_all, 3)

    @pl.when(p == 1)
    def _():
        pl.semaphore_wait(go, 1)
        relay0("P1")
        relay1("P1")
        relay0("P2")
        relay1("P2")
        relay0("Q", "O", "E", "Gi", "Go", "F1", "F2")
        first_relays(lambda s: line_step("dx3", dx3_all, s))
        remote(c_in, c_in, h_send.at[1], h_recv.at[1], sib).wait_recv()
        conv_entry()
        line_step("dx3", dx3_all, 3)
        line_step("f", f_all, 1)

    relay2("Q")
    relay2("O")
    relay1("E", "Gi", "Go")
    relay3("P2", (0, 1))

    @pl.when(p == 1)
    def _():
        line_step("f", f_all, 2, 3)

    relay4("P1")

    def conv_hidden(j):
        act, der = gelu_pair(mm(flat(f_all[...]), flat(W["P1"][j])))
        r[j] = low(act)
        rp[j] = low(der)

    conv_hidden(0)

    relay3("P2", (2, 3))
    for name in ("E", "Gi", "Go"):
        relay2(name)
    relay1("F1")
    conv_hidden(1)
    relay3("Q")
    relay3("O")
    relay2("F1")
    relay1("F2")

    @pl.when(p == 0)
    def _():
        pl.semaphore_signal(go, inc=1, device_id=sib, device_id_type=pl.DeviceIdType.MESH)

    relay4("P2")

    def pair_rows(name, pair):
        zs = pl.ds(pair * 2, 2)
        return side_by_side([flat(W[name][0, zs]), flat(W[name][1, zs])])

    def pair_out(left, name, sb, width):
        both = side_by_side([left[0], left[1]])

        @pl.loop(0, Z // 2)
        def _(pair):
            acc = mm_nt(both, pair_rows(name, pair))
            sb[:, :, lanes_of(pair, 2 * width)] = low(acc).reshape(Z, TOK, 2 * width)

    pair_out(r, "P2", cv_sb, cz)

    sum_start("cv", cv_sb, cv_rb)

    for name in ("E", "Gi", "Go"):
        relay3(name)
    sum_step("cv", cv_sb, cv_rb, 2)
    relay2("F2")
    sum_step("cv", cv_sb, cv_rb, 1)

    @pl.when(p == 1)
    def _():
        remote(x_in, x_in, h_send.at[0], h_recv.at[0], sib).wait_recv()
        token_entry()
        line_step("n1", n1_all, 1, 2, 3)

    relay4("Q", "O")
    wide_q = side_by_side([flat(W["Q"][j, :, :, s]) for j in range(2) for s in range(3)])
    qkv_both = low(mm(flat(n1_all[...]), wide_q))
    for j in range(2):
        qkv[j] = qkv_both[:, j * 3 * hq : (j + 1) * 3 * hq]
    for j in range(2):
        for b in range(Z):
            rows = slice(b * TOK, (b + 1) * TOK)
            outs = []
            for h in range(hq // HD):
                q, kk, vals = (qkv[j, rows, s * hq + h * HD : s * hq + (h + 1) * HD] for s in range(3))
                sc = mm_nt(q, kk) * HD ** (-0.5)
                e = jnp.exp(sc - jnp.max(sc, axis=-1, keepdims=True))
                pr = low(e / jnp.sum(e, axis=-1, keepdims=True))
                prob[j, h, b] = pr
                outs.append(mm(pr, vals))
            ctx[j, rows, :] = low(side_by_side(outs))

    out_cols = [
        jnp.concatenate([W["O"][0, z, rr], W["O"][1, z, rr]], axis=0) for z in range(Z) for rr in range(R)
    ]
    o_sb[...] = low(mm(side_by_side([ctx[0], ctx[1]]), side_by_side(out_cols))).reshape(Z, TOK, d_dim)
    sum_start("o", o_sb, o_rb)

    relay3("F1")

    sum_wait("cv", cv_rb)
    cv_sum[...] = summed(cv_sb, cv_rb)
    c2f[...] = wide(c_in[...]) + gain_c(50) * cv_sum[...]
    c2_low = low(c2f[...])
    c2_all[zi] = c2_low
    line_start("c2", c2_all)
    sum_step("o", o_sb, o_rb, 2)
    hid_grid[x] = c2_low

    @pl.when(p == 0)
    def _():
        remote(hid_grid.at[x], c_in, h_send.at[1], h_recv.at[1], sib).start()

    relay3("F2")
    sum_step("o", o_sb, o_rb, 1)
    line_step("c2", c2_all, 1)
    sum_wait("o", o_rb)
    x1[...] = wide(x_in[...]) + summed(o_sb, o_rb)
    n_hat, _ = normed(x1[...])
    n2_all[zi] = low(n_hat * gain_d(1))
    line_start("n2", n2_all)

    relay4("E", "Gi", "Go")
    line_step("c2", c2_all, 2)
    line_step("n2", n2_all, 1)
    line_step("c2", c2_all, 3)
    row8 = lax.broadcasted_iota(jnp.int32, (8, adq), 0)
    gs_part = None
    ad_both = mm(flat(c2_all[...]), side_by_side([flat(W["E"][0]), flat(W["E"][1])]))
    for j in range(2):
        ad = ad_both[:, j * adq : (j + 1) * adq]
        adapted[j] = ad
        taps = aq[j]
        pool = jnp.zeros((8, adq), F32)
        for b in range(Z):
            sp = depthwise(ad[b * TOK : (b + 1) * TOK], lambda k: taps[k : k + 1], 3)
            spread[j, b] = sp
            pool = jnp.where(row8 == b, jnp.mean(sp, axis=0, keepdims=True), pool)
        pooled[j] = pool
        term = mm_nt(low(pool), flat(W["Gi"][j]))
        gs_part = term if gs_part is None else gs_part + term
    gsb[3] = gs_part
    share_start("gs", gsb)
    line_step("n2", n2_all, 2)

    relay4("F1")
    line_step("n2", n2_all, 3)
    for j in range(2):
        act, der = gelu_pair(mm(flat(n2_all[...]), flat(W["F1"][j])))
        u[j] = low(act)
        up[j] = low(der)

    scatter_wait("gs", gsb)

    def gate_hidden():
        return gelu_pair((gsb[0] + gsb[1]) + (gsb[2] + gsb[3]))

    gh, _ = gate_hidden()
    for j in range(2):
        g8 = jnp.tanh(mm(low(gh), flat(W["Go"][j])))
        gate[j] = g8
        for b in range(Z):
            br_sb[b, :, j * adq : (j + 1) * adq] = low(g8[b : b + 1] * spread[j, b])
    scatter_start("br", br_sb, br_rb)
    relay4("F2")

    u_both = side_by_side([u[0], u[1]])

    @pl.loop(0, Z // 2)
    def _(pair):
        halves = [
            side_by_side([W["F2"][j, 2 * pair + dz_, rr] for dz_ in range(2) for rr in range(R)])
            for j in range(2)
        ]
        acc = mm(u_both, jnp.concatenate(halves, axis=0))
        m_sb[:, :, lanes_of(pair, 2 * dz)] = low(acc).reshape(Z, TOK, 2 * dz)

    sum_start("m", m_sb, m_rb)

    def exchange(n, buf):
        remote(buf.at[x], buf.at[x], xo_send.at[n], xo_recv.at[n], over_x).start()

    def layer_output(total):
        sum_step("m", m_sb, m_rb, 2)
        scatter_wait("br", br_rb)
        total[...] = x1[...]
        for d in range(Z):
            piece = br_sb[zi] if d == 0 else br_rb[d - 1]
            for j in range(2):
                lanes = pl.ds(pl.multiple_of(j * adh + zfrom(d) * adq, LANE), adq)
                total[:, lanes] += wide(piece[:, j * adq : (j + 1) * adq])
        sum_step("m", m_sb, m_rb, 1)
        sum_wait("m", m_rb)
        hid_tok[x] = low(total[...] + summed(m_sb, m_rb))

    @pl.when(p == 0)
    def _():
        layer_output(dx1)
        remote(hid_tok.at[x], x_in, h_send.at[0], h_recv.at[0], sib).start()
        exchange(0, hid_tok)

    exchange(1, hid_grid)
    relay_sent()

    def over_cores(d):
        return remote(
            out_gtok.at[x], dx3_all.at[zi], b_send.at[d], b_recv.at[d], dev(zto(d), pp=1 - p)
        )

    @pl.when(p == 0)
    def _():
        for d in range(Z):
            slot = dx3_all.at[zfrom(d)]
            remote(slot, slot, b_send.at[d], b_recv.at[d], sib).wait_recv()
        dx3[...] = dx3_all[zi]

    def own_lanes(j):
        return pl.ds(pl.multiple_of(j * adh + zi * adq, LANE), adq)

    gh, ghp = gate_hidden()
    dgh_part = None
    dgp = []
    for j in range(2):
        dgate = jnp.zeros((8, adq), F32)
        for b in range(Z):
            dbr = wide(dx3_all[b, :, own_lanes(j)])
            dgate = jnp.where(row8 == b, jnp.sum(dbr * spread[j, b], axis=0, keepdims=True), dgate)
        dg8 = low(dgate * (1.0 - gate[j] * gate[j]))
        dgp.append(dg8)
        term = mm_nt(dg8, flat(W["Go"][j]))
        dgh_part = term if dgh_part is None else dgh_part + term
    dgb[3] = dgh_part
    share_start("dgh", dgb)

    for j in range(2):
        cols = side_by_side([W["F2"][j, z, rr] for z in range(Z) for rr in range(R)])
        dh[j] = low(mm_nt(flat(dx3_all[...]), cols) * wide(up[j]))

    scatter_wait("dgh", dgb)
    dgs = low(((dgb[0] + dgb[1]) + (dgb[2] + dgb[3])) * ghp)
    for j in range(2):
        dpool = mm(dgs, flat(W["Gi"][j])) * (1.0 / TOK)
        taps = aq[j]
        tap_rows = [None] * 9
        for b in range(Z):
            dsp = gate[j, b : b + 1] * wide(dx3_all[b, :, own_lanes(j)]) + dpool[b : b + 1]
            dad[j, b * TOK : (b + 1) * TOK] = low(depthwise(dsp, lambda k: taps[8 - k : 9 - k], 3))

            def put(k, row):
                tap_rows[k] = row if tap_rows[k] is None else tap_rows[k] + row

            depthwise_taps(adapted[j, b * TOK : (b + 1) * TOK], dsp, 3, put)
        for k in range(9):
            gad[j, k : k + 1] = tap_rows[k]
        gad[j, 9:16] = jnp.zeros((7, adq), F32)

    pair_out(dad, "E", dc2_sb, cz)

    sum_start("dc2", dc2_sb, dc2_rb)

    pair_out(dh, "F1", dn2_sb, dz)

    sum_start("dn2", dn2_sb, dn2_rb)
    sum_step("dc2", dc2_sb, dc2_rb, 2)

    def half_rows(name, upper):
        half = W[name].shape[-2] // 2
        rows = slice(half, None) if upper else slice(0, half)
        return (slice(None), rows) if len(W[name].shape) == 6 else (rows,)

    fine = ("P1", "P2")

    def pieces(name):
        return (1, 2, 3, 0) if name in fine else (None,)

    def block_at(d):
        return slice(None) if d is None else zto(d)

    def hop_copy(name, which, d):
        n = ids[name]
        lower, upper = half_rows(name, False), half_rows(name, True)
        z = block_at(d)
        w, buf = W[name], RX[name]
        src, dst, to = (
            lambda: (w.at[(xo, z, slice(None)) + lower], buf[0].at[z], over_x),
            lambda: (w.at[(slice(None), z, ro) + upper], buf[1].at[:, z], over_r),
            lambda: (buf[0].at[z, ro], buf[2].at[z], over_r),
            lambda: (buf[1].at[xo, z], buf[3].at[z], over_x),
        )[which]()
        k = 0 if d is None else d
        return remote(src, dst, g_send.at[n, which, k], g_recv.at[n, which, k], to)

    def reduce_start(name, d=None):
        hop_copy(name, 0, d).start()
        hop_copy(name, 1, d).start()

    def each_block(d, body):
        if d is None:
            pl.loop(0, Z)(body)
        else:
            body(zto(d))

    def reduce_middle(*names):
        for name in names:
            lower, upper = half_rows(name, False), half_rows(name, True)
            buf = RX[name]
            for d in pieces(name):
                hop_copy(name, 0, d).wait_recv()

                def add_lower(z):
                    for rr in range(R):
                        own = W[name][(x, z, rr) + lower]
                        buf[0][z, rr] = low(wide(own) + wide(buf[0][z, rr]))

                each_block(d, add_lower)
                hop_copy(name, 2, d).start()
                hop_copy(name, 1, d).wait_recv()

                def add_upper(z):
                    for j in range(2):
                        own = W[name][(j, z, ri) + upper]
                        buf[1][j, z] = low(wide(own) + wide(buf[1][j, z]))

                each_block(d, add_upper)
                hop_copy(name, 3, d).start()

    def reduce_end(*names):
        for name in names:
            lower, upper = half_rows(name, False), half_rows(name, True)
            buf = RX[name]
            for d in pieces(name):
                hop_copy(name, 2, d).wait_recv()
                hop_copy(name, 3, d).wait_recv()

                def add_both(z):
                    W[name][(x, z, ri) + lower] = low(wide(buf[0][z, ri]) + wide(buf[2][z]))
                    W[name][(x, z, ri) + upper] = low(wide(buf[1][x, z]) + wide(buf[3][z]))

                each_block(d, add_both)
                for k in range(Z) if d is None else (d,):
                    (back_copy(name, k) if k else back_local(name)).start()

    def back_copy(name, d):
        n = ids[name]
        return remote(
            W[name].at[x, zto(d), ri], quarter_of(name, native[name], zi),
            a_send.at[n, d - 1], a_recv.at[n, d - 1], dev(zto(d)),
        )

    def back_local(name):
        return pltpu.make_async_copy(
            W[name].at[x, zi, ri], quarter_of(name, native[name], zi), loc_sem.at[ids[name]]
        )

    peers = ((1, 0), (0, 1), (1, 1))

    def owner(k):
        return (ro if peers[k][0] else ri), (xo if peers[k][1] else x)

    def row_grad(name, left, right):
        width = W[name].shape[3]
        span = R * width
        for k, d in enumerate((1, 2, 3, 0)):
            z = zto(d)
            half = (k % 2) * span
            turned[half : half + span] = flat(left[:, :, lanes_of(z, span)]).T
            for j in range(2):
                W[name][j, z] = low(mm(turned[half : half + span], right[j])).reshape(R, width, -1)
            if name in fine:
                reduce_start(name, d)
        if name not in fine:
            reduce_start(name)

    def col_grad(name, left, right):
        width = left.shape[2]
        for j in range(2):
            turned[j * width : (j + 1) * width] = left[j].T
        for d in (1, 2, 3, 0):
            z = zto(d)
            rhs = flat(right[:, :, lanes_of(z, dz)])
            for j in range(2):
                g = low(mm(turned[j * width : (j + 1) * width], rhs))
                for rr in range(R):
                    W[name][j, z, rr] = g[:, rr * LANE : (rr + 1) * LANE]
            if name in fine:
                reduce_start(name, d)
        if name not in fine:
            reduce_start(name)

    for j in range(2):
        W["Gi"][j] = low(mm_tn(dgs, low(pooled[j]))).reshape(Z, R, -1, adq)
        W["Go"][j] = low(mm_tn(low(gh), dgp[j])).reshape(Z, R, -1, adq)
    sum_step("dc2", dc2_sb, dc2_rb, 1)
    sum_step("dn2", dn2_sb, dn2_rb, 2)
    reduce_start("Gi")
    reduce_start("Go")
    row_grad("E", c2_all, dad)
    sum_step("dn2", dn2_sb, dn2_rb, 1)

    @pl.when(p == 0)
    def _():
        remote(dcot, dcot, c_send, c_recv, sib).wait_recv()

    sum_wait("dc2", dc2_rb)
    dc2t[...] = wide(dcot[...]) + summed(dc2_sb, dc2_rb)
    gvs_ls = jnp.sum(cv_sum[...] * dc2t[...], axis=0, keepdims=True)
    dcv_all[zi] = low(dc2t[...] * gain_c(50))
    line_start("dcv", dcv_all)

    sum_wait("dn2", dn2_rb)
    dn2 = summed(dn2_sb, dn2_rb)
    n_hat, rs = normed(x1[...])
    gvs_d1 = jnp.sum(dn2 * n_hat, axis=0, keepdims=True)
    dx1[...] = wide(dx3[...]) + norm_back(dn2, n_hat, rs, gain_d(1))
    dx1_all[zi] = low(dx1[...])
    line_start("dx1", dx1_all)
    line_step("dcv", dcv_all, 1)
    col_grad("F2", u, dx3_all)
    line_step("dcv", dcv_all, 2)
    line_step("dx1", dx1_all, 1)
    row_grad("F1", n2_all, dh)

    reduce_middle("Gi", "Go", "E", "F2")
    line_step("dcv", dcv_all, 3)
    line_step("dx1", dx1_all, 2)
    for j in range(2):
        dhc[j] = low(mm(flat(dcv_all[...]), flat(W["P2"][j])) * wide(rp[j]))

    pair_out(dhc, "P1", df_sb, cz)

    sum_start("df", df_sb, df_rb)

    early = ("Gi", "Go", "E", "F2", "F1")

    def pw_grads():
        row_grad("P2", dcv_all, r)
        row_grad("P1", f_all, dhc)

    line_step("dx1", dx1_all, 3)

    @pl.when(p == 0)
    def _():
        pw_grads()

    sum_step("df", df_sb, df_rb, 2)

    out_rows = [
        side_by_side([W["O"][j, z, rr] for z in range(Z) for rr in range(R)]) for j in range(2)
    ]
    do_both = low(mm_nt(flat(dx1_all[...]), jnp.concatenate(out_rows, axis=0)))
    for j in range(2):
        do_all[j] = do_both[:, j * hq : (j + 1) * hq]
    for j in range(2):
        for b in range(Z):
            rows = slice(b * TOK, (b + 1) * TOK)
            parts = [[], [], []]
            for h in range(hq // HD):
                q, kk, vals = (qkv[j, rows, s * hq + h * HD : s * hq + (h + 1) * HD] for s in range(3))
                do = do_all[j, rows, h * HD : (h + 1) * HD]
                pr = prob[j, h, b]
                dp = mm_nt(do, vals)
                prw = wide(pr)
                ds = low(prw * (dp - jnp.sum(dp * prw, axis=-1, keepdims=True)) * HD ** (-0.5))
                parts[0].append(mm(ds, kk))
                parts[1].append(mm_tn(ds, q))
                parts[2].append(mm_tn(pr, do))
            for s in range(3):
                dqkv[j, rows, s * hq : (s + 1) * hq] = low(side_by_side(parts[s]))

    dqkv_both = side_by_side([dqkv[0], dqkv[1]])

    @pl.loop(0, Z // 2)
    def _(pair):
        zs = pl.ds(pair * 2, 2)
        rows_q = side_by_side([flat(W["Q"][j, zs, :, s]) for j in range(2) for s in range(3)])
        acc = mm_nt(dqkv_both, rows_q)
        dn1_sb[:, :, lanes_of(pair, 2 * dz)] = low(acc).reshape(Z, TOK, 2 * dz)

    sum_start("dn1", dn1_sb, dn1_rb)
    sum_step("df", df_sb, df_rb, 1)

    def attention_grads():
        @pl.loop(0, Z)
        def _(z):
            turned[0:dz] = flat(n1_all[:, :, lanes_of(z, dz)]).T
            for j in range(2):
                g = low(mm(turned[0:dz], dqkv[j]))
                for s in range(3):
                    W["Q"][j, z, :, s] = g[:, s * hq : (s + 1) * hq].reshape(R, -1, hq)

        reduce_start("Q")
        col_grad("O", ctx, dx1_all)

    sum_step("dn1", dn1_sb, dn1_rb, 2)
    reduce_middle("F1")
    sum_step("dn1", dn1_sb, dn1_rb, 1)

    @pl.when(p == 0)
    def _():
        reduce_middle("P2")
        attention_grads()
        reduce_middle("P1")
        reduce_end("P2")
        reduce_end(*early)

    sum_wait("dn1", dn1_rb)
    dn1 = summed(dn1_sb, dn1_rb)
    n_hat, rs = normed(wide(x_in[...]))
    gvs_d0 = jnp.sum(dn1 * n_hat, axis=0, keepdims=True)
    out_gtok[x] = low(dx1[...] + norm_back(dn1, n_hat, rs, gain_d(0)))

    @pl.when(p == 1)
    def _():
        for d in (1, 2, 3, 0):
            over_cores(d).start()

    sum_wait("df", df_rb)
    dfv = summed(df_sb, df_rb)
    gvs_lc = jnp.sum(dfv * cn[...], axis=0, keepdims=True)
    dcn[...] = norm_back(dfv, cn[...], crs[:, 0:1], gain_c(49))

    @pl.when(p == 0)
    def _():
        reduce_end("P1")

    @pl.loop(0, c_dim // LANE)
    def _(ch):
        lanes = lanes_of(ch, LANE)
        taps = vec_c[:, lanes]
        back = depthwise(dcn[:, lanes], lambda k: taps[48 - k : 49 - k], 7)
        out_ggrid[x, :, lanes] = low(dc2t[:, lanes] + back)

    @pl.when(p == 1)
    def _():
        remote(out_ggrid.at[x], dcot, c_send, c_recv, sib).start()
        pw_grads()
        attention_grads()
        layer_output(dx1)
        exchange(0, hid_tok)
        reduce_end(*early)


    exchange(2, out_gtok)
    exchange(3, out_ggrid)

    @pl.loop(0, Z)
    def _(z):
        for part in range(cz // LANE):
            lanes = pl.ds(pl.multiple_of(z * cz + part * LANE, LANE), LANE)

            def put(k, row):
                gvs[z, k : k + 1, part * LANE : (part + 1) * LANE] = row

            depthwise_taps(wide(c_in[:, lanes]), dcn[:, lanes], 7, put)

    for z in range(Z):
        gvs[z, 49:50] = gvs_lc[:, z * cz : (z + 1) * cz]
        gvs[z, 50:51] = gvs_ls[:, z * cz : (z + 1) * cz]
        gvs[z, 51:64] = jnp.zeros((13, cz), F32)
        gvs[z, 56:57, 0:dz] = gvs_d0[:, z * dz : (z + 1) * dz]
        gvs[z, 57:58, 0:dz] = gvs_d1[:, z * dz : (z + 1) * dz]
    gvs_low[...] = low(gvs[...])
    scatter_start("gv", gvs_low, gv_rb)

    def group_copy(n, k, src, dst):
        rr, xx = owner(k)
        return remote(src, dst, gx_send.at[n, k], gx_recv.at[n, k], dev(rr=rr, xx=xx))

    for k in range(3):
        c = group_copy(1, k, gad, gad_rb.at[k])
        c.start()
        sent.append(c)
    @pl.when(p == 1)
    def _():
        reduce_middle("P2", "P1")
        reduce_end("P2", "P1")

    scatter_wait("gv", gv_rb)
    gvx[3] = (gvs[zi] + wide(gv_rb[0])) + (wide(gv_rb[1]) + wide(gv_rb[2]))
    for k in range(3):
        c = group_copy(0, k, gvx.at[3], gvx.at[k])
        c.start()
        sent.append(c)
    for k in range(3):
        group_copy(1, k, gad, gad_rb.at[k]).wait_recv()
    gad_all[zi] = (gad[x] + gad_rb[0, x]) + (gad_rb[1, x] + gad_rb[2, x])
    gather_start("gad", gad_all)

    reduce_middle("Q", "O")
    reduce_end("Q", "O")

    for k in range(3):
        group_copy(0, k, gvx.at[k], gvx.at[k]).wait_recv()
    total = (gvx[0] + gvx[1]) + (gvx[2] + gvx[3])
    mine = jnp.where(ri == 1, pltpu.roll(total, c_own, 1), total)[:, 0:c_own]
    mine_d = jnp.where(ri == 1, total[:, LANE : 2 * LANE], total[:, 0:LANE])

    def flag(n):
        return train_in[0, n].astype(F32)

    out_depth[...] = mine[0:taps7] * flag(0)
    out_ln_conv[...] = mine[49:50] * flag(1)
    out_scale[...] = mine[50:51] * flag(4)
    out_ln_attn[...] = mine_d[56:57]
    out_ln_mlp[...] = mine_d[57:58]
    gather_wait("gad", gad_all)
    for z in range(Z):
        out_ad[:, z * adq : (z + 1) * adq] = gad_all[z][0:9]
    for name in ARRAYS:
        back_local(name).wait()
        for d in range(1, Z):
            n = ids[name]
            slot = quarter_of(name, native[name], zfrom(d))
            remote(slot, slot, a_send.at[n, d - 1], a_recv.at[n, d - 1], dev(zto(d))).wait_recv()
    for n, buf in enumerate((hid_tok, hid_grid, out_gtok, out_ggrid)):
        c = remote(buf.at[x], buf.at[x], xo_send.at[n], xo_recv.at[n], over_x)
        c.wait_send()
        remote(buf.at[xo], buf.at[xo], xo_send.at[n], xo_recv.at[n], over_x).wait_recv()

    @pl.when(p == 0)
    def _():
        remote(hid_tok.at[x], x_in, h_send.at[0], h_recv.at[0], sib).wait_send()
        remote(hid_grid.at[x], c_in, h_send.at[1], h_recv.at[1], sib).wait_send()

    @pl.when(p == 1)
    def _():
        for d in range(Z):
            over_cores(d).wait_send()
        remote(out_ggrid.at[x], dcot, c_send, c_recv, sib).wait_send()

    for name, buf in line_gathers:
        line_sent(name, buf)

    @pl.when(p == 1)
    def _():
        line_sent("dx3", dx3_all)

    for name, sb, rb in line_sums:
        sum_sent(name, sb, rb)
    for c in sent:
        c.wait_send()
    for name in ARRAYS:
        for which in range(4):
            for d in pieces(name):
                hop_copy(name, which, d).wait_send()
        for d in range(1, Z):
            back_copy(name, d).wait_send()


def run_layers(weights, vectors, order, train, streams, sizes, outer):
    d_dim, c_dim, hq, ffq, cfq, adw, dg = sizes
    vm = pltpu.VMEM
    blocks = []
    for name, value in zip(ARRAYS, weights):
        if name == "Q":
            blocks.append((3, value.shape[1], hq))
        elif name in ("O", "F2"):
            blocks.append((value.shape[0] // Z, value.shape[1]))
        else:
            blocks.append((value.shape[0], value.shape[1] // Z))
    rows = Z * TOK

    def act(width, count=Z, kind=BF):
        return vm((count, TOK, width), kind)

    def line(width):
        return vm((2, 3, TOK, width), BF)

    scratch = [vm((2, Z, R) + s, BF) for s in blocks] + [
        vm(lead + s[:-2] + (s[-2] // 2, s[-1]), BF)
        for s in blocks
        for lead in ((Z, R), (2, Z), (Z,), (Z,))
    ]
    scratch += [
        vm((64, 2 * LANE), F32), vm((64, 2 * LANE), BF), vm((Z * R, 64, 2 * LANE), BF), vm((2, 16, adw), F32), vm((64, c_dim), F32), vm((8, d_dim), F32),
        vm((TOK, d_dim), BF), vm((TOK, c_dim), BF), act(d_dim), act(c_dim), act(d_dim), act(c_dim),
        act(d_dim), line(d_dim), act(c_dim), line(c_dim), act(d_dim), line(d_dim),
        act(2 * adw), act(2 * adw, 3), vm((4, 8, dg), F32), vm((4, 8, dg), F32),
        vm((2, rows, 3 * hq), BF), vm((2, hq // HD, Z, TOK, TOK), BF), vm((2, rows, hq), BF),
        vm((2, rows, ffq), BF), vm((2, rows, ffq), BF), vm((2, rows, cfq), BF), vm((2, rows, cfq), BF),
        vm((TOK, c_dim), F32), vm((TOK, LANE), F32), vm((TOK, c_dim), F32), vm((TOK, d_dim), F32), vm((TOK, c_dim), F32),
        vm((2, rows, adw), F32), vm((2, Z, TOK, adw), F32), vm((2, 8, adw), F32), vm((2, 8, adw), F32),
        vm((TOK, d_dim), BF), vm((TOK, c_dim), BF), act(d_dim), act(d_dim), line(d_dim), act(c_dim), line(c_dim),
        act(d_dim), act(c_dim),
        act(d_dim), line(d_dim), act(c_dim), line(c_dim), vm((2, rows, ffq), BF), vm((2, rows, hq), BF),
        vm((2, rows, 3 * hq), BF), vm((2, rows, cfq), BF), vm((TOK, d_dim), F32), vm((TOK, c_dim), F32), vm((2, rows, adw), BF),
        vm((TOK, c_dim), F32),
        vm((Z, 64, c_dim // Z), F32), vm((Z, 64, c_dim // Z), BF), vm((3, 64, c_dim // Z), BF), vm((4, 64, c_dim // Z), F32),
        vm((2, 16, adw), F32), vm((3, 2, 16, adw), F32), vm((Z, 16, adw), F32),
        vm((2 * ffq, rows), BF),
    ]
    dma = pltpu.SemaphoreType.DMA
    na = len(ARRAYS)
    scratch += [
        dma((len(EVENTS), 3)), dma((len(EVENTS), 3)), dma((len(EVENTS), 6)), dma((len(EVENTS), 6)), dma((na, 3)), dma((na, 3)), dma((na,)),
        dma((na, 4, Z)), dma((na, 4, Z)), dma((7,)), dma((7,)), dma, dma, dma((2,)), dma((2,)), dma((Z,)), dma((Z,)), dma, dma,
        dma((4,)), dma((4,)), dma((na, 4, Z)), dma((na, 4, Z)), dma((na, 3)), dma((na, 3)), dma((2, 3)), dma((2, 3)),
        pltpu.SemaphoreType.REGULAR,
    ]
    sds = jax.ShapeDtypeStruct
    out_shape = [sds((2, TOK, d_dim), BF), sds((2, TOK, c_dim), BF)] * 2
    out_shape += [sds(value.shape, BF) for value in weights]
    out_shape += [sds(value.shape, F32) for value in vectors]
    any_spec = pl.BlockSpec(memory_space=pl.ANY)
    vm_spec = pl.BlockSpec(memory_space=pltpu.VMEM)
    sm_spec = pl.BlockSpec(memory_space=pltpu.SMEM)
    return pl.pallas_call(
        functools.partial(main_kernel, sizes, outer),
        out_shape=out_shape,
        in_specs=[any_spec] * na + [vm_spec] * 6 + [sm_spec] * 2 + [vm_spec] * 4,
        out_specs=[vm_spec] * 4 + [any_spec] * na + [vm_spec] * 6,
        scratch_shapes=scratch,
        compiler_params=pltpu.CompilerParams(
            collective_id=0, has_side_effects=True, vmem_limit_bytes=62 * 1024 * 1024
        ),
        cost_estimate=pl.CostEstimate(flops=26 * 10**9, bytes_accessed=10**8, transcendentals=10**7),
        name="layers",
    )(*weights, *vectors, order, train, *streams)


def finish_kernel(flagged, layer_zero, count, *refs):
    grads, streams, vectors = refs[:count], refs[count : count + 4], refs[count + 4 : count + 10]
    order, train = refs[count + 10 : count + 12]
    refs = refs[count + 12 :]
    out_grads, out_streams, out_vectors = refs[:count], refs[count : count + 4], refs[count + 4 : count + 10]
    refs = refs[count + 10 :]
    held, wide_ones = refs[:count], refs[count : 2 * count]
    in_sem, out_sem = refs[2 * count :]

    def fetch(n):
        return pltpu.make_async_copy(grads[n], held[n], in_sem.at[n])

    def put_back(n):
        return pltpu.make_async_copy(wide_ones[n], out_grads[n], out_sem.at[n])

    for n in range(count):
        fetch(n).start()
    swap = (lax.axis_index("pipe") == layer_zero) & (order[0, 0] == 1)
    for n, (src, dst) in enumerate(zip(streams, out_streams)):
        for m in range(2):
            dst[m] = src[m] if n < 2 else jnp.where(swap, src[1 - m], src[m])
    for src, dst in zip(vectors, out_vectors):
        dst[...] = src[...]
    for n in range(count):
        fetch(n).wait()
        src, dst = held[n], wide_ones[n]
        scale = train[0, flagged[n]].astype(F32) if n in flagged else None
        lead = src.shape[0] if len(src.shape) == 3 else 1

        @pl.loop(0, lead * (src.shape[-2] // 16))
        def _(step):
            rows = pl.ds(pl.multiple_of((step // lead) * 16, 16), 16)
            at = (step % lead, rows) if len(src.shape) == 3 else (rows,)
            value = wide(src[at])
            dst[at] = value if scale is None else value * scale

        put_back(n).start()
    for n in range(count):
        put_back(n).wait()


def finish(outs, order, train):
    count = len(ARRAYS)
    streams, grads, vectors = outs[:4], outs[4 : 4 + count], outs[4 + count :]
    any_spec = pl.BlockSpec(memory_space=pl.ANY)
    sm_spec = pl.BlockSpec(memory_space=pltpu.SMEM)
    vm_spec = pl.BlockSpec(memory_space=pltpu.VMEM)
    sds = jax.ShapeDtypeStruct
    dma = pltpu.SemaphoreType.DMA
    flagged = {ARRAYS.index("P1"): 2, ARRAYS.index("P2"): 3}
    return pl.pallas_call(
        functools.partial(finish_kernel, flagged, 0, count),
        out_shape=[sds(g.shape, F32) for g in grads]
        + [sds(value.shape, value.dtype) for value in (*streams, *vectors)],
        in_specs=[any_spec] * count + [vm_spec] * 10 + [sm_spec] * 2,
        out_specs=[any_spec] * count + [vm_spec] * 10,
        scratch_shapes=[pltpu.VMEM(g.shape, BF) for g in grads]
        + [pltpu.VMEM(g.shape, F32) for g in grads]
        + [dma((count,)), dma((count,))],
        compiler_params=pltpu.CompilerParams(vmem_limit_bytes=62 * 1024 * 1024),
        name="finish",
    )(*grads, *streams, *vectors, order, train)


def per_device(
    tokens,
    conv_grid,
    order,
    trainable,
    ln_attn,
    w_qkv,
    w_attn_out,
    ln_mlp,
    w_fc_in,
    w_fc_out,
    conv_depth,
    ln_conv,
    w_pw_in,
    w_pw_out,
    layer_scale,
    w_adapt,
    adapt_depth,
    w_gate_in,
    w_gate_out,
    tok_cot,
    grid_cot,
):
    dp_count = lax.axis_size("dp")
    outer = dp_count // (Z * R)
    groups = [[g * outer + o for o in range(outer)] for g in range(Z * R)]

    def block(value, axis):
        value = value[0]
        if outer == 1:
            return value
        return lax.all_gather(value, "dp", axis=axis, tiled=True, axis_index_groups=groups)

    def share(value, axis):
        if outer > 1:
            value = lax.psum_scatter(
                value, "dp", scatter_dimension=axis, tiled=True, axis_index_groups=groups
            )
        return value[None]

    qkv = block(w_qkv, 1)
    gate_in = block(w_gate_in, 1).T
    pw_in = block(w_pw_in, 0)
    adapt = block(w_adapt, 0)
    fc_in = block(w_fc_in, 0)
    weights = (
        pw_in,
        block(w_pw_out, 1).T,
        qkv,
        block(w_attn_out, 1),
        adapt,
        gate_in,
        block(w_gate_out, 0),
        fc_in,
        block(w_fc_out, 1),
    )
    vectors = (
        block(conv_depth, 1),
        block(ln_conv, 0)[None],
        block(layer_scale, 0)[None],
        block(ln_attn, 0)[None],
        block(ln_mlp, 0)[None],
        adapt_depth[0],
    )
    spread = Z * R
    sizes = (
        qkv.shape[1] * spread, pw_in.shape[0] * spread, qkv.shape[2] // Z, fc_in.shape[1] // Z,
        pw_in.shape[1] // Z, adapt.shape[1] // Z, gate_in.shape[0] * spread,
    )

    def rows_of(value):
        return value.reshape(value.shape[0], TOK, value.shape[-1])

    streams = [rows_of(value) for value in (tokens, conv_grid, tok_cot, grid_cot)]
    outs = run_layers(weights, vectors, order, trainable, streams, sizes, outer)
    done = finish(outs, order, trainable)
    g_p1, g_p2, g_q, g_o, g_e, g_gi, g_go, g_f1, g_f2 = done[:9]
    hid_tok, hid_grid, g_tok, g_grid = done[9:13]
    g_depth, g_ln_conv, g_scale, g_ln_attn, g_ln_mlp, g_ad = done[13:]
    grid_shape = (1,) + conv_grid.shape
    tok_shape = (1,) + tokens.shape
    if outer > 1:
        g_ad = lax.psum(g_ad, "dp", axis_index_groups=groups)
    return (
        hid_tok.reshape(tok_shape),
        hid_grid.reshape(grid_shape),
        g_tok.reshape(tok_shape),
        g_grid.reshape(grid_shape),
        share(g_ln_attn[0], 0),
        share(g_q, 1),
        share(g_o, 1),
        share(g_ln_mlp[0], 0),
        share(g_f1, 0),
        share(g_f2, 1),
        share(g_depth, 1),
        share(g_ln_conv[0], 0),
        share(g_p1, 0),
        share(g_p2.T, 1),
        share(g_scale[0], 0),
        share(g_e, 0),
        g_ad[None],
        share(g_gi.T, 1),
        share(g_go, 0),
    )


def solution(mesh):
    in_specs = (
        P(None, "dp", None, None),
        P(None, "dp", None, None, None),
        P("dp", None),
        P("pipe", None),
        P("pipe", "dp"),
        P("pipe", None, "dp", "tensor"),
        P("pipe", "tensor", "dp"),
        P("pipe", "dp"),
        P("pipe", "dp", "tensor"),
        P("pipe", "tensor", "dp"),
        P("pipe", None, "dp"),
        P("pipe", "dp"),
        P("pipe", "dp", "tensor"),
        P("pipe", "tensor", "dp"),
        P("pipe", "dp"),
        P("pipe", "dp", "tensor"),
        P("pipe", None, "tensor"),
        P("pipe", "tensor", "dp"),
        P("pipe", "dp", "tensor"),
        P(None, "dp", None, None),
        P(None, "dp", None, None, None),
    )
    out_specs = (
        P("pipe", None, "dp", None, None),
        P("pipe", None, "dp", None, None, None),
        P("pipe", None, "dp", None, None),
        P("pipe", None, "dp", None, None, None),
        P("pipe", "dp"),
        P("pipe", None, "dp", "tensor"),
        P("pipe", "tensor", "dp"),
        P("pipe", "dp"),
        P("pipe", "dp", "tensor"),
        P("pipe", "tensor", "dp"),
        P("pipe", None, "dp"),
        P("pipe", "dp"),
        P("pipe", "dp", "tensor"),
        P("pipe", "tensor", "dp"),
        P("pipe", "dp"),
        P("pipe", "dp", "tensor"),
        P("pipe", None, "tensor"),
        P("pipe", "tensor", "dp"),
        P("pipe", "dp", "tensor"),
    )
    return jax.shard_map(
        per_device, mesh=mesh, in_specs=in_specs, out_specs=out_specs, check_vma=False
    )
```

```python
import functools

import jax
import jax.numpy as jnp
from jax import lax
from jax.experimental import pallas as pl
from jax.experimental.pallas import tpu as pltpu
from jax.sharding import PartitionSpec as P

HD = 64
Z = 4
R = 2
TOK = 64
SIDE = 8
LANE = 128
BF = jnp.bfloat16
F32 = jnp.float32
ARRAYS = ("P1", "P2", "Q", "O", "E", "Gi", "Go", "F1", "F2")
EVENTS = (
    "n1", "f", "o", "cv", "n2", "c2", "m", "br", "gs",
    "dx3", "dgh", "dn2", "dc2", "dx1", "dcv", "dn1", "df", "gv", "gad",
)


def mm(a, b):
    return lax.dot_general(a, b, (((1,), (0,)), ((), ())), preferred_element_type=F32)


def mm_nt(a, b):
    return lax.dot_general(a, b, (((1,), (1,)), ((), ())), preferred_element_type=F32)


def mm_tn(a, b):
    return lax.dot_general(a, b, (((0,), (0,)), ((), ())), preferred_element_type=F32)


def flat(value):
    return value.reshape(-1, value.shape[-1])


def low(value):
    return value.astype(BF)


def wide(value):
    return value.astype(F32)


def gelu_pair(h):
    phi = 0.5 * (1.0 + lax.erf(h * 0.7071067811865476))
    dens = jnp.exp(-0.5 * h * h) * 0.3989422804014327
    return h * phi, phi + h * dens


def normed(value):
    centred = value - jnp.mean(value, axis=-1, keepdims=True)
    rs = lax.rsqrt(jnp.mean(centred * centred, axis=-1, keepdims=True) + 1e-06)
    return centred * rs, rs


def norm_back(dn, n_hat, rs, gain):
    gd = dn * gain
    return (
        gd
        - jnp.mean(gd, axis=-1, keepdims=True)
        - n_hat * jnp.mean(gd * n_hat, axis=-1, keepdims=True)
    ) * rs


def col_shift(value, by):
    if by == 0:
        return value
    at = lax.broadcasted_iota(jnp.int32, value.shape, 0) % SIDE
    rolled = pltpu.roll(value, (-by) % TOK, 0)
    return jnp.where((at + by >= 0) & (at + by < SIDE), rolled, 0.0)


def row_shift(value, by):
    if by == 0:
        return value
    gap = jnp.zeros((abs(by) * SIDE, value.shape[1]), value.dtype)
    if by > 0:
        return jnp.concatenate([value[by * SIDE :], gap], axis=0)
    return jnp.concatenate([gap, value[: TOK + by * SIDE]], axis=0)


def depthwise(value, tap, side):
    half = side // 2
    shifted = [col_shift(value, b - half) for b in range(side)]
    total = None
    for a in range(side):
        line = None
        for b in range(side):
            term = shifted[b] * tap(a * side + b)
            line = term if line is None else line + term
        line = row_shift(line, a - half)
        total = line if total is None else total + line
    return total


def depthwise_taps(value, grad, side, put):
    half = side // 2
    shifted = [col_shift(value, b - half) for b in range(side)]
    for a in range(side):
        d = a - half
        lo, hi = max(0, -d) * SIDE, (SIDE - max(0, d)) * SIDE
        for b in range(side):
            part = shifted[b][lo + d * SIDE : hi + d * SIDE] * grad[lo:hi]
            put(a * side + b, jnp.sum(part, axis=0, keepdims=True))


def lanes_of(at, width):
    return pl.ds(pl.multiple_of(at * width, width), width)


def side_by_side(blocks):
    return jnp.concatenate(blocks, axis=1)


def main_kernel(dims, outer, *refs):
    at = iter(refs)

    def take(count):
        return [next(at) for _ in range(count)]

    na = len(ARRAYS)
    source = dict(zip(ARRAYS, take(na)))
    (
        depth_in, ln_conv_in, scale_in, ln_attn_in, ln_mlp_in, adapt_depth_in,
        order_in, train_in, tok_in, grid_in, tcot_in, gcot_in,
    ) = take(12)
    hid_tok, hid_grid, out_gtok, out_ggrid = take(4)
    native = dict(zip(ARRAYS, take(na)))
    out_depth, out_ln_conv, out_scale, out_ln_attn, out_ln_mlp, out_ad = take(6)
    W = dict(zip(ARRAYS, take(na)))
    hops = take(4 * na)
    RX = {name: hops[4 * n : 4 * n + 4] for n, name in enumerate(ARRAYS)}
    (
        v_loc, v_low, vv, aq, vec_c, vec_d, x_in, c_in, n1_all, f_all, n2_all, c2_all,
        o_sb, o_rb, cv_sb, cv_rb, m_sb, m_rb, br_sb, br_rb, gsb, dgb,
        qkv, prob, ctx, u, up, r, rp, cn, crs, cv_sum, x1, c2f,
        adapted, spread, pooled, gate,
        dx3, dcot, dx3_all, dn2_sb, dn2_rb, dc2_sb, dc2_rb, dx1_all, dcv_all,
        dn1_sb, dn1_rb, df_sb, df_rb, dh, do_all, dqkv, dhc, dx1, dc2t, dad, dcn,
        gvs, gvs_low, gv_rb, gvx, gad, gad_rb, gad_all, turned,
    ) = take(67)
    (
        zs_send, zs_recv, l_send, l_recv, s1_send, s1_recv, loc_sem, s2_send, s2_recv,
        v_send, v_recv, q_send, q_recv, h_send, h_recv, b_send, b_recv, c_send, c_recv,
        xo_send, xo_recv, g_send, g_recv, a_send, a_recv, gx_send, gx_recv, go,
    ) = take(28)

    p = lax.axis_index("pipe")
    dpi = lax.axis_index("dp")
    x = lax.axis_index("tensor")
    rest = dpi % outer
    zi = dpi // (outer * R)
    ri = (dpi // outer) % R
    xo = 1 - x
    ro = 1 - ri
    d_dim, c_dim, hq, ffq, cfq, adq, dg = dims
    adh = Z * adq
    dz, cz = d_dim // Z, c_dim // Z
    tile = 256
    ids = {name: number for number, name in enumerate(ARRAYS)}
    ev = {name: number for number, name in enumerate(EVENTS)}

    def dev(z=None, rr=None, xx=None, pp=None):
        z = zi if z is None else z
        rr = ri if rr is None else rr
        return (
            p if pp is None else pp,
            (z * R + rr) * outer + rest,
            x if xx is None else xx,
        )

    def zto(d):
        return lax.rem(zi + d, Z)

    def zfrom(d):
        return lax.rem(zi + Z - d, Z)

    def remote(src, dst, ssem, rsem, device):
        return pltpu.make_async_remote_copy(
            src_ref=src, dst_ref=dst, send_sem=ssem, recv_sem=rsem,
            device_id=device, device_id_type=pl.DeviceIdType.MESH,
        )

    sib = dev(pp=1 - p)
    over_r, over_x = dev(rr=ro), dev(xx=xo)

    def z_copy(e, d, src, dst):
        return remote(src, dst, zs_send.at[e, d - 1], zs_recv.at[e, d - 1], dev(zto(d)))

    sent = []

    def gather_copies(name, buf):
        return [z_copy(ev[name], d, buf.at[zi], buf.at[zi]) for d in range(1, Z)]

    def gather_start(name, buf, keep=True):
        copies = gather_copies(name, buf)
        for c in copies:
            c.start()
        if keep:
            sent.extend(copies)

    def gather_wait(name, buf):
        for d in range(1, Z):
            slot = buf.at[zfrom(d)]
            z_copy(ev[name], d, slot, slot).wait_recv()

    def scatter_start(name, sb, rb):
        for d in range(1, Z):
            c = z_copy(ev[name], d, sb.at[zto(d)], rb.at[d - 1])
            c.start()
            sent.append(c)

    def scatter_wait(name, rb):
        for d in range(1, Z):
            z_copy(ev[name], d, rb.at[d - 1], rb.at[d - 1]).wait_recv()

    def right():
        return dev(zi + 1)

    def left():
        return dev(zi - 1)

    def pass_copy(name, buf, toward, s):
        e, k = ev[name], (0 if toward > 0 else 3) + s
        blk = buf.at[zi - toward * s]
        return remote(blk, blk, l_send.at[e, k], l_recv.at[e, k], right() if toward > 0 else left())

    def pass_cond(toward, s):
        if toward > 0:
            return (zi < Z - 1) & (zi - s >= 0)
        return (zi > 0) & (zi + s <= Z - 1)

    def line_start(name, buf):
        for toward in (1, -1):

            @pl.when(pass_cond(toward, 0))
            def _():
                pass_copy(name, buf, toward, 0).start()

    def line_step(name, buf, *steps):
        e = ev[name]
        for s in steps:
            for toward in (1, -1):
                src = zi - toward * s

                @pl.when((src >= 0) & (src <= Z - 1))
                def _():
                    blk = buf.at[src]
                    k = (0 if toward > 0 else 3) + s - 1
                    remote(blk, blk, l_send.at[e, k], l_recv.at[e, k], sib).wait_recv()

                if s < Z - 1:

                    @pl.when(pass_cond(toward, s))
                    def _():
                        pass_copy(name, buf, toward, s).start()

    def line_sent(name, buf):
        for toward in (1, -1):
            for s in range(Z - 1):

                @pl.when(pass_cond(toward, s))
                def _():
                    pass_copy(name, buf, toward, s).wait_send()

    def sum_copy(name, sb, rb, toward, k, first):
        e, way = ev[name], (0 if toward > 0 else 1)
        src = sb.at[zi + toward * k] if first else rb.at[way, k]
        q = way * 3 + k - 1
        return remote(src, rb.at[way, k - 1], l_send.at[e, q], l_recv.at[e, q], right() if toward > 0 else left())

    def at_end(toward):
        return zi == (0 if toward > 0 else Z - 1)

    def passes(toward, k):
        dest = zi + toward * k
        return jnp.logical_not(at_end(toward)) & (dest >= 0) & (dest <= Z - 1)

    def sum_start(name, sb, rb):
        for toward in (1, -1):

            @pl.when(at_end(toward))
            def _():
                for k in (3, 2, 1):
                    sum_copy(name, sb, rb, toward, k, True).start()

    def sum_arrival(name, rb, way, k):
        e = ev[name]
        slot = rb.at[way, k]
        return remote(slot, slot, l_send.at[e, way * 3 + k], l_recv.at[e, way * 3 + k], sib)

    def sum_step(name, sb, rb, *ks):
        for k in ks:
            for way, toward in enumerate((1, -1)):

                @pl.when(passes(toward, k))
                def _():
                    sum_arrival(name, rb, way, k).wait_recv()
                    rb[way, k] = low(wide(rb[way, k]) + wide(sb[zi + toward * k]))
                    sum_copy(name, sb, rb, toward, k, False).start()

    def sum_wait(name, rb):
        for way, toward in enumerate((1, -1)):

            @pl.when(jnp.logical_not(at_end(toward)))
            def _():
                sum_arrival(name, rb, way, 0).wait_recv()

    def summed(sb, rb):
        return wide(sb[zi]) + (wide(rb[0, 0]) + wide(rb[1, 0]))

    def sum_sent(name, sb, rb):
        for toward in (1, -1):

            @pl.when(at_end(toward))
            def _():
                for k in (3, 2, 1):
                    sum_copy(name, sb, rb, toward, k, True).wait_send()

            for k in (2, 1):

                @pl.when(passes(toward, k))
                def _():
                    sum_copy(name, sb, rb, toward, k, False).wait_send()

    def share_start(name, buf):
        for d in range(1, Z):
            c = z_copy(ev[name], d, buf.at[3], buf.at[d - 1])
            c.start()
            sent.append(c)

    def scattered(sb, rb):
        return (wide(sb[zi]) + wide(rb[0])) + (wide(rb[1]) + wide(rb[2]))

    barrier = pltpu.get_barrier_semaphore()
    greeted = [sib]
    for d in range(1, Z):
        greeted += [dev(zto(d)), dev(zto(d), ro), dev(zto(d), pp=1 - p)]
    greeted += [over_r, over_x, dev(rr=ro, xx=xo)]
    for device in greeted:
        pl.semaphore_signal(barrier, inc=1, device_id=device, device_id_type=pl.DeviceIdType.MESH)
    v_loc[...] = jnp.zeros(v_loc.shape, F32)
    taps7 = depth_in.shape[0]
    c_own = depth_in.shape[1]
    v_loc[0:taps7, 0:c_own] = wide(depth_in[...])
    v_loc[49:50, 0:c_own] = wide(ln_conv_in[...])
    v_loc[50:51, 0:c_own] = wide(scale_in[...])
    v_loc[56:57, 0:LANE] = wide(ln_attn_in[...])
    v_loc[57:58, 0:LANE] = wide(ln_mlp_in[...])
    aq[x] = jnp.zeros(aq.shape[1:], F32)
    aq[x, 0:9] = wide(adapt_depth_in[:, lanes_of(zi, adq)])
    v_low[...] = low(v_loc[...])
    line_sums = (
        ("o", o_sb, o_rb), ("cv", cv_sb, cv_rb), ("m", m_sb, m_rb), ("dn2", dn2_sb, dn2_rb),
        ("dc2", dc2_sb, dc2_rb), ("dn1", dn1_sb, dn1_rb), ("df", df_sb, df_rb),
    )
    line_gathers = (
        ("n1", n1_all), ("f", f_all), ("n2", n2_all), ("c2", c2_all), ("dx1", dx1_all), ("dcv", dcv_all),
    )
    for _, _, rb in line_sums:
        for way, toward in enumerate((1, -1)):

            @pl.when(at_end(toward))
            def _():
                rb[way, 0] = jnp.zeros(rb.shape[2:], BF)

    pl.semaphore_wait(barrier, len(greeted))

    me8 = zi * R + ri
    v_arrivals = []
    for n, (d, flip) in enumerate([(d, s) for d in range(Z) for s in (0, 1)][1:]):
        tr = ro if flip else ri
        c = remote(v_low, vv.at[me8], v_send.at[n], v_recv.at[n], dev(zto(d), tr))
        c.start()
        sent.append(c)
        fr = zfrom(d) * R + tr
        v_arrivals.append(remote(vv.at[fr], vv.at[fr], v_send.at[n], v_recv.at[n], dev(zto(d), tr)))
    vv[me8] = v_low[...]
    c = remote(aq.at[x], aq.at[x], q_send, q_recv, over_x)
    c.start()
    sent.append(c)

    by_rows = ("O", "F2")

    def quarter_of(name, ref, z):
        if name == "Q":
            return ref.at[:, :, lanes_of(z, hq)]
        if name in by_rows:
            height = ref.shape[0] // Z
            return ref.at[pl.ds(pl.multiple_of(z * height, height), height)]
        return ref.at[:, lanes_of(z, ref.shape[1] // Z)]

    def step1_local(name):
        return pltpu.make_async_copy(
            quarter_of(name, source[name], zi), W[name].at[x, zi, ri], loc_sem.at[ids[name]]
        )

    def step1_copy(name, d):
        k = ids[name]
        return remote(
            quarter_of(name, source[name], zto(d)), W[name].at[x, zi, ri],
            s1_send.at[k, d - 1], s1_recv.at[k, d - 1], dev(zto(d)),
        )

    def half_of(name, j, z, rr, upper):
        w = W[name]
        half = w.shape[-2] // 2
        rows = slice(half, None) if upper else slice(0, half)
        if len(w.shape) == 6:
            return w.at[j, z, rr, :, rows]
        return w.at[j, z, rr, rows]

    def step2_copy(name, which, d):
        k = ids[name]
        z = zfrom(d)
        if which < 2:
            src = quarter_of(name, source[name], zi) if d == 0 else W[name].at[x, z, ri]
            dst = W[name].at[x, z, ri]
        else:
            src = dst = half_of(name, x, z, ro, False) if which == 2 else half_of(name, xo, z, ri, True)
        to = over_x if which in (1, 2) else over_r
        return remote(src, dst, s2_send.at[k, which, d], s2_recv.at[k, which, d], to)

    def step2_arrival(name, which, d):
        k = ids[name]
        z = zfrom(d)
        if which < 2:
            ref = W[name].at[x, z, ro] if which == 0 else W[name].at[xo, z, ri]
        else:
            ref = half_of(name, xo, z, ro, which == 3)
        to = over_x if which in (1, 2) else over_r
        return remote(ref, ref, s2_send.at[k, which, d], s2_recv.at[k, which, d], to)

    def relay1(*names):
        for name in names:
            for d in range(1, Z):
                step1_copy(name, d).start()

    def relay0(*names):
        for name in names:
            step1_local(name).start()
            step2_copy(name, 0, 0).start()
            step2_copy(name, 1, 0).start()

    def relay2(name, ds=(1, 2, 3)):
        k = ids[name]
        for d in ds:
            slot = W[name].at[x, zfrom(d), ri]
            remote(slot, slot, s1_send.at[k, d - 1], s1_recv.at[k, d - 1], dev(zto(d))).wait_recv()
            step2_copy(name, 0, d).start()
            step2_copy(name, 1, d).start()

    def relay3(name, ds=(0, 1, 2, 3)):
        for d in ds:
            step2_arrival(name, 0, d).wait_recv()
            step2_copy(name, 2, d).start()
            step2_arrival(name, 1, d).wait_recv()
            step2_copy(name, 3, d).start()

    def relay4(*names):
        for name in names:
            step1_local(name).wait()
            for d in range(Z):
                step2_arrival(name, 2, d).wait_recv()
                step2_arrival(name, 3, d).wait_recv()

    def relay_sent():
        for name in ARRAYS:
            for d in range(1, Z):
                step1_copy(name, d).wait_send()
            for which in range(4):
                for d in range(Z):
                    step2_copy(name, which, d).wait_send()

    @pl.when(p == 0)
    def _():
        relay0("P1")
        relay1("P1")
        relay0("P2")
        relay1("P2")
        relay0("Q", "O", "E", "Gi", "Go", "F1", "F2")

    @pl.when(p == 1)
    def _():
        dx3[...] = tcot_in[x]
        dcot[...] = gcot_in[x]
        dx3_all[zi] = tcot_in[x]
        line_start("dx3", dx3_all)

    for c in v_arrivals:
        c.wait_recv()
    remote(aq.at[xo], aq.at[xo], q_send, q_recv, over_x).wait_recv()
    low_lanes = lax.broadcasted_iota(jnp.int32, (64, LANE), 1) < LANE // 2
    for z in range(Z):
        first, second = wide(vv[2 * z]), pltpu.roll(wide(vv[2 * z + 1]), LANE // 2, 1)
        vec_c[:, z * cz : z * cz + LANE] = first[:, 0:LANE]
        vec_c[:, z * cz + LANE : z * cz + 2 * LANE] = jnp.where(
            low_lanes, first[:, LANE:], second[:, 0:LANE]
        )
        vec_c[:, z * cz + 2 * LANE : (z + 1) * cz] = second[:, LANE:]
    for i in range(Z * R):
        vec_d[:, i * LANE : (i + 1) * LANE] = wide(vv[i])[56:64, 0:LANE]

    def gain_d(row):
        return vec_d[row : row + 1, :]

    def gain_c(row):
        return vec_c[row : row + 1, :]

    def token_entry():
        n_hat, _ = normed(wide(x_in[...]))
        n1_all[zi] = low(n_hat * gain_d(0))
        line_start("n1", n1_all)

    def conv_entry():
        @pl.loop(0, c_dim // LANE)
        def _(ch):
            lanes = lanes_of(ch, LANE)
            taps = vec_c[:, lanes]
            cn[:, lanes] = depthwise(wide(c_in[:, lanes]), lambda k: taps[k : k + 1], 7)

        n_hat, rs = normed(cn[...])
        cn[...] = n_hat
        crs[...] = jnp.broadcast_to(rs, crs.shape)
        f_all[zi] = low(n_hat * gain_c(49))
        line_start("f", f_all)

    def first_relays(pump):
        relay2("P1")
        pump(1)
        relay1("Q", "O")
        relay2("P2")
        pump(2)
        relay3("P1")


    @pl.when(p == 0)
    def _():
        first = order_in[0, x] == 0
        c_in[...] = jnp.where(first, grid_in[0], grid_in[1])
        x_in[...] = jnp.where(first, tok_in[0], tok_in[1])
        conv_entry()
        token_entry()

        def pump(s):
            line_step("f", f_all, s)
            line_step("n1", n1_all, s)

        first_relays(pump)
        line_step("f", f_all, 3)
        line_step("n1", n1_all, 3)

    @pl.when(p == 1)
    def _():
        pl.semaphore_wait(go, 1)
        relay0("P1")
        relay1("P1")
        relay0("P2")
        relay1("P2")
        relay0("Q", "O", "E", "Gi", "Go", "F1", "F2")
        first_relays(lambda s: line_step("dx3", dx3_all, s))
        remote(c_in, c_in, h_send.at[1], h_recv.at[1], sib).wait_recv()
        conv_entry()
        line_step("dx3", dx3_all, 3)
        line_step("f", f_all, 1)

    relay2("Q")
    relay2("O")
    relay1("E", "Gi", "Go")
    relay3("P2", (0, 1))

    @pl.when(p == 1)
    def _():
        line_step("f", f_all, 2, 3)

    relay4("P1")

    def conv_hidden(j):
        act, der = gelu_pair(mm(flat(f_all[...]), flat(W["P1"][j])))
        r[j] = low(act)
        rp[j] = low(der)

    conv_hidden(0)

    relay3("P2", (2, 3))
    for name in ("E", "Gi", "Go"):
        relay2(name)
    relay1("F1")
    conv_hidden(1)
    relay3("Q")
    relay3("O")
    relay2("F1")
    relay1("F2")

    @pl.when(p == 0)
    def _():
        pl.semaphore_signal(go, inc=1, device_id=sib, device_id_type=pl.DeviceIdType.MESH)

    relay4("P2")

    def pair_rows(name, pair):
        zs = pl.ds(pair * 2, 2)
        return side_by_side([flat(W[name][0, zs]), flat(W[name][1, zs])])

    def pair_out(left, name, sb, width):
        both = side_by_side([left[0], left[1]])

        @pl.loop(0, Z // 2)
        def _(pair):
            acc = mm_nt(both, pair_rows(name, pair))
            sb[:, :, lanes_of(pair, 2 * width)] = low(acc).reshape(Z, TOK, 2 * width)

    pair_out(r, "P2", cv_sb, cz)

    sum_start("cv", cv_sb, cv_rb)

    for name in ("E", "Gi", "Go"):
        relay3(name)
    sum_step("cv", cv_sb, cv_rb, 2)
    relay2("F2")
    sum_step("cv", cv_sb, cv_rb, 1)

    @pl.when(p == 1)
    def _():
        remote(x_in, x_in, h_send.at[0], h_recv.at[0], sib).wait_recv()
        token_entry()
        line_step("n1", n1_all, 1, 2, 3)

    relay4("Q", "O")
    wide_q = side_by_side([flat(W["Q"][j, :, :, s]) for j in range(2) for s in range(3)])
    qkv_both = low(mm(flat(n1_all[...]), wide_q))
    for j in range(2):
        qkv[j] = qkv_both[:, j * 3 * hq : (j + 1) * 3 * hq]
    for j in range(2):
        for b in range(Z):
            rows = slice(b * TOK, (b + 1) * TOK)
            outs = []
            for h in range(hq // HD):
                q, kk, vals = (qkv[j, rows, s * hq + h * HD : s * hq + (h + 1) * HD] for s in range(3))
                sc = mm_nt(q, kk) * HD ** (-0.5)
                e = jnp.exp(sc - jnp.max(sc, axis=-1, keepdims=True))
                pr = low(e / jnp.sum(e, axis=-1, keepdims=True))
                prob[j, h, b] = pr
                outs.append(mm(pr, vals))
            ctx[j, rows, :] = low(side_by_side(outs))

    out_cols = [
        jnp.concatenate([W["O"][0, z, rr], W["O"][1, z, rr]], axis=0) for z in range(Z) for rr in range(R)
    ]
    o_sb[...] = low(mm(side_by_side([ctx[0], ctx[1]]), side_by_side(out_cols))).reshape(Z, TOK, d_dim)
    sum_start("o", o_sb, o_rb)

    relay3("F1")

    sum_wait("cv", cv_rb)
    cv_sum[...] = summed(cv_sb, cv_rb)
    c2f[...] = wide(c_in[...]) + gain_c(50) * cv_sum[...]
    c2_low = low(c2f[...])
    c2_all[zi] = c2_low
    line_start("c2", c2_all)
    sum_step("o", o_sb, o_rb, 2)
    hid_grid[x] = c2_low

    @pl.when(p == 0)
    def _():
        remote(hid_grid.at[x], c_in, h_send.at[1], h_recv.at[1], sib).start()

    relay3("F2")
    sum_step("o", o_sb, o_rb, 1)
    line_step("c2", c2_all, 1)
    sum_wait("o", o_rb)
    x1[...] = wide(x_in[...]) + summed(o_sb, o_rb)
    n_hat, _ = normed(x1[...])
    n2_all[zi] = low(n_hat * gain_d(1))
    line_start("n2", n2_all)

    relay4("E", "Gi", "Go")
    line_step("c2", c2_all, 2)
    line_step("n2", n2_all, 1)
    line_step("c2", c2_all, 3)
    row8 = lax.broadcasted_iota(jnp.int32, (8, adq), 0)
    gs_part = None
    ad_both = mm(flat(c2_all[...]), side_by_side([flat(W["E"][0]), flat(W["E"][1])]))
    for j in range(2):
        ad = ad_both[:, j * adq : (j + 1) * adq]
        adapted[j] = ad
        taps = aq[j]
        pool = jnp.zeros((8, adq), F32)
        for b in range(Z):
            sp = depthwise(ad[b * TOK : (b + 1) * TOK], lambda k: taps[k : k + 1], 3)
            spread[j, b] = sp
            pool = jnp.where(row8 == b, jnp.mean(sp, axis=0, keepdims=True), pool)
        pooled[j] = pool
        term = mm_nt(low(pool), flat(W["Gi"][j]))
        gs_part = term if gs_part is None else gs_part + term
    gsb[3] = gs_part
    share_start("gs", gsb)
    line_step("n2", n2_all, 2)

    relay4("F1")
    line_step("n2", n2_all, 3)
    for j in range(2):
        act, der = gelu_pair(mm(flat(n2_all[...]), flat(W["F1"][j])))
        u[j] = low(act)
        up[j] = low(der)

    scatter_wait("gs", gsb)

    def gate_hidden():
        return gelu_pair((gsb[0] + gsb[1]) + (gsb[2] + gsb[3]))

    gh, _ = gate_hidden()
    for j in range(2):
        g8 = jnp.tanh(mm(low(gh), flat(W["Go"][j])))
        gate[j] = g8
        for b in range(Z):
            br_sb[b, :, j * adq : (j + 1) * adq] = low(g8[b : b + 1] * spread[j, b])
    scatter_start("br", br_sb, br_rb)
    relay4("F2")

    u_both = side_by_side([u[0], u[1]])

    @pl.loop(0, Z // 2)
    def _(pair):
        halves = [
            side_by_side([W["F2"][j, 2 * pair + dz_, rr] for dz_ in range(2) for rr in range(R)])
            for j in range(2)
        ]
        acc = mm(u_both, jnp.concatenate(halves, axis=0))
        m_sb[:, :, lanes_of(pair, 2 * dz)] = low(acc).reshape(Z, TOK, 2 * dz)

    sum_start("m", m_sb, m_rb)

    def exchange(n, buf):
        remote(buf.at[x], buf.at[x], xo_send.at[n], xo_recv.at[n], over_x).start()

    def layer_output(total):
        sum_step("m", m_sb, m_rb, 2)
        scatter_wait("br", br_rb)
        total[...] = x1[...]
        for d in range(Z):
            piece = br_sb[zi] if d == 0 else br_rb[d - 1]
            for j in range(2):
                lanes = pl.ds(pl.multiple_of(j * adh + zfrom(d) * adq, LANE), adq)
                total[:, lanes] += wide(piece[:, j * adq : (j + 1) * adq])
        sum_step("m", m_sb, m_rb, 1)
        sum_wait("m", m_rb)
        hid_tok[x] = low(total[...] + summed(m_sb, m_rb))

    @pl.when(p == 0)
    def _():
        layer_output(dx1)
        remote(hid_tok.at[x], x_in, h_send.at[0], h_recv.at[0], sib).start()
        exchange(0, hid_tok)

    exchange(1, hid_grid)
    relay_sent()

    def over_cores(d):
        return remote(
            out_gtok.at[x], dx3_all.at[zi], b_send.at[d], b_recv.at[d], dev(zto(d), pp=1 - p)
        )

    @pl.when(p == 0)
    def _():
        for d in range(Z):
            slot = dx3_all.at[zfrom(d)]
            remote(slot, slot, b_send.at[d], b_recv.at[d], sib).wait_recv()
        dx3[...] = dx3_all[zi]

    def own_lanes(j):
        return pl.ds(pl.multiple_of(j * adh + zi * adq, LANE), adq)

    gh, ghp = gate_hidden()
    dgh_part = None
    dgp = []
    for j in range(2):
        dgate = jnp.zeros((8, adq), F32)
        for b in range(Z):
            dbr = wide(dx3_all[b, :, own_lanes(j)])
            dgate = jnp.where(row8 == b, jnp.sum(dbr * spread[j, b], axis=0, keepdims=True), dgate)
        dg8 = low(dgate * (1.0 - gate[j] * gate[j]))
        dgp.append(dg8)
        term = mm_nt(dg8, flat(W["Go"][j]))
        dgh_part = term if dgh_part is None else dgh_part + term
    dgb[3] = dgh_part
    share_start("dgh", dgb)

    for j in range(2):
        cols = side_by_side([W["F2"][j, z, rr] for z in range(Z) for rr in range(R)])
        dh[j] = low(mm_nt(flat(dx3_all[...]), cols) * wide(up[j]))

    scatter_wait("dgh", dgb)
    dgs = low(((dgb[0] + dgb[1]) + (dgb[2] + dgb[3])) * ghp)
    for j in range(2):
        dpool = mm(dgs, flat(W["Gi"][j])) * (1.0 / TOK)
        taps = aq[j]
        tap_rows = [None] * 9
        for b in range(Z):
            dsp = gate[j, b : b + 1] * wide(dx3_all[b, :, own_lanes(j)]) + dpool[b : b + 1]
            dad[j, b * TOK : (b + 1) * TOK] = low(depthwise(dsp, lambda k: taps[8 - k : 9 - k], 3))

            def put(k, row):
                tap_rows[k] = row if tap_rows[k] is None else tap_rows[k] + row

            depthwise_taps(adapted[j, b * TOK : (b + 1) * TOK], dsp, 3, put)
        for k in range(9):
            gad[j, k : k + 1] = tap_rows[k]
        gad[j, 9:16] = jnp.zeros((7, adq), F32)

    pair_out(dad, "E", dc2_sb, cz)

    sum_start("dc2", dc2_sb, dc2_rb)

    pair_out(dh, "F1", dn2_sb, dz)

    sum_start("dn2", dn2_sb, dn2_rb)
    sum_step("dc2", dc2_sb, dc2_rb, 2)

    def half_rows(name, upper):
        half = W[name].shape[-2] // 2
        rows = slice(half, None) if upper else slice(0, half)
        return (slice(None), rows) if len(W[name].shape) == 6 else (rows,)

    fine = ("P1", "P2")

    def pieces(name):
        return (1, 2, 3, 0) if name in fine else (None,)

    def block_at(d):
        return slice(None) if d is None else zto(d)

    def hop_copy(name, which, d):
        n = ids[name]
        lower, upper = half_rows(name, False), half_rows(name, True)
        z = block_at(d)
        w, buf = W[name], RX[name]
        src, dst, to = (
            lambda: (w.at[(xo, z, slice(None)) + lower], buf[0].at[z], over_x),
            lambda: (w.at[(slice(None), z, ro) + upper], buf[1].at[:, z], over_r),
            lambda: (buf[0].at[z, ro], buf[2].at[z], over_r),
            lambda: (buf[1].at[xo, z], buf[3].at[z], over_x),
        )[which]()
        k = 0 if d is None else d
        return remote(src, dst, g_send.at[n, which, k], g_recv.at[n, which, k], to)

    def reduce_start(name, d=None):
        hop_copy(name, 0, d).start()
        hop_copy(name, 1, d).start()

    def each_block(d, body):
        if d is None:
            pl.loop(0, Z)(body)
        else:
            body(zto(d))

    def reduce_middle(*names):
        for name in names:
            lower, upper = half_rows(name, False), half_rows(name, True)
            buf = RX[name]
            for d in pieces(name):
                hop_copy(name, 0, d).wait_recv()

                def add_lower(z):
                    for rr in range(R):
                        own = W[name][(x, z, rr) + lower]
                        buf[0][z, rr] = low(wide(own) + wide(buf[0][z, rr]))

                each_block(d, add_lower)
                hop_copy(name, 2, d).start()
                hop_copy(name, 1, d).wait_recv()

                def add_upper(z):
                    for j in range(2):
                        own = W[name][(j, z, ri) + upper]
                        buf[1][j, z] = low(wide(own) + wide(buf[1][j, z]))

                each_block(d, add_upper)
                hop_copy(name, 3, d).start()

    def reduce_end(*names):
        for name in names:
            lower, upper = half_rows(name, False), half_rows(name, True)
            buf = RX[name]
            for d in pieces(name):
                hop_copy(name, 2, d).wait_recv()
                hop_copy(name, 3, d).wait_recv()

                def add_both(z):
                    W[name][(x, z, ri) + lower] = low(wide(buf[0][z, ri]) + wide(buf[2][z]))
                    W[name][(x, z, ri) + upper] = low(wide(buf[1][x, z]) + wide(buf[3][z]))

                each_block(d, add_both)
                for k in range(Z) if d is None else (d,):
                    (back_copy(name, k) if k else back_local(name)).start()

    def back_copy(name, d):
        n = ids[name]
        return remote(
            W[name].at[x, zto(d), ri], quarter_of(name, native[name], zi),
            a_send.at[n, d - 1], a_recv.at[n, d - 1], dev(zto(d)),
        )

    def back_local(name):
        return pltpu.make_async_copy(
            W[name].at[x, zi, ri], quarter_of(name, native[name], zi), loc_sem.at[ids[name]]
        )

    peers = ((1, 0), (0, 1), (1, 1))

    def owner(k):
        return (ro if peers[k][0] else ri), (xo if peers[k][1] else x)

    def row_grad(name, left, right, pump=None):
        width = W[name].shape[3]
        span = R * width
        for k, d in enumerate((1, 2, 3, 0)):
            z = zto(d)
            half = (k % 2) * span
            turned[half : half + span] = flat(left[:, :, lanes_of(z, span)]).T
            for j in range(2):
                W[name][j, z] = low(mm(turned[half : half + span], right[j])).reshape(R, width, -1)
            if name in fine:
                reduce_start(name, d)
            if pump is not None:
                pump(k)
        if name not in fine:
            reduce_start(name)

    def col_grad(name, left, right):
        width = left.shape[2]
        for j in range(2):
            turned[j * width : (j + 1) * width] = left[j].T
        for d in (1, 2, 3, 0):
            z = zto(d)
            rhs = flat(right[:, :, lanes_of(z, dz)])
            for j in range(2):
                g = low(mm(turned[j * width : (j + 1) * width], rhs))
                for rr in range(R):
                    W[name][j, z, rr] = g[:, rr * LANE : (rr + 1) * LANE]
            if name in fine:
                reduce_start(name, d)
        if name not in fine:
            reduce_start(name)

    for j in range(2):
        W["Gi"][j] = low(mm_tn(dgs, low(pooled[j]))).reshape(Z, R, -1, adq)
        W["Go"][j] = low(mm_tn(low(gh), dgp[j])).reshape(Z, R, -1, adq)
    sum_step("dc2", dc2_sb, dc2_rb, 1)
    sum_step("dn2", dn2_sb, dn2_rb, 2)
    reduce_start("Gi")
    reduce_start("Go")
    row_grad("E", c2_all, dad)
    sum_step("dn2", dn2_sb, dn2_rb, 1)

    @pl.when(p == 0)
    def _():
        remote(dcot, dcot, c_send, c_recv, sib).wait_recv()

    sum_wait("dc2", dc2_rb)
    dc2t[...] = wide(dcot[...]) + summed(dc2_sb, dc2_rb)
    gvs_ls = jnp.sum(cv_sum[...] * dc2t[...], axis=0, keepdims=True)
    dcv_all[zi] = low(dc2t[...] * gain_c(50))
    line_start("dcv", dcv_all)

    sum_wait("dn2", dn2_rb)
    dn2 = summed(dn2_sb, dn2_rb)
    n_hat, rs = normed(x1[...])
    gvs_d1 = jnp.sum(dn2 * n_hat, axis=0, keepdims=True)
    dx1[...] = wide(dx3[...]) + norm_back(dn2, n_hat, rs, gain_d(1))
    dx1_all[zi] = low(dx1[...])
    line_start("dx1", dx1_all)
    line_step("dcv", dcv_all, 1)
    col_grad("F2", u, dx3_all)
    line_step("dcv", dcv_all, 2)
    line_step("dx1", dx1_all, 1)
    row_grad("F1", n2_all, dh)

    reduce_middle("Gi", "Go", "E", "F2")
    line_step("dcv", dcv_all, 3)
    line_step("dx1", dx1_all, 2)
    for j in range(2):
        dhc[j] = low(mm(flat(dcv_all[...]), flat(W["P2"][j])) * wide(rp[j]))

    pair_out(dhc, "P1", df_sb, cz)

    sum_start("df", df_sb, df_rb)

    early = ("Gi", "Go", "E", "F2", "F1")

    def pw_grads():
        row_grad("P2", dcv_all, r)
        row_grad("P1", f_all, dhc)

    line_step("dx1", dx1_all, 3)
    reduce_middle("F1")

    @pl.when(p == 0)
    def _():
        pw_grads()

    sum_step("df", df_sb, df_rb, 2)

    out_rows = [
        side_by_side([W["O"][j, z, rr] for z in range(Z) for rr in range(R)]) for j in range(2)
    ]
    do_both = low(mm_nt(flat(dx1_all[...]), jnp.concatenate(out_rows, axis=0)))
    for j in range(2):
        do_all[j] = do_both[:, j * hq : (j + 1) * hq]
    for j in range(2):
        for b in range(Z):
            rows = slice(b * TOK, (b + 1) * TOK)
            parts = [[], [], []]
            for h in range(hq // HD):
                q, kk, vals = (qkv[j, rows, s * hq + h * HD : s * hq + (h + 1) * HD] for s in range(3))
                do = do_all[j, rows, h * HD : (h + 1) * HD]
                pr = prob[j, h, b]
                dp = mm_nt(do, vals)
                prw = wide(pr)
                ds = low(prw * (dp - jnp.sum(dp * prw, axis=-1, keepdims=True)) * HD ** (-0.5))
                parts[0].append(mm(ds, kk))
                parts[1].append(mm_tn(ds, q))
                parts[2].append(mm_tn(pr, do))
            for s in range(3):
                dqkv[j, rows, s * hq : (s + 1) * hq] = low(side_by_side(parts[s]))

    dqkv_both = side_by_side([dqkv[0], dqkv[1]])

    @pl.loop(0, Z // 2)
    def _(pair):
        zs = pl.ds(pair * 2, 2)
        rows_q = side_by_side([flat(W["Q"][j, zs, :, s]) for j in range(2) for s in range(3)])
        acc = mm_nt(dqkv_both, rows_q)
        dn1_sb[:, :, lanes_of(pair, 2 * dz)] = low(acc).reshape(Z, TOK, 2 * dz)

    sum_start("dn1", dn1_sb, dn1_rb)
    sum_step("df", df_sb, df_rb, 1)

    def attention_grads():
        @pl.loop(0, Z)
        def _(z):
            turned[0:dz] = flat(n1_all[:, :, lanes_of(z, dz)]).T
            for j in range(2):
                g = low(mm(turned[0:dz], dqkv[j]))
                for s in range(3):
                    W["Q"][j, z, :, s] = g[:, s * hq : (s + 1) * hq].reshape(R, -1, hq)

        reduce_start("Q")
        col_grad("O", ctx, dx1_all)


    @pl.when(p == 1)
    def _():
        def pump(k):
            if k in (0, 2):
                sum_step("dn1", dn1_sb, dn1_rb, 2 if k == 0 else 1)

        row_grad("P2", dcv_all, r, pump)

    @pl.when(p == 0)
    def _():
        sum_step("dn1", dn1_sb, dn1_rb, 2)
        reduce_middle("P2")
        sum_step("dn1", dn1_sb, dn1_rb, 1)
        attention_grads()
        reduce_middle("P1")
        reduce_end(*early)

    sum_wait("dn1", dn1_rb)
    dn1 = summed(dn1_sb, dn1_rb)
    n_hat, rs = normed(wide(x_in[...]))
    gvs_d0 = jnp.sum(dn1 * n_hat, axis=0, keepdims=True)
    out_gtok[x] = low(dx1[...] + norm_back(dn1, n_hat, rs, gain_d(0)))

    @pl.when(p == 1)
    def _():
        for d in (1, 2, 3, 0):
            over_cores(d).start()
        row_grad("P1", f_all, dhc)

    sum_wait("df", df_rb)
    dfv = summed(df_sb, df_rb)
    gvs_lc = jnp.sum(dfv * cn[...], axis=0, keepdims=True)
    dcn[...] = norm_back(dfv, cn[...], crs[:, 0:1], gain_c(49))

    @pl.loop(0, c_dim // LANE)
    def _(ch):
        lanes = lanes_of(ch, LANE)
        taps = vec_c[:, lanes]
        back = depthwise(dcn[:, lanes], lambda k: taps[48 - k : 49 - k], 7)
        out_ggrid[x, :, lanes] = low(dc2t[:, lanes] + back)

    @pl.when(p == 1)
    def _():
        remote(out_ggrid.at[x], dcot, c_send, c_recv, sib).start()
        attention_grads()
        layer_output(dx1)
        exchange(0, hid_tok)
        reduce_end(*early)

    @pl.when(p == 0)
    def _():
        reduce_end("P2")

    exchange(2, out_gtok)
    exchange(3, out_ggrid)

    @pl.loop(0, Z)
    def _(z):
        for part in range(cz // LANE):
            lanes = pl.ds(pl.multiple_of(z * cz + part * LANE, LANE), LANE)

            def put(k, row):
                gvs[z, k : k + 1, part * LANE : (part + 1) * LANE] = row

            depthwise_taps(wide(c_in[:, lanes]), dcn[:, lanes], 7, put)

    for z in range(Z):
        gvs[z, 49:50] = gvs_lc[:, z * cz : (z + 1) * cz]
        gvs[z, 50:51] = gvs_ls[:, z * cz : (z + 1) * cz]
        gvs[z, 51:64] = jnp.zeros((13, cz), F32)
        gvs[z, 56:57, 0:dz] = gvs_d0[:, z * dz : (z + 1) * dz]
        gvs[z, 57:58, 0:dz] = gvs_d1[:, z * dz : (z + 1) * dz]
    gvs_low[...] = low(gvs[...])
    scatter_start("gv", gvs_low, gv_rb)

    def group_copy(n, k, src, dst):
        rr, xx = owner(k)
        return remote(src, dst, gx_send.at[n, k], gx_recv.at[n, k], dev(rr=rr, xx=xx))

    for k in range(3):
        c = group_copy(1, k, gad, gad_rb.at[k])
        c.start()
        sent.append(c)
    @pl.when(p == 1)
    def _():
        reduce_middle("P2", "P1")
        reduce_end("P2")

    reduce_end("P1")
    scatter_wait("gv", gv_rb)
    gvx[3] = (gvs[zi] + wide(gv_rb[0])) + (wide(gv_rb[1]) + wide(gv_rb[2]))
    for k in range(3):
        c = group_copy(0, k, gvx.at[3], gvx.at[k])
        c.start()
        sent.append(c)
    for k in range(3):
        group_copy(1, k, gad, gad_rb.at[k]).wait_recv()
    gad_all[zi] = (gad[x] + gad_rb[0, x]) + (gad_rb[1, x] + gad_rb[2, x])
    gather_start("gad", gad_all)

    reduce_middle("Q", "O")
    reduce_end("Q", "O")

    for k in range(3):
        group_copy(0, k, gvx.at[k], gvx.at[k]).wait_recv()
    total = (gvx[0] + gvx[1]) + (gvx[2] + gvx[3])
    mine = jnp.where(ri == 1, pltpu.roll(total, c_own, 1), total)[:, 0:c_own]
    mine_d = jnp.where(ri == 1, total[:, LANE : 2 * LANE], total[:, 0:LANE])

    def flag(n):
        return train_in[0, n].astype(F32)

    out_depth[...] = mine[0:taps7] * flag(0)
    out_ln_conv[...] = mine[49:50] * flag(1)
    out_scale[...] = mine[50:51] * flag(4)
    out_ln_attn[...] = mine_d[56:57]
    out_ln_mlp[...] = mine_d[57:58]
    gather_wait("gad", gad_all)
    for z in range(Z):
        out_ad[:, z * adq : (z + 1) * adq] = gad_all[z][0:9]
    for name in ARRAYS:
        back_local(name).wait()
        for d in range(1, Z):
            n = ids[name]
            slot = quarter_of(name, native[name], zfrom(d))
            remote(slot, slot, a_send.at[n, d - 1], a_recv.at[n, d - 1], dev(zto(d))).wait_recv()
    for n, buf in enumerate((hid_tok, hid_grid, out_gtok, out_ggrid)):
        c = remote(buf.at[x], buf.at[x], xo_send.at[n], xo_recv.at[n], over_x)
        c.wait_send()
        remote(buf.at[xo], buf.at[xo], xo_send.at[n], xo_recv.at[n], over_x).wait_recv()

    @pl.when(p == 0)
    def _():
        remote(hid_tok.at[x], x_in, h_send.at[0], h_recv.at[0], sib).wait_send()
        remote(hid_grid.at[x], c_in, h_send.at[1], h_recv.at[1], sib).wait_send()

    @pl.when(p == 1)
    def _():
        for d in range(Z):
            over_cores(d).wait_send()
        remote(out_ggrid.at[x], dcot, c_send, c_recv, sib).wait_send()

    for name, buf in line_gathers:
        line_sent(name, buf)

    @pl.when(p == 1)
    def _():
        line_sent("dx3", dx3_all)

    for name, sb, rb in line_sums:
        sum_sent(name, sb, rb)
    for c in sent:
        c.wait_send()
    for name in ARRAYS:
        for which in range(4):
            for d in pieces(name):
                hop_copy(name, which, d).wait_send()
        for d in range(1, Z):
            back_copy(name, d).wait_send()


def run_layers(weights, vectors, order, train, streams, sizes, outer):
    d_dim, c_dim, hq, ffq, cfq, adw, dg = sizes
    vm = pltpu.VMEM
    blocks = []
    for name, value in zip(ARRAYS, weights):
        if name == "Q":
            blocks.append((3, value.shape[1], hq))
        elif name in ("O", "F2"):
            blocks.append((value.shape[0] // Z, value.shape[1]))
        else:
            blocks.append((value.shape[0], value.shape[1] // Z))
    rows = Z * TOK

    def act(width, count=Z, kind=BF):
        return vm((count, TOK, width), kind)

    def line(width):
        return vm((2, 3, TOK, width), BF)

    scratch = [vm((2, Z, R) + s, BF) for s in blocks] + [
        vm(lead + s[:-2] + (s[-2] // 2, s[-1]), BF)
        for s in blocks
        for lead in ((Z, R), (2, Z), (Z,), (Z,))
    ]
    scratch += [
        vm((64, 2 * LANE), F32), vm((64, 2 * LANE), BF), vm((Z * R, 64, 2 * LANE), BF), vm((2, 16, adw), F32), vm((64, c_dim), F32), vm((8, d_dim), F32),
        vm((TOK, d_dim), BF), vm((TOK, c_dim), BF), act(d_dim), act(c_dim), act(d_dim), act(c_dim),
        act(d_dim), line(d_dim), act(c_dim), line(c_dim), act(d_dim), line(d_dim),
        act(2 * adw), act(2 * adw, 3), vm((4, 8, dg), F32), vm((4, 8, dg), F32),
        vm((2, rows, 3 * hq), BF), vm((2, hq // HD, Z, TOK, TOK), BF), vm((2, rows, hq), BF),
        vm((2, rows, ffq), BF), vm((2, rows, ffq), BF), vm((2, rows, cfq), BF), vm((2, rows, cfq), BF),
        vm((TOK, c_dim), F32), vm((TOK, LANE), F32), vm((TOK, c_dim), F32), vm((TOK, d_dim), F32), vm((TOK, c_dim), F32),
        vm((2, rows, adw), F32), vm((2, Z, TOK, adw), F32), vm((2, 8, adw), F32), vm((2, 8, adw), F32),
        vm((TOK, d_dim), BF), vm((TOK, c_dim), BF), act(d_dim), act(d_dim), line(d_dim), act(c_dim), line(c_dim),
        act(d_dim), act(c_dim),
        act(d_dim), line(d_dim), act(c_dim), line(c_dim), vm((2, rows, ffq), BF), vm((2, rows, hq), BF),
        vm((2, rows, 3 * hq), BF), vm((2, rows, cfq), BF), vm((TOK, d_dim), F32), vm((TOK, c_dim), F32), vm((2, rows, adw), BF),
        vm((TOK, c_dim), F32),
        vm((Z, 64, c_dim // Z), F32), vm((Z, 64, c_dim // Z), BF), vm((3, 64, c_dim // Z), BF), vm((4, 64, c_dim // Z), F32),
        vm((2, 16, adw), F32), vm((3, 2, 16, adw), F32), vm((Z, 16, adw), F32),
        vm((2 * ffq, rows), BF),
    ]
    dma = pltpu.SemaphoreType.DMA
    na = len(ARRAYS)
    scratch += [
        dma((len(EVENTS), 3)), dma((len(EVENTS), 3)), dma((len(EVENTS), 6)), dma((len(EVENTS), 6)), dma((na, 3)), dma((na, 3)), dma((na,)),
        dma((na, 4, Z)), dma((na, 4, Z)), dma((7,)), dma((7,)), dma, dma, dma((2,)), dma((2,)), dma((Z,)), dma((Z,)), dma, dma,
        dma((4,)), dma((4,)), dma((na, 4, Z)), dma((na, 4, Z)), dma((na, 3)), dma((na, 3)), dma((2, 3)), dma((2, 3)),
        pltpu.SemaphoreType.REGULAR,
    ]
    sds = jax.ShapeDtypeStruct
    out_shape = [sds((2, TOK, d_dim), BF), sds((2, TOK, c_dim), BF)] * 2
    out_shape += [sds(value.shape, BF) for value in weights]
    out_shape += [sds(value.shape, F32) for value in vectors]
    any_spec = pl.BlockSpec(memory_space=pl.ANY)
    vm_spec = pl.BlockSpec(memory_space=pltpu.VMEM)
    sm_spec = pl.BlockSpec(memory_space=pltpu.SMEM)
    return pl.pallas_call(
        functools.partial(main_kernel, sizes, outer),
        out_shape=out_shape,
        in_specs=[any_spec] * na + [vm_spec] * 6 + [sm_spec] * 2 + [vm_spec] * 4,
        out_specs=[vm_spec] * 4 + [any_spec] * na + [vm_spec] * 6,
        scratch_shapes=scratch,
        compiler_params=pltpu.CompilerParams(
            collective_id=0, has_side_effects=True, vmem_limit_bytes=62 * 1024 * 1024
        ),
        cost_estimate=pl.CostEstimate(flops=26 * 10**9, bytes_accessed=10**8, transcendentals=10**7),
        name="layers",
    )(*weights, *vectors, order, train, *streams)


def per_device(
    tokens,
    conv_grid,
    order,
    trainable,
    ln_attn,
    w_qkv,
    w_attn_out,
    ln_mlp,
    w_fc_in,
    w_fc_out,
    conv_depth,
    ln_conv,
    w_pw_in,
    w_pw_out,
    layer_scale,
    w_adapt,
    adapt_depth,
    w_gate_in,
    w_gate_out,
    tok_cot,
    grid_cot,
):
    dp_count = lax.axis_size("dp")
    outer = dp_count // (Z * R)
    groups = [[g * outer + o for o in range(outer)] for g in range(Z * R)]
    layer_at = lax.axis_index("pipe")

    def block(value, axis):
        value = value[0]
        if outer == 1:
            return value
        return lax.all_gather(value, "dp", axis=axis, tiled=True, axis_index_groups=groups)

    def share(value, axis):
        if outer > 1:
            value = lax.psum_scatter(
                value, "dp", scatter_dimension=axis, tiled=True, axis_index_groups=groups
            )
        return value[None]

    qkv = block(w_qkv, 1)
    gate_in = block(w_gate_in, 1).T
    pw_in = block(w_pw_in, 0)
    adapt = block(w_adapt, 0)
    fc_in = block(w_fc_in, 0)
    weights = (
        pw_in,
        block(w_pw_out, 1).T,
        qkv,
        block(w_attn_out, 1),
        adapt,
        gate_in,
        block(w_gate_out, 0),
        fc_in,
        block(w_fc_out, 1),
    )
    vectors = (
        block(conv_depth, 1),
        block(ln_conv, 0)[None],
        block(layer_scale, 0)[None],
        block(ln_attn, 0)[None],
        block(ln_mlp, 0)[None],
        adapt_depth[0],
    )
    spread = Z * R
    sizes = (
        qkv.shape[1] * spread, pw_in.shape[0] * spread, qkv.shape[2] // Z, fc_in.shape[1] // Z,
        pw_in.shape[1] // Z, adapt.shape[1] // Z, gate_in.shape[0] * spread,
    )

    def rows_of(value):
        return value.reshape(value.shape[0], TOK, value.shape[-1])

    streams = [rows_of(value) for value in (tokens, conv_grid, tok_cot, grid_cot)]
    outs = run_layers(weights, vectors, order, trainable, streams, sizes, outer)
    hid_tok, hid_grid, g_tok, g_grid = outs[:4]
    g_p1, g_p2, g_q, g_o, g_e, g_gi, g_go, g_f1, g_f2 = [value.astype(F32) for value in outs[4:13]]
    g_depth, g_ln_conv, g_scale, g_ln_attn, g_ln_mlp, g_ad = outs[13:]

    swap = (layer_at == 0) & (order[0, 0] == 1)
    g_tok = jnp.where(swap, g_tok[::-1], g_tok)
    g_grid = jnp.where(swap, g_grid[::-1], g_grid)
    grid_shape = (1,) + conv_grid.shape
    tok_shape = (1,) + tokens.shape
    flags = trainable[0].astype(F32)
    if outer > 1:
        g_ad = lax.psum(g_ad, "dp", axis_index_groups=groups)
    return (
        hid_tok.reshape(tok_shape),
        hid_grid.reshape(grid_shape),
        g_tok.reshape(tok_shape),
        g_grid.reshape(grid_shape),
        share(g_ln_attn[0], 0),
        share(g_q, 1),
        share(g_o, 1),
        share(g_ln_mlp[0], 0),
        share(g_f1, 0),
        share(g_f2, 1),
        share(g_depth, 1),
        share(g_ln_conv[0], 0),
        share(g_p1 * flags[2], 0),
        share((g_p2 * flags[3]).T, 1),
        share(g_scale[0], 0),
        share(g_e, 0),
        g_ad[None],
        share(g_gi.T, 1),
        share(g_go, 0),
    )


def solution(mesh):
    in_specs = (
        P(None, "dp", None, None),
        P(None, "dp", None, None, None),
        P("dp", None),
        P("pipe", None),
        P("pipe", "dp"),
        P("pipe", None, "dp", "tensor"),
        P("pipe", "tensor", "dp"),
        P("pipe", "dp"),
        P("pipe", "dp", "tensor"),
        P("pipe", "tensor", "dp"),
        P("pipe", None, "dp"),
        P("pipe", "dp"),
        P("pipe", "dp", "tensor"),
        P("pipe", "tensor", "dp"),
        P("pipe", "dp"),
        P("pipe", "dp", "tensor"),
        P("pipe", None, "tensor"),
        P("pipe", "tensor", "dp"),
        P("pipe", "dp", "tensor"),
        P(None, "dp", None, None),
        P(None, "dp", None, None, None),
    )
    out_specs = (
        P("pipe", None, "dp", None, None),
        P("pipe", None, "dp", None, None, None),
        P("pipe", None, "dp", None, None),
        P("pipe", None, "dp", None, None, None),
        P("pipe", "dp"),
        P("pipe", None, "dp", "tensor"),
        P("pipe", "tensor", "dp"),
        P("pipe", "dp"),
        P("pipe", "dp", "tensor"),
        P("pipe", "tensor", "dp"),
        P("pipe", None, "dp"),
        P("pipe", "dp"),
        P("pipe", "dp", "tensor"),
        P("pipe", "tensor", "dp"),
        P("pipe", "dp"),
        P("pipe", "dp", "tensor"),
        P("pipe", None, "tensor"),
        P("pipe", "tensor", "dp"),
        P("pipe", "dp", "tensor"),
    )
    return jax.shard_map(
        per_device, mesh=mesh, in_specs=in_specs, out_specs=out_specs, check_vma=False
    )
```

```python
import functools

import jax
import jax.numpy as jnp
from jax import lax
from jax.experimental import pallas as pl
from jax.experimental.pallas import tpu as pltpu
from jax.sharding import PartitionSpec as P

HD = 64
Z = 4
R = 2
TOK = 64
SIDE = 8
LANE = 128
BF = jnp.bfloat16
F32 = jnp.float32
ARRAYS = ("P1", "P2", "Q", "O", "E", "Gi", "Go", "F1", "F2")
EVENTS = (
    "n1", "f", "o", "cv", "n2", "c2", "m", "br", "gs",
    "dx3", "dgh", "dn2", "dc2", "dx1", "dcv", "dn1", "df", "gv", "gad",
)


def mm(a, b):
    return lax.dot_general(a, b, (((1,), (0,)), ((), ())), preferred_element_type=F32)


def mm_nt(a, b):
    return lax.dot_general(a, b, (((1,), (1,)), ((), ())), preferred_element_type=F32)


def mm_tn(a, b):
    return lax.dot_general(a, b, (((0,), (0,)), ((), ())), preferred_element_type=F32)


def flat(value):
    return value.reshape(-1, value.shape[-1])


def low(value):
    return value.astype(BF)


def wide(value):
    return value.astype(F32)


def gelu_pair(h):
    phi = 0.5 * (1.0 + lax.erf(h * 0.7071067811865476))
    dens = jnp.exp(-0.5 * h * h) * 0.3989422804014327
    return h * phi, phi + h * dens


def normed(value):
    centred = value - jnp.mean(value, axis=-1, keepdims=True)
    rs = lax.rsqrt(jnp.mean(centred * centred, axis=-1, keepdims=True) + 1e-06)
    return centred * rs, rs


def norm_back(dn, n_hat, rs, gain):
    gd = dn * gain
    return (
        gd
        - jnp.mean(gd, axis=-1, keepdims=True)
        - n_hat * jnp.mean(gd * n_hat, axis=-1, keepdims=True)
    ) * rs


def col_shift(value, by):
    if by == 0:
        return value
    at = lax.broadcasted_iota(jnp.int32, value.shape, 0) % SIDE
    rolled = pltpu.roll(value, (-by) % TOK, 0)
    return jnp.where((at + by >= 0) & (at + by < SIDE), rolled, 0.0)


def row_shift(value, by):
    if by == 0:
        return value
    gap = jnp.zeros((abs(by) * SIDE, value.shape[1]), value.dtype)
    if by > 0:
        return jnp.concatenate([value[by * SIDE :], gap], axis=0)
    return jnp.concatenate([gap, value[: TOK + by * SIDE]], axis=0)


def depthwise(value, tap, side):
    half = side // 2
    shifted = [col_shift(value, b - half) for b in range(side)]
    total = None
    for a in range(side):
        line = None
        for b in range(side):
            term = shifted[b] * tap(a * side + b)
            line = term if line is None else line + term
        line = row_shift(line, a - half)
        total = line if total is None else total + line
    return total


def depthwise_taps(value, grad, side, put):
    half = side // 2
    shifted = [col_shift(value, b - half) for b in range(side)]
    for a in range(side):
        d = a - half
        lo, hi = max(0, -d) * SIDE, (SIDE - max(0, d)) * SIDE
        for b in range(side):
            part = shifted[b][lo + d * SIDE : hi + d * SIDE] * grad[lo:hi]
            put(a * side + b, jnp.sum(part, axis=0, keepdims=True))


def lanes_of(at, width):
    return pl.ds(pl.multiple_of(at * width, width), width)


def side_by_side(blocks):
    return jnp.concatenate(blocks, axis=1)


def main_kernel(dims, outer, *refs):
    at = iter(refs)

    def take(count):
        return [next(at) for _ in range(count)]

    na = len(ARRAYS)
    source = dict(zip(ARRAYS, take(na)))
    (
        depth_in, ln_conv_in, scale_in, ln_attn_in, ln_mlp_in, adapt_depth_in,
        order_in, train_in, tok_in, grid_in, tcot_in, gcot_in,
    ) = take(12)
    hid_tok, hid_grid, out_gtok, out_ggrid = take(4)
    native = dict(zip(ARRAYS, take(na)))
    out_depth, out_ln_conv, out_scale, out_ln_attn, out_ln_mlp, out_ad = take(6)
    W = dict(zip(ARRAYS, take(na)))
    hops = take(4 * na)
    RX = {name: hops[4 * n : 4 * n + 4] for n, name in enumerate(ARRAYS)}
    (
        v_loc, v_low, vv, aq, vec_c, vec_d, x_in, c_in, n1_all, f_all, n2_all, c2_all,
        o_sb, o_rb, cv_sb, cv_rb, m_sb, m_rb, br_sb, br_rb, gsb, dgb,
        qkv, prob, ctx, u, up, r, rp, cn, crs, cv_sum, x1, c2f,
        adapted, spread, pooled, gate,
        dx3, dcot, dx3_all, dn2_sb, dn2_rb, dc2_sb, dc2_rb, dx1_all, dcv_all,
        dn1_sb, dn1_rb, df_sb, df_rb, dh, do_all, dqkv, dhc, dx1, dc2t, dad, dcn,
        gvs, gvs_low, gv_rb, gvx, gad, gad_rb, gad_all, turned,
    ) = take(67)
    (
        zs_send, zs_recv, l_send, l_recv, s1_send, s1_recv, loc_sem, s2_send, s2_recv,
        v_send, v_recv, q_send, q_recv, h_send, h_recv, b_send, b_recv, c_send, c_recv,
        xo_send, xo_recv, g_send, g_recv, a_send, a_recv, gx_send, gx_recv, go,
    ) = take(28)

    p = lax.axis_index("pipe")
    dpi = lax.axis_index("dp")
    x = lax.axis_index("tensor")
    rest = dpi % outer
    zi = dpi // (outer * R)
    ri = (dpi // outer) % R
    xo = 1 - x
    ro = 1 - ri
    d_dim, c_dim, hq, ffq, cfq, adq, dg = dims
    adh = Z * adq
    dz, cz = d_dim // Z, c_dim // Z
    tile = 256
    ids = {name: number for number, name in enumerate(ARRAYS)}
    ev = {name: number for number, name in enumerate(EVENTS)}

    def dev(z=None, rr=None, xx=None, pp=None):
        z = zi if z is None else z
        rr = ri if rr is None else rr
        return (
            p if pp is None else pp,
            (z * R + rr) * outer + rest,
            x if xx is None else xx,
        )

    def zto(d):
        return lax.rem(zi + d, Z)

    def zfrom(d):
        return lax.rem(zi + Z - d, Z)

    def remote(src, dst, ssem, rsem, device):
        return pltpu.make_async_remote_copy(
            src_ref=src, dst_ref=dst, send_sem=ssem, recv_sem=rsem,
            device_id=device, device_id_type=pl.DeviceIdType.MESH,
        )

    sib = dev(pp=1 - p)
    over_r, over_x = dev(rr=ro), dev(xx=xo)

    def z_copy(e, d, src, dst):
        return remote(src, dst, zs_send.at[e, d - 1], zs_recv.at[e, d - 1], dev(zto(d)))

    sent = []

    def gather_copies(name, buf):
        return [z_copy(ev[name], d, buf.at[zi], buf.at[zi]) for d in range(1, Z)]

    def gather_start(name, buf, keep=True):
        copies = gather_copies(name, buf)
        for c in copies:
            c.start()
        if keep:
            sent.extend(copies)

    def gather_wait(name, buf):
        for d in range(1, Z):
            slot = buf.at[zfrom(d)]
            z_copy(ev[name], d, slot, slot).wait_recv()

    def scatter_start(name, sb, rb):
        for d in range(1, Z):
            c = z_copy(ev[name], d, sb.at[zto(d)], rb.at[d - 1])
            c.start()
            sent.append(c)

    def scatter_wait(name, rb):
        for d in range(1, Z):
            z_copy(ev[name], d, rb.at[d - 1], rb.at[d - 1]).wait_recv()

    def right():
        return dev(zi + 1)

    def left():
        return dev(zi - 1)

    def pass_copy(name, buf, toward, s):
        e, k = ev[name], (0 if toward > 0 else 3) + s
        blk = buf.at[zi - toward * s]
        return remote(blk, blk, l_send.at[e, k], l_recv.at[e, k], right() if toward > 0 else left())

    def pass_cond(toward, s):
        if toward > 0:
            return (zi < Z - 1) & (zi - s >= 0)
        return (zi > 0) & (zi + s <= Z - 1)

    def line_start(name, buf):
        for toward in (1, -1):

            @pl.when(pass_cond(toward, 0))
            def _():
                pass_copy(name, buf, toward, 0).start()

    def line_step(name, buf, *steps):
        e = ev[name]
        for s in steps:
            for toward in (1, -1):
                src = zi - toward * s

                @pl.when((src >= 0) & (src <= Z - 1))
                def _():
                    blk = buf.at[src]
                    k = (0 if toward > 0 else 3) + s - 1
                    remote(blk, blk, l_send.at[e, k], l_recv.at[e, k], sib).wait_recv()

                if s < Z - 1:

                    @pl.when(pass_cond(toward, s))
                    def _():
                        pass_copy(name, buf, toward, s).start()

    def line_sent(name, buf):
        for toward in (1, -1):
            for s in range(Z - 1):

                @pl.when(pass_cond(toward, s))
                def _():
                    pass_copy(name, buf, toward, s).wait_send()

    def sum_copy(name, sb, rb, toward, k, first):
        e, way = ev[name], (0 if toward > 0 else 1)
        src = sb.at[zi + toward * k] if first else rb.at[way, k]
        q = way * 3 + k - 1
        return remote(src, rb.at[way, k - 1], l_send.at[e, q], l_recv.at[e, q], right() if toward > 0 else left())

    def at_end(toward):
        return zi == (0 if toward > 0 else Z - 1)

    def passes(toward, k):
        dest = zi + toward * k
        return jnp.logical_not(at_end(toward)) & (dest >= 0) & (dest <= Z - 1)

    def sum_start(name, sb, rb):
        for toward in (1, -1):

            @pl.when(at_end(toward))
            def _():
                for k in (3, 2, 1):
                    sum_copy(name, sb, rb, toward, k, True).start()

    def sum_arrival(name, rb, way, k):
        e = ev[name]
        slot = rb.at[way, k]
        return remote(slot, slot, l_send.at[e, way * 3 + k], l_recv.at[e, way * 3 + k], sib)

    def sum_step(name, sb, rb, *ks):
        for k in ks:
            for way, toward in enumerate((1, -1)):

                @pl.when(passes(toward, k))
                def _():
                    sum_arrival(name, rb, way, k).wait_recv()
                    rb[way, k] = low(wide(rb[way, k]) + wide(sb[zi + toward * k]))
                    sum_copy(name, sb, rb, toward, k, False).start()

    def sum_wait(name, rb):
        for way, toward in enumerate((1, -1)):

            @pl.when(jnp.logical_not(at_end(toward)))
            def _():
                sum_arrival(name, rb, way, 0).wait_recv()

    def summed(sb, rb):
        return wide(sb[zi]) + (wide(rb[0, 0]) + wide(rb[1, 0]))

    def sum_sent(name, sb, rb):
        for toward in (1, -1):

            @pl.when(at_end(toward))
            def _():
                for k in (3, 2, 1):
                    sum_copy(name, sb, rb, toward, k, True).wait_send()

            for k in (2, 1):

                @pl.when(passes(toward, k))
                def _():
                    sum_copy(name, sb, rb, toward, k, False).wait_send()

    def share_start(name, buf):
        for d in range(1, Z):
            c = z_copy(ev[name], d, buf.at[3], buf.at[d - 1])
            c.start()
            sent.append(c)

    def scattered(sb, rb):
        return (wide(sb[zi]) + wide(rb[0])) + (wide(rb[1]) + wide(rb[2]))

    barrier = pltpu.get_barrier_semaphore()
    greeted = [sib]
    for d in range(1, Z):
        greeted += [dev(zto(d)), dev(zto(d), ro), dev(zto(d), pp=1 - p)]
    greeted += [over_r, over_x, dev(rr=ro, xx=xo)]
    for device in greeted:
        pl.semaphore_signal(barrier, inc=1, device_id=device, device_id_type=pl.DeviceIdType.MESH)
    v_loc[...] = jnp.zeros(v_loc.shape, F32)
    taps7 = depth_in.shape[0]
    c_own = depth_in.shape[1]
    v_loc[0:taps7, 0:c_own] = wide(depth_in[...])
    v_loc[49:50, 0:c_own] = wide(ln_conv_in[...])
    v_loc[50:51, 0:c_own] = wide(scale_in[...])
    v_loc[56:57, 0:LANE] = wide(ln_attn_in[...])
    v_loc[57:58, 0:LANE] = wide(ln_mlp_in[...])
    aq[x] = jnp.zeros(aq.shape[1:], F32)
    aq[x, 0:9] = wide(adapt_depth_in[:, lanes_of(zi, adq)])
    v_low[...] = low(v_loc[...])
    line_sums = (
        ("o", o_sb, o_rb), ("cv", cv_sb, cv_rb), ("m", m_sb, m_rb), ("dn2", dn2_sb, dn2_rb),
        ("dc2", dc2_sb, dc2_rb), ("dn1", dn1_sb, dn1_rb), ("df", df_sb, df_rb),
    )
    line_gathers = (
        ("n1", n1_all), ("f", f_all), ("n2", n2_all), ("c2", c2_all), ("dx1", dx1_all), ("dcv", dcv_all),
    )
    for _, _, rb in line_sums:
        for way, toward in enumerate((1, -1)):

            @pl.when(at_end(toward))
            def _():
                rb[way, 0] = jnp.zeros(rb.shape[2:], BF)

    pl.semaphore_wait(barrier, len(greeted))

    me8 = zi * R + ri
    v_arrivals = []
    for n, (d, flip) in enumerate([(d, s) for d in range(Z) for s in (0, 1)][1:]):
        tr = ro if flip else ri
        c = remote(v_low, vv.at[me8], v_send.at[n], v_recv.at[n], dev(zto(d), tr))
        c.start()
        sent.append(c)
        fr = zfrom(d) * R + tr
        v_arrivals.append(remote(vv.at[fr], vv.at[fr], v_send.at[n], v_recv.at[n], dev(zto(d), tr)))
    vv[me8] = v_low[...]
    c = remote(aq.at[x], aq.at[x], q_send, q_recv, over_x)
    c.start()
    sent.append(c)

    by_rows = ("O", "F2")

    def quarter_of(name, ref, z):
        if name == "Q":
            return ref.at[:, :, lanes_of(z, hq)]
        if name in by_rows:
            height = ref.shape[0] // Z
            return ref.at[pl.ds(pl.multiple_of(z * height, height), height)]
        return ref.at[:, lanes_of(z, ref.shape[1] // Z)]

    def step1_local(name):
        return pltpu.make_async_copy(
            quarter_of(name, source[name], zi), W[name].at[x, zi, ri], loc_sem.at[ids[name]]
        )

    def step1_copy(name, d):
        k = ids[name]
        return remote(
            quarter_of(name, source[name], zto(d)), W[name].at[x, zi, ri],
            s1_send.at[k, d - 1], s1_recv.at[k, d - 1], dev(zto(d)),
        )

    def half_of(name, j, z, rr, upper):
        w = W[name]
        half = w.shape[-2] // 2
        rows = slice(half, None) if upper else slice(0, half)
        if len(w.shape) == 6:
            return w.at[j, z, rr, :, rows]
        return w.at[j, z, rr, rows]

    def step2_copy(name, which, d):
        k = ids[name]
        z = zfrom(d)
        if which < 2:
            src = quarter_of(name, source[name], zi) if d == 0 else W[name].at[x, z, ri]
            dst = W[name].at[x, z, ri]
        else:
            src = dst = half_of(name, x, z, ro, False) if which == 2 else half_of(name, xo, z, ri, True)
        to = over_x if which in (1, 2) else over_r
        return remote(src, dst, s2_send.at[k, which, d], s2_recv.at[k, which, d], to)

    def step2_arrival(name, which, d):
        k = ids[name]
        z = zfrom(d)
        if which < 2:
            ref = W[name].at[x, z, ro] if which == 0 else W[name].at[xo, z, ri]
        else:
            ref = half_of(name, xo, z, ro, which == 3)
        to = over_x if which in (1, 2) else over_r
        return remote(ref, ref, s2_send.at[k, which, d], s2_recv.at[k, which, d], to)

    def relay1(*names):
        for name in names:
            for d in range(1, Z):
                step1_copy(name, d).start()

    def relay0(*names):
        for name in names:
            step1_local(name).start()
            step2_copy(name, 0, 0).start()
            step2_copy(name, 1, 0).start()

    def relay2(name, ds=(1, 2, 3)):
        k = ids[name]
        for d in ds:
            slot = W[name].at[x, zfrom(d), ri]
            remote(slot, slot, s1_send.at[k, d - 1], s1_recv.at[k, d - 1], dev(zto(d))).wait_recv()
            step2_copy(name, 0, d).start()
            step2_copy(name, 1, d).start()

    def relay3(name, ds=(0, 1, 2, 3)):
        for d in ds:
            step2_arrival(name, 0, d).wait_recv()
            step2_copy(name, 2, d).start()
            step2_arrival(name, 1, d).wait_recv()
            step2_copy(name, 3, d).start()

    def relay4(*names):
        for name in names:
            step1_local(name).wait()
            for d in range(Z):
                step2_arrival(name, 2, d).wait_recv()
                step2_arrival(name, 3, d).wait_recv()

    def relay_sent():
        for name in ARRAYS:
            for d in range(1, Z):
                step1_copy(name, d).wait_send()
            for which in range(4):
                for d in range(Z):
                    step2_copy(name, which, d).wait_send()

    @pl.when(p == 0)
    def _():
        relay0("P1")
        relay1("P1")
        relay0("P2")
        relay1("P2")
        relay0("Q", "O", "E", "Gi", "Go", "F1", "F2")

    @pl.when(p == 1)
    def _():
        dx3[...] = tcot_in[x]
        dcot[...] = gcot_in[x]
        dx3_all[zi] = tcot_in[x]
        line_start("dx3", dx3_all)

    for c in v_arrivals:
        c.wait_recv()
    remote(aq.at[xo], aq.at[xo], q_send, q_recv, over_x).wait_recv()
    low_lanes = lax.broadcasted_iota(jnp.int32, (64, LANE), 1) < LANE // 2
    for z in range(Z):
        first, second = wide(vv[2 * z]), pltpu.roll(wide(vv[2 * z + 1]), LANE // 2, 1)
        vec_c[:, z * cz : z * cz + LANE] = first[:, 0:LANE]
        vec_c[:, z * cz + LANE : z * cz + 2 * LANE] = jnp.where(
            low_lanes, first[:, LANE:], second[:, 0:LANE]
        )
        vec_c[:, z * cz + 2 * LANE : (z + 1) * cz] = second[:, LANE:]
    for i in range(Z * R):
        vec_d[:, i * LANE : (i + 1) * LANE] = wide(vv[i])[56:64, 0:LANE]

    def gain_d(row):
        return vec_d[row : row + 1, :]

    def gain_c(row):
        return vec_c[row : row + 1, :]

    def token_entry():
        n_hat, _ = normed(wide(x_in[...]))
        n1_all[zi] = low(n_hat * gain_d(0))
        line_start("n1", n1_all)

    def conv_entry():
        @pl.loop(0, c_dim // LANE)
        def _(ch):
            lanes = lanes_of(ch, LANE)
            taps = vec_c[:, lanes]
            cn[:, lanes] = depthwise(wide(c_in[:, lanes]), lambda k: taps[k : k + 1], 7)

        n_hat, rs = normed(cn[...])
        cn[...] = n_hat
        crs[...] = jnp.broadcast_to(rs, crs.shape)
        f_all[zi] = low(n_hat * gain_c(49))
        line_start("f", f_all)

    def first_relays(pump):
        relay2("P1")
        pump(1)
        relay1("Q", "O")
        relay2("P2")
        pump(2)
        relay3("P1")


    @pl.when(p == 0)
    def _():
        first = order_in[0, x] == 0
        c_in[...] = jnp.where(first, grid_in[0], grid_in[1])
        x_in[...] = jnp.where(first, tok_in[0], tok_in[1])
        conv_entry()
        token_entry()

        def pump(s):
            line_step("f", f_all, s)
            line_step("n1", n1_all, s)

        first_relays(pump)
        line_step("f", f_all, 3)
        line_step("n1", n1_all, 3)

    @pl.when(p == 1)
    def _():
        pl.semaphore_wait(go, 1)
        relay0("P1")
        relay1("P1")
        relay0("P2")
        relay1("P2")
        relay0("Q", "O", "E", "Gi", "Go", "F1", "F2")
        first_relays(lambda s: line_step("dx3", dx3_all, s))
        remote(c_in, c_in, h_send.at[1], h_recv.at[1], sib).wait_recv()
        conv_entry()
        line_step("dx3", dx3_all, 3)
        line_step("f", f_all, 1)

    relay2("Q")
    relay2("O")
    relay1("E", "Gi", "Go")
    relay3("P2", (0, 1))

    @pl.when(p == 1)
    def _():
        line_step("f", f_all, 2, 3)

    relay4("P1")

    def conv_hidden(j):
        act, der = gelu_pair(mm(flat(f_all[...]), flat(W["P1"][j])))
        r[j] = low(act)
        rp[j] = low(der)

    conv_hidden(0)

    relay3("P2", (2, 3))
    for name in ("E", "Gi", "Go"):
        relay2(name)
    relay1("F1")
    conv_hidden(1)
    relay3("Q")
    relay3("O")
    relay2("F1")
    relay1("F2")

    @pl.when(p == 0)
    def _():
        pl.semaphore_signal(go, inc=1, device_id=sib, device_id_type=pl.DeviceIdType.MESH)

    relay4("P2")

    def pair_rows(name, pair):
        zs = pl.ds(pair * 2, 2)
        return side_by_side([flat(W[name][0, zs]), flat(W[name][1, zs])])

    def pair_out(left, name, sb, width):
        both = side_by_side([left[0], left[1]])

        @pl.loop(0, Z // 2)
        def _(pair):
            acc = mm_nt(both, pair_rows(name, pair))
            sb[:, :, lanes_of(pair, 2 * width)] = low(acc).reshape(Z, TOK, 2 * width)

    pair_out(r, "P2", cv_sb, cz)

    sum_start("cv", cv_sb, cv_rb)

    for name in ("E", "Gi", "Go"):
        relay3(name)
    sum_step("cv", cv_sb, cv_rb, 2)
    relay2("F2")
    sum_step("cv", cv_sb, cv_rb, 1)

    @pl.when(p == 1)
    def _():
        remote(x_in, x_in, h_send.at[0], h_recv.at[0], sib).wait_recv()
        token_entry()
        line_step("n1", n1_all, 1, 2, 3)

    relay4("Q", "O")
    wide_q = side_by_side([flat(W["Q"][j, :, :, s]) for j in range(2) for s in range(3)])
    qkv_both = low(mm(flat(n1_all[...]), wide_q))
    for j in range(2):
        qkv[j] = qkv_both[:, j * 3 * hq : (j + 1) * 3 * hq]
    @pl.loop(0, Z)
    def _(b):
        rows = lanes_of(b, TOK)
        for j in range(2):
            outs = []
            for h in range(hq // HD):
                q, kk, vals = (qkv[j, rows, s * hq + h * HD : s * hq + (h + 1) * HD] for s in range(3))
                sc = mm_nt(q, kk) * HD ** (-0.5)
                e = jnp.exp(sc - jnp.max(sc, axis=-1, keepdims=True))
                pr = low(e / jnp.sum(e, axis=-1, keepdims=True))
                prob[j, h, b] = pr
                outs.append(mm(pr, vals))
            ctx[j, rows, :] = low(side_by_side(outs))

    out_cols = [
        jnp.concatenate([W["O"][0, z, rr], W["O"][1, z, rr]], axis=0) for z in range(Z) for rr in range(R)
    ]
    o_sb[...] = low(mm(side_by_side([ctx[0], ctx[1]]), side_by_side(out_cols))).reshape(Z, TOK, d_dim)
    sum_start("o", o_sb, o_rb)

    relay3("F1")

    sum_wait("cv", cv_rb)
    cv_sum[...] = summed(cv_sb, cv_rb)
    c2f[...] = wide(c_in[...]) + gain_c(50) * cv_sum[...]
    c2_low = low(c2f[...])
    c2_all[zi] = c2_low
    line_start("c2", c2_all)
    sum_step("o", o_sb, o_rb, 2)
    hid_grid[x] = c2_low

    @pl.when(p == 0)
    def _():
        remote(hid_grid.at[x], c_in, h_send.at[1], h_recv.at[1], sib).start()

    relay3("F2")
    sum_step("o", o_sb, o_rb, 1)
    line_step("c2", c2_all, 1)
    sum_wait("o", o_rb)
    x1[...] = wide(x_in[...]) + summed(o_sb, o_rb)
    n_hat, _ = normed(x1[...])
    n2_all[zi] = low(n_hat * gain_d(1))
    line_start("n2", n2_all)

    relay4("E", "Gi", "Go")
    line_step("c2", c2_all, 2)
    line_step("n2", n2_all, 1)
    line_step("c2", c2_all, 3)
    row8 = lax.broadcasted_iota(jnp.int32, (8, adq), 0)
    gs_part = None
    ad_both = mm(flat(c2_all[...]), side_by_side([flat(W["E"][0]), flat(W["E"][1])]))
    for j in range(2):
        ad = ad_both[:, j * adq : (j + 1) * adq]
        adapted[j] = ad
        taps = aq[j]
        pool = jnp.zeros((8, adq), F32)
        for b in range(Z):
            sp = depthwise(ad[b * TOK : (b + 1) * TOK], lambda k: taps[k : k + 1], 3)
            spread[j, b] = sp
            pool = jnp.where(row8 == b, jnp.mean(sp, axis=0, keepdims=True), pool)
        pooled[j] = pool
        term = mm_nt(low(pool), flat(W["Gi"][j]))
        gs_part = term if gs_part is None else gs_part + term
    gsb[3] = gs_part
    share_start("gs", gsb)
    line_step("n2", n2_all, 2)

    relay4("F1")
    line_step("n2", n2_all, 3)
    for j in range(2):
        act, der = gelu_pair(mm(flat(n2_all[...]), flat(W["F1"][j])))
        u[j] = low(act)
        up[j] = low(der)

    scatter_wait("gs", gsb)

    def gate_hidden():
        return gelu_pair((gsb[0] + gsb[1]) + (gsb[2] + gsb[3]))

    gh, _ = gate_hidden()
    for j in range(2):
        g8 = jnp.tanh(mm(low(gh), flat(W["Go"][j])))
        gate[j] = g8
        for b in range(Z):
            br_sb[b, :, j * adq : (j + 1) * adq] = low(g8[b : b + 1] * spread[j, b])
    scatter_start("br", br_sb, br_rb)
    relay4("F2")

    u_both = side_by_side([u[0], u[1]])

    @pl.loop(0, Z // 2)
    def _(pair):
        halves = [
            side_by_side([W["F2"][j, 2 * pair + dz_, rr] for dz_ in range(2) for rr in range(R)])
            for j in range(2)
        ]
        acc = mm(u_both, jnp.concatenate(halves, axis=0))
        m_sb[:, :, lanes_of(pair, 2 * dz)] = low(acc).reshape(Z, TOK, 2 * dz)

    sum_start("m", m_sb, m_rb)

    def exchange(n, buf):
        remote(buf.at[x], buf.at[x], xo_send.at[n], xo_recv.at[n], over_x).start()

    def layer_output(total):
        sum_step("m", m_sb, m_rb, 2)
        scatter_wait("br", br_rb)
        total[...] = x1[...]
        for d in range(Z):
            piece = br_sb[zi] if d == 0 else br_rb[d - 1]
            for j in range(2):
                lanes = pl.ds(pl.multiple_of(j * adh + zfrom(d) * adq, LANE), adq)
                total[:, lanes] += wide(piece[:, j * adq : (j + 1) * adq])
        sum_step("m", m_sb, m_rb, 1)
        sum_wait("m", m_rb)
        hid_tok[x] = low(total[...] + summed(m_sb, m_rb))

    @pl.when(p == 0)
    def _():
        layer_output(dx1)
        remote(hid_tok.at[x], x_in, h_send.at[0], h_recv.at[0], sib).start()
        exchange(0, hid_tok)

    exchange(1, hid_grid)
    relay_sent()

    def over_cores(d):
        return remote(
            out_gtok.at[x], dx3_all.at[zi], b_send.at[d], b_recv.at[d], dev(zto(d), pp=1 - p)
        )

    @pl.when(p == 0)
    def _():
        for d in range(Z):
            slot = dx3_all.at[zfrom(d)]
            remote(slot, slot, b_send.at[d], b_recv.at[d], sib).wait_recv()
        dx3[...] = dx3_all[zi]

    def own_lanes(j):
        return pl.ds(pl.multiple_of(j * adh + zi * adq, LANE), adq)

    gh, ghp = gate_hidden()
    dgh_part = None
    dgp = []
    for j in range(2):
        dgate = jnp.zeros((8, adq), F32)
        for b in range(Z):
            dbr = wide(dx3_all[b, :, own_lanes(j)])
            dgate = jnp.where(row8 == b, jnp.sum(dbr * spread[j, b], axis=0, keepdims=True), dgate)
        dg8 = low(dgate * (1.0 - gate[j] * gate[j]))
        dgp.append(dg8)
        term = mm_nt(dg8, flat(W["Go"][j]))
        dgh_part = term if dgh_part is None else dgh_part + term
    dgb[3] = dgh_part
    share_start("dgh", dgb)

    for j in range(2):
        cols = side_by_side([W["F2"][j, z, rr] for z in range(Z) for rr in range(R)])
        dh[j] = low(mm_nt(flat(dx3_all[...]), cols) * wide(up[j]))

    scatter_wait("dgh", dgb)
    dgs = low(((dgb[0] + dgb[1]) + (dgb[2] + dgb[3])) * ghp)
    for j in range(2):
        dpool = mm(dgs, flat(W["Gi"][j])) * (1.0 / TOK)
        taps = aq[j]
        tap_rows = [None] * 9
        for b in range(Z):
            dsp = gate[j, b : b + 1] * wide(dx3_all[b, :, own_lanes(j)]) + dpool[b : b + 1]
            dad[j, b * TOK : (b + 1) * TOK] = low(depthwise(dsp, lambda k: taps[8 - k : 9 - k], 3))

            def put(k, row):
                tap_rows[k] = row if tap_rows[k] is None else tap_rows[k] + row

            depthwise_taps(adapted[j, b * TOK : (b + 1) * TOK], dsp, 3, put)
        for k in range(9):
            gad[j, k : k + 1] = tap_rows[k]
        gad[j, 9:16] = jnp.zeros((7, adq), F32)

    pair_out(dad, "E", dc2_sb, cz)

    sum_start("dc2", dc2_sb, dc2_rb)

    pair_out(dh, "F1", dn2_sb, dz)

    sum_start("dn2", dn2_sb, dn2_rb)
    sum_step("dc2", dc2_sb, dc2_rb, 2)

    def half_rows(name, upper):
        half = W[name].shape[-2] // 2
        rows = slice(half, None) if upper else slice(0, half)
        return (slice(None), rows) if len(W[name].shape) == 6 else (rows,)

    fine = ("P1", "P2")

    def pieces(name):
        return (1, 2, 3, 0) if name in fine else (None,)

    def block_at(d):
        return slice(None) if d is None else zto(d)

    def hop_copy(name, which, d):
        n = ids[name]
        lower, upper = half_rows(name, False), half_rows(name, True)
        z = block_at(d)
        w, buf = W[name], RX[name]
        src, dst, to = (
            lambda: (w.at[(xo, z, slice(None)) + lower], buf[0].at[z], over_x),
            lambda: (w.at[(slice(None), z, ro) + upper], buf[1].at[:, z], over_r),
            lambda: (buf[0].at[z, ro], buf[2].at[z], over_r),
            lambda: (buf[1].at[xo, z], buf[3].at[z], over_x),
        )[which]()
        k = 0 if d is None else d
        return remote(src, dst, g_send.at[n, which, k], g_recv.at[n, which, k], to)

    def reduce_start(name, d=None):
        hop_copy(name, 0, d).start()
        hop_copy(name, 1, d).start()

    def each_block(d, body):
        if d is None:
            pl.loop(0, Z)(body)
        else:
            body(zto(d))

    def per_piece(name, body):
        if name in fine:
            pl.loop(0, Z)(lambda k: body(lax.rem(k + 1, Z)))
        else:
            body(None)

    def reduce_middle(*names):
        for name in names:
            lower, upper = half_rows(name, False), half_rows(name, True)
            buf = RX[name]

            def middle(d):
                hop_copy(name, 0, d).wait_recv()

                def add_lower(z):
                    for rr in range(R):
                        own = W[name][(x, z, rr) + lower]
                        buf[0][z, rr] = low(wide(own) + wide(buf[0][z, rr]))

                each_block(d, add_lower)
                hop_copy(name, 2, d).start()
                hop_copy(name, 1, d).wait_recv()

                def add_upper(z):
                    for j in range(2):
                        own = W[name][(j, z, ri) + upper]
                        buf[1][j, z] = low(wide(own) + wide(buf[1][j, z]))

                each_block(d, add_upper)
                hop_copy(name, 3, d).start()

            per_piece(name, middle)

    def reduce_end(*names):
        for name in names:
            lower, upper = half_rows(name, False), half_rows(name, True)
            buf = RX[name]

            def end(d):
                hop_copy(name, 2, d).wait_recv()
                hop_copy(name, 3, d).wait_recv()

                def add_both(z):
                    W[name][(x, z, ri) + lower] = low(wide(buf[0][z, ri]) + wide(buf[2][z]))
                    W[name][(x, z, ri) + upper] = low(wide(buf[1][x, z]) + wide(buf[3][z]))

                each_block(d, add_both)

            if name in fine:

                @pl.loop(1, Z)
                def _(d):
                    end(d)
                    back_copy(name, d).start()

                end(0)
            else:
                end(None)
                for d in range(1, Z):
                    back_copy(name, d).start()
            back_local(name).start()

    def back_copy(name, d):
        n = ids[name]
        return remote(
            W[name].at[x, zto(d), ri], quarter_of(name, native[name], zi),
            a_send.at[n, d - 1], a_recv.at[n, d - 1], dev(zto(d)),
        )

    def back_local(name):
        return pltpu.make_async_copy(
            W[name].at[x, zi, ri], quarter_of(name, native[name], zi), loc_sem.at[ids[name]]
        )

    peers = ((1, 0), (0, 1), (1, 1))

    def owner(k):
        return (ro if peers[k][0] else ri), (xo if peers[k][1] else x)

    def row_grad(name, left, right):
        width = W[name].shape[3]
        span = R * width

        @pl.loop(0, Z)
        def _(k):
            d = lax.rem(k + 1, Z)
            z = zto(d)
            turned[0:span] = flat(left[:, :, lanes_of(z, span)]).T
            for j in range(2):
                W[name][j, z] = low(mm(turned[0:span], right[j])).reshape(R, width, -1)
            if name in fine:
                reduce_start(name, d)

        if name not in fine:
            reduce_start(name)

    def col_grad(name, left, right):
        width = left.shape[2]
        for j in range(2):
            turned[j * width : (j + 1) * width] = left[j].T

        @pl.loop(0, Z)
        def _(z):
            rhs = flat(right[:, :, lanes_of(z, dz)])
            for j in range(2):
                g = low(mm(turned[j * width : (j + 1) * width], rhs))
                for rr in range(R):
                    W[name][j, z, rr] = g[:, rr * LANE : (rr + 1) * LANE]

        reduce_start(name)

    for j in range(2):
        W["Gi"][j] = low(mm_tn(dgs, low(pooled[j]))).reshape(Z, R, -1, adq)
        W["Go"][j] = low(mm_tn(low(gh), dgp[j])).reshape(Z, R, -1, adq)
    sum_step("dc2", dc2_sb, dc2_rb, 1)
    sum_step("dn2", dn2_sb, dn2_rb, 2)
    reduce_start("Gi")
    reduce_start("Go")
    row_grad("E", c2_all, dad)
    sum_step("dn2", dn2_sb, dn2_rb, 1)

    @pl.when(p == 0)
    def _():
        remote(dcot, dcot, c_send, c_recv, sib).wait_recv()

    sum_wait("dc2", dc2_rb)
    dc2t[...] = wide(dcot[...]) + summed(dc2_sb, dc2_rb)
    gvs_ls = jnp.sum(cv_sum[...] * dc2t[...], axis=0, keepdims=True)
    dcv_all[zi] = low(dc2t[...] * gain_c(50))
    line_start("dcv", dcv_all)

    sum_wait("dn2", dn2_rb)
    dn2 = summed(dn2_sb, dn2_rb)
    n_hat, rs = normed(x1[...])
    gvs_d1 = jnp.sum(dn2 * n_hat, axis=0, keepdims=True)
    dx1[...] = wide(dx3[...]) + norm_back(dn2, n_hat, rs, gain_d(1))
    dx1_all[zi] = low(dx1[...])
    line_start("dx1", dx1_all)
    line_step("dcv", dcv_all, 1)
    col_grad("F2", u, dx3_all)
    line_step("dcv", dcv_all, 2)
    line_step("dx1", dx1_all, 1)
    row_grad("F1", n2_all, dh)

    line_step("dcv", dcv_all, 3)
    line_step("dx1", dx1_all, 2)
    for j in range(2):
        dhc[j] = low(mm(flat(dcv_all[...]), flat(W["P2"][j])) * wide(rp[j]))

    pair_out(dhc, "P1", df_sb, cz)

    sum_start("df", df_sb, df_rb)

    early = ("Gi", "Go", "E", "F2", "F1")

    def pw_grads():
        row_grad("P2", dcv_all, r)
        row_grad("P1", f_all, dhc)

    line_step("dx1", dx1_all, 3)

    @pl.when(p == 0)
    def _():
        pw_grads()

    sum_step("df", df_sb, df_rb, 2)

    out_rows = [
        side_by_side([W["O"][j, z, rr] for z in range(Z) for rr in range(R)]) for j in range(2)
    ]
    do_both = low(mm_nt(flat(dx1_all[...]), jnp.concatenate(out_rows, axis=0)))
    for j in range(2):
        do_all[j] = do_both[:, j * hq : (j + 1) * hq]
    @pl.loop(0, Z)
    def _(b):
        rows = lanes_of(b, TOK)
        for j in range(2):
            parts = [[], [], []]
            for h in range(hq // HD):
                q, kk, vals = (qkv[j, rows, s * hq + h * HD : s * hq + (h + 1) * HD] for s in range(3))
                do = do_all[j, rows, h * HD : (h + 1) * HD]
                pr = prob[j, h, b]
                dp = mm_nt(do, vals)
                prw = wide(pr)
                ds = low(prw * (dp - jnp.sum(dp * prw, axis=-1, keepdims=True)) * HD ** (-0.5))
                parts[0].append(mm(ds, kk))
                parts[1].append(mm_tn(ds, q))
                parts[2].append(mm_tn(pr, do))
            for s in range(3):
                dqkv[j, rows, s * hq : (s + 1) * hq] = low(side_by_side(parts[s]))

    dqkv_both = side_by_side([dqkv[0], dqkv[1]])

    @pl.loop(0, Z // 2)
    def _(pair):
        zs = pl.ds(pair * 2, 2)
        rows_q = side_by_side([flat(W["Q"][j, zs, :, s]) for j in range(2) for s in range(3)])
        acc = mm_nt(dqkv_both, rows_q)
        dn1_sb[:, :, lanes_of(pair, 2 * dz)] = low(acc).reshape(Z, TOK, 2 * dz)

    sum_start("dn1", dn1_sb, dn1_rb)
    sum_step("df", df_sb, df_rb, 1)
    reduce_middle("Gi", "Go", "E")

    def attention_grads():
        @pl.loop(0, Z)
        def _(z):
            turned[0:dz] = flat(n1_all[:, :, lanes_of(z, dz)]).T
            for j in range(2):
                g = low(mm(turned[0:dz], dqkv[j]))
                for s in range(3):
                    W["Q"][j, z, :, s] = g[:, s * hq : (s + 1) * hq].reshape(R, -1, hq)

        reduce_start("Q")
        col_grad("O", ctx, dx1_all)

    sum_step("dn1", dn1_sb, dn1_rb, 2)
    reduce_middle("F2", "F1")
    sum_step("dn1", dn1_sb, dn1_rb, 1)

    @pl.when(p == 0)
    def _():
        reduce_middle("P2")
        attention_grads()
        reduce_middle("P1")
        reduce_end(*early)

    sum_wait("dn1", dn1_rb)
    dn1 = summed(dn1_sb, dn1_rb)
    n_hat, rs = normed(wide(x_in[...]))
    gvs_d0 = jnp.sum(dn1 * n_hat, axis=0, keepdims=True)
    out_gtok[x] = low(dx1[...] + norm_back(dn1, n_hat, rs, gain_d(0)))

    @pl.when(p == 1)
    def _():
        for d in (1, 2, 3, 0):
            over_cores(d).start()

    sum_wait("df", df_rb)
    dfv = summed(df_sb, df_rb)
    gvs_lc = jnp.sum(dfv * cn[...], axis=0, keepdims=True)
    dcn[...] = norm_back(dfv, cn[...], crs[:, 0:1], gain_c(49))

    @pl.loop(0, c_dim // LANE)
    def _(ch):
        lanes = lanes_of(ch, LANE)
        taps = vec_c[:, lanes]
        back = depthwise(dcn[:, lanes], lambda k: taps[48 - k : 49 - k], 7)
        out_ggrid[x, :, lanes] = low(dc2t[:, lanes] + back)

    @pl.when(p == 1)
    def _():
        remote(out_ggrid.at[x], dcot, c_send, c_recv, sib).start()
        pw_grads()
        attention_grads()
        layer_output(dx1)
        exchange(0, hid_tok)
        reduce_end(*early)

    @pl.when(p == 0)
    def _():
        reduce_end("P2")

    exchange(2, out_gtok)
    exchange(3, out_ggrid)

    @pl.loop(0, Z)
    def _(z):
        for part in range(cz // LANE):
            lanes = pl.ds(pl.multiple_of(z * cz + part * LANE, LANE), LANE)

            def put(k, row):
                gvs[z, k : k + 1, part * LANE : (part + 1) * LANE] = row

            depthwise_taps(wide(c_in[:, lanes]), dcn[:, lanes], 7, put)

    for z in range(Z):
        gvs[z, 49:50] = gvs_lc[:, z * cz : (z + 1) * cz]
        gvs[z, 50:51] = gvs_ls[:, z * cz : (z + 1) * cz]
        gvs[z, 51:64] = jnp.zeros((13, cz), F32)
        gvs[z, 56:57, 0:dz] = gvs_d0[:, z * dz : (z + 1) * dz]
        gvs[z, 57:58, 0:dz] = gvs_d1[:, z * dz : (z + 1) * dz]
    gvs_low[...] = low(gvs[...])
    scatter_start("gv", gvs_low, gv_rb)

    def group_copy(n, k, src, dst):
        rr, xx = owner(k)
        return remote(src, dst, gx_send.at[n, k], gx_recv.at[n, k], dev(rr=rr, xx=xx))

    for k in range(3):
        c = group_copy(1, k, gad, gad_rb.at[k])
        c.start()
        sent.append(c)
    @pl.when(p == 1)
    def _():
        reduce_middle("P2", "P1")
        reduce_end("P2")

    reduce_end("P1")
    scatter_wait("gv", gv_rb)
    gvx[3] = (gvs[zi] + wide(gv_rb[0])) + (wide(gv_rb[1]) + wide(gv_rb[2]))
    for k in range(3):
        c = group_copy(0, k, gvx.at[3], gvx.at[k])
        c.start()
        sent.append(c)
    for k in range(3):
        group_copy(1, k, gad, gad_rb.at[k]).wait_recv()
    gad_all[zi] = (gad[x] + gad_rb[0, x]) + (gad_rb[1, x] + gad_rb[2, x])
    gather_start("gad", gad_all)

    reduce_middle("Q", "O")
    reduce_end("Q", "O")

    for k in range(3):
        group_copy(0, k, gvx.at[k], gvx.at[k]).wait_recv()
    total = (gvx[0] + gvx[1]) + (gvx[2] + gvx[3])
    mine = jnp.where(ri == 1, pltpu.roll(total, c_own, 1), total)[:, 0:c_own]
    mine_d = jnp.where(ri == 1, total[:, LANE : 2 * LANE], total[:, 0:LANE])

    def flag(n):
        return train_in[0, n].astype(F32)

    out_depth[...] = mine[0:taps7] * flag(0)
    out_ln_conv[...] = mine[49:50] * flag(1)
    out_scale[...] = mine[50:51] * flag(4)
    out_ln_attn[...] = mine_d[56:57]
    out_ln_mlp[...] = mine_d[57:58]
    gather_wait("gad", gad_all)
    for z in range(Z):
        out_ad[:, z * adq : (z + 1) * adq] = gad_all[z][0:9]
    for name in ARRAYS:
        back_local(name).wait()
        for d in range(1, Z):
            n = ids[name]
            slot = quarter_of(name, native[name], zfrom(d))
            remote(slot, slot, a_send.at[n, d - 1], a_recv.at[n, d - 1], dev(zto(d))).wait_recv()
    for n, buf in enumerate((hid_tok, hid_grid, out_gtok, out_ggrid)):
        c = remote(buf.at[x], buf.at[x], xo_send.at[n], xo_recv.at[n], over_x)
        c.wait_send()
        remote(buf.at[xo], buf.at[xo], xo_send.at[n], xo_recv.at[n], over_x).wait_recv()

    @pl.when(p == 0)
    def _():
        remote(hid_tok.at[x], x_in, h_send.at[0], h_recv.at[0], sib).wait_send()
        remote(hid_grid.at[x], c_in, h_send.at[1], h_recv.at[1], sib).wait_send()

    @pl.when(p == 1)
    def _():
        for d in range(Z):
            over_cores(d).wait_send()
        remote(out_ggrid.at[x], dcot, c_send, c_recv, sib).wait_send()

    for name, buf in line_gathers:
        line_sent(name, buf)

    @pl.when(p == 1)
    def _():
        line_sent("dx3", dx3_all)

    for name, sb, rb in line_sums:
        sum_sent(name, sb, rb)
    for c in sent:
        c.wait_send()
    for name in ARRAYS:
        for which in range(4):
            for d in pieces(name):
                hop_copy(name, which, d).wait_send()
        for d in range(1, Z):
            back_copy(name, d).wait_send()


def run_layers(weights, vectors, order, train, streams, sizes, outer):
    d_dim, c_dim, hq, ffq, cfq, adw, dg = sizes
    vm = pltpu.VMEM
    blocks = []
    for name, value in zip(ARRAYS, weights):
        if name == "Q":
            blocks.append((3, value.shape[1], hq))
        elif name in ("O", "F2"):
            blocks.append((value.shape[0] // Z, value.shape[1]))
        else:
            blocks.append((value.shape[0], value.shape[1] // Z))
    rows = Z * TOK

    def act(width, count=Z, kind=BF):
        return vm((count, TOK, width), kind)

    def line(width):
        return vm((2, 3, TOK, width), BF)

    scratch = [vm((2, Z, R) + s, BF) for s in blocks] + [
        vm(lead + s[:-2] + (s[-2] // 2, s[-1]), BF)
        for s in blocks
        for lead in ((Z, R), (2, Z), (Z,), (Z,))
    ]
    scratch += [
        vm((64, 2 * LANE), F32), vm((64, 2 * LANE), BF), vm((Z * R, 64, 2 * LANE), BF), vm((2, 16, adw), F32), vm((64, c_dim), F32), vm((8, d_dim), F32),
        vm((TOK, d_dim), BF), vm((TOK, c_dim), BF), act(d_dim), act(c_dim), act(d_dim), act(c_dim),
        act(d_dim), line(d_dim), act(c_dim), line(c_dim), act(d_dim), line(d_dim),
        act(2 * adw), act(2 * adw, 3), vm((4, 8, dg), F32), vm((4, 8, dg), F32),
        vm((2, rows, 3 * hq), BF), vm((2, hq // HD, Z, TOK, TOK), BF), vm((2, rows, hq), BF),
        vm((2, rows, ffq), BF), vm((2, rows, ffq), BF), vm((2, rows, cfq), BF), vm((2, rows, cfq), BF),
        vm((TOK, c_dim), F32), vm((TOK, LANE), F32), vm((TOK, c_dim), F32), vm((TOK, d_dim), F32), vm((TOK, c_dim), F32),
        vm((2, rows, adw), F32), vm((2, Z, TOK, adw), F32), vm((2, 8, adw), F32), vm((2, 8, adw), F32),
        vm((TOK, d_dim), BF), vm((TOK, c_dim), BF), act(d_dim), act(d_dim), line(d_dim), act(c_dim), line(c_dim),
        act(d_dim), act(c_dim),
        act(d_dim), line(d_dim), act(c_dim), line(c_dim), vm((2, rows, ffq), BF), vm((2, rows, hq), BF),
        vm((2, rows, 3 * hq), BF), vm((2, rows, cfq), BF), vm((TOK, d_dim), F32), vm((TOK, c_dim), F32), vm((2, rows, adw), BF),
        vm((TOK, c_dim), F32),
        vm((Z, 64, c_dim // Z), F32), vm((Z, 64, c_dim // Z), BF), vm((3, 64, c_dim // Z), BF), vm((4, 64, c_dim // Z), F32),
        vm((2, 16, adw), F32), vm((3, 2, 16, adw), F32), vm((Z, 16, adw), F32),
        vm((2 * ffq, rows), BF),
    ]
    dma = pltpu.SemaphoreType.DMA
    na = len(ARRAYS)
    scratch += [
        dma((len(EVENTS), 3)), dma((len(EVENTS), 3)), dma((len(EVENTS), 6)), dma((len(EVENTS), 6)), dma((na, 3)), dma((na, 3)), dma((na,)),
        dma((na, 4, Z)), dma((na, 4, Z)), dma((7,)), dma((7,)), dma, dma, dma((2,)), dma((2,)), dma((Z,)), dma((Z,)), dma, dma,
        dma((4,)), dma((4,)), dma((na, 4, Z)), dma((na, 4, Z)), dma((na, 3)), dma((na, 3)), dma((2, 3)), dma((2, 3)),
        pltpu.SemaphoreType.REGULAR,
    ]
    sds = jax.ShapeDtypeStruct
    out_shape = [sds((2, TOK, d_dim), BF), sds((2, TOK, c_dim), BF)] * 2
    out_shape += [sds(value.shape, BF) for value in weights]
    out_shape += [sds(value.shape, F32) for value in vectors]
    any_spec = pl.BlockSpec(memory_space=pl.ANY)
    vm_spec = pl.BlockSpec(memory_space=pltpu.VMEM)
    sm_spec = pl.BlockSpec(memory_space=pltpu.SMEM)
    return pl.pallas_call(
        functools.partial(main_kernel, sizes, outer),
        out_shape=out_shape,
        in_specs=[any_spec] * na + [vm_spec] * 6 + [sm_spec] * 2 + [vm_spec] * 4,
        out_specs=[vm_spec] * 4 + [any_spec] * na + [vm_spec] * 6,
        scratch_shapes=scratch,
        compiler_params=pltpu.CompilerParams(
            collective_id=0, has_side_effects=True, vmem_limit_bytes=62 * 1024 * 1024
        ),
        cost_estimate=pl.CostEstimate(flops=26 * 10**9, bytes_accessed=10**8, transcendentals=10**7),
        name="layers",
    )(*weights, *vectors, order, train, *streams)


def finish_kernel(flagged, layer_zero, count, *refs):
    grads, streams, vectors = refs[:count], refs[count : count + 4], refs[count + 4 : count + 10]
    order, train = refs[count + 10 : count + 12]
    refs = refs[count + 12 :]
    out_grads, out_streams, out_vectors = refs[:count], refs[count : count + 4], refs[count + 4 : count + 10]
    refs = refs[count + 10 :]
    held, wide_ones = refs[:count], refs[count : 2 * count]
    in_sem, out_sem = refs[2 * count :]

    def fetch(n):
        return pltpu.make_async_copy(grads[n], held[n], in_sem.at[n])

    def put_back(n):
        return pltpu.make_async_copy(wide_ones[n], out_grads[n], out_sem.at[n])

    for n in range(count):
        fetch(n).start()
    swap = (lax.axis_index("pipe") == layer_zero) & (order[0, 0] == 1)
    for n, (src, dst) in enumerate(zip(streams, out_streams)):
        for m in range(2):
            dst[m] = src[m] if n < 2 else jnp.where(swap, src[1 - m], src[m])
    for src, dst in zip(vectors, out_vectors):
        dst[...] = src[...]
    for n in range(count):
        fetch(n).wait()
        src, dst = held[n], wide_ones[n]
        scale = train[0, flagged[n]].astype(F32) if n in flagged else None
        lead = src.shape[0] if len(src.shape) == 3 else 1

        @pl.loop(0, lead * (src.shape[-2] // 16))
        def _(step):
            rows = pl.ds(pl.multiple_of((step // lead) * 16, 16), 16)
            at = (step % lead, rows) if len(src.shape) == 3 else (rows,)
            value = wide(src[at])
            dst[at] = value if scale is None else value * scale

        put_back(n).start()
    for n in range(count):
        put_back(n).wait()


def finish(outs, order, train):
    count = len(ARRAYS)
    streams, grads, vectors = outs[:4], outs[4 : 4 + count], outs[4 + count :]
    any_spec = pl.BlockSpec(memory_space=pl.ANY)
    sm_spec = pl.BlockSpec(memory_space=pltpu.SMEM)
    vm_spec = pl.BlockSpec(memory_space=pltpu.VMEM)
    sds = jax.ShapeDtypeStruct
    dma = pltpu.SemaphoreType.DMA
    flagged = {ARRAYS.index("P1"): 2, ARRAYS.index("P2"): 3}
    return pl.pallas_call(
        functools.partial(finish_kernel, flagged, 0, count),
        out_shape=[sds(g.shape, F32) for g in grads]
        + [sds(value.shape, value.dtype) for value in (*streams, *vectors)],
        in_specs=[any_spec] * count + [vm_spec] * 10 + [sm_spec] * 2,
        out_specs=[any_spec] * count + [vm_spec] * 10,
        scratch_shapes=[pltpu.VMEM(g.shape, BF) for g in grads]
        + [pltpu.VMEM(g.shape, F32) for g in grads]
        + [dma((count,)), dma((count,))],
        compiler_params=pltpu.CompilerParams(vmem_limit_bytes=62 * 1024 * 1024),
        name="finish",
    )(*grads, *streams, *vectors, order, train)


def per_device(
    tokens,
    conv_grid,
    order,
    trainable,
    ln_attn,
    w_qkv,
    w_attn_out,
    ln_mlp,
    w_fc_in,
    w_fc_out,
    conv_depth,
    ln_conv,
    w_pw_in,
    w_pw_out,
    layer_scale,
    w_adapt,
    adapt_depth,
    w_gate_in,
    w_gate_out,
    tok_cot,
    grid_cot,
):
    dp_count = lax.axis_size("dp")
    outer = dp_count // (Z * R)
    groups = [[g * outer + o for o in range(outer)] for g in range(Z * R)]

    def block(value, axis):
        value = value[0]
        if outer == 1:
            return value
        return lax.all_gather(value, "dp", axis=axis, tiled=True, axis_index_groups=groups)

    def share(value, axis):
        if outer > 1:
            value = lax.psum_scatter(
                value, "dp", scatter_dimension=axis, tiled=True, axis_index_groups=groups
            )
        return value[None]

    qkv = block(w_qkv, 1)
    gate_in = block(w_gate_in, 1).T
    pw_in = block(w_pw_in, 0)
    adapt = block(w_adapt, 0)
    fc_in = block(w_fc_in, 0)
    weights = (
        pw_in,
        block(w_pw_out, 1).T,
        qkv,
        block(w_attn_out, 1),
        adapt,
        gate_in,
        block(w_gate_out, 0),
        fc_in,
        block(w_fc_out, 1),
    )
    vectors = (
        block(conv_depth, 1),
        block(ln_conv, 0)[None],
        block(layer_scale, 0)[None],
        block(ln_attn, 0)[None],
        block(ln_mlp, 0)[None],
        adapt_depth[0],
    )
    spread = Z * R
    sizes = (
        qkv.shape[1] * spread, pw_in.shape[0] * spread, qkv.shape[2] // Z, fc_in.shape[1] // Z,
        pw_in.shape[1] // Z, adapt.shape[1] // Z, gate_in.shape[0] * spread,
    )

    def rows_of(value):
        return value.reshape(value.shape[0], TOK, value.shape[-1])

    streams = [rows_of(value) for value in (tokens, conv_grid, tok_cot, grid_cot)]
    outs = run_layers(weights, vectors, order, trainable, streams, sizes, outer)
    done = finish(outs, order, trainable)
    g_p1, g_p2, g_q, g_o, g_e, g_gi, g_go, g_f1, g_f2 = done[:9]
    hid_tok, hid_grid, g_tok, g_grid = done[9:13]
    g_depth, g_ln_conv, g_scale, g_ln_attn, g_ln_mlp, g_ad = done[13:]
    grid_shape = (1,) + conv_grid.shape
    tok_shape = (1,) + tokens.shape
    if outer > 1:
        g_ad = lax.psum(g_ad, "dp", axis_index_groups=groups)
    return (
        hid_tok.reshape(tok_shape),
        hid_grid.reshape(grid_shape),
        g_tok.reshape(tok_shape),
        g_grid.reshape(grid_shape),
        share(g_ln_attn[0], 0),
        share(g_q, 1),
        share(g_o, 1),
        share(g_ln_mlp[0], 0),
        share(g_f1, 0),
        share(g_f2, 1),
        share(g_depth, 1),
        share(g_ln_conv[0], 0),
        share(g_p1, 0),
        share(g_p2.T, 1),
        share(g_scale[0], 0),
        share(g_e, 0),
        g_ad[None],
        share(g_gi.T, 1),
        share(g_go, 0),
    )


def solution(mesh):
    in_specs = (
        P(None, "dp", None, None),
        P(None, "dp", None, None, None),
        P("dp", None),
        P("pipe", None),
        P("pipe", "dp"),
        P("pipe", None, "dp", "tensor"),
        P("pipe", "tensor", "dp"),
        P("pipe", "dp"),
        P("pipe", "dp", "tensor"),
        P("pipe", "tensor", "dp"),
        P("pipe", None, "dp"),
        P("pipe", "dp"),
        P("pipe", "dp", "tensor"),
        P("pipe", "tensor", "dp"),
        P("pipe", "dp"),
        P("pipe", "dp", "tensor"),
        P("pipe", None, "tensor"),
        P("pipe", "tensor", "dp"),
        P("pipe", "dp", "tensor"),
        P(None, "dp", None, None),
        P(None, "dp", None, None, None),
    )
    out_specs = (
        P("pipe", None, "dp", None, None),
        P("pipe", None, "dp", None, None, None),
        P("pipe", None, "dp", None, None),
        P("pipe", None, "dp", None, None, None),
        P("pipe", "dp"),
        P("pipe", None, "dp", "tensor"),
        P("pipe", "tensor", "dp"),
        P("pipe", "dp"),
        P("pipe", "dp", "tensor"),
        P("pipe", "tensor", "dp"),
        P("pipe", None, "dp"),
        P("pipe", "dp"),
        P("pipe", "dp", "tensor"),
        P("pipe", "tensor", "dp"),
        P("pipe", "dp"),
        P("pipe", "dp", "tensor"),
        P("pipe", None, "tensor"),
        P("pipe", "tensor", "dp"),
        P("pipe", "dp", "tensor"),
    )
    return jax.shard_map(
        per_device, mesh=mesh, in_specs=in_specs, out_specs=out_specs, check_vma=False
    )
```

```python
import functools

import jax
import jax.numpy as jnp
from jax import lax
from jax.experimental import pallas as pl
from jax.experimental.pallas import tpu as pltpu
from jax.sharding import PartitionSpec as P

HD = 64
Z = 4
R = 2
TOK = 64
SIDE = 8
LANE = 128
BF = jnp.bfloat16
F32 = jnp.float32
ARRAYS = ("P1", "P2", "Q", "O", "E", "Gi", "Go", "F1", "F2")
EVENTS = (
    "n1", "f", "o", "cv", "n2", "c2", "m", "br", "gs",
    "dx3", "dgh", "dn2", "dc2", "dx1", "dcv", "dn1", "df", "gv", "gad",
)


def mm(a, b):
    return lax.dot_general(a, b, (((1,), (0,)), ((), ())), preferred_element_type=F32)


def mm_nt(a, b):
    return lax.dot_general(a, b, (((1,), (1,)), ((), ())), preferred_element_type=F32)


def mm_tn(a, b):
    return lax.dot_general(a, b, (((0,), (0,)), ((), ())), preferred_element_type=F32)


def flat(value):
    return value.reshape(-1, value.shape[-1])


def low(value):
    return value.astype(BF)


def wide(value):
    return value.astype(F32)


def gelu_pair(h):
    phi = 0.5 * (1.0 + lax.erf(h * 0.7071067811865476))
    dens = jnp.exp(-0.5 * h * h) * 0.3989422804014327
    return h * phi, phi + h * dens


def normed(value):
    centred = value - jnp.mean(value, axis=-1, keepdims=True)
    rs = lax.rsqrt(jnp.mean(centred * centred, axis=-1, keepdims=True) + 1e-06)
    return centred * rs, rs


def norm_back(dn, n_hat, rs, gain):
    gd = dn * gain
    return (
        gd
        - jnp.mean(gd, axis=-1, keepdims=True)
        - n_hat * jnp.mean(gd * n_hat, axis=-1, keepdims=True)
    ) * rs


def col_shift(value, by):
    if by == 0:
        return value
    at = lax.broadcasted_iota(jnp.int32, value.shape, 0) % SIDE
    rolled = pltpu.roll(value, (-by) % TOK, 0)
    return jnp.where((at + by >= 0) & (at + by < SIDE), rolled, 0.0)


def row_shift(value, by):
    if by == 0:
        return value
    gap = jnp.zeros((abs(by) * SIDE, value.shape[1]), value.dtype)
    if by > 0:
        return jnp.concatenate([value[by * SIDE :], gap], axis=0)
    return jnp.concatenate([gap, value[: TOK + by * SIDE]], axis=0)


def depthwise(value, tap, side):
    half = side // 2
    shifted = [col_shift(value, b - half) for b in range(side)]
    total = None
    for a in range(side):
        line = None
        for b in range(side):
            term = shifted[b] * tap(a * side + b)
            line = term if line is None else line + term
        line = row_shift(line, a - half)
        total = line if total is None else total + line
    return total


def depthwise_taps(value, grad, side, put):
    half = side // 2
    shifted = [col_shift(value, b - half) for b in range(side)]
    for a in range(side):
        d = a - half
        lo, hi = max(0, -d) * SIDE, (SIDE - max(0, d)) * SIDE
        for b in range(side):
            part = shifted[b][lo + d * SIDE : hi + d * SIDE] * grad[lo:hi]
            put(a * side + b, jnp.sum(part, axis=0, keepdims=True))


def lanes_of(at, width):
    return pl.ds(pl.multiple_of(at * width, width), width)


def side_by_side(blocks):
    return jnp.concatenate(blocks, axis=1)


def main_kernel(dims, outer, *refs):
    at = iter(refs)

    def take(count):
        return [next(at) for _ in range(count)]

    na = len(ARRAYS)
    source = dict(zip(ARRAYS, take(na)))
    (
        depth_in, ln_conv_in, scale_in, ln_attn_in, ln_mlp_in, adapt_depth_in,
        order_in, train_in, tok_in, grid_in, tcot_in, gcot_in,
    ) = take(12)
    hid_tok, hid_grid, out_gtok, out_ggrid = take(4)
    native = dict(zip(ARRAYS, take(na)))
    out_depth, out_ln_conv, out_scale, out_ln_attn, out_ln_mlp, out_ad = take(6)
    W = dict(zip(ARRAYS, take(na)))
    hops = take(4 * na)
    RX = {name: hops[4 * n : 4 * n + 4] for n, name in enumerate(ARRAYS)}
    (
        v_loc, v_low, vv, aq, vec_c, vec_d, x_in, c_in, n1_all, f_all, n2_all, c2_all,
        o_sb, o_rb, cv_sb, cv_rb, m_sb, m_rb, br_sb, br_rb, gsb, dgb,
        qkv, prob, ctx, u, up, r, rp, cn, crs, cv_sum, x1, c2f,
        adapted, spread, pooled, gate,
        dx3, dcot, dx3_all, dn2_sb, dn2_rb, dc2_sb, dc2_rb, dx1_all, dcv_all,
        dn1_sb, dn1_rb, df_sb, df_rb, dh, do_all, dqkv, dhc, dx1, dc2t, dad, dcn,
        gvs, gvs_low, gv_rb, gvx, gad, gad_rb, gad_all, turned,
    ) = take(67)
    (
        zs_send, zs_recv, l_send, l_recv, s1_send, s1_recv, loc_sem, s2_send, s2_recv,
        v_send, v_recv, q_send, q_recv, h_send, h_recv, b_send, b_recv, c_send, c_recv,
        xo_send, xo_recv, g_send, g_recv, a_send, a_recv, gx_send, gx_recv, go,
    ) = take(28)

    p = lax.axis_index("pipe")
    dpi = lax.axis_index("dp")
    x = lax.axis_index("tensor")
    rest = dpi % outer
    zi = dpi // (outer * R)
    ri = (dpi // outer) % R
    xo = 1 - x
    ro = 1 - ri
    d_dim, c_dim, hq, ffq, cfq, adq, dg = dims
    adh = Z * adq
    dz, cz = d_dim // Z, c_dim // Z
    tile = 256
    ids = {name: number for number, name in enumerate(ARRAYS)}
    ev = {name: number for number, name in enumerate(EVENTS)}

    def dev(z=None, rr=None, xx=None, pp=None):
        z = zi if z is None else z
        rr = ri if rr is None else rr
        return (
            p if pp is None else pp,
            (z * R + rr) * outer + rest,
            x if xx is None else xx,
        )

    def zto(d):
        return lax.rem(zi + d, Z)

    def zfrom(d):
        return lax.rem(zi + Z - d, Z)

    def remote(src, dst, ssem, rsem, device):
        return pltpu.make_async_remote_copy(
            src_ref=src, dst_ref=dst, send_sem=ssem, recv_sem=rsem,
            device_id=device, device_id_type=pl.DeviceIdType.MESH,
        )

    sib = dev(pp=1 - p)
    over_r, over_x = dev(rr=ro), dev(xx=xo)

    def z_copy(e, d, src, dst):
        return remote(src, dst, zs_send.at[e, d - 1], zs_recv.at[e, d - 1], dev(zto(d)))

    sent = []

    def gather_copies(name, buf):
        return [z_copy(ev[name], d, buf.at[zi], buf.at[zi]) for d in range(1, Z)]

    def gather_start(name, buf, keep=True):
        copies = gather_copies(name, buf)
        for c in copies:
            c.start()
        if keep:
            sent.extend(copies)

    def gather_wait(name, buf):
        for d in range(1, Z):
            slot = buf.at[zfrom(d)]
            z_copy(ev[name], d, slot, slot).wait_recv()

    def scatter_start(name, sb, rb):
        for d in range(1, Z):
            c = z_copy(ev[name], d, sb.at[zto(d)], rb.at[d - 1])
            c.start()
            sent.append(c)

    def scatter_wait(name, rb):
        for d in range(1, Z):
            z_copy(ev[name], d, rb.at[d - 1], rb.at[d - 1]).wait_recv()

    def right():
        return dev(zi + 1)

    def left():
        return dev(zi - 1)

    def pass_copy(name, buf, toward, s):
        e, k = ev[name], (0 if toward > 0 else 3) + s
        blk = buf.at[zi - toward * s]
        return remote(blk, blk, l_send.at[e, k], l_recv.at[e, k], right() if toward > 0 else left())

    def pass_cond(toward, s):
        if toward > 0:
            return (zi < Z - 1) & (zi - s >= 0)
        return (zi > 0) & (zi + s <= Z - 1)

    def line_start(name, buf):
        for toward in (1, -1):

            @pl.when(pass_cond(toward, 0))
            def _():
                pass_copy(name, buf, toward, 0).start()

    def line_step(name, buf, *steps):
        e = ev[name]
        for s in steps:
            for toward in (1, -1):
                src = zi - toward * s

                @pl.when((src >= 0) & (src <= Z - 1))
                def _():
                    blk = buf.at[src]
                    k = (0 if toward > 0 else 3) + s - 1
                    remote(blk, blk, l_send.at[e, k], l_recv.at[e, k], sib).wait_recv()

                if s < Z - 1:

                    @pl.when(pass_cond(toward, s))
                    def _():
                        pass_copy(name, buf, toward, s).start()

    def line_sent(name, buf):
        for toward in (1, -1):
            for s in range(Z - 1):

                @pl.when(pass_cond(toward, s))
                def _():
                    pass_copy(name, buf, toward, s).wait_send()

    def sum_copy(name, sb, rb, toward, k, first):
        e, way = ev[name], (0 if toward > 0 else 1)
        src = sb.at[zi + toward * k] if first else rb.at[way, k]
        q = way * 3 + k - 1
        return remote(src, rb.at[way, k - 1], l_send.at[e, q], l_recv.at[e, q], right() if toward > 0 else left())

    def at_end(toward):
        return zi == (0 if toward > 0 else Z - 1)

    def passes(toward, k):
        dest = zi + toward * k
        return jnp.logical_not(at_end(toward)) & (dest >= 0) & (dest <= Z - 1)

    def sum_start(name, sb, rb):
        for toward in (1, -1):

            @pl.when(at_end(toward))
            def _():
                for k in (3, 2, 1):
                    sum_copy(name, sb, rb, toward, k, True).start()

    def sum_arrival(name, rb, way, k):
        e = ev[name]
        slot = rb.at[way, k]
        return remote(slot, slot, l_send.at[e, way * 3 + k], l_recv.at[e, way * 3 + k], sib)

    def sum_step(name, sb, rb, *ks):
        for k in ks:
            for way, toward in enumerate((1, -1)):

                @pl.when(passes(toward, k))
                def _():
                    sum_arrival(name, rb, way, k).wait_recv()
                    rb[way, k] = low(wide(rb[way, k]) + wide(sb[zi + toward * k]))
                    sum_copy(name, sb, rb, toward, k, False).start()

    def sum_wait(name, rb):
        for way, toward in enumerate((1, -1)):

            @pl.when(jnp.logical_not(at_end(toward)))
            def _():
                sum_arrival(name, rb, way, 0).wait_recv()

    def summed(sb, rb):
        return wide(sb[zi]) + (wide(rb[0, 0]) + wide(rb[1, 0]))

    def sum_sent(name, sb, rb):
        for toward in (1, -1):

            @pl.when(at_end(toward))
            def _():
                for k in (3, 2, 1):
                    sum_copy(name, sb, rb, toward, k, True).wait_send()

            for k in (2, 1):

                @pl.when(passes(toward, k))
                def _():
                    sum_copy(name, sb, rb, toward, k, False).wait_send()

    def share_start(name, buf):
        for d in range(1, Z):
            c = z_copy(ev[name], d, buf.at[3], buf.at[d - 1])
            c.start()
            sent.append(c)

    def scattered(sb, rb):
        return (wide(sb[zi]) + wide(rb[0])) + (wide(rb[1]) + wide(rb[2]))

    barrier = pltpu.get_barrier_semaphore()
    greeted = [sib]
    for d in range(1, Z):
        greeted += [dev(zto(d)), dev(zto(d), ro), dev(zto(d), pp=1 - p)]
    greeted += [over_r, over_x, dev(rr=ro, xx=xo)]
    for device in greeted:
        pl.semaphore_signal(barrier, inc=1, device_id=device, device_id_type=pl.DeviceIdType.MESH)
    v_loc[...] = jnp.zeros(v_loc.shape, F32)
    taps7 = depth_in.shape[0]
    c_own = depth_in.shape[1]
    v_loc[0:taps7, 0:c_own] = wide(depth_in[...])
    v_loc[49:50, 0:c_own] = wide(ln_conv_in[...])
    v_loc[50:51, 0:c_own] = wide(scale_in[...])
    v_loc[56:57, 0:LANE] = wide(ln_attn_in[...])
    v_loc[57:58, 0:LANE] = wide(ln_mlp_in[...])
    aq[x] = jnp.zeros(aq.shape[1:], F32)
    aq[x, 0:9] = wide(adapt_depth_in[:, lanes_of(zi, adq)])
    v_low[...] = low(v_loc[...])
    line_sums = (
        ("o", o_sb, o_rb), ("cv", cv_sb, cv_rb), ("m", m_sb, m_rb), ("dn2", dn2_sb, dn2_rb),
        ("dc2", dc2_sb, dc2_rb), ("dn1", dn1_sb, dn1_rb), ("df", df_sb, df_rb),
    )
    line_gathers = (
        ("n1", n1_all), ("f", f_all), ("n2", n2_all), ("c2", c2_all), ("dx1", dx1_all), ("dcv", dcv_all),
    )
    for _, _, rb in line_sums:
        for way, toward in enumerate((1, -1)):

            @pl.when(at_end(toward))
            def _():
                rb[way, 0] = jnp.zeros(rb.shape[2:], BF)

    pl.semaphore_wait(barrier, len(greeted))

    me8 = zi * R + ri
    v_arrivals = []
    for n, (d, flip) in enumerate([(d, s) for d in range(Z) for s in (0, 1)][1:]):
        tr = ro if flip else ri
        c = remote(v_low, vv.at[me8], v_send.at[n], v_recv.at[n], dev(zto(d), tr))
        c.start()
        sent.append(c)
        fr = zfrom(d) * R + tr
        v_arrivals.append(remote(vv.at[fr], vv.at[fr], v_send.at[n], v_recv.at[n], dev(zto(d), tr)))
    vv[me8] = v_low[...]
    c = remote(aq.at[x], aq.at[x], q_send, q_recv, over_x)
    c.start()
    sent.append(c)

    by_rows = ("O", "F2")

    def quarter_of(name, ref, z):
        if name == "Q":
            return ref.at[:, :, lanes_of(z, hq)]
        if name in by_rows:
            height = ref.shape[0] // Z
            return ref.at[pl.ds(pl.multiple_of(z * height, height), height)]
        return ref.at[:, lanes_of(z, ref.shape[1] // Z)]

    def step1_local(name):
        return pltpu.make_async_copy(
            quarter_of(name, source[name], zi), W[name].at[x, zi, ri], loc_sem.at[ids[name]]
        )

    def step1_copy(name, d):
        k = ids[name]
        return remote(
            quarter_of(name, source[name], zto(d)), W[name].at[x, zi, ri],
            s1_send.at[k, d - 1], s1_recv.at[k, d - 1], dev(zto(d)),
        )

    def half_of(name, j, z, rr, upper):
        w = W[name]
        half = w.shape[-2] // 2
        rows = slice(half, None) if upper else slice(0, half)
        if len(w.shape) == 6:
            return w.at[j, z, rr, :, rows]
        return w.at[j, z, rr, rows]

    def step2_copy(name, which, d):
        k = ids[name]
        z = zfrom(d)
        if which < 2:
            src = quarter_of(name, source[name], zi) if d == 0 else W[name].at[x, z, ri]
            dst = W[name].at[x, z, ri]
        else:
            src = dst = half_of(name, x, z, ro, False) if which == 2 else half_of(name, xo, z, ri, True)
        to = over_x if which in (1, 2) else over_r
        return remote(src, dst, s2_send.at[k, which, d], s2_recv.at[k, which, d], to)

    def step2_arrival(name, which, d):
        k = ids[name]
        z = zfrom(d)
        if which < 2:
            ref = W[name].at[x, z, ro] if which == 0 else W[name].at[xo, z, ri]
        else:
            ref = half_of(name, xo, z, ro, which == 3)
        to = over_x if which in (1, 2) else over_r
        return remote(ref, ref, s2_send.at[k, which, d], s2_recv.at[k, which, d], to)

    def relay1(*names):
        for name in names:
            for d in range(1, Z):
                step1_copy(name, d).start()

    def relay0(*names):
        for name in names:
            step1_local(name).start()
            step2_copy(name, 0, 0).start()
            step2_copy(name, 1, 0).start()

    def relay2(name, ds=(1, 2, 3)):
        k = ids[name]
        for d in ds:
            slot = W[name].at[x, zfrom(d), ri]
            remote(slot, slot, s1_send.at[k, d - 1], s1_recv.at[k, d - 1], dev(zto(d))).wait_recv()
            step2_copy(name, 0, d).start()
            step2_copy(name, 1, d).start()

    def relay3(name, ds=(0, 1, 2, 3)):
        for d in ds:
            step2_arrival(name, 0, d).wait_recv()
            step2_copy(name, 2, d).start()
            step2_arrival(name, 1, d).wait_recv()
            step2_copy(name, 3, d).start()

    def relay4(*names):
        for name in names:
            step1_local(name).wait()
            for d in range(Z):
                step2_arrival(name, 2, d).wait_recv()
                step2_arrival(name, 3, d).wait_recv()

    def relay_sent():
        for name in ARRAYS:
            for d in range(1, Z):
                step1_copy(name, d).wait_send()
            for which in range(4):
                for d in range(Z):
                    step2_copy(name, which, d).wait_send()

    @pl.when(p == 0)
    def _():
        relay0("P1")
        relay1("P1")
        relay0("P2")
        relay1("P2")
        relay0("Q", "O", "E", "Gi", "Go", "F1", "F2")

    @pl.when(p == 1)
    def _():
        dx3[...] = tcot_in[x]
        dcot[...] = gcot_in[x]
        dx3_all[zi] = tcot_in[x]
        line_start("dx3", dx3_all)

    for c in v_arrivals:
        c.wait_recv()
    remote(aq.at[xo], aq.at[xo], q_send, q_recv, over_x).wait_recv()
    low_lanes = lax.broadcasted_iota(jnp.int32, (64, LANE), 1) < LANE // 2
    for z in range(Z):
        first, second = wide(vv[2 * z]), pltpu.roll(wide(vv[2 * z + 1]), LANE // 2, 1)
        vec_c[:, z * cz : z * cz + LANE] = first[:, 0:LANE]
        vec_c[:, z * cz + LANE : z * cz + 2 * LANE] = jnp.where(
            low_lanes, first[:, LANE:], second[:, 0:LANE]
        )
        vec_c[:, z * cz + 2 * LANE : (z + 1) * cz] = second[:, LANE:]
    for i in range(Z * R):
        vec_d[:, i * LANE : (i + 1) * LANE] = wide(vv[i])[56:64, 0:LANE]

    def gain_d(row):
        return vec_d[row : row + 1, :]

    def gain_c(row):
        return vec_c[row : row + 1, :]

    def token_entry():
        n_hat, _ = normed(wide(x_in[...]))
        n1_all[zi] = low(n_hat * gain_d(0))
        line_start("n1", n1_all)

    def conv_entry():
        @pl.loop(0, c_dim // LANE)
        def _(ch):
            lanes = lanes_of(ch, LANE)
            taps = vec_c[:, lanes]
            cn[:, lanes] = depthwise(wide(c_in[:, lanes]), lambda k: taps[k : k + 1], 7)

        n_hat, rs = normed(cn[...])
        cn[...] = n_hat
        crs[...] = jnp.broadcast_to(rs, crs.shape)
        f_all[zi] = low(n_hat * gain_c(49))
        line_start("f", f_all)

    def first_relays(pump):
        relay2("P1")
        pump(1)
        relay1("Q", "O")
        relay2("P2")
        pump(2)
        relay3("P1")


    @pl.when(p == 0)
    def _():
        first = order_in[0, x] == 0
        c_in[...] = jnp.where(first, grid_in[0], grid_in[1])
        x_in[...] = jnp.where(first, tok_in[0], tok_in[1])
        conv_entry()
        token_entry()

        def pump(s):
            line_step("f", f_all, s)
            line_step("n1", n1_all, s)

        first_relays(pump)
        line_step("f", f_all, 3)
        line_step("n1", n1_all, 3)

    @pl.when(p == 1)
    def _():
        pl.semaphore_wait(go, 1)
        relay0("P1")
        relay1("P1")
        relay0("P2")
        relay1("P2")
        relay0("Q", "O", "E", "Gi", "Go", "F1", "F2")
        first_relays(lambda s: line_step("dx3", dx3_all, s))
        remote(c_in, c_in, h_send.at[1], h_recv.at[1], sib).wait_recv()
        conv_entry()
        line_step("dx3", dx3_all, 3)
        line_step("f", f_all, 1)

    relay2("Q")
    relay2("O")
    relay1("E", "Gi", "Go")
    relay3("P2", (0, 1))

    @pl.when(p == 1)
    def _():
        line_step("f", f_all, 2, 3)

    relay4("P1")

    def conv_hidden(j):
        act, der = gelu_pair(mm(flat(f_all[...]), flat(W["P1"][j])))
        r[j] = low(act)
        rp[j] = low(der)

    conv_hidden(0)

    relay3("P2", (2, 3))
    for name in ("E", "Gi", "Go"):
        relay2(name)
    relay1("F1")
    conv_hidden(1)
    relay3("Q")
    relay3("O")
    relay2("F1")
    relay1("F2")

    @pl.when(p == 0)
    def _():
        pl.semaphore_signal(go, inc=1, device_id=sib, device_id_type=pl.DeviceIdType.MESH)

    relay4("P2")

    def pair_rows(name, pair):
        zs = pl.ds(pair * 2, 2)
        return side_by_side([flat(W[name][0, zs]), flat(W[name][1, zs])])

    def pair_out(left, name, sb, width):
        both = side_by_side([left[0], left[1]])

        @pl.loop(0, Z // 2)
        def _(pair):
            acc = mm_nt(both, pair_rows(name, pair))
            sb[:, :, lanes_of(pair, 2 * width)] = low(acc).reshape(Z, TOK, 2 * width)

    pair_out(r, "P2", cv_sb, cz)

    sum_start("cv", cv_sb, cv_rb)

    for name in ("E", "Gi", "Go"):
        relay3(name)
    sum_step("cv", cv_sb, cv_rb, 2)
    relay2("F2")
    sum_step("cv", cv_sb, cv_rb, 1)

    @pl.when(p == 1)
    def _():
        remote(x_in, x_in, h_send.at[0], h_recv.at[0], sib).wait_recv()
        token_entry()
        line_step("n1", n1_all, 1, 2, 3)

    relay4("Q", "O")
    wide_q = side_by_side([flat(W["Q"][j, :, :, s]) for j in range(2) for s in range(3)])
    qkv_both = low(mm(flat(n1_all[...]), wide_q))
    for j in range(2):
        qkv[j] = qkv_both[:, j * 3 * hq : (j + 1) * 3 * hq]
    @pl.loop(0, Z)
    def _(b):
        rows = lanes_of(b, TOK)
        for j in range(2):
            outs = []
            for h in range(hq // HD):
                q, kk, vals = (qkv[j, rows, s * hq + h * HD : s * hq + (h + 1) * HD] for s in range(3))
                sc = mm_nt(q, kk) * HD ** (-0.5)
                e = jnp.exp(sc - jnp.max(sc, axis=-1, keepdims=True))
                pr = low(e / jnp.sum(e, axis=-1, keepdims=True))
                prob[j, h, b] = pr
                outs.append(mm(pr, vals))
            ctx[j, rows, :] = low(side_by_side(outs))

    out_cols = [
        jnp.concatenate([W["O"][0, z, rr], W["O"][1, z, rr]], axis=0) for z in range(Z) for rr in range(R)
    ]
    o_sb[...] = low(mm(side_by_side([ctx[0], ctx[1]]), side_by_side(out_cols))).reshape(Z, TOK, d_dim)
    sum_start("o", o_sb, o_rb)

    relay3("F1")

    sum_wait("cv", cv_rb)
    cv_sum[...] = summed(cv_sb, cv_rb)
    c2f[...] = wide(c_in[...]) + gain_c(50) * cv_sum[...]
    c2_low = low(c2f[...])
    c2_all[zi] = c2_low
    line_start("c2", c2_all)
    sum_step("o", o_sb, o_rb, 2)
    hid_grid[x] = c2_low

    @pl.when(p == 0)
    def _():
        remote(hid_grid.at[x], c_in, h_send.at[1], h_recv.at[1], sib).start()

    relay3("F2")
    sum_step("o", o_sb, o_rb, 1)
    line_step("c2", c2_all, 1)
    sum_wait("o", o_rb)
    x1[...] = wide(x_in[...]) + summed(o_sb, o_rb)
    n_hat, _ = normed(x1[...])
    n2_all[zi] = low(n_hat * gain_d(1))
    line_start("n2", n2_all)

    relay4("E", "Gi", "Go")
    line_step("c2", c2_all, 2)
    line_step("n2", n2_all, 1)
    line_step("c2", c2_all, 3)
    row8 = lax.broadcasted_iota(jnp.int32, (8, adq), 0)
    gs_part = None
    ad_both = mm(flat(c2_all[...]), side_by_side([flat(W["E"][0]), flat(W["E"][1])]))
    for j in range(2):
        ad = ad_both[:, j * adq : (j + 1) * adq]
        adapted[j] = ad
        taps = aq[j]
        pool = jnp.zeros((8, adq), F32)
        for b in range(Z):
            sp = depthwise(ad[b * TOK : (b + 1) * TOK], lambda k: taps[k : k + 1], 3)
            spread[j, b] = sp
            pool = jnp.where(row8 == b, jnp.mean(sp, axis=0, keepdims=True), pool)
        pooled[j] = pool
        term = mm_nt(low(pool), flat(W["Gi"][j]))
        gs_part = term if gs_part is None else gs_part + term
    gsb[3] = gs_part
    share_start("gs", gsb)
    line_step("n2", n2_all, 2)

    relay4("F1")
    line_step("n2", n2_all, 3)
    for j in range(2):
        act, der = gelu_pair(mm(flat(n2_all[...]), flat(W["F1"][j])))
        u[j] = low(act)
        up[j] = low(der)

    scatter_wait("gs", gsb)

    def gate_hidden():
        return gelu_pair((gsb[0] + gsb[1]) + (gsb[2] + gsb[3]))

    gh, _ = gate_hidden()
    for j in range(2):
        g8 = jnp.tanh(mm(low(gh), flat(W["Go"][j])))
        gate[j] = g8
        for b in range(Z):
            br_sb[b, :, j * adq : (j + 1) * adq] = low(g8[b : b + 1] * spread[j, b])
    scatter_start("br", br_sb, br_rb)
    relay4("F2")

    u_both = side_by_side([u[0], u[1]])

    @pl.loop(0, Z // 2)
    def _(pair):
        halves = [
            side_by_side([W["F2"][j, 2 * pair + dz_, rr] for dz_ in range(2) for rr in range(R)])
            for j in range(2)
        ]
        acc = mm(u_both, jnp.concatenate(halves, axis=0))
        m_sb[:, :, lanes_of(pair, 2 * dz)] = low(acc).reshape(Z, TOK, 2 * dz)

    sum_start("m", m_sb, m_rb)

    def exchange(n, buf):
        remote(buf.at[x], buf.at[x], xo_send.at[n], xo_recv.at[n], over_x).start()

    def layer_output(total):
        sum_step("m", m_sb, m_rb, 2)
        scatter_wait("br", br_rb)
        total[...] = x1[...]
        for d in range(Z):
            piece = br_sb[zi] if d == 0 else br_rb[d - 1]
            for j in range(2):
                lanes = pl.ds(pl.multiple_of(j * adh + zfrom(d) * adq, LANE), adq)
                total[:, lanes] += wide(piece[:, j * adq : (j + 1) * adq])
        sum_step("m", m_sb, m_rb, 1)
        sum_wait("m", m_rb)
        hid_tok[x] = low(total[...] + summed(m_sb, m_rb))

    @pl.when(p == 0)
    def _():
        layer_output(dx1)
        remote(hid_tok.at[x], x_in, h_send.at[0], h_recv.at[0], sib).start()
        exchange(0, hid_tok)

    exchange(1, hid_grid)
    relay_sent()

    def over_cores(d):
        return remote(
            out_gtok.at[x], dx3_all.at[zi], b_send.at[d], b_recv.at[d], dev(zto(d), pp=1 - p)
        )

    @pl.when(p == 0)
    def _():
        for d in range(Z):
            slot = dx3_all.at[zfrom(d)]
            remote(slot, slot, b_send.at[d], b_recv.at[d], sib).wait_recv()
        dx3[...] = dx3_all[zi]

    def own_lanes(j):
        return pl.ds(pl.multiple_of(j * adh + zi * adq, LANE), adq)

    gh, ghp = gate_hidden()
    dgh_part = None
    dgp = []
    for j in range(2):
        dgate = jnp.zeros((8, adq), F32)
        for b in range(Z):
            dbr = wide(dx3_all[b, :, own_lanes(j)])
            dgate = jnp.where(row8 == b, jnp.sum(dbr * spread[j, b], axis=0, keepdims=True), dgate)
        dg8 = low(dgate * (1.0 - gate[j] * gate[j]))
        dgp.append(dg8)
        term = mm_nt(dg8, flat(W["Go"][j]))
        dgh_part = term if dgh_part is None else dgh_part + term
    dgb[3] = dgh_part
    share_start("dgh", dgb)

    for j in range(2):
        cols = side_by_side([W["F2"][j, z, rr] for z in range(Z) for rr in range(R)])
        dh[j] = low(mm_nt(flat(dx3_all[...]), cols) * wide(up[j]))

    scatter_wait("dgh", dgb)
    dgs = low(((dgb[0] + dgb[1]) + (dgb[2] + dgb[3])) * ghp)
    for j in range(2):
        dpool = mm(dgs, flat(W["Gi"][j])) * (1.0 / TOK)
        taps = aq[j]
        tap_rows = [None] * 9
        for b in range(Z):
            dsp = gate[j, b : b + 1] * wide(dx3_all[b, :, own_lanes(j)]) + dpool[b : b + 1]
            dad[j, b * TOK : (b + 1) * TOK] = low(depthwise(dsp, lambda k: taps[8 - k : 9 - k], 3))

            def put(k, row):
                tap_rows[k] = row if tap_rows[k] is None else tap_rows[k] + row

            depthwise_taps(adapted[j, b * TOK : (b + 1) * TOK], dsp, 3, put)
        for k in range(9):
            gad[j, k : k + 1] = tap_rows[k]
        gad[j, 9:16] = jnp.zeros((7, adq), F32)

    pair_out(dad, "E", dc2_sb, cz)

    sum_start("dc2", dc2_sb, dc2_rb)

    pair_out(dh, "F1", dn2_sb, dz)

    sum_start("dn2", dn2_sb, dn2_rb)
    sum_step("dc2", dc2_sb, dc2_rb, 2)

    def half_rows(name, upper):
        half = W[name].shape[-2] // 2
        rows = slice(half, None) if upper else slice(0, half)
        return (slice(None), rows) if len(W[name].shape) == 6 else (rows,)

    fine = ("P1", "P2")

    def pieces(name):
        return (1, 2, 3, 0) if name in fine else (None,)

    def block_at(d):
        return slice(None) if d is None else zto(d)

    def hop_copy(name, which, d):
        n = ids[name]
        lower, upper = half_rows(name, False), half_rows(name, True)
        z = block_at(d)
        w, buf = W[name], RX[name]
        src, dst, to = (
            lambda: (w.at[(xo, z, slice(None)) + lower], buf[0].at[z], over_x),
            lambda: (w.at[(slice(None), z, ro) + upper], buf[1].at[:, z], over_r),
            lambda: (buf[0].at[z, ro], buf[2].at[z], over_r),
            lambda: (buf[1].at[xo, z], buf[3].at[z], over_x),
        )[which]()
        k = 0 if d is None else d
        return remote(src, dst, g_send.at[n, which, k], g_recv.at[n, which, k], to)

    def reduce_start(name, d=None):
        hop_copy(name, 0, d).start()
        hop_copy(name, 1, d).start()

    def each_block(d, body):
        if d is None:
            pl.loop(0, Z)(body)
        else:
            body(zto(d))

    def per_piece(name, body):
        if name in fine:
            pl.loop(0, Z)(lambda k: body(lax.rem(k + 1, Z)))
        else:
            body(None)

    def reduce_middle(*names):
        for name in names:
            lower, upper = half_rows(name, False), half_rows(name, True)
            buf = RX[name]

            def middle(d):
                hop_copy(name, 0, d).wait_recv()

                def add_lower(z):
                    for rr in range(R):
                        own = W[name][(x, z, rr) + lower]
                        buf[0][z, rr] = low(wide(own) + wide(buf[0][z, rr]))

                each_block(d, add_lower)
                hop_copy(name, 2, d).start()
                hop_copy(name, 1, d).wait_recv()

                def add_upper(z):
                    for j in range(2):
                        own = W[name][(j, z, ri) + upper]
                        buf[1][j, z] = low(wide(own) + wide(buf[1][j, z]))

                each_block(d, add_upper)
                hop_copy(name, 3, d).start()

            per_piece(name, middle)

    def reduce_end(*names):
        for name in names:
            lower, upper = half_rows(name, False), half_rows(name, True)
            buf = RX[name]

            def end(d):
                hop_copy(name, 2, d).wait_recv()
                hop_copy(name, 3, d).wait_recv()

                def add_both(z):
                    W[name][(x, z, ri) + lower] = low(wide(buf[0][z, ri]) + wide(buf[2][z]))
                    W[name][(x, z, ri) + upper] = low(wide(buf[1][x, z]) + wide(buf[3][z]))

                each_block(d, add_both)

            if name in fine:

                @pl.loop(1, Z)
                def _(d):
                    end(d)
                    back_copy(name, d).start()

                end(0)
            else:
                end(None)
                for d in range(1, Z):
                    back_copy(name, d).start()
            back_local(name).start()

    def back_copy(name, d):
        n = ids[name]
        return remote(
            W[name].at[x, zto(d), ri], quarter_of(name, native[name], zi),
            a_send.at[n, d - 1], a_recv.at[n, d - 1], dev(zto(d)),
        )

    def back_local(name):
        return pltpu.make_async_copy(
            W[name].at[x, zi, ri], quarter_of(name, native[name], zi), loc_sem.at[ids[name]]
        )

    peers = ((1, 0), (0, 1), (1, 1))

    def owner(k):
        return (ro if peers[k][0] else ri), (xo if peers[k][1] else x)

    def row_grad(name, left, right):
        width = W[name].shape[3]
        span = R * width

        @pl.loop(0, Z)
        def _(k):
            d = lax.rem(k + 1, Z)
            z = zto(d)
            turned[0:span] = flat(left[:, :, lanes_of(z, span)]).T
            for j in range(2):
                W[name][j, z] = low(mm(turned[0:span], right[j])).reshape(R, width, -1)
            if name in fine:
                reduce_start(name, d)

        if name not in fine:
            reduce_start(name)

    def col_grad(name, left, right):
        width = left.shape[2]
        for j in range(2):
            turned[j * width : (j + 1) * width] = left[j].T

        @pl.loop(0, Z)
        def _(z):
            rhs = flat(right[:, :, lanes_of(z, dz)])
            for j in range(2):
                g = low(mm(turned[j * width : (j + 1) * width], rhs))
                for rr in range(R):
                    W[name][j, z, rr] = g[:, rr * LANE : (rr + 1) * LANE]

        reduce_start(name)

    for j in range(2):
        W["Gi"][j] = low(mm_tn(dgs, low(pooled[j]))).reshape(Z, R, -1, adq)
        W["Go"][j] = low(mm_tn(low(gh), dgp[j])).reshape(Z, R, -1, adq)
    sum_step("dc2", dc2_sb, dc2_rb, 1)
    sum_step("dn2", dn2_sb, dn2_rb, 2)
    reduce_start("Gi")
    reduce_start("Go")
    row_grad("E", c2_all, dad)
    sum_step("dn2", dn2_sb, dn2_rb, 1)

    @pl.when(p == 0)
    def _():
        remote(dcot, dcot, c_send, c_recv, sib).wait_recv()

    sum_wait("dc2", dc2_rb)
    dc2t[...] = wide(dcot[...]) + summed(dc2_sb, dc2_rb)
    gvs_ls = jnp.sum(cv_sum[...] * dc2t[...], axis=0, keepdims=True)
    dcv_all[zi] = low(dc2t[...] * gain_c(50))
    line_start("dcv", dcv_all)

    sum_wait("dn2", dn2_rb)
    dn2 = summed(dn2_sb, dn2_rb)
    n_hat, rs = normed(x1[...])
    gvs_d1 = jnp.sum(dn2 * n_hat, axis=0, keepdims=True)
    dx1[...] = wide(dx3[...]) + norm_back(dn2, n_hat, rs, gain_d(1))
    dx1_all[zi] = low(dx1[...])
    line_start("dx1", dx1_all)
    line_step("dcv", dcv_all, 1)
    col_grad("F2", u, dx3_all)
    line_step("dcv", dcv_all, 2)
    line_step("dx1", dx1_all, 1)
    row_grad("F1", n2_all, dh)

    @pl.when(p == 1)
    def _():
        reduce_middle("Gi", "Go", "E", "F2")

    line_step("dcv", dcv_all, 3)
    line_step("dx1", dx1_all, 2)
    for j in range(2):
        dhc[j] = low(mm(flat(dcv_all[...]), flat(W["P2"][j])) * wide(rp[j]))

    pair_out(dhc, "P1", df_sb, cz)

    sum_start("df", df_sb, df_rb)

    early = ("Gi", "Go", "E", "F2", "F1")

    def pw_grads():
        row_grad("P2", dcv_all, r)
        row_grad("P1", f_all, dhc)

    line_step("dx1", dx1_all, 3)

    @pl.when(p == 1)
    def _():
        reduce_middle("F1")

    @pl.when(p == 0)
    def _():
        pw_grads()

    sum_step("df", df_sb, df_rb, 2)

    out_rows = [
        side_by_side([W["O"][j, z, rr] for z in range(Z) for rr in range(R)]) for j in range(2)
    ]
    do_both = low(mm_nt(flat(dx1_all[...]), jnp.concatenate(out_rows, axis=0)))
    for j in range(2):
        do_all[j] = do_both[:, j * hq : (j + 1) * hq]
    @pl.loop(0, Z)
    def _(b):
        rows = lanes_of(b, TOK)
        for j in range(2):
            parts = [[], [], []]
            for h in range(hq // HD):
                q, kk, vals = (qkv[j, rows, s * hq + h * HD : s * hq + (h + 1) * HD] for s in range(3))
                do = do_all[j, rows, h * HD : (h + 1) * HD]
                pr = prob[j, h, b]
                dp = mm_nt(do, vals)
                prw = wide(pr)
                ds = low(prw * (dp - jnp.sum(dp * prw, axis=-1, keepdims=True)) * HD ** (-0.5))
                parts[0].append(mm(ds, kk))
                parts[1].append(mm_tn(ds, q))
                parts[2].append(mm_tn(pr, do))
            for s in range(3):
                dqkv[j, rows, s * hq : (s + 1) * hq] = low(side_by_side(parts[s]))

    dqkv_both = side_by_side([dqkv[0], dqkv[1]])

    @pl.loop(0, Z // 2)
    def _(pair):
        zs = pl.ds(pair * 2, 2)
        rows_q = side_by_side([flat(W["Q"][j, zs, :, s]) for j in range(2) for s in range(3)])
        acc = mm_nt(dqkv_both, rows_q)
        dn1_sb[:, :, lanes_of(pair, 2 * dz)] = low(acc).reshape(Z, TOK, 2 * dz)

    sum_start("dn1", dn1_sb, dn1_rb)
    sum_step("df", df_sb, df_rb, 1)

    @pl.when(p == 0)
    def _():
        reduce_middle("Gi", "Go", "E")

    @pl.when(p == 1)
    def _():
        reduce_end("Gi", "Go", "E", "F2")


    def attention_grads():
        @pl.loop(0, Z)
        def _(z):
            turned[0:dz] = flat(n1_all[:, :, lanes_of(z, dz)]).T
            for j in range(2):
                g = low(mm(turned[0:dz], dqkv[j]))
                for s in range(3):
                    W["Q"][j, z, :, s] = g[:, s * hq : (s + 1) * hq].reshape(R, -1, hq)

        reduce_start("Q")
        col_grad("O", ctx, dx1_all)

    sum_step("dn1", dn1_sb, dn1_rb, 2)

    @pl.when(p == 0)
    def _():
        reduce_middle("F2", "F1")

    sum_step("dn1", dn1_sb, dn1_rb, 1)

    @pl.when(p == 0)
    def _():
        reduce_middle("P2")
        attention_grads()
        reduce_middle("P1")
        reduce_end(*early)

    sum_wait("dn1", dn1_rb)
    dn1 = summed(dn1_sb, dn1_rb)
    n_hat, rs = normed(wide(x_in[...]))
    gvs_d0 = jnp.sum(dn1 * n_hat, axis=0, keepdims=True)
    out_gtok[x] = low(dx1[...] + norm_back(dn1, n_hat, rs, gain_d(0)))

    @pl.when(p == 1)
    def _():
        for d in (1, 2, 3, 0):
            over_cores(d).start()

    sum_wait("df", df_rb)
    dfv = summed(df_sb, df_rb)
    gvs_lc = jnp.sum(dfv * cn[...], axis=0, keepdims=True)
    dcn[...] = norm_back(dfv, cn[...], crs[:, 0:1], gain_c(49))

    @pl.loop(0, c_dim // LANE)
    def _(ch):
        lanes = lanes_of(ch, LANE)
        taps = vec_c[:, lanes]
        back = depthwise(dcn[:, lanes], lambda k: taps[48 - k : 49 - k], 7)
        out_ggrid[x, :, lanes] = low(dc2t[:, lanes] + back)

    @pl.when(p == 1)
    def _():
        remote(out_ggrid.at[x], dcot, c_send, c_recv, sib).start()
        pw_grads()
        attention_grads()
        reduce_end("F1")
        layer_output(dx1)
        exchange(0, hid_tok)

    @pl.when(p == 0)
    def _():
        reduce_end("P2")

    exchange(2, out_gtok)
    exchange(3, out_ggrid)

    @pl.loop(0, Z)
    def _(z):
        for part in range(cz // LANE):
            lanes = pl.ds(pl.multiple_of(z * cz + part * LANE, LANE), LANE)

            def put(k, row):
                gvs[z, k : k + 1, part * LANE : (part + 1) * LANE] = row

            depthwise_taps(wide(c_in[:, lanes]), dcn[:, lanes], 7, put)

    for z in range(Z):
        gvs[z, 49:50] = gvs_lc[:, z * cz : (z + 1) * cz]
        gvs[z, 50:51] = gvs_ls[:, z * cz : (z + 1) * cz]
        gvs[z, 51:64] = jnp.zeros((13, cz), F32)
        gvs[z, 56:57, 0:dz] = gvs_d0[:, z * dz : (z + 1) * dz]
        gvs[z, 57:58, 0:dz] = gvs_d1[:, z * dz : (z + 1) * dz]
    gvs_low[...] = low(gvs[...])
    scatter_start("gv", gvs_low, gv_rb)

    def group_copy(n, k, src, dst):
        rr, xx = owner(k)
        return remote(src, dst, gx_send.at[n, k], gx_recv.at[n, k], dev(rr=rr, xx=xx))

    for k in range(3):
        c = group_copy(1, k, gad, gad_rb.at[k])
        c.start()
        sent.append(c)
    @pl.when(p == 1)
    def _():
        reduce_middle("P2", "P1")
        reduce_end("P2")

    reduce_end("P1")
    scatter_wait("gv", gv_rb)
    gvx[3] = (gvs[zi] + wide(gv_rb[0])) + (wide(gv_rb[1]) + wide(gv_rb[2]))
    for k in range(3):
        c = group_copy(0, k, gvx.at[3], gvx.at[k])
        c.start()
        sent.append(c)
    for k in range(3):
        group_copy(1, k, gad, gad_rb.at[k]).wait_recv()
    gad_all[zi] = (gad[x] + gad_rb[0, x]) + (gad_rb[1, x] + gad_rb[2, x])
    gather_start("gad", gad_all)

    reduce_middle("Q", "O")
    reduce_end("Q", "O")

    for k in range(3):
        group_copy(0, k, gvx.at[k], gvx.at[k]).wait_recv()
    total = (gvx[0] + gvx[1]) + (gvx[2] + gvx[3])
    mine = jnp.where(ri == 1, pltpu.roll(total, c_own, 1), total)[:, 0:c_own]
    mine_d = jnp.where(ri == 1, total[:, LANE : 2 * LANE], total[:, 0:LANE])

    def flag(n):
        return train_in[0, n].astype(F32)

    out_depth[...] = mine[0:taps7] * flag(0)
    out_ln_conv[...] = mine[49:50] * flag(1)
    out_scale[...] = mine[50:51] * flag(4)
    out_ln_attn[...] = mine_d[56:57]
    out_ln_mlp[...] = mine_d[57:58]
    gather_wait("gad", gad_all)
    for z in range(Z):
        out_ad[:, z * adq : (z + 1) * adq] = gad_all[z][0:9]
    for name in ARRAYS:
        back_local(name).wait()
        for d in range(1, Z):
            n = ids[name]
            slot = quarter_of(name, native[name], zfrom(d))
            remote(slot, slot, a_send.at[n, d - 1], a_recv.at[n, d - 1], dev(zto(d))).wait_recv()
    for n, buf in enumerate((hid_tok, hid_grid, out_gtok, out_ggrid)):
        c = remote(buf.at[x], buf.at[x], xo_send.at[n], xo_recv.at[n], over_x)
        c.wait_send()
        remote(buf.at[xo], buf.at[xo], xo_send.at[n], xo_recv.at[n], over_x).wait_recv()

    @pl.when(p == 0)
    def _():
        remote(hid_tok.at[x], x_in, h_send.at[0], h_recv.at[0], sib).wait_send()
        remote(hid_grid.at[x], c_in, h_send.at[1], h_recv.at[1], sib).wait_send()

    @pl.when(p == 1)
    def _():
        for d in range(Z):
            over_cores(d).wait_send()
        remote(out_ggrid.at[x], dcot, c_send, c_recv, sib).wait_send()

    for name, buf in line_gathers:
        line_sent(name, buf)

    @pl.when(p == 1)
    def _():
        line_sent("dx3", dx3_all)

    for name, sb, rb in line_sums:
        sum_sent(name, sb, rb)
    for c in sent:
        c.wait_send()
    for name in ARRAYS:
        for which in range(4):
            for d in pieces(name):
                hop_copy(name, which, d).wait_send()
        for d in range(1, Z):
            back_copy(name, d).wait_send()


def run_layers(weights, vectors, order, train, streams, sizes, outer):
    d_dim, c_dim, hq, ffq, cfq, adw, dg = sizes
    vm = pltpu.VMEM
    blocks = []
    for name, value in zip(ARRAYS, weights):
        if name == "Q":
            blocks.append((3, value.shape[1], hq))
        elif name in ("O", "F2"):
            blocks.append((value.shape[0] // Z, value.shape[1]))
        else:
            blocks.append((value.shape[0], value.shape[1] // Z))
    rows = Z * TOK

    def act(width, count=Z, kind=BF):
        return vm((count, TOK, width), kind)

    def line(width):
        return vm((2, 3, TOK, width), BF)

    scratch = [vm((2, Z, R) + s, BF) for s in blocks] + [
        vm(lead + s[:-2] + (s[-2] // 2, s[-1]), BF)
        for s in blocks
        for lead in ((Z, R), (2, Z), (Z,), (Z,))
    ]
    scratch += [
        vm((64, 2 * LANE), F32), vm((64, 2 * LANE), BF), vm((Z * R, 64, 2 * LANE), BF), vm((2, 16, adw), F32), vm((64, c_dim), F32), vm((8, d_dim), F32),
        vm((TOK, d_dim), BF), vm((TOK, c_dim), BF), act(d_dim), act(c_dim), act(d_dim), act(c_dim),
        act(d_dim), line(d_dim), act(c_dim), line(c_dim), act(d_dim), line(d_dim),
        act(2 * adw), act(2 * adw, 3), vm((4, 8, dg), F32), vm((4, 8, dg), F32),
        vm((2, rows, 3 * hq), BF), vm((2, hq // HD, Z, TOK, TOK), BF), vm((2, rows, hq), BF),
        vm((2, rows, ffq), BF), vm((2, rows, ffq), BF), vm((2, rows, cfq), BF), vm((2, rows, cfq), BF),
        vm((TOK, c_dim), F32), vm((TOK, LANE), F32), vm((TOK, c_dim), F32), vm((TOK, d_dim), F32), vm((TOK, c_dim), F32),
        vm((2, rows, adw), F32), vm((2, Z, TOK, adw), F32), vm((2, 8, adw), F32), vm((2, 8, adw), F32),
        vm((TOK, d_dim), BF), vm((TOK, c_dim), BF), act(d_dim), act(d_dim), line(d_dim), act(c_dim), line(c_dim),
        act(d_dim), act(c_dim),
        act(d_dim), line(d_dim), act(c_dim), line(c_dim), vm((2, rows, ffq), BF), vm((2, rows, hq), BF),
        vm((2, rows, 3 * hq), BF), vm((2, rows, cfq), BF), vm((TOK, d_dim), F32), vm((TOK, c_dim), F32), vm((2, rows, adw), BF),
        vm((TOK, c_dim), F32),
        vm((Z, 64, c_dim // Z), F32), vm((Z, 64, c_dim // Z), BF), vm((3, 64, c_dim // Z), BF), vm((4, 64, c_dim // Z), F32),
        vm((2, 16, adw), F32), vm((3, 2, 16, adw), F32), vm((Z, 16, adw), F32),
        vm((2 * ffq, rows), BF),
    ]
    dma = pltpu.SemaphoreType.DMA
    na = len(ARRAYS)
    scratch += [
        dma((len(EVENTS), 3)), dma((len(EVENTS), 3)), dma((len(EVENTS), 6)), dma((len(EVENTS), 6)), dma((na, 3)), dma((na, 3)), dma((na,)),
        dma((na, 4, Z)), dma((na, 4, Z)), dma((7,)), dma((7,)), dma, dma, dma((2,)), dma((2,)), dma((Z,)), dma((Z,)), dma, dma,
        dma((4,)), dma((4,)), dma((na, 4, Z)), dma((na, 4, Z)), dma((na, 3)), dma((na, 3)), dma((2, 3)), dma((2, 3)),
        pltpu.SemaphoreType.REGULAR,
    ]
    sds = jax.ShapeDtypeStruct
    out_shape = [sds((2, TOK, d_dim), BF), sds((2, TOK, c_dim), BF)] * 2
    out_shape += [sds(value.shape, BF) for value in weights]
    out_shape += [sds(value.shape, F32) for value in vectors]
    any_spec = pl.BlockSpec(memory_space=pl.ANY)
    vm_spec = pl.BlockSpec(memory_space=pltpu.VMEM)
    sm_spec = pl.BlockSpec(memory_space=pltpu.SMEM)
    return pl.pallas_call(
        functools.partial(main_kernel, sizes, outer),
        out_shape=out_shape,
        in_specs=[any_spec] * na + [vm_spec] * 6 + [sm_spec] * 2 + [vm_spec] * 4,
        out_specs=[vm_spec] * 4 + [any_spec] * na + [vm_spec] * 6,
        scratch_shapes=scratch,
        compiler_params=pltpu.CompilerParams(
            collective_id=0, has_side_effects=True, vmem_limit_bytes=62 * 1024 * 1024
        ),
        cost_estimate=pl.CostEstimate(flops=26 * 10**9, bytes_accessed=10**8, transcendentals=10**7),
        name="layers",
    )(*weights, *vectors, order, train, *streams)


def finish_kernel(flagged, layer_zero, count, *refs):
    grads, streams, vectors = refs[:count], refs[count : count + 4], refs[count + 4 : count + 10]
    order, train = refs[count + 10 : count + 12]
    refs = refs[count + 12 :]
    out_grads, out_streams, out_vectors = refs[:count], refs[count : count + 4], refs[count + 4 : count + 10]
    refs = refs[count + 10 :]
    held, wide_ones = refs[:count], refs[count : 2 * count]
    in_sem, out_sem = refs[2 * count :]

    def fetch(n):
        return pltpu.make_async_copy(grads[n], held[n], in_sem.at[n])

    def put_back(n):
        return pltpu.make_async_copy(wide_ones[n], out_grads[n], out_sem.at[n])

    for n in range(count):
        fetch(n).start()
    swap = (lax.axis_index("pipe") == layer_zero) & (order[0, 0] == 1)
    for n, (src, dst) in enumerate(zip(streams, out_streams)):
        for m in range(2):
            dst[m] = src[m] if n < 2 else jnp.where(swap, src[1 - m], src[m])
    for src, dst in zip(vectors, out_vectors):
        if len(dst.shape) == 3:
            for row in range(dst.shape[0]):
                dst[row] = src[row : row + 1]
        else:
            dst[...] = src[...]
    for n in range(count):
        fetch(n).wait()
        src, dst = held[n], wide_ones[n]
        scale = train[0, flagged[n]].astype(F32) if n in flagged else None
        lead = src.shape[0] if len(src.shape) == 3 else 1

        @pl.loop(0, lead * (src.shape[-2] // 16))
        def _(step):
            rows = pl.ds(pl.multiple_of((step // lead) * 16, 16), 16)
            at = (step % lead, rows) if len(src.shape) == 3 else (rows,)
            value = wide(src[at])
            dst[at] = value if scale is None else value * scale

        put_back(n).start()
    for n in range(count):
        put_back(n).wait()


def finish(outs, order, train):
    count = len(ARRAYS)
    streams, grads, vectors = outs[:4], outs[4 : 4 + count], outs[4 + count :]
    any_spec = pl.BlockSpec(memory_space=pl.ANY)
    sm_spec = pl.BlockSpec(memory_space=pltpu.SMEM)
    vm_spec = pl.BlockSpec(memory_space=pltpu.VMEM)
    sds = jax.ShapeDtypeStruct
    dma = pltpu.SemaphoreType.DMA
    flagged = {ARRAYS.index("P1"): 2, ARRAYS.index("P2"): 3}
    return pl.pallas_call(
        functools.partial(finish_kernel, flagged, 0, count),
        out_shape=[sds(g.shape, F32) for g in grads]
        + [sds(value.shape, value.dtype) for value in streams]
        + [sds(value.shape if value.shape[0] == 1 else (value.shape[0], 1, value.shape[1]), F32) for value in vectors],
        in_specs=[any_spec] * count + [vm_spec] * 10 + [sm_spec] * 2,
        out_specs=[any_spec] * count + [vm_spec] * 10,
        scratch_shapes=[pltpu.VMEM(g.shape, BF) for g in grads]
        + [pltpu.VMEM(g.shape, F32) for g in grads]
        + [dma((count,)), dma((count,))],
        compiler_params=pltpu.CompilerParams(vmem_limit_bytes=62 * 1024 * 1024),
        name="finish",
    )(*grads, *streams, *vectors, order, train)


def per_device(
    tokens,
    conv_grid,
    order,
    trainable,
    ln_attn,
    w_qkv,
    w_attn_out,
    ln_mlp,
    w_fc_in,
    w_fc_out,
    conv_depth,
    ln_conv,
    w_pw_in,
    w_pw_out,
    layer_scale,
    w_adapt,
    adapt_depth,
    w_gate_in,
    w_gate_out,
    tok_cot,
    grid_cot,
):
    dp_count = lax.axis_size("dp")
    outer = dp_count // (Z * R)
    groups = [[g * outer + o for o in range(outer)] for g in range(Z * R)]

    def block(value, axis):
        value = value[0]
        if outer == 1:
            return value
        return lax.all_gather(value, "dp", axis=axis, tiled=True, axis_index_groups=groups)

    def share(value, axis):
        if outer > 1:
            value = lax.psum_scatter(
                value, "dp", scatter_dimension=axis, tiled=True, axis_index_groups=groups
            )
        return value[None]

    qkv = block(w_qkv, 1)
    gate_in = block(w_gate_in, 1).T
    pw_in = block(w_pw_in, 0)
    adapt = block(w_adapt, 0)
    fc_in = block(w_fc_in, 0)
    weights = (
        pw_in,
        block(w_pw_out, 1).T,
        qkv,
        block(w_attn_out, 1),
        adapt,
        gate_in,
        block(w_gate_out, 0),
        fc_in,
        block(w_fc_out, 1),
    )
    vectors = (
        block(conv_depth, 1),
        block(ln_conv, 0)[None],
        block(layer_scale, 0)[None],
        block(ln_attn, 0)[None],
        block(ln_mlp, 0)[None],
        adapt_depth[0],
    )
    spread = Z * R
    sizes = (
        qkv.shape[1] * spread, pw_in.shape[0] * spread, qkv.shape[2] // Z, fc_in.shape[1] // Z,
        pw_in.shape[1] // Z, adapt.shape[1] // Z, gate_in.shape[0] * spread,
    )

    def rows_of(value):
        return value.reshape(value.shape[0], TOK, value.shape[-1])

    streams = [rows_of(value) for value in (tokens, conv_grid, tok_cot, grid_cot)]
    outs = run_layers(weights, vectors, order, trainable, streams, sizes, outer)
    done = finish(outs, order, trainable)
    g_p1, g_p2, g_q, g_o, g_e, g_gi, g_go, g_f1, g_f2 = done[:9]
    hid_tok, hid_grid, g_tok, g_grid = done[9:13]
    g_depth, g_ln_conv, g_scale, g_ln_attn, g_ln_mlp, g_ad = done[13:]
    grid_shape = (1,) + conv_grid.shape
    tok_shape = (1,) + tokens.shape
    g_depth, g_ad = g_depth[:, 0], g_ad[:, 0]
    if outer > 1:
        g_ad = lax.psum(g_ad, "dp", axis_index_groups=groups)
    return (
        hid_tok.reshape(tok_shape),
        hid_grid.reshape(grid_shape),
        g_tok.reshape(tok_shape),
        g_grid.reshape(grid_shape),
        share(g_ln_attn[0], 0),
        share(g_q, 1),
        share(g_o, 1),
        share(g_ln_mlp[0], 0),
        share(g_f1, 0),
        share(g_f2, 1),
        share(g_depth, 1),
        share(g_ln_conv[0], 0),
        share(g_p1, 0),
        share(g_p2.T, 1),
        share(g_scale[0], 0),
        share(g_e, 0),
        g_ad[None],
        share(g_gi.T, 1),
        share(g_go, 0),
    )


def solution(mesh):
    in_specs = (
        P(None, "dp", None, None),
        P(None, "dp", None, None, None),
        P("dp", None),
        P("pipe", None),
        P("pipe", "dp"),
        P("pipe", None, "dp", "tensor"),
        P("pipe", "tensor", "dp"),
        P("pipe", "dp"),
        P("pipe", "dp", "tensor"),
        P("pipe", "tensor", "dp"),
        P("pipe", None, "dp"),
        P("pipe", "dp"),
        P("pipe", "dp", "tensor"),
        P("pipe", "tensor", "dp"),
        P("pipe", "dp"),
        P("pipe", "dp", "tensor"),
        P("pipe", None, "tensor"),
        P("pipe", "tensor", "dp"),
        P("pipe", "dp", "tensor"),
        P(None, "dp", None, None),
        P(None, "dp", None, None, None),
    )
    out_specs = (
        P("pipe", None, "dp", None, None),
        P("pipe", None, "dp", None, None, None),
        P("pipe", None, "dp", None, None),
        P("pipe", None, "dp", None, None, None),
        P("pipe", "dp"),
        P("pipe", None, "dp", "tensor"),
        P("pipe", "tensor", "dp"),
        P("pipe", "dp"),
        P("pipe", "dp", "tensor"),
        P("pipe", "tensor", "dp"),
        P("pipe", None, "dp"),
        P("pipe", "dp"),
        P("pipe", "dp", "tensor"),
        P("pipe", "tensor", "dp"),
        P("pipe", "dp"),
        P("pipe", "dp", "tensor"),
        P("pipe", None, "tensor"),
        P("pipe", "tensor", "dp"),
        P("pipe", "dp", "tensor"),
    )
    return jax.shard_map(
        per_device, mesh=mesh, in_specs=in_specs, out_specs=out_specs, check_vma=False
    )
```

```python
import functools

import jax
import jax.numpy as jnp
from jax import lax
from jax.experimental import pallas as pl
from jax.experimental.pallas import tpu as pltpu
from jax.sharding import PartitionSpec as P

HD = 64
Z = 4
R = 2
TOK = 64
SIDE = 8
LANE = 128
BF = jnp.bfloat16
F32 = jnp.float32
ARRAYS = ("P1", "P2", "Q", "O", "E", "Gi", "Go", "F1", "F2")
EVENTS = (
    "n1", "f", "o", "cv", "n2", "c2", "m", "br", "gs",
    "dx3", "dgh", "dn2", "dc2", "dx1", "dcv", "dn1", "df", "gv", "gad",
)


def mm(a, b):
    return lax.dot_general(a, b, (((1,), (0,)), ((), ())), preferred_element_type=F32)


def mm_nt(a, b):
    return lax.dot_general(a, b, (((1,), (1,)), ((), ())), preferred_element_type=F32)


def mm_tn(a, b):
    return lax.dot_general(a, b, (((0,), (0,)), ((), ())), preferred_element_type=F32)


def flat(value):
    return value.reshape(-1, value.shape[-1])


def low(value):
    return value.astype(BF)


def wide(value):
    return value.astype(F32)


def gelu_pair(h):
    phi = 0.5 * (1.0 + lax.erf(h * 0.7071067811865476))
    dens = jnp.exp(-0.5 * h * h) * 0.3989422804014327
    return h * phi, phi + h * dens


def normed(value):
    centred = value - jnp.mean(value, axis=-1, keepdims=True)
    rs = lax.rsqrt(jnp.mean(centred * centred, axis=-1, keepdims=True) + 1e-06)
    return centred * rs, rs


def norm_back(dn, n_hat, rs, gain):
    gd = dn * gain
    return (
        gd
        - jnp.mean(gd, axis=-1, keepdims=True)
        - n_hat * jnp.mean(gd * n_hat, axis=-1, keepdims=True)
    ) * rs


def col_shift(value, by):
    if by == 0:
        return value
    at = lax.broadcasted_iota(jnp.int32, value.shape, 0) % SIDE
    rolled = pltpu.roll(value, (-by) % TOK, 0)
    return jnp.where((at + by >= 0) & (at + by < SIDE), rolled, 0.0)


def row_shift(value, by):
    if by == 0:
        return value
    gap = jnp.zeros((abs(by) * SIDE, value.shape[1]), value.dtype)
    if by > 0:
        return jnp.concatenate([value[by * SIDE :], gap], axis=0)
    return jnp.concatenate([gap, value[: TOK + by * SIDE]], axis=0)


def depthwise(value, tap, side):
    half = side // 2
    shifted = [col_shift(value, b - half) for b in range(side)]
    total = None
    for a in range(side):
        line = None
        for b in range(side):
            term = shifted[b] * tap(a * side + b)
            line = term if line is None else line + term
        line = row_shift(line, a - half)
        total = line if total is None else total + line
    return total


def depthwise_taps(value, grad, side, put):
    half = side // 2
    shifted = [col_shift(value, b - half) for b in range(side)]
    for a in range(side):
        d = a - half
        lo, hi = max(0, -d) * SIDE, (SIDE - max(0, d)) * SIDE
        for b in range(side):
            part = shifted[b][lo + d * SIDE : hi + d * SIDE] * grad[lo:hi]
            put(a * side + b, jnp.sum(part, axis=0, keepdims=True))


def lanes_of(at, width):
    return pl.ds(pl.multiple_of(at * width, width), width)


def side_by_side(blocks):
    return jnp.concatenate(blocks, axis=1)


def main_kernel(dims, outer, *refs):
    at = iter(refs)

    def take(count):
        return [next(at) for _ in range(count)]

    na = len(ARRAYS)
    source = dict(zip(ARRAYS, take(na)))
    (
        depth_in, ln_conv_in, scale_in, ln_attn_in, ln_mlp_in, adapt_depth_in,
        order_in, train_in, tok_in, grid_in, tcot_in, gcot_in,
    ) = take(12)
    hid_tok, hid_grid, out_gtok, out_ggrid = take(4)
    native = dict(zip(ARRAYS, take(na)))
    out_depth, out_ln_conv, out_scale, out_ln_attn, out_ln_mlp, out_ad = take(6)
    W = dict(zip(ARRAYS, take(na)))
    hops = take(4 * na)
    RX = {name: hops[4 * n : 4 * n + 4] for n, name in enumerate(ARRAYS)}
    (
        v_loc, v_low, vv, aq, vec_c, vec_d, x_in, c_in, n1_all, f_all, n2_all, c2_all,
        o_sb, o_rb, cv_sb, cv_rb, m_sb, m_rb, br_sb, br_rb, gsb, dgb,
        qkv, prob, ctx, u, up, r, rp, cn, crs, cv_sum, x1, c2f,
        adapted, spread, pooled, gate,
        dx3, dcot, dx3_all, dn2_sb, dn2_rb, dc2_sb, dc2_rb, dx1_all, dcv_all,
        dn1_sb, dn1_rb, df_sb, df_rb, dh, do_all, dqkv, dhc, dx1, dc2t, dad, dcn,
        gvs, gvs_low, gv_rb, gvx, gad, gad_rb, gad_all, turned,
    ) = take(67)
    (
        zs_send, zs_recv, l_send, l_recv, s1_send, s1_recv, loc_sem, s2_send, s2_recv,
        v_send, v_recv, q_send, q_recv, h_send, h_recv, b_send, b_recv, c_send, c_recv,
        xo_send, xo_recv, g_send, g_recv, a_send, a_recv, gx_send, gx_recv, go,
    ) = take(28)

    p = lax.axis_index("pipe")
    dpi = lax.axis_index("dp")
    x = lax.axis_index("tensor")
    rest = dpi % outer
    zi = dpi // (outer * R)
    ri = (dpi // outer) % R
    xo = 1 - x
    ro = 1 - ri
    d_dim, c_dim, hq, ffq, cfq, adq, dg = dims
    adh = Z * adq
    dz, cz = d_dim // Z, c_dim // Z
    tile = 256
    ids = {name: number for number, name in enumerate(ARRAYS)}
    ev = {name: number for number, name in enumerate(EVENTS)}

    def dev(z=None, rr=None, xx=None, pp=None):
        z = zi if z is None else z
        rr = ri if rr is None else rr
        return (
            p if pp is None else pp,
            (z * R + rr) * outer + rest,
            x if xx is None else xx,
        )

    def zto(d):
        return lax.rem(zi + d, Z)

    def zfrom(d):
        return lax.rem(zi + Z - d, Z)

    def remote(src, dst, ssem, rsem, device):
        return pltpu.make_async_remote_copy(
            src_ref=src, dst_ref=dst, send_sem=ssem, recv_sem=rsem,
            device_id=device, device_id_type=pl.DeviceIdType.MESH,
        )

    sib = dev(pp=1 - p)
    over_r, over_x = dev(rr=ro), dev(xx=xo)

    def z_copy(e, d, src, dst):
        return remote(src, dst, zs_send.at[e, d - 1], zs_recv.at[e, d - 1], dev(zto(d)))

    sent = []

    def gather_copies(name, buf):
        return [z_copy(ev[name], d, buf.at[zi], buf.at[zi]) for d in range(1, Z)]

    def gather_start(name, buf, keep=True):
        copies = gather_copies(name, buf)
        for c in copies:
            c.start()
        if keep:
            sent.extend(copies)

    def gather_wait(name, buf):
        for d in range(1, Z):
            slot = buf.at[zfrom(d)]
            z_copy(ev[name], d, slot, slot).wait_recv()

    def scatter_start(name, sb, rb):
        for d in range(1, Z):
            c = z_copy(ev[name], d, sb.at[zto(d)], rb.at[d - 1])
            c.start()
            sent.append(c)

    def scatter_wait(name, rb):
        for d in range(1, Z):
            z_copy(ev[name], d, rb.at[d - 1], rb.at[d - 1]).wait_recv()

    def right():
        return dev(zi + 1)

    def left():
        return dev(zi - 1)

    def pass_copy(name, buf, toward, s):
        e, k = ev[name], (0 if toward > 0 else 3) + s
        blk = buf.at[zi - toward * s]
        return remote(blk, blk, l_send.at[e, k], l_recv.at[e, k], right() if toward > 0 else left())

    def pass_cond(toward, s):
        if toward > 0:
            return (zi < Z - 1) & (zi - s >= 0)
        return (zi > 0) & (zi + s <= Z - 1)

    def line_start(name, buf):
        for toward in (1, -1):

            @pl.when(pass_cond(toward, 0))
            def _():
                pass_copy(name, buf, toward, 0).start()

    def line_step(name, buf, *steps):
        e = ev[name]
        for s in steps:
            for toward in (1, -1):
                src = zi - toward * s

                @pl.when((src >= 0) & (src <= Z - 1))
                def _():
                    blk = buf.at[src]
                    k = (0 if toward > 0 else 3) + s - 1
                    remote(blk, blk, l_send.at[e, k], l_recv.at[e, k], sib).wait_recv()

                if s < Z - 1:

                    @pl.when(pass_cond(toward, s))
                    def _():
                        pass_copy(name, buf, toward, s).start()

    def line_sent(name, buf):
        for toward in (1, -1):
            for s in range(Z - 1):

                @pl.when(pass_cond(toward, s))
                def _():
                    pass_copy(name, buf, toward, s).wait_send()

    def sum_copy(name, sb, rb, toward, k, first):
        e, way = ev[name], (0 if toward > 0 else 1)
        src = sb.at[zi + toward * k] if first else rb.at[way, k]
        q = way * 3 + k - 1
        return remote(src, rb.at[way, k - 1], l_send.at[e, q], l_recv.at[e, q], right() if toward > 0 else left())

    def at_end(toward):
        return zi == (0 if toward > 0 else Z - 1)

    def passes(toward, k):
        dest = zi + toward * k
        return jnp.logical_not(at_end(toward)) & (dest >= 0) & (dest <= Z - 1)

    def sum_start(name, sb, rb):
        for toward in (1, -1):

            @pl.when(at_end(toward))
            def _():
                for k in (3, 2, 1):
                    sum_copy(name, sb, rb, toward, k, True).start()

    def sum_arrival(name, rb, way, k):
        e = ev[name]
        slot = rb.at[way, k]
        return remote(slot, slot, l_send.at[e, way * 3 + k], l_recv.at[e, way * 3 + k], sib)

    def sum_step(name, sb, rb, *ks):
        for k in ks:
            for way, toward in enumerate((1, -1)):

                @pl.when(passes(toward, k))
                def _():
                    sum_arrival(name, rb, way, k).wait_recv()
                    rb[way, k] = low(wide(rb[way, k]) + wide(sb[zi + toward * k]))
                    sum_copy(name, sb, rb, toward, k, False).start()

    def sum_wait(name, rb):
        for way, toward in enumerate((1, -1)):

            @pl.when(jnp.logical_not(at_end(toward)))
            def _():
                sum_arrival(name, rb, way, 0).wait_recv()

    def summed(sb, rb):
        return wide(sb[zi]) + (wide(rb[0, 0]) + wide(rb[1, 0]))

    def sum_sent(name, sb, rb):
        for toward in (1, -1):

            @pl.when(at_end(toward))
            def _():
                for k in (3, 2, 1):
                    sum_copy(name, sb, rb, toward, k, True).wait_send()

            for k in (2, 1):

                @pl.when(passes(toward, k))
                def _():
                    sum_copy(name, sb, rb, toward, k, False).wait_send()

    def share_start(name, buf):
        for d in range(1, Z):
            c = z_copy(ev[name], d, buf.at[3], buf.at[d - 1])
            c.start()
            sent.append(c)

    def scattered(sb, rb):
        return (wide(sb[zi]) + wide(rb[0])) + (wide(rb[1]) + wide(rb[2]))

    barrier = pltpu.get_barrier_semaphore()
    greeted = [sib]
    for d in range(1, Z):
        greeted += [dev(zto(d)), dev(zto(d), ro), dev(zto(d), pp=1 - p)]
    greeted += [over_r, over_x, dev(rr=ro, xx=xo)]
    for device in greeted:
        pl.semaphore_signal(barrier, inc=1, device_id=device, device_id_type=pl.DeviceIdType.MESH)
    v_loc[...] = jnp.zeros(v_loc.shape, F32)
    taps7 = depth_in.shape[0]
    c_own = depth_in.shape[1]
    v_loc[0:taps7, 0:c_own] = wide(depth_in[...])
    v_loc[49:50, 0:c_own] = wide(ln_conv_in[...])
    v_loc[50:51, 0:c_own] = wide(scale_in[...])
    v_loc[56:57, 0:LANE] = wide(ln_attn_in[...])
    v_loc[57:58, 0:LANE] = wide(ln_mlp_in[...])
    aq[x] = jnp.zeros(aq.shape[1:], F32)
    aq[x, 0:9] = wide(adapt_depth_in[:, lanes_of(zi, adq)])
    v_low[...] = low(v_loc[...])
    line_sums = (
        ("o", o_sb, o_rb), ("cv", cv_sb, cv_rb), ("m", m_sb, m_rb), ("dn2", dn2_sb, dn2_rb),
        ("dc2", dc2_sb, dc2_rb), ("dn1", dn1_sb, dn1_rb), ("df", df_sb, df_rb),
    )
    line_gathers = (
        ("n1", n1_all), ("f", f_all), ("n2", n2_all), ("c2", c2_all), ("dx1", dx1_all), ("dcv", dcv_all),
    )
    for _, _, rb in line_sums:
        for way, toward in enumerate((1, -1)):

            @pl.when(at_end(toward))
            def _():
                rb[way, 0] = jnp.zeros(rb.shape[2:], BF)

    pl.semaphore_wait(barrier, len(greeted))

    me8 = zi * R + ri
    v_arrivals = []
    for n, (d, flip) in enumerate([(d, s) for d in range(Z) for s in (0, 1)][1:]):
        tr = ro if flip else ri
        c = remote(v_low, vv.at[me8], v_send.at[n], v_recv.at[n], dev(zto(d), tr))
        c.start()
        sent.append(c)
        fr = zfrom(d) * R + tr
        v_arrivals.append(remote(vv.at[fr], vv.at[fr], v_send.at[n], v_recv.at[n], dev(zto(d), tr)))
    vv[me8] = v_low[...]
    c = remote(aq.at[x], aq.at[x], q_send, q_recv, over_x)
    c.start()
    sent.append(c)

    by_rows = ("O", "F2")

    def quarter_of(name, ref, z):
        if name == "Q":
            return ref.at[:, :, lanes_of(z, hq)]
        if name in by_rows:
            height = ref.shape[0] // Z
            return ref.at[pl.ds(pl.multiple_of(z * height, height), height)]
        return ref.at[:, lanes_of(z, ref.shape[1] // Z)]

    def step1_local(name):
        return pltpu.make_async_copy(
            quarter_of(name, source[name], zi), W[name].at[x, zi, ri], loc_sem.at[ids[name]]
        )

    def step1_copy(name, d):
        k = ids[name]
        return remote(
            quarter_of(name, source[name], zto(d)), W[name].at[x, zi, ri],
            s1_send.at[k, d - 1], s1_recv.at[k, d - 1], dev(zto(d)),
        )

    def half_of(name, j, z, rr, upper):
        w = W[name]
        half = w.shape[-2] // 2
        rows = slice(half, None) if upper else slice(0, half)
        if len(w.shape) == 6:
            return w.at[j, z, rr, :, rows]
        return w.at[j, z, rr, rows]

    def step2_copy(name, which, d):
        k = ids[name]
        z = zfrom(d)
        if which < 2:
            src = quarter_of(name, source[name], zi) if d == 0 else W[name].at[x, z, ri]
            dst = W[name].at[x, z, ri]
        else:
            src = dst = half_of(name, x, z, ro, False) if which == 2 else half_of(name, xo, z, ri, True)
        to = over_x if which in (1, 2) else over_r
        return remote(src, dst, s2_send.at[k, which, d], s2_recv.at[k, which, d], to)

    def step2_arrival(name, which, d):
        k = ids[name]
        z = zfrom(d)
        if which < 2:
            ref = W[name].at[x, z, ro] if which == 0 else W[name].at[xo, z, ri]
        else:
            ref = half_of(name, xo, z, ro, which == 3)
        to = over_x if which in (1, 2) else over_r
        return remote(ref, ref, s2_send.at[k, which, d], s2_recv.at[k, which, d], to)

    def relay1(*names):
        for name in names:
            for d in range(1, Z):
                step1_copy(name, d).start()

    def relay0(*names):
        for name in names:
            step1_local(name).start()
            step2_copy(name, 0, 0).start()
            step2_copy(name, 1, 0).start()

    def relay2(name, ds=(1, 2, 3)):
        k = ids[name]
        for d in ds:
            slot = W[name].at[x, zfrom(d), ri]
            remote(slot, slot, s1_send.at[k, d - 1], s1_recv.at[k, d - 1], dev(zto(d))).wait_recv()
            step2_copy(name, 0, d).start()
            step2_copy(name, 1, d).start()

    def relay3(name, ds=(0, 1, 2, 3)):
        for d in ds:
            step2_arrival(name, 0, d).wait_recv()
            step2_copy(name, 2, d).start()
            step2_arrival(name, 1, d).wait_recv()
            step2_copy(name, 3, d).start()

    def relay4(*names):
        for name in names:
            step1_local(name).wait()
            for d in range(Z):
                step2_arrival(name, 2, d).wait_recv()
                step2_arrival(name, 3, d).wait_recv()

    def relay_sent():
        for name in ARRAYS:
            for d in range(1, Z):
                step1_copy(name, d).wait_send()
            for which in range(4):
                for d in range(Z):
                    step2_copy(name, which, d).wait_send()

    @pl.when(p == 0)
    def _():
        relay0("P1")
        relay1("P1")
        relay0("P2")
        relay1("P2")
        relay0("Q", "O", "E", "Gi", "Go", "F1", "F2")

    @pl.when(p == 1)
    def _():
        dx3[...] = tcot_in[x]
        dcot[...] = gcot_in[x]
        dx3_all[zi] = tcot_in[x]
        line_start("dx3", dx3_all)

    for c in v_arrivals:
        c.wait_recv()
    remote(aq.at[xo], aq.at[xo], q_send, q_recv, over_x).wait_recv()
    low_lanes = lax.broadcasted_iota(jnp.int32, (64, LANE), 1) < LANE // 2
    for z in range(Z):
        first, second = wide(vv[2 * z]), pltpu.roll(wide(vv[2 * z + 1]), LANE // 2, 1)
        vec_c[:, z * cz : z * cz + LANE] = first[:, 0:LANE]
        vec_c[:, z * cz + LANE : z * cz + 2 * LANE] = jnp.where(
            low_lanes, first[:, LANE:], second[:, 0:LANE]
        )
        vec_c[:, z * cz + 2 * LANE : (z + 1) * cz] = second[:, LANE:]
    for i in range(Z * R):
        vec_d[:, i * LANE : (i + 1) * LANE] = wide(vv[i])[56:64, 0:LANE]

    def gain_d(row):
        return vec_d[row : row + 1, :]

    def gain_c(row):
        return vec_c[row : row + 1, :]

    def token_entry():
        n_hat, _ = normed(wide(x_in[...]))
        n1_all[zi] = low(n_hat * gain_d(0))
        line_start("n1", n1_all)

    def conv_entry():
        @pl.loop(0, c_dim // LANE)
        def _(ch):
            lanes = lanes_of(ch, LANE)
            taps = vec_c[:, lanes]
            cn[:, lanes] = depthwise(wide(c_in[:, lanes]), lambda k: taps[k : k + 1], 7)

        n_hat, rs = normed(cn[...])
        cn[...] = n_hat
        crs[...] = jnp.broadcast_to(rs, crs.shape)
        f_all[zi] = low(n_hat * gain_c(49))
        line_start("f", f_all)

    def first_relays(pump):
        relay2("P1")
        pump(1)
        relay1("Q", "O")
        relay2("P2")
        pump(2)
        relay3("P1")


    @pl.when(p == 0)
    def _():
        first = order_in[0, x] == 0
        c_in[...] = jnp.where(first, grid_in[0], grid_in[1])
        x_in[...] = jnp.where(first, tok_in[0], tok_in[1])
        conv_entry()
        token_entry()

        def pump(s):
            line_step("f", f_all, s)
            line_step("n1", n1_all, s)

        first_relays(pump)
        line_step("f", f_all, 3)
        line_step("n1", n1_all, 3)

    @pl.when(p == 1)
    def _():
        pl.semaphore_wait(go, 1)
        relay0("P1")
        relay1("P1")
        relay0("P2")
        relay1("P2")
        relay0("Q", "O", "E", "Gi", "Go", "F1", "F2")
        first_relays(lambda s: line_step("dx3", dx3_all, s))
        remote(c_in, c_in, h_send.at[1], h_recv.at[1], sib).wait_recv()
        conv_entry()
        line_step("dx3", dx3_all, 3)
        line_step("f", f_all, 1)

    relay2("Q")
    relay2("O")
    relay1("E", "Gi", "Go")
    relay3("P2", (0, 1))

    @pl.when(p == 1)
    def _():
        line_step("f", f_all, 2, 3)

    relay4("P1")

    def conv_hidden(j):
        act, der = gelu_pair(mm(flat(f_all[...]), flat(W["P1"][j])))
        r[j] = low(act)
        rp[j] = low(der)

    conv_hidden(0)

    relay3("P2", (2, 3))
    for name in ("E", "Gi", "Go"):
        relay2(name)
    relay1("F1")
    conv_hidden(1)
    relay3("Q")
    relay3("O")
    relay2("F1")
    relay1("F2")

    @pl.when(p == 0)
    def _():
        pl.semaphore_signal(go, inc=1, device_id=sib, device_id_type=pl.DeviceIdType.MESH)

    relay4("P2")

    def pair_rows(name, pair):
        zs = pl.ds(pair * 2, 2)
        return side_by_side([flat(W[name][0, zs]), flat(W[name][1, zs])])

    def pair_out(left, name, sb, width):
        both = side_by_side([left[0], left[1]])

        @pl.loop(0, Z // 2)
        def _(pair):
            acc = mm_nt(both, pair_rows(name, pair))
            sb[:, :, lanes_of(pair, 2 * width)] = low(acc).reshape(Z, TOK, 2 * width)

    pair_out(r, "P2", cv_sb, cz)

    sum_start("cv", cv_sb, cv_rb)

    for name in ("E", "Gi", "Go"):
        relay3(name)
    sum_step("cv", cv_sb, cv_rb, 2)
    relay2("F2")
    sum_step("cv", cv_sb, cv_rb, 1)

    @pl.when(p == 1)
    def _():
        remote(x_in, x_in, h_send.at[0], h_recv.at[0], sib).wait_recv()
        token_entry()
        line_step("n1", n1_all, 1, 2, 3)

    relay4("Q", "O")
    wide_q = side_by_side([flat(W["Q"][j, :, :, s]) for j in range(2) for s in range(3)])
    qkv_both = low(mm(flat(n1_all[...]), wide_q))
    for j in range(2):
        qkv[j] = qkv_both[:, j * 3 * hq : (j + 1) * 3 * hq]
    @pl.loop(0, Z)
    def _(b):
        rows = lanes_of(b, TOK)
        for j in range(2):
            outs = []
            for h in range(hq // HD):
                q, kk, vals = (qkv[j, rows, s * hq + h * HD : s * hq + (h + 1) * HD] for s in range(3))
                sc = mm_nt(q, kk) * HD ** (-0.5)
                e = jnp.exp(sc - jnp.max(sc, axis=-1, keepdims=True))
                pr = low(e / jnp.sum(e, axis=-1, keepdims=True))
                prob[j, h, b] = pr
                outs.append(mm(pr, vals))
            ctx[j, rows, :] = low(side_by_side(outs))

    out_cols = [
        jnp.concatenate([W["O"][0, z, rr], W["O"][1, z, rr]], axis=0) for z in range(Z) for rr in range(R)
    ]
    o_sb[...] = low(mm(side_by_side([ctx[0], ctx[1]]), side_by_side(out_cols))).reshape(Z, TOK, d_dim)
    sum_start("o", o_sb, o_rb)

    relay3("F1")

    sum_wait("cv", cv_rb)
    cv_sum[...] = summed(cv_sb, cv_rb)
    c2f[...] = wide(c_in[...]) + gain_c(50) * cv_sum[...]
    c2_low = low(c2f[...])
    c2_all[zi] = c2_low
    line_start("c2", c2_all)
    sum_step("o", o_sb, o_rb, 2)
    hid_grid[x] = c2_low

    @pl.when(p == 0)
    def _():
        remote(hid_grid.at[x], c_in, h_send.at[1], h_recv.at[1], sib).start()

    relay3("F2")
    sum_step("o", o_sb, o_rb, 1)
    line_step("c2", c2_all, 1)
    sum_wait("o", o_rb)
    x1[...] = wide(x_in[...]) + summed(o_sb, o_rb)
    n_hat, _ = normed(x1[...])
    n2_all[zi] = low(n_hat * gain_d(1))
    line_start("n2", n2_all)

    relay4("E", "Gi", "Go")
    line_step("c2", c2_all, 2)
    line_step("n2", n2_all, 1)
    line_step("c2", c2_all, 3)
    row8 = lax.broadcasted_iota(jnp.int32, (8, adq), 0)
    gs_part = None
    ad_both = mm(flat(c2_all[...]), side_by_side([flat(W["E"][0]), flat(W["E"][1])]))
    for j in range(2):
        ad = ad_both[:, j * adq : (j + 1) * adq]
        adapted[j] = ad
        taps = aq[j]
        pool = jnp.zeros((8, adq), F32)
        for b in range(Z):
            sp = depthwise(ad[b * TOK : (b + 1) * TOK], lambda k: taps[k : k + 1], 3)
            spread[j, b] = sp
            pool = jnp.where(row8 == b, jnp.mean(sp, axis=0, keepdims=True), pool)
        pooled[j] = pool
        term = mm_nt(low(pool), flat(W["Gi"][j]))
        gs_part = term if gs_part is None else gs_part + term
    gsb[3] = gs_part
    share_start("gs", gsb)
    line_step("n2", n2_all, 2)

    relay4("F1")
    line_step("n2", n2_all, 3)
    for j in range(2):
        act, der = gelu_pair(mm(flat(n2_all[...]), flat(W["F1"][j])))
        u[j] = low(act)
        up[j] = low(der)

    scatter_wait("gs", gsb)

    def gate_hidden():
        return gelu_pair((gsb[0] + gsb[1]) + (gsb[2] + gsb[3]))

    gh, _ = gate_hidden()
    for j in range(2):
        g8 = jnp.tanh(mm(low(gh), flat(W["Go"][j])))
        gate[j] = g8
        for b in range(Z):
            br_sb[b, :, j * adq : (j + 1) * adq] = low(g8[b : b + 1] * spread[j, b])
    scatter_start("br", br_sb, br_rb)
    relay4("F2")

    u_both = side_by_side([u[0], u[1]])

    @pl.loop(0, Z // 2)
    def _(pair):
        halves = [
            side_by_side([W["F2"][j, 2 * pair + dz_, rr] for dz_ in range(2) for rr in range(R)])
            for j in range(2)
        ]
        acc = mm(u_both, jnp.concatenate(halves, axis=0))
        m_sb[:, :, lanes_of(pair, 2 * dz)] = low(acc).reshape(Z, TOK, 2 * dz)

    sum_start("m", m_sb, m_rb)

    def exchange(n, buf):
        remote(buf.at[x], buf.at[x], xo_send.at[n], xo_recv.at[n], over_x).start()

    def layer_output(total):
        sum_step("m", m_sb, m_rb, 2)
        scatter_wait("br", br_rb)
        total[...] = x1[...]
        for d in range(Z):
            piece = br_sb[zi] if d == 0 else br_rb[d - 1]
            for j in range(2):
                lanes = pl.ds(pl.multiple_of(j * adh + zfrom(d) * adq, LANE), adq)
                total[:, lanes] += wide(piece[:, j * adq : (j + 1) * adq])
        sum_step("m", m_sb, m_rb, 1)
        sum_wait("m", m_rb)
        hid_tok[x] = low(total[...] + summed(m_sb, m_rb))

    @pl.when(p == 0)
    def _():
        layer_output(dx1)
        remote(hid_tok.at[x], x_in, h_send.at[0], h_recv.at[0], sib).start()
        exchange(0, hid_tok)

    exchange(1, hid_grid)
    relay_sent()

    def over_cores(d):
        return remote(
            out_gtok.at[x], dx3_all.at[zi], b_send.at[d], b_recv.at[d], dev(zto(d), pp=1 - p)
        )

    @pl.when(p == 0)
    def _():
        for d in range(Z):
            slot = dx3_all.at[zfrom(d)]
            remote(slot, slot, b_send.at[d], b_recv.at[d], sib).wait_recv()
        dx3[...] = dx3_all[zi]

    def own_lanes(j):
        return pl.ds(pl.multiple_of(j * adh + zi * adq, LANE), adq)

    gh, ghp = gate_hidden()
    dgh_part = None
    dgp = []
    for j in range(2):
        dgate = jnp.zeros((8, adq), F32)
        for b in range(Z):
            dbr = wide(dx3_all[b, :, own_lanes(j)])
            dgate = jnp.where(row8 == b, jnp.sum(dbr * spread[j, b], axis=0, keepdims=True), dgate)
        dg8 = low(dgate * (1.0 - gate[j] * gate[j]))
        dgp.append(dg8)
        term = mm_nt(dg8, flat(W["Go"][j]))
        dgh_part = term if dgh_part is None else dgh_part + term
    dgb[3] = dgh_part
    share_start("dgh", dgb)

    for j in range(2):
        cols = side_by_side([W["F2"][j, z, rr] for z in range(Z) for rr in range(R)])
        dh[j] = low(mm_nt(flat(dx3_all[...]), cols) * wide(up[j]))

    scatter_wait("dgh", dgb)
    dgs = low(((dgb[0] + dgb[1]) + (dgb[2] + dgb[3])) * ghp)
    for j in range(2):
        dpool = mm(dgs, flat(W["Gi"][j])) * (1.0 / TOK)
        taps = aq[j]
        tap_rows = [None] * 9
        for b in range(Z):
            dsp = gate[j, b : b + 1] * wide(dx3_all[b, :, own_lanes(j)]) + dpool[b : b + 1]
            dad[j, b * TOK : (b + 1) * TOK] = low(depthwise(dsp, lambda k: taps[8 - k : 9 - k], 3))

            def put(k, row):
                tap_rows[k] = row if tap_rows[k] is None else tap_rows[k] + row

            depthwise_taps(adapted[j, b * TOK : (b + 1) * TOK], dsp, 3, put)
        for k in range(9):
            gad[j, k : k + 1] = tap_rows[k]
        gad[j, 9:16] = jnp.zeros((7, adq), F32)

    pair_out(dad, "E", dc2_sb, cz)

    sum_start("dc2", dc2_sb, dc2_rb)

    pair_out(dh, "F1", dn2_sb, dz)

    sum_start("dn2", dn2_sb, dn2_rb)
    sum_step("dc2", dc2_sb, dc2_rb, 2)

    def half_rows(name, upper):
        half = W[name].shape[-2] // 2
        rows = slice(half, None) if upper else slice(0, half)
        return (slice(None), rows) if len(W[name].shape) == 6 else (rows,)

    fine = ("P1", "P2")

    def pieces(name):
        return (1, 2, 3, 0) if name in fine else (None,)

    def block_at(d):
        return slice(None) if d is None else zto(d)

    def hop_copy(name, which, d):
        n = ids[name]
        lower, upper = half_rows(name, False), half_rows(name, True)
        z = block_at(d)
        w, buf = W[name], RX[name]
        src, dst, to = (
            lambda: (w.at[(xo, z, slice(None)) + lower], buf[0].at[z], over_x),
            lambda: (w.at[(slice(None), z, ro) + upper], buf[1].at[:, z], over_r),
            lambda: (buf[0].at[z, ro], buf[2].at[z], over_r),
            lambda: (buf[1].at[xo, z], buf[3].at[z], over_x),
        )[which]()
        k = 0 if d is None else d
        return remote(src, dst, g_send.at[n, which, k], g_recv.at[n, which, k], to)

    def reduce_start(name, d=None):
        hop_copy(name, 0, d).start()
        hop_copy(name, 1, d).start()

    def each_block(d, body):
        if d is None:
            pl.loop(0, Z)(body)
        else:
            body(zto(d))

    def per_piece(name, body):
        if name in fine:
            pl.loop(0, Z)(lambda k: body(lax.rem(k + 1, Z)))
        else:
            body(None)

    def reduce_middle(*names):
        for name in names:
            lower, upper = half_rows(name, False), half_rows(name, True)
            buf = RX[name]

            def middle(d):
                hop_copy(name, 0, d).wait_recv()

                def add_lower(z):
                    for rr in range(R):
                        own = W[name][(x, z, rr) + lower]
                        buf[0][z, rr] = low(wide(own) + wide(buf[0][z, rr]))

                each_block(d, add_lower)
                hop_copy(name, 2, d).start()
                hop_copy(name, 1, d).wait_recv()

                def add_upper(z):
                    for j in range(2):
                        own = W[name][(j, z, ri) + upper]
                        buf[1][j, z] = low(wide(own) + wide(buf[1][j, z]))

                each_block(d, add_upper)
                hop_copy(name, 3, d).start()

            per_piece(name, middle)

    def reduce_end(*names):
        for name in names:
            lower, upper = half_rows(name, False), half_rows(name, True)
            buf = RX[name]

            def end(d):
                hop_copy(name, 2, d).wait_recv()
                hop_copy(name, 3, d).wait_recv()

                def add_both(z):
                    W[name][(x, z, ri) + lower] = low(wide(buf[0][z, ri]) + wide(buf[2][z]))
                    W[name][(x, z, ri) + upper] = low(wide(buf[1][x, z]) + wide(buf[3][z]))

                each_block(d, add_both)

            if name in fine:

                @pl.loop(1, Z)
                def _(d):
                    end(d)
                    back_copy(name, d).start()

                end(0)
            else:
                end(None)
                for d in range(1, Z):
                    back_copy(name, d).start()
            back_local(name).start()

    def back_copy(name, d):
        n = ids[name]
        return remote(
            W[name].at[x, zto(d), ri], quarter_of(name, native[name], zi),
            a_send.at[n, d - 1], a_recv.at[n, d - 1], dev(zto(d)),
        )

    def back_local(name):
        return pltpu.make_async_copy(
            W[name].at[x, zi, ri], quarter_of(name, native[name], zi), loc_sem.at[ids[name]]
        )

    peers = ((1, 0), (0, 1), (1, 1))

    def owner(k):
        return (ro if peers[k][0] else ri), (xo if peers[k][1] else x)

    def row_grad(name, left, right):
        width = W[name].shape[3]
        span = R * width

        @pl.loop(0, Z)
        def _(k):
            d = lax.rem(k + 1, Z)
            z = zto(d)
            turned[0:span] = flat(left[:, :, lanes_of(z, span)]).T
            for j in range(2):
                W[name][j, z] = low(mm(turned[0:span], right[j])).reshape(R, width, -1)
            if name in fine:
                reduce_start(name, d)

        if name not in fine:
            reduce_start(name)

    def col_grad(name, left, right):
        width = left.shape[2]
        for j in range(2):
            turned[j * width : (j + 1) * width] = left[j].T

        @pl.loop(0, Z)
        def _(z):
            rhs = flat(right[:, :, lanes_of(z, dz)])
            for j in range(2):
                g = low(mm(turned[j * width : (j + 1) * width], rhs))
                for rr in range(R):
                    W[name][j, z, rr] = g[:, rr * LANE : (rr + 1) * LANE]

        reduce_start(name)

    for j in range(2):
        W["Gi"][j] = low(mm_tn(dgs, low(pooled[j]))).reshape(Z, R, -1, adq)
        W["Go"][j] = low(mm_tn(low(gh), dgp[j])).reshape(Z, R, -1, adq)
    sum_step("dc2", dc2_sb, dc2_rb, 1)
    sum_step("dn2", dn2_sb, dn2_rb, 2)
    reduce_start("Gi")
    reduce_start("Go")
    row_grad("E", c2_all, dad)
    sum_step("dn2", dn2_sb, dn2_rb, 1)

    @pl.when(p == 0)
    def _():
        remote(dcot, dcot, c_send, c_recv, sib).wait_recv()

    sum_wait("dc2", dc2_rb)
    dc2t[...] = wide(dcot[...]) + summed(dc2_sb, dc2_rb)
    gvs_ls = jnp.sum(cv_sum[...] * dc2t[...], axis=0, keepdims=True)
    dcv_all[zi] = low(dc2t[...] * gain_c(50))
    line_start("dcv", dcv_all)

    sum_wait("dn2", dn2_rb)
    dn2 = summed(dn2_sb, dn2_rb)
    n_hat, rs = normed(x1[...])
    gvs_d1 = jnp.sum(dn2 * n_hat, axis=0, keepdims=True)
    dx1[...] = wide(dx3[...]) + norm_back(dn2, n_hat, rs, gain_d(1))
    dx1_all[zi] = low(dx1[...])
    line_start("dx1", dx1_all)
    line_step("dcv", dcv_all, 1)
    col_grad("F2", u, dx3_all)
    line_step("dcv", dcv_all, 2)
    line_step("dx1", dx1_all, 1)
    row_grad("F1", n2_all, dh)

    line_step("dcv", dcv_all, 3)
    line_step("dx1", dx1_all, 2)
    for j in range(2):
        dhc[j] = low(mm(flat(dcv_all[...]), flat(W["P2"][j])) * wide(rp[j]))

    pair_out(dhc, "P1", df_sb, cz)

    sum_start("df", df_sb, df_rb)

    early = ("Gi", "Go", "E", "F2", "F1")

    def pw_grads():
        row_grad("P2", dcv_all, r)
        row_grad("P1", f_all, dhc)

    line_step("dx1", dx1_all, 3)

    @pl.when(p == 0)
    def _():
        pw_grads()

    sum_step("df", df_sb, df_rb, 2)

    out_rows = [
        side_by_side([W["O"][j, z, rr] for z in range(Z) for rr in range(R)]) for j in range(2)
    ]
    do_both = low(mm_nt(flat(dx1_all[...]), jnp.concatenate(out_rows, axis=0)))
    for j in range(2):
        do_all[j] = do_both[:, j * hq : (j + 1) * hq]
    @pl.loop(0, Z)
    def _(b):
        rows = lanes_of(b, TOK)
        for j in range(2):
            parts = [[], [], []]
            for h in range(hq // HD):
                q, kk, vals = (qkv[j, rows, s * hq + h * HD : s * hq + (h + 1) * HD] for s in range(3))
                do = do_all[j, rows, h * HD : (h + 1) * HD]
                pr = prob[j, h, b]
                dp = mm_nt(do, vals)
                prw = wide(pr)
                ds = low(prw * (dp - jnp.sum(dp * prw, axis=-1, keepdims=True)) * HD ** (-0.5))
                parts[0].append(mm(ds, kk))
                parts[1].append(mm_tn(ds, q))
                parts[2].append(mm_tn(pr, do))
            for s in range(3):
                dqkv[j, rows, s * hq : (s + 1) * hq] = low(side_by_side(parts[s]))

    dqkv_both = side_by_side([dqkv[0], dqkv[1]])

    @pl.loop(0, Z // 2)
    def _(pair):
        zs = pl.ds(pair * 2, 2)
        rows_q = side_by_side([flat(W["Q"][j, zs, :, s]) for j in range(2) for s in range(3)])
        acc = mm_nt(dqkv_both, rows_q)
        dn1_sb[:, :, lanes_of(pair, 2 * dz)] = low(acc).reshape(Z, TOK, 2 * dz)

    sum_start("dn1", dn1_sb, dn1_rb)
    sum_step("df", df_sb, df_rb, 1)

    @pl.when(p == 0)
    def _():
        reduce_middle("Gi", "Go", "E")


    def attention_grads():
        @pl.loop(0, Z)
        def _(z):
            turned[0:dz] = flat(n1_all[:, :, lanes_of(z, dz)]).T
            for j in range(2):
                g = low(mm(turned[0:dz], dqkv[j]))
                for s in range(3):
                    W["Q"][j, z, :, s] = g[:, s * hq : (s + 1) * hq].reshape(R, -1, hq)

        reduce_start("Q")
        col_grad("O", ctx, dx1_all)

    sum_step("dn1", dn1_sb, dn1_rb, 2)

    @pl.when(p == 0)
    def _():
        reduce_middle("F2", "F1")

    sum_step("dn1", dn1_sb, dn1_rb, 1)

    @pl.when(p == 0)
    def _():
        reduce_middle("P2")
        attention_grads()
        reduce_middle("P1")
        reduce_end(*early)

    sum_wait("dn1", dn1_rb)
    dn1 = summed(dn1_sb, dn1_rb)
    n_hat, rs = normed(wide(x_in[...]))
    gvs_d0 = jnp.sum(dn1 * n_hat, axis=0, keepdims=True)
    out_gtok[x] = low(dx1[...] + norm_back(dn1, n_hat, rs, gain_d(0)))

    @pl.when(p == 1)
    def _():
        for d in (1, 2, 3, 0):
            over_cores(d).start()

    sum_wait("df", df_rb)
    dfv = summed(df_sb, df_rb)
    gvs_lc = jnp.sum(dfv * cn[...], axis=0, keepdims=True)
    dcn[...] = norm_back(dfv, cn[...], crs[:, 0:1], gain_c(49))

    @pl.loop(0, c_dim // LANE)
    def _(ch):
        lanes = lanes_of(ch, LANE)
        taps = vec_c[:, lanes]
        back = depthwise(dcn[:, lanes], lambda k: taps[48 - k : 49 - k], 7)
        out_ggrid[x, :, lanes] = low(dc2t[:, lanes] + back)

    @pl.when(p == 1)
    def _():
        remote(out_ggrid.at[x], dcot, c_send, c_recv, sib).start()
        reduce_middle(*early)
        pw_grads()
        attention_grads()
        layer_output(dx1)
        exchange(0, hid_tok)
        reduce_end(*early)

    @pl.when(p == 0)
    def _():
        reduce_end("P2")
        reduce_middle("Q", "O")

    exchange(2, out_gtok)
    exchange(3, out_ggrid)

    @pl.loop(0, Z)
    def _(z):
        for part in range(cz // LANE):
            lanes = pl.ds(pl.multiple_of(z * cz + part * LANE, LANE), LANE)

            def put(k, row):
                gvs[z, k : k + 1, part * LANE : (part + 1) * LANE] = row

            depthwise_taps(wide(c_in[:, lanes]), dcn[:, lanes], 7, put)

    for z in range(Z):
        gvs[z, 49:50] = gvs_lc[:, z * cz : (z + 1) * cz]
        gvs[z, 50:51] = gvs_ls[:, z * cz : (z + 1) * cz]
        gvs[z, 51:64] = jnp.zeros((13, cz), F32)
        gvs[z, 56:57, 0:dz] = gvs_d0[:, z * dz : (z + 1) * dz]
        gvs[z, 57:58, 0:dz] = gvs_d1[:, z * dz : (z + 1) * dz]
    gvs_low[...] = low(gvs[...])
    scatter_start("gv", gvs_low, gv_rb)

    def group_copy(n, k, src, dst):
        rr, xx = owner(k)
        return remote(src, dst, gx_send.at[n, k], gx_recv.at[n, k], dev(rr=rr, xx=xx))

    for k in range(3):
        c = group_copy(1, k, gad, gad_rb.at[k])
        c.start()
        sent.append(c)
    @pl.when(p == 1)
    def _():
        reduce_middle("P2", "P1", "Q", "O")
        reduce_end("P2")

    scatter_wait("gv", gv_rb)
    gvx[3] = (gvs[zi] + wide(gv_rb[0])) + (wide(gv_rb[1]) + wide(gv_rb[2]))
    for k in range(3):
        c = group_copy(0, k, gvx.at[3], gvx.at[k])
        c.start()
        sent.append(c)
    reduce_end("P1")
    for k in range(3):
        group_copy(1, k, gad, gad_rb.at[k]).wait_recv()
    gad_all[zi] = (gad[x] + gad_rb[0, x]) + (gad_rb[1, x] + gad_rb[2, x])
    gather_start("gad", gad_all)
    reduce_end("Q", "O")

    for k in range(3):
        group_copy(0, k, gvx.at[k], gvx.at[k]).wait_recv()
    total = (gvx[0] + gvx[1]) + (gvx[2] + gvx[3])
    mine = jnp.where(ri == 1, pltpu.roll(total, c_own, 1), total)[:, 0:c_own]
    mine_d = jnp.where(ri == 1, total[:, LANE : 2 * LANE], total[:, 0:LANE])

    def flag(n):
        return train_in[0, n].astype(F32)

    out_depth[...] = mine[0:taps7] * flag(0)
    out_ln_conv[...] = mine[49:50] * flag(1)
    out_scale[...] = mine[50:51] * flag(4)
    out_ln_attn[...] = mine_d[56:57]
    out_ln_mlp[...] = mine_d[57:58]
    gather_wait("gad", gad_all)
    for z in range(Z):
        out_ad[:, z * adq : (z + 1) * adq] = gad_all[z][0:9]
    for name in ARRAYS:
        back_local(name).wait()
        for d in range(1, Z):
            n = ids[name]
            slot = quarter_of(name, native[name], zfrom(d))
            remote(slot, slot, a_send.at[n, d - 1], a_recv.at[n, d - 1], dev(zto(d))).wait_recv()
    for n, buf in enumerate((hid_tok, hid_grid, out_gtok, out_ggrid)):
        c = remote(buf.at[x], buf.at[x], xo_send.at[n], xo_recv.at[n], over_x)
        c.wait_send()
        remote(buf.at[xo], buf.at[xo], xo_send.at[n], xo_recv.at[n], over_x).wait_recv()

    @pl.when(p == 0)
    def _():
        remote(hid_tok.at[x], x_in, h_send.at[0], h_recv.at[0], sib).wait_send()
        remote(hid_grid.at[x], c_in, h_send.at[1], h_recv.at[1], sib).wait_send()

    @pl.when(p == 1)
    def _():
        for d in range(Z):
            over_cores(d).wait_send()
        remote(out_ggrid.at[x], dcot, c_send, c_recv, sib).wait_send()

    for name, buf in line_gathers:
        line_sent(name, buf)

    @pl.when(p == 1)
    def _():
        line_sent("dx3", dx3_all)

    for name, sb, rb in line_sums:
        sum_sent(name, sb, rb)
    for c in sent:
        c.wait_send()
    for name in ARRAYS:
        for which in range(4):
            for d in pieces(name):
                hop_copy(name, which, d).wait_send()
        for d in range(1, Z):
            back_copy(name, d).wait_send()


def run_layers(weights, vectors, order, train, streams, sizes, outer):
    d_dim, c_dim, hq, ffq, cfq, adw, dg = sizes
    vm = pltpu.VMEM
    blocks = []
    for name, value in zip(ARRAYS, weights):
        if name == "Q":
            blocks.append((3, value.shape[1], hq))
        elif name in ("O", "F2"):
            blocks.append((value.shape[0] // Z, value.shape[1]))
        else:
            blocks.append((value.shape[0], value.shape[1] // Z))
    rows = Z * TOK

    def act(width, count=Z, kind=BF):
        return vm((count, TOK, width), kind)

    def line(width):
        return vm((2, 3, TOK, width), BF)

    scratch = [vm((2, Z, R) + s, BF) for s in blocks] + [
        vm(lead + s[:-2] + (s[-2] // 2, s[-1]), BF)
        for s in blocks
        for lead in ((Z, R), (2, Z), (Z,), (Z,))
    ]
    scratch += [
        vm((64, 2 * LANE), F32), vm((64, 2 * LANE), BF), vm((Z * R, 64, 2 * LANE), BF), vm((2, 16, adw), F32), vm((64, c_dim), F32), vm((8, d_dim), F32),
        vm((TOK, d_dim), BF), vm((TOK, c_dim), BF), act(d_dim), act(c_dim), act(d_dim), act(c_dim),
        act(d_dim), line(d_dim), act(c_dim), line(c_dim), act(d_dim), line(d_dim),
        act(2 * adw), act(2 * adw, 3), vm((4, 8, dg), F32), vm((4, 8, dg), F32),
        vm((2, rows, 3 * hq), BF), vm((2, hq // HD, Z, TOK, TOK), BF), vm((2, rows, hq), BF),
        vm((2, rows, ffq), BF), vm((2, rows, ffq), BF), vm((2, rows, cfq), BF), vm((2, rows, cfq), BF),
        vm((TOK, c_dim), F32), vm((TOK, LANE), F32), vm((TOK, c_dim), F32), vm((TOK, d_dim), F32), vm((TOK, c_dim), F32),
        vm((2, rows, adw), F32), vm((2, Z, TOK, adw), F32), vm((2, 8, adw), F32), vm((2, 8, adw), F32),
        vm((TOK, d_dim), BF), vm((TOK, c_dim), BF), act(d_dim), act(d_dim), line(d_dim), act(c_dim), line(c_dim),
        act(d_dim), act(c_dim),
        act(d_dim), line(d_dim), act(c_dim), line(c_dim), vm((2, rows, ffq), BF), vm((2, rows, hq), BF),
        vm((2, rows, 3 * hq), BF), vm((2, rows, cfq), BF), vm((TOK, d_dim), F32), vm((TOK, c_dim), F32), vm((2, rows, adw), BF),
        vm((TOK, c_dim), F32),
        vm((Z, 64, c_dim // Z), F32), vm((Z, 64, c_dim // Z), BF), vm((3, 64, c_dim // Z), BF), vm((4, 64, c_dim // Z), F32),
        vm((2, 16, adw), F32), vm((3, 2, 16, adw), F32), vm((Z, 16, adw), F32),
        vm((2 * ffq, rows), BF),
    ]
    dma = pltpu.SemaphoreType.DMA
    na = len(ARRAYS)
    scratch += [
        dma((len(EVENTS), 3)), dma((len(EVENTS), 3)), dma((len(EVENTS), 6)), dma((len(EVENTS), 6)), dma((na, 3)), dma((na, 3)), dma((na,)),
        dma((na, 4, Z)), dma((na, 4, Z)), dma((7,)), dma((7,)), dma, dma, dma((2,)), dma((2,)), dma((Z,)), dma((Z,)), dma, dma,
        dma((4,)), dma((4,)), dma((na, 4, Z)), dma((na, 4, Z)), dma((na, 3)), dma((na, 3)), dma((2, 3)), dma((2, 3)),
        pltpu.SemaphoreType.REGULAR,
    ]
    sds = jax.ShapeDtypeStruct
    out_shape = [sds((2, TOK, d_dim), BF), sds((2, TOK, c_dim), BF)] * 2
    out_shape += [sds(value.shape, BF) for value in weights]
    out_shape += [sds(value.shape, F32) for value in vectors]
    any_spec = pl.BlockSpec(memory_space=pl.ANY)
    vm_spec = pl.BlockSpec(memory_space=pltpu.VMEM)
    sm_spec = pl.BlockSpec(memory_space=pltpu.SMEM)
    return pl.pallas_call(
        functools.partial(main_kernel, sizes, outer),
        out_shape=out_shape,
        in_specs=[any_spec] * na + [vm_spec] * 6 + [sm_spec] * 2 + [vm_spec] * 4,
        out_specs=[vm_spec] * 4 + [any_spec] * na + [vm_spec] * 6,
        scratch_shapes=scratch,
        compiler_params=pltpu.CompilerParams(
            collective_id=0, has_side_effects=True, vmem_limit_bytes=62 * 1024 * 1024
        ),
        cost_estimate=pl.CostEstimate(flops=26 * 10**9, bytes_accessed=10**8, transcendentals=10**7),
        name="layers",
    )(*weights, *vectors, order, train, *streams)


def finish_kernel(flagged, layer_zero, count, *refs):
    grads, streams, vectors = refs[:count], refs[count : count + 4], refs[count + 4 : count + 10]
    order, train = refs[count + 10 : count + 12]
    refs = refs[count + 12 :]
    out_grads, out_streams, out_vectors = refs[:count], refs[count : count + 4], refs[count + 4 : count + 10]
    refs = refs[count + 10 :]
    held, wide_ones = refs[:count], refs[count : 2 * count]
    in_sem, out_sem = refs[2 * count :]

    def fetch(n):
        return pltpu.make_async_copy(grads[n], held[n], in_sem.at[n])

    def put_back(n):
        return pltpu.make_async_copy(wide_ones[n], out_grads[n], out_sem.at[n])

    for n in range(count):
        fetch(n).start()
    swap = (lax.axis_index("pipe") == layer_zero) & (order[0, 0] == 1)
    for n, (src, dst) in enumerate(zip(streams, out_streams)):
        for m in range(2):
            dst[m] = src[m] if n < 2 else jnp.where(swap, src[1 - m], src[m])
    for src, dst in zip(vectors, out_vectors):
        if len(dst.shape) == 3:
            for row in range(dst.shape[0]):
                dst[row] = src[row : row + 1]
        else:
            dst[...] = src[...]
    for n in range(count):
        fetch(n).wait()
        src, dst = held[n], wide_ones[n]
        scale = train[0, flagged[n]].astype(F32) if n in flagged else None
        lead = src.shape[0] if len(src.shape) == 3 else 1

        @pl.loop(0, lead * (src.shape[-2] // 16))
        def _(step):
            rows = pl.ds(pl.multiple_of((step // lead) * 16, 16), 16)
            at = (step % lead, rows) if len(src.shape) == 3 else (rows,)
            value = wide(src[at])
            dst[at] = value if scale is None else value * scale

        put_back(n).start()
    for n in range(count):
        put_back(n).wait()


def finish(outs, order, train):
    count = len(ARRAYS)
    streams, grads, vectors = outs[:4], outs[4 : 4 + count], outs[4 + count :]
    any_spec = pl.BlockSpec(memory_space=pl.ANY)
    sm_spec = pl.BlockSpec(memory_space=pltpu.SMEM)
    vm_spec = pl.BlockSpec(memory_space=pltpu.VMEM)
    sds = jax.ShapeDtypeStruct
    dma = pltpu.SemaphoreType.DMA
    flagged = {ARRAYS.index("P1"): 2, ARRAYS.index("P2"): 3}
    return pl.pallas_call(
        functools.partial(finish_kernel, flagged, 0, count),
        out_shape=[sds(g.shape, F32) for g in grads]
        + [sds(value.shape, value.dtype) for value in streams]
        + [sds(value.shape if value.shape[0] == 1 else (value.shape[0], 1, value.shape[1]), F32) for value in vectors],
        in_specs=[any_spec] * count + [vm_spec] * 10 + [sm_spec] * 2,
        out_specs=[any_spec] * count + [vm_spec] * 10,
        scratch_shapes=[pltpu.VMEM(g.shape, BF) for g in grads]
        + [pltpu.VMEM(g.shape, F32) for g in grads]
        + [dma((count,)), dma((count,))],
        compiler_params=pltpu.CompilerParams(vmem_limit_bytes=62 * 1024 * 1024),
        name="finish",
    )(*grads, *streams, *vectors, order, train)


def per_device(
    tokens,
    conv_grid,
    order,
    trainable,
    ln_attn,
    w_qkv,
    w_attn_out,
    ln_mlp,
    w_fc_in,
    w_fc_out,
    conv_depth,
    ln_conv,
    w_pw_in,
    w_pw_out,
    layer_scale,
    w_adapt,
    adapt_depth,
    w_gate_in,
    w_gate_out,
    tok_cot,
    grid_cot,
):
    dp_count = lax.axis_size("dp")
    outer = dp_count // (Z * R)
    groups = [[g * outer + o for o in range(outer)] for g in range(Z * R)]

    def block(value, axis):
        value = value[0]
        if outer == 1:
            return value
        return lax.all_gather(value, "dp", axis=axis, tiled=True, axis_index_groups=groups)

    def share(value, axis):
        if outer > 1:
            value = lax.psum_scatter(
                value, "dp", scatter_dimension=axis, tiled=True, axis_index_groups=groups
            )
        return value[None]

    qkv = block(w_qkv, 1)
    gate_in = block(w_gate_in, 1).T
    pw_in = block(w_pw_in, 0)
    adapt = block(w_adapt, 0)
    fc_in = block(w_fc_in, 0)
    weights = (
        pw_in,
        block(w_pw_out, 1).T,
        qkv,
        block(w_attn_out, 1),
        adapt,
        gate_in,
        block(w_gate_out, 0),
        fc_in,
        block(w_fc_out, 1),
    )
    vectors = (
        block(conv_depth, 1),
        block(ln_conv, 0)[None],
        block(layer_scale, 0)[None],
        block(ln_attn, 0)[None],
        block(ln_mlp, 0)[None],
        adapt_depth[0],
    )
    spread = Z * R
    sizes = (
        qkv.shape[1] * spread, pw_in.shape[0] * spread, qkv.shape[2] // Z, fc_in.shape[1] // Z,
        pw_in.shape[1] // Z, adapt.shape[1] // Z, gate_in.shape[0] * spread,
    )

    def rows_of(value):
        return value.reshape(value.shape[0], TOK, value.shape[-1])

    streams = [rows_of(value) for value in (tokens, conv_grid, tok_cot, grid_cot)]
    outs = run_layers(weights, vectors, order, trainable, streams, sizes, outer)
    done = finish(outs, order, trainable)
    g_p1, g_p2, g_q, g_o, g_e, g_gi, g_go, g_f1, g_f2 = done[:9]
    hid_tok, hid_grid, g_tok, g_grid = done[9:13]
    g_depth, g_ln_conv, g_scale, g_ln_attn, g_ln_mlp, g_ad = done[13:]
    grid_shape = (1,) + conv_grid.shape
    tok_shape = (1,) + tokens.shape
    g_depth, g_ad = g_depth[:, 0], g_ad[:, 0]
    if outer > 1:
        g_ad = lax.psum(g_ad, "dp", axis_index_groups=groups)
    return (
        hid_tok.reshape(tok_shape),
        hid_grid.reshape(grid_shape),
        g_tok.reshape(tok_shape),
        g_grid.reshape(grid_shape),
        share(g_ln_attn[0], 0),
        share(g_q, 1),
        share(g_o, 1),
        share(g_ln_mlp[0], 0),
        share(g_f1, 0),
        share(g_f2, 1),
        share(g_depth, 1),
        share(g_ln_conv[0], 0),
        share(g_p1, 0),
        share(g_p2.T, 1),
        share(g_scale[0], 0),
        share(g_e, 0),
        g_ad[None],
        share(g_gi.T, 1),
        share(g_go, 0),
    )


def solution(mesh):
    in_specs = (
        P(None, "dp", None, None),
        P(None, "dp", None, None, None),
        P("dp", None),
        P("pipe", None),
        P("pipe", "dp"),
        P("pipe", None, "dp", "tensor"),
        P("pipe", "tensor", "dp"),
        P("pipe", "dp"),
        P("pipe", "dp", "tensor"),
        P("pipe", "tensor", "dp"),
        P("pipe", None, "dp"),
        P("pipe", "dp"),
        P("pipe", "dp", "tensor"),
        P("pipe", "tensor", "dp"),
        P("pipe", "dp"),
        P("pipe", "dp", "tensor"),
        P("pipe", None, "tensor"),
        P("pipe", "tensor", "dp"),
        P("pipe", "dp", "tensor"),
        P(None, "dp", None, None),
        P(None, "dp", None, None, None),
    )
    out_specs = (
        P("pipe", None, "dp", None, None),
        P("pipe", None, "dp", None, None, None),
        P("pipe", None, "dp", None, None),
        P("pipe", None, "dp", None, None, None),
        P("pipe", "dp"),
        P("pipe", None, "dp", "tensor"),
        P("pipe", "tensor", "dp"),
        P("pipe", "dp"),
        P("pipe", "dp", "tensor"),
        P("pipe", "tensor", "dp"),
        P("pipe", None, "dp"),
        P("pipe", "dp"),
        P("pipe", "dp", "tensor"),
        P("pipe", "tensor", "dp"),
        P("pipe", "dp"),
        P("pipe", "dp", "tensor"),
        P("pipe", None, "tensor"),
        P("pipe", "tensor", "dp"),
        P("pipe", "dp", "tensor"),
    )
    return jax.shard_map(
        per_device, mesh=mesh, in_specs=in_specs, out_specs=out_specs, check_vma=False
    )
```

```python
import functools

import jax
import jax.numpy as jnp
from jax import lax
from jax.experimental import pallas as pl
from jax.experimental.pallas import tpu as pltpu
from jax.sharding import PartitionSpec as P

HD = 64
Z = 4
R = 2
TOK = 64
SIDE = 8
LANE = 128
BF = jnp.bfloat16
F32 = jnp.float32
ARRAYS = ("P1", "P2", "Q", "O", "E", "Gi", "Go", "F1", "F2")
EVENTS = (
    "n1", "f", "o", "cv", "n2", "c2", "m", "br", "gs",
    "dx3", "dgh", "dn2", "dc2", "dx1", "dcv", "dn1", "df", "gv", "gad",
)


def mm(a, b):
    return lax.dot_general(a, b, (((1,), (0,)), ((), ())), preferred_element_type=F32)


def mm_nt(a, b):
    return lax.dot_general(a, b, (((1,), (1,)), ((), ())), preferred_element_type=F32)


def mm_tn(a, b):
    return lax.dot_general(a, b, (((0,), (0,)), ((), ())), preferred_element_type=F32)


def flat(value):
    return value.reshape(-1, value.shape[-1])


def low(value):
    return value.astype(BF)


def wide(value):
    return value.astype(F32)


def gelu_pair(h):
    phi = 0.5 * (1.0 + lax.erf(h * 0.7071067811865476))
    dens = jnp.exp(-0.5 * h * h) * 0.3989422804014327
    return h * phi, phi + h * dens


def normed(value):
    centred = value - jnp.mean(value, axis=-1, keepdims=True)
    rs = lax.rsqrt(jnp.mean(centred * centred, axis=-1, keepdims=True) + 1e-06)
    return centred * rs, rs


def norm_back(dn, n_hat, rs, gain):
    gd = dn * gain
    return (
        gd
        - jnp.mean(gd, axis=-1, keepdims=True)
        - n_hat * jnp.mean(gd * n_hat, axis=-1, keepdims=True)
    ) * rs


def col_shift(value, by):
    if by == 0:
        return value
    at = lax.broadcasted_iota(jnp.int32, value.shape, 0) % SIDE
    rolled = pltpu.roll(value, (-by) % TOK, 0)
    return jnp.where((at + by >= 0) & (at + by < SIDE), rolled, 0.0)


def row_shift(value, by):
    if by == 0:
        return value
    gap = jnp.zeros((abs(by) * SIDE, value.shape[1]), value.dtype)
    if by > 0:
        return jnp.concatenate([value[by * SIDE :], gap], axis=0)
    return jnp.concatenate([gap, value[: TOK + by * SIDE]], axis=0)


def depthwise(value, tap, side):
    half = side // 2
    shifted = [col_shift(value, b - half) for b in range(side)]
    total = None
    for a in range(side):
        line = None
        for b in range(side):
            term = shifted[b] * tap(a * side + b)
            line = term if line is None else line + term
        line = row_shift(line, a - half)
        total = line if total is None else total + line
    return total


def depthwise_taps(value, grad, side, put):
    half = side // 2
    shifted = [col_shift(value, b - half) for b in range(side)]
    for a in range(side):
        d = a - half
        lo, hi = max(0, -d) * SIDE, (SIDE - max(0, d)) * SIDE
        for b in range(side):
            part = shifted[b][lo + d * SIDE : hi + d * SIDE] * grad[lo:hi]
            put(a * side + b, jnp.sum(part, axis=0, keepdims=True))


def lanes_of(at, width):
    return pl.ds(pl.multiple_of(at * width, width), width)


def side_by_side(blocks):
    return jnp.concatenate(blocks, axis=1)


def main_kernel(dims, outer, *refs):
    at = iter(refs)

    def take(count):
        return [next(at) for _ in range(count)]

    na = len(ARRAYS)
    source = dict(zip(ARRAYS, take(na)))
    (
        depth_in, ln_conv_in, scale_in, ln_attn_in, ln_mlp_in, adapt_depth_in,
        order_in, train_in, tok_in, grid_in, tcot_in, gcot_in,
    ) = take(12)
    hid_tok, hid_grid, out_gtok, out_ggrid = take(4)
    native = dict(zip(ARRAYS, take(na)))
    out_depth, out_ln_conv, out_scale, out_ln_attn, out_ln_mlp, out_ad = take(6)
    W = dict(zip(ARRAYS, take(na)))
    hops = take(4 * (na - 1))
    RX = {name: hops[4 * max(n - 1, 0) : 4 * max(n - 1, 0) + 4] for n, name in enumerate(ARRAYS)}
    (
        v_loc, v_low, vv, aq, vec_c, vec_d, x_in, c_in, n1_all, f_all, n2_all, c2_all,
        o_sb, o_rb, cv_sb, cv_rb, m_sb, m_rb, br_sb, br_rb, gsb, dgb,
        qkv, prob, ctx, u, up, r, rp, cn, crs, cv_sum, x1, c2f,
        adapted, spread, pooled, gate,
        dx3, dcot, dx3_all, dn2_sb, dn2_rb, dc2_sb, dc2_rb, dx1_all, dcv_all,
        dn1_sb, dn1_rb, df_sb, df_rb, dh, do_all, dqkv, dhc, dx1, dc2t, dad, dcn,
        gvs, gvs_low, gv_rb, gvx, gad, gad_rb, gad_all, turned, alt_a, alt_b, nat,
    ) = take(70)
    (
        zs_send, zs_recv, l_send, l_recv, s1_send, s1_recv, loc_sem, s2_send, s2_recv,
        v_send, v_recv, q_send, q_recv, h_send, h_recv, b_send, b_recv, c_send, c_recv,
        xo_send, xo_recv, g_send, g_recv, a_send, a_recv, gx_send, gx_recv, go,
        m_send, m_recv, f_sem, f_send, f_recv,
    ) = take(33)

    p = lax.axis_index("pipe")
    dpi = lax.axis_index("dp")
    x = lax.axis_index("tensor")
    rest = dpi % outer
    zi = dpi // (outer * R)
    ri = (dpi // outer) % R
    xo = 1 - x
    ro = 1 - ri
    d_dim, c_dim, hq, ffq, cfq, adq, dg = dims
    adh = Z * adq
    dz, cz = d_dim // Z, c_dim // Z
    tile = 256
    ids = {name: number for number, name in enumerate(ARRAYS)}
    ev = {name: number for number, name in enumerate(EVENTS)}

    def dev(z=None, rr=None, xx=None, pp=None):
        z = zi if z is None else z
        rr = ri if rr is None else rr
        return (
            p if pp is None else pp,
            (z * R + rr) * outer + rest,
            x if xx is None else xx,
        )

    def zto(d):
        return lax.rem(zi + d, Z)

    def zfrom(d):
        return lax.rem(zi + Z - d, Z)

    def remote(src, dst, ssem, rsem, device):
        return pltpu.make_async_remote_copy(
            src_ref=src, dst_ref=dst, send_sem=ssem, recv_sem=rsem,
            device_id=device, device_id_type=pl.DeviceIdType.MESH,
        )

    sib = dev(pp=1 - p)
    over_r, over_x = dev(rr=ro), dev(xx=xo)

    def z_copy(e, d, src, dst):
        return remote(src, dst, zs_send.at[e, d - 1], zs_recv.at[e, d - 1], dev(zto(d)))

    sent = []

    def gather_copies(name, buf):
        return [z_copy(ev[name], d, buf.at[zi], buf.at[zi]) for d in range(1, Z)]

    def gather_start(name, buf, keep=True):
        copies = gather_copies(name, buf)
        for c in copies:
            c.start()
        if keep:
            sent.extend(copies)

    def gather_wait(name, buf):
        for d in range(1, Z):
            slot = buf.at[zfrom(d)]
            z_copy(ev[name], d, slot, slot).wait_recv()

    def scatter_start(name, sb, rb):
        for d in range(1, Z):
            c = z_copy(ev[name], d, sb.at[zto(d)], rb.at[d - 1])
            c.start()
            sent.append(c)

    def scatter_wait(name, rb):
        for d in range(1, Z):
            z_copy(ev[name], d, rb.at[d - 1], rb.at[d - 1]).wait_recv()

    def right():
        return dev(zi + 1)

    def left():
        return dev(zi - 1)

    def pass_copy(name, buf, toward, s):
        e, k = ev[name], (0 if toward > 0 else 3) + s
        blk = buf.at[zi - toward * s]
        return remote(blk, blk, l_send.at[e, k], l_recv.at[e, k], right() if toward > 0 else left())

    def pass_cond(toward, s):
        if toward > 0:
            return (zi < Z - 1) & (zi - s >= 0)
        return (zi > 0) & (zi + s <= Z - 1)

    def line_start(name, buf):
        for toward in (1, -1):

            @pl.when(pass_cond(toward, 0))
            def _():
                pass_copy(name, buf, toward, 0).start()

    def line_step(name, buf, *steps):
        e = ev[name]
        for s in steps:
            for toward in (1, -1):
                src = zi - toward * s

                @pl.when((src >= 0) & (src <= Z - 1))
                def _():
                    blk = buf.at[src]
                    k = (0 if toward > 0 else 3) + s - 1
                    remote(blk, blk, l_send.at[e, k], l_recv.at[e, k], sib).wait_recv()

                if s < Z - 1:

                    @pl.when(pass_cond(toward, s))
                    def _():
                        pass_copy(name, buf, toward, s).start()

    def line_sent(name, buf):
        for toward in (1, -1):
            for s in range(Z - 1):

                @pl.when(pass_cond(toward, s))
                def _():
                    pass_copy(name, buf, toward, s).wait_send()

    def sum_copy(name, sb, rb, toward, k, first):
        e, way = ev[name], (0 if toward > 0 else 1)
        src = sb.at[zi + toward * k] if first else rb.at[way, k]
        q = way * 3 + k - 1
        return remote(src, rb.at[way, k - 1], l_send.at[e, q], l_recv.at[e, q], right() if toward > 0 else left())

    def at_end(toward):
        return zi == (0 if toward > 0 else Z - 1)

    def passes(toward, k):
        dest = zi + toward * k
        return jnp.logical_not(at_end(toward)) & (dest >= 0) & (dest <= Z - 1)

    def sum_start(name, sb, rb):
        for toward in (1, -1):

            @pl.when(at_end(toward))
            def _():
                for k in (3, 2, 1):
                    sum_copy(name, sb, rb, toward, k, True).start()

    def sum_arrival(name, rb, way, k):
        e = ev[name]
        slot = rb.at[way, k]
        return remote(slot, slot, l_send.at[e, way * 3 + k], l_recv.at[e, way * 3 + k], sib)

    def sum_step(name, sb, rb, *ks):
        for k in ks:
            for way, toward in enumerate((1, -1)):

                @pl.when(passes(toward, k))
                def _():
                    sum_arrival(name, rb, way, k).wait_recv()
                    rb[way, k] = low(wide(rb[way, k]) + wide(sb[zi + toward * k]))
                    sum_copy(name, sb, rb, toward, k, False).start()

    def sum_wait(name, rb):
        for way, toward in enumerate((1, -1)):

            @pl.when(jnp.logical_not(at_end(toward)))
            def _():
                sum_arrival(name, rb, way, 0).wait_recv()

    def summed(sb, rb):
        return wide(sb[zi]) + (wide(rb[0, 0]) + wide(rb[1, 0]))

    def sum_sent(name, sb, rb):
        for toward in (1, -1):

            @pl.when(at_end(toward))
            def _():
                for k in (3, 2, 1):
                    sum_copy(name, sb, rb, toward, k, True).wait_send()

            for k in (2, 1):

                @pl.when(passes(toward, k))
                def _():
                    sum_copy(name, sb, rb, toward, k, False).wait_send()

    def share_start(name, buf):
        for d in range(1, Z):
            c = z_copy(ev[name], d, buf.at[3], buf.at[d - 1])
            c.start()
            sent.append(c)

    def scattered(sb, rb):
        return (wide(sb[zi]) + wide(rb[0])) + (wide(rb[1]) + wide(rb[2]))

    barrier = pltpu.get_barrier_semaphore()
    greeted = [sib]
    for d in range(1, Z):
        greeted += [dev(zto(d)), dev(zto(d), ro), dev(zto(d), pp=1 - p)]
    greeted += [over_r, over_x, dev(rr=ro, xx=xo)]
    for device in greeted:
        pl.semaphore_signal(barrier, inc=1, device_id=device, device_id_type=pl.DeviceIdType.MESH)
    v_loc[...] = jnp.zeros(v_loc.shape, F32)
    taps7 = depth_in.shape[0]
    c_own = depth_in.shape[1]
    v_loc[0:taps7, 0:c_own] = wide(depth_in[...])
    v_loc[49:50, 0:c_own] = wide(ln_conv_in[...])
    v_loc[50:51, 0:c_own] = wide(scale_in[...])
    v_loc[56:57, 0:LANE] = wide(ln_attn_in[...])
    v_loc[57:58, 0:LANE] = wide(ln_mlp_in[...])
    aq[x] = jnp.zeros(aq.shape[1:], F32)
    aq[x, 0:9] = wide(adapt_depth_in[:, lanes_of(zi, adq)])
    v_low[...] = low(v_loc[...])
    line_sums = (
        ("o", o_sb, o_rb), ("cv", cv_sb, cv_rb), ("m", m_sb, m_rb), ("dn2", dn2_sb, dn2_rb),
        ("dc2", dc2_sb, dc2_rb), ("dn1", dn1_sb, dn1_rb), ("df", df_sb, df_rb),
    )
    line_gathers = (
        ("n1", n1_all), ("f", f_all), ("n2", n2_all), ("c2", c2_all), ("dx1", dx1_all), ("dcv", dcv_all),
    )
    for _, _, rb in line_sums:
        for way, toward in enumerate((1, -1)):

            @pl.when(at_end(toward))
            def _():
                rb[way, 0] = jnp.zeros(rb.shape[2:], BF)

    pl.semaphore_wait(barrier, len(greeted))

    me8 = zi * R + ri
    v_arrivals = []
    for n, (d, flip) in enumerate([(d, s) for d in range(Z) for s in (0, 1)][1:]):
        tr = ro if flip else ri
        c = remote(v_low, vv.at[me8], v_send.at[n], v_recv.at[n], dev(zto(d), tr))
        c.start()
        sent.append(c)
        fr = zfrom(d) * R + tr
        v_arrivals.append(remote(vv.at[fr], vv.at[fr], v_send.at[n], v_recv.at[n], dev(zto(d), tr)))
    vv[me8] = v_low[...]
    c = remote(aq.at[x], aq.at[x], q_send, q_recv, over_x)
    c.start()
    sent.append(c)

    by_rows = ("O", "F2")

    def quarter_of(name, ref, z):
        if name == "Q":
            return ref.at[:, :, lanes_of(z, hq)]
        if name in by_rows:
            height = ref.shape[0] // Z
            return ref.at[pl.ds(pl.multiple_of(z * height, height), height)]
        return ref.at[:, lanes_of(z, ref.shape[1] // Z)]

    def step1_local(name):
        return pltpu.make_async_copy(
            quarter_of(name, source[name], zi), W[name].at[x, zi, ri], loc_sem.at[ids[name]]
        )

    def step1_copy(name, d):
        k = ids[name]
        return remote(
            quarter_of(name, source[name], zto(d)), W[name].at[x, zi, ri],
            s1_send.at[k, d - 1], s1_recv.at[k, d - 1], dev(zto(d)),
        )

    def half_of(name, j, z, rr, upper):
        w = W[name]
        half = w.shape[-2] // 2
        rows = slice(half, None) if upper else slice(0, half)
        if len(w.shape) == 6:
            return w.at[j, z, rr, :, rows]
        return w.at[j, z, rr, rows]

    def step2_copy(name, which, d):
        k = ids[name]
        z = zfrom(d)
        if which < 2:
            src = quarter_of(name, source[name], zi) if d == 0 else W[name].at[x, z, ri]
            dst = W[name].at[x, z, ri]
        else:
            src = dst = half_of(name, x, z, ro, False) if which == 2 else half_of(name, xo, z, ri, True)
        to = over_x if which in (1, 2) else over_r
        return remote(src, dst, s2_send.at[k, which, d], s2_recv.at[k, which, d], to)

    def step2_arrival(name, which, d):
        k = ids[name]
        z = zfrom(d)
        if which < 2:
            ref = W[name].at[x, z, ro] if which == 0 else W[name].at[xo, z, ri]
        else:
            ref = half_of(name, xo, z, ro, which == 3)
        to = over_x if which in (1, 2) else over_r
        return remote(ref, ref, s2_send.at[k, which, d], s2_recv.at[k, which, d], to)

    def relay1(*names):
        for name in names:
            for d in range(1, Z):
                step1_copy(name, d).start()

    def relay0(*names):
        for name in names:
            step1_local(name).start()
            step2_copy(name, 0, 0).start()
            step2_copy(name, 1, 0).start()

    def relay2(name, ds=(1, 2, 3)):
        k = ids[name]
        for d in ds:
            slot = W[name].at[x, zfrom(d), ri]
            remote(slot, slot, s1_send.at[k, d - 1], s1_recv.at[k, d - 1], dev(zto(d))).wait_recv()
            step2_copy(name, 0, d).start()
            step2_copy(name, 1, d).start()

    def relay3(name, ds=(0, 1, 2, 3)):
        for d in ds:
            step2_arrival(name, 0, d).wait_recv()
            step2_copy(name, 2, d).start()
            step2_arrival(name, 1, d).wait_recv()
            step2_copy(name, 3, d).start()

    def relay4(*names):
        for name in names:
            step1_local(name).wait()
            for d in range(Z):
                step2_arrival(name, 2, d).wait_recv()
                step2_arrival(name, 3, d).wait_recv()

    def relay_sent():
        for name in ARRAYS:
            for d in range(1, Z):
                step1_copy(name, d).wait_send()
            for which in range(4):
                for d in range(Z):
                    step2_copy(name, which, d).wait_send()

    @pl.when(p == 0)
    def _():
        relay0("P1")
        relay1("P1")
        relay0("P2")
        relay1("P2")
        relay0("Q", "O", "E", "Gi", "Go", "F1", "F2")

    @pl.when(p == 1)
    def _():
        dx3[...] = tcot_in[x]
        dcot[...] = gcot_in[x]
        dx3_all[zi] = tcot_in[x]
        line_start("dx3", dx3_all)

    for c in v_arrivals:
        c.wait_recv()
    remote(aq.at[xo], aq.at[xo], q_send, q_recv, over_x).wait_recv()
    low_lanes = lax.broadcasted_iota(jnp.int32, (64, LANE), 1) < LANE // 2
    for z in range(Z):
        first, second = wide(vv[2 * z]), pltpu.roll(wide(vv[2 * z + 1]), LANE // 2, 1)
        vec_c[:, z * cz : z * cz + LANE] = first[:, 0:LANE]
        vec_c[:, z * cz + LANE : z * cz + 2 * LANE] = jnp.where(
            low_lanes, first[:, LANE:], second[:, 0:LANE]
        )
        vec_c[:, z * cz + 2 * LANE : (z + 1) * cz] = second[:, LANE:]
    for i in range(Z * R):
        vec_d[:, i * LANE : (i + 1) * LANE] = wide(vv[i])[56:64, 0:LANE]

    def gain_d(row):
        return vec_d[row : row + 1, :]

    def gain_c(row):
        return vec_c[row : row + 1, :]

    def token_entry():
        n_hat, _ = normed(wide(x_in[...]))
        n1_all[zi] = low(n_hat * gain_d(0))
        line_start("n1", n1_all)

    def conv_entry():
        @pl.loop(0, c_dim // LANE)
        def _(ch):
            lanes = lanes_of(ch, LANE)
            taps = vec_c[:, lanes]
            cn[:, lanes] = depthwise(wide(c_in[:, lanes]), lambda k: taps[k : k + 1], 7)

        n_hat, rs = normed(cn[...])
        cn[...] = n_hat
        crs[...] = jnp.broadcast_to(rs, crs.shape)
        f_all[zi] = low(n_hat * gain_c(49))
        line_start("f", f_all)

    def first_relays(pump):
        relay2("P1")
        pump(1)
        relay1("Q", "O")
        relay2("P2")
        pump(2)
        relay3("P1")


    @pl.when(p == 0)
    def _():
        first = order_in[0, x] == 0
        c_in[...] = jnp.where(first, grid_in[0], grid_in[1])
        x_in[...] = jnp.where(first, tok_in[0], tok_in[1])
        conv_entry()
        token_entry()

        def pump(s):
            line_step("f", f_all, s)
            line_step("n1", n1_all, s)

        first_relays(pump)
        line_step("f", f_all, 3)
        line_step("n1", n1_all, 3)

    @pl.when(p == 1)
    def _():
        pl.semaphore_wait(go, 1)
        relay0("P1")
        relay1("P1")
        relay0("P2")
        relay1("P2")
        relay0("Q", "O", "E", "Gi", "Go", "F1", "F2")
        first_relays(lambda s: line_step("dx3", dx3_all, s))
        remote(c_in, c_in, h_send.at[1], h_recv.at[1], sib).wait_recv()
        conv_entry()
        line_step("dx3", dx3_all, 3)
        line_step("f", f_all, 1)

    relay2("Q")
    relay2("O")
    relay1("E", "Gi", "Go")
    relay3("P2", (0, 1))

    @pl.when(p == 1)
    def _():
        line_step("f", f_all, 2, 3)

    relay4("P1")

    def conv_hidden(j):
        act, der = gelu_pair(mm(flat(f_all[...]), flat(W["P1"][j])))
        r[j] = low(act)
        rp[j] = low(der)

    conv_hidden(0)

    relay3("P2", (2, 3))
    for name in ("E", "Gi", "Go"):
        relay2(name)
    relay1("F1")
    conv_hidden(1)
    relay3("Q")
    relay3("O")
    relay2("F1")
    relay1("F2")

    @pl.when(p == 0)
    def _():
        pl.semaphore_signal(go, inc=1, device_id=sib, device_id_type=pl.DeviceIdType.MESH)

    relay4("P2")

    def pair_rows(name, pair):
        zs = pl.ds(pair * 2, 2)
        return side_by_side([flat(W[name][0, zs]), flat(W[name][1, zs])])

    def pair_out(left, name, sb, width):
        both = side_by_side([left[0], left[1]])

        @pl.loop(0, Z // 2)
        def _(pair):
            acc = mm_nt(both, pair_rows(name, pair))
            sb[:, :, lanes_of(pair, 2 * width)] = low(acc).reshape(Z, TOK, 2 * width)

    pair_out(r, "P2", cv_sb, cz)

    sum_start("cv", cv_sb, cv_rb)

    for name in ("E", "Gi", "Go"):
        relay3(name)
    sum_step("cv", cv_sb, cv_rb, 2)
    relay2("F2")
    sum_step("cv", cv_sb, cv_rb, 1)

    @pl.when(p == 1)
    def _():
        remote(x_in, x_in, h_send.at[0], h_recv.at[0], sib).wait_recv()
        token_entry()
        line_step("n1", n1_all, 1, 2, 3)

    relay4("Q", "O")
    wide_q = side_by_side([flat(W["Q"][j, :, :, s]) for j in range(2) for s in range(3)])
    qkv_both = low(mm(flat(n1_all[...]), wide_q))
    for j in range(2):
        qkv[j] = qkv_both[:, j * 3 * hq : (j + 1) * 3 * hq]
    @pl.loop(0, Z)
    def _(b):
        rows = lanes_of(b, TOK)
        for j in range(2):
            outs = []
            for h in range(hq // HD):
                q, kk, vals = (qkv[j, rows, s * hq + h * HD : s * hq + (h + 1) * HD] for s in range(3))
                sc = mm_nt(q, kk) * HD ** (-0.5)
                e = jnp.exp(sc - jnp.max(sc, axis=-1, keepdims=True))
                pr = low(e / jnp.sum(e, axis=-1, keepdims=True))
                prob[j, h, b] = pr
                outs.append(mm(pr, vals))
            ctx[j, rows, :] = low(side_by_side(outs))

    out_cols = [
        jnp.concatenate([W["O"][0, z, rr], W["O"][1, z, rr]], axis=0) for z in range(Z) for rr in range(R)
    ]
    o_sb[...] = low(mm(side_by_side([ctx[0], ctx[1]]), side_by_side(out_cols))).reshape(Z, TOK, d_dim)
    sum_start("o", o_sb, o_rb)

    relay3("F1")

    sum_wait("cv", cv_rb)
    cv_sum[...] = summed(cv_sb, cv_rb)
    c2f[...] = wide(c_in[...]) + gain_c(50) * cv_sum[...]
    c2_low = low(c2f[...])
    c2_all[zi] = c2_low
    line_start("c2", c2_all)
    sum_step("o", o_sb, o_rb, 2)
    hid_grid[x] = c2_low

    @pl.when(p == 0)
    def _():
        remote(hid_grid.at[x], c_in, h_send.at[1], h_recv.at[1], sib).start()

    relay3("F2")
    sum_step("o", o_sb, o_rb, 1)
    line_step("c2", c2_all, 1)
    sum_wait("o", o_rb)
    x1[...] = wide(x_in[...]) + summed(o_sb, o_rb)
    n_hat, _ = normed(x1[...])
    n2_all[zi] = low(n_hat * gain_d(1))
    line_start("n2", n2_all)

    relay4("E", "Gi", "Go")
    line_step("c2", c2_all, 2)
    line_step("n2", n2_all, 1)
    line_step("c2", c2_all, 3)
    row8 = lax.broadcasted_iota(jnp.int32, (8, adq), 0)
    gs_part = None
    ad_both = mm(flat(c2_all[...]), side_by_side([flat(W["E"][0]), flat(W["E"][1])]))
    for j in range(2):
        ad = ad_both[:, j * adq : (j + 1) * adq]
        adapted[j] = ad
        taps = aq[j]
        pool = jnp.zeros((8, adq), F32)
        for b in range(Z):
            sp = depthwise(ad[b * TOK : (b + 1) * TOK], lambda k: taps[k : k + 1], 3)
            spread[j, b] = sp
            pool = jnp.where(row8 == b, jnp.mean(sp, axis=0, keepdims=True), pool)
        pooled[j] = pool
        term = mm_nt(low(pool), flat(W["Gi"][j]))
        gs_part = term if gs_part is None else gs_part + term
    gsb[3] = gs_part
    share_start("gs", gsb)
    line_step("n2", n2_all, 2)

    relay4("F1")
    line_step("n2", n2_all, 3)
    for j in range(2):
        act, der = gelu_pair(mm(flat(n2_all[...]), flat(W["F1"][j])))
        u[j] = low(act)
        up[j] = low(der)

    scatter_wait("gs", gsb)

    def gate_hidden():
        return gelu_pair((gsb[0] + gsb[1]) + (gsb[2] + gsb[3]))

    gh, _ = gate_hidden()
    for j in range(2):
        g8 = jnp.tanh(mm(low(gh), flat(W["Go"][j])))
        gate[j] = g8
        for b in range(Z):
            br_sb[b, :, j * adq : (j + 1) * adq] = low(g8[b : b + 1] * spread[j, b])
    scatter_start("br", br_sb, br_rb)
    relay4("F2")

    u_both = side_by_side([u[0], u[1]])

    @pl.loop(0, Z // 2)
    def _(pair):
        halves = [
            side_by_side([W["F2"][j, 2 * pair + dz_, rr] for dz_ in range(2) for rr in range(R)])
            for j in range(2)
        ]
        acc = mm(u_both, jnp.concatenate(halves, axis=0))
        m_sb[:, :, lanes_of(pair, 2 * dz)] = low(acc).reshape(Z, TOK, 2 * dz)

    sum_start("m", m_sb, m_rb)

    def exchange(n, buf):
        remote(buf.at[x], buf.at[x], xo_send.at[n], xo_recv.at[n], over_x).start()

    def layer_output(total):
        sum_step("m", m_sb, m_rb, 2)
        scatter_wait("br", br_rb)
        total[...] = x1[...]
        for d in range(Z):
            piece = br_sb[zi] if d == 0 else br_rb[d - 1]
            for j in range(2):
                lanes = pl.ds(pl.multiple_of(j * adh + zfrom(d) * adq, LANE), adq)
                total[:, lanes] += wide(piece[:, j * adq : (j + 1) * adq])
        sum_step("m", m_sb, m_rb, 1)
        sum_wait("m", m_rb)
        hid_tok[x] = low(total[...] + summed(m_sb, m_rb))

    @pl.when(p == 0)
    def _():
        layer_output(dx1)
        remote(hid_tok.at[x], x_in, h_send.at[0], h_recv.at[0], sib).start()
        exchange(0, hid_tok)

    exchange(1, hid_grid)
    relay_sent()

    def over_cores(d):
        return remote(
            out_gtok.at[x], dx3_all.at[zi], b_send.at[d], b_recv.at[d], dev(zto(d), pp=1 - p)
        )

    @pl.when(p == 0)
    def _():
        for d in range(Z):
            slot = dx3_all.at[zfrom(d)]
            remote(slot, slot, b_send.at[d], b_recv.at[d], sib).wait_recv()
        dx3[...] = dx3_all[zi]

    def own_lanes(j):
        return pl.ds(pl.multiple_of(j * adh + zi * adq, LANE), adq)

    gh, ghp = gate_hidden()
    dgh_part = None
    dgp = []
    for j in range(2):
        dgate = jnp.zeros((8, adq), F32)
        for b in range(Z):
            dbr = wide(dx3_all[b, :, own_lanes(j)])
            dgate = jnp.where(row8 == b, jnp.sum(dbr * spread[j, b], axis=0, keepdims=True), dgate)
        dg8 = low(dgate * (1.0 - gate[j] * gate[j]))
        dgp.append(dg8)
        term = mm_nt(dg8, flat(W["Go"][j]))
        dgh_part = term if dgh_part is None else dgh_part + term
    dgb[3] = dgh_part
    share_start("dgh", dgb)

    for j in range(2):
        cols = side_by_side([W["F2"][j, z, rr] for z in range(Z) for rr in range(R)])
        dh[j] = low(mm_nt(flat(dx3_all[...]), cols) * wide(up[j]))

    scatter_wait("dgh", dgb)
    dgs = low(((dgb[0] + dgb[1]) + (dgb[2] + dgb[3])) * ghp)
    for j in range(2):
        dpool = mm(dgs, flat(W["Gi"][j])) * (1.0 / TOK)
        taps = aq[j]
        tap_rows = [None] * 9
        for b in range(Z):
            dsp = gate[j, b : b + 1] * wide(dx3_all[b, :, own_lanes(j)]) + dpool[b : b + 1]
            dad[j, b * TOK : (b + 1) * TOK] = low(depthwise(dsp, lambda k: taps[8 - k : 9 - k], 3))

            def put(k, row):
                tap_rows[k] = row if tap_rows[k] is None else tap_rows[k] + row

            depthwise_taps(adapted[j, b * TOK : (b + 1) * TOK], dsp, 3, put)
        for k in range(9):
            gad[j, k : k + 1] = tap_rows[k]
        gad[j, 9:16] = jnp.zeros((7, adq), F32)

    pair_out(dad, "E", dc2_sb, cz)

    sum_start("dc2", dc2_sb, dc2_rb)

    pair_out(dh, "F1", dn2_sb, dz)

    sum_start("dn2", dn2_sb, dn2_rb)
    sum_step("dc2", dc2_sb, dc2_rb, 2)

    def half_rows(name, upper):
        half = W[name].shape[-2] // 2
        rows = slice(half, None) if upper else slice(0, half)
        return (slice(None), rows) if len(W[name].shape) == 6 else (rows,)

    fine = ("P1", "P2")

    def pieces(name):
        return (1, 2, 3, 0) if name in fine else (None,)

    def block_at(d):
        return slice(None) if d is None else zto(d)

    def hop_copy(name, which, d):
        n = ids[name]
        lower, upper = half_rows(name, False), half_rows(name, True)
        z = block_at(d)
        w, buf = W[name], RX[name]
        src, dst, to = (
            lambda: (w.at[(xo, z, slice(None)) + lower], buf[0].at[z], over_x),
            lambda: (w.at[(slice(None), z, ro) + upper], buf[1].at[:, z], over_r),
            lambda: (buf[0].at[z, ro], buf[2].at[z], over_r),
            lambda: (buf[1].at[xo, z], buf[3].at[z], over_x),
        )[which]()
        k = 0 if d is None else d
        return remote(src, dst, g_send.at[n, which, k], g_recv.at[n, which, k], to)

    def reduce_start(name, d=None):
        hop_copy(name, 0, d).start()
        hop_copy(name, 1, d).start()

    def each_block(d, body):
        if d is None:
            pl.loop(0, Z)(body)
        else:
            body(zto(d))

    def per_piece(name, body):
        if name in fine:
            pl.loop(0, Z)(lambda k: body(lax.rem(k + 1, Z)))
        else:
            body(None)

    def reduce_middle(*names):
        for name in names:
            lower, upper = half_rows(name, False), half_rows(name, True)
            buf = RX[name]

            def middle(d):
                hop_copy(name, 0, d).wait_recv()

                def add_lower(z):
                    for rr in range(R):
                        own = W[name][(x, z, rr) + lower]
                        buf[0][z, rr] = low(wide(own) + wide(buf[0][z, rr]))

                each_block(d, add_lower)
                hop_copy(name, 2, d).start()
                hop_copy(name, 1, d).wait_recv()

                def add_upper(z):
                    for j in range(2):
                        own = W[name][(j, z, ri) + upper]
                        buf[1][j, z] = low(wide(own) + wide(buf[1][j, z]))

                each_block(d, add_upper)
                hop_copy(name, 3, d).start()

            per_piece(name, middle)

    def reduce_end(*names):
        for name in names:
            lower, upper = half_rows(name, False), half_rows(name, True)
            buf = RX[name]

            def end(d):
                hop_copy(name, 2, d).wait_recv()
                hop_copy(name, 3, d).wait_recv()

                def add_both(z):
                    W[name][(x, z, ri) + lower] = low(wide(buf[0][z, ri]) + wide(buf[2][z]))
                    W[name][(x, z, ri) + upper] = low(wide(buf[1][x, z]) + wide(buf[3][z]))

                each_block(d, add_both)

            if name in fine:

                @pl.loop(1, Z)
                def _(d):
                    end(d)
                    back_copy(name, d).start()

                end(0)
            else:
                end(None)
                for d in range(1, Z):
                    back_copy(name, d).start()
            back_local(name).start()

    def landing(name):
        return nat if name in ("P1", "P2") else native[name]

    def back_copy(name, d):
        n = ids[name]
        return remote(
            W[name].at[x, zto(d), ri], quarter_of(name, landing(name), zi),
            a_send.at[n, d - 1], a_recv.at[n, d - 1], dev(zto(d)),
        )

    def back_local(name):
        return pltpu.make_async_copy(
            W[name].at[x, zi, ri], quarter_of(name, landing(name), zi), loc_sem.at[ids[name]]
        )

    peers = ((1, 0), (0, 1), (1, 1))

    def owner(k):
        return (ro if peers[k][0] else ri), (xo if peers[k][1] else x)

    def row_grad(name, left, right):
        width = W[name].shape[3]
        span = R * width

        @pl.loop(0, Z)
        def _(k):
            d = lax.rem(k + 1, Z)
            z = zto(d)
            turned[0:span] = flat(left[:, :, lanes_of(z, span)]).T
            for j in range(2):
                W[name][j, z] = low(mm(turned[0:span], right[j])).reshape(R, width, -1)
            if name in fine:
                reduce_start(name, d)

        if name not in fine:
            reduce_start(name)

    def col_grad(name, left, right):
        width = left.shape[2]
        for j in range(2):
            turned[j * width : (j + 1) * width] = left[j].T

        @pl.loop(0, Z)
        def _(z):
            rhs = flat(right[:, :, lanes_of(z, dz)])
            for j in range(2):
                g = low(mm(turned[j * width : (j + 1) * width], rhs))
                for rr in range(R):
                    W[name][j, z, rr] = g[:, rr * LANE : (rr + 1) * LANE]

        reduce_start(name)

    for j in range(2):
        W["Gi"][j] = low(mm_tn(dgs, low(pooled[j]))).reshape(Z, R, -1, adq)
        W["Go"][j] = low(mm_tn(low(gh), dgp[j])).reshape(Z, R, -1, adq)
    sum_step("dc2", dc2_sb, dc2_rb, 1)
    sum_step("dn2", dn2_sb, dn2_rb, 2)
    reduce_start("Gi")
    reduce_start("Go")
    row_grad("E", c2_all, dad)
    sum_step("dn2", dn2_sb, dn2_rb, 1)

    @pl.when(p == 0)
    def _():
        remote(dcot, dcot, c_send, c_recv, sib).wait_recv()

    sum_wait("dc2", dc2_rb)
    dc2t[...] = wide(dcot[...]) + summed(dc2_sb, dc2_rb)
    gvs_ls = jnp.sum(cv_sum[...] * dc2t[...], axis=0, keepdims=True)
    dcv_all[zi] = low(dc2t[...] * gain_c(50))
    line_start("dcv", dcv_all)

    sum_wait("dn2", dn2_rb)
    dn2 = summed(dn2_sb, dn2_rb)
    n_hat, rs = normed(x1[...])
    gvs_d1 = jnp.sum(dn2 * n_hat, axis=0, keepdims=True)
    dx1[...] = wide(dx3[...]) + norm_back(dn2, n_hat, rs, gain_d(1))
    dx1_all[zi] = low(dx1[...])
    line_start("dx1", dx1_all)
    line_step("dcv", dcv_all, 1)
    col_grad("F2", u, dx3_all)
    line_step("dcv", dcv_all, 2)
    line_step("dx1", dx1_all, 1)
    row_grad("F1", n2_all, dh)

    line_step("dcv", dcv_all, 3)
    line_step("dx1", dx1_all, 2)

    def operand_copies():
        return [
            remote(src, dst, m_send.at[n], m_recv.at[n], sib)
            for n, (src, dst) in enumerate(((dcv_all, alt_a), (r, alt_b)))
        ]

    def operand_copies_back():
        return [
            remote(src, dst, m_send.at[n], m_recv.at[n], sib)
            for n, (src, dst) in enumerate(((f_all, alt_a), (dhc, alt_b)))
        ]

    def chosen(flag_at, left, right):
        for n, buf in enumerate((alt_a, alt_b)):
            remote(buf, buf, m_send.at[n], m_recv.at[n], sib).wait_recv()
        mine = train_in[0, flag_at] == 1
        alt_a[...] = jnp.where(mine, left[...], alt_a[...])
        alt_b[...] = jnp.where(mine, right[...], alt_b[...])

    @pl.when(p == 1)
    def _():
        for c in operand_copies():
            c.start()

    for j in range(2):
        dhc[j] = low(mm(flat(dcv_all[...]), flat(W["P2"][j])) * wide(rp[j]))

    pair_out(dhc, "P1", df_sb, cz)

    sum_start("df", df_sb, df_rb)

    early = ("Gi", "Go", "E", "F2", "F1")

    def pw_grads():
        for c in operand_copies_back():
            c.start()
        chosen(3, dcv_all, r)
        row_grad("P2", alt_a, alt_b)

    line_step("dx1", dx1_all, 3)

    @pl.when(p == 0)
    def _():
        pw_grads()

    sum_step("df", df_sb, df_rb, 2)

    out_rows = [
        side_by_side([W["O"][j, z, rr] for z in range(Z) for rr in range(R)]) for j in range(2)
    ]
    do_both = low(mm_nt(flat(dx1_all[...]), jnp.concatenate(out_rows, axis=0)))
    for j in range(2):
        do_all[j] = do_both[:, j * hq : (j + 1) * hq]
    @pl.loop(0, Z)
    def _(b):
        rows = lanes_of(b, TOK)
        for j in range(2):
            parts = [[], [], []]
            for h in range(hq // HD):
                q, kk, vals = (qkv[j, rows, s * hq + h * HD : s * hq + (h + 1) * HD] for s in range(3))
                do = do_all[j, rows, h * HD : (h + 1) * HD]
                pr = prob[j, h, b]
                dp = mm_nt(do, vals)
                prw = wide(pr)
                ds = low(prw * (dp - jnp.sum(dp * prw, axis=-1, keepdims=True)) * HD ** (-0.5))
                parts[0].append(mm(ds, kk))
                parts[1].append(mm_tn(ds, q))
                parts[2].append(mm_tn(pr, do))
            for s in range(3):
                dqkv[j, rows, s * hq : (s + 1) * hq] = low(side_by_side(parts[s]))

    dqkv_both = side_by_side([dqkv[0], dqkv[1]])

    @pl.loop(0, Z // 2)
    def _(pair):
        zs = pl.ds(pair * 2, 2)
        rows_q = side_by_side([flat(W["Q"][j, zs, :, s]) for j in range(2) for s in range(3)])
        acc = mm_nt(dqkv_both, rows_q)
        dn1_sb[:, :, lanes_of(pair, 2 * dz)] = low(acc).reshape(Z, TOK, 2 * dz)

    sum_start("dn1", dn1_sb, dn1_rb)
    sum_step("df", df_sb, df_rb, 1)
    reduce_middle("Gi", "Go", "E")

    def attention_grads():
        @pl.loop(0, Z)
        def _(z):
            turned[0:dz] = flat(n1_all[:, :, lanes_of(z, dz)]).T
            for j in range(2):
                g = low(mm(turned[0:dz], dqkv[j]))
                for s in range(3):
                    W["Q"][j, z, :, s] = g[:, s * hq : (s + 1) * hq].reshape(R, -1, hq)

        reduce_start("Q")
        col_grad("O", ctx, dx1_all)

    sum_step("dn1", dn1_sb, dn1_rb, 2)
    reduce_middle("F2", "F1")
    sum_step("dn1", dn1_sb, dn1_rb, 1)

    @pl.when(p == 0)
    def _():
        reduce_middle("P2")
        attention_grads()
        reduce_end(*early)

    sum_wait("dn1", dn1_rb)
    dn1 = summed(dn1_sb, dn1_rb)
    n_hat, rs = normed(wide(x_in[...]))
    gvs_d0 = jnp.sum(dn1 * n_hat, axis=0, keepdims=True)
    out_gtok[x] = low(dx1[...] + norm_back(dn1, n_hat, rs, gain_d(0)))

    @pl.when(p == 1)
    def _():
        for d in (1, 2, 3, 0):
            over_cores(d).start()

    sum_wait("df", df_rb)
    dfv = summed(df_sb, df_rb)
    gvs_lc = jnp.sum(dfv * cn[...], axis=0, keepdims=True)
    dcn[...] = norm_back(dfv, cn[...], crs[:, 0:1], gain_c(49))

    @pl.loop(0, c_dim // LANE)
    def _(ch):
        lanes = lanes_of(ch, LANE)
        taps = vec_c[:, lanes]
        back = depthwise(dcn[:, lanes], lambda k: taps[48 - k : 49 - k], 7)
        out_ggrid[x, :, lanes] = low(dc2t[:, lanes] + back)

    @pl.when(p == 1)
    def _():
        remote(out_ggrid.at[x], dcot, c_send, c_recv, sib).start()
        attention_grads()
        layer_output(dx1)
        exchange(0, hid_tok)
        reduce_end(*early)

    @pl.when(p == 0)
    def _():
        reduce_end("P2")

    exchange(2, out_gtok)
    exchange(3, out_ggrid)

    @pl.loop(0, Z)
    def _(z):
        for part in range(cz // LANE):
            lanes = pl.ds(pl.multiple_of(z * cz + part * LANE, LANE), LANE)

            def put(k, row):
                gvs[z, k : k + 1, part * LANE : (part + 1) * LANE] = row

            depthwise_taps(wide(c_in[:, lanes]), dcn[:, lanes], 7, put)

    for z in range(Z):
        gvs[z, 49:50] = gvs_lc[:, z * cz : (z + 1) * cz]
        gvs[z, 50:51] = gvs_ls[:, z * cz : (z + 1) * cz]
        gvs[z, 51:64] = jnp.zeros((13, cz), F32)
        gvs[z, 56:57, 0:dz] = gvs_d0[:, z * dz : (z + 1) * dz]
        gvs[z, 57:58, 0:dz] = gvs_d1[:, z * dz : (z + 1) * dz]
    gvs_low[...] = low(gvs[...])
    scatter_start("gv", gvs_low, gv_rb)

    def group_copy(n, k, src, dst):
        rr, xx = owner(k)
        return remote(src, dst, gx_send.at[n, k], gx_recv.at[n, k], dev(rr=rr, xx=xx))

    for k in range(3):
        c = group_copy(1, k, gad, gad_rb.at[k])
        c.start()
        sent.append(c)
    scatter_wait("gv", gv_rb)
    gvx[3] = (gvs[zi] + wide(gv_rb[0])) + (wide(gv_rb[1]) + wide(gv_rb[2]))
    for k in range(3):
        c = group_copy(0, k, gvx.at[3], gvx.at[k])
        c.start()
        sent.append(c)
    for k in range(3):
        group_copy(1, k, gad, gad_rb.at[k]).wait_recv()
    gad_all[zi] = (gad[x] + gad_rb[0, x]) + (gad_rb[1, x] + gad_rb[2, x])
    gather_start("gad", gad_all)
    reduce_middle("Q", "O")
    reduce_end("Q", "O")

    @pl.when(p == 1)
    def _():
        chosen(2, f_all, dhc)
        row_grad("P1", alt_a, alt_b)
        reduce_middle("P1")
        reduce_end("P1")

    def to_both(name):
        n = ids[name]
        back_local(name).wait()
        for d in range(1, Z):
            slot = quarter_of(name, nat, zfrom(d))
            remote(slot, slot, a_send.at[n, d - 1], a_recv.at[n, d - 1], dev(zto(d))).wait_recv()
        pltpu.make_async_copy(nat, native[name], f_sem).start()
        remote(nat, native[name], f_send, f_recv, sib).start()

    def both_done(name, other):
        pltpu.make_async_copy(nat, native[name], f_sem).wait()
        remote(nat, native[name], f_send, f_recv, sib).wait_send()
        remote(nat, native[other], f_send, f_recv, sib).wait_recv()

    @pl.when(p == 0)
    def _():
        to_both("P2")

    @pl.when(p == 1)
    def _():
        to_both("P1")

    for k in range(3):
        group_copy(0, k, gvx.at[k], gvx.at[k]).wait_recv()
    total = (gvx[0] + gvx[1]) + (gvx[2] + gvx[3])
    mine = jnp.where(ri == 1, pltpu.roll(total, c_own, 1), total)[:, 0:c_own]
    mine_d = jnp.where(ri == 1, total[:, LANE : 2 * LANE], total[:, 0:LANE])

    def flag(n):
        return train_in[0, n].astype(F32)

    out_depth[...] = mine[0:taps7] * flag(0)
    out_ln_conv[...] = mine[49:50] * flag(1)
    out_scale[...] = mine[50:51] * flag(4)
    out_ln_attn[...] = mine_d[56:57]
    out_ln_mlp[...] = mine_d[57:58]
    gather_wait("gad", gad_all)
    for z in range(Z):
        out_ad[:, z * adq : (z + 1) * adq] = gad_all[z][0:9]
    for name in ARRAYS[2:]:
        back_local(name).wait()
        for d in range(1, Z):
            n = ids[name]
            slot = quarter_of(name, native[name], zfrom(d))
            remote(slot, slot, a_send.at[n, d - 1], a_recv.at[n, d - 1], dev(zto(d))).wait_recv()
    for n, buf in enumerate((hid_tok, hid_grid, out_gtok, out_ggrid)):
        c = remote(buf.at[x], buf.at[x], xo_send.at[n], xo_recv.at[n], over_x)
        c.wait_send()
        remote(buf.at[xo], buf.at[xo], xo_send.at[n], xo_recv.at[n], over_x).wait_recv()

    @pl.when(p == 0)
    def _():
        remote(hid_tok.at[x], x_in, h_send.at[0], h_recv.at[0], sib).wait_send()
        remote(hid_grid.at[x], c_in, h_send.at[1], h_recv.at[1], sib).wait_send()

    @pl.when(p == 1)
    def _():
        for d in range(Z):
            over_cores(d).wait_send()
        remote(out_ggrid.at[x], dcot, c_send, c_recv, sib).wait_send()

    for name, buf in line_gathers:
        line_sent(name, buf)

    @pl.when(p == 1)
    def _():
        line_sent("dx3", dx3_all)

    for name, sb, rb in line_sums:
        sum_sent(name, sb, rb)
    for c in sent:
        c.wait_send()
    def all_sent(name):
        for which in range(4):
            for d in pieces(name):
                hop_copy(name, which, d).wait_send()
        for d in range(1, Z):
            back_copy(name, d).wait_send()

    for name in ARRAYS[2:]:
        all_sent(name)

    @pl.when(p == 0)
    def _():
        all_sent("P2")
        for c in operand_copies_back():
            c.wait_send()
        both_done("P2", "P1")

    @pl.when(p == 1)
    def _():
        all_sent("P1")
        for c in operand_copies():
            c.wait_send()
        both_done("P1", "P2")


def run_layers(weights, vectors, order, train, streams, sizes, outer):
    d_dim, c_dim, hq, ffq, cfq, adw, dg = sizes
    vm = pltpu.VMEM
    blocks = []
    for name, value in zip(ARRAYS, weights):
        if name == "Q":
            blocks.append((3, value.shape[1], hq))
        elif name in ("O", "F2"):
            blocks.append((value.shape[0] // Z, value.shape[1]))
        else:
            blocks.append((value.shape[0], value.shape[1] // Z))
    rows = Z * TOK

    def act(width, count=Z, kind=BF):
        return vm((count, TOK, width), kind)

    def line(width):
        return vm((2, 3, TOK, width), BF)

    scratch = [vm((2, Z, R) + s, BF) for s in blocks] + [
        vm(lead + s[:-2] + (s[-2] // 2, s[-1]), BF)
        for s in blocks[1:]
        for lead in ((Z, R), (2, Z), (Z,), (Z,))
    ]
    scratch += [
        vm((64, 2 * LANE), F32), vm((64, 2 * LANE), BF), vm((Z * R, 64, 2 * LANE), BF), vm((2, 16, adw), F32), vm((64, c_dim), F32), vm((8, d_dim), F32),
        vm((TOK, d_dim), BF), vm((TOK, c_dim), BF), act(d_dim), act(c_dim), act(d_dim), act(c_dim),
        act(d_dim), line(d_dim), act(c_dim), line(c_dim), act(d_dim), line(d_dim),
        act(2 * adw), act(2 * adw, 3), vm((4, 8, dg), F32), vm((4, 8, dg), F32),
        vm((2, rows, 3 * hq), BF), vm((2, hq // HD, Z, TOK, TOK), BF), vm((2, rows, hq), BF),
        vm((2, rows, ffq), BF), vm((2, rows, ffq), BF), vm((2, rows, cfq), BF), vm((2, rows, cfq), BF),
        vm((TOK, c_dim), F32), vm((TOK, LANE), F32), vm((TOK, c_dim), F32), vm((TOK, d_dim), F32), vm((TOK, c_dim), F32),
        vm((2, rows, adw), F32), vm((2, Z, TOK, adw), F32), vm((2, 8, adw), F32), vm((2, 8, adw), F32),
        vm((TOK, d_dim), BF), vm((TOK, c_dim), BF), act(d_dim), act(d_dim), line(d_dim), act(c_dim), line(c_dim),
        act(d_dim), act(c_dim),
        act(d_dim), line(d_dim), act(c_dim), line(c_dim), vm((2, rows, ffq), BF), vm((2, rows, hq), BF),
        vm((2, rows, 3 * hq), BF), vm((2, rows, cfq), BF), vm((TOK, d_dim), F32), vm((TOK, c_dim), F32), vm((2, rows, adw), BF),
        vm((TOK, c_dim), F32),
        vm((Z, 64, c_dim // Z), F32), vm((Z, 64, c_dim // Z), BF), vm((3, 64, c_dim // Z), BF), vm((4, 64, c_dim // Z), F32),
        vm((2, 16, adw), F32), vm((3, 2, 16, adw), F32), vm((Z, 16, adw), F32),
        vm((2 * ffq, rows), BF), act(c_dim), vm((2, rows, cfq), BF), vm(weights[0].shape, BF),
    ]
    dma = pltpu.SemaphoreType.DMA
    na = len(ARRAYS)
    scratch += [
        dma((len(EVENTS), 3)), dma((len(EVENTS), 3)), dma((len(EVENTS), 6)), dma((len(EVENTS), 6)), dma((na, 3)), dma((na, 3)), dma((na,)),
        dma((na, 4, Z)), dma((na, 4, Z)), dma((7,)), dma((7,)), dma, dma, dma((2,)), dma((2,)), dma((Z,)), dma((Z,)), dma, dma,
        dma((4,)), dma((4,)), dma((na, 4, Z)), dma((na, 4, Z)), dma((na, 3)), dma((na, 3)), dma((2, 3)), dma((2, 3)),
        pltpu.SemaphoreType.REGULAR,
        dma((2,)), dma((2,)), dma, dma, dma,
    ]
    sds = jax.ShapeDtypeStruct
    out_shape = [sds((2, TOK, d_dim), BF), sds((2, TOK, c_dim), BF)] * 2
    out_shape += [sds(value.shape, BF) for value in weights]
    out_shape += [sds(value.shape, F32) for value in vectors]
    any_spec = pl.BlockSpec(memory_space=pl.ANY)
    vm_spec = pl.BlockSpec(memory_space=pltpu.VMEM)
    sm_spec = pl.BlockSpec(memory_space=pltpu.SMEM)
    return pl.pallas_call(
        functools.partial(main_kernel, sizes, outer),
        out_shape=out_shape,
        in_specs=[any_spec] * na + [vm_spec] * 6 + [sm_spec] * 2 + [vm_spec] * 4,
        out_specs=[vm_spec] * 4 + [any_spec] * na + [vm_spec] * 6,
        scratch_shapes=scratch,
        compiler_params=pltpu.CompilerParams(
            collective_id=0, has_side_effects=True, vmem_limit_bytes=62 * 1024 * 1024
        ),
        cost_estimate=pl.CostEstimate(flops=26 * 10**9, bytes_accessed=10**8, transcendentals=10**7),
        name="layers",
    )(*weights, *vectors, order, train, *streams)


def finish_kernel(flagged, layer_zero, count, *refs):
    grads, streams, vectors = refs[:count], refs[count : count + 4], refs[count + 4 : count + 10]
    order, train = refs[count + 10 : count + 12]
    refs = refs[count + 12 :]
    out_grads, out_streams, out_vectors = refs[:count], refs[count : count + 4], refs[count + 4 : count + 10]
    refs = refs[count + 10 :]
    held, wide_ones = refs[:count], refs[count : 2 * count]
    in_sem, out_sem = refs[2 * count :]

    def fetch(n):
        return pltpu.make_async_copy(grads[n], held[n], in_sem.at[n])

    def put_back(n):
        return pltpu.make_async_copy(wide_ones[n], out_grads[n], out_sem.at[n])

    for n in range(count):
        fetch(n).start()
    swap = (lax.axis_index("pipe") == layer_zero) & (order[0, 0] == 1)
    for n, (src, dst) in enumerate(zip(streams, out_streams)):
        for m in range(2):
            dst[m] = src[m] if n < 2 else jnp.where(swap, src[1 - m], src[m])
    for src, dst in zip(vectors, out_vectors):
        if len(dst.shape) == 3:
            for row in range(dst.shape[0]):
                dst[row] = src[row : row + 1]
        else:
            dst[...] = src[...]
    for n in range(count):
        fetch(n).wait()
        src, dst = held[n], wide_ones[n]
        scale = train[0, flagged[n]].astype(F32) if n in flagged else None
        lead = src.shape[0] if len(src.shape) == 3 else 1

        @pl.loop(0, lead * (src.shape[-2] // 16))
        def _(step):
            rows = pl.ds(pl.multiple_of((step // lead) * 16, 16), 16)
            at = (step % lead, rows) if len(src.shape) == 3 else (rows,)
            value = wide(src[at])
            dst[at] = value if scale is None else value * scale

        put_back(n).start()
    for n in range(count):
        put_back(n).wait()


def finish(outs, order, train):
    count = len(ARRAYS)
    streams, grads, vectors = outs[:4], outs[4 : 4 + count], outs[4 + count :]
    any_spec = pl.BlockSpec(memory_space=pl.ANY)
    sm_spec = pl.BlockSpec(memory_space=pltpu.SMEM)
    vm_spec = pl.BlockSpec(memory_space=pltpu.VMEM)
    sds = jax.ShapeDtypeStruct
    dma = pltpu.SemaphoreType.DMA
    flagged = {ARRAYS.index("P1"): 2, ARRAYS.index("P2"): 3}
    return pl.pallas_call(
        functools.partial(finish_kernel, flagged, 0, count),
        out_shape=[sds(g.shape, F32) for g in grads]
        + [sds(value.shape, value.dtype) for value in streams]
        + [sds(value.shape if value.shape[0] == 1 else (value.shape[0], 1, value.shape[1]), F32) for value in vectors],
        in_specs=[any_spec] * count + [vm_spec] * 10 + [sm_spec] * 2,
        out_specs=[any_spec] * count + [vm_spec] * 10,
        scratch_shapes=[pltpu.VMEM(g.shape, BF) for g in grads]
        + [pltpu.VMEM(g.shape, F32) for g in grads]
        + [dma((count,)), dma((count,))],
        compiler_params=pltpu.CompilerParams(vmem_limit_bytes=62 * 1024 * 1024),
        name="finish",
    )(*grads, *streams, *vectors, order, train)


def per_device(
    tokens,
    conv_grid,
    order,
    trainable,
    ln_attn,
    w_qkv,
    w_attn_out,
    ln_mlp,
    w_fc_in,
    w_fc_out,
    conv_depth,
    ln_conv,
    w_pw_in,
    w_pw_out,
    layer_scale,
    w_adapt,
    adapt_depth,
    w_gate_in,
    w_gate_out,
    tok_cot,
    grid_cot,
):
    dp_count = lax.axis_size("dp")
    outer = dp_count // (Z * R)
    groups = [[g * outer + o for o in range(outer)] for g in range(Z * R)]

    def block(value, axis):
        value = value[0]
        if outer == 1:
            return value
        return lax.all_gather(value, "dp", axis=axis, tiled=True, axis_index_groups=groups)

    def share(value, axis):
        if outer > 1:
            value = lax.psum_scatter(
                value, "dp", scatter_dimension=axis, tiled=True, axis_index_groups=groups
            )
        return value[None]

    qkv = block(w_qkv, 1)
    gate_in = block(w_gate_in, 1).T
    pw_in = block(w_pw_in, 0)
    adapt = block(w_adapt, 0)
    fc_in = block(w_fc_in, 0)
    weights = (
        pw_in,
        block(w_pw_out, 1).T,
        qkv,
        block(w_attn_out, 1),
        adapt,
        gate_in,
        block(w_gate_out, 0),
        fc_in,
        block(w_fc_out, 1),
    )
    vectors = (
        block(conv_depth, 1),
        block(ln_conv, 0)[None],
        block(layer_scale, 0)[None],
        block(ln_attn, 0)[None],
        block(ln_mlp, 0)[None],
        adapt_depth[0],
    )
    spread = Z * R
    sizes = (
        qkv.shape[1] * spread, pw_in.shape[0] * spread, qkv.shape[2] // Z, fc_in.shape[1] // Z,
        pw_in.shape[1] // Z, adapt.shape[1] // Z, gate_in.shape[0] * spread,
    )

    def rows_of(value):
        return value.reshape(value.shape[0], TOK, value.shape[-1])

    streams = [rows_of(value) for value in (tokens, conv_grid, tok_cot, grid_cot)]
    outs = run_layers(weights, vectors, order, trainable, streams, sizes, outer)
    done = finish(outs, order, trainable)
    g_p1, g_p2, g_q, g_o, g_e, g_gi, g_go, g_f1, g_f2 = done[:9]
    hid_tok, hid_grid, g_tok, g_grid = done[9:13]
    g_depth, g_ln_conv, g_scale, g_ln_attn, g_ln_mlp, g_ad = done[13:]
    grid_shape = (1,) + conv_grid.shape
    tok_shape = (1,) + tokens.shape
    g_depth, g_ad = g_depth[:, 0], g_ad[:, 0]
    if outer > 1:
        g_ad = lax.psum(g_ad, "dp", axis_index_groups=groups)
    return (
        hid_tok.reshape(tok_shape),
        hid_grid.reshape(grid_shape),
        g_tok.reshape(tok_shape),
        g_grid.reshape(grid_shape),
        share(g_ln_attn[0], 0),
        share(g_q, 1),
        share(g_o, 1),
        share(g_ln_mlp[0], 0),
        share(g_f1, 0),
        share(g_f2, 1),
        share(g_depth, 1),
        share(g_ln_conv[0], 0),
        share(g_p1, 0),
        share(g_p2.T, 1),
        share(g_scale[0], 0),
        share(g_e, 0),
        g_ad[None],
        share(g_gi.T, 1),
        share(g_go, 0),
    )


def solution(mesh):
    in_specs = (
        P(None, "dp", None, None),
        P(None, "dp", None, None, None),
        P("dp", None),
        P("pipe", None),
        P("pipe", "dp"),
        P("pipe", None, "dp", "tensor"),
        P("pipe", "tensor", "dp"),
        P("pipe", "dp"),
        P("pipe", "dp", "tensor"),
        P("pipe", "tensor", "dp"),
        P("pipe", None, "dp"),
        P("pipe", "dp"),
        P("pipe", "dp", "tensor"),
        P("pipe", "tensor", "dp"),
        P("pipe", "dp"),
        P("pipe", "dp", "tensor"),
        P("pipe", None, "tensor"),
        P("pipe", "tensor", "dp"),
        P("pipe", "dp", "tensor"),
        P(None, "dp", None, None),
        P(None, "dp", None, None, None),
    )
    out_specs = (
        P("pipe", None, "dp", None, None),
        P("pipe", None, "dp", None, None, None),
        P("pipe", None, "dp", None, None),
        P("pipe", None, "dp", None, None, None),
        P("pipe", "dp"),
        P("pipe", None, "dp", "tensor"),
        P("pipe", "tensor", "dp"),
        P("pipe", "dp"),
        P("pipe", "dp", "tensor"),
        P("pipe", "tensor", "dp"),
        P("pipe", None, "dp"),
        P("pipe", "dp"),
        P("pipe", "dp", "tensor"),
        P("pipe", "tensor", "dp"),
        P("pipe", "dp"),
        P("pipe", "dp", "tensor"),
        P("pipe", None, "tensor"),
        P("pipe", "tensor", "dp"),
        P("pipe", "dp", "tensor"),
    )
    return jax.shard_map(
        per_device, mesh=mesh, in_specs=in_specs, out_specs=out_specs, check_vma=False
    )
```

```python
import functools

import jax
import jax.numpy as jnp
from jax import lax
from jax.experimental import pallas as pl
from jax.experimental.pallas import tpu as pltpu
from jax.sharding import PartitionSpec as P

HD = 64
Z = 4
R = 2
TOK = 64
SIDE = 8
LANE = 128
BF = jnp.bfloat16
F32 = jnp.float32
ARRAYS = ("P1", "P2", "Q", "O", "E", "Gi", "Go", "F1", "F2")
EVENTS = (
    "n1", "f", "o", "cv", "n2", "c2", "m", "br", "gs",
    "dx3", "dgh", "dn2", "dc2", "dx1", "dcv", "dn1", "df", "gv", "gad",
)


def mm(a, b):
    return lax.dot_general(a, b, (((1,), (0,)), ((), ())), preferred_element_type=F32)


def mm_nt(a, b):
    return lax.dot_general(a, b, (((1,), (1,)), ((), ())), preferred_element_type=F32)


def mm_tn(a, b):
    return lax.dot_general(a, b, (((0,), (0,)), ((), ())), preferred_element_type=F32)


def flat(value):
    return value.reshape(-1, value.shape[-1])


def low(value):
    return value.astype(BF)


def wide(value):
    return value.astype(F32)


def gelu_pair(h):
    phi = 0.5 * (1.0 + lax.erf(h * 0.7071067811865476))
    dens = jnp.exp(-0.5 * h * h) * 0.3989422804014327
    return h * phi, phi + h * dens


def normed(value):
    centred = value - jnp.mean(value, axis=-1, keepdims=True)
    rs = lax.rsqrt(jnp.mean(centred * centred, axis=-1, keepdims=True) + 1e-06)
    return centred * rs, rs


def norm_back(dn, n_hat, rs, gain):
    gd = dn * gain
    return (
        gd
        - jnp.mean(gd, axis=-1, keepdims=True)
        - n_hat * jnp.mean(gd * n_hat, axis=-1, keepdims=True)
    ) * rs


def col_shift(value, by):
    if by == 0:
        return value
    at = lax.broadcasted_iota(jnp.int32, value.shape, 0) % SIDE
    rolled = pltpu.roll(value, (-by) % TOK, 0)
    return jnp.where((at + by >= 0) & (at + by < SIDE), rolled, 0.0)


def row_shift(value, by):
    if by == 0:
        return value
    gap = jnp.zeros((abs(by) * SIDE, value.shape[1]), value.dtype)
    if by > 0:
        return jnp.concatenate([value[by * SIDE :], gap], axis=0)
    return jnp.concatenate([gap, value[: TOK + by * SIDE]], axis=0)


def depthwise(value, tap, side):
    half = side // 2
    shifted = [col_shift(value, b - half) for b in range(side)]
    total = None
    for a in range(side):
        line = None
        for b in range(side):
            term = shifted[b] * tap(a * side + b)
            line = term if line is None else line + term
        line = row_shift(line, a - half)
        total = line if total is None else total + line
    return total


def depthwise_taps(value, grad, side, put):
    half = side // 2
    shifted = [col_shift(value, b - half) for b in range(side)]
    for a in range(side):
        d = a - half
        lo, hi = max(0, -d) * SIDE, (SIDE - max(0, d)) * SIDE
        for b in range(side):
            part = shifted[b][lo + d * SIDE : hi + d * SIDE] * grad[lo:hi]
            put(a * side + b, jnp.sum(part, axis=0, keepdims=True))


def lanes_of(at, width):
    return pl.ds(pl.multiple_of(at * width, width), width)


def side_by_side(blocks):
    return jnp.concatenate(blocks, axis=1)


def main_kernel(dims, outer, *refs):
    at = iter(refs)

    def take(count):
        return [next(at) for _ in range(count)]

    na = len(ARRAYS)
    source = dict(zip(ARRAYS, take(na)))
    (
        depth_in, ln_conv_in, scale_in, ln_attn_in, ln_mlp_in, adapt_depth_in,
        order_in, train_in, tok_in, grid_in, tcot_in, gcot_in,
    ) = take(12)
    hid_tok, hid_grid, out_gtok, out_ggrid = take(4)
    native = dict(zip(ARRAYS, take(na)))
    out_depth, out_ln_conv, out_scale, out_ln_attn, out_ln_mlp, out_ad = take(6)
    W = dict(zip(ARRAYS, take(na)))
    hops = take(4 * (na - 1))
    RX = {name: hops[4 * max(n - 1, 0) : 4 * max(n - 1, 0) + 4] for n, name in enumerate(ARRAYS)}
    (
        v_loc, v_low, vv, aq, vec_c, vec_d, x_in, c_in, n1_all, f_all, n2_all, c2_all,
        o_sb, o_rb, cv_sb, cv_rb, m_sb, m_rb, br_sb, br_rb, gsb, dgb,
        qkv, prob, ctx, u, up, r, rp, cn, crs, cv_sum, x1, c2f,
        adapted, spread, pooled, gate,
        dx3, dcot, dx3_all, dn2_sb, dn2_rb, dc2_sb, dc2_rb, dx1_all, dcv_all,
        dn1_sb, dn1_rb, df_sb, df_rb, dh, do_all, dqkv, dhc, dx1, dc2t, dad, dcn,
        gvs, gvs_low, gv_rb, gvx, gad, gad_rb, gad_all, turned, alt_a, alt_b, nat,
    ) = take(70)
    (
        zs_send, zs_recv, l_send, l_recv, s1_send, s1_recv, loc_sem, s2_send, s2_recv,
        v_send, v_recv, q_send, q_recv, h_send, h_recv, b_send, b_recv, c_send, c_recv,
        xo_send, xo_recv, g_send, g_recv, a_send, a_recv, gx_send, gx_recv, go,
        m_send, m_recv, f_sem, f_send, f_recv,
    ) = take(33)

    p = lax.axis_index("pipe")
    dpi = lax.axis_index("dp")
    x = lax.axis_index("tensor")
    rest = dpi % outer
    zi = dpi // (outer * R)
    ri = (dpi // outer) % R
    xo = 1 - x
    ro = 1 - ri
    d_dim, c_dim, hq, ffq, cfq, adq, dg = dims
    adh = Z * adq
    dz, cz = d_dim // Z, c_dim // Z
    tile = 256
    ids = {name: number for number, name in enumerate(ARRAYS)}
    ev = {name: number for number, name in enumerate(EVENTS)}

    def dev(z=None, rr=None, xx=None, pp=None):
        z = zi if z is None else z
        rr = ri if rr is None else rr
        return (
            p if pp is None else pp,
            (z * R + rr) * outer + rest,
            x if xx is None else xx,
        )

    def zto(d):
        return lax.rem(zi + d, Z)

    def zfrom(d):
        return lax.rem(zi + Z - d, Z)

    def remote(src, dst, ssem, rsem, device):
        return pltpu.make_async_remote_copy(
            src_ref=src, dst_ref=dst, send_sem=ssem, recv_sem=rsem,
            device_id=device, device_id_type=pl.DeviceIdType.MESH,
        )

    sib = dev(pp=1 - p)
    over_r, over_x = dev(rr=ro), dev(xx=xo)

    def z_copy(e, d, src, dst):
        return remote(src, dst, zs_send.at[e, d - 1], zs_recv.at[e, d - 1], dev(zto(d)))

    sent = []

    def gather_copies(name, buf):
        return [z_copy(ev[name], d, buf.at[zi], buf.at[zi]) for d in range(1, Z)]

    def gather_start(name, buf, keep=True):
        copies = gather_copies(name, buf)
        for c in copies:
            c.start()
        if keep:
            sent.extend(copies)

    def gather_wait(name, buf):
        for d in range(1, Z):
            slot = buf.at[zfrom(d)]
            z_copy(ev[name], d, slot, slot).wait_recv()

    def scatter_start(name, sb, rb):
        for d in range(1, Z):
            c = z_copy(ev[name], d, sb.at[zto(d)], rb.at[d - 1])
            c.start()
            sent.append(c)

    def scatter_wait(name, rb):
        for d in range(1, Z):
            z_copy(ev[name], d, rb.at[d - 1], rb.at[d - 1]).wait_recv()

    def right():
        return dev(zi + 1)

    def left():
        return dev(zi - 1)

    def pass_copy(name, buf, toward, s):
        e, k = ev[name], (0 if toward > 0 else 3) + s
        blk = buf.at[zi - toward * s]
        return remote(blk, blk, l_send.at[e, k], l_recv.at[e, k], right() if toward > 0 else left())

    def pass_cond(toward, s):
        if toward > 0:
            return (zi < Z - 1) & (zi - s >= 0)
        return (zi > 0) & (zi + s <= Z - 1)

    def line_start(name, buf):
        for toward in (1, -1):

            @pl.when(pass_cond(toward, 0))
            def _():
                pass_copy(name, buf, toward, 0).start()

    def line_step(name, buf, *steps):
        e = ev[name]
        for s in steps:
            for toward in (1, -1):
                src = zi - toward * s

                @pl.when((src >= 0) & (src <= Z - 1))
                def _():
                    blk = buf.at[src]
                    k = (0 if toward > 0 else 3) + s - 1
                    remote(blk, blk, l_send.at[e, k], l_recv.at[e, k], sib).wait_recv()

                if s < Z - 1:

                    @pl.when(pass_cond(toward, s))
                    def _():
                        pass_copy(name, buf, toward, s).start()

    def line_sent(name, buf):
        for toward in (1, -1):
            for s in range(Z - 1):

                @pl.when(pass_cond(toward, s))
                def _():
                    pass_copy(name, buf, toward, s).wait_send()

    def sum_copy(name, sb, rb, toward, k, first):
        e, way = ev[name], (0 if toward > 0 else 1)
        src = sb.at[zi + toward * k] if first else rb.at[way, k]
        q = way * 3 + k - 1
        return remote(src, rb.at[way, k - 1], l_send.at[e, q], l_recv.at[e, q], right() if toward > 0 else left())

    def at_end(toward):
        return zi == (0 if toward > 0 else Z - 1)

    def passes(toward, k):
        dest = zi + toward * k
        return jnp.logical_not(at_end(toward)) & (dest >= 0) & (dest <= Z - 1)

    def sum_start(name, sb, rb):
        for toward in (1, -1):

            @pl.when(at_end(toward))
            def _():
                for k in (3, 2, 1):
                    sum_copy(name, sb, rb, toward, k, True).start()

    def sum_arrival(name, rb, way, k):
        e = ev[name]
        slot = rb.at[way, k]
        return remote(slot, slot, l_send.at[e, way * 3 + k], l_recv.at[e, way * 3 + k], sib)

    def sum_step(name, sb, rb, *ks):
        for k in ks:
            for way, toward in enumerate((1, -1)):

                @pl.when(passes(toward, k))
                def _():
                    sum_arrival(name, rb, way, k).wait_recv()
                    rb[way, k] = low(wide(rb[way, k]) + wide(sb[zi + toward * k]))
                    sum_copy(name, sb, rb, toward, k, False).start()

    def sum_wait(name, rb):
        for way, toward in enumerate((1, -1)):

            @pl.when(jnp.logical_not(at_end(toward)))
            def _():
                sum_arrival(name, rb, way, 0).wait_recv()

    def summed(sb, rb):
        return wide(sb[zi]) + (wide(rb[0, 0]) + wide(rb[1, 0]))

    def sum_sent(name, sb, rb):
        for toward in (1, -1):

            @pl.when(at_end(toward))
            def _():
                for k in (3, 2, 1):
                    sum_copy(name, sb, rb, toward, k, True).wait_send()

            for k in (2, 1):

                @pl.when(passes(toward, k))
                def _():
                    sum_copy(name, sb, rb, toward, k, False).wait_send()

    def share_start(name, buf):
        for d in range(1, Z):
            c = z_copy(ev[name], d, buf.at[3], buf.at[d - 1])
            c.start()
            sent.append(c)

    def scattered(sb, rb):
        return (wide(sb[zi]) + wide(rb[0])) + (wide(rb[1]) + wide(rb[2]))

    barrier = pltpu.get_barrier_semaphore()
    greeted = [sib]
    for d in range(1, Z):
        greeted += [dev(zto(d)), dev(zto(d), ro), dev(zto(d), pp=1 - p)]
    greeted += [over_r, over_x, dev(rr=ro, xx=xo)]
    for device in greeted:
        pl.semaphore_signal(barrier, inc=1, device_id=device, device_id_type=pl.DeviceIdType.MESH)
    v_loc[...] = jnp.zeros(v_loc.shape, F32)
    taps7 = depth_in.shape[0]
    c_own = depth_in.shape[1]
    v_loc[0:taps7, 0:c_own] = wide(depth_in[...])
    v_loc[49:50, 0:c_own] = wide(ln_conv_in[...])
    v_loc[50:51, 0:c_own] = wide(scale_in[...])
    v_loc[56:57, 0:LANE] = wide(ln_attn_in[...])
    v_loc[57:58, 0:LANE] = wide(ln_mlp_in[...])
    aq[x] = jnp.zeros(aq.shape[1:], F32)
    aq[x, 0:9] = wide(adapt_depth_in[:, lanes_of(zi, adq)])
    v_low[...] = low(v_loc[...])
    line_sums = (
        ("o", o_sb, o_rb), ("cv", cv_sb, cv_rb), ("m", m_sb, m_rb), ("dn2", dn2_sb, dn2_rb),
        ("dc2", dc2_sb, dc2_rb), ("dn1", dn1_sb, dn1_rb), ("df", df_sb, df_rb),
    )
    line_gathers = (
        ("n1", n1_all), ("f", f_all), ("n2", n2_all), ("c2", c2_all), ("dx1", dx1_all), ("dcv", dcv_all),
    )
    for _, _, rb in line_sums:
        for way, toward in enumerate((1, -1)):

            @pl.when(at_end(toward))
            def _():
                rb[way, 0] = jnp.zeros(rb.shape[2:], BF)

    pl.semaphore_wait(barrier, len(greeted))

    me8 = zi * R + ri
    v_arrivals = []
    for n, (d, flip) in enumerate([(d, s) for d in range(Z) for s in (0, 1)][1:]):
        tr = ro if flip else ri
        c = remote(v_low, vv.at[me8], v_send.at[n], v_recv.at[n], dev(zto(d), tr))
        c.start()
        sent.append(c)
        fr = zfrom(d) * R + tr
        v_arrivals.append(remote(vv.at[fr], vv.at[fr], v_send.at[n], v_recv.at[n], dev(zto(d), tr)))
    vv[me8] = v_low[...]
    c = remote(aq.at[x], aq.at[x], q_send, q_recv, over_x)
    c.start()
    sent.append(c)

    by_rows = ("O", "F2")

    def quarter_of(name, ref, z):
        if name == "Q":
            return ref.at[:, :, lanes_of(z, hq)]
        if name in by_rows:
            height = ref.shape[0] // Z
            return ref.at[pl.ds(pl.multiple_of(z * height, height), height)]
        return ref.at[:, lanes_of(z, ref.shape[1] // Z)]

    def step1_local(name):
        return pltpu.make_async_copy(
            quarter_of(name, source[name], zi), W[name].at[x, zi, ri], loc_sem.at[ids[name]]
        )

    def step1_copy(name, d):
        k = ids[name]
        return remote(
            quarter_of(name, source[name], zto(d)), W[name].at[x, zi, ri],
            s1_send.at[k, d - 1], s1_recv.at[k, d - 1], dev(zto(d)),
        )

    def half_of(name, j, z, rr, upper):
        w = W[name]
        half = w.shape[-2] // 2
        rows = slice(half, None) if upper else slice(0, half)
        if len(w.shape) == 6:
            return w.at[j, z, rr, :, rows]
        return w.at[j, z, rr, rows]

    def step2_copy(name, which, d):
        k = ids[name]
        z = zfrom(d)
        if which < 2:
            src = quarter_of(name, source[name], zi) if d == 0 else W[name].at[x, z, ri]
            dst = W[name].at[x, z, ri]
        else:
            src = dst = half_of(name, x, z, ro, False) if which == 2 else half_of(name, xo, z, ri, True)
        to = over_x if which in (1, 2) else over_r
        return remote(src, dst, s2_send.at[k, which, d], s2_recv.at[k, which, d], to)

    def step2_arrival(name, which, d):
        k = ids[name]
        z = zfrom(d)
        if which < 2:
            ref = W[name].at[x, z, ro] if which == 0 else W[name].at[xo, z, ri]
        else:
            ref = half_of(name, xo, z, ro, which == 3)
        to = over_x if which in (1, 2) else over_r
        return remote(ref, ref, s2_send.at[k, which, d], s2_recv.at[k, which, d], to)

    def relay1(*names):
        for name in names:
            for d in range(1, Z):
                step1_copy(name, d).start()

    def relay0(*names):
        for name in names:
            step1_local(name).start()
            step2_copy(name, 0, 0).start()
            step2_copy(name, 1, 0).start()

    def relay2(name, ds=(1, 2, 3)):
        k = ids[name]
        for d in ds:
            slot = W[name].at[x, zfrom(d), ri]
            remote(slot, slot, s1_send.at[k, d - 1], s1_recv.at[k, d - 1], dev(zto(d))).wait_recv()
            step2_copy(name, 0, d).start()
            step2_copy(name, 1, d).start()

    def relay3(name, ds=(0, 1, 2, 3)):
        for d in ds:
            step2_arrival(name, 0, d).wait_recv()
            step2_copy(name, 2, d).start()
            step2_arrival(name, 1, d).wait_recv()
            step2_copy(name, 3, d).start()

    def relay4(*names):
        for name in names:
            step1_local(name).wait()
            for d in range(Z):
                step2_arrival(name, 2, d).wait_recv()
                step2_arrival(name, 3, d).wait_recv()

    def relay_sent():
        for name in ARRAYS:
            for d in range(1, Z):
                step1_copy(name, d).wait_send()
            for which in range(4):
                for d in range(Z):
                    step2_copy(name, which, d).wait_send()

    @pl.when(p == 0)
    def _():
        relay0("P1")
        relay1("P1")
        relay0("P2")
        relay1("P2")
        relay0("Q", "O", "E", "Gi", "Go", "F1", "F2")

    @pl.when(p == 1)
    def _():
        dx3[...] = tcot_in[x]
        dcot[...] = gcot_in[x]
        dx3_all[zi] = tcot_in[x]
        line_start("dx3", dx3_all)

    for c in v_arrivals:
        c.wait_recv()
    remote(aq.at[xo], aq.at[xo], q_send, q_recv, over_x).wait_recv()
    low_lanes = lax.broadcasted_iota(jnp.int32, (64, LANE), 1) < LANE // 2
    for z in range(Z):
        first, second = wide(vv[2 * z]), pltpu.roll(wide(vv[2 * z + 1]), LANE // 2, 1)
        vec_c[:, z * cz : z * cz + LANE] = first[:, 0:LANE]
        vec_c[:, z * cz + LANE : z * cz + 2 * LANE] = jnp.where(
            low_lanes, first[:, LANE:], second[:, 0:LANE]
        )
        vec_c[:, z * cz + 2 * LANE : (z + 1) * cz] = second[:, LANE:]
    for i in range(Z * R):
        vec_d[:, i * LANE : (i + 1) * LANE] = wide(vv[i])[56:64, 0:LANE]

    def gain_d(row):
        return vec_d[row : row + 1, :]

    def gain_c(row):
        return vec_c[row : row + 1, :]

    def token_entry():
        n_hat, _ = normed(wide(x_in[...]))
        n1_all[zi] = low(n_hat * gain_d(0))
        line_start("n1", n1_all)

    def conv_entry():
        @pl.loop(0, c_dim // LANE)
        def _(ch):
            lanes = lanes_of(ch, LANE)
            taps = vec_c[:, lanes]
            cn[:, lanes] = depthwise(wide(c_in[:, lanes]), lambda k: taps[k : k + 1], 7)

        n_hat, rs = normed(cn[...])
        cn[...] = n_hat
        crs[...] = jnp.broadcast_to(rs, crs.shape)
        f_all[zi] = low(n_hat * gain_c(49))
        line_start("f", f_all)

    def first_relays(pump):
        relay2("P1")
        pump(1)
        relay1("Q", "O")
        relay2("P2")
        pump(2)
        relay3("P1")


    @pl.when(p == 0)
    def _():
        first = order_in[0, x] == 0
        c_in[...] = jnp.where(first, grid_in[0], grid_in[1])
        x_in[...] = jnp.where(first, tok_in[0], tok_in[1])
        conv_entry()
        token_entry()

        def pump(s):
            line_step("f", f_all, s)
            line_step("n1", n1_all, s)

        first_relays(pump)
        line_step("f", f_all, 3)
        line_step("n1", n1_all, 3)

    @pl.when(p == 1)
    def _():
        pl.semaphore_wait(go, 1)
        relay0("P1")
        relay1("P1")
        relay0("P2")
        relay1("P2")
        relay0("Q", "O", "E", "Gi", "Go", "F1", "F2")
        first_relays(lambda s: line_step("dx3", dx3_all, s))
        remote(c_in, c_in, h_send.at[1], h_recv.at[1], sib).wait_recv()
        conv_entry()
        line_step("dx3", dx3_all, 3)
        line_step("f", f_all, 1)

    relay2("Q")
    relay2("O")
    relay1("E", "Gi", "Go")
    relay3("P2", (0, 1))

    @pl.when(p == 1)
    def _():
        line_step("f", f_all, 2, 3)

    relay4("P1")

    def conv_hidden(j):
        act, der = gelu_pair(mm(flat(f_all[...]), flat(W["P1"][j])))
        r[j] = low(act)
        rp[j] = low(der)

    conv_hidden(0)

    relay3("P2", (2, 3))
    for name in ("E", "Gi", "Go"):
        relay2(name)
    relay1("F1")
    conv_hidden(1)
    relay3("Q")
    relay3("O")
    relay2("F1")
    relay1("F2")

    @pl.when(p == 0)
    def _():
        pl.semaphore_signal(go, inc=1, device_id=sib, device_id_type=pl.DeviceIdType.MESH)

    relay4("P2")

    def pair_rows(name, pair):
        zs = pl.ds(pair * 2, 2)
        return side_by_side([flat(W[name][0, zs]), flat(W[name][1, zs])])

    def pair_out(left, name, sb, width):
        both = side_by_side([left[0], left[1]])

        @pl.loop(0, Z // 2)
        def _(pair):
            acc = mm_nt(both, pair_rows(name, pair))
            sb[:, :, lanes_of(pair, 2 * width)] = low(acc).reshape(Z, TOK, 2 * width)

    pair_out(r, "P2", cv_sb, cz)

    sum_start("cv", cv_sb, cv_rb)

    for name in ("E", "Gi", "Go"):
        relay3(name)
    sum_step("cv", cv_sb, cv_rb, 2)
    relay2("F2")
    sum_step("cv", cv_sb, cv_rb, 1)

    @pl.when(p == 1)
    def _():
        remote(x_in, x_in, h_send.at[0], h_recv.at[0], sib).wait_recv()
        token_entry()
        line_step("n1", n1_all, 1, 2, 3)

    relay4("Q", "O")
    wide_q = side_by_side([flat(W["Q"][j, :, :, s]) for j in range(2) for s in range(3)])
    qkv_both = low(mm(flat(n1_all[...]), wide_q))
    for j in range(2):
        qkv[j] = qkv_both[:, j * 3 * hq : (j + 1) * 3 * hq]
    @pl.loop(0, Z)
    def _(b):
        rows = lanes_of(b, TOK)
        for j in range(2):
            outs = []
            for h in range(hq // HD):
                q, kk, vals = (qkv[j, rows, s * hq + h * HD : s * hq + (h + 1) * HD] for s in range(3))
                sc = mm_nt(q, kk) * HD ** (-0.5)
                e = jnp.exp(sc - jnp.max(sc, axis=-1, keepdims=True))
                pr = low(e / jnp.sum(e, axis=-1, keepdims=True))
                prob[j, h, b] = pr
                outs.append(mm(pr, vals))
            ctx[j, rows, :] = low(side_by_side(outs))

    out_cols = [
        jnp.concatenate([W["O"][0, z, rr], W["O"][1, z, rr]], axis=0) for z in range(Z) for rr in range(R)
    ]
    o_sb[...] = low(mm(side_by_side([ctx[0], ctx[1]]), side_by_side(out_cols))).reshape(Z, TOK, d_dim)
    sum_start("o", o_sb, o_rb)

    relay3("F1")

    sum_wait("cv", cv_rb)
    cv_sum[...] = summed(cv_sb, cv_rb)
    c2f[...] = wide(c_in[...]) + gain_c(50) * cv_sum[...]
    c2_low = low(c2f[...])
    c2_all[zi] = c2_low
    line_start("c2", c2_all)
    sum_step("o", o_sb, o_rb, 2)
    hid_grid[x] = c2_low

    @pl.when(p == 0)
    def _():
        remote(hid_grid.at[x], c_in, h_send.at[1], h_recv.at[1], sib).start()

    relay3("F2")
    sum_step("o", o_sb, o_rb, 1)
    line_step("c2", c2_all, 1)
    sum_wait("o", o_rb)
    x1[...] = wide(x_in[...]) + summed(o_sb, o_rb)
    n_hat, _ = normed(x1[...])
    n2_all[zi] = low(n_hat * gain_d(1))
    line_start("n2", n2_all)

    relay4("E", "Gi", "Go")
    line_step("c2", c2_all, 2)
    line_step("n2", n2_all, 1)
    line_step("c2", c2_all, 3)
    row8 = lax.broadcasted_iota(jnp.int32, (8, adq), 0)
    gs_part = None
    ad_both = mm(flat(c2_all[...]), side_by_side([flat(W["E"][0]), flat(W["E"][1])]))
    for j in range(2):
        ad = ad_both[:, j * adq : (j + 1) * adq]
        adapted[j] = ad
        taps = aq[j]
        pool = jnp.zeros((8, adq), F32)
        for b in range(Z):
            sp = depthwise(ad[b * TOK : (b + 1) * TOK], lambda k: taps[k : k + 1], 3)
            spread[j, b] = sp
            pool = jnp.where(row8 == b, jnp.mean(sp, axis=0, keepdims=True), pool)
        pooled[j] = pool
        term = mm_nt(low(pool), flat(W["Gi"][j]))
        gs_part = term if gs_part is None else gs_part + term
    gsb[3] = gs_part
    share_start("gs", gsb)
    line_step("n2", n2_all, 2)

    relay4("F1")
    line_step("n2", n2_all, 3)
    for j in range(2):
        act, der = gelu_pair(mm(flat(n2_all[...]), flat(W["F1"][j])))
        u[j] = low(act)
        up[j] = low(der)

    scatter_wait("gs", gsb)

    def gate_hidden():
        return gelu_pair((gsb[0] + gsb[1]) + (gsb[2] + gsb[3]))

    gh, _ = gate_hidden()
    for j in range(2):
        g8 = jnp.tanh(mm(low(gh), flat(W["Go"][j])))
        gate[j] = g8
        for b in range(Z):
            br_sb[b, :, j * adq : (j + 1) * adq] = low(g8[b : b + 1] * spread[j, b])
    scatter_start("br", br_sb, br_rb)
    relay4("F2")

    u_both = side_by_side([u[0], u[1]])

    @pl.loop(0, Z // 2)
    def _(pair):
        halves = [
            side_by_side([W["F2"][j, 2 * pair + dz_, rr] for dz_ in range(2) for rr in range(R)])
            for j in range(2)
        ]
        acc = mm(u_both, jnp.concatenate(halves, axis=0))
        m_sb[:, :, lanes_of(pair, 2 * dz)] = low(acc).reshape(Z, TOK, 2 * dz)

    sum_start("m", m_sb, m_rb)

    def exchange(n, buf):
        remote(buf.at[x], buf.at[x], xo_send.at[n], xo_recv.at[n], over_x).start()

    def layer_output(total):
        sum_step("m", m_sb, m_rb, 2)
        scatter_wait("br", br_rb)
        total[...] = x1[...]
        for d in range(Z):
            piece = br_sb[zi] if d == 0 else br_rb[d - 1]
            for j in range(2):
                lanes = pl.ds(pl.multiple_of(j * adh + zfrom(d) * adq, LANE), adq)
                total[:, lanes] += wide(piece[:, j * adq : (j + 1) * adq])
        sum_step("m", m_sb, m_rb, 1)
        sum_wait("m", m_rb)
        hid_tok[x] = low(total[...] + summed(m_sb, m_rb))

    @pl.when(p == 0)
    def _():
        layer_output(dx1)
        remote(hid_tok.at[x], x_in, h_send.at[0], h_recv.at[0], sib).start()
        exchange(0, hid_tok)

    exchange(1, hid_grid)
    relay_sent()

    def over_cores(d):
        return remote(
            out_gtok.at[x], dx3_all.at[zi], b_send.at[d], b_recv.at[d], dev(zto(d), pp=1 - p)
        )

    @pl.when(p == 0)
    def _():
        for d in range(Z):
            slot = dx3_all.at[zfrom(d)]
            remote(slot, slot, b_send.at[d], b_recv.at[d], sib).wait_recv()
        dx3[...] = dx3_all[zi]

    def own_lanes(j):
        return pl.ds(pl.multiple_of(j * adh + zi * adq, LANE), adq)

    gh, ghp = gate_hidden()
    dgh_part = None
    dgp = []
    for j in range(2):
        dgate = jnp.zeros((8, adq), F32)
        for b in range(Z):
            dbr = wide(dx3_all[b, :, own_lanes(j)])
            dgate = jnp.where(row8 == b, jnp.sum(dbr * spread[j, b], axis=0, keepdims=True), dgate)
        dg8 = low(dgate * (1.0 - gate[j] * gate[j]))
        dgp.append(dg8)
        term = mm_nt(dg8, flat(W["Go"][j]))
        dgh_part = term if dgh_part is None else dgh_part + term
    dgb[3] = dgh_part
    share_start("dgh", dgb)

    for j in range(2):
        cols = side_by_side([W["F2"][j, z, rr] for z in range(Z) for rr in range(R)])
        dh[j] = low(mm_nt(flat(dx3_all[...]), cols) * wide(up[j]))

    scatter_wait("dgh", dgb)
    dgs = low(((dgb[0] + dgb[1]) + (dgb[2] + dgb[3])) * ghp)
    for j in range(2):
        dpool = mm(dgs, flat(W["Gi"][j])) * (1.0 / TOK)
        taps = aq[j]
        tap_rows = [None] * 9
        for b in range(Z):
            dsp = gate[j, b : b + 1] * wide(dx3_all[b, :, own_lanes(j)]) + dpool[b : b + 1]
            dad[j, b * TOK : (b + 1) * TOK] = low(depthwise(dsp, lambda k: taps[8 - k : 9 - k], 3))

            def put(k, row):
                tap_rows[k] = row if tap_rows[k] is None else tap_rows[k] + row

            depthwise_taps(adapted[j, b * TOK : (b + 1) * TOK], dsp, 3, put)
        for k in range(9):
            gad[j, k : k + 1] = tap_rows[k]
        gad[j, 9:16] = jnp.zeros((7, adq), F32)

    pair_out(dad, "E", dc2_sb, cz)

    sum_start("dc2", dc2_sb, dc2_rb)

    pair_out(dh, "F1", dn2_sb, dz)

    sum_start("dn2", dn2_sb, dn2_rb)
    sum_step("dc2", dc2_sb, dc2_rb, 2)

    def half_rows(name, upper):
        half = W[name].shape[-2] // 2
        rows = slice(half, None) if upper else slice(0, half)
        return (slice(None), rows) if len(W[name].shape) == 6 else (rows,)

    fine = ("P1", "P2")

    def pieces(name):
        return (1, 2, 3, 0) if name in fine else (None,)

    def block_at(d):
        return slice(None) if d is None else zto(d)

    def hop_copy(name, which, d):
        n = ids[name]
        lower, upper = half_rows(name, False), half_rows(name, True)
        z = block_at(d)
        w, buf = W[name], RX[name]
        src, dst, to = (
            lambda: (w.at[(xo, z, slice(None)) + lower], buf[0].at[z], over_x),
            lambda: (w.at[(slice(None), z, ro) + upper], buf[1].at[:, z], over_r),
            lambda: (buf[0].at[z, ro], buf[2].at[z], over_r),
            lambda: (buf[1].at[xo, z], buf[3].at[z], over_x),
        )[which]()
        k = 0 if d is None else d
        return remote(src, dst, g_send.at[n, which, k], g_recv.at[n, which, k], to)

    def reduce_start(name, d=None):
        hop_copy(name, 0, d).start()
        hop_copy(name, 1, d).start()

    def each_block(d, body):
        if d is None:
            pl.loop(0, Z)(body)
        else:
            body(zto(d))

    def per_piece(name, body):
        if name in fine:
            pl.loop(0, Z)(lambda k: body(lax.rem(k + 1, Z)))
        else:
            body(None)

    def reduce_middle(*names):
        for name in names:
            lower, upper = half_rows(name, False), half_rows(name, True)
            buf = RX[name]

            def middle(d):
                hop_copy(name, 0, d).wait_recv()

                def add_lower(z):
                    for rr in range(R):
                        own = W[name][(x, z, rr) + lower]
                        buf[0][z, rr] = low(wide(own) + wide(buf[0][z, rr]))

                each_block(d, add_lower)
                hop_copy(name, 2, d).start()
                hop_copy(name, 1, d).wait_recv()

                def add_upper(z):
                    for j in range(2):
                        own = W[name][(j, z, ri) + upper]
                        buf[1][j, z] = low(wide(own) + wide(buf[1][j, z]))

                each_block(d, add_upper)
                hop_copy(name, 3, d).start()

            per_piece(name, middle)

    def reduce_end(*names):
        for name in names:
            lower, upper = half_rows(name, False), half_rows(name, True)
            buf = RX[name]

            def end(d):
                hop_copy(name, 2, d).wait_recv()
                hop_copy(name, 3, d).wait_recv()

                def add_both(z):
                    W[name][(x, z, ri) + lower] = low(wide(buf[0][z, ri]) + wide(buf[2][z]))
                    W[name][(x, z, ri) + upper] = low(wide(buf[1][x, z]) + wide(buf[3][z]))

                each_block(d, add_both)

            if name in fine:

                @pl.loop(1, Z)
                def _(d):
                    end(d)
                    back_copy(name, d).start()

                end(0)
            else:
                end(None)
                for d in range(1, Z):
                    back_copy(name, d).start()
            back_local(name).start()

    def landing(name):
        return nat if name in ("P1", "P2") else native[name]

    def back_copy(name, d):
        n = ids[name]
        return remote(
            W[name].at[x, zto(d), ri], quarter_of(name, landing(name), zi),
            a_send.at[n, d - 1], a_recv.at[n, d - 1], dev(zto(d)),
        )

    def back_local(name):
        return pltpu.make_async_copy(
            W[name].at[x, zi, ri], quarter_of(name, landing(name), zi), loc_sem.at[ids[name]]
        )

    peers = ((1, 0), (0, 1), (1, 1))

    def owner(k):
        return (ro if peers[k][0] else ri), (xo if peers[k][1] else x)

    def row_grad(name, left, right):
        width = W[name].shape[3]
        span = R * width

        @pl.loop(0, Z)
        def _(k):
            d = lax.rem(k + 1, Z)
            z = zto(d)
            turned[0:span] = flat(left[:, :, lanes_of(z, span)]).T
            for j in range(2):
                W[name][j, z] = low(mm(turned[0:span], right[j])).reshape(R, width, -1)
            if name in fine:
                reduce_start(name, d)

        if name not in fine:
            reduce_start(name)

    def col_grad(name, left, right):
        width = left.shape[2]
        for j in range(2):
            turned[j * width : (j + 1) * width] = left[j].T

        @pl.loop(0, Z)
        def _(z):
            rhs = flat(right[:, :, lanes_of(z, dz)])
            for j in range(2):
                g = low(mm(turned[j * width : (j + 1) * width], rhs))
                for rr in range(R):
                    W[name][j, z, rr] = g[:, rr * LANE : (rr + 1) * LANE]

        reduce_start(name)

    for j in range(2):
        W["Gi"][j] = low(mm_tn(dgs, low(pooled[j]))).reshape(Z, R, -1, adq)
        W["Go"][j] = low(mm_tn(low(gh), dgp[j])).reshape(Z, R, -1, adq)
    sum_step("dc2", dc2_sb, dc2_rb, 1)
    sum_step("dn2", dn2_sb, dn2_rb, 2)
    reduce_start("Gi")
    reduce_start("Go")
    row_grad("E", c2_all, dad)
    sum_step("dn2", dn2_sb, dn2_rb, 1)

    @pl.when(p == 0)
    def _():
        remote(dcot, dcot, c_send, c_recv, sib).wait_recv()

    sum_wait("dc2", dc2_rb)
    dc2t[...] = wide(dcot[...]) + summed(dc2_sb, dc2_rb)
    gvs_ls = jnp.sum(cv_sum[...] * dc2t[...], axis=0, keepdims=True)
    dcv_all[zi] = low(dc2t[...] * gain_c(50))
    line_start("dcv", dcv_all)

    sum_wait("dn2", dn2_rb)
    dn2 = summed(dn2_sb, dn2_rb)
    n_hat, rs = normed(x1[...])
    gvs_d1 = jnp.sum(dn2 * n_hat, axis=0, keepdims=True)
    dx1[...] = wide(dx3[...]) + norm_back(dn2, n_hat, rs, gain_d(1))
    dx1_all[zi] = low(dx1[...])
    line_start("dx1", dx1_all)
    line_step("dcv", dcv_all, 1)
    col_grad("F2", u, dx3_all)
    line_step("dcv", dcv_all, 2)
    line_step("dx1", dx1_all, 1)
    row_grad("F1", n2_all, dh)

    line_step("dcv", dcv_all, 3)
    line_step("dx1", dx1_all, 2)

    def operand_copies():
        return [
            remote(src, dst, m_send.at[n], m_recv.at[n], sib)
            for n, (src, dst) in enumerate(((f_all, alt_a), (dhc, alt_b)))
        ]

    def operand_copies_back():
        return [
            remote(src, dst, m_send.at[n], m_recv.at[n], sib)
            for n, (src, dst) in enumerate(((dcv_all, alt_a), (r, alt_b)))
        ]

    def chosen(flag_at, left, right):
        for n, buf in enumerate((alt_a, alt_b)):
            remote(buf, buf, m_send.at[n], m_recv.at[n], sib).wait_recv()
        mine = train_in[0, flag_at] == 1
        alt_a[...] = jnp.where(mine, left[...], alt_a[...])
        alt_b[...] = jnp.where(mine, right[...], alt_b[...])

    @pl.when(p == 0)
    def _():
        for c in operand_copies_back():
            c.start()

    for j in range(2):
        dhc[j] = low(mm(flat(dcv_all[...]), flat(W["P2"][j])) * wide(rp[j]))

    @pl.when(p == 1)
    def _():
        for c in operand_copies():
            c.start()

    pair_out(dhc, "P1", df_sb, cz)

    sum_start("df", df_sb, df_rb)

    early = ("Gi", "Go", "E", "F2", "F1")

    def pw_grads():
        chosen(2, f_all, dhc)
        row_grad("P1", alt_a, alt_b)

    line_step("dx1", dx1_all, 3)

    @pl.when(p == 0)
    def _():
        pw_grads()

    sum_step("df", df_sb, df_rb, 2)

    out_rows = [
        side_by_side([W["O"][j, z, rr] for z in range(Z) for rr in range(R)]) for j in range(2)
    ]
    do_both = low(mm_nt(flat(dx1_all[...]), jnp.concatenate(out_rows, axis=0)))
    for j in range(2):
        do_all[j] = do_both[:, j * hq : (j + 1) * hq]
    @pl.loop(0, Z)
    def _(b):
        rows = lanes_of(b, TOK)
        for j in range(2):
            parts = [[], [], []]
            for h in range(hq // HD):
                q, kk, vals = (qkv[j, rows, s * hq + h * HD : s * hq + (h + 1) * HD] for s in range(3))
                do = do_all[j, rows, h * HD : (h + 1) * HD]
                pr = prob[j, h, b]
                dp = mm_nt(do, vals)
                prw = wide(pr)
                ds = low(prw * (dp - jnp.sum(dp * prw, axis=-1, keepdims=True)) * HD ** (-0.5))
                parts[0].append(mm(ds, kk))
                parts[1].append(mm_tn(ds, q))
                parts[2].append(mm_tn(pr, do))
            for s in range(3):
                dqkv[j, rows, s * hq : (s + 1) * hq] = low(side_by_side(parts[s]))

    dqkv_both = side_by_side([dqkv[0], dqkv[1]])

    @pl.loop(0, Z // 2)
    def _(pair):
        zs = pl.ds(pair * 2, 2)
        rows_q = side_by_side([flat(W["Q"][j, zs, :, s]) for j in range(2) for s in range(3)])
        acc = mm_nt(dqkv_both, rows_q)
        dn1_sb[:, :, lanes_of(pair, 2 * dz)] = low(acc).reshape(Z, TOK, 2 * dz)

    sum_start("dn1", dn1_sb, dn1_rb)
    sum_step("df", df_sb, df_rb, 1)
    reduce_middle("Gi", "Go", "E")

    def attention_grads():
        @pl.loop(0, Z)
        def _(z):
            turned[0:dz] = flat(n1_all[:, :, lanes_of(z, dz)]).T
            for j in range(2):
                g = low(mm(turned[0:dz], dqkv[j]))
                for s in range(3):
                    W["Q"][j, z, :, s] = g[:, s * hq : (s + 1) * hq].reshape(R, -1, hq)

        reduce_start("Q")
        col_grad("O", ctx, dx1_all)

    sum_step("dn1", dn1_sb, dn1_rb, 2)
    reduce_middle("F2", "F1")
    sum_step("dn1", dn1_sb, dn1_rb, 1)

    @pl.when(p == 0)
    def _():
        reduce_middle("P1")
        attention_grads()
        reduce_end(*early)

    sum_wait("dn1", dn1_rb)
    dn1 = summed(dn1_sb, dn1_rb)
    n_hat, rs = normed(wide(x_in[...]))
    gvs_d0 = jnp.sum(dn1 * n_hat, axis=0, keepdims=True)
    out_gtok[x] = low(dx1[...] + norm_back(dn1, n_hat, rs, gain_d(0)))

    @pl.when(p == 1)
    def _():
        for d in (1, 2, 3, 0):
            over_cores(d).start()

    sum_wait("df", df_rb)
    dfv = summed(df_sb, df_rb)
    gvs_lc = jnp.sum(dfv * cn[...], axis=0, keepdims=True)
    dcn[...] = norm_back(dfv, cn[...], crs[:, 0:1], gain_c(49))

    @pl.loop(0, c_dim // LANE)
    def _(ch):
        lanes = lanes_of(ch, LANE)
        taps = vec_c[:, lanes]
        back = depthwise(dcn[:, lanes], lambda k: taps[48 - k : 49 - k], 7)
        out_ggrid[x, :, lanes] = low(dc2t[:, lanes] + back)

    @pl.when(p == 1)
    def _():
        remote(out_ggrid.at[x], dcot, c_send, c_recv, sib).start()
        attention_grads()
        layer_output(dx1)
        exchange(0, hid_tok)
        reduce_end(*early)

    @pl.when(p == 0)
    def _():
        reduce_end("P1")

    exchange(2, out_gtok)
    exchange(3, out_ggrid)

    @pl.loop(0, Z)
    def _(z):
        for part in range(cz // LANE):
            lanes = pl.ds(pl.multiple_of(z * cz + part * LANE, LANE), LANE)

            def put(k, row):
                gvs[z, k : k + 1, part * LANE : (part + 1) * LANE] = row

            depthwise_taps(wide(c_in[:, lanes]), dcn[:, lanes], 7, put)

    for z in range(Z):
        gvs[z, 49:50] = gvs_lc[:, z * cz : (z + 1) * cz]
        gvs[z, 50:51] = gvs_ls[:, z * cz : (z + 1) * cz]
        gvs[z, 51:64] = jnp.zeros((13, cz), F32)
        gvs[z, 56:57, 0:dz] = gvs_d0[:, z * dz : (z + 1) * dz]
        gvs[z, 57:58, 0:dz] = gvs_d1[:, z * dz : (z + 1) * dz]
    gvs_low[...] = low(gvs[...])
    scatter_start("gv", gvs_low, gv_rb)

    def group_copy(n, k, src, dst):
        rr, xx = owner(k)
        return remote(src, dst, gx_send.at[n, k], gx_recv.at[n, k], dev(rr=rr, xx=xx))

    for k in range(3):
        c = group_copy(1, k, gad, gad_rb.at[k])
        c.start()
        sent.append(c)
    scatter_wait("gv", gv_rb)
    gvx[3] = (gvs[zi] + wide(gv_rb[0])) + (wide(gv_rb[1]) + wide(gv_rb[2]))
    for k in range(3):
        c = group_copy(0, k, gvx.at[3], gvx.at[k])
        c.start()
        sent.append(c)
    for k in range(3):
        group_copy(1, k, gad, gad_rb.at[k]).wait_recv()
    gad_all[zi] = (gad[x] + gad_rb[0, x]) + (gad_rb[1, x] + gad_rb[2, x])
    gather_start("gad", gad_all)
    reduce_middle("Q", "O")
    reduce_end("Q", "O")

    @pl.when(p == 1)
    def _():
        chosen(3, dcv_all, r)
        row_grad("P2", alt_a, alt_b)
        reduce_middle("P2")
        reduce_end("P2")

    def to_both(name):
        n = ids[name]
        back_local(name).wait()
        for d in range(1, Z):
            slot = quarter_of(name, nat, zfrom(d))
            remote(slot, slot, a_send.at[n, d - 1], a_recv.at[n, d - 1], dev(zto(d))).wait_recv()
        pltpu.make_async_copy(nat, native[name], f_sem).start()
        remote(nat, native[name], f_send, f_recv, sib).start()

    def both_done(name, other):
        pltpu.make_async_copy(nat, native[name], f_sem).wait()
        remote(nat, native[name], f_send, f_recv, sib).wait_send()
        remote(nat, native[other], f_send, f_recv, sib).wait_recv()

    @pl.when(p == 0)
    def _():
        to_both("P1")

    @pl.when(p == 1)
    def _():
        to_both("P2")

    for k in range(3):
        group_copy(0, k, gvx.at[k], gvx.at[k]).wait_recv()
    total = (gvx[0] + gvx[1]) + (gvx[2] + gvx[3])
    mine = jnp.where(ri == 1, pltpu.roll(total, c_own, 1), total)[:, 0:c_own]
    mine_d = jnp.where(ri == 1, total[:, LANE : 2 * LANE], total[:, 0:LANE])

    def flag(n):
        return train_in[0, n].astype(F32)

    out_depth[...] = mine[0:taps7] * flag(0)
    out_ln_conv[...] = mine[49:50] * flag(1)
    out_scale[...] = mine[50:51] * flag(4)
    out_ln_attn[...] = mine_d[56:57]
    out_ln_mlp[...] = mine_d[57:58]
    gather_wait("gad", gad_all)
    for z in range(Z):
        out_ad[:, z * adq : (z + 1) * adq] = gad_all[z][0:9]
    for name in ARRAYS[2:]:
        back_local(name).wait()
        for d in range(1, Z):
            n = ids[name]
            slot = quarter_of(name, native[name], zfrom(d))
            remote(slot, slot, a_send.at[n, d - 1], a_recv.at[n, d - 1], dev(zto(d))).wait_recv()
    for n, buf in enumerate((hid_tok, hid_grid, out_gtok, out_ggrid)):
        c = remote(buf.at[x], buf.at[x], xo_send.at[n], xo_recv.at[n], over_x)
        c.wait_send()
        remote(buf.at[xo], buf.at[xo], xo_send.at[n], xo_recv.at[n], over_x).wait_recv()

    @pl.when(p == 0)
    def _():
        remote(hid_tok.at[x], x_in, h_send.at[0], h_recv.at[0], sib).wait_send()
        remote(hid_grid.at[x], c_in, h_send.at[1], h_recv.at[1], sib).wait_send()

    @pl.when(p == 1)
    def _():
        for d in range(Z):
            over_cores(d).wait_send()
        remote(out_ggrid.at[x], dcot, c_send, c_recv, sib).wait_send()

    for name, buf in line_gathers:
        line_sent(name, buf)

    @pl.when(p == 1)
    def _():
        line_sent("dx3", dx3_all)

    for name, sb, rb in line_sums:
        sum_sent(name, sb, rb)
    for c in sent:
        c.wait_send()
    def all_sent(name):
        for which in range(4):
            for d in pieces(name):
                hop_copy(name, which, d).wait_send()
        for d in range(1, Z):
            back_copy(name, d).wait_send()

    for name in ARRAYS[2:]:
        all_sent(name)

    @pl.when(p == 0)
    def _():
        all_sent("P1")
        for c in operand_copies_back():
            c.wait_send()
        both_done("P1", "P2")

    @pl.when(p == 1)
    def _():
        all_sent("P2")
        for c in operand_copies():
            c.wait_send()
        both_done("P2", "P1")


def run_layers(weights, vectors, order, train, streams, sizes, outer):
    d_dim, c_dim, hq, ffq, cfq, adw, dg = sizes
    vm = pltpu.VMEM
    blocks = []
    for name, value in zip(ARRAYS, weights):
        if name == "Q":
            blocks.append((3, value.shape[1], hq))
        elif name in ("O", "F2"):
            blocks.append((value.shape[0] // Z, value.shape[1]))
        else:
            blocks.append((value.shape[0], value.shape[1] // Z))
    rows = Z * TOK

    def act(width, count=Z, kind=BF):
        return vm((count, TOK, width), kind)

    def line(width):
        return vm((2, 3, TOK, width), BF)

    scratch = [vm((2, Z, R) + s, BF) for s in blocks] + [
        vm(lead + s[:-2] + (s[-2] // 2, s[-1]), BF)
        for s in blocks[1:]
        for lead in ((Z, R), (2, Z), (Z,), (Z,))
    ]
    scratch += [
        vm((64, 2 * LANE), F32), vm((64, 2 * LANE), BF), vm((Z * R, 64, 2 * LANE), BF), vm((2, 16, adw), F32), vm((64, c_dim), F32), vm((8, d_dim), F32),
        vm((TOK, d_dim), BF), vm((TOK, c_dim), BF), act(d_dim), act(c_dim), act(d_dim), act(c_dim),
        act(d_dim), line(d_dim), act(c_dim), line(c_dim), act(d_dim), line(d_dim),
        act(2 * adw), act(2 * adw, 3), vm((4, 8, dg), F32), vm((4, 8, dg), F32),
        vm((2, rows, 3 * hq), BF), vm((2, hq // HD, Z, TOK, TOK), BF), vm((2, rows, hq), BF),
        vm((2, rows, ffq), BF), vm((2, rows, ffq), BF), vm((2, rows, cfq), BF), vm((2, rows, cfq), BF),
        vm((TOK, c_dim), F32), vm((TOK, LANE), F32), vm((TOK, c_dim), F32), vm((TOK, d_dim), F32), vm((TOK, c_dim), F32),
        vm((2, rows, adw), F32), vm((2, Z, TOK, adw), F32), vm((2, 8, adw), F32), vm((2, 8, adw), F32),
        vm((TOK, d_dim), BF), vm((TOK, c_dim), BF), act(d_dim), act(d_dim), line(d_dim), act(c_dim), line(c_dim),
        act(d_dim), act(c_dim),
        act(d_dim), line(d_dim), act(c_dim), line(c_dim), vm((2, rows, ffq), BF), vm((2, rows, hq), BF),
        vm((2, rows, 3 * hq), BF), vm((2, rows, cfq), BF), vm((TOK, d_dim), F32), vm((TOK, c_dim), F32), vm((2, rows, adw), BF),
        vm((TOK, c_dim), F32),
        vm((Z, 64, c_dim // Z), F32), vm((Z, 64, c_dim // Z), BF), vm((3, 64, c_dim // Z), BF), vm((4, 64, c_dim // Z), F32),
        vm((2, 16, adw), F32), vm((3, 2, 16, adw), F32), vm((Z, 16, adw), F32),
        vm((2 * ffq, rows), BF), act(c_dim), vm((2, rows, cfq), BF), vm(weights[0].shape, BF),
    ]
    dma = pltpu.SemaphoreType.DMA
    na = len(ARRAYS)
    scratch += [
        dma((len(EVENTS), 3)), dma((len(EVENTS), 3)), dma((len(EVENTS), 6)), dma((len(EVENTS), 6)), dma((na, 3)), dma((na, 3)), dma((na,)),
        dma((na, 4, Z)), dma((na, 4, Z)), dma((7,)), dma((7,)), dma, dma, dma((2,)), dma((2,)), dma((Z,)), dma((Z,)), dma, dma,
        dma((4,)), dma((4,)), dma((na, 4, Z)), dma((na, 4, Z)), dma((na, 3)), dma((na, 3)), dma((2, 3)), dma((2, 3)),
        pltpu.SemaphoreType.REGULAR,
        dma((2,)), dma((2,)), dma, dma, dma,
    ]
    sds = jax.ShapeDtypeStruct
    out_shape = [sds((2, TOK, d_dim), BF), sds((2, TOK, c_dim), BF)] * 2
    out_shape += [sds(value.shape, BF) for value in weights]
    out_shape += [sds(value.shape, F32) for value in vectors]
    any_spec = pl.BlockSpec(memory_space=pl.ANY)
    vm_spec = pl.BlockSpec(memory_space=pltpu.VMEM)
    sm_spec = pl.BlockSpec(memory_space=pltpu.SMEM)
    return pl.pallas_call(
        functools.partial(main_kernel, sizes, outer),
        out_shape=out_shape,
        in_specs=[any_spec] * na + [vm_spec] * 6 + [sm_spec] * 2 + [vm_spec] * 4,
        out_specs=[vm_spec] * 4 + [any_spec] * na + [vm_spec] * 6,
        scratch_shapes=scratch,
        compiler_params=pltpu.CompilerParams(
            collective_id=0, has_side_effects=True, vmem_limit_bytes=62 * 1024 * 1024
        ),
        cost_estimate=pl.CostEstimate(flops=26 * 10**9, bytes_accessed=10**8, transcendentals=10**7),
        name="layers",
    )(*weights, *vectors, order, train, *streams)


def finish_kernel(flagged, layer_zero, count, *refs):
    grads, streams, vectors = refs[:count], refs[count : count + 4], refs[count + 4 : count + 10]
    order, train = refs[count + 10 : count + 12]
    refs = refs[count + 12 :]
    out_grads, out_streams, out_vectors = refs[:count], refs[count : count + 4], refs[count + 4 : count + 10]
    refs = refs[count + 10 :]
    held, wide_ones = refs[:count], refs[count : 2 * count]
    in_sem, out_sem = refs[2 * count :]

    def fetch(n):
        return pltpu.make_async_copy(grads[n], held[n], in_sem.at[n])

    def put_back(n):
        return pltpu.make_async_copy(wide_ones[n], out_grads[n], out_sem.at[n])

    for n in range(count):
        fetch(n).start()
    swap = (lax.axis_index("pipe") == layer_zero) & (order[0, 0] == 1)
    for n, (src, dst) in enumerate(zip(streams, out_streams)):
        for m in range(2):
            dst[m] = src[m] if n < 2 else jnp.where(swap, src[1 - m], src[m])
    for src, dst in zip(vectors, out_vectors):
        if len(dst.shape) == 3:
            for row in range(dst.shape[0]):
                dst[row] = src[row : row + 1]
        else:
            dst[...] = src[...]
    for n in range(count):
        fetch(n).wait()
        src, dst = held[n], wide_ones[n]
        scale = train[0, flagged[n]].astype(F32) if n in flagged else None
        lead = src.shape[0] if len(src.shape) == 3 else 1

        @pl.loop(0, lead * (src.shape[-2] // 16))
        def _(step):
            rows = pl.ds(pl.multiple_of((step // lead) * 16, 16), 16)
            at = (step % lead, rows) if len(src.shape) == 3 else (rows,)
            value = wide(src[at])
            dst[at] = value if scale is None else value * scale

        put_back(n).start()
    for n in range(count):
        put_back(n).wait()


def finish(outs, order, train):
    count = len(ARRAYS)
    streams, grads, vectors = outs[:4], outs[4 : 4 + count], outs[4 + count :]
    any_spec = pl.BlockSpec(memory_space=pl.ANY)
    sm_spec = pl.BlockSpec(memory_space=pltpu.SMEM)
    vm_spec = pl.BlockSpec(memory_space=pltpu.VMEM)
    sds = jax.ShapeDtypeStruct
    dma = pltpu.SemaphoreType.DMA
    flagged = {ARRAYS.index("P1"): 2, ARRAYS.index("P2"): 3}
    return pl.pallas_call(
        functools.partial(finish_kernel, flagged, 0, count),
        out_shape=[sds(g.shape, F32) for g in grads]
        + [sds(value.shape, value.dtype) for value in streams]
        + [sds(value.shape if value.shape[0] == 1 else (value.shape[0], 1, value.shape[1]), F32) for value in vectors],
        in_specs=[any_spec] * count + [vm_spec] * 10 + [sm_spec] * 2,
        out_specs=[any_spec] * count + [vm_spec] * 10,
        scratch_shapes=[pltpu.VMEM(g.shape, BF) for g in grads]
        + [pltpu.VMEM(g.shape, F32) for g in grads]
        + [dma((count,)), dma((count,))],
        compiler_params=pltpu.CompilerParams(vmem_limit_bytes=62 * 1024 * 1024),
        name="finish",
    )(*grads, *streams, *vectors, order, train)


def per_device(
    tokens,
    conv_grid,
    order,
    trainable,
    ln_attn,
    w_qkv,
    w_attn_out,
    ln_mlp,
    w_fc_in,
    w_fc_out,
    conv_depth,
    ln_conv,
    w_pw_in,
    w_pw_out,
    layer_scale,
    w_adapt,
    adapt_depth,
    w_gate_in,
    w_gate_out,
    tok_cot,
    grid_cot,
):
    dp_count = lax.axis_size("dp")
    outer = dp_count // (Z * R)
    groups = [[g * outer + o for o in range(outer)] for g in range(Z * R)]

    def block(value, axis):
        value = value[0]
        if outer == 1:
            return value
        return lax.all_gather(value, "dp", axis=axis, tiled=True, axis_index_groups=groups)

    def share(value, axis):
        if outer > 1:
            value = lax.psum_scatter(
                value, "dp", scatter_dimension=axis, tiled=True, axis_index_groups=groups
            )
        return value[None]

    qkv = block(w_qkv, 1)
    gate_in = block(w_gate_in, 1).T
    pw_in = block(w_pw_in, 0)
    adapt = block(w_adapt, 0)
    fc_in = block(w_fc_in, 0)
    weights = (
        pw_in,
        block(w_pw_out, 1).T,
        qkv,
        block(w_attn_out, 1),
        adapt,
        gate_in,
        block(w_gate_out, 0),
        fc_in,
        block(w_fc_out, 1),
    )
    vectors = (
        block(conv_depth, 1),
        block(ln_conv, 0)[None],
        block(layer_scale, 0)[None],
        block(ln_attn, 0)[None],
        block(ln_mlp, 0)[None],
        adapt_depth[0],
    )
    spread = Z * R
    sizes = (
        qkv.shape[1] * spread, pw_in.shape[0] * spread, qkv.shape[2] // Z, fc_in.shape[1] // Z,
        pw_in.shape[1] // Z, adapt.shape[1] // Z, gate_in.shape[0] * spread,
    )

    def rows_of(value):
        return value.reshape(value.shape[0], TOK, value.shape[-1])

    streams = [rows_of(value) for value in (tokens, conv_grid, tok_cot, grid_cot)]
    outs = run_layers(weights, vectors, order, trainable, streams, sizes, outer)
    done = finish(outs, order, trainable)
    g_p1, g_p2, g_q, g_o, g_e, g_gi, g_go, g_f1, g_f2 = done[:9]
    hid_tok, hid_grid, g_tok, g_grid = done[9:13]
    g_depth, g_ln_conv, g_scale, g_ln_attn, g_ln_mlp, g_ad = done[13:]
    grid_shape = (1,) + conv_grid.shape
    tok_shape = (1,) + tokens.shape
    g_depth, g_ad = g_depth[:, 0], g_ad[:, 0]
    if outer > 1:
        g_ad = lax.psum(g_ad, "dp", axis_index_groups=groups)
    return (
        hid_tok.reshape(tok_shape),
        hid_grid.reshape(grid_shape),
        g_tok.reshape(tok_shape),
        g_grid.reshape(grid_shape),
        share(g_ln_attn[0], 0),
        share(g_q, 1),
        share(g_o, 1),
        share(g_ln_mlp[0], 0),
        share(g_f1, 0),
        share(g_f2, 1),
        share(g_depth, 1),
        share(g_ln_conv[0], 0),
        share(g_p1, 0),
        share(g_p2.T, 1),
        share(g_scale[0], 0),
        share(g_e, 0),
        g_ad[None],
        share(g_gi.T, 1),
        share(g_go, 0),
    )


def solution(mesh):
    in_specs = (
        P(None, "dp", None, None),
        P(None, "dp", None, None, None),
        P("dp", None),
        P("pipe", None),
        P("pipe", "dp"),
        P("pipe", None, "dp", "tensor"),
        P("pipe", "tensor", "dp"),
        P("pipe", "dp"),
        P("pipe", "dp", "tensor"),
        P("pipe", "tensor", "dp"),
        P("pipe", None, "dp"),
        P("pipe", "dp"),
        P("pipe", "dp", "tensor"),
        P("pipe", "tensor", "dp"),
        P("pipe", "dp"),
        P("pipe", "dp", "tensor"),
        P("pipe", None, "tensor"),
        P("pipe", "tensor", "dp"),
        P("pipe", "dp", "tensor"),
        P(None, "dp", None, None),
        P(None, "dp", None, None, None),
    )
    out_specs = (
        P("pipe", None, "dp", None, None),
        P("pipe", None, "dp", None, None, None),
        P("pipe", None, "dp", None, None),
        P("pipe", None, "dp", None, None, None),
        P("pipe", "dp"),
        P("pipe", None, "dp", "tensor"),
        P("pipe", "tensor", "dp"),
        P("pipe", "dp"),
        P("pipe", "dp", "tensor"),
        P("pipe", "tensor", "dp"),
        P("pipe", None, "dp"),
        P("pipe", "dp"),
        P("pipe", "dp", "tensor"),
        P("pipe", "tensor", "dp"),
        P("pipe", "dp"),
        P("pipe", "dp", "tensor"),
        P("pipe", None, "tensor"),
        P("pipe", "tensor", "dp"),
        P("pipe", "dp", "tensor"),
    )
    return jax.shard_map(
        per_device, mesh=mesh, in_specs=in_specs, out_specs=out_specs, check_vma=False
    )
```
